32 devices in a mesh: group: 2 (over y), gx: 8 (over z, x), gy: 2 (over core).
Axes of the slice: x: 2, y: 2, z: 4, core: 2. Of those that a mesh axis runs over, the one named last changes fastest.
Arguments:
- flow_field: bfloat16 [64, 512, 512], P(('group', 'gx'), 'gy'), parts along dimension 0, may hold values from -6 to 6
- spectral_weight: bfloat16 [2, 512, 64, 128], P('gy', 'gx'), may hold values from -0.5 to 0.5
- local_weight: bfloat16 [64, 64], replicated, may hold values from -0.75 to 0.75
- bias_terms: float32 [64], replicated, may hold values from -3 to 3
Outputs:
- output: bfloat16 [64, 512, 512], P(('group', 'gx'), 'gy'), parts along dimension 0
- mixed_modes: float32 [4, 512, 1024], P(('group', 'gy'), 'gx'), parts along dimension 0
The draws below stay inside these ranges and needn't reach their ends.
There are 2 independent parts, one for each index of `group`. The reference program is written for one: setup_inputs(seed, part) draws one part's arguments, and reference() takes and returns one part's arrays. A program takes and returns all parts, laid end to end along the dimension named above; an argument that names none is the same for every part. Nothing has to cross between parts.
All inputs are finite; a program needn't handle non-finite values.
Results may differ from the reference program's by a relative error of at most 0.0027.
Values sent between devices are 32-bit elements; how exact they have to be, the bound alone decides.
No kernel may reach another device: no remote copies, remote signals or barrier semaphores. Data moves between devices by JAX's collectives and lax.ppermute only.
A program may use at most 64 MiB of HBM per device.

```python
import math
import jax
import jax.numpy as jnp
from jax import lax

C = 64
MX = 32
MY = 32
NZ = 8
NX = 32
NY = 512
FEAT = 512
HALVES = 2
HALF = 512


def block_levels(key, shape, split, low, top_value):
    gain, own = 1.0, jax.random.fold_in(key, 6)
    for position, blocks in split:
        steps = jnp.exp(jax.random.uniform(jax.random.fold_in(own, position), (blocks,), jnp.float32, low / len(split), top_value / len(split)))
        gain = gain * jnp.repeat(steps, shape[position] // blocks).reshape([-1 if axis == position else 1 for axis in range(len(shape))])
    return gain


def centred(rng, dims, spread, most, shards=(), kind=jnp.bfloat16):
    loudness = block_levels(rng, dims, shards, -0.22, 0.18) if shards else 1.0
    array = jax.random.normal(rng, dims, jnp.float32) * spread * loudness
    return jnp.minimum(jnp.maximum(array, -most), most).astype(kind)


def setup_inputs(seed: int = 0, part: int = 0) -> dict:
    arg_keys = jax.random.split(jax.random.key(seed), 5)
    part_splits = jax.random.split(jax.random.fold_in(arg_keys[4], part), 5)
    return {
        "flow_field": centred(part_splits[0], (NX, NY, FEAT), 1.0, 6.0, ((0, 8), (1, 2))),
        "spectral_weight": centred(arg_keys[1], (HALVES, HALF, C, 2 * C), (2 * C) ** -0.5, 0.5, ((0, 2), (1, 8))),
        "local_weight": centred(arg_keys[2], (C, C), C ** -0.5, 0.75),
        "bias_terms": centred(arg_keys[3], (C,), 0.5, 3.0, (), jnp.float32),
    }


def wave_number(count):
    index = jnp.arange(count, dtype=jnp.int32)
    return jnp.where(index < count // 2, index, index - count)

def phase_table(waves, places, extent):
    product = waves[:, None] * places[None, :] % extent
    return 2.0 * math.pi / extent * product.astype(jnp.float32)

def reference(flow_field, spectral_weight, local_weight, bias_terms):
    high = lax.Precision.HIGHEST
    y_angle = phase_table(wave_number(MY), jnp.arange(NY, dtype=jnp.int32), NY)
    y_table = jnp.stack([jnp.cos(y_angle), -jnp.sin(y_angle)], axis=1).reshape(2 * MY, NY).astype(jnp.bfloat16)

    def y_section(plane):
        return jnp.dot(y_table, plane, preferred_element_type=jnp.float32)
    y_modes = lax.map(y_section, flow_field).reshape(NX, MY, 2, FEAT)
    x_angle = phase_table(wave_number(MX), jnp.arange(NX, dtype=jnp.int32), NX)
    x_cos = jnp.cos(x_angle)
    x_sin = jnp.sin(x_angle)

    def along_x(table, values):
        return jnp.einsum('kx,xyf->ykf', table, values, precision=high)
    real_in = y_modes[:, :, 0]
    imag_in = y_modes[:, :, 1]
    forward_scale = 1.0 / math.sqrt(NX * NY)
    spec_real = (along_x(x_cos, real_in) + along_x(x_sin, imag_in)) * forward_scale
    spec_imag = (along_x(x_cos, imag_in) - along_x(x_sin, real_in)) * forward_scale
    coeffs = jnp.stack([spec_real, spec_imag], axis=2).reshape(MY, MX, 2, NZ, C)
    weights = spectral_weight.reshape(MY, MX, C, 2 * C).astype(jnp.float32)
    product = jnp.einsum('abpzc,abco->abpzo', coeffs, weights, precision=high)
    mixed_real = product[:, :, 0, :, :C] - product[:, :, 1, :, C:]
    mixed_imag = product[:, :, 0, :, C:] + product[:, :, 1, :, :C]
    mixed_modes = jnp.stack([mixed_real, mixed_imag], axis=2).reshape(HALVES, HALF, 2 * FEAT)
    flat_real = mixed_real.reshape(MY, MX, FEAT)
    flat_imag = mixed_imag.reshape(MY, MX, FEAT)

    def back_x(table, values):
        return jnp.einsum('kx,ykf->xyf', table, values, precision=high)
    back_real = back_x(x_cos, flat_real) - back_x(x_sin, flat_imag)
    back_imag = back_x(x_cos, flat_imag) + back_x(x_sin, flat_real)
    y_cos = jnp.cos(y_angle)
    y_sin = jnp.sin(y_angle)
    inverse_scale = 1.0 / math.sqrt(MX * MY)

    def plane_out(operands):
        plane, part_real, part_imag = operands
        spectral = (jnp.dot(y_cos.T, part_real, precision=high) - jnp.dot(y_sin.T, part_imag, precision=high)) * inverse_scale
        pointwise = jnp.dot(plane.reshape(NY * NZ, C), local_weight, preferred_element_type=jnp.float32).reshape(NY, NZ, C)
        total = spectral.reshape(NY, NZ, C) + pointwise + bias_terms
        return jax.nn.gelu(total, approximate=False).reshape(NY, FEAT).astype(jnp.bfloat16)
    output = lax.map(plane_out, (flow_field, back_real, back_imag))
    return (output, mixed_modes)
```

```python
import functools
import math

import jax
import jax.numpy as jnp
import ml_dtypes
import numpy as np
from jax import lax
from jax.experimental import pallas as pl
from jax.experimental.pallas import tpu as pltpu
from jax.sharding import PartitionSpec as P

MX = 32
MY = 32


def wave_number(index, count):
    return jnp.where(index < count // 2, index, index - count)


def phase_table(waves, places, extent):
    product = waves[:, None] * places[None, :] % extent
    return 2.0 * math.pi / extent * product.astype(jnp.float32)


def row_tables(ky_rows, kx_rows, x_places, extent, width):
    angle = phase_table(wave_number(kx_rows, MX), x_places, extent)
    select = (ky_rows[:, None] == jnp.arange(width, dtype=jnp.int32)[None, :]).astype(jnp.float32)
    cosine = jnp.cos(angle)[:, :, None] * select[:, None, :]
    sine_part = jnp.sin(angle)[:, :, None] * select[:, None, :]
    return (cosine, sine_part)


def forward_rows(y_local, ky_rows, kx_rows, x_places, extent):
    cosine, sine_part = row_tables(ky_rows, kx_rows, x_places, extent, y_local.shape[0])
    real_in = y_local[:, 0]
    imag_in = y_local[:, 1]

    def contract(table, values):
        return jnp.einsum("rxk,kxf->rf", table, values, precision=lax.Precision.HIGHEST)

    real_out = contract(cosine, real_in) + contract(sine_part, imag_in)
    imag_out = contract(cosine, imag_in) - contract(sine_part, real_in)
    return jnp.concatenate([real_out, imag_out], axis=1)


def inverse_rows(running, shard_rows, ky_rows, kx_rows, x_places, extent):
    cosine, sine_part = row_tables(ky_rows, kx_rows, x_places, extent, running.shape[0])
    feat_count = shard_rows.shape[1] // 2
    real_part = shard_rows[:, :feat_count]
    imag_part = shard_rows[:, feat_count:]

    def contract(table, values):
        return jnp.einsum("rxk,rf->kxf", table, values, precision=lax.Precision.HIGHEST)

    new_real = contract(cosine, real_part) - contract(sine_part, imag_part)
    new_imag = contract(cosine, imag_part) + contract(sine_part, real_part)
    return jnp.stack([new_real, new_imag], axis=1)


def general_body(flow_field, spectral_weight, local_weight, bias_terms):
    cells_x, cells_y, feat_count = flow_field.shape
    channels = local_weight.shape[0]
    planes = feat_count // channels
    groups_x = lax.axis_size("gx")
    groups_y = lax.axis_size("gy")
    extent_x = cells_x * groups_x
    extent_y = cells_y * groups_y
    half_width = MY // groups_y
    quota_rows = spectral_weight.shape[1]
    high = lax.Precision.HIGHEST
    x_places = lax.axis_index("gx") * cells_x + jnp.arange(cells_x, dtype=jnp.int32)
    y_places = lax.axis_index("gy") * cells_y + jnp.arange(cells_y, dtype=jnp.int32)
    y_angle = phase_table(wave_number(jnp.arange(MY, dtype=jnp.int32), MY), y_places, extent_y)
    y_table = (
        jnp.stack([jnp.cos(y_angle), -jnp.sin(y_angle)], axis=1)
        .reshape(2 * MY, cells_y)
        .astype(jnp.bfloat16)
    )
    y_local = lax.psum_scatter(
        jnp.einsum("qy,xyf->qxf", y_table, flow_field, preferred_element_type=jnp.float32),
        "gy",
        scatter_dimension=0,
        tiled=True,
    )
    y_local = y_local.reshape(half_width, 2, cells_x, feat_count)
    rest_index = jnp.arange(lax.axis_size("gx") * quota_rows, dtype=jnp.int32)
    spectrum = lax.psum_scatter(
        forward_rows(y_local, rest_index // MX, rest_index % MX, x_places, extent_x),
        "gx",
        scatter_dimension=0,
        tiled=True,
    )
    spectrum = spectrum * (1.0 / math.sqrt(extent_x * extent_y))
    coeffs = spectrum.reshape(quota_rows, 2, planes, channels)
    weights = spectral_weight[0].astype(jnp.float32)
    product = jnp.einsum("rpzc,rco->rpzo", coeffs, weights, precision=high)
    mixed_real = product[:, 0, :, :channels] - product[:, 1, :, channels:]
    mixed_imag = product[:, 0, :, channels:] + product[:, 1, :, :channels]
    mixed_local = jnp.stack([mixed_real, mixed_imag], axis=1).reshape(quota_rows, 2 * feat_count)
    pointwise = jnp.einsum(
        "xyzc,co->xyzo",
        flow_field.reshape(cells_x, cells_y, planes, channels),
        local_weight,
        preferred_element_type=jnp.float32,
    )
    start_half = jnp.zeros((half_width, 2, cells_x, feat_count), jnp.float32)
    shard_rows = lax.all_gather(mixed_local, "gx", axis=0, tiled=True)
    rest_index = jnp.arange(shard_rows.shape[0], dtype=jnp.int32)
    back_half = inverse_rows(
        start_half, shard_rows, rest_index // MX, rest_index % MX, x_places, extent_x
    )
    back_whole = lax.all_gather(back_half, "gy", axis=0, tiled=True)
    y_cos = jnp.cos(y_angle)
    y_sin = jnp.sin(y_angle)
    spectral = (
        jnp.einsum("kn,kxf->xnf", y_cos, back_whole[:, 0], precision=high)
        - jnp.einsum("kn,kxf->xnf", y_sin, back_whole[:, 1], precision=high)
    ) * (1.0 / math.sqrt(MX * MY))
    total = spectral.reshape(cells_x, cells_y, planes, channels) + pointwise + bias_terms
    output = (
        jax.nn.gelu(total, approximate=False)
        .reshape(cells_x, cells_y, feat_count)
        .astype(jnp.bfloat16)
    )
    return (output, mixed_local.reshape(1, quota_rows, 2 * feat_count))


def angles(count, places, extent):
    index = np.arange(count)
    waves = np.where(index < count // 2, index, index - count)
    product = (waves[:, None] * np.asarray(places)[None, :]) % extent
    return (np.float32(2.0 * math.pi / extent) * product.astype(np.float32)).astype(np.float64)


def split_table(table):
    high = table.astype(ml_dtypes.bfloat16)
    low = (table - high.astype(np.float64)).astype(ml_dtypes.bfloat16)
    return high, low


def split_terms(values):
    high = values.astype(jnp.bfloat16)
    low = (values - high.astype(jnp.float32)).astype(jnp.bfloat16)
    return high, low


def forward_y_table(cells_y, groups_y, peers, rows_ky):
    extent = cells_y * groups_y
    angle = angles(MY, np.arange(extent), extent).astype(np.float32)
    full = np.stack([np.cos(angle), -np.sin(angle)], axis=1).astype(ml_dtypes.bfloat16)
    full = full.reshape(groups_y, peers, rows_ky, 2, groups_y, cells_y)
    out = np.zeros((groups_y, 2, peers, 2, rows_ky, 2, 2, cells_y), ml_dtypes.bfloat16)
    for place in range(groups_y):
        for side, half in enumerate((1 - place, place)):
            for parity in range(2):
                out[place, side, :, parity, :, :, parity, :] = full[half, :, :, :, place, :]
    return out.reshape(groups_y, 2 * peers * 4 * rows_ky, 2 * cells_y)


def forward_x_table(cells_x, peers, rows_ky):
    extent = cells_x * peers
    angle = angles(MX, np.arange(extent), extent)
    cosine, sine = np.cos(angle), np.sin(angle)
    out = np.zeros((2, rows_ky, MX, extent, rows_ky, 2))
    for row in range(rows_ky):
        out[0, row, :, :, row, 0] = cosine
        out[0, row, :, :, row, 1] = sine
        out[1, row, :, :, row, 1] = cosine
        out[1, row, :, :, row, 0] = -sine
    return out.reshape(2 * rows_ky * MX, extent * rows_ky * 2)


def inverse_x_table(cells_x, peers, rows_ky):
    extent = cells_x * peers
    angle = angles(MX, np.arange(extent), extent)
    cosine, sine = np.cos(angle).T, np.sin(angle).T
    out = np.zeros((extent, rows_ky, 2, 2, rows_ky, MX))
    for row in range(rows_ky):
        out[:, row, 0, 0, row, :] = cosine
        out[:, row, 0, 1, row, :] = -sine
        out[:, row, 1, 1, row, :] = cosine
        out[:, row, 1, 0, row, :] = sine
    return out.reshape(extent * rows_ky * 2, 2 * rows_ky * MX)


def inverse_y_table(cells_y, groups_y, peers, rows_ky):
    extent = cells_y * groups_y
    angle = angles(MY, np.arange(extent), extent)
    full = np.stack([np.cos(angle), -np.sin(angle)], axis=1)
    full = full.reshape(groups_y, peers, rows_ky, 2, groups_y, cells_y)
    out = np.zeros((groups_y, 2, cells_y, 2, peers, 2, rows_ky, 2))
    for place in range(groups_y):
        for side, half in enumerate((place, 1 - place)):
            block = np.moveaxis(full[half, :, :, :, place, :], -1, 0)
            for parity in range(2):
                out[place, parity, :, side, :, parity] = block
    return out.reshape(groups_y, 2, cells_y, 2 * peers * 4 * rows_ky)


def dot(left, right):
    return jnp.dot(left, right, preferred_element_type=jnp.float32)


def forward_y_kernel(flow_ref, table_ref, send_ref, keep_ref):
    table = table_ref[lax.axis_index("gy")]
    pairs, cells_y, feat_count = flow_ref.shape
    result = dot(table, flow_ref[...].reshape(pairs * cells_y, feat_count))
    result = result.reshape((2,) + send_ref.shape)
    send_ref[...] = result[0]
    keep_ref[...] = result[1]


def forward_y(flow_field, table, peers, rows_ky):
    cells_x, cells_y, feat_count = flow_field.shape
    rows = 4 * rows_ky
    shape = jax.ShapeDtypeStruct((peers, cells_x // 2 * rows, feat_count), jnp.float32)
    spec = pl.BlockSpec((peers, rows, feat_count), lambda i: (0, i, 0))
    return pl.pallas_call(
        forward_y_kernel,
        grid=(cells_x // 2,),
        in_specs=[
            pl.BlockSpec((2, cells_y, feat_count), lambda i: (i, 0, 0)),
            pl.BlockSpec(table.shape, lambda i: (0, 0, 0)),
        ],
        out_specs=[spec, spec],
        out_shape=[shape, shape],
        name="forward_y",
    )(flow_field, table)


def mix_kernel(
    modes_ref, weight_ref, forward_high, forward_low, inverse_high, inverse_low,
    mixed_ref, back_ref, spread_ref, result_ref,
):
    feat_count = modes_ref.shape[-1]
    count = weight_ref.shape[1]
    channels = weight_ref.shape[2]
    tiles = feat_count // 128
    group = 2 * tiles
    high, low = split_terms(modes_ref[...].reshape(-1, feat_count))
    spectrum = (
        dot(forward_high[...], high) + dot(forward_high[...], low) + dot(forward_low[...], high)
    )
    for part in range(2):
        for tile in range(tiles):
            spread_ref[pl.ds(part * tiles + tile, count, stride=group), :] = spectrum[
                part * count : (part + 1) * count, tile * 128 : (tile + 1) * 128
            ]
    lane = lax.broadcasted_iota(jnp.int32, (group, 128), 1) < channels
    sign = jnp.where(lax.broadcasted_iota(jnp.int32, (group, 128), 0) < tiles, -1.0, 1.0)
    for mode in range(count):
        block = spread_ref[mode * group : (mode + 1) * group, :]
        turned = pltpu.roll(block, channels, 1)
        left = jnp.concatenate([block, turned], axis=0)[:, :channels]
        left_high, left_low = split_terms(left)
        product = dot(jnp.concatenate([left_high, left_low], axis=0), weight_ref[0, mode])
        product = product[: 2 * group] + product[2 * group :]
        first, second = product[:group], product[group:]
        real = jnp.where(lane, first, pltpu.roll(second, channels, 1))
        imag = jnp.where(lane, pltpu.roll(first, channels, 1), second)
        result_ref[mode * group : (mode + 1) * group, :] = real + sign * pltpu.roll(imag, tiles, 0)
    parts = []
    for part in range(2):
        parts.append(
            jnp.concatenate(
                [
                    result_ref[pl.ds(part * tiles + tile, count, stride=group), :]
                    for tile in range(tiles)
                ],
                axis=1,
            )
        )
        mixed_ref[0, :, part * feat_count : (part + 1) * feat_count] = parts[part]
    high, low = split_terms(jnp.concatenate(parts, axis=0))
    back = dot(inverse_high[...], high) + dot(inverse_high[...], low) + dot(inverse_low[...], high)
    back_ref[...] = back.reshape(back_ref.shape)


def mix(modes, weights, forward_table, inverse_table):
    feat_count = modes.shape[-1]
    count = weights.shape[1]
    scratch = pltpu.VMEM((count * feat_count // 64, 128), jnp.float32)
    return pl.pallas_call(
        mix_kernel,
        out_shape=[
            jax.ShapeDtypeStruct((1, count, 2 * feat_count), jnp.float32),
            jax.ShapeDtypeStruct(modes.shape, jnp.float32),
        ],
        scratch_shapes=[scratch, scratch],
        name="mix",
    )(modes, weights, *split_table(forward_table), *split_table(inverse_table))


def output_kernel(place_ref, flow_ref, own_ref, other_ref, table_ref, local_ref, bias_ref, out_ref):
    step = pl.program_id(0)
    rows = table_ref.shape[-1] // 3 // 2 // own_ref.shape[0]
    feat_count = flow_ref.shape[-1]
    pair = pl.ds(pl.multiple_of(step // 2 * rows, rows), rows)
    both = jnp.concatenate([own_ref[:, pair, :], other_ref[:, pair, :]], axis=0)
    high, low = split_terms(both.reshape(-1, feat_count))
    stacked = jnp.concatenate([high, low, high], axis=0)
    table = table_ref[0, step % 2]
    width = local_ref.shape[0]
    for start in range(0, feat_count, width):
        columns = slice(start, start + width)
        total = (
            dot(table, stacked[:, columns])
            + dot(flow_ref[0, :, columns], local_ref[...])
            + bias_ref[:, columns]
        )
        out_ref[0, :, columns] = (
            0.5 * total * (1.0 + lax.erf(total * math.sqrt(0.5)))
        ).astype(out_ref.dtype)


def make_output(flow_field, own, other, table, local, bias):
    cells_x, cells_y, feat_count = flow_field.shape
    place = jnp.reshape(lax.axis_index("gy"), (1,))
    whole = lambda array: pl.BlockSpec(array.shape, lambda i, p: (0,) * array.ndim)
    block = pl.BlockSpec((1, cells_y, feat_count), lambda i, p: (i, 0, 0))
    return pl.pallas_call(
        output_kernel,
        grid_spec=pltpu.PrefetchScalarGridSpec(
            num_scalar_prefetch=1,
            grid=(cells_x,),
            in_specs=[
                block,
                whole(own),
                whole(other),
                pl.BlockSpec((1,) + table.shape[1:], lambda i, p: (p[0], 0, 0, 0)),
                whole(local),
                whole(bias),
            ],
            out_specs=block,
        ),
        out_shape=jax.ShapeDtypeStruct(flow_field.shape, jnp.bfloat16),
        name="make_output",
    )(place, flow_field, own, other, table, local, bias)


def row_body(flow_field, spectral_weight, local_weight, bias_terms):
    cells_x, cells_y, feat_count = flow_field.shape
    channels = local_weight.shape[0]
    peers = lax.axis_size("gx")
    groups_y = lax.axis_size("gy")
    rows_ky = MY // groups_y // peers
    forward_scale = 1.0 / math.sqrt(cells_x * peers * cells_y * groups_y)
    inverse_scale = 1.0 / math.sqrt(MX * MY)
    swap = [(0, 1), (1, 0)]

    send, keep = forward_y(
        flow_field, forward_y_table(cells_y, groups_y, peers, rows_ky), peers, rows_ky
    )
    modes = keep + lax.ppermute(send, "gy", swap)
    modes = lax.all_to_all(modes, "gx", 0, 0, tiled=True)
    mixed, back = mix(
        modes,
        spectral_weight,
        forward_x_table(cells_x, peers, rows_ky) * forward_scale,
        inverse_x_table(cells_x, peers, rows_ky),
    )
    own = lax.all_to_all(back, "gx", 0, 0, tiled=True)
    other = lax.ppermute(own, "gy", swap)
    high, low = split_table(inverse_y_table(cells_y, groups_y, peers, rows_ky) * inverse_scale)
    copies = 256 // channels
    local = jnp.einsum("ij,co->icjo", jnp.eye(copies, dtype=local_weight.dtype), local_weight)
    output = make_output(
        flow_field,
        own,
        other,
        np.concatenate([high, high, low], axis=-1),
        local.reshape(copies * channels, copies * channels),
        jnp.tile(bias_terms, feat_count // channels)[None, :],
    )
    return output, mixed


def body(flow_field, spectral_weight, local_weight, bias_terms):
    whole_rows = spectral_weight.shape[1] % MX == 0
    if whole_rows and lax.axis_size("gy") == 2 and spectral_weight.shape[1] == 2 * MX:
        return row_body(flow_field, spectral_weight, local_weight, bias_terms)
    return general_body(flow_field, spectral_weight, local_weight, bias_terms)


def solution(mesh):
    placed = (P(("group", "gx"), "gy", None), P("gy", "gx", None, None), P(), P())
    return jax.shard_map(
        body,
        mesh=mesh,
        in_specs=placed,
        out_specs=(P(("group", "gx"), "gy", None), P(("group", "gy"), "gx", None)),
        check_vma=False,
    )
```

```python
import functools
import math

import jax
import jax.numpy as jnp
import ml_dtypes
import numpy as np
from jax import lax
from jax.experimental import pallas as pl
from jax.experimental.pallas import tpu as pltpu
from jax.sharding import PartitionSpec as P

MX = 32
MY = 32


def wave_number(index, count):
    return jnp.where(index < count // 2, index, index - count)


def phase_table(waves, places, extent):
    product = waves[:, None] * places[None, :] % extent
    return 2.0 * math.pi / extent * product.astype(jnp.float32)


def row_tables(ky_rows, kx_rows, x_places, extent, width):
    angle = phase_table(wave_number(kx_rows, MX), x_places, extent)
    select = (ky_rows[:, None] == jnp.arange(width, dtype=jnp.int32)[None, :]).astype(jnp.float32)
    cosine = jnp.cos(angle)[:, :, None] * select[:, None, :]
    sine_part = jnp.sin(angle)[:, :, None] * select[:, None, :]
    return (cosine, sine_part)


def forward_rows(y_local, ky_rows, kx_rows, x_places, extent):
    cosine, sine_part = row_tables(ky_rows, kx_rows, x_places, extent, y_local.shape[0])
    real_in = y_local[:, 0]
    imag_in = y_local[:, 1]

    def contract(table, values):
        return jnp.einsum("rxk,kxf->rf", table, values, precision=lax.Precision.HIGHEST)

    real_out = contract(cosine, real_in) + contract(sine_part, imag_in)
    imag_out = contract(cosine, imag_in) - contract(sine_part, real_in)
    return jnp.concatenate([real_out, imag_out], axis=1)


def inverse_rows(running, shard_rows, ky_rows, kx_rows, x_places, extent):
    cosine, sine_part = row_tables(ky_rows, kx_rows, x_places, extent, running.shape[0])
    feat_count = shard_rows.shape[1] // 2
    real_part = shard_rows[:, :feat_count]
    imag_part = shard_rows[:, feat_count:]

    def contract(table, values):
        return jnp.einsum("rxk,rf->kxf", table, values, precision=lax.Precision.HIGHEST)

    new_real = contract(cosine, real_part) - contract(sine_part, imag_part)
    new_imag = contract(cosine, imag_part) + contract(sine_part, real_part)
    return jnp.stack([new_real, new_imag], axis=1)


def general_body(flow_field, spectral_weight, local_weight, bias_terms):
    cells_x, cells_y, feat_count = flow_field.shape
    channels = local_weight.shape[0]
    planes = feat_count // channels
    groups_x = lax.axis_size("gx")
    groups_y = lax.axis_size("gy")
    extent_x = cells_x * groups_x
    extent_y = cells_y * groups_y
    half_width = MY // groups_y
    quota_rows = spectral_weight.shape[1]
    high = lax.Precision.HIGHEST
    x_places = lax.axis_index("gx") * cells_x + jnp.arange(cells_x, dtype=jnp.int32)
    y_places = lax.axis_index("gy") * cells_y + jnp.arange(cells_y, dtype=jnp.int32)
    y_angle = phase_table(wave_number(jnp.arange(MY, dtype=jnp.int32), MY), y_places, extent_y)
    y_table = (
        jnp.stack([jnp.cos(y_angle), -jnp.sin(y_angle)], axis=1)
        .reshape(2 * MY, cells_y)
        .astype(jnp.bfloat16)
    )
    y_local = lax.psum_scatter(
        jnp.einsum("qy,xyf->qxf", y_table, flow_field, preferred_element_type=jnp.float32),
        "gy",
        scatter_dimension=0,
        tiled=True,
    )
    y_local = y_local.reshape(half_width, 2, cells_x, feat_count)
    rest_index = jnp.arange(lax.axis_size("gx") * quota_rows, dtype=jnp.int32)
    spectrum = lax.psum_scatter(
        forward_rows(y_local, rest_index // MX, rest_index % MX, x_places, extent_x),
        "gx",
        scatter_dimension=0,
        tiled=True,
    )
    spectrum = spectrum * (1.0 / math.sqrt(extent_x * extent_y))
    coeffs = spectrum.reshape(quota_rows, 2, planes, channels)
    weights = spectral_weight[0].astype(jnp.float32)
    product = jnp.einsum("rpzc,rco->rpzo", coeffs, weights, precision=high)
    mixed_real = product[:, 0, :, :channels] - product[:, 1, :, channels:]
    mixed_imag = product[:, 0, :, channels:] + product[:, 1, :, :channels]
    mixed_local = jnp.stack([mixed_real, mixed_imag], axis=1).reshape(quota_rows, 2 * feat_count)
    pointwise = jnp.einsum(
        "xyzc,co->xyzo",
        flow_field.reshape(cells_x, cells_y, planes, channels),
        local_weight,
        preferred_element_type=jnp.float32,
    )
    start_half = jnp.zeros((half_width, 2, cells_x, feat_count), jnp.float32)
    shard_rows = lax.all_gather(mixed_local, "gx", axis=0, tiled=True)
    rest_index = jnp.arange(shard_rows.shape[0], dtype=jnp.int32)
    back_half = inverse_rows(
        start_half, shard_rows, rest_index // MX, rest_index % MX, x_places, extent_x
    )
    back_whole = lax.all_gather(back_half, "gy", axis=0, tiled=True)
    y_cos = jnp.cos(y_angle)
    y_sin = jnp.sin(y_angle)
    spectral = (
        jnp.einsum("kn,kxf->xnf", y_cos, back_whole[:, 0], precision=high)
        - jnp.einsum("kn,kxf->xnf", y_sin, back_whole[:, 1], precision=high)
    ) * (1.0 / math.sqrt(MX * MY))
    total = spectral.reshape(cells_x, cells_y, planes, channels) + pointwise + bias_terms
    output = (
        jax.nn.gelu(total, approximate=False)
        .reshape(cells_x, cells_y, feat_count)
        .astype(jnp.bfloat16)
    )
    return (output, mixed_local.reshape(1, quota_rows, 2 * feat_count))


SMALL = pltpu.CompilerParams(vmem_limit_bytes=20 * 1024 * 1024)


def angles(count, places, extent):
    index = np.arange(count)
    waves = np.where(index < count // 2, index, index - count)
    product = (waves[:, None] * np.asarray(places)[None, :]) % extent
    return (np.float32(2.0 * math.pi / extent) * product.astype(np.float32)).astype(np.float64)


def split_table(table):
    high = table.astype(ml_dtypes.bfloat16)
    low = (table - high.astype(np.float64)).astype(ml_dtypes.bfloat16)
    return high, low


def split_terms(values):
    high = values.astype(jnp.bfloat16)
    low = (values - high.astype(jnp.float32)).astype(jnp.bfloat16)
    return high, low


def forward_y_table(cells_y, groups_y, peers, rows_ky):
    extent = cells_y * groups_y
    angle = angles(MY, np.arange(extent), extent).astype(np.float32)
    full = np.stack([np.cos(angle), -np.sin(angle)], axis=1).astype(ml_dtypes.bfloat16)
    full = full.reshape(groups_y, peers, rows_ky, 2, groups_y, cells_y)
    out = np.zeros((groups_y, 2, peers, 2, rows_ky, 2, 2, cells_y), ml_dtypes.bfloat16)
    for place in range(groups_y):
        for side, half in enumerate((1 - place, place)):
            for parity in range(2):
                out[place, side, :, parity, :, :, parity, :] = full[half, :, :, :, place, :]
    return out.reshape(groups_y, 2 * peers * 4 * rows_ky, 2 * cells_y)


def forward_x_table(cells_x, peers, rows_ky):
    extent = cells_x * peers
    angle = angles(MX, np.arange(extent), extent)
    cosine, sine = np.cos(angle), np.sin(angle)
    out = np.zeros((2, rows_ky, MX, extent, rows_ky, 2))
    for row in range(rows_ky):
        out[0, row, :, :, row, 0] = cosine
        out[0, row, :, :, row, 1] = sine
        out[1, row, :, :, row, 1] = cosine
        out[1, row, :, :, row, 0] = -sine
    return out.reshape(2 * rows_ky * MX, extent * rows_ky * 2)


def inverse_x_table(cells_x, peers, rows_ky):
    extent = cells_x * peers
    angle = angles(MX, np.arange(extent), extent)
    cosine, sine = np.cos(angle).T, np.sin(angle).T
    out = np.zeros((extent, rows_ky, 2, 2, rows_ky, MX))
    for row in range(rows_ky):
        out[:, row, 0, 0, row, :] = cosine
        out[:, row, 0, 1, row, :] = -sine
        out[:, row, 1, 1, row, :] = cosine
        out[:, row, 1, 0, row, :] = sine
    return out.reshape(extent * rows_ky * 2, 2 * rows_ky * MX)


def inverse_y_table(cells_y, groups_y, peers, rows_ky):
    extent = cells_y * groups_y
    angle = angles(MY, np.arange(extent), extent)
    full = np.stack([np.cos(angle), -np.sin(angle)], axis=1)
    full = full.reshape(groups_y, peers, rows_ky, 2, groups_y, cells_y)
    out = np.zeros((groups_y, 2, cells_y, 2, peers, 2, rows_ky, 2))
    for place in range(groups_y):
        for side, half in enumerate((place, 1 - place)):
            block = np.moveaxis(full[half, :, :, :, place, :], -1, 0)
            for parity in range(2):
                out[place, parity, :, side, :, parity] = block
    return out.reshape(groups_y, 2, cells_y, 2 * peers * 4 * rows_ky)


def dot(left, right):
    return jnp.dot(left, right, preferred_element_type=jnp.float32)


def forward_y_kernel(flow_ref, table_ref, send_ref, keep_ref):
    table = table_ref[lax.axis_index("gy")]
    pairs, cells_y, feat_count = flow_ref.shape
    result = dot(table, flow_ref[...].reshape(pairs * cells_y, feat_count))
    result = result.reshape((2,) + send_ref.shape)
    send_ref[...] = result[0]
    keep_ref[...] = result[1]


def forward_y(flow_field, table, peers, rows_ky):
    cells_x, cells_y, feat_count = flow_field.shape
    rows = 4 * rows_ky
    shape = jax.ShapeDtypeStruct((peers, cells_x // 2 * rows, feat_count), jnp.float32)
    spec = pl.BlockSpec((peers, rows, feat_count), lambda i: (0, i, 0))
    return pl.pallas_call(
        forward_y_kernel,
        grid=(cells_x // 2,),
        in_specs=[
            pl.BlockSpec((2, cells_y, feat_count), lambda i: (i, 0, 0)),
            pl.BlockSpec(table.shape, lambda i: (0, 0, 0)),
        ],
        out_specs=[spec, spec],
        out_shape=[shape, shape],
        compiler_params=SMALL,
        name="forward_y",
    )(flow_field, table)


def combine_kernel(keep_ref, arrived_ref, *out_refs):
    me = lax.axis_index("gx")
    for step, out_ref in enumerate(out_refs):
        out_ref[...] = keep_ref[me ^ step] + arrived_ref[me ^ step]


def combine(keep, arrived):
    peers = keep.shape[0]
    return pl.pallas_call(
        combine_kernel,
        out_shape=[jax.ShapeDtypeStruct(keep.shape[1:], keep.dtype)] * peers,
        compiler_params=SMALL,
        name="combine",
    )(keep, arrived)


def exchange(blocks):
    peers = len(blocks)
    arrived = [blocks[0]]
    for step in range(1, peers):
        pairs = [(place, place ^ step) for place in range(peers)]
        arrived.append(lax.ppermute(blocks[step], "gx", pairs))
    return arrived


def mix_kernel(peers, *refs):
    block_refs = refs[:peers]
    weight_ref, forward_high, forward_low, inverse_high, inverse_low, mixed_ref = refs[
        peers : peers + 6
    ]
    back_refs = refs[peers + 6 : 2 * peers + 6]
    order_ref, spread_ref, result_ref = refs[2 * peers + 6 :]
    me = lax.axis_index("gx")
    feat_count = order_ref.shape[-1]
    count = weight_ref.shape[1]
    channels = weight_ref.shape[2]
    tiles = feat_count // 128
    group = 2 * tiles
    for step in range(peers):
        order_ref[me ^ step] = block_refs[step][...]
    high, low = split_terms(order_ref[...].reshape(-1, feat_count))
    spectrum = (
        dot(forward_high[...], high) + dot(forward_high[...], low) + dot(forward_low[...], high)
    )
    for part in range(2):
        for tile in range(tiles):
            spread_ref[pl.ds(part * tiles + tile, count, stride=group), :] = spectrum[
                part * count : (part + 1) * count, tile * 128 : (tile + 1) * 128
            ]
    lane = lax.broadcasted_iota(jnp.int32, (group, 128), 1) < channels
    sign = jnp.where(lax.broadcasted_iota(jnp.int32, (group, 128), 0) < tiles, -1.0, 1.0)
    for mode in range(count):
        block = spread_ref[mode * group : (mode + 1) * group, :]
        turned = pltpu.roll(block, channels, 1)
        left = jnp.concatenate([block, turned], axis=0)[:, :channels]
        left_high, left_low = split_terms(left)
        product = dot(jnp.concatenate([left_high, left_low], axis=0), weight_ref[0, mode])
        product = product[: 2 * group] + product[2 * group :]
        first, second = product[:group], product[group:]
        real = jnp.where(lane, first, pltpu.roll(second, channels, 1))
        imag = jnp.where(lane, pltpu.roll(first, channels, 1), second)
        result_ref[mode * group : (mode + 1) * group, :] = real + sign * pltpu.roll(imag, tiles, 0)
    parts = []
    for part in range(2):
        parts.append(
            jnp.concatenate(
                [
                    result_ref[pl.ds(part * tiles + tile, count, stride=group), :]
                    for tile in range(tiles)
                ],
                axis=1,
            )
        )
        mixed_ref[0, :, part * feat_count : (part + 1) * feat_count] = parts[part]
    high, low = split_terms(jnp.concatenate(parts, axis=0))
    back = dot(inverse_high[...], high) + dot(inverse_high[...], low) + dot(inverse_low[...], high)
    order_ref[...] = back.reshape(order_ref.shape)
    for step in range(peers):
        back_refs[step][...] = order_ref[me ^ step]


def mix(blocks, weights, forward_table, inverse_table):
    rows, feat_count = blocks[0].shape
    peers = len(blocks)
    count = weights.shape[1]
    scratch = pltpu.VMEM((count * feat_count // 64, 128), jnp.float32)
    mixed, *back = pl.pallas_call(
        functools.partial(mix_kernel, peers),
        out_shape=[jax.ShapeDtypeStruct((1, count, 2 * feat_count), jnp.float32)]
        + [jax.ShapeDtypeStruct(blocks[0].shape, jnp.float32)] * peers,
        scratch_shapes=[pltpu.VMEM((peers, rows, feat_count), jnp.float32), scratch, scratch],
        compiler_params=SMALL,
        name="mix",
    )(*blocks, weights, *split_table(forward_table), *split_table(inverse_table))
    return mixed, back


def output_kernel(peers, place_ref, flow_ref, table_ref, local_ref, bias_ref, *refs):
    block_refs = refs[: 2 * peers]
    out_ref, order_ref, stack_ref, wide_ref, level_ref = refs[2 * peers :]
    step = pl.program_id(0)
    feat_count = flow_ref.shape[-1]
    channels = local_ref.shape[0]
    width = wide_ref.shape[0]
    pairs = stack_ref.shape[0]
    rows = order_ref.shape[1] // pairs

    @pl.when(step == 0)
    def _():
        me = lax.axis_index("gx")
        for side in range(2):
            for turn in range(peers):
                order_ref[side * peers + (me ^ turn)] = block_refs[side * peers + turn][...]
        for pair in range(pairs):
            both = order_ref[:, pair * rows : (pair + 1) * rows, :].reshape(-1, feat_count)
            high, low = split_terms(both)
            stack_ref[pair] = jnp.concatenate([high, low, high], axis=0)
        wide_ref[...] = jnp.zeros_like(wide_ref)
        for start in range(0, width, channels):
            span = slice(start, start + channels)
            wide_ref[span, span] = local_ref[...]
        for start in range(0, width, channels):
            level_ref[:, start : start + channels] = bias_ref[...]

    table = table_ref[0, step % 2]
    for start in range(0, feat_count, width):
        columns = slice(start, start + width)
        total = (
            dot(table, stack_ref[step // 2, :, columns])
            + dot(flow_ref[0, :, columns], wide_ref[...])
            + level_ref[...]
        )
        out_ref[0, :, columns] = (
            0.5 * total * (1.0 + lax.erf(total * math.sqrt(0.5)))
        ).astype(out_ref.dtype)


def make_output(flow_field, own, other, table, local, bias):
    cells_x, cells_y, feat_count = flow_field.shape
    peers = len(own)
    rows = own[0].shape[0]
    width = 256
    place = jnp.reshape(lax.axis_index("gy"), (1,))
    whole = lambda array: pl.BlockSpec(array.shape, lambda i, p: (0,) * array.ndim)
    block = pl.BlockSpec((1, cells_y, feat_count), lambda i, p: (i, 0, 0))
    return pl.pallas_call(
        functools.partial(output_kernel, peers),
        grid_spec=pltpu.PrefetchScalarGridSpec(
            num_scalar_prefetch=1,
            grid=(cells_x,),
            in_specs=[
                block,
                pl.BlockSpec((1,) + table.shape[1:], lambda i, p: (p[0], 0, 0, 0)),
                whole(local),
                whole(bias),
            ]
            + [whole(array) for array in own + other],
            out_specs=block,
            scratch_shapes=[
                pltpu.VMEM((2 * peers, rows, feat_count), jnp.float32),
                pltpu.VMEM((cells_x // 2, table.shape[-1], feat_count), jnp.bfloat16),
                pltpu.VMEM((width, width), jnp.bfloat16),
                pltpu.VMEM((1, width), jnp.float32),
            ],
        ),
        out_shape=jax.ShapeDtypeStruct(flow_field.shape, jnp.bfloat16),
        compiler_params=SMALL,
        name="make_output",
    )(place, flow_field, table, local, bias, *own, *other)


def row_body(flow_field, spectral_weight, local_weight, bias_terms):
    cells_x, cells_y, feat_count = flow_field.shape
    peers = lax.axis_size("gx")
    groups_y = lax.axis_size("gy")
    rows_ky = MY // groups_y // peers
    forward_scale = 1.0 / math.sqrt(cells_x * peers * cells_y * groups_y)
    inverse_scale = 1.0 / math.sqrt(MX * MY)
    swap = [(0, 1), (1, 0)]

    send, keep = forward_y(
        flow_field, forward_y_table(cells_y, groups_y, peers, rows_ky), peers, rows_ky
    )
    blocks = exchange(combine(keep, lax.ppermute(send, "gy", swap)))
    mixed, back = mix(
        blocks,
        spectral_weight,
        forward_x_table(cells_x, peers, rows_ky) * forward_scale,
        inverse_x_table(cells_x, peers, rows_ky),
    )
    own = exchange(back)
    other = [lax.ppermute(block, "gy", swap) for block in own]
    high, low = split_table(inverse_y_table(cells_y, groups_y, peers, rows_ky) * inverse_scale)
    output = make_output(
        flow_field,
        own,
        other,
        np.concatenate([high, high, low], axis=-1),
        local_weight,
        bias_terms[None, :],
    )
    return output, mixed


def body(flow_field, spectral_weight, local_weight, bias_terms):
    whole_rows = spectral_weight.shape[1] % MX == 0
    if whole_rows and lax.axis_size("gy") == 2 and spectral_weight.shape[1] == 2 * MX:
        return row_body(flow_field, spectral_weight, local_weight, bias_terms)
    return general_body(flow_field, spectral_weight, local_weight, bias_terms)


def solution(mesh):
    placed = (P(("group", "gx"), "gy", None), P("gy", "gx", None, None), P(), P())
    return jax.shard_map(
        body,
        mesh=mesh,
        in_specs=placed,
        out_specs=(P(("group", "gx"), "gy", None), P(("group", "gy"), "gx", None)),
        check_vma=False,
    )
```

```python
import math

import jax
import jax.numpy as jnp
import ml_dtypes
import numpy as np
from jax import lax
from jax.experimental import pallas as pl
from jax.experimental.pallas import tpu as pltpu
from jax.sharding import PartitionSpec as P

MX = 32
MY = 32


def wave_number(index, count):
    return jnp.where(index < count // 2, index, index - count)


def phase_table(waves, places, extent):
    product = waves[:, None] * places[None, :] % extent
    return 2.0 * math.pi / extent * product.astype(jnp.float32)


def row_tables(ky_rows, kx_rows, x_places, extent, width):
    angle = phase_table(wave_number(kx_rows, MX), x_places, extent)
    select = (ky_rows[:, None] == jnp.arange(width, dtype=jnp.int32)[None, :]).astype(jnp.float32)
    cosine = jnp.cos(angle)[:, :, None] * select[:, None, :]
    sine_part = jnp.sin(angle)[:, :, None] * select[:, None, :]
    return (cosine, sine_part)


def forward_rows(y_local, ky_rows, kx_rows, x_places, extent):
    cosine, sine_part = row_tables(ky_rows, kx_rows, x_places, extent, y_local.shape[0])
    real_in = y_local[:, 0]
    imag_in = y_local[:, 1]

    def contract(table, values):
        return jnp.einsum("rxk,kxf->rf", table, values, precision=lax.Precision.HIGHEST)

    real_out = contract(cosine, real_in) + contract(sine_part, imag_in)
    imag_out = contract(cosine, imag_in) - contract(sine_part, real_in)
    return jnp.concatenate([real_out, imag_out], axis=1)


def inverse_rows(running, shard_rows, ky_rows, kx_rows, x_places, extent):
    cosine, sine_part = row_tables(ky_rows, kx_rows, x_places, extent, running.shape[0])
    feat_count = shard_rows.shape[1] // 2
    real_part = shard_rows[:, :feat_count]
    imag_part = shard_rows[:, feat_count:]

    def contract(table, values):
        return jnp.einsum("rxk,rf->kxf", table, values, precision=lax.Precision.HIGHEST)

    new_real = contract(cosine, real_part) - contract(sine_part, imag_part)
    new_imag = contract(cosine, imag_part) + contract(sine_part, real_part)
    return jnp.stack([new_real, new_imag], axis=1)


def general_body(flow_field, spectral_weight, local_weight, bias_terms):
    cells_x, cells_y, feat_count = flow_field.shape
    channels = local_weight.shape[0]
    planes = feat_count // channels
    groups_x = lax.axis_size("gx")
    groups_y = lax.axis_size("gy")
    extent_x = cells_x * groups_x
    extent_y = cells_y * groups_y
    half_width = MY // groups_y
    quota_rows = spectral_weight.shape[1]
    high = lax.Precision.HIGHEST
    x_places = lax.axis_index("gx") * cells_x + jnp.arange(cells_x, dtype=jnp.int32)
    y_places = lax.axis_index("gy") * cells_y + jnp.arange(cells_y, dtype=jnp.int32)
    y_angle = phase_table(wave_number(jnp.arange(MY, dtype=jnp.int32), MY), y_places, extent_y)
    y_table = (
        jnp.stack([jnp.cos(y_angle), -jnp.sin(y_angle)], axis=1)
        .reshape(2 * MY, cells_y)
        .astype(jnp.bfloat16)
    )
    y_local = lax.psum_scatter(
        jnp.einsum("qy,xyf->qxf", y_table, flow_field, preferred_element_type=jnp.float32),
        "gy",
        scatter_dimension=0,
        tiled=True,
    )
    y_local = y_local.reshape(half_width, 2, cells_x, feat_count)
    rest_index = jnp.arange(lax.axis_size("gx") * quota_rows, dtype=jnp.int32)
    spectrum = lax.psum_scatter(
        forward_rows(y_local, rest_index // MX, rest_index % MX, x_places, extent_x),
        "gx",
        scatter_dimension=0,
        tiled=True,
    )
    spectrum = spectrum * (1.0 / math.sqrt(extent_x * extent_y))
    coeffs = spectrum.reshape(quota_rows, 2, planes, channels)
    weights = spectral_weight[0].astype(jnp.float32)
    product = jnp.einsum("rpzc,rco->rpzo", coeffs, weights, precision=high)
    mixed_real = product[:, 0, :, :channels] - product[:, 1, :, channels:]
    mixed_imag = product[:, 0, :, channels:] + product[:, 1, :, :channels]
    mixed_local = jnp.stack([mixed_real, mixed_imag], axis=1).reshape(quota_rows, 2 * feat_count)
    pointwise = jnp.einsum(
        "xyzc,co->xyzo",
        flow_field.reshape(cells_x, cells_y, planes, channels),
        local_weight,
        preferred_element_type=jnp.float32,
    )
    start_half = jnp.zeros((half_width, 2, cells_x, feat_count), jnp.float32)
    shard_rows = lax.all_gather(mixed_local, "gx", axis=0, tiled=True)
    rest_index = jnp.arange(shard_rows.shape[0], dtype=jnp.int32)
    back_half = inverse_rows(
        start_half, shard_rows, rest_index // MX, rest_index % MX, x_places, extent_x
    )
    back_whole = lax.all_gather(back_half, "gy", axis=0, tiled=True)
    y_cos = jnp.cos(y_angle)
    y_sin = jnp.sin(y_angle)
    spectral = (
        jnp.einsum("kn,kxf->xnf", y_cos, back_whole[:, 0], precision=high)
        - jnp.einsum("kn,kxf->xnf", y_sin, back_whole[:, 1], precision=high)
    ) * (1.0 / math.sqrt(MX * MY))
    total = spectral.reshape(cells_x, cells_y, planes, channels) + pointwise + bias_terms
    output = (
        jax.nn.gelu(total, approximate=False)
        .reshape(cells_x, cells_y, feat_count)
        .astype(jnp.bfloat16)
    )
    return (output, mixed_local.reshape(1, quota_rows, 2 * feat_count))


SMALL = pltpu.CompilerParams(vmem_limit_bytes=20 * 1024 * 1024)


def angles(count, places, extent):
    index = np.arange(count)
    waves = np.where(index < count // 2, index, index - count)
    product = (waves[:, None] * np.asarray(places)[None, :]) % extent
    return (np.float32(2.0 * math.pi / extent) * product.astype(np.float32)).astype(np.float64)


def split_table(table):
    high = table.astype(ml_dtypes.bfloat16)
    low = (table - high.astype(np.float64)).astype(ml_dtypes.bfloat16)
    return high, low


def split_terms(values):
    high = values.astype(jnp.bfloat16)
    low = (values - high.astype(jnp.float32)).astype(jnp.bfloat16)
    return high, low


def forward_y_table(cells_y, groups_y, peers, rows_ky):
    extent = cells_y * groups_y
    angle = angles(MY, np.arange(extent), extent).astype(np.float32)
    full = np.stack([np.cos(angle), -np.sin(angle)], axis=1).astype(ml_dtypes.bfloat16)
    full = full.reshape(groups_y, peers, rows_ky, 2, groups_y, cells_y)
    out = np.zeros((groups_y, 2, peers, 2, rows_ky, 2, 2, cells_y), ml_dtypes.bfloat16)
    for place in range(groups_y):
        for side, half in enumerate((1 - place, place)):
            for parity in range(2):
                out[place, side, :, parity, :, :, parity, :] = full[half, :, :, :, place, :]
    return out.reshape(groups_y, 2 * peers * 4 * rows_ky, 2 * cells_y)


def forward_x_table(cells_x, peers, rows_ky):
    extent = cells_x * peers
    angle = angles(MX, np.arange(extent), extent)
    cosine, sine = np.cos(angle), np.sin(angle)
    out = np.zeros((2, rows_ky, MX, extent, rows_ky, 2))
    for row in range(rows_ky):
        out[0, row, :, :, row, 0] = cosine
        out[0, row, :, :, row, 1] = sine
        out[1, row, :, :, row, 1] = cosine
        out[1, row, :, :, row, 0] = -sine
    return out.reshape(2 * rows_ky * MX, extent * rows_ky * 2)


def inverse_x_table(cells_x, peers, rows_ky):
    extent = cells_x * peers
    angle = angles(MX, np.arange(extent), extent)
    cosine, sine = np.cos(angle).T, np.sin(angle).T
    out = np.zeros((extent, rows_ky, 2, 2, rows_ky, MX))
    for row in range(rows_ky):
        out[:, row, 0, 0, row, :] = cosine
        out[:, row, 0, 1, row, :] = -sine
        out[:, row, 1, 1, row, :] = cosine
        out[:, row, 1, 0, row, :] = sine
    return out.reshape(extent * rows_ky * 2, 2 * rows_ky * MX)


def inverse_y_table(cells_y, groups_y, peers, rows_ky):
    extent = cells_y * groups_y
    angle = angles(MY, np.arange(extent), extent)
    full = np.stack([np.cos(angle), -np.sin(angle)], axis=1)
    full = full.reshape(groups_y, peers, rows_ky, 2, groups_y, cells_y)
    out = np.zeros((groups_y, 2, cells_y, 2, peers, 2, rows_ky, 2))
    for place in range(groups_y):
        for side, half in enumerate((place, 1 - place)):
            block = np.moveaxis(full[half, :, :, :, place, :], -1, 0)
            for parity in range(2):
                out[place, parity, :, side, :, parity] = block
    return out.reshape(groups_y, 2, cells_y, 2 * peers * 4 * rows_ky)


def dot(left, right):
    return jnp.dot(left, right, preferred_element_type=jnp.float32)


def forward_y_kernel(flow_hbm, table_hbm, send_ref, keep_ref, flow_ref, table_ref, arrivals):
    cells_x, cells_y, feat_count = flow_ref.shape
    rows = table_ref.shape[0] // 2 // send_ref.shape[0]
    table_copy = pltpu.make_async_copy(
        table_hbm.at[lax.axis_index("gy")], table_ref, arrivals.at[cells_x]
    )
    table_copy.start()
    copies = []
    for x in range(cells_x):
        copies.append(pltpu.make_async_copy(flow_hbm.at[x], flow_ref.at[x], arrivals.at[x]))
        copies[x].start()
    table_copy.wait()
    for pair in range(cells_x // 2):
        copies[2 * pair].wait()
        copies[2 * pair + 1].wait()
        flow = flow_ref[2 * pair : 2 * pair + 2].reshape(2 * cells_y, feat_count)
        result = dot(table_ref[...], flow).reshape(2, send_ref.shape[0], rows, feat_count)
        send_ref[:, pair * rows : (pair + 1) * rows, :] = result[0]
        keep_ref[:, pair * rows : (pair + 1) * rows, :] = result[1]


def forward_y(flow_field, table, peers, rows_ky):
    cells_x, cells_y, feat_count = flow_field.shape
    shape = jax.ShapeDtypeStruct((peers, cells_x * 2 * rows_ky, feat_count), jnp.float32)
    spec = pl.BlockSpec(memory_space=pltpu.VMEM)
    source = pl.BlockSpec(memory_space=pltpu.HBM)
    return pl.pallas_call(
        forward_y_kernel,
        in_specs=[source, source],
        out_specs=[spec, spec],
        out_shape=[shape, shape],
        scratch_shapes=[
            pltpu.VMEM(flow_field.shape, flow_field.dtype),
            pltpu.VMEM(table.shape[1:], table.dtype),
            pltpu.SemaphoreType.DMA((cells_x + 1,)),
        ],
        compiler_params=SMALL,
        name="forward_y",
    )(flow_field, table)


def mix_kernel(
    modes_ref, weight_ref, forward_high, forward_low, inverse_high, inverse_low,
    mixed_ref, back_ref, spread_ref, result_ref,
):
    feat_count = modes_ref.shape[-1]
    count = weight_ref.shape[1]
    channels = weight_ref.shape[2]
    tiles = feat_count // 128
    group = 2 * tiles
    high, low = split_terms(modes_ref[...].reshape(-1, feat_count))
    spectrum = (
        dot(forward_high[...], high) + dot(forward_high[...], low) + dot(forward_low[...], high)
    )
    for part in range(2):
        for tile in range(tiles):
            spread_ref[pl.ds(part * tiles + tile, count, stride=group), :] = spectrum[
                part * count : (part + 1) * count, tile * 128 : (tile + 1) * 128
            ]
    lane = lax.broadcasted_iota(jnp.int32, (group, 128), 1) < channels
    sign = jnp.where(lax.broadcasted_iota(jnp.int32, (group, 128), 0) < tiles, -1.0, 1.0)
    for mode in range(count):
        block = spread_ref[mode * group : (mode + 1) * group, :]
        turned = pltpu.roll(block, channels, 1)
        left = jnp.concatenate([block, turned], axis=0)[:, :channels]
        left_high, left_low = split_terms(left)
        product = dot(jnp.concatenate([left_high, left_low], axis=0), weight_ref[0, mode])
        product = product[: 2 * group] + product[2 * group :]
        first, second = product[:group], product[group:]
        real = jnp.where(lane, first, pltpu.roll(second, channels, 1))
        imag = jnp.where(lane, pltpu.roll(first, channels, 1), second)
        result_ref[mode * group : (mode + 1) * group, :] = real + sign * pltpu.roll(imag, tiles, 0)
    parts = []
    for part in range(2):
        parts.append(
            jnp.concatenate(
                [
                    result_ref[pl.ds(part * tiles + tile, count, stride=group), :]
                    for tile in range(tiles)
                ],
                axis=1,
            )
        )
        mixed_ref[0, :, part * feat_count : (part + 1) * feat_count] = parts[part]
    high, low = split_terms(jnp.concatenate(parts, axis=0))
    back = dot(inverse_high[...], high) + dot(inverse_high[...], low) + dot(inverse_low[...], high)
    back_ref[...] = back.reshape(back_ref.shape)


def mix(modes, weights, forward_table, inverse_table):
    feat_count = modes.shape[-1]
    count = weights.shape[1]
    scratch = pltpu.VMEM((count * feat_count // 64, 128), jnp.float32)
    return pl.pallas_call(
        mix_kernel,
        out_shape=[
            jax.ShapeDtypeStruct((1, count, 2 * feat_count), jnp.float32),
            jax.ShapeDtypeStruct(modes.shape, jnp.float32),
        ],
        scratch_shapes=[scratch, scratch],
        compiler_params=SMALL,
        name="mix",
    )(modes, weights, *split_table(forward_table), *split_table(inverse_table))


def output_kernel(
    place_ref, flow_ref, table_ref, local_ref, bias_ref, own_ref, other_ref,
    out_ref, stack_ref, wide_ref, level_ref,
):
    step = pl.program_id(0)
    feat_count = flow_ref.shape[-1]
    channels = local_ref.shape[0]
    width = wide_ref.shape[0]
    pairs = stack_ref.shape[0]
    rows = own_ref.shape[1] // pairs

    @pl.when(step == 0)
    def _():
        for pair in range(pairs):
            span = slice(pair * rows, (pair + 1) * rows)
            both = jnp.concatenate([own_ref[:, span, :], other_ref[:, span, :]], axis=0)
            high, low = split_terms(both.reshape(-1, feat_count))
            stack_ref[pair] = jnp.concatenate([high, low, high], axis=0)
        wide_ref[...] = jnp.zeros_like(wide_ref)
        for start in range(0, width, channels):
            span = slice(start, start + channels)
            wide_ref[span, span] = local_ref[...]
            level_ref[:, span] = bias_ref[...]

    table = table_ref[0, step % 2]
    for start in range(0, feat_count, width):
        columns = slice(start, start + width)
        total = (
            dot(table, stack_ref[step // 2, :, columns])
            + dot(flow_ref[0, :, columns], wide_ref[...])
            + level_ref[...]
        )
        out_ref[0, :, columns] = (
            0.5 * total * (1.0 + lax.erf(total * math.sqrt(0.5)))
        ).astype(out_ref.dtype)


def make_output(flow_field, own, other, table, local, bias):
    cells_x, cells_y, feat_count = flow_field.shape
    width = 256
    place = jnp.reshape(lax.axis_index("gy"), (1,))
    whole = lambda array: pl.BlockSpec(array.shape, lambda i, p: (0,) * array.ndim)
    block = pl.BlockSpec((1, cells_y, feat_count), lambda i, p: (i, 0, 0))
    return pl.pallas_call(
        output_kernel,
        grid_spec=pltpu.PrefetchScalarGridSpec(
            num_scalar_prefetch=1,
            grid=(cells_x,),
            in_specs=[
                block,
                pl.BlockSpec((1,) + table.shape[1:], lambda i, p: (p[0], 0, 0, 0)),
                whole(local),
                whole(bias),
                whole(own),
                whole(other),
            ],
            out_specs=block,
            scratch_shapes=[
                pltpu.VMEM((cells_x // 2, table.shape[-1], feat_count), jnp.bfloat16),
                pltpu.VMEM((width, width), jnp.bfloat16),
                pltpu.VMEM((1, width), jnp.float32),
            ],
        ),
        out_shape=jax.ShapeDtypeStruct(flow_field.shape, jnp.bfloat16),
        compiler_params=SMALL,
        name="make_output",
    )(place, flow_field, table, local, bias, own, other)


def row_body(flow_field, spectral_weight, local_weight, bias_terms):
    cells_x, cells_y, feat_count = flow_field.shape
    peers = lax.axis_size("gx")
    groups_y = lax.axis_size("gy")
    rows_ky = MY // groups_y // peers
    forward_scale = 1.0 / math.sqrt(cells_x * peers * cells_y * groups_y)
    inverse_scale = 1.0 / math.sqrt(MX * MY)
    swap = [(0, 1), (1, 0)]

    send, keep = forward_y(
        flow_field, forward_y_table(cells_y, groups_y, peers, rows_ky), peers, rows_ky
    )
    modes = keep + lax.ppermute(send, "gy", swap)
    mixed, back = mix(
        lax.all_to_all(modes, "gx", 0, 0, tiled=True),
        spectral_weight,
        forward_x_table(cells_x, peers, rows_ky) * forward_scale,
        inverse_x_table(cells_x, peers, rows_ky),
    )
    own = lax.all_to_all(back, "gx", 0, 0, tiled=True)
    other = lax.ppermute(own, "gy", swap)
    high, low = split_table(inverse_y_table(cells_y, groups_y, peers, rows_ky) * inverse_scale)
    output = make_output(
        flow_field,
        own,
        other,
        np.concatenate([high, high, low], axis=-1),
        local_weight,
        bias_terms[None, :],
    )
    return output, mixed


def body(flow_field, spectral_weight, local_weight, bias_terms):
    whole_rows = spectral_weight.shape[1] % MX == 0
    if whole_rows and lax.axis_size("gy") == 2 and spectral_weight.shape[1] == 2 * MX:
        return row_body(flow_field, spectral_weight, local_weight, bias_terms)
    return general_body(flow_field, spectral_weight, local_weight, bias_terms)


def solution(mesh):
    placed = (P(("group", "gx"), "gy", None), P("gy", "gx", None, None), P(), P())
    return jax.shard_map(
        body,
        mesh=mesh,
        in_specs=placed,
        out_specs=(P(("group", "gx"), "gy", None), P(("group", "gy"), "gx", None)),
        check_vma=False,
    )
```

```python
import functools
import math

import jax
import jax.numpy as jnp
import ml_dtypes
import numpy as np
from jax import lax
from jax.experimental import pallas as pl
from jax.experimental.pallas import tpu as pltpu
from jax.sharding import PartitionSpec as P

MX = 32
MY = 32


def wave_number(index, count):
    return jnp.where(index < count // 2, index, index - count)


def phase_table(waves, places, extent):
    product = waves[:, None] * places[None, :] % extent
    return 2.0 * math.pi / extent * product.astype(jnp.float32)


def row_tables(ky_rows, kx_rows, x_places, extent, width):
    angle = phase_table(wave_number(kx_rows, MX), x_places, extent)
    select = (ky_rows[:, None] == jnp.arange(width, dtype=jnp.int32)[None, :]).astype(jnp.float32)
    cosine = jnp.cos(angle)[:, :, None] * select[:, None, :]
    sine_part = jnp.sin(angle)[:, :, None] * select[:, None, :]
    return (cosine, sine_part)


def forward_rows(y_local, ky_rows, kx_rows, x_places, extent):
    cosine, sine_part = row_tables(ky_rows, kx_rows, x_places, extent, y_local.shape[0])
    real_in = y_local[:, 0]
    imag_in = y_local[:, 1]

    def contract(table, values):
        return jnp.einsum("rxk,kxf->rf", table, values, precision=lax.Precision.HIGHEST)

    real_out = contract(cosine, real_in) + contract(sine_part, imag_in)
    imag_out = contract(cosine, imag_in) - contract(sine_part, real_in)
    return jnp.concatenate([real_out, imag_out], axis=1)


def inverse_rows(running, shard_rows, ky_rows, kx_rows, x_places, extent):
    cosine, sine_part = row_tables(ky_rows, kx_rows, x_places, extent, running.shape[0])
    feat_count = shard_rows.shape[1] // 2
    real_part = shard_rows[:, :feat_count]
    imag_part = shard_rows[:, feat_count:]

    def contract(table, values):
        return jnp.einsum("rxk,rf->kxf", table, values, precision=lax.Precision.HIGHEST)

    new_real = contract(cosine, real_part) - contract(sine_part, imag_part)
    new_imag = contract(cosine, imag_part) + contract(sine_part, real_part)
    return jnp.stack([new_real, new_imag], axis=1)


def general_body(flow_field, spectral_weight, local_weight, bias_terms):
    cells_x, cells_y, feat_count = flow_field.shape
    channels = local_weight.shape[0]
    planes = feat_count // channels
    groups_x = lax.axis_size("gx")
    groups_y = lax.axis_size("gy")
    extent_x = cells_x * groups_x
    extent_y = cells_y * groups_y
    half_width = MY // groups_y
    quota_rows = spectral_weight.shape[1]
    high = lax.Precision.HIGHEST
    x_places = lax.axis_index("gx") * cells_x + jnp.arange(cells_x, dtype=jnp.int32)
    y_places = lax.axis_index("gy") * cells_y + jnp.arange(cells_y, dtype=jnp.int32)
    y_angle = phase_table(wave_number(jnp.arange(MY, dtype=jnp.int32), MY), y_places, extent_y)
    y_table = (
        jnp.stack([jnp.cos(y_angle), -jnp.sin(y_angle)], axis=1)
        .reshape(2 * MY, cells_y)
        .astype(jnp.bfloat16)
    )
    y_local = lax.psum_scatter(
        jnp.einsum("qy,xyf->qxf", y_table, flow_field, preferred_element_type=jnp.float32),
        "gy",
        scatter_dimension=0,
        tiled=True,
    )
    y_local = y_local.reshape(half_width, 2, cells_x, feat_count)
    rest_index = jnp.arange(lax.axis_size("gx") * quota_rows, dtype=jnp.int32)
    spectrum = lax.psum_scatter(
        forward_rows(y_local, rest_index // MX, rest_index % MX, x_places, extent_x),
        "gx",
        scatter_dimension=0,
        tiled=True,
    )
    spectrum = spectrum * (1.0 / math.sqrt(extent_x * extent_y))
    coeffs = spectrum.reshape(quota_rows, 2, planes, channels)
    weights = spectral_weight[0].astype(jnp.float32)
    product = jnp.einsum("rpzc,rco->rpzo", coeffs, weights, precision=high)
    mixed_real = product[:, 0, :, :channels] - product[:, 1, :, channels:]
    mixed_imag = product[:, 0, :, channels:] + product[:, 1, :, :channels]
    mixed_local = jnp.stack([mixed_real, mixed_imag], axis=1).reshape(quota_rows, 2 * feat_count)
    pointwise = jnp.einsum(
        "xyzc,co->xyzo",
        flow_field.reshape(cells_x, cells_y, planes, channels),
        local_weight,
        preferred_element_type=jnp.float32,
    )
    start_half = jnp.zeros((half_width, 2, cells_x, feat_count), jnp.float32)
    shard_rows = lax.all_gather(mixed_local, "gx", axis=0, tiled=True)
    rest_index = jnp.arange(shard_rows.shape[0], dtype=jnp.int32)
    back_half = inverse_rows(
        start_half, shard_rows, rest_index // MX, rest_index % MX, x_places, extent_x
    )
    back_whole = lax.all_gather(back_half, "gy", axis=0, tiled=True)
    y_cos = jnp.cos(y_angle)
    y_sin = jnp.sin(y_angle)
    spectral = (
        jnp.einsum("kn,kxf->xnf", y_cos, back_whole[:, 0], precision=high)
        - jnp.einsum("kn,kxf->xnf", y_sin, back_whole[:, 1], precision=high)
    ) * (1.0 / math.sqrt(MX * MY))
    total = spectral.reshape(cells_x, cells_y, planes, channels) + pointwise + bias_terms
    output = (
        jax.nn.gelu(total, approximate=False)
        .reshape(cells_x, cells_y, feat_count)
        .astype(jnp.bfloat16)
    )
    return (output, mixed_local.reshape(1, quota_rows, 2 * feat_count))


SMALL = pltpu.CompilerParams(vmem_limit_bytes=20 * 1024 * 1024)
LARGE = pltpu.CompilerParams(vmem_limit_bytes=211 * 256 * 1024)
WIDTH = 256


def angles(count, places, extent):
    index = np.arange(count)
    waves = np.where(index < count // 2, index, index - count)
    product = (waves[:, None] * np.asarray(places)[None, :]) % extent
    return (np.float32(2.0 * math.pi / extent) * product.astype(np.float32)).astype(np.float64)


def split_table(table):
    high = table.astype(ml_dtypes.bfloat16)
    low = (table - high.astype(np.float64)).astype(ml_dtypes.bfloat16)
    return high, low


def split_terms(values):
    high = values.astype(jnp.bfloat16)
    low = (values - high.astype(jnp.float32)).astype(jnp.bfloat16)
    return high, low


def forward_y_table(cells_y, groups_y, peers, rows_ky):
    extent = cells_y * groups_y
    angle = angles(MY, np.arange(extent), extent).astype(np.float32)
    full = np.stack([np.cos(angle), -np.sin(angle)], axis=1).astype(ml_dtypes.bfloat16)
    full = full.reshape(groups_y, peers, rows_ky, 2, groups_y, cells_y)
    out = np.zeros((groups_y, 2, peers, 2, rows_ky, 2, 2, cells_y), ml_dtypes.bfloat16)
    for place in range(groups_y):
        for side, half in enumerate((1 - place, place)):
            for parity in range(2):
                out[place, side, :, parity, :, :, parity, :] = full[half, :, :, :, place, :]
    return out.reshape(groups_y, 2 * peers * 4 * rows_ky, 2 * cells_y)


def forward_x_table(cells_x, peers, rows_ky):
    extent = cells_x * peers
    angle = angles(MX, np.arange(extent), extent)
    cosine, sine = np.cos(angle), np.sin(angle)
    out = np.zeros((2, rows_ky, MX, extent, rows_ky, 2))
    for row in range(rows_ky):
        out[0, row, :, :, row, 0] = cosine
        out[0, row, :, :, row, 1] = sine
        out[1, row, :, :, row, 1] = cosine
        out[1, row, :, :, row, 0] = -sine
    return out.reshape(2 * rows_ky * MX, extent * rows_ky * 2)


def inverse_x_table(cells_x, peers, rows_ky):
    extent = cells_x * peers
    angle = angles(MX, np.arange(extent), extent)
    cosine, sine = np.cos(angle).T, np.sin(angle).T
    out = np.zeros((extent, rows_ky, 2, 2, rows_ky, MX))
    for row in range(rows_ky):
        out[:, row, 0, 0, row, :] = cosine
        out[:, row, 0, 1, row, :] = -sine
        out[:, row, 1, 1, row, :] = cosine
        out[:, row, 1, 0, row, :] = sine
    return out.reshape(extent * rows_ky * 2, 2 * rows_ky * MX)


def inverse_y_table(cells_y, groups_y, peers, rows_ky):
    extent = cells_y * groups_y
    angle = angles(MY, np.arange(extent), extent)
    full = np.stack([np.cos(angle), -np.sin(angle)], axis=1)
    full = full.reshape(groups_y, peers, rows_ky, 2, groups_y, cells_y)
    out = np.zeros((groups_y, 2, cells_y, 2, peers, 2, rows_ky, 2))
    for place in range(groups_y):
        for side, half in enumerate((place, 1 - place)):
            block = np.moveaxis(full[half, :, :, :, place, :], -1, 0)
            for parity in range(2):
                out[place, parity, :, side, :, parity] = block
    return out.reshape(groups_y, 2, cells_y, 2 * peers * 4 * rows_ky)


def dot(left, right):
    return jnp.dot(left, right, preferred_element_type=jnp.float32)


def forward_y_kernel(
    flow_hbm, table_hbm, local_hbm, bias_hbm, send_ref, keep_ref, wide_ref, level_ref,
    flow_ref, table_ref, local_ref, bias_ref, arrivals,
):
    cells_x, cells_y, feat_count = flow_ref.shape
    channels = local_ref.shape[0]
    rows = table_ref.shape[0] // 2 // send_ref.shape[0]
    table_copy = pltpu.make_async_copy(
        table_hbm.at[lax.axis_index("gy")], table_ref, arrivals.at[cells_x]
    )
    table_copy.start()
    copies = []
    for x in range(cells_x):
        copies.append(pltpu.make_async_copy(flow_hbm.at[x], flow_ref.at[x], arrivals.at[x]))
        copies[x].start()
    local_copy = pltpu.make_async_copy(local_hbm, local_ref, arrivals.at[cells_x + 1])
    local_copy.start()
    bias_copy = pltpu.make_async_copy(bias_hbm, bias_ref, arrivals.at[cells_x + 2])
    bias_copy.start()
    table_copy.wait()
    for pair in range(cells_x // 2):
        copies[2 * pair].wait()
        copies[2 * pair + 1].wait()
        flow = flow_ref[2 * pair : 2 * pair + 2].reshape(2 * cells_y, feat_count)
        result = dot(table_ref[...], flow).reshape(2, send_ref.shape[0], rows, feat_count)
        send_ref[:, pair * rows : (pair + 1) * rows, :] = result[0]
        keep_ref[:, pair * rows : (pair + 1) * rows, :] = result[1]
    local_copy.wait()
    bias_copy.wait()
    wide_ref[...] = jnp.zeros_like(wide_ref)
    for start in range(0, wide_ref.shape[0], channels):
        span = slice(start, start + channels)
        wide_ref[span, span] = local_ref[...]
        level_ref[:, span] = bias_ref[...]


def forward_y(flow_field, table, local, bias, peers, rows_ky):
    cells_x, cells_y, feat_count = flow_field.shape
    shape = jax.ShapeDtypeStruct((peers, cells_x * 2 * rows_ky, feat_count), jnp.float32)
    spec = pl.BlockSpec(memory_space=pltpu.VMEM)
    source = pl.BlockSpec(memory_space=pltpu.HBM)
    return pl.pallas_call(
        forward_y_kernel,
        in_specs=[source] * 4,
        out_specs=[spec] * 4,
        out_shape=[
            shape,
            shape,
            jax.ShapeDtypeStruct((WIDTH, WIDTH), local.dtype),
            jax.ShapeDtypeStruct((1, WIDTH), bias.dtype),
        ],
        scratch_shapes=[
            pltpu.VMEM(flow_field.shape, flow_field.dtype),
            pltpu.VMEM(table.shape[1:], table.dtype),
            pltpu.VMEM(local.shape, local.dtype),
            pltpu.VMEM(bias.shape, bias.dtype),
            pltpu.SemaphoreType.DMA((cells_x + 3,)),
        ],
        compiler_params=LARGE,
        name="forward_y",
    )(flow_field, table, local, bias)


def turns(peers):
    return sorted(range(1, peers), key=lambda turn: (-(turn // 2), turn)) + [0]


def combine_kernel(keep_ref, arrived_ref, *out_refs):
    me = lax.axis_index("gx")
    for turn, out_ref in zip(turns(len(out_refs)), out_refs):
        out_ref[...] = keep_ref[me ^ turn] + arrived_ref[me ^ turn]


def combine(keep, arrived):
    peers = keep.shape[0]
    return pl.pallas_call(
        combine_kernel,
        out_shape=[jax.ShapeDtypeStruct(keep.shape[1:], keep.dtype)] * peers,
        compiler_params=SMALL,
        name="combine",
    )(keep, arrived)


def exchange(blocks):
    peers = len(blocks)
    arrived = []
    for turn, block in zip(turns(peers), blocks):
        pairs = [(place, place ^ turn) for place in range(peers)]
        arrived.append(lax.ppermute(block, "gx", pairs) if turn else block)
    return arrived


def gather_kernel(*refs):
    me = lax.axis_index("gx")
    for turn, block_ref in zip(turns(len(refs) - 1), refs):
        refs[-1][me ^ turn] = block_ref[...]


def gather(blocks):
    return pl.pallas_call(
        gather_kernel,
        out_shape=jax.ShapeDtypeStruct((len(blocks),) + blocks[0].shape, blocks[0].dtype),
        compiler_params=SMALL,
        name="gather",
    )(*blocks)


def mix_kernel(peers, *refs):
    block_refs = refs[:peers]
    weight_ref, forward_high, forward_low, inverse_high, inverse_low, mixed_ref = refs[
        peers : peers + 6
    ]
    back_refs = refs[peers + 6 : 2 * peers + 6]
    order_ref, spread_ref, result_ref = refs[2 * peers + 6 :]
    me = lax.axis_index("gx")
    feat_count = order_ref.shape[-1]
    count = weight_ref.shape[1]
    channels = weight_ref.shape[2]
    tiles = feat_count // 128
    group = 2 * tiles
    for turn, block_ref in zip(turns(peers), block_refs):
        order_ref[me ^ turn] = block_ref[...]
    high, low = split_terms(order_ref[...].reshape(-1, feat_count))
    spectrum = (
        dot(forward_high[...], high) + dot(forward_high[...], low) + dot(forward_low[...], high)
    )
    for part in range(2):
        for tile in range(tiles):
            spread_ref[pl.ds(part * tiles + tile, count, stride=group), :] = spectrum[
                part * count : (part + 1) * count, tile * 128 : (tile + 1) * 128
            ]
    lane = lax.broadcasted_iota(jnp.int32, (group, 128), 1) < channels
    sign = jnp.where(lax.broadcasted_iota(jnp.int32, (group, 128), 0) < tiles, -1.0, 1.0)
    for mode in range(count):
        block = spread_ref[mode * group : (mode + 1) * group, :]
        turned = pltpu.roll(block, channels, 1)
        left = jnp.concatenate([block, turned], axis=0)[:, :channels]
        left_high, left_low = split_terms(left)
        product = dot(jnp.concatenate([left_high, left_low], axis=0), weight_ref[0, mode])
        product = product[: 2 * group] + product[2 * group :]
        first, second = product[:group], product[group:]
        real = jnp.where(lane, first, pltpu.roll(second, channels, 1))
        imag = jnp.where(lane, pltpu.roll(first, channels, 1), second)
        result_ref[mode * group : (mode + 1) * group, :] = real + sign * pltpu.roll(imag, tiles, 0)
    parts = []
    for part in range(2):
        parts.append(
            jnp.concatenate(
                [
                    result_ref[pl.ds(part * tiles + tile, count, stride=group), :]
                    for tile in range(tiles)
                ],
                axis=1,
            )
        )
        mixed_ref[0, :, part * feat_count : (part + 1) * feat_count] = parts[part]
    high, low = split_terms(jnp.concatenate(parts, axis=0))
    back = dot(inverse_high[...], high) + dot(inverse_high[...], low) + dot(inverse_low[...], high)
    order_ref[...] = back.reshape(order_ref.shape)
    for turn, back_ref in zip(turns(peers), back_refs):
        back_ref[...] = order_ref[me ^ turn]


def mix(blocks, weights, forward_table, inverse_table):
    rows, feat_count = blocks[0].shape
    peers = len(blocks)
    count = weights.shape[1]
    scratch = pltpu.VMEM((count * feat_count // 64, 128), jnp.float32)
    mixed, *back = pl.pallas_call(
        functools.partial(mix_kernel, peers),
        out_shape=[jax.ShapeDtypeStruct((1, count, 2 * feat_count), jnp.float32)]
        + [jax.ShapeDtypeStruct(blocks[0].shape, jnp.float32)] * peers,
        scratch_shapes=[pltpu.VMEM((peers, rows, feat_count), jnp.float32), scratch, scratch],
        compiler_params=SMALL,
        name="mix",
    )(*blocks, weights, *split_table(forward_table), *split_table(inverse_table))
    return mixed, back


def output_kernel(
    place_ref, flow_ref, table_ref, wide_ref, level_ref, own_ref, other_ref, out_ref, stack_ref
):
    step = pl.program_id(0)
    feat_count = flow_ref.shape[-1]
    width = wide_ref.shape[0]
    pairs = stack_ref.shape[0]
    rows = own_ref.shape[1] // pairs

    @pl.when(step == 0)
    def _():
        for pair in range(pairs):
            span = slice(pair * rows, (pair + 1) * rows)
            both = jnp.concatenate([own_ref[:, span, :], other_ref[:, span, :]], axis=0)
            high, low = split_terms(both.reshape(-1, feat_count))
            stack_ref[pair] = jnp.concatenate([high, low, high], axis=0)

    table = table_ref[0, step % 2]
    for start in range(0, feat_count, width):
        columns = slice(start, start + width)
        total = (
            dot(table, stack_ref[step // 2, :, columns])
            + dot(flow_ref[0, :, columns], wide_ref[...])
            + level_ref[...]
        )
        out_ref[0, :, columns] = (
            0.5 * total * (1.0 + lax.erf(total * math.sqrt(0.5)))
        ).astype(out_ref.dtype)


def make_output(flow_field, own, other, table, wide, level):
    cells_x, cells_y, feat_count = flow_field.shape
    place = jnp.reshape(lax.axis_index("gy"), (1,))
    whole = lambda array: pl.BlockSpec(array.shape, lambda i, p: (0,) * array.ndim)
    block = pl.BlockSpec((1, cells_y, feat_count), lambda i, p: (i, 0, 0))
    return pl.pallas_call(
        output_kernel,
        grid_spec=pltpu.PrefetchScalarGridSpec(
            num_scalar_prefetch=1,
            grid=(cells_x,),
            in_specs=[
                block,
                pl.BlockSpec((1,) + table.shape[1:], lambda i, p: (p[0], 0, 0, 0)),
                whole(wide),
                whole(level),
                whole(own),
                whole(other),
            ],
            out_specs=block,
            scratch_shapes=[
                pltpu.VMEM((cells_x // 2, table.shape[-1], feat_count), jnp.bfloat16),
            ],
        ),
        out_shape=jax.ShapeDtypeStruct(flow_field.shape, jnp.bfloat16),
        compiler_params=SMALL,
        name="make_output",
    )(place, flow_field, table, wide, level, own, other)


def row_body(flow_field, spectral_weight, local_weight, bias_terms):
    cells_x, cells_y, feat_count = flow_field.shape
    peers = lax.axis_size("gx")
    groups_y = lax.axis_size("gy")
    rows_ky = MY // groups_y // peers
    forward_scale = 1.0 / math.sqrt(cells_x * peers * cells_y * groups_y)
    inverse_scale = 1.0 / math.sqrt(MX * MY)
    swap = [(0, 1), (1, 0)]

    send, keep, wide, level = forward_y(
        flow_field,
        forward_y_table(cells_y, groups_y, peers, rows_ky),
        local_weight,
        bias_terms[None, :],
        peers,
        rows_ky,
    )
    blocks = exchange(combine(keep, lax.ppermute(send, "gy", swap)))
    mixed, back = mix(
        blocks,
        spectral_weight,
        forward_x_table(cells_x, peers, rows_ky) * forward_scale,
        inverse_x_table(cells_x, peers, rows_ky),
    )
    own = gather(exchange(back))
    other = lax.ppermute(own, "gy", swap)
    high, low = split_table(inverse_y_table(cells_y, groups_y, peers, rows_ky) * inverse_scale)
    output = make_output(
        flow_field,
        own,
        other,
        np.concatenate([high, high, low], axis=-1),
        wide,
        level,
    )
    return output, mixed


def body(flow_field, spectral_weight, local_weight, bias_terms):
    peers = lax.axis_size("gx")
    paired = lax.axis_size("gy") == 2 and peers & (peers - 1) == 0
    if paired and spectral_weight.shape[1] == 2 * MX and WIDTH % local_weight.shape[0] == 0:
        return row_body(flow_field, spectral_weight, local_weight, bias_terms)
    return general_body(flow_field, spectral_weight, local_weight, bias_terms)


def solution(mesh):
    placed = (P(("group", "gx"), "gy", None), P("gy", "gx", None, None), P(), P())
    return jax.shard_map(
        body,
        mesh=mesh,
        in_specs=placed,
        out_specs=(P(("group", "gx"), "gy", None), P(("group", "gy"), "gx", None)),
        check_vma=False,
    )
```

```python
import functools
import math

import jax
import jax.numpy as jnp
import ml_dtypes
import numpy as np
from jax import lax
from jax.experimental import pallas as pl
from jax.experimental.pallas import tpu as pltpu
from jax.sharding import PartitionSpec as P

MX = 32
MY = 32


def wave_number(index, count):
    return jnp.where(index < count // 2, index, index - count)


def phase_table(waves, places, extent):
    product = waves[:, None] * places[None, :] % extent
    return 2.0 * math.pi / extent * product.astype(jnp.float32)


def row_tables(ky_rows, kx_rows, x_places, extent, width):
    angle = phase_table(wave_number(kx_rows, MX), x_places, extent)
    select = (ky_rows[:, None] == jnp.arange(width, dtype=jnp.int32)[None, :]).astype(jnp.float32)
    cosine = jnp.cos(angle)[:, :, None] * select[:, None, :]
    sine_part = jnp.sin(angle)[:, :, None] * select[:, None, :]
    return (cosine, sine_part)


def forward_rows(y_local, ky_rows, kx_rows, x_places, extent):
    cosine, sine_part = row_tables(ky_rows, kx_rows, x_places, extent, y_local.shape[0])
    real_in = y_local[:, 0]
    imag_in = y_local[:, 1]

    def contract(table, values):
        return jnp.einsum("rxk,kxf->rf", table, values, precision=lax.Precision.HIGHEST)

    real_out = contract(cosine, real_in) + contract(sine_part, imag_in)
    imag_out = contract(cosine, imag_in) - contract(sine_part, real_in)
    return jnp.concatenate([real_out, imag_out], axis=1)


def inverse_rows(running, shard_rows, ky_rows, kx_rows, x_places, extent):
    cosine, sine_part = row_tables(ky_rows, kx_rows, x_places, extent, running.shape[0])
    feat_count = shard_rows.shape[1] // 2
    real_part = shard_rows[:, :feat_count]
    imag_part = shard_rows[:, feat_count:]

    def contract(table, values):
        return jnp.einsum("rxk,rf->kxf", table, values, precision=lax.Precision.HIGHEST)

    new_real = contract(cosine, real_part) - contract(sine_part, imag_part)
    new_imag = contract(cosine, imag_part) + contract(sine_part, real_part)
    return jnp.stack([new_real, new_imag], axis=1)


def general_body(flow_field, spectral_weight, local_weight, bias_terms):
    cells_x, cells_y, feat_count = flow_field.shape
    channels = local_weight.shape[0]
    planes = feat_count // channels
    groups_x = lax.axis_size("gx")
    groups_y = lax.axis_size("gy")
    extent_x = cells_x * groups_x
    extent_y = cells_y * groups_y
    half_width = MY // groups_y
    quota_rows = spectral_weight.shape[1]
    high = lax.Precision.HIGHEST
    x_places = lax.axis_index("gx") * cells_x + jnp.arange(cells_x, dtype=jnp.int32)
    y_places = lax.axis_index("gy") * cells_y + jnp.arange(cells_y, dtype=jnp.int32)
    y_angle = phase_table(wave_number(jnp.arange(MY, dtype=jnp.int32), MY), y_places, extent_y)
    y_table = (
        jnp.stack([jnp.cos(y_angle), -jnp.sin(y_angle)], axis=1)
        .reshape(2 * MY, cells_y)
        .astype(jnp.bfloat16)
    )
    y_local = lax.psum_scatter(
        jnp.einsum("qy,xyf->qxf", y_table, flow_field, preferred_element_type=jnp.float32),
        "gy",
        scatter_dimension=0,
        tiled=True,
    )
    y_local = y_local.reshape(half_width, 2, cells_x, feat_count)
    rest_index = jnp.arange(lax.axis_size("gx") * quota_rows, dtype=jnp.int32)
    spectrum = lax.psum_scatter(
        forward_rows(y_local, rest_index // MX, rest_index % MX, x_places, extent_x),
        "gx",
        scatter_dimension=0,
        tiled=True,
    )
    spectrum = spectrum * (1.0 / math.sqrt(extent_x * extent_y))
    coeffs = spectrum.reshape(quota_rows, 2, planes, channels)
    weights = spectral_weight[0].astype(jnp.float32)
    product = jnp.einsum("rpzc,rco->rpzo", coeffs, weights, precision=high)
    mixed_real = product[:, 0, :, :channels] - product[:, 1, :, channels:]
    mixed_imag = product[:, 0, :, channels:] + product[:, 1, :, :channels]
    mixed_local = jnp.stack([mixed_real, mixed_imag], axis=1).reshape(quota_rows, 2 * feat_count)
    pointwise = jnp.einsum(
        "xyzc,co->xyzo",
        flow_field.reshape(cells_x, cells_y, planes, channels),
        local_weight,
        preferred_element_type=jnp.float32,
    )
    start_half = jnp.zeros((half_width, 2, cells_x, feat_count), jnp.float32)
    shard_rows = lax.all_gather(mixed_local, "gx", axis=0, tiled=True)
    rest_index = jnp.arange(shard_rows.shape[0], dtype=jnp.int32)
    back_half = inverse_rows(
        start_half, shard_rows, rest_index // MX, rest_index % MX, x_places, extent_x
    )
    back_whole = lax.all_gather(back_half, "gy", axis=0, tiled=True)
    y_cos = jnp.cos(y_angle)
    y_sin = jnp.sin(y_angle)
    spectral = (
        jnp.einsum("kn,kxf->xnf", y_cos, back_whole[:, 0], precision=high)
        - jnp.einsum("kn,kxf->xnf", y_sin, back_whole[:, 1], precision=high)
    ) * (1.0 / math.sqrt(MX * MY))
    total = spectral.reshape(cells_x, cells_y, planes, channels) + pointwise + bias_terms
    output = (
        jax.nn.gelu(total, approximate=False)
        .reshape(cells_x, cells_y, feat_count)
        .astype(jnp.bfloat16)
    )
    return (output, mixed_local.reshape(1, quota_rows, 2 * feat_count))


SMALL = pltpu.CompilerParams(vmem_limit_bytes=20 * 1024 * 1024)
CHUNKS = 2


def angles(count, places, extent):
    index = np.arange(count)
    waves = np.where(index < count // 2, index, index - count)
    product = (waves[:, None] * np.asarray(places)[None, :]) % extent
    return (np.float32(2.0 * math.pi / extent) * product.astype(np.float32)).astype(np.float64)


def split_table(table):
    high = table.astype(ml_dtypes.bfloat16)
    low = (table - high.astype(np.float64)).astype(ml_dtypes.bfloat16)
    return high, low


def split_terms(values):
    high = values.astype(jnp.bfloat16)
    low = (values - high.astype(jnp.float32)).astype(jnp.bfloat16)
    return high, low


def forward_y_table(cells_y, groups_y):
    place = lax.axis_index("gy")
    row = jnp.arange(2 * MY, dtype=jnp.int32)
    half = MY // groups_y
    index = (row // 2 + (1 - place) * half) % MY
    y_places = place * cells_y + jnp.arange(cells_y, dtype=jnp.int32)
    angle = phase_table(wave_number(index, MY), y_places, cells_y * groups_y)
    return jnp.where(row[:, None] % 2 == 0, jnp.cos(angle), -jnp.sin(angle)).astype(jnp.bfloat16)


def forward_x_table(cells_x, peers, rows_ky):
    extent = cells_x * peers
    angle = angles(MX, np.arange(extent), extent)
    cosine, sine = np.cos(angle), np.sin(angle)
    out = np.zeros((2, rows_ky, MX, extent, rows_ky, 2))
    for row in range(rows_ky):
        out[0, row, :, :, row, 0] = cosine
        out[0, row, :, :, row, 1] = sine
        out[1, row, :, :, row, 1] = cosine
        out[1, row, :, :, row, 0] = -sine
    return out.reshape(2 * rows_ky * MX, extent * rows_ky * 2)


def inverse_x_table(cells_x, peers, rows_ky):
    extent = cells_x * peers
    angle = angles(MX, np.arange(extent), extent)
    cosine, sine = np.cos(angle).T, np.sin(angle).T
    out = np.zeros((extent, rows_ky, 2, 2, rows_ky, MX))
    for row in range(rows_ky):
        out[:, row, 0, 0, row, :] = cosine
        out[:, row, 0, 1, row, :] = -sine
        out[:, row, 1, 1, row, :] = cosine
        out[:, row, 1, 0, row, :] = sine
    return out.reshape(extent * rows_ky * 2, 2 * rows_ky * MX)


def inverse_y_table(cells_y, groups_y, peers, rows_ky):
    extent = cells_y * groups_y
    angle = angles(MY, np.arange(extent), extent)
    full = np.stack([np.cos(angle), -np.sin(angle)], axis=1)
    full = full.reshape(groups_y, peers, rows_ky, 2, groups_y, cells_y)
    out = np.zeros((groups_y, 2, cells_y, 2, peers, 2, rows_ky, 2))
    for place in range(groups_y):
        for side, half in enumerate((place, 1 - place)):
            block = np.moveaxis(full[half, :, :, :, place, :], -1, 0)
            for parity in range(2):
                out[place, parity, :, side, :, parity] = block
    return out.reshape(groups_y, 2, cells_y, 2 * peers * 4 * rows_ky)


def dot(left, right):
    return jnp.dot(left, right, preferred_element_type=jnp.float32)


def forward_y_kernel(flow_ref, table_ref, *out_refs):
    chunks = len(out_refs) // 2
    peers, rows, width = out_refs[0].shape
    cells_x = flow_ref.shape[0]
    rows = rows // cells_x
    for x in range(cells_x):
        result = dot(table_ref[...], flow_ref[x]).reshape(2, peers, rows, chunks * width)
        for chunk in range(chunks):
            for side in range(2):
                out_refs[2 * chunk + side][:, x * rows : (x + 1) * rows, :] = result[
                    side, :, :, chunk * width : (chunk + 1) * width
                ]


def forward_y(flow_field, table, peers, rows_ky):
    cells_x, _, feat_count = flow_field.shape
    shape = jax.ShapeDtypeStruct(
        (peers, cells_x * 2 * rows_ky, feat_count // CHUNKS), jnp.float32
    )
    return pl.pallas_call(
        forward_y_kernel,
        out_shape=[shape] * (2 * CHUNKS),
        compiler_params=SMALL,
        name="forward_y",
    )(flow_field, table)


def mix_kernel(
    modes_ref, weight_ref, forward_high, forward_low, inverse_high, inverse_low,
    mixed_ref, back_ref, spread_ref, result_ref,
):
    feat_count = modes_ref.shape[-1]
    count = weight_ref.shape[1]
    channels = weight_ref.shape[2]
    tiles = feat_count // 128
    group = 2 * tiles
    high, low = split_terms(modes_ref[...].reshape(-1, feat_count))
    spectrum = (
        dot(forward_high[...], high) + dot(forward_high[...], low) + dot(forward_low[...], high)
    )
    for part in range(2):
        for tile in range(tiles):
            spread_ref[pl.ds(part * tiles + tile, count, stride=group), :] = spectrum[
                part * count : (part + 1) * count, tile * 128 : (tile + 1) * 128
            ]
    rows = lax.broadcasted_iota(jnp.int32, (8, 128), 0) % group
    lane = lax.broadcasted_iota(jnp.int32, (8, 128), 1) < channels
    sign = jnp.where(rows < tiles, -1.0, 1.0)
    for base in range(0, count * group, 8):
        block = spread_ref[base : base + 8, :]
        turned = pltpu.roll(block, channels, 1)
        firsts, seconds = [], []
        for start in range(0, 8, group):
            span = slice(start, start + group)
            left = jnp.concatenate([block[span], turned[span]], axis=0)[:, :channels]
            left_high, left_low = split_terms(left)
            left = jnp.concatenate([left_high, left_low], axis=0)
            product = dot(left, weight_ref[0, (base + start) // group])
            product = product[: 2 * group] + product[2 * group :]
            firsts.append(product[:group])
            seconds.append(product[group:])
        first = jnp.concatenate(firsts, axis=0)
        second = jnp.concatenate(seconds, axis=0)
        real = jnp.where(lane, first, pltpu.roll(second, channels, 1))
        imag = jnp.where(lane, pltpu.roll(first, channels, 1), second)
        crossed = jnp.where(rows < tiles, pltpu.roll(imag, 8 - tiles, 0), pltpu.roll(imag, tiles, 0))
        result_ref[base : base + 8, :] = real + sign * crossed
    parts = []
    for part in range(2):
        parts.append(
            jnp.concatenate(
                [
                    result_ref[pl.ds(part * tiles + tile, count, stride=group), :]
                    for tile in range(tiles)
                ],
                axis=1,
            )
        )
        mixed_ref[part] = parts[part]
    high, low = split_terms(jnp.concatenate(parts, axis=0))
    back = dot(inverse_high[...], high) + dot(inverse_high[...], low) + dot(inverse_low[...], high)
    back_ref[...] = back.reshape(back_ref.shape)


def mix(modes, weights, forward_table, inverse_table):
    feat_count = modes.shape[-1]
    count = weights.shape[1]
    scratch = pltpu.VMEM((count * feat_count // 64, 128), jnp.float32)
    return pl.pallas_call(
        mix_kernel,
        out_shape=[
            jax.ShapeDtypeStruct((2, count, feat_count), jnp.float32),
            jax.ShapeDtypeStruct(modes.shape, jnp.float32),
        ],
        scratch_shapes=[scratch, scratch],
        compiler_params=SMALL,
        name="mix",
    )(modes, weights, *split_table(forward_table), *split_table(inverse_table))


def output_kernel(
    place_ref, flow_ref, table_ref, local_ref, bias_ref, own_ref, other_ref, *refs
):
    out_ref, stack_ref, wide_ref, level_ref = refs[-4:]
    step = pl.program_id(0)
    feat_count = flow_ref.shape[-1]
    channels = local_ref.shape[0]
    pairs = stack_ref.shape[0]
    rows = own_ref.shape[1] // pairs

    @pl.when(step == 0)
    def _():
        for pair in range(pairs):
            span = slice(pair * rows, (pair + 1) * rows)
            both = jnp.concatenate([own_ref[:, span, :], other_ref[:, span, :]], axis=0)
            high, low = split_terms(both.reshape(-1, feat_count))
            stack_ref[pair] = jnp.concatenate([high, low, high], axis=0)
        wide_ref[...] = jnp.zeros_like(wide_ref)
        for start in range(0, feat_count, channels):
            span = slice(start, start + channels)
            wide_ref[span, span] = local_ref[...]
            level_ref[:, span] = bias_ref[...].reshape(1, channels)

    total = (
        dot(table_ref[0, step % 2], stack_ref[step // 2])
        + dot(flow_ref[0], wide_ref[...])
        + level_ref[...]
    )
    out_ref[0] = (0.5 * total * (1.0 + lax.erf(total * math.sqrt(0.5)))).astype(out_ref.dtype)


def make_output(chunk, earlier, flow_field, own, other, table, local, bias):
    cells_x, cells_y, feat_count = flow_field.shape
    width = feat_count // CHUNKS
    place = jnp.reshape(lax.axis_index("gy"), (1,))
    whole = lambda array: pl.BlockSpec(array.shape, lambda i, p: (0,) * array.ndim)
    block = pl.BlockSpec((1, cells_y, width), lambda i, p: (i, 0, chunk))
    return pl.pallas_call(
        output_kernel,
        grid_spec=pltpu.PrefetchScalarGridSpec(
            num_scalar_prefetch=1,
            grid=(cells_x,),
            in_specs=[
                block,
                pl.BlockSpec((1,) + table.shape[1:], lambda i, p: (p[0], 0, 0, 0)),
                whole(local),
                whole(bias),
                whole(own),
                whole(other),
            ]
            + [pl.BlockSpec(memory_space=pl.ANY)] * len(earlier),
            out_specs=block,
            scratch_shapes=[
                pltpu.VMEM((cells_x // 2, table.shape[-1], width), jnp.bfloat16),
                pltpu.VMEM((width, width), jnp.bfloat16),
                pltpu.VMEM((1, width), jnp.float32),
            ],
        ),
        out_shape=jax.ShapeDtypeStruct(flow_field.shape, jnp.bfloat16),
        input_output_aliases={7: 0} if earlier else {},
        compiler_params=SMALL,
        name="make_output",
    )(place, flow_field, table, local, bias, own, other, *earlier)


def row_body(flow_field, spectral_weight, local_weight, bias_terms):
    cells_x, cells_y, feat_count = flow_field.shape
    peers = lax.axis_size("gx")
    groups_y = lax.axis_size("gy")
    rows_ky = MY // groups_y // peers
    forward_scale = 1.0 / math.sqrt(cells_x * peers * cells_y * groups_y)
    inverse_scale = 1.0 / math.sqrt(MX * MY)
    swap = [(0, 1), (1, 0)]

    parts = forward_y(flow_field, forward_y_table(cells_y, groups_y), peers, rows_ky)
    forward_table = forward_x_table(cells_x, peers, rows_ky) * forward_scale
    inverse_table = inverse_x_table(cells_x, peers, rows_ky)
    high, low = split_table(inverse_y_table(cells_y, groups_y, peers, rows_ky) * inverse_scale)
    table = np.concatenate([high, high, low], axis=-1)
    mixed, earlier = [], []
    for chunk in range(CHUNKS):
        send, keep = parts[2 * chunk : 2 * chunk + 2]
        modes = keep + lax.ppermute(send, "gy", swap)
        modes = lax.all_to_all(modes, "gx", 0, 0, tiled=True)
        part, back = mix(modes, spectral_weight, forward_table, inverse_table)
        mixed.append(part)
        own = lax.all_to_all(back, "gx", 0, 0, tiled=True)
        other = lax.ppermute(own, "gy", swap)
        output = make_output(
            chunk, earlier, flow_field, own, other, table, local_weight, bias_terms
        )
        earlier = [output]
    mixed = jnp.concatenate([part[turn] for turn in range(2) for part in mixed], axis=-1)
    return output, mixed[None]


def body(flow_field, spectral_weight, local_weight, bias_terms):
    whole_rows = spectral_weight.shape[1] % MX == 0
    width = flow_field.shape[2] // CHUNKS
    even = flow_field.shape[2] % CHUNKS == 0 and width == 256 and width % local_weight.shape[0] == 0
    if even and whole_rows and lax.axis_size("gy") == 2 and spectral_weight.shape[1] == 2 * MX:
        return row_body(flow_field, spectral_weight, local_weight, bias_terms)
    return general_body(flow_field, spectral_weight, local_weight, bias_terms)


def solution(mesh):
    placed = (P(("group", "gx"), "gy", None), P("gy", "gx", None, None), P(), P())
    return jax.shard_map(
        body,
        mesh=mesh,
        in_specs=placed,
        out_specs=(P(("group", "gx"), "gy", None), P(("group", "gy"), "gx", None)),
        check_vma=False,
    )
```

```python
import functools
import math

import jax
import jax.numpy as jnp
import ml_dtypes
import numpy as np
from jax import lax
from jax.experimental import pallas as pl
from jax.experimental.pallas import tpu as pltpu
from jax.sharding import PartitionSpec as P

MX = 32
MY = 32


def wave_number(index, count):
    return jnp.where(index < count // 2, index, index - count)


def phase_table(waves, places, extent):
    product = waves[:, None] * places[None, :] % extent
    return 2.0 * math.pi / extent * product.astype(jnp.float32)


def row_tables(ky_rows, kx_rows, x_places, extent, width):
    angle = phase_table(wave_number(kx_rows, MX), x_places, extent)
    select = (ky_rows[:, None] == jnp.arange(width, dtype=jnp.int32)[None, :]).astype(jnp.float32)
    cosine = jnp.cos(angle)[:, :, None] * select[:, None, :]
    sine_part = jnp.sin(angle)[:, :, None] * select[:, None, :]
    return (cosine, sine_part)


def forward_rows(y_local, ky_rows, kx_rows, x_places, extent):
    cosine, sine_part = row_tables(ky_rows, kx_rows, x_places, extent, y_local.shape[0])
    real_in = y_local[:, 0]
    imag_in = y_local[:, 1]

    def contract(table, values):
        return jnp.einsum("rxk,kxf->rf", table, values, precision=lax.Precision.HIGHEST)

    real_out = contract(cosine, real_in) + contract(sine_part, imag_in)
    imag_out = contract(cosine, imag_in) - contract(sine_part, real_in)
    return jnp.concatenate([real_out, imag_out], axis=1)


def inverse_rows(running, shard_rows, ky_rows, kx_rows, x_places, extent):
    cosine, sine_part = row_tables(ky_rows, kx_rows, x_places, extent, running.shape[0])
    feat_count = shard_rows.shape[1] // 2
    real_part = shard_rows[:, :feat_count]
    imag_part = shard_rows[:, feat_count:]

    def contract(table, values):
        return jnp.einsum("rxk,rf->kxf", table, values, precision=lax.Precision.HIGHEST)

    new_real = contract(cosine, real_part) - contract(sine_part, imag_part)
    new_imag = contract(cosine, imag_part) + contract(sine_part, real_part)
    return jnp.stack([new_real, new_imag], axis=1)


def general_body(flow_field, spectral_weight, local_weight, bias_terms):
    cells_x, cells_y, feat_count = flow_field.shape
    channels = local_weight.shape[0]
    planes = feat_count // channels
    groups_x = lax.axis_size("gx")
    groups_y = lax.axis_size("gy")
    extent_x = cells_x * groups_x
    extent_y = cells_y * groups_y
    half_width = MY // groups_y
    quota_rows = spectral_weight.shape[1]
    high = lax.Precision.HIGHEST
    x_places = lax.axis_index("gx") * cells_x + jnp.arange(cells_x, dtype=jnp.int32)
    y_places = lax.axis_index("gy") * cells_y + jnp.arange(cells_y, dtype=jnp.int32)
    y_angle = phase_table(wave_number(jnp.arange(MY, dtype=jnp.int32), MY), y_places, extent_y)
    y_table = (
        jnp.stack([jnp.cos(y_angle), -jnp.sin(y_angle)], axis=1)
        .reshape(2 * MY, cells_y)
        .astype(jnp.bfloat16)
    )
    y_local = lax.psum_scatter(
        jnp.einsum("qy,xyf->qxf", y_table, flow_field, preferred_element_type=jnp.float32),
        "gy",
        scatter_dimension=0,
        tiled=True,
    )
    y_local = y_local.reshape(half_width, 2, cells_x, feat_count)
    rest_index = jnp.arange(lax.axis_size("gx") * quota_rows, dtype=jnp.int32)
    spectrum = lax.psum_scatter(
        forward_rows(y_local, rest_index // MX, rest_index % MX, x_places, extent_x),
        "gx",
        scatter_dimension=0,
        tiled=True,
    )
    spectrum = spectrum * (1.0 / math.sqrt(extent_x * extent_y))
    coeffs = spectrum.reshape(quota_rows, 2, planes, channels)
    weights = spectral_weight[0].astype(jnp.float32)
    product = jnp.einsum("rpzc,rco->rpzo", coeffs, weights, precision=high)
    mixed_real = product[:, 0, :, :channels] - product[:, 1, :, channels:]
    mixed_imag = product[:, 0, :, channels:] + product[:, 1, :, :channels]
    mixed_local = jnp.stack([mixed_real, mixed_imag], axis=1).reshape(quota_rows, 2 * feat_count)
    pointwise = jnp.einsum(
        "xyzc,co->xyzo",
        flow_field.reshape(cells_x, cells_y, planes, channels),
        local_weight,
        preferred_element_type=jnp.float32,
    )
    start_half = jnp.zeros((half_width, 2, cells_x, feat_count), jnp.float32)
    shard_rows = lax.all_gather(mixed_local, "gx", axis=0, tiled=True)
    rest_index = jnp.arange(shard_rows.shape[0], dtype=jnp.int32)
    back_half = inverse_rows(
        start_half, shard_rows, rest_index // MX, rest_index % MX, x_places, extent_x
    )
    back_whole = lax.all_gather(back_half, "gy", axis=0, tiled=True)
    y_cos = jnp.cos(y_angle)
    y_sin = jnp.sin(y_angle)
    spectral = (
        jnp.einsum("kn,kxf->xnf", y_cos, back_whole[:, 0], precision=high)
        - jnp.einsum("kn,kxf->xnf", y_sin, back_whole[:, 1], precision=high)
    ) * (1.0 / math.sqrt(MX * MY))
    total = spectral.reshape(cells_x, cells_y, planes, channels) + pointwise + bias_terms
    output = (
        jax.nn.gelu(total, approximate=False)
        .reshape(cells_x, cells_y, feat_count)
        .astype(jnp.bfloat16)
    )
    return (output, mixed_local.reshape(1, quota_rows, 2 * feat_count))


SMALL = pltpu.CompilerParams(vmem_limit_bytes=20 * 1024 * 1024)
WIDTH = 256


def angles(count, places, extent):
    index = np.arange(count)
    waves = np.where(index < count // 2, index, index - count)
    product = (waves[:, None] * np.asarray(places)[None, :]) % extent
    return (np.float32(2.0 * math.pi / extent) * product.astype(np.float32)).astype(np.float64)


def split_table(table):
    high = table.astype(ml_dtypes.bfloat16)
    low = (table - high.astype(np.float64)).astype(ml_dtypes.bfloat16)
    return high, low


def split_terms(values):
    high = values.astype(jnp.bfloat16)
    low = (values - high.astype(jnp.float32)).astype(jnp.bfloat16)
    return high, low


def quad():
    place = lax.axis_index("gx")
    return place // 2, place % 2, lax.axis_index("gy")


def turns(layers):
    return list(range(layers - 1, 0, -1)) + [0]


def forward_y_table(cells_y, groups_y, peers, rows_ky):
    z, x, y = quad()
    layers = peers // 2
    row = jnp.arange(2 * MY, dtype=jnp.int32)
    block = row // (2 * rows_ky)
    turn = layers - 1 - block % layers
    owner = (z ^ turn) * 2 + (x ^ (1 - block // layers % 2))
    owner = (y ^ (1 - block // peers)) * peers + owner
    index = owner * rows_ky + row // 2 % rows_ky
    y_places = y * cells_y + jnp.arange(cells_y, dtype=jnp.int32)
    angle = phase_table(wave_number(index, MY), y_places, cells_y * groups_y)
    return jnp.where(row[:, None] % 2 == 0, jnp.cos(angle), -jnp.sin(angle)).astype(jnp.bfloat16)


def forward_x_table(cells_x, peers, rows_ky):
    extent = cells_x * peers
    angle = angles(MX, np.arange(extent), extent)
    cosine, sine = np.cos(angle), np.sin(angle)
    out = np.zeros((2, rows_ky, MX, extent, rows_ky, 2))
    for row in range(rows_ky):
        out[0, row, :, :, row, 0] = cosine
        out[0, row, :, :, row, 1] = sine
        out[1, row, :, :, row, 1] = cosine
        out[1, row, :, :, row, 0] = -sine
    return out.reshape(2 * rows_ky * MX, extent * rows_ky * 2)


def inverse_x_table(cells_x, peers, rows_ky):
    extent = cells_x * peers
    angle = angles(MX, np.arange(extent), extent)
    cosine, sine = np.cos(angle).T, np.sin(angle).T
    out = np.zeros((extent, rows_ky, 2, 2, rows_ky, MX))
    for row in range(rows_ky):
        out[:, row, 0, 0, row, :] = cosine
        out[:, row, 0, 1, row, :] = -sine
        out[:, row, 1, 1, row, :] = cosine
        out[:, row, 1, 0, row, :] = sine
    return out.reshape(extent * rows_ky * 2, 2 * rows_ky * MX)


def inverse_y_table(cells_y, groups_y, peers, rows_ky):
    extent = cells_y * groups_y
    angle = angles(MY, np.arange(extent), extent)
    full = np.stack([np.cos(angle), -np.sin(angle)], axis=1)
    full = full.reshape(groups_y, peers, rows_ky, 2, groups_y, cells_y)
    out = np.zeros((groups_y, 2, cells_y, 2, peers, 2, rows_ky, 2))
    for place in range(groups_y):
        for side, half in enumerate((place, 1 - place)):
            block = np.moveaxis(full[half, :, :, :, place, :], -1, 0)
            for parity in range(2):
                out[place, parity, :, side, :, parity] = block
    return out.reshape(groups_y, 2, cells_y, 2 * peers * 4 * rows_ky)


def dot(left, right):
    return jnp.dot(left, right, preferred_element_type=jnp.float32)


def forward_y_kernel(flow_ref, table_ref, *out_refs):
    layers, rows, feat_count = out_refs[0].shape
    cells_x = flow_ref.shape[0]
    rows = rows // cells_x
    for x in range(cells_x):
        result = dot(table_ref[...], flow_ref[x]).reshape(4, layers, rows, feat_count)
        for part, out_ref in enumerate(out_refs):
            out_ref[:, x * rows : (x + 1) * rows, :] = result[part]


def forward_y(flow_field, table, layers, rows_ky):
    cells_x, _, feat_count = flow_field.shape
    shape = jax.ShapeDtypeStruct((layers, cells_x * 2 * rows_ky, feat_count), jnp.float32)
    return pl.pallas_call(
        forward_y_kernel,
        out_shape=[shape] * 4,
        compiler_params=SMALL,
        name="forward_y",
    )(flow_field, table)


def flip_both(block, peers):
    pairs = [(place, place ^ 3) for place in range(2 * peers)]
    return lax.ppermute(block, ("gx", "gy"), pairs)


def flip_column(block, peers):
    return lax.ppermute(block, "gx", [(place, place ^ 1) for place in range(peers)])


def flip_core(block):
    return lax.ppermute(block, "gy", [(0, 1), (1, 0)])


def along_z(blocks, peers):
    arrived = []
    for turn, block in zip(turns(len(blocks)), blocks):
        pairs = [(place, place ^ (2 * turn)) for place in range(peers)]
        arrived.append(lax.ppermute(block, "gx", pairs) if turn else block)
    return arrived


def combine_kernel(both_ref, column_ref, core_ref, own_ref, *out_refs):
    for turn, out_ref in enumerate(out_refs):
        out_ref[0] = own_ref[turn] + core_ref[turn]
        out_ref[1] = column_ref[turn] + both_ref[turn]


def combine(both, column, core, own):
    return pl.pallas_call(
        combine_kernel,
        out_shape=[jax.ShapeDtypeStruct((2,) + own.shape[1:], own.dtype)] * own.shape[0],
        compiler_params=SMALL,
        name="combine",
    )(both, column, core, own)


def gather_kernel(*refs):
    for turn, block_ref in enumerate(refs[:-2]):
        refs[-2][turn] = block_ref[0]
        refs[-1][turn] = block_ref[1]


def gather(blocks):
    shape = jax.ShapeDtypeStruct((len(blocks),) + blocks[0].shape[1:], blocks[0].dtype)
    return pl.pallas_call(
        gather_kernel, out_shape=[shape] * 2, compiler_params=SMALL, name="gather"
    )(*blocks)


def mix_kernel(layers, *refs):
    block_refs = refs[:layers]
    weight_ref, forward_high, forward_low, inverse_high, inverse_low, mixed_ref = refs[
        layers : layers + 6
    ]
    back_refs = refs[layers + 6 : 2 * layers + 6]
    order_ref, spread_ref, result_ref = refs[2 * layers + 6 :]
    z, x, _ = quad()
    for turn, block_ref in zip(turns(layers), block_refs):
        for side in range(2):
            order_ref[(z ^ turn) * 2 + (x ^ side)] = block_ref[side]
    feat_count = order_ref.shape[-1]
    count = weight_ref.shape[1]
    channels = weight_ref.shape[2]
    tiles = feat_count // 128
    group = 2 * tiles
    high, low = split_terms(order_ref[...].reshape(-1, feat_count))
    spectrum = (
        dot(forward_high[...], high) + dot(forward_high[...], low) + dot(forward_low[...], high)
    )
    for part in range(2):
        for tile in range(tiles):
            spread_ref[pl.ds(part * tiles + tile, count, stride=group), :] = spectrum[
                part * count : (part + 1) * count, tile * 128 : (tile + 1) * 128
            ]
    rows = lax.broadcasted_iota(jnp.int32, (8, 128), 0) % group
    lane = lax.broadcasted_iota(jnp.int32, (8, 128), 1) < channels
    sign = jnp.where(rows < tiles, -1.0, 1.0)
    for base in range(0, count * group, 8):
        block = spread_ref[base : base + 8, :]
        turned = pltpu.roll(block, channels, 1)
        firsts, seconds = [], []
        for start in range(0, 8, group):
            span = slice(start, start + group)
            left = jnp.concatenate([block[span], turned[span]], axis=0)[:, :channels]
            left_high, left_low = split_terms(left)
            left = jnp.concatenate([left_high, left_low], axis=0)
            product = dot(left, weight_ref[0, (base + start) // group])
            product = product[: 2 * group] + product[2 * group :]
            firsts.append(product[:group])
            seconds.append(product[group:])
        first = jnp.concatenate(firsts, axis=0)
        second = jnp.concatenate(seconds, axis=0)
        real = jnp.where(lane, first, pltpu.roll(second, channels, 1))
        imag = jnp.where(lane, pltpu.roll(first, channels, 1), second)
        crossed = jnp.where(rows < tiles, pltpu.roll(imag, 8 - tiles, 0), pltpu.roll(imag, tiles, 0))
        result_ref[base : base + 8, :] = real + sign * crossed
    parts = []
    for part in range(2):
        parts.append(
            jnp.concatenate(
                [
                    result_ref[pl.ds(part * tiles + tile, count, stride=group), :]
                    for tile in range(tiles)
                ],
                axis=1,
            )
        )
        mixed_ref[0, :, part * feat_count : (part + 1) * feat_count] = parts[part]
    high, low = split_terms(jnp.concatenate(parts, axis=0))
    back = dot(inverse_high[...], high) + dot(inverse_high[...], low) + dot(inverse_low[...], high)
    order_ref[...] = back.reshape(order_ref.shape)
    for turn, back_ref in zip(turns(layers), back_refs):
        for side in range(2):
            back_ref[side] = order_ref[(z ^ turn) * 2 + (x ^ side)]


def mix(blocks, weights, forward_table, inverse_table):
    _, rows, feat_count = blocks[0].shape
    layers = len(blocks)
    count = weights.shape[1]
    scratch = pltpu.VMEM((count * feat_count // 64, 128), jnp.float32)
    mixed, *back = pl.pallas_call(
        functools.partial(mix_kernel, layers),
        out_shape=[jax.ShapeDtypeStruct((1, count, 2 * feat_count), jnp.float32)]
        + [jax.ShapeDtypeStruct(blocks[0].shape, jnp.float32)] * layers,
        scratch_shapes=[pltpu.VMEM((2 * layers, rows, feat_count), jnp.float32), scratch, scratch],
        compiler_params=SMALL,
        name="mix",
    )(*blocks, weights, *split_table(forward_table), *split_table(inverse_table))
    return mixed, back


def output_kernel(
    place_ref, flow_ref, table_ref, local_ref, bias_ref, own_ref, core_ref, column_ref, both_ref,
    out_ref, order_ref, stack_ref, wide_ref, level_ref,
):
    step = pl.program_id(0)
    feat_count = flow_ref.shape[-1]
    channels = local_ref.shape[0]
    width = wide_ref.shape[0]
    pairs = stack_ref.shape[0]
    layers = own_ref.shape[0]
    rows = own_ref.shape[1] // pairs

    @pl.when(step == 0)
    def _():
        z, x, _ = quad()
        for index, turn in enumerate(turns(layers)):
            peer = (z ^ turn) * 2
            order_ref[peer + x] = own_ref[index]
            order_ref[peer + (x ^ 1)] = column_ref[index]
            order_ref[2 * layers + peer + x] = core_ref[index]
            order_ref[2 * layers + peer + (x ^ 1)] = both_ref[index]
        for pair in range(pairs):
            span = slice(pair * rows, (pair + 1) * rows)
            high, low = split_terms(order_ref[:, span, :].reshape(-1, feat_count))
            stack_ref[pair] = jnp.concatenate([high, low, high], axis=0)
        wide_ref[...] = jnp.zeros_like(wide_ref)
        for start in range(0, width, channels):
            span = slice(start, start + channels)
            wide_ref[span, span] = local_ref[...]
            level_ref[:, span] = bias_ref[...].reshape(1, channels)

    table = table_ref[0, step % 2]
    for start in range(0, feat_count, width):
        columns = slice(start, start + width)
        total = (
            dot(table, stack_ref[step // 2, :, columns])
            + dot(flow_ref[0, :, columns], wide_ref[...])
            + level_ref[...]
        )
        out_ref[0, :, columns] = (
            0.5 * total * (1.0 + lax.erf(total * math.sqrt(0.5)))
        ).astype(out_ref.dtype)


def make_output(flow_field, parts, table, local, bias):
    cells_x, cells_y, feat_count = flow_field.shape
    layers, rows, _ = parts[0].shape
    place = jnp.reshape(lax.axis_index("gy"), (1,))
    whole = lambda array: pl.BlockSpec(array.shape, lambda i, p: (0,) * array.ndim)
    block = pl.BlockSpec((1, cells_y, feat_count), lambda i, p: (i, 0, 0))
    return pl.pallas_call(
        output_kernel,
        grid_spec=pltpu.PrefetchScalarGridSpec(
            num_scalar_prefetch=1,
            grid=(cells_x,),
            in_specs=[
                block,
                pl.BlockSpec((1,) + table.shape[1:], lambda i, p: (p[0], 0, 0, 0)),
                whole(local),
                whole(bias),
            ]
            + [whole(part) for part in parts],
            out_specs=block,
            scratch_shapes=[
                pltpu.VMEM((4 * layers, rows, feat_count), jnp.float32),
                pltpu.VMEM((cells_x // 2, table.shape[-1], feat_count), jnp.bfloat16),
                pltpu.VMEM((WIDTH, WIDTH), jnp.bfloat16),
                pltpu.VMEM((1, WIDTH), jnp.float32),
            ],
        ),
        out_shape=jax.ShapeDtypeStruct(flow_field.shape, jnp.bfloat16),
        compiler_params=SMALL,
        name="make_output",
    )(place, flow_field, table, local, bias, *parts)


def row_body(flow_field, spectral_weight, local_weight, bias_terms):
    cells_x, cells_y, feat_count = flow_field.shape
    peers = lax.axis_size("gx")
    groups_y = lax.axis_size("gy")
    rows_ky = MY // groups_y // peers
    forward_scale = 1.0 / math.sqrt(cells_x * peers * cells_y * groups_y)
    inverse_scale = 1.0 / math.sqrt(MX * MY)

    table = forward_y_table(cells_y, groups_y, peers, rows_ky)
    both, core, column, own = forward_y(flow_field, table, peers // 2, rows_ky)
    blocks = combine(flip_both(both, peers), flip_column(column, peers), flip_core(core), own)
    mixed, back = mix(
        along_z(blocks, peers),
        spectral_weight,
        forward_x_table(cells_x, peers, rows_ky) * forward_scale,
        inverse_x_table(cells_x, peers, rows_ky),
    )
    own, column = gather(along_z(back, peers))
    parts = [own, flip_core(own), flip_column(column, peers), flip_both(column, peers)]
    high, low = split_table(inverse_y_table(cells_y, groups_y, peers, rows_ky) * inverse_scale)
    table = np.concatenate([high, high, low], axis=-1)
    return make_output(flow_field, parts, table, local_weight, bias_terms), mixed


def body(flow_field, spectral_weight, local_weight, bias_terms):
    peers = lax.axis_size("gx")
    paired = lax.axis_size("gy") == 2 and peers & (peers - 1) == 0
    if paired and spectral_weight.shape[1] == 2 * MX and WIDTH % local_weight.shape[0] == 0:
        return row_body(flow_field, spectral_weight, local_weight, bias_terms)
    return general_body(flow_field, spectral_weight, local_weight, bias_terms)


def solution(mesh):
    placed = (P(("group", "gx"), "gy", None), P("gy", "gx", None, None), P(), P())
    return jax.shard_map(
        body,
        mesh=mesh,
        in_specs=placed,
        out_specs=(P(("group", "gx"), "gy", None), P(("group", "gy"), "gx", None)),
        check_vma=False,
    )
```

```python
import functools
import math

import jax
import jax.numpy as jnp
import ml_dtypes
import numpy as np
from jax import lax
from jax.experimental import pallas as pl
from jax.experimental.pallas import tpu as pltpu
from jax.sharding import PartitionSpec as P

MX = 32
MY = 32


def wave_number(index, count):
    return jnp.where(index < count // 2, index, index - count)


def phase_table(waves, places, extent):
    product = waves[:, None] * places[None, :] % extent
    return 2.0 * math.pi / extent * product.astype(jnp.float32)


def row_tables(ky_rows, kx_rows, x_places, extent, width):
    angle = phase_table(wave_number(kx_rows, MX), x_places, extent)
    select = (ky_rows[:, None] == jnp.arange(width, dtype=jnp.int32)[None, :]).astype(jnp.float32)
    cosine = jnp.cos(angle)[:, :, None] * select[:, None, :]
    sine_part = jnp.sin(angle)[:, :, None] * select[:, None, :]
    return (cosine, sine_part)


def forward_rows(y_local, ky_rows, kx_rows, x_places, extent):
    cosine, sine_part = row_tables(ky_rows, kx_rows, x_places, extent, y_local.shape[0])
    real_in = y_local[:, 0]
    imag_in = y_local[:, 1]

    def contract(table, values):
        return jnp.einsum("rxk,kxf->rf", table, values, precision=lax.Precision.HIGHEST)

    real_out = contract(cosine, real_in) + contract(sine_part, imag_in)
    imag_out = contract(cosine, imag_in) - contract(sine_part, real_in)
    return jnp.concatenate([real_out, imag_out], axis=1)


def inverse_rows(running, shard_rows, ky_rows, kx_rows, x_places, extent):
    cosine, sine_part = row_tables(ky_rows, kx_rows, x_places, extent, running.shape[0])
    feat_count = shard_rows.shape[1] // 2
    real_part = shard_rows[:, :feat_count]
    imag_part = shard_rows[:, feat_count:]

    def contract(table, values):
        return jnp.einsum("rxk,rf->kxf", table, values, precision=lax.Precision.HIGHEST)

    new_real = contract(cosine, real_part) - contract(sine_part, imag_part)
    new_imag = contract(cosine, imag_part) + contract(sine_part, real_part)
    return jnp.stack([new_real, new_imag], axis=1)


def general_body(flow_field, spectral_weight, local_weight, bias_terms):
    cells_x, cells_y, feat_count = flow_field.shape
    channels = local_weight.shape[0]
    planes = feat_count // channels
    groups_x = lax.axis_size("gx")
    groups_y = lax.axis_size("gy")
    extent_x = cells_x * groups_x
    extent_y = cells_y * groups_y
    half_width = MY // groups_y
    quota_rows = spectral_weight.shape[1]
    high = lax.Precision.HIGHEST
    x_places = lax.axis_index("gx") * cells_x + jnp.arange(cells_x, dtype=jnp.int32)
    y_places = lax.axis_index("gy") * cells_y + jnp.arange(cells_y, dtype=jnp.int32)
    y_angle = phase_table(wave_number(jnp.arange(MY, dtype=jnp.int32), MY), y_places, extent_y)
    y_table = (
        jnp.stack([jnp.cos(y_angle), -jnp.sin(y_angle)], axis=1)
        .reshape(2 * MY, cells_y)
        .astype(jnp.bfloat16)
    )
    y_local = lax.psum_scatter(
        jnp.einsum("qy,xyf->qxf", y_table, flow_field, preferred_element_type=jnp.float32),
        "gy",
        scatter_dimension=0,
        tiled=True,
    )
    y_local = y_local.reshape(half_width, 2, cells_x, feat_count)
    rest_index = jnp.arange(lax.axis_size("gx") * quota_rows, dtype=jnp.int32)
    spectrum = lax.psum_scatter(
        forward_rows(y_local, rest_index // MX, rest_index % MX, x_places, extent_x),
        "gx",
        scatter_dimension=0,
        tiled=True,
    )
    spectrum = spectrum * (1.0 / math.sqrt(extent_x * extent_y))
    coeffs = spectrum.reshape(quota_rows, 2, planes, channels)
    weights = spectral_weight[0].astype(jnp.float32)
    product = jnp.einsum("rpzc,rco->rpzo", coeffs, weights, precision=high)
    mixed_real = product[:, 0, :, :channels] - product[:, 1, :, channels:]
    mixed_imag = product[:, 0, :, channels:] + product[:, 1, :, :channels]
    mixed_local = jnp.stack([mixed_real, mixed_imag], axis=1).reshape(quota_rows, 2 * feat_count)
    pointwise = jnp.einsum(
        "xyzc,co->xyzo",
        flow_field.reshape(cells_x, cells_y, planes, channels),
        local_weight,
        preferred_element_type=jnp.float32,
    )
    start_half = jnp.zeros((half_width, 2, cells_x, feat_count), jnp.float32)
    shard_rows = lax.all_gather(mixed_local, "gx", axis=0, tiled=True)
    rest_index = jnp.arange(shard_rows.shape[0], dtype=jnp.int32)
    back_half = inverse_rows(
        start_half, shard_rows, rest_index // MX, rest_index % MX, x_places, extent_x
    )
    back_whole = lax.all_gather(back_half, "gy", axis=0, tiled=True)
    y_cos = jnp.cos(y_angle)
    y_sin = jnp.sin(y_angle)
    spectral = (
        jnp.einsum("kn,kxf->xnf", y_cos, back_whole[:, 0], precision=high)
        - jnp.einsum("kn,kxf->xnf", y_sin, back_whole[:, 1], precision=high)
    ) * (1.0 / math.sqrt(MX * MY))
    total = spectral.reshape(cells_x, cells_y, planes, channels) + pointwise + bias_terms
    output = (
        jax.nn.gelu(total, approximate=False)
        .reshape(cells_x, cells_y, feat_count)
        .astype(jnp.bfloat16)
    )
    return (output, mixed_local.reshape(1, quota_rows, 2 * feat_count))


SMALL = pltpu.CompilerParams(vmem_limit_bytes=20 * 1024 * 1024)
WIDTH = 256


def angles(count, places, extent):
    index = np.arange(count)
    waves = np.where(index < count // 2, index, index - count)
    product = (waves[:, None] * np.asarray(places)[None, :]) % extent
    return (np.float32(2.0 * math.pi / extent) * product.astype(np.float32)).astype(np.float64)


def split_table(table):
    high = table.astype(ml_dtypes.bfloat16)
    low = (table - high.astype(np.float64)).astype(ml_dtypes.bfloat16)
    return high, low


def split_terms(values):
    high = values.astype(jnp.bfloat16)
    low = (values - high.astype(jnp.float32)).astype(jnp.bfloat16)
    return high, low


def quad():
    place = lax.axis_index("gx")
    return place // 2, place % 2, lax.axis_index("gy")


def turns(layers):
    return list(range(layers - 1, 0, -1)) + [0]


def forward_y_table(cells_y, groups_y, peers, rows_ky):
    z, x, y = quad()
    layers = peers // 2
    row = jnp.arange(2 * MY, dtype=jnp.int32)
    block = row // (2 * rows_ky)
    turn = layers - 1 - block // 2 % layers
    side = y ^ (1 - block // peers)
    column = x ^ side
    half = side ^ (block % 2)
    owner = half * peers + (z ^ turn) * 2 + column
    index = owner * rows_ky + row // 2 % rows_ky
    y_places = y * cells_y + jnp.arange(cells_y, dtype=jnp.int32)
    angle = phase_table(wave_number(index, MY), y_places, cells_y * groups_y)
    return jnp.where(row[:, None] % 2 == 0, jnp.cos(angle), -jnp.sin(angle)).astype(jnp.bfloat16)


def forward_x_table(cells_x, peers, rows_ky):
    extent = cells_x * peers
    angle = angles(MX, np.arange(extent), extent)
    cosine, sine = np.cos(angle), np.sin(angle)
    out = np.zeros((2, rows_ky, MX, extent, rows_ky, 2))
    for row in range(rows_ky):
        out[0, row, :, :, row, 0] = cosine
        out[0, row, :, :, row, 1] = sine
        out[1, row, :, :, row, 1] = cosine
        out[1, row, :, :, row, 0] = -sine
    return out.reshape(2 * rows_ky * MX, extent * rows_ky * 2)


def inverse_x_table(cells_x, peers, rows_ky):
    extent = cells_x * peers
    angle = angles(MX, np.arange(extent), extent)
    cosine, sine = np.cos(angle).T, np.sin(angle).T
    out = np.zeros((extent, rows_ky, 2, 2, rows_ky, MX))
    for row in range(rows_ky):
        out[:, row, 0, 0, row, :] = cosine
        out[:, row, 0, 1, row, :] = -sine
        out[:, row, 1, 1, row, :] = cosine
        out[:, row, 1, 0, row, :] = sine
    return out.reshape(extent * rows_ky * 2, 2 * rows_ky * MX)


def inverse_y_table(cells_y, groups_y, peers, rows_ky):
    extent = cells_y * groups_y
    angle = angles(MY, np.arange(extent), extent)
    full = np.stack([np.cos(angle), -np.sin(angle)], axis=1)
    full = full.reshape(groups_y, peers, rows_ky, 2, groups_y, cells_y)
    out = np.zeros((groups_y, 2, cells_y, 2, peers, 2, rows_ky, 2))
    for place in range(groups_y):
        for side, half in enumerate((place, 1 - place)):
            block = np.moveaxis(full[half, :, :, :, place, :], -1, 0)
            for parity in range(2):
                out[place, parity, :, side, :, parity] = block
    return out.reshape(groups_y, 2, cells_y, 2 * peers * 4 * rows_ky)


def dot(left, right):
    return jnp.dot(left, right, preferred_element_type=jnp.float32)


def forward_y_kernel(flow_ref, table_ref, send_ref, keep_ref):
    layers, _, rows, feat_count = send_ref.shape
    cells_x = flow_ref.shape[0]
    rows = rows // cells_x
    for x in range(cells_x):
        result = dot(table_ref[...], flow_ref[x]).reshape(2, layers, 2, rows, feat_count)
        send_ref[:, :, x * rows : (x + 1) * rows, :] = result[0]
        keep_ref[:, :, x * rows : (x + 1) * rows, :] = result[1]


def forward_y(flow_field, table, layers, rows_ky):
    cells_x, _, feat_count = flow_field.shape
    shape = jax.ShapeDtypeStruct((layers, 2, cells_x * 2 * rows_ky, feat_count), jnp.float32)
    return pl.pallas_call(
        forward_y_kernel,
        out_shape=[shape] * 2,
        compiler_params=SMALL,
        name="forward_y",
    )(flow_field, table)


def flip_core(block):
    return lax.ppermute(block, "gy", [(0, 1), (1, 0)])


def along_columns(blocks, peers):
    arrived = []
    for turn, block in zip(turns(len(blocks)), blocks):
        pairs = [
            (2 * place + core, 2 * (place ^ (2 * turn + core)) + core)
            for place in range(peers)
            for core in range(2)
        ]
        arrived.append(lax.ppermute(block, ("gx", "gy"), pairs))
    return arrived


def small_call(kernel, out_shape, name):
    return pl.pallas_call(kernel, out_shape=out_shape, compiler_params=SMALL, name=name)


def add_kernel(keep_ref, arrived_ref, *out_refs):
    for turn, out_ref in enumerate(out_refs):
        out_ref[...] = keep_ref[turn] + arrived_ref[turn]


def add_blocks(keep, arrived):
    shape = jax.ShapeDtypeStruct(keep.shape[1:], keep.dtype)
    return small_call(add_kernel, [shape] * keep.shape[0], "add_blocks")(keep, arrived)


def join_kernel(keep_ref, arrived_ref, *out_refs):
    for turn, out_ref in enumerate(out_refs):
        out_ref[0] = keep_ref[turn]
        out_ref[1] = arrived_ref[turn]


def join_blocks(keep, arrived):
    shape = jax.ShapeDtypeStruct((2,) + keep.shape[1:], keep.dtype)
    return small_call(join_kernel, [shape] * keep.shape[0], "join_blocks")(keep, arrived)


def second_kernel(*refs):
    for turn, block_ref in enumerate(refs[:-1]):
        refs[-1][turn] = block_ref[1]


def second_halves(blocks):
    shape = jax.ShapeDtypeStruct((len(blocks),) + blocks[0].shape[1:], blocks[0].dtype)
    return small_call(second_kernel, shape, "second_halves")(*blocks)


def stack_kernel(*refs):
    for turn, block_ref in enumerate(refs[:-1]):
        refs[-1][turn] = block_ref[...]


def stack_blocks(blocks):
    shape = jax.ShapeDtypeStruct((len(blocks),) + blocks[0].shape, blocks[0].dtype)
    return small_call(stack_kernel, shape, "stack_blocks")(*blocks)


def mix_kernel(layers, *refs):
    block_refs = refs[:layers]
    arrived_ref, weight_ref, forward_high, forward_low, inverse_high, inverse_low = refs[
        layers : layers + 6
    ]
    mixed_ref, send_ref, keep_ref, order_ref, spread_ref, result_ref = refs[layers + 6 :]
    z, x, y = quad()
    column = x ^ y
    for index, turn in enumerate(turns(layers)):
        order_ref[(z ^ turn) * 2 + column] = block_refs[index][0]
        order_ref[(z ^ turn) * 2 + (column ^ 1)] = arrived_ref[index]
    feat_count = order_ref.shape[-1]
    count = weight_ref.shape[1]
    channels = weight_ref.shape[2]
    tiles = feat_count // 128
    group = 2 * tiles
    high, low = split_terms(order_ref[...].reshape(-1, feat_count))
    spectrum = (
        dot(forward_high[...], high) + dot(forward_high[...], low) + dot(forward_low[...], high)
    )
    for part in range(2):
        for tile in range(tiles):
            spread_ref[pl.ds(part * tiles + tile, count, stride=group), :] = spectrum[
                part * count : (part + 1) * count, tile * 128 : (tile + 1) * 128
            ]
    rows = lax.broadcasted_iota(jnp.int32, (8, 128), 0) % group
    lane = lax.broadcasted_iota(jnp.int32, (8, 128), 1) < channels
    sign = jnp.where(rows < tiles, -1.0, 1.0)
    for base in range(0, count * group, 8):
        block = spread_ref[base : base + 8, :]
        turned = pltpu.roll(block, channels, 1)
        firsts, seconds = [], []
        for start in range(0, 8, group):
            span = slice(start, start + group)
            left = jnp.concatenate([block[span], turned[span]], axis=0)[:, :channels]
            left_high, left_low = split_terms(left)
            left = jnp.concatenate([left_high, left_low], axis=0)
            product = dot(left, weight_ref[0, (base + start) // group])
            product = product[: 2 * group] + product[2 * group :]
            firsts.append(product[:group])
            seconds.append(product[group:])
        first = jnp.concatenate(firsts, axis=0)
        second = jnp.concatenate(seconds, axis=0)
        real = jnp.where(lane, first, pltpu.roll(second, channels, 1))
        imag = jnp.where(lane, pltpu.roll(first, channels, 1), second)
        crossed = jnp.where(rows < tiles, pltpu.roll(imag, 8 - tiles, 0), pltpu.roll(imag, tiles, 0))
        result_ref[base : base + 8, :] = real + sign * crossed
    parts = []
    for part in range(2):
        parts.append(
            jnp.concatenate(
                [
                    result_ref[pl.ds(part * tiles + tile, count, stride=group), :]
                    for tile in range(tiles)
                ],
                axis=1,
            )
        )
        mixed_ref[0, :, part * feat_count : (part + 1) * feat_count] = parts[part]
    high, low = split_terms(jnp.concatenate(parts, axis=0))
    back = dot(inverse_high[...], high) + dot(inverse_high[...], low) + dot(inverse_low[...], high)
    order_ref[...] = back.reshape(order_ref.shape)
    for index, turn in enumerate(turns(layers)):
        send_ref[index] = order_ref[(z ^ turn) * 2 + (column ^ 1)]
        keep_ref[index] = order_ref[(z ^ turn) * 2 + column]


def mix(blocks, arrived, weights, forward_table, inverse_table):
    layers, rows, feat_count = arrived.shape
    count = weights.shape[1]
    scratch = pltpu.VMEM((count * feat_count // 64, 128), jnp.float32)
    return pl.pallas_call(
        functools.partial(mix_kernel, layers),
        out_shape=[jax.ShapeDtypeStruct((1, count, 2 * feat_count), jnp.float32)]
        + [jax.ShapeDtypeStruct(arrived.shape, jnp.float32)] * 2,
        scratch_shapes=[pltpu.VMEM((2 * layers, rows, feat_count), jnp.float32), scratch, scratch],
        compiler_params=SMALL,
        name="mix",
    )(*blocks, arrived, weights, *split_table(forward_table), *split_table(inverse_table))


def output_kernel(
    place_ref, flow_ref, table_ref, local_ref, bias_ref, own_ref, core_ref,
    out_ref, order_ref, stack_ref, wide_ref, level_ref,
):
    step = pl.program_id(0)
    feat_count = flow_ref.shape[-1]
    channels = local_ref.shape[0]
    width = wide_ref.shape[0]
    pairs = stack_ref.shape[0]
    layers = own_ref.shape[0]
    rows = own_ref.shape[2] // pairs

    @pl.when(step == 0)
    def _():
        z, x, y = quad()
        for index, turn in enumerate(turns(layers)):
            for side in range(2):
                peer = 2 * layers * side + (z ^ turn) * 2
                order_ref[peer + (x ^ y)] = own_ref[index, side]
                order_ref[peer + (x ^ y ^ 1)] = core_ref[index, 1 - side]
        for pair in range(pairs):
            span = slice(pair * rows, (pair + 1) * rows)
            high, low = split_terms(order_ref[:, span, :].reshape(-1, feat_count))
            stack_ref[pair] = jnp.concatenate([high, low, high], axis=0)
        wide_ref[...] = jnp.zeros_like(wide_ref)
        for start in range(0, width, channels):
            span = slice(start, start + channels)
            wide_ref[span, span] = local_ref[...]
            level_ref[:, span] = bias_ref[...].reshape(1, channels)

    table = table_ref[0, step % 2]
    for start in range(0, feat_count, width):
        columns = slice(start, start + width)
        total = (
            dot(table, stack_ref[step // 2, :, columns])
            + dot(flow_ref[0, :, columns], wide_ref[...])
            + level_ref[...]
        )
        out_ref[0, :, columns] = (
            0.5 * total * (1.0 + lax.erf(total * math.sqrt(0.5)))
        ).astype(out_ref.dtype)


def make_output(flow_field, parts, table, local, bias):
    cells_x, cells_y, feat_count = flow_field.shape
    layers, _, rows, _ = parts[0].shape
    place = jnp.reshape(lax.axis_index("gy"), (1,))
    whole = lambda array: pl.BlockSpec(array.shape, lambda i, p: (0,) * array.ndim)
    block = pl.BlockSpec((1, cells_y, feat_count), lambda i, p: (i, 0, 0))
    return pl.pallas_call(
        output_kernel,
        grid_spec=pltpu.PrefetchScalarGridSpec(
            num_scalar_prefetch=1,
            grid=(cells_x,),
            in_specs=[
                block,
                pl.BlockSpec((1,) + table.shape[1:], lambda i, p: (p[0], 0, 0, 0)),
                whole(local),
                whole(bias),
            ]
            + [whole(part) for part in parts],
            out_specs=block,
            scratch_shapes=[
                pltpu.VMEM((4 * layers, rows, feat_count), jnp.float32),
                pltpu.VMEM((cells_x // 2, table.shape[-1], feat_count), jnp.bfloat16),
                pltpu.VMEM((WIDTH, WIDTH), jnp.bfloat16),
                pltpu.VMEM((1, WIDTH), jnp.float32),
            ],
        ),
        out_shape=jax.ShapeDtypeStruct(flow_field.shape, jnp.bfloat16),
        compiler_params=SMALL,
        name="make_output",
    )(place, flow_field, table, local, bias, *parts)


def row_body(flow_field, spectral_weight, local_weight, bias_terms):
    cells_x, cells_y, feat_count = flow_field.shape
    peers = lax.axis_size("gx")
    groups_y = lax.axis_size("gy")
    rows_ky = MY // groups_y // peers
    forward_scale = 1.0 / math.sqrt(cells_x * peers * cells_y * groups_y)
    inverse_scale = 1.0 / math.sqrt(MX * MY)

    table = forward_y_table(cells_y, groups_y, peers, rows_ky)
    send, keep = forward_y(flow_field, table, peers // 2, rows_ky)
    blocks = along_columns(add_blocks(keep, flip_core(send)), peers)
    mixed, send, keep = mix(
        blocks,
        flip_core(second_halves(blocks)),
        spectral_weight,
        forward_x_table(cells_x, peers, rows_ky) * forward_scale,
        inverse_x_table(cells_x, peers, rows_ky),
    )
    own = stack_blocks(along_columns(join_blocks(keep, flip_core(send)), peers))
    parts = [own, flip_core(own)]
    high, low = split_table(inverse_y_table(cells_y, groups_y, peers, rows_ky) * inverse_scale)
    table = np.concatenate([high, high, low], axis=-1)
    return make_output(flow_field, parts, table, local_weight, bias_terms), mixed


def body(flow_field, spectral_weight, local_weight, bias_terms):
    peers = lax.axis_size("gx")
    paired = lax.axis_size("gy") == 2 and peers & (peers - 1) == 0
    if paired and spectral_weight.shape[1] == 2 * MX and WIDTH % local_weight.shape[0] == 0:
        return row_body(flow_field, spectral_weight, local_weight, bias_terms)
    return general_body(flow_field, spectral_weight, local_weight, bias_terms)


def solution(mesh):
    placed = (P(("group", "gx"), "gy", None), P("gy", "gx", None, None), P(), P())
    return jax.shard_map(
        body,
        mesh=mesh,
        in_specs=placed,
        out_specs=(P(("group", "gx"), "gy", None), P(("group", "gy"), "gx", None)),
        check_vma=False,
    )
```

```python
import functools
import math

import jax
import jax.numpy as jnp
import ml_dtypes
import numpy as np
from jax import lax
from jax.experimental import pallas as pl
from jax.experimental.pallas import tpu as pltpu
from jax.sharding import PartitionSpec as P

MX = 32
MY = 32


def wave_number(index, count):
    return jnp.where(index < count // 2, index, index - count)


def phase_table(waves, places, extent):
    product = waves[:, None] * places[None, :] % extent
    return 2.0 * math.pi / extent * product.astype(jnp.float32)


def row_tables(ky_rows, kx_rows, x_places, extent, width):
    angle = phase_table(wave_number(kx_rows, MX), x_places, extent)
    select = (ky_rows[:, None] == jnp.arange(width, dtype=jnp.int32)[None, :]).astype(jnp.float32)
    cosine = jnp.cos(angle)[:, :, None] * select[:, None, :]
    sine_part = jnp.sin(angle)[:, :, None] * select[:, None, :]
    return (cosine, sine_part)


def forward_rows(y_local, ky_rows, kx_rows, x_places, extent):
    cosine, sine_part = row_tables(ky_rows, kx_rows, x_places, extent, y_local.shape[0])
    real_in = y_local[:, 0]
    imag_in = y_local[:, 1]

    def contract(table, values):
        return jnp.einsum("rxk,kxf->rf", table, values, precision=lax.Precision.HIGHEST)

    real_out = contract(cosine, real_in) + contract(sine_part, imag_in)
    imag_out = contract(cosine, imag_in) - contract(sine_part, real_in)
    return jnp.concatenate([real_out, imag_out], axis=1)


def inverse_rows(running, shard_rows, ky_rows, kx_rows, x_places, extent):
    cosine, sine_part = row_tables(ky_rows, kx_rows, x_places, extent, running.shape[0])
    feat_count = shard_rows.shape[1] // 2
    real_part = shard_rows[:, :feat_count]
    imag_part = shard_rows[:, feat_count:]

    def contract(table, values):
        return jnp.einsum("rxk,rf->kxf", table, values, precision=lax.Precision.HIGHEST)

    new_real = contract(cosine, real_part) - contract(sine_part, imag_part)
    new_imag = contract(cosine, imag_part) + contract(sine_part, real_part)
    return jnp.stack([new_real, new_imag], axis=1)


def general_body(flow_field, spectral_weight, local_weight, bias_terms):
    cells_x, cells_y, feat_count = flow_field.shape
    channels = local_weight.shape[0]
    planes = feat_count // channels
    groups_x = lax.axis_size("gx")
    groups_y = lax.axis_size("gy")
    extent_x = cells_x * groups_x
    extent_y = cells_y * groups_y
    half_width = MY // groups_y
    quota_rows = spectral_weight.shape[1]
    high = lax.Precision.HIGHEST
    x_places = lax.axis_index("gx") * cells_x + jnp.arange(cells_x, dtype=jnp.int32)
    y_places = lax.axis_index("gy") * cells_y + jnp.arange(cells_y, dtype=jnp.int32)
    y_angle = phase_table(wave_number(jnp.arange(MY, dtype=jnp.int32), MY), y_places, extent_y)
    y_table = (
        jnp.stack([jnp.cos(y_angle), -jnp.sin(y_angle)], axis=1)
        .reshape(2 * MY, cells_y)
        .astype(jnp.bfloat16)
    )
    y_local = lax.psum_scatter(
        jnp.einsum("qy,xyf->qxf", y_table, flow_field, preferred_element_type=jnp.float32),
        "gy",
        scatter_dimension=0,
        tiled=True,
    )
    y_local = y_local.reshape(half_width, 2, cells_x, feat_count)
    rest_index = jnp.arange(lax.axis_size("gx") * quota_rows, dtype=jnp.int32)
    spectrum = lax.psum_scatter(
        forward_rows(y_local, rest_index // MX, rest_index % MX, x_places, extent_x),
        "gx",
        scatter_dimension=0,
        tiled=True,
    )
    spectrum = spectrum * (1.0 / math.sqrt(extent_x * extent_y))
    coeffs = spectrum.reshape(quota_rows, 2, planes, channels)
    weights = spectral_weight[0].astype(jnp.float32)
    product = jnp.einsum("rpzc,rco->rpzo", coeffs, weights, precision=high)
    mixed_real = product[:, 0, :, :channels] - product[:, 1, :, channels:]
    mixed_imag = product[:, 0, :, channels:] + product[:, 1, :, :channels]
    mixed_local = jnp.stack([mixed_real, mixed_imag], axis=1).reshape(quota_rows, 2 * feat_count)
    pointwise = jnp.einsum(
        "xyzc,co->xyzo",
        flow_field.reshape(cells_x, cells_y, planes, channels),
        local_weight,
        preferred_element_type=jnp.float32,
    )
    start_half = jnp.zeros((half_width, 2, cells_x, feat_count), jnp.float32)
    shard_rows = lax.all_gather(mixed_local, "gx", axis=0, tiled=True)
    rest_index = jnp.arange(shard_rows.shape[0], dtype=jnp.int32)
    back_half = inverse_rows(
        start_half, shard_rows, rest_index // MX, rest_index % MX, x_places, extent_x
    )
    back_whole = lax.all_gather(back_half, "gy", axis=0, tiled=True)
    y_cos = jnp.cos(y_angle)
    y_sin = jnp.sin(y_angle)
    spectral = (
        jnp.einsum("kn,kxf->xnf", y_cos, back_whole[:, 0], precision=high)
        - jnp.einsum("kn,kxf->xnf", y_sin, back_whole[:, 1], precision=high)
    ) * (1.0 / math.sqrt(MX * MY))
    total = spectral.reshape(cells_x, cells_y, planes, channels) + pointwise + bias_terms
    output = (
        jax.nn.gelu(total, approximate=False)
        .reshape(cells_x, cells_y, feat_count)
        .astype(jnp.bfloat16)
    )
    return (output, mixed_local.reshape(1, quota_rows, 2 * feat_count))


SMALL = pltpu.CompilerParams(vmem_limit_bytes=20 * 1024 * 1024)
WIDTH = 256


def angles(count, places, extent):
    index = np.arange(count)
    waves = np.where(index < count // 2, index, index - count)
    product = (waves[:, None] * np.asarray(places)[None, :]) % extent
    return (np.float32(2.0 * math.pi / extent) * product.astype(np.float32)).astype(np.float64)


def split_table(table):
    high = table.astype(ml_dtypes.bfloat16)
    low = (table - high.astype(np.float64)).astype(ml_dtypes.bfloat16)
    return high, low


def split_terms(values):
    high = values.astype(jnp.bfloat16)
    low = (values - high.astype(jnp.float32)).astype(jnp.bfloat16)
    return high, low


def quad():
    place = lax.axis_index("gx")
    return place // 2, place % 2, lax.axis_index("gy")


def turns(layers):
    half = layers // 2
    return list(range(half, layers)) + list(range(half - 1, -1, -1))


def forward_y_table(cells_y, groups_y, peers, rows_ky):
    z, x, y = quad()
    layers = peers // 2
    row = jnp.arange(2 * MY, dtype=jnp.int32)
    block = row // (2 * rows_ky)
    place = block // 2 % layers
    turn = jnp.where(place < layers // 2, place + layers // 2, layers - 1 - place)
    side = y ^ (1 - block // peers)
    column = x ^ side
    half = side ^ (block % 2)
    owner = half * peers + (z ^ turn) * 2 + column
    index = owner * rows_ky + row // 2 % rows_ky
    y_places = y * cells_y + jnp.arange(cells_y, dtype=jnp.int32)
    angle = phase_table(wave_number(index, MY), y_places, cells_y * groups_y)
    return jnp.where(row[:, None] % 2 == 0, jnp.cos(angle), -jnp.sin(angle)).astype(jnp.bfloat16)


def forward_x_table(cells_x, peers, rows_ky):
    extent = cells_x * peers
    angle = angles(MX, np.arange(extent), extent)
    cosine, sine = np.cos(angle), np.sin(angle)
    out = np.zeros((2, rows_ky, MX, extent, rows_ky, 2))
    for row in range(rows_ky):
        out[0, row, :, :, row, 0] = cosine
        out[0, row, :, :, row, 1] = sine
        out[1, row, :, :, row, 1] = cosine
        out[1, row, :, :, row, 0] = -sine
    return out.reshape(2 * rows_ky * MX, extent * rows_ky * 2)


def inverse_x_table(cells_x, peers, rows_ky):
    extent = cells_x * peers
    angle = angles(MX, np.arange(extent), extent)
    cosine, sine = np.cos(angle).T, np.sin(angle).T
    out = np.zeros((extent, rows_ky, 2, 2, rows_ky, MX))
    for row in range(rows_ky):
        out[:, row, 0, 0, row, :] = cosine
        out[:, row, 0, 1, row, :] = -sine
        out[:, row, 1, 1, row, :] = cosine
        out[:, row, 1, 0, row, :] = sine
    return out.reshape(extent * rows_ky * 2, 2 * rows_ky * MX)


def inverse_y_table(cells_y, groups_y, peers, rows_ky):
    extent = cells_y * groups_y
    angle = angles(MY, np.arange(extent), extent)
    full = np.stack([np.cos(angle), -np.sin(angle)], axis=1)
    full = full.reshape(groups_y, peers, rows_ky, 2, groups_y, cells_y)
    out = np.zeros((groups_y, 2, cells_y, 2, peers, 2, rows_ky, 2))
    for place in range(groups_y):
        for side, half in enumerate((place, 1 - place)):
            block = np.moveaxis(full[half, :, :, :, place, :], -1, 0)
            for parity in range(2):
                out[place, parity, :, side, :, parity] = block
    return out.reshape(groups_y, 2, cells_y, 2 * peers * 4 * rows_ky)


def dot(left, right):
    return jnp.dot(left, right, preferred_element_type=jnp.float32)


def forward_y_kernel(flow_ref, table_ref, send_ref, keep_ref):
    layers, _, rows, feat_count = send_ref.shape
    cells_x = flow_ref.shape[0]
    rows = rows // cells_x
    for x in range(cells_x):
        result = dot(table_ref[...], flow_ref[x]).reshape(2, layers, 2, rows, feat_count)
        send_ref[:, :, x * rows : (x + 1) * rows, :] = result[0]
        keep_ref[:, :, x * rows : (x + 1) * rows, :] = result[1]


def forward_y(flow_field, table, layers, rows_ky):
    cells_x, _, feat_count = flow_field.shape
    shape = jax.ShapeDtypeStruct((layers, 2, cells_x * 2 * rows_ky, feat_count), jnp.float32)
    return pl.pallas_call(
        forward_y_kernel,
        out_shape=[shape] * 2,
        compiler_params=SMALL,
        name="forward_y",
    )(flow_field, table)


def flip_core(block):
    return lax.ppermute(block, "gy", [(0, 1), (1, 0)])


def along_columns(blocks, peers):
    arrived = []
    for turn, block in zip(turns(len(blocks)), blocks):
        pairs = [
            (2 * place + core, 2 * (place ^ (2 * turn + core)) + core)
            for place in range(peers)
            for core in range(2)
        ]
        arrived.append(lax.ppermute(block, ("gx", "gy"), pairs))
    return arrived


def small_call(kernel, out_shape, name):
    return pl.pallas_call(kernel, out_shape=out_shape, compiler_params=SMALL, name=name)


def add_kernel(keep_ref, arrived_ref, *out_refs):
    for turn, out_ref in enumerate(out_refs):
        out_ref[...] = keep_ref[turn] + arrived_ref[turn]


def add_blocks(keep, arrived):
    shape = jax.ShapeDtypeStruct(keep.shape[1:], keep.dtype)
    return small_call(add_kernel, [shape] * keep.shape[0], "add_blocks")(keep, arrived)


def join_kernel(keep_ref, arrived_ref, *out_refs):
    for turn, out_ref in enumerate(out_refs):
        out_ref[0] = keep_ref[turn]
        out_ref[1] = arrived_ref[turn]


def join_blocks(keep, arrived):
    shape = jax.ShapeDtypeStruct((2,) + keep.shape[1:], keep.dtype)
    return small_call(join_kernel, [shape] * keep.shape[0], "join_blocks")(keep, arrived)


def mix_kernel(layers, *refs):
    block_refs, arrived_refs = refs[:layers], refs[layers : 2 * layers]
    weight_ref, forward_high, forward_low, inverse_high, inverse_low = refs[
        2 * layers : 2 * layers + 5
    ]
    mixed_ref, send_ref, keep_ref, order_ref, spread_ref, result_ref = refs[2 * layers + 5 :]
    z, x, y = quad()
    column = x ^ y
    for index, turn in enumerate(turns(layers)):
        order_ref[(z ^ turn) * 2 + column] = block_refs[index][0]
        order_ref[(z ^ turn) * 2 + (column ^ 1)] = arrived_refs[index][1]
    feat_count = order_ref.shape[-1]
    count = weight_ref.shape[1]
    channels = weight_ref.shape[2]
    tiles = feat_count // 128
    group = 2 * tiles
    high, low = split_terms(order_ref[...].reshape(-1, feat_count))
    spectrum = (
        dot(forward_high[...], high) + dot(forward_high[...], low) + dot(forward_low[...], high)
    )
    for part in range(2):
        for tile in range(tiles):
            spread_ref[pl.ds(part * tiles + tile, count, stride=group), :] = spectrum[
                part * count : (part + 1) * count, tile * 128 : (tile + 1) * 128
            ]
    rows = lax.broadcasted_iota(jnp.int32, (8, 128), 0) % group
    lane = lax.broadcasted_iota(jnp.int32, (8, 128), 1) < channels
    sign = jnp.where(rows < tiles, -1.0, 1.0)
    for base in range(0, count * group, 8):
        block = spread_ref[base : base + 8, :]
        turned = pltpu.roll(block, channels, 1)
        firsts, seconds = [], []
        for start in range(0, 8, group):
            span = slice(start, start + group)
            left = jnp.concatenate([block[span], turned[span]], axis=0)[:, :channels]
            left_high, left_low = split_terms(left)
            left = jnp.concatenate([left_high, left_low], axis=0)
            product = dot(left, weight_ref[0, (base + start) // group])
            product = product[: 2 * group] + product[2 * group :]
            firsts.append(product[:group])
            seconds.append(product[group:])
        first = jnp.concatenate(firsts, axis=0)
        second = jnp.concatenate(seconds, axis=0)
        real = jnp.where(lane, first, pltpu.roll(second, channels, 1))
        imag = jnp.where(lane, pltpu.roll(first, channels, 1), second)
        crossed = jnp.where(rows < tiles, pltpu.roll(imag, 8 - tiles, 0), pltpu.roll(imag, tiles, 0))
        result_ref[base : base + 8, :] = real + sign * crossed
    parts = []
    for part in range(2):
        parts.append(
            jnp.concatenate(
                [
                    result_ref[pl.ds(part * tiles + tile, count, stride=group), :]
                    for tile in range(tiles)
                ],
                axis=1,
            )
        )
        mixed_ref[0, :, part * feat_count : (part + 1) * feat_count] = parts[part]
    high, low = split_terms(jnp.concatenate(parts, axis=0))
    back = dot(inverse_high[...], high) + dot(inverse_high[...], low) + dot(inverse_low[...], high)
    order_ref[...] = back.reshape(order_ref.shape)
    for index, turn in enumerate(turns(layers)):
        send_ref[index] = order_ref[(z ^ turn) * 2 + (column ^ 1)]
        keep_ref[index] = order_ref[(z ^ turn) * 2 + column]


def mix(blocks, arrived, weights, forward_table, inverse_table):
    layers = len(blocks)
    _, rows, feat_count = blocks[0].shape
    count = weights.shape[1]
    half = jax.ShapeDtypeStruct((layers, rows, feat_count), jnp.float32)
    scratch = pltpu.VMEM((count * feat_count // 64, 128), jnp.float32)
    return pl.pallas_call(
        functools.partial(mix_kernel, layers),
        out_shape=[jax.ShapeDtypeStruct((1, count, 2 * feat_count), jnp.float32), half, half],
        scratch_shapes=[pltpu.VMEM((2 * layers, rows, feat_count), jnp.float32), scratch, scratch],
        compiler_params=SMALL,
        name="mix",
    )(*blocks, *arrived, weights, *split_table(forward_table), *split_table(inverse_table))


def output_kernel(
    layers, place_ref, flow_ref, table_ref, local_ref, bias_ref, *refs
):
    own_refs, core_refs = refs[:layers], refs[layers : 2 * layers]
    out_ref, order_ref, stack_ref, wide_ref, level_ref = refs[2 * layers :]
    step = pl.program_id(0)
    feat_count = flow_ref.shape[-1]
    channels = local_ref.shape[0]
    width = wide_ref.shape[0]
    pairs = stack_ref.shape[0]
    rows = order_ref.shape[1] // pairs

    @pl.when(step == 0)
    def _():
        z, x, y = quad()
        for index, turn in enumerate(turns(layers)):
            for side in range(2):
                peer = 2 * layers * side + (z ^ turn) * 2
                order_ref[peer + (x ^ y)] = own_refs[index][side]
                order_ref[peer + (x ^ y ^ 1)] = core_refs[index][1 - side]
        for pair in range(pairs):
            span = slice(pair * rows, (pair + 1) * rows)
            high, low = split_terms(order_ref[:, span, :].reshape(-1, feat_count))
            stack_ref[pair] = jnp.concatenate([high, low, high], axis=0)
        wide_ref[...] = jnp.zeros_like(wide_ref)
        for start in range(0, width, channels):
            span = slice(start, start + channels)
            wide_ref[span, span] = local_ref[...]
            level_ref[:, span] = bias_ref[...].reshape(1, channels)

    table = table_ref[0, step % 2]
    for start in range(0, feat_count, width):
        columns = slice(start, start + width)
        total = (
            dot(table, stack_ref[step // 2, :, columns])
            + dot(flow_ref[0, :, columns], wide_ref[...])
            + level_ref[...]
        )
        out_ref[0, :, columns] = (
            0.5 * total * (1.0 + lax.erf(total * math.sqrt(0.5)))
        ).astype(out_ref.dtype)


def make_output(flow_field, parts, table, local, bias):
    cells_x, cells_y, feat_count = flow_field.shape
    layers = len(parts) // 2
    rows = parts[0].shape[1]
    place = jnp.reshape(lax.axis_index("gy"), (1,))
    whole = lambda array: pl.BlockSpec(array.shape, lambda i, p: (0,) * array.ndim)
    block = pl.BlockSpec((1, cells_y, feat_count), lambda i, p: (i, 0, 0))
    return pl.pallas_call(
        functools.partial(output_kernel, layers),
        grid_spec=pltpu.PrefetchScalarGridSpec(
            num_scalar_prefetch=1,
            grid=(cells_x,),
            in_specs=[
                block,
                pl.BlockSpec((1,) + table.shape[1:], lambda i, p: (p[0], 0, 0, 0)),
                whole(local),
                whole(bias),
            ]
            + [whole(part) for part in parts],
            out_specs=block,
            scratch_shapes=[
                pltpu.VMEM((4 * layers, rows, feat_count), jnp.float32),
                pltpu.VMEM((cells_x // 2, table.shape[-1], feat_count), jnp.bfloat16),
                pltpu.VMEM((WIDTH, WIDTH), jnp.bfloat16),
                pltpu.VMEM((1, WIDTH), jnp.float32),
            ],
        ),
        out_shape=jax.ShapeDtypeStruct(flow_field.shape, jnp.bfloat16),
        compiler_params=SMALL,
        name="make_output",
    )(place, flow_field, table, local, bias, *parts)


def row_body(flow_field, spectral_weight, local_weight, bias_terms):
    cells_x, cells_y, feat_count = flow_field.shape
    peers = lax.axis_size("gx")
    groups_y = lax.axis_size("gy")
    rows_ky = MY // groups_y // peers
    forward_scale = 1.0 / math.sqrt(cells_x * peers * cells_y * groups_y)
    inverse_scale = 1.0 / math.sqrt(MX * MY)

    table = forward_y_table(cells_y, groups_y, peers, rows_ky)
    send, keep = forward_y(flow_field, table, peers // 2, rows_ky)
    blocks = along_columns(add_blocks(keep, flip_core(send)), peers)
    mixed, send, keep = mix(
        blocks,
        [flip_core(block) for block in blocks],
        spectral_weight,
        forward_x_table(cells_x, peers, rows_ky) * forward_scale,
        inverse_x_table(cells_x, peers, rows_ky),
    )
    own = along_columns(join_blocks(keep, flip_core(send)), peers)
    parts = own + [flip_core(block) for block in own]
    high, low = split_table(inverse_y_table(cells_y, groups_y, peers, rows_ky) * inverse_scale)
    table = np.concatenate([high, high, low], axis=-1)
    return make_output(flow_field, parts, table, local_weight, bias_terms), mixed


def body(flow_field, spectral_weight, local_weight, bias_terms):
    peers = lax.axis_size("gx")
    paired = lax.axis_size("gy") == 2 and peers & (peers - 1) == 0
    if paired and spectral_weight.shape[1] == 2 * MX and WIDTH % local_weight.shape[0] == 0:
        return row_body(flow_field, spectral_weight, local_weight, bias_terms)
    return general_body(flow_field, spectral_weight, local_weight, bias_terms)


def solution(mesh):
    placed = (P(("group", "gx"), "gy", None), P("gy", "gx", None, None), P(), P())
    return jax.shard_map(
        body,
        mesh=mesh,
        in_specs=placed,
        out_specs=(P(("group", "gx"), "gy", None), P(("group", "gy"), "gx", None)),
        check_vma=False,
    )
```

```python
import functools
import math

import jax
import jax.numpy as jnp
import ml_dtypes
import numpy as np
from jax import lax
from jax.experimental import pallas as pl
from jax.experimental.pallas import tpu as pltpu
from jax.sharding import PartitionSpec as P

MX = 32
MY = 32


def wave_number(index, count):
    return jnp.where(index < count // 2, index, index - count)


def phase_table(waves, places, extent):
    product = waves[:, None] * places[None, :] % extent
    return 2.0 * math.pi / extent * product.astype(jnp.float32)


def row_tables(ky_rows, kx_rows, x_places, extent, width):
    angle = phase_table(wave_number(kx_rows, MX), x_places, extent)
    select = (ky_rows[:, None] == jnp.arange(width, dtype=jnp.int32)[None, :]).astype(jnp.float32)
    cosine = jnp.cos(angle)[:, :, None] * select[:, None, :]
    sine_part = jnp.sin(angle)[:, :, None] * select[:, None, :]
    return (cosine, sine_part)


def forward_rows(y_local, ky_rows, kx_rows, x_places, extent):
    cosine, sine_part = row_tables(ky_rows, kx_rows, x_places, extent, y_local.shape[0])
    real_in = y_local[:, 0]
    imag_in = y_local[:, 1]

    def contract(table, values):
        return jnp.einsum("rxk,kxf->rf", table, values, precision=lax.Precision.HIGHEST)

    real_out = contract(cosine, real_in) + contract(sine_part, imag_in)
    imag_out = contract(cosine, imag_in) - contract(sine_part, real_in)
    return jnp.concatenate([real_out, imag_out], axis=1)


def inverse_rows(running, shard_rows, ky_rows, kx_rows, x_places, extent):
    cosine, sine_part = row_tables(ky_rows, kx_rows, x_places, extent, running.shape[0])
    feat_count = shard_rows.shape[1] // 2
    real_part = shard_rows[:, :feat_count]
    imag_part = shard_rows[:, feat_count:]

    def contract(table, values):
        return jnp.einsum("rxk,rf->kxf", table, values, precision=lax.Precision.HIGHEST)

    new_real = contract(cosine, real_part) - contract(sine_part, imag_part)
    new_imag = contract(cosine, imag_part) + contract(sine_part, real_part)
    return jnp.stack([new_real, new_imag], axis=1)


def general_body(flow_field, spectral_weight, local_weight, bias_terms):
    cells_x, cells_y, feat_count = flow_field.shape
    channels = local_weight.shape[0]
    planes = feat_count // channels
    groups_x = lax.axis_size("gx")
    groups_y = lax.axis_size("gy")
    extent_x = cells_x * groups_x
    extent_y = cells_y * groups_y
    half_width = MY // groups_y
    quota_rows = spectral_weight.shape[1]
    high = lax.Precision.HIGHEST
    x_places = lax.axis_index("gx") * cells_x + jnp.arange(cells_x, dtype=jnp.int32)
    y_places = lax.axis_index("gy") * cells_y + jnp.arange(cells_y, dtype=jnp.int32)
    y_angle = phase_table(wave_number(jnp.arange(MY, dtype=jnp.int32), MY), y_places, extent_y)
    y_table = (
        jnp.stack([jnp.cos(y_angle), -jnp.sin(y_angle)], axis=1)
        .reshape(2 * MY, cells_y)
        .astype(jnp.bfloat16)
    )
    y_local = lax.psum_scatter(
        jnp.einsum("qy,xyf->qxf", y_table, flow_field, preferred_element_type=jnp.float32),
        "gy",
        scatter_dimension=0,
        tiled=True,
    )
    y_local = y_local.reshape(half_width, 2, cells_x, feat_count)
    rest_index = jnp.arange(lax.axis_size("gx") * quota_rows, dtype=jnp.int32)
    spectrum = lax.psum_scatter(
        forward_rows(y_local, rest_index // MX, rest_index % MX, x_places, extent_x),
        "gx",
        scatter_dimension=0,
        tiled=True,
    )
    spectrum = spectrum * (1.0 / math.sqrt(extent_x * extent_y))
    coeffs = spectrum.reshape(quota_rows, 2, planes, channels)
    weights = spectral_weight[0].astype(jnp.float32)
    product = jnp.einsum("rpzc,rco->rpzo", coeffs, weights, precision=high)
    mixed_real = product[:, 0, :, :channels] - product[:, 1, :, channels:]
    mixed_imag = product[:, 0, :, channels:] + product[:, 1, :, :channels]
    mixed_local = jnp.stack([mixed_real, mixed_imag], axis=1).reshape(quota_rows, 2 * feat_count)
    pointwise = jnp.einsum(
        "xyzc,co->xyzo",
        flow_field.reshape(cells_x, cells_y, planes, channels),
        local_weight,
        preferred_element_type=jnp.float32,
    )
    start_half = jnp.zeros((half_width, 2, cells_x, feat_count), jnp.float32)
    shard_rows = lax.all_gather(mixed_local, "gx", axis=0, tiled=True)
    rest_index = jnp.arange(shard_rows.shape[0], dtype=jnp.int32)
    back_half = inverse_rows(
        start_half, shard_rows, rest_index // MX, rest_index % MX, x_places, extent_x
    )
    back_whole = lax.all_gather(back_half, "gy", axis=0, tiled=True)
    y_cos = jnp.cos(y_angle)
    y_sin = jnp.sin(y_angle)
    spectral = (
        jnp.einsum("kn,kxf->xnf", y_cos, back_whole[:, 0], precision=high)
        - jnp.einsum("kn,kxf->xnf", y_sin, back_whole[:, 1], precision=high)
    ) * (1.0 / math.sqrt(MX * MY))
    total = spectral.reshape(cells_x, cells_y, planes, channels) + pointwise + bias_terms
    output = (
        jax.nn.gelu(total, approximate=False)
        .reshape(cells_x, cells_y, feat_count)
        .astype(jnp.bfloat16)
    )
    return (output, mixed_local.reshape(1, quota_rows, 2 * feat_count))


SMALL = pltpu.CompilerParams(vmem_limit_bytes=20 * 1024 * 1024)
WIDTH = 256
GELU_TERMS = (
    0.7978849411010742,
    0.03633308410644531,
    -3.259492223151028e-05,
    -5.530622001970187e-05,
    3.964749794249656e-06,
    -1.3226382122866198e-07,
    1.7561855303327434e-09,
)


def angles(count, places, extent):
    index = np.arange(count)
    waves = np.where(index < count // 2, index, index - count)
    product = (waves[:, None] * np.asarray(places)[None, :]) % extent
    return (np.float32(2.0 * math.pi / extent) * product.astype(np.float32)).astype(np.float64)


def split_table(table):
    high = table.astype(ml_dtypes.bfloat16)
    low = (table - high.astype(np.float64)).astype(ml_dtypes.bfloat16)
    return high, low


def split_terms(values):
    high = values.astype(jnp.bfloat16)
    low = (values - high.astype(jnp.float32)).astype(jnp.bfloat16)
    return high, low


def quad():
    place = lax.axis_index("gx")
    return place // 2, place % 2, lax.axis_index("gy")


def turns(layers):
    half = layers // 2
    return list(range(half, layers)) + list(range(half - 1, -1, -1))


def forward_y_table(cells_y, groups_y, peers, rows_ky):
    z, x, y = quad()
    layers = peers // 2
    row = jnp.arange(2 * MY, dtype=jnp.int32)
    block = row // (2 * rows_ky)
    place = block // 2 % layers
    turn = jnp.where(place < layers // 2, place + layers // 2, layers - 1 - place)
    side = y ^ (1 - block // peers)
    column = x ^ side
    half = side ^ (block % 2)
    owner = half * peers + (z ^ turn) * 2 + column
    index = owner * rows_ky + row // 2 % rows_ky
    y_places = y * cells_y + jnp.arange(cells_y, dtype=jnp.int32)
    angle = phase_table(wave_number(index, MY), y_places, cells_y * groups_y)
    return jnp.where(row[:, None] % 2 == 0, jnp.cos(angle), -jnp.sin(angle)).astype(jnp.bfloat16)


def forward_x_table(cells_x, peers, rows_ky):
    extent = cells_x * peers
    angle = angles(MX, np.arange(extent), extent)
    cosine, sine = np.cos(angle), np.sin(angle)
    out = np.zeros((2, rows_ky, MX, extent, rows_ky, 2))
    for row in range(rows_ky):
        out[0, row, :, :, row, 0] = cosine
        out[0, row, :, :, row, 1] = sine
        out[1, row, :, :, row, 1] = cosine
        out[1, row, :, :, row, 0] = -sine
    return out.reshape(2 * rows_ky * MX, extent * rows_ky * 2)


def inverse_x_table(cells_x, peers, rows_ky):
    extent = cells_x * peers
    angle = angles(MX, np.arange(extent), extent)
    cosine, sine = np.cos(angle).T, np.sin(angle).T
    out = np.zeros((extent, rows_ky, 2, 2, rows_ky, MX))
    for row in range(rows_ky):
        out[:, row, 0, 0, row, :] = cosine
        out[:, row, 0, 1, row, :] = -sine
        out[:, row, 1, 1, row, :] = cosine
        out[:, row, 1, 0, row, :] = sine
    out = out.reshape(peers // 2, 2, cells_x * rows_ky * 2, 2 * rows_ky * MX)
    return np.moveaxis(out, 1, 0).reshape(2, -1, 2 * rows_ky * MX)


def inverse_y_table(cells_y, groups_y, peers, rows_ky):
    extent = cells_y * groups_y
    angle = angles(MY, np.arange(extent), extent)
    full = np.stack([np.cos(angle), -np.sin(angle)], axis=1)
    full = full.reshape(groups_y, peers, rows_ky, 2, groups_y, cells_y)
    out = np.zeros((groups_y, 2, cells_y, 2, peers, 2, rows_ky, 2))
    for place in range(groups_y):
        for side, half in enumerate((place, 1 - place)):
            block = np.moveaxis(full[half, :, :, :, place, :], -1, 0)
            for parity in range(2):
                out[place, parity, :, side, :, parity] = block
    return out.reshape(groups_y, 2, cells_y, 2 * peers * 4 * rows_ky)


def dot(left, right):
    return jnp.dot(left, right, preferred_element_type=jnp.float32)


def forward_y_kernel(flow_ref, table_ref, send_ref, keep_ref):
    layers, _, rows, feat_count = send_ref.shape
    cells_x = flow_ref.shape[0]
    rows = rows // cells_x
    for x in range(cells_x):
        result = dot(table_ref[...], flow_ref[x]).reshape(2, layers, 2, rows, feat_count)
        send_ref[:, :, x * rows : (x + 1) * rows, :] = result[0]
        keep_ref[:, :, x * rows : (x + 1) * rows, :] = result[1]


def forward_y(flow_field, table, layers, rows_ky):
    cells_x, _, feat_count = flow_field.shape
    shape = jax.ShapeDtypeStruct((layers, 2, cells_x * 2 * rows_ky, feat_count), jnp.float32)
    return pl.pallas_call(
        forward_y_kernel,
        out_shape=[shape] * 2,
        compiler_params=SMALL,
        name="forward_y",
    )(flow_field, table)


def flip_core(block):
    return lax.ppermute(block, "gy", [(0, 1), (1, 0)])


def along_columns(blocks, peers):
    arrived = []
    for turn, block in zip(turns(len(blocks)), blocks):
        pairs = [
            (2 * place + core, 2 * (place ^ (2 * turn + core)) + core)
            for place in range(peers)
            for core in range(2)
        ]
        arrived.append(lax.ppermute(block, ("gx", "gy"), pairs))
    return arrived


def small_call(kernel, out_shape, name):
    return pl.pallas_call(kernel, out_shape=out_shape, compiler_params=SMALL, name=name)


def add_kernel(keep_ref, arrived_ref, *out_refs):
    for turn, out_ref in enumerate(out_refs):
        out_ref[...] = keep_ref[turn] + arrived_ref[turn]


def add_blocks(keep, arrived):
    shape = jax.ShapeDtypeStruct(keep.shape[1:], keep.dtype)
    return small_call(add_kernel, [shape] * keep.shape[0], "add_blocks")(keep, arrived)


def join_kernel(keep_ref, arrived_ref, *out_refs):
    for turn, out_ref in enumerate(out_refs):
        out_ref[0] = keep_ref[turn]
        out_ref[1] = arrived_ref[turn]


def join_blocks(keep, arrived):
    shape = jax.ShapeDtypeStruct((2,) + keep.shape[1:], keep.dtype)
    return small_call(join_kernel, [shape] * keep.shape[0], "join_blocks")(keep, arrived)


def back_rows(inverse_high, inverse_low, column, modes):
    high, low = split_terms(modes)
    table = inverse_high[column]
    return dot(table, high) + dot(table, low) + dot(inverse_low[column], high)


def store_turns(out_ref, order_ref, z):
    for index, turn in enumerate(turns(out_ref.shape[0])):
        out_ref[index] = order_ref[z ^ turn]


def mix_kernel(layers, *refs):
    block_refs, arrived_refs = refs[:layers], refs[layers : 2 * layers]
    weight_ref, forward_high, forward_low, inverse_high, inverse_low = refs[
        2 * layers : 2 * layers + 5
    ]
    modes_ref, send_ref, order_ref, spread_ref, result_ref = refs[2 * layers + 5 :]
    z, x, y = quad()
    column = x ^ y
    for index, turn in enumerate(turns(layers)):
        order_ref[(z ^ turn) * 2 + column] = block_refs[index][0]
        order_ref[(z ^ turn) * 2 + (column ^ 1)] = arrived_refs[index][1]
    feat_count = order_ref.shape[-1]
    count = weight_ref.shape[1]
    channels = weight_ref.shape[2]
    tiles = feat_count // 128
    group = 2 * tiles
    high, low = split_terms(order_ref[...].reshape(-1, feat_count))
    spectrum = (
        dot(forward_high[...], high) + dot(forward_high[...], low) + dot(forward_low[...], high)
    )
    for part in range(2):
        for tile in range(tiles):
            spread_ref[pl.ds(part * tiles + tile, count, stride=group), :] = spectrum[
                part * count : (part + 1) * count, tile * 128 : (tile + 1) * 128
            ]
    rows = lax.broadcasted_iota(jnp.int32, (8, 128), 0) % group
    lane = lax.broadcasted_iota(jnp.int32, (8, 128), 1) < channels
    sign = jnp.where(rows < tiles, -1.0, 1.0)
    for base in range(0, count * group, 8):
        block = spread_ref[base : base + 8, :]
        turned = pltpu.roll(block, channels, 1)
        firsts, seconds = [], []
        for start in range(0, 8, group):
            span = slice(start, start + group)
            left = jnp.concatenate([block[span], turned[span]], axis=0)[:, :channels]
            left_high, left_low = split_terms(left)
            left = jnp.concatenate([left_high, left_low], axis=0)
            product = dot(left, weight_ref[0, (base + start) // group])
            product = product[: 2 * group] + product[2 * group :]
            firsts.append(product[:group])
            seconds.append(product[group:])
        first = jnp.concatenate(firsts, axis=0)
        second = jnp.concatenate(seconds, axis=0)
        real = jnp.where(lane, first, pltpu.roll(second, channels, 1))
        imag = jnp.where(lane, pltpu.roll(first, channels, 1), second)
        crossed = jnp.where(rows < tiles, pltpu.roll(imag, 8 - tiles, 0), pltpu.roll(imag, tiles, 0))
        result_ref[base : base + 8, :] = real + sign * crossed
    for part in range(2):
        for tile in range(tiles):
            modes_ref[part * count : (part + 1) * count, tile * 128 : (tile + 1) * 128] = (
                result_ref[pl.ds(part * tiles + tile, count, stride=group), :]
            )
    back = back_rows(inverse_high, inverse_low, column ^ 1, modes_ref[...])
    order_ref[:layers] = back.reshape(send_ref.shape)
    store_turns(send_ref, order_ref, z)


def mix(blocks, arrived, weights, forward_table, inverse_tables):
    layers = len(blocks)
    _, rows, feat_count = blocks[0].shape
    count = weights.shape[1]
    scratch = pltpu.VMEM((count * feat_count // 64, 128), jnp.float32)
    return pl.pallas_call(
        functools.partial(mix_kernel, layers),
        out_shape=[
            jax.ShapeDtypeStruct((2 * count, feat_count), jnp.float32),
            jax.ShapeDtypeStruct((layers, rows, feat_count), jnp.float32),
        ],
        scratch_shapes=[pltpu.VMEM((2 * layers, rows, feat_count), jnp.float32), scratch, scratch],
        compiler_params=SMALL,
        name="mix",
    )(*blocks, *arrived, weights, *split_table(forward_table), *inverse_tables)


def keep_kernel(modes_ref, inverse_high, inverse_low, mixed_ref, keep_ref, order_ref):
    z, x, y = quad()
    count = mixed_ref.shape[1]
    feat_count = modes_ref.shape[1]
    for part in range(2):
        mixed_ref[0, :, part * feat_count : (part + 1) * feat_count] = modes_ref[
            part * count : (part + 1) * count
        ]
    back = back_rows(inverse_high, inverse_low, x ^ y, modes_ref[...])
    order_ref[...] = back.reshape(keep_ref.shape)
    store_turns(keep_ref, order_ref, z)


def keep_rows(modes, inverse_tables, like):
    rows, feat_count = modes.shape
    return pl.pallas_call(
        keep_kernel,
        out_shape=[
            jax.ShapeDtypeStruct((1, rows // 2, 2 * feat_count), jnp.float32),
            jax.ShapeDtypeStruct(like.shape, jnp.float32),
        ],
        scratch_shapes=[pltpu.VMEM(like.shape, jnp.float32)],
        compiler_params=SMALL,
        cost_estimate=pl.CostEstimate(
            flops=6 * rows * rows * feat_count, bytes_accessed=2**20, transcendentals=0
        ),
        name="keep_rows",
    )(modes, *inverse_tables)


def gelu(values):
    square = jnp.minimum(values * values, 31.36)
    inner = jnp.full_like(square, GELU_TERMS[-1])
    for term in GELU_TERMS[-2::-1]:
        inner = inner * square + term
    half = 0.5 * values
    return half + half * jnp.tanh(values * inner)


def output_kernel(layers, flow_ref, table_ref, local_ref, bias_ref, *refs):
    own_refs, core_refs = refs[:layers], refs[layers : 2 * layers]
    out_hbm, order_ref, stack_ref, wide_ref, level_ref, done_ref, sent = refs[2 * layers :]
    cells_x, _, feat_count = flow_ref.shape
    channels = local_ref.shape[0]
    pairs = stack_ref.shape[0]
    rows = order_ref.shape[1] // pairs
    z, x, y = quad()
    wide_ref[...] = jnp.zeros_like(wide_ref)
    for start in range(0, WIDTH, channels):
        span = slice(start, start + channels)
        wide_ref[span, span] = local_ref[...]
        level_ref[:, span] = bias_ref[...].reshape(1, channels)
    for index, turn in enumerate(turns(layers)):
        for side in range(2):
            peer = 2 * layers * side + (z ^ turn) * 2
            order_ref[peer + (x ^ y)] = own_refs[index][side]
            order_ref[peer + (x ^ y ^ 1)] = core_refs[index][1 - side]
    copies = []
    for cell in range(cells_x):
        pair = cell // 2
        if cell % 2 == 0:
            span = slice(pair * rows, (pair + 1) * rows)
            high, low = split_terms(order_ref[:, span, :].reshape(-1, feat_count))
            stack_ref[pair] = jnp.concatenate([high, low, high], axis=0)
        for start in range(0, feat_count, WIDTH):
            columns = slice(start, start + WIDTH)
            left = jnp.concatenate([table_ref[y, cell % 2], flow_ref[cell, :, columns]], axis=1)
            right = jnp.concatenate([stack_ref[pair, :, columns], wide_ref[...]], axis=0)
            total = dot(left, right) + level_ref[...]
            done_ref[cell, :, columns] = gelu(total).astype(done_ref.dtype)
        copies.append(pltpu.make_async_copy(done_ref.at[cell], out_hbm.at[cell], sent.at[cell]))
        copies[-1].start()
    for copy in copies:
        copy.wait()


def make_output(flow_field, parts, table, local, bias):
    cells_x, _, feat_count = flow_field.shape
    layers = len(parts) // 2
    rows = parts[0].shape[1]
    return pl.pallas_call(
        functools.partial(output_kernel, layers),
        out_specs=pl.BlockSpec(memory_space=pl.ANY),
        scratch_shapes=[
            pltpu.VMEM((4 * layers, rows, feat_count), jnp.float32),
            pltpu.VMEM((cells_x // 2, table.shape[-1], feat_count), jnp.bfloat16),
            pltpu.VMEM((WIDTH, WIDTH), jnp.bfloat16),
            pltpu.VMEM((1, WIDTH), jnp.float32),
            pltpu.VMEM(flow_field.shape, jnp.bfloat16),
            pltpu.SemaphoreType.DMA((cells_x,)),
        ],
        out_shape=jax.ShapeDtypeStruct(flow_field.shape, jnp.bfloat16),
        compiler_params=SMALL,
        name="make_output",
    )(flow_field, table, local, bias, *parts)


def row_body(flow_field, spectral_weight, local_weight, bias_terms):
    cells_x, cells_y, feat_count = flow_field.shape
    peers = lax.axis_size("gx")
    groups_y = lax.axis_size("gy")
    rows_ky = MY // groups_y // peers
    forward_scale = 1.0 / math.sqrt(cells_x * peers * cells_y * groups_y)
    inverse_scale = 1.0 / math.sqrt(MX * MY)

    table = forward_y_table(cells_y, groups_y, peers, rows_ky)
    send, keep = forward_y(flow_field, table, peers // 2, rows_ky)
    blocks = along_columns(add_blocks(keep, flip_core(send)), peers)
    inverse_tables = split_table(inverse_x_table(cells_x, peers, rows_ky))
    modes, send = mix(
        blocks,
        [flip_core(block) for block in blocks],
        spectral_weight,
        forward_x_table(cells_x, peers, rows_ky) * forward_scale,
        inverse_tables,
    )
    arrived = flip_core(send)
    mixed, keep = keep_rows(modes, inverse_tables, send)
    own = along_columns(join_blocks(keep, arrived), peers)
    parts = own + [flip_core(block) for block in own]
    high, low = split_table(inverse_y_table(cells_y, groups_y, peers, rows_ky) * inverse_scale)
    table = np.concatenate([high, high, low], axis=-1)
    return make_output(flow_field, parts, table, local_weight, bias_terms), mixed


def body(flow_field, spectral_weight, local_weight, bias_terms):
    peers = lax.axis_size("gx")
    paired = lax.axis_size("gy") == 2 and peers & (peers - 1) == 0
    if paired and spectral_weight.shape[1] == 2 * MX and WIDTH % local_weight.shape[0] == 0:
        return row_body(flow_field, spectral_weight, local_weight, bias_terms)
    return general_body(flow_field, spectral_weight, local_weight, bias_terms)


def solution(mesh):
    placed = (P(("group", "gx"), "gy", None), P("gy", "gx", None, None), P(), P())
    return jax.shard_map(
        body,
        mesh=mesh,
        in_specs=placed,
        out_specs=(P(("group", "gx"), "gy", None), P(("group", "gy"), "gx", None)),
        check_vma=False,
    )
```

```python
import functools
import math

import jax
import jax.numpy as jnp
import ml_dtypes
import numpy as np
from jax import lax
from jax.experimental import pallas as pl
from jax.experimental.pallas import tpu as pltpu
from jax.sharding import PartitionSpec as P

MX = 32
MY = 32


def wave_number(index, count):
    return jnp.where(index < count // 2, index, index - count)


def phase_table(waves, places, extent):
    product = waves[:, None] * places[None, :] % extent
    return 2.0 * math.pi / extent * product.astype(jnp.float32)


def row_tables(ky_rows, kx_rows, x_places, extent, width):
    angle = phase_table(wave_number(kx_rows, MX), x_places, extent)
    select = (ky_rows[:, None] == jnp.arange(width, dtype=jnp.int32)[None, :]).astype(jnp.float32)
    cosine = jnp.cos(angle)[:, :, None] * select[:, None, :]
    sine_part = jnp.sin(angle)[:, :, None] * select[:, None, :]
    return (cosine, sine_part)


def forward_rows(y_local, ky_rows, kx_rows, x_places, extent):
    cosine, sine_part = row_tables(ky_rows, kx_rows, x_places, extent, y_local.shape[0])
    real_in = y_local[:, 0]
    imag_in = y_local[:, 1]

    def contract(table, values):
        return jnp.einsum("rxk,kxf->rf", table, values, precision=lax.Precision.HIGHEST)

    real_out = contract(cosine, real_in) + contract(sine_part, imag_in)
    imag_out = contract(cosine, imag_in) - contract(sine_part, real_in)
    return jnp.concatenate([real_out, imag_out], axis=1)


def inverse_rows(running, shard_rows, ky_rows, kx_rows, x_places, extent):
    cosine, sine_part = row_tables(ky_rows, kx_rows, x_places, extent, running.shape[0])
    feat_count = shard_rows.shape[1] // 2
    real_part = shard_rows[:, :feat_count]
    imag_part = shard_rows[:, feat_count:]

    def contract(table, values):
        return jnp.einsum("rxk,rf->kxf", table, values, precision=lax.Precision.HIGHEST)

    new_real = contract(cosine, real_part) - contract(sine_part, imag_part)
    new_imag = contract(cosine, imag_part) + contract(sine_part, real_part)
    return jnp.stack([new_real, new_imag], axis=1)


def general_body(flow_field, spectral_weight, local_weight, bias_terms):
    cells_x, cells_y, feat_count = flow_field.shape
    channels = local_weight.shape[0]
    planes = feat_count // channels
    groups_x = lax.axis_size("gx")
    groups_y = lax.axis_size("gy")
    extent_x = cells_x * groups_x
    extent_y = cells_y * groups_y
    half_width = MY // groups_y
    quota_rows = spectral_weight.shape[1]
    high = lax.Precision.HIGHEST
    x_places = lax.axis_index("gx") * cells_x + jnp.arange(cells_x, dtype=jnp.int32)
    y_places = lax.axis_index("gy") * cells_y + jnp.arange(cells_y, dtype=jnp.int32)
    y_angle = phase_table(wave_number(jnp.arange(MY, dtype=jnp.int32), MY), y_places, extent_y)
    y_table = (
        jnp.stack([jnp.cos(y_angle), -jnp.sin(y_angle)], axis=1)
        .reshape(2 * MY, cells_y)
        .astype(jnp.bfloat16)
    )
    y_local = lax.psum_scatter(
        jnp.einsum("qy,xyf->qxf", y_table, flow_field, preferred_element_type=jnp.float32),
        "gy",
        scatter_dimension=0,
        tiled=True,
    )
    y_local = y_local.reshape(half_width, 2, cells_x, feat_count)
    rest_index = jnp.arange(lax.axis_size("gx") * quota_rows, dtype=jnp.int32)
    spectrum = lax.psum_scatter(
        forward_rows(y_local, rest_index // MX, rest_index % MX, x_places, extent_x),
        "gx",
        scatter_dimension=0,
        tiled=True,
    )
    spectrum = spectrum * (1.0 / math.sqrt(extent_x * extent_y))
    coeffs = spectrum.reshape(quota_rows, 2, planes, channels)
    weights = spectral_weight[0].astype(jnp.float32)
    product = jnp.einsum("rpzc,rco->rpzo", coeffs, weights, precision=high)
    mixed_real = product[:, 0, :, :channels] - product[:, 1, :, channels:]
    mixed_imag = product[:, 0, :, channels:] + product[:, 1, :, :channels]
    mixed_local = jnp.stack([mixed_real, mixed_imag], axis=1).reshape(quota_rows, 2 * feat_count)
    pointwise = jnp.einsum(
        "xyzc,co->xyzo",
        flow_field.reshape(cells_x, cells_y, planes, channels),
        local_weight,
        preferred_element_type=jnp.float32,
    )
    start_half = jnp.zeros((half_width, 2, cells_x, feat_count), jnp.float32)
    shard_rows = lax.all_gather(mixed_local, "gx", axis=0, tiled=True)
    rest_index = jnp.arange(shard_rows.shape[0], dtype=jnp.int32)
    back_half = inverse_rows(
        start_half, shard_rows, rest_index // MX, rest_index % MX, x_places, extent_x
    )
    back_whole = lax.all_gather(back_half, "gy", axis=0, tiled=True)
    y_cos = jnp.cos(y_angle)
    y_sin = jnp.sin(y_angle)
    spectral = (
        jnp.einsum("kn,kxf->xnf", y_cos, back_whole[:, 0], precision=high)
        - jnp.einsum("kn,kxf->xnf", y_sin, back_whole[:, 1], precision=high)
    ) * (1.0 / math.sqrt(MX * MY))
    total = spectral.reshape(cells_x, cells_y, planes, channels) + pointwise + bias_terms
    output = (
        jax.nn.gelu(total, approximate=False)
        .reshape(cells_x, cells_y, feat_count)
        .astype(jnp.bfloat16)
    )
    return (output, mixed_local.reshape(1, quota_rows, 2 * feat_count))


SMALL = pltpu.CompilerParams(vmem_limit_bytes=20 * 1024 * 1024)
WIDTH = 256
GELU_TERMS = (
    0.7978849411010742,
    0.03633308410644531,
    -3.259492223151028e-05,
    -5.530622001970187e-05,
    3.964749794249656e-06,
    -1.3226382122866198e-07,
    1.7561855303327434e-09,
)


def angles(count, places, extent):
    index = np.arange(count)
    waves = np.where(index < count // 2, index, index - count)
    product = (waves[:, None] * np.asarray(places)[None, :]) % extent
    return (np.float32(2.0 * math.pi / extent) * product.astype(np.float32)).astype(np.float64)


def split_table(table):
    high = table.astype(ml_dtypes.bfloat16)
    low = (table - high.astype(np.float64)).astype(ml_dtypes.bfloat16)
    return high, low


def split_terms(values):
    high = values.astype(jnp.bfloat16)
    low = (values - high.astype(jnp.float32)).astype(jnp.bfloat16)
    return high, low


def quad():
    place = lax.axis_index("gx")
    return place // 2, place % 2, lax.axis_index("gy")


def turns(layers):
    half = layers // 2
    return list(range(half, layers)) + list(range(half - 1, -1, -1))


def forward_y_table(cells_y, groups_y, peers, rows_ky):
    z, x, y = quad()
    layers = peers // 2
    row = jnp.arange(2 * MY, dtype=jnp.int32)
    block = row // (2 * rows_ky)
    place = block // 2 % layers
    turn = jnp.where(place < layers // 2, place + layers // 2, layers - 1 - place)
    side = y ^ (1 - block // peers)
    column = x ^ side
    half = side ^ (block % 2)
    owner = half * peers + (z ^ turn) * 2 + column
    index = owner * rows_ky + row // 2 % rows_ky
    y_places = y * cells_y + jnp.arange(cells_y, dtype=jnp.int32)
    angle = phase_table(wave_number(index, MY), y_places, cells_y * groups_y)
    return jnp.where(row[:, None] % 2 == 0, jnp.cos(angle), -jnp.sin(angle)).astype(jnp.bfloat16)


def forward_x_table(cells_x, peers, rows_ky):
    extent = cells_x * peers
    angle = angles(MX, np.arange(extent), extent)
    cosine, sine = np.cos(angle), np.sin(angle)
    out = np.zeros((2, rows_ky, MX, extent, rows_ky, 2))
    for row in range(rows_ky):
        out[0, row, :, :, row, 0] = cosine
        out[0, row, :, :, row, 1] = sine
        out[1, row, :, :, row, 1] = cosine
        out[1, row, :, :, row, 0] = -sine
    return out.reshape(2 * rows_ky * MX, extent * rows_ky * 2)


def inverse_x_table(cells_x, peers, rows_ky):
    extent = cells_x * peers
    angle = angles(MX, np.arange(extent), extent)
    cosine, sine = np.cos(angle).T, np.sin(angle).T
    out = np.zeros((extent, rows_ky, 2, 2, rows_ky, MX))
    for row in range(rows_ky):
        out[:, row, 0, 0, row, :] = cosine
        out[:, row, 0, 1, row, :] = -sine
        out[:, row, 1, 1, row, :] = cosine
        out[:, row, 1, 0, row, :] = sine
    out = out.reshape(peers // 2, 2, cells_x * rows_ky * 2, 2 * rows_ky * MX)
    return np.moveaxis(out, 1, 0).reshape(2, -1, 2 * rows_ky * MX)


def inverse_y_table(cells_y, groups_y, peers, rows_ky):
    extent = cells_y * groups_y
    angle = angles(MY, np.arange(extent), extent)
    full = np.stack([np.cos(angle), -np.sin(angle)], axis=1)
    full = full.reshape(groups_y, peers, rows_ky, 2, groups_y, cells_y)
    out = np.zeros((groups_y, 2, cells_y, peers, 2, rows_ky, 2))
    for y in range(groups_y):
        for column in range(2):
            for peer in range(peers):
                for place in range(2):
                    half = y ^ place ^ column ^ (peer % 2)
                    out[y, column, :, peer, place] = np.moveaxis(full[half, peer, :, :, y], -1, 0)
    return out.reshape(groups_y, 2, cells_y, 4 * peers * rows_ky)


def dot(left, right):
    return jnp.dot(left, right, preferred_element_type=jnp.float32)


def forward_y_kernel(flow_ref, table_ref, send_ref, keep_ref):
    layers, _, rows, feat_count = send_ref.shape
    cells_x = flow_ref.shape[0]
    rows = rows // cells_x
    for x in range(cells_x):
        result = dot(table_ref[...], flow_ref[x]).reshape(2, layers, 2, rows, feat_count)
        send_ref[:, :, x * rows : (x + 1) * rows, :] = result[0]
        keep_ref[:, :, x * rows : (x + 1) * rows, :] = result[1]


def forward_y(flow_field, table, layers, rows_ky):
    cells_x, _, feat_count = flow_field.shape
    shape = jax.ShapeDtypeStruct((layers, 2, cells_x * 2 * rows_ky, feat_count), jnp.float32)
    return pl.pallas_call(
        forward_y_kernel,
        out_shape=[shape] * 2,
        compiler_params=SMALL,
        name="forward_y",
    )(flow_field, table)


def flip_core(block):
    return lax.ppermute(block, "gy", [(0, 1), (1, 0)])


def along_columns(blocks, peers):
    arrived = []
    for turn, block in zip(turns(len(blocks)), blocks):
        pairs = [
            (2 * place + core, 2 * (place ^ (2 * turn + core)) + core)
            for place in range(peers)
            for core in range(2)
        ]
        arrived.append(lax.ppermute(block, ("gx", "gy"), pairs))
    return arrived


def small_call(kernel, out_shape, name):
    return pl.pallas_call(kernel, out_shape=out_shape, compiler_params=SMALL, name=name)


def add_kernel(keep_ref, arrived_ref, *out_refs):
    for turn, out_ref in enumerate(out_refs):
        out_ref[...] = keep_ref[turn] + arrived_ref[turn]


def add_blocks(keep, arrived):
    shape = jax.ShapeDtypeStruct(keep.shape[1:], keep.dtype)
    return small_call(add_kernel, [shape] * keep.shape[0], "add_blocks")(keep, arrived)


def join_kernel(keep_ref, arrived_ref, *out_refs):
    cells_x, rows, _ = out_refs[0].shape
    rows = rows // 2
    for turn, out_ref in enumerate(out_refs):
        for cell in range(cells_x):
            span = slice(cell * rows, (cell + 1) * rows)
            out_ref[cell] = jnp.concatenate(
                [keep_ref[turn, span, :], arrived_ref[turn, span, :]], axis=0
            )


def join_blocks(keep, arrived, cells_x):
    layers, rows, feat_count = keep.shape
    shape = jax.ShapeDtypeStruct((cells_x, 2 * rows // cells_x, feat_count), keep.dtype)
    return small_call(join_kernel, [shape] * layers, "join_blocks")(keep, arrived)


def back_rows(inverse_high, inverse_low, column, modes):
    high, low = split_terms(modes)
    table = inverse_high[column]
    return dot(table, high) + dot(table, low) + dot(inverse_low[column], high)


def store_turns(out_ref, order_ref, z):
    for index, turn in enumerate(turns(out_ref.shape[0])):
        out_ref[index] = order_ref[z ^ turn]


def mix_kernel(layers, *refs):
    block_refs, arrived_refs = refs[:layers], refs[layers : 2 * layers]
    weight_ref, forward_high, forward_low, inverse_high, inverse_low = refs[
        2 * layers : 2 * layers + 5
    ]
    modes_ref, send_ref, order_ref, spread_ref, result_ref = refs[2 * layers + 5 :]
    z, x, y = quad()
    column = x ^ y
    for index, turn in enumerate(turns(layers)):
        order_ref[(z ^ turn) * 2 + column] = block_refs[index][0]
        order_ref[(z ^ turn) * 2 + (column ^ 1)] = arrived_refs[index][1]
    feat_count = order_ref.shape[-1]
    count = weight_ref.shape[1]
    channels = weight_ref.shape[2]
    tiles = feat_count // 128
    group = 2 * tiles
    high, low = split_terms(order_ref[...].reshape(-1, feat_count))
    spectrum = (
        dot(forward_high[...], high) + dot(forward_high[...], low) + dot(forward_low[...], high)
    )
    for part in range(2):
        for tile in range(tiles):
            spread_ref[pl.ds(part * tiles + tile, count, stride=group), :] = spectrum[
                part * count : (part + 1) * count, tile * 128 : (tile + 1) * 128
            ]
    rows = lax.broadcasted_iota(jnp.int32, (8, 128), 0) % group
    lane = lax.broadcasted_iota(jnp.int32, (8, 128), 1) < channels
    sign = jnp.where(rows < tiles, -1.0, 1.0)
    for base in range(0, count * group, 8):
        block = spread_ref[base : base + 8, :]
        turned = pltpu.roll(block, channels, 1)
        firsts, seconds = [], []
        for start in range(0, 8, group):
            span = slice(start, start + group)
            left = jnp.concatenate([block[span], turned[span]], axis=0)[:, :channels]
            left_high, left_low = split_terms(left)
            left = jnp.concatenate([left_high, left_low], axis=0)
            product = dot(left, weight_ref[0, (base + start) // group])
            product = product[: 2 * group] + product[2 * group :]
            firsts.append(product[:group])
            seconds.append(product[group:])
        first = jnp.concatenate(firsts, axis=0)
        second = jnp.concatenate(seconds, axis=0)
        real = jnp.where(lane, first, pltpu.roll(second, channels, 1))
        imag = jnp.where(lane, pltpu.roll(first, channels, 1), second)
        crossed = jnp.where(rows < tiles, pltpu.roll(imag, 8 - tiles, 0), pltpu.roll(imag, tiles, 0))
        result_ref[base : base + 8, :] = real + sign * crossed
    for part in range(2):
        for tile in range(tiles):
            modes_ref[part * count : (part + 1) * count, tile * 128 : (tile + 1) * 128] = (
                result_ref[pl.ds(part * tiles + tile, count, stride=group), :]
            )
    back = back_rows(inverse_high, inverse_low, column ^ 1, modes_ref[...])
    order_ref[:layers] = back.reshape(send_ref.shape)
    store_turns(send_ref, order_ref, z)


def mix(blocks, arrived, weights, forward_table, inverse_tables):
    layers = len(blocks)
    _, rows, feat_count = blocks[0].shape
    count = weights.shape[1]
    scratch = pltpu.VMEM((count * feat_count // 64, 128), jnp.float32)
    return pl.pallas_call(
        functools.partial(mix_kernel, layers),
        out_shape=[
            jax.ShapeDtypeStruct((2 * count, feat_count), jnp.float32),
            jax.ShapeDtypeStruct((layers, rows, feat_count), jnp.float32),
        ],
        scratch_shapes=[pltpu.VMEM((2 * layers, rows, feat_count), jnp.float32), scratch, scratch],
        compiler_params=SMALL,
        name="mix",
    )(*blocks, *arrived, weights, *split_table(forward_table), *inverse_tables)


def keep_kernel(modes_ref, inverse_high, inverse_low, mixed_ref, keep_ref, order_ref):
    z, x, y = quad()
    count = mixed_ref.shape[1]
    feat_count = modes_ref.shape[1]
    for part in range(2):
        mixed_ref[0, :, part * feat_count : (part + 1) * feat_count] = modes_ref[
            part * count : (part + 1) * count
        ]
    back = back_rows(inverse_high, inverse_low, x ^ y, modes_ref[...])
    order_ref[...] = back.reshape(keep_ref.shape)
    store_turns(keep_ref, order_ref, z)


def keep_rows(modes, inverse_tables, like):
    rows, feat_count = modes.shape
    return pl.pallas_call(
        keep_kernel,
        out_shape=[
            jax.ShapeDtypeStruct((1, rows // 2, 2 * feat_count), jnp.float32),
            jax.ShapeDtypeStruct(like.shape, jnp.float32),
        ],
        scratch_shapes=[pltpu.VMEM(like.shape, jnp.float32)],
        compiler_params=SMALL,
        cost_estimate=pl.CostEstimate(
            flops=6 * rows * rows * feat_count, bytes_accessed=2**20, transcendentals=0
        ),
        name="keep_rows",
    )(modes, *inverse_tables)


def gelu(values):
    square = jnp.minimum(values * values, 31.36)
    inner = jnp.full_like(square, GELU_TERMS[-1])
    for term in GELU_TERMS[-2::-1]:
        inner = inner * square + term
    half = 0.5 * values
    return half + half * jnp.tanh(values * inner)


def point_kernel(flow_ref, local_ref, bias_ref, _, out_ref, __, wide_ref, level_ref):
    cells_x, _, feat_count = flow_ref.shape
    channels = local_ref.shape[0]
    wide_ref[...] = jnp.zeros_like(wide_ref)
    for start in range(0, WIDTH, channels):
        span = slice(start, start + channels)
        wide_ref[span, span] = local_ref[...]
        level_ref[:, span] = bias_ref[...].reshape(1, channels)
    for cell in range(cells_x):
        for start in range(0, feat_count, WIDTH):
            columns = slice(start, start + WIDTH)
            out_ref[cell, :, columns] = dot(flow_ref[cell, :, columns], wide_ref[...]) + level_ref[...]


def pointwise_terms(flow_field, local, bias, first):
    spec = pl.BlockSpec(memory_space=pltpu.VMEM)
    whole = pl.BlockSpec(memory_space=pl.ANY)
    return pl.pallas_call(
        point_kernel,
        in_specs=[spec, spec, spec, whole],
        out_specs=[spec, whole],
        out_shape=[
            jax.ShapeDtypeStruct(flow_field.shape, jnp.float32),
            jax.ShapeDtypeStruct(first.shape, first.dtype),
        ],
        input_output_aliases={3: 1},
        scratch_shapes=[
            pltpu.VMEM((WIDTH, WIDTH), jnp.bfloat16),
            pltpu.VMEM((1, WIDTH), jnp.float32),
        ],
        compiler_params=SMALL,
        cost_estimate=pl.CostEstimate(
            flops=2 * WIDTH * flow_field.size,
            bytes_accessed=6 * flow_field.size,
            transcendentals=0,
        ),
        name="pointwise_terms",
    )(flow_field, local, bias, first)


def output_kernel(layers, point_ref, table_ref, *refs):
    own_refs, core_refs = refs[:layers], refs[layers : 2 * layers]
    out_hbm, order_ref, done_ref, sent = refs[2 * layers :]
    cells_x, _, feat_count = point_ref.shape
    z, x, y = quad()
    for index, turn in enumerate(turns(layers)):
        peer = (z ^ turn) * 2
        order_ref[:, peer + (x ^ y)] = own_refs[index][...]
        order_ref[:, peer + (x ^ y ^ 1)] = core_refs[index][...]
    table = table_ref[y, x ^ y]
    copies = []
    for cell in range(cells_x):
        high, low = split_terms(order_ref[cell].reshape(-1, feat_count))
        stack = jnp.concatenate([high, low, high], axis=0)
        for start in range(0, feat_count, WIDTH):
            columns = slice(start, start + WIDTH)
            total = dot(table, stack[:, columns]) + point_ref[cell, :, columns]
            done_ref[cell, :, columns] = gelu(total).astype(done_ref.dtype)
        copies.append(pltpu.make_async_copy(done_ref.at[cell], out_hbm.at[cell], sent.at[cell]))
        copies[-1].start()
    for copy in copies:
        copy.wait()


def make_output(point, parts, table):
    cells_x, _, feat_count = point.shape
    layers = len(parts) // 2
    rows = parts[0].shape[1]
    return pl.pallas_call(
        functools.partial(output_kernel, layers),
        out_specs=pl.BlockSpec(memory_space=pl.ANY),
        scratch_shapes=[
            pltpu.VMEM((cells_x, 2 * layers, rows, feat_count), jnp.float32),
            pltpu.VMEM(point.shape, jnp.bfloat16),
            pltpu.SemaphoreType.DMA((cells_x,)),
        ],
        out_shape=jax.ShapeDtypeStruct(point.shape, jnp.bfloat16),
        compiler_params=SMALL,
        name="make_output",
    )(point, table, *parts)


def row_body(flow_field, spectral_weight, local_weight, bias_terms):
    cells_x, cells_y, feat_count = flow_field.shape
    peers = lax.axis_size("gx")
    groups_y = lax.axis_size("gy")
    rows_ky = MY // groups_y // peers
    forward_scale = 1.0 / math.sqrt(cells_x * peers * cells_y * groups_y)
    inverse_scale = 1.0 / math.sqrt(MX * MY)

    table = forward_y_table(cells_y, groups_y, peers, rows_ky)
    send, keep = forward_y(flow_field, table, peers // 2, rows_ky)
    blocks = along_columns(add_blocks(keep, flip_core(send)), peers)
    inverse_tables = split_table(inverse_x_table(cells_x, peers, rows_ky))
    modes, send = mix(
        blocks,
        [flip_core(block) for block in blocks],
        spectral_weight,
        forward_x_table(cells_x, peers, rows_ky) * forward_scale,
        inverse_tables,
    )
    arrived = flip_core(send)
    mixed, keep = keep_rows(modes, inverse_tables, send)
    own = along_columns(join_blocks(keep, arrived, cells_x), peers)
    point, own[0] = pointwise_terms(flow_field, local_weight, bias_terms, own[0])
    parts = own + [flip_core(block) for block in own]
    high, low = split_table(inverse_y_table(cells_y, groups_y, peers, rows_ky) * inverse_scale)
    return make_output(point, parts, np.concatenate([high, high, low], axis=-1)), mixed


def body(flow_field, spectral_weight, local_weight, bias_terms):
    peers = lax.axis_size("gx")
    paired = lax.axis_size("gy") == 2 and peers & (peers - 1) == 0
    if paired and spectral_weight.shape[1] == 2 * MX and WIDTH % local_weight.shape[0] == 0:
        return row_body(flow_field, spectral_weight, local_weight, bias_terms)
    return general_body(flow_field, spectral_weight, local_weight, bias_terms)


def solution(mesh):
    placed = (P(("group", "gx"), "gy", None), P("gy", "gx", None, None), P(), P())
    return jax.shard_map(
        body,
        mesh=mesh,
        in_specs=placed,
        out_specs=(P(("group", "gx"), "gy", None), P(("group", "gy"), "gx", None)),
        check_vma=False,
    )
```

```python
import functools
import math

import jax
import jax.numpy as jnp
import ml_dtypes
import numpy as np
from jax import lax
from jax.experimental import pallas as pl
from jax.experimental.pallas import tpu as pltpu
from jax.sharding import PartitionSpec as P

MX = 32
MY = 32


def wave_number(index, count):
    return jnp.where(index < count // 2, index, index - count)


def phase_table(waves, places, extent):
    product = waves[:, None] * places[None, :] % extent
    return 2.0 * math.pi / extent * product.astype(jnp.float32)


def row_tables(ky_rows, kx_rows, x_places, extent, width):
    angle = phase_table(wave_number(kx_rows, MX), x_places, extent)
    select = (ky_rows[:, None] == jnp.arange(width, dtype=jnp.int32)[None, :]).astype(jnp.float32)
    cosine = jnp.cos(angle)[:, :, None] * select[:, None, :]
    sine_part = jnp.sin(angle)[:, :, None] * select[:, None, :]
    return (cosine, sine_part)


def forward_rows(y_local, ky_rows, kx_rows, x_places, extent):
    cosine, sine_part = row_tables(ky_rows, kx_rows, x_places, extent, y_local.shape[0])
    real_in = y_local[:, 0]
    imag_in = y_local[:, 1]

    def contract(table, values):
        return jnp.einsum("rxk,kxf->rf", table, values, precision=lax.Precision.HIGHEST)

    real_out = contract(cosine, real_in) + contract(sine_part, imag_in)
    imag_out = contract(cosine, imag_in) - contract(sine_part, real_in)
    return jnp.concatenate([real_out, imag_out], axis=1)


def inverse_rows(running, shard_rows, ky_rows, kx_rows, x_places, extent):
    cosine, sine_part = row_tables(ky_rows, kx_rows, x_places, extent, running.shape[0])
    feat_count = shard_rows.shape[1] // 2
    real_part = shard_rows[:, :feat_count]
    imag_part = shard_rows[:, feat_count:]

    def contract(table, values):
        return jnp.einsum("rxk,rf->kxf", table, values, precision=lax.Precision.HIGHEST)

    new_real = contract(cosine, real_part) - contract(sine_part, imag_part)
    new_imag = contract(cosine, imag_part) + contract(sine_part, real_part)
    return jnp.stack([new_real, new_imag], axis=1)


def general_body(flow_field, spectral_weight, local_weight, bias_terms):
    cells_x, cells_y, feat_count = flow_field.shape
    channels = local_weight.shape[0]
    planes = feat_count // channels
    groups_x = lax.axis_size("gx")
    groups_y = lax.axis_size("gy")
    extent_x = cells_x * groups_x
    extent_y = cells_y * groups_y
    half_width = MY // groups_y
    quota_rows = spectral_weight.shape[1]
    high = lax.Precision.HIGHEST
    x_places = lax.axis_index("gx") * cells_x + jnp.arange(cells_x, dtype=jnp.int32)
    y_places = lax.axis_index("gy") * cells_y + jnp.arange(cells_y, dtype=jnp.int32)
    y_angle = phase_table(wave_number(jnp.arange(MY, dtype=jnp.int32), MY), y_places, extent_y)
    y_table = (
        jnp.stack([jnp.cos(y_angle), -jnp.sin(y_angle)], axis=1)
        .reshape(2 * MY, cells_y)
        .astype(jnp.bfloat16)
    )
    y_local = lax.psum_scatter(
        jnp.einsum("qy,xyf->qxf", y_table, flow_field, preferred_element_type=jnp.float32),
        "gy",
        scatter_dimension=0,
        tiled=True,
    )
    y_local = y_local.reshape(half_width, 2, cells_x, feat_count)
    rest_index = jnp.arange(lax.axis_size("gx") * quota_rows, dtype=jnp.int32)
    spectrum = lax.psum_scatter(
        forward_rows(y_local, rest_index // MX, rest_index % MX, x_places, extent_x),
        "gx",
        scatter_dimension=0,
        tiled=True,
    )
    spectrum = spectrum * (1.0 / math.sqrt(extent_x * extent_y))
    coeffs = spectrum.reshape(quota_rows, 2, planes, channels)
    weights = spectral_weight[0].astype(jnp.float32)
    product = jnp.einsum("rpzc,rco->rpzo", coeffs, weights, precision=high)
    mixed_real = product[:, 0, :, :channels] - product[:, 1, :, channels:]
    mixed_imag = product[:, 0, :, channels:] + product[:, 1, :, :channels]
    mixed_local = jnp.stack([mixed_real, mixed_imag], axis=1).reshape(quota_rows, 2 * feat_count)
    pointwise = jnp.einsum(
        "xyzc,co->xyzo",
        flow_field.reshape(cells_x, cells_y, planes, channels),
        local_weight,
        preferred_element_type=jnp.float32,
    )
    start_half = jnp.zeros((half_width, 2, cells_x, feat_count), jnp.float32)
    shard_rows = lax.all_gather(mixed_local, "gx", axis=0, tiled=True)
    rest_index = jnp.arange(shard_rows.shape[0], dtype=jnp.int32)
    back_half = inverse_rows(
        start_half, shard_rows, rest_index // MX, rest_index % MX, x_places, extent_x
    )
    back_whole = lax.all_gather(back_half, "gy", axis=0, tiled=True)
    y_cos = jnp.cos(y_angle)
    y_sin = jnp.sin(y_angle)
    spectral = (
        jnp.einsum("kn,kxf->xnf", y_cos, back_whole[:, 0], precision=high)
        - jnp.einsum("kn,kxf->xnf", y_sin, back_whole[:, 1], precision=high)
    ) * (1.0 / math.sqrt(MX * MY))
    total = spectral.reshape(cells_x, cells_y, planes, channels) + pointwise + bias_terms
    output = (
        jax.nn.gelu(total, approximate=False)
        .reshape(cells_x, cells_y, feat_count)
        .astype(jnp.bfloat16)
    )
    return (output, mixed_local.reshape(1, quota_rows, 2 * feat_count))


SMALL = pltpu.CompilerParams(vmem_limit_bytes=20 * 1024 * 1024)
LARGE = pltpu.CompilerParams(vmem_limit_bytes=53 * 1024 * 1024)
WIDTH = 256
GELU_TERMS = (
    0.7978849411010742,
    0.03633308410644531,
    -3.259492223151028e-05,
    -5.530622001970187e-05,
    3.964749794249656e-06,
    -1.3226382122866198e-07,
    1.7561855303327434e-09,
)


def angles(count, places, extent):
    index = np.arange(count)
    waves = np.where(index < count // 2, index, index - count)
    product = (waves[:, None] * np.asarray(places)[None, :]) % extent
    return (np.float32(2.0 * math.pi / extent) * product.astype(np.float32)).astype(np.float64)


def split_table(table):
    high = table.astype(ml_dtypes.bfloat16)
    low = (table - high.astype(np.float64)).astype(ml_dtypes.bfloat16)
    return high, low


def split_terms(values):
    high = values.astype(jnp.bfloat16)
    low = (values - high.astype(jnp.float32)).astype(jnp.bfloat16)
    return high, low


def quad():
    place = lax.axis_index("gx")
    return place // 2, place % 2, lax.axis_index("gy")


def turns(layers):
    half = layers // 2
    return list(range(half, layers)) + list(range(half - 1, -1, -1))


def forward_x_table(cells_x, peers, rows_ky):
    extent = cells_x * peers
    angle = angles(MX, np.arange(extent), extent)
    cosine, sine = np.cos(angle), np.sin(angle)
    out = np.zeros((2, rows_ky, MX, extent, rows_ky, 2))
    for row in range(rows_ky):
        out[0, row, :, :, row, 0] = cosine
        out[0, row, :, :, row, 1] = sine
        out[1, row, :, :, row, 1] = cosine
        out[1, row, :, :, row, 0] = -sine
    return out.reshape(2 * rows_ky * MX, extent * rows_ky * 2)


def inverse_x_table(cells_x, peers, rows_ky):
    extent = cells_x * peers
    angle = angles(MX, np.arange(extent), extent)
    cosine, sine = np.cos(angle).T, np.sin(angle).T
    out = np.zeros((extent, rows_ky, 2, 2, rows_ky, MX))
    for row in range(rows_ky):
        out[:, row, 0, 0, row, :] = cosine
        out[:, row, 0, 1, row, :] = -sine
        out[:, row, 1, 1, row, :] = cosine
        out[:, row, 1, 0, row, :] = sine
    out = out.reshape(peers // 2, 2, cells_x * rows_ky * 2, 2 * rows_ky * MX)
    return np.moveaxis(out, 1, 0).reshape(2, -1, 2 * rows_ky * MX)


def inverse_y_table(cells_y, groups_y, peers, rows_ky):
    extent = cells_y * groups_y
    angle = angles(MY, np.arange(extent), extent)
    full = np.stack([np.cos(angle), -np.sin(angle)], axis=1)
    full = full.reshape(groups_y, peers, rows_ky, 2, groups_y, cells_y)
    out = np.zeros((groups_y, 2, cells_y, peers, 2, rows_ky, 2))
    for y in range(groups_y):
        for column in range(2):
            for peer in range(peers):
                for place in range(2):
                    half = y ^ place ^ column ^ (peer % 2)
                    out[y, column, :, peer, place] = np.moveaxis(full[half, peer, :, :, y], -1, 0)
    return out.reshape(groups_y, 2, cells_y, 4 * peers * rows_ky)


def dot(left, right):
    return jnp.dot(left, right, preferred_element_type=jnp.float32)


def forward_y_table(shape, extent, layers, rows_ky):
    z, x, y = quad()
    peers = 2 * layers
    row = lax.broadcasted_iota(jnp.int32, (shape[0], 1), 0)
    block = row // (2 * rows_ky)
    place = block // 2 % layers
    turn = jnp.where(place < layers // 2, place + layers // 2, layers - 1 - place)
    side = y ^ (1 - block // peers)
    owner = (side ^ (block % 2)) * peers + (z ^ turn) * 2 + (x ^ side)
    index = owner * rows_ky + row // 2 % rows_ky
    y_places = lax.broadcasted_iota(jnp.int32, (1, shape[1]), 1) + y * shape[1]
    steps = (wave_number(index, MY) * y_places) & (extent - 1)
    angle = 2.0 * math.pi / extent * steps.astype(jnp.float32)
    return jnp.where(row % 2 == 0, jnp.cos(angle), -jnp.sin(angle)).astype(jnp.bfloat16)


def forward_y_kernel(extent, rows_ky, flow_hbm, send_ref, keep_ref, flow_ref, arrived):
    layers, _, rows, feat_count = send_ref.shape
    cells_x, cells_y, _ = flow_ref.shape
    rows = rows // cells_x
    copies = [
        pltpu.make_async_copy(flow_hbm.at[x], flow_ref.at[x], arrived.at[x])
        for x in range(cells_x)
    ]
    for copy in copies:
        copy.start()
    table = forward_y_table((2 * MY, cells_y), extent, layers, rows_ky)
    for x in range(cells_x):
        copies[x].wait()
        result = dot(table, flow_ref[x]).reshape(2, layers, 2, rows, feat_count)
        send_ref[:, :, x * rows : (x + 1) * rows, :] = result[0]
        keep_ref[:, :, x * rows : (x + 1) * rows, :] = result[1]


def forward_y(flow_field, extent, layers, rows_ky):
    cells_x, _, feat_count = flow_field.shape
    shape = jax.ShapeDtypeStruct((layers, 2, cells_x * 2 * rows_ky, feat_count), jnp.float32)
    return pl.pallas_call(
        functools.partial(forward_y_kernel, extent, rows_ky),
        in_specs=[pl.BlockSpec(memory_space=pltpu.HBM)],
        out_shape=[shape] * 2,
        scratch_shapes=[
            pltpu.VMEM(flow_field.shape, flow_field.dtype),
            pltpu.SemaphoreType.DMA((cells_x,)),
        ],
        compiler_params=LARGE,
        name="forward_y",
    )(flow_field)


def flip_core(block):
    return lax.ppermute(block, "gy", [(0, 1), (1, 0)])


def along_columns(blocks, peers):
    arrived = []
    for turn, block in zip(turns(len(blocks)), blocks):
        pairs = [
            (2 * place + core, 2 * (place ^ (2 * turn + core)) + core)
            for place in range(peers)
            for core in range(2)
        ]
        arrived.append(lax.ppermute(block, ("gx", "gy"), pairs))
    return arrived


def small_call(kernel, out_shape, name):
    return pl.pallas_call(kernel, out_shape=out_shape, compiler_params=SMALL, name=name)


def add_kernel(keep_ref, arrived_ref, *out_refs):
    for turn, out_ref in enumerate(out_refs):
        out_ref[...] = keep_ref[turn] + arrived_ref[turn]


def add_blocks(keep, arrived):
    shape = jax.ShapeDtypeStruct(keep.shape[1:], keep.dtype)
    return small_call(add_kernel, [shape] * keep.shape[0], "add_blocks")(keep, arrived)


def join_kernel(keep_ref, arrived_ref, *out_refs):
    cells_x, rows, _ = out_refs[0].shape
    rows = rows // 2
    for turn, out_ref in enumerate(out_refs):
        for cell in range(cells_x):
            span = slice(cell * rows, (cell + 1) * rows)
            out_ref[cell] = jnp.concatenate(
                [keep_ref[turn, span, :], arrived_ref[turn, span, :]], axis=0
            )


def join_blocks(keep, arrived, cells_x):
    layers, rows, feat_count = keep.shape
    shape = jax.ShapeDtypeStruct((cells_x, 2 * rows // cells_x, feat_count), keep.dtype)
    return small_call(join_kernel, [shape] * layers, "join_blocks")(keep, arrived)


def back_rows(inverse_high, inverse_low, column, modes):
    high, low = split_terms(modes)
    table = inverse_high[column]
    return dot(table, high) + dot(table, low) + dot(inverse_low[column], high)


def store_turns(out_ref, order_ref, z):
    for index, turn in enumerate(turns(out_ref.shape[0])):
        out_ref[index] = order_ref[z ^ turn]


def mix_kernel(layers, *refs):
    block_refs, arrived_refs = refs[:layers], refs[layers : 2 * layers]
    weight_ref, forward_high, forward_low, inverse_high, inverse_low = refs[
        2 * layers : 2 * layers + 5
    ]
    modes_ref, send_ref, order_ref, spread_ref, result_ref = refs[2 * layers + 5 :]
    z, x, y = quad()
    column = x ^ y
    for index, turn in enumerate(turns(layers)):
        order_ref[(z ^ turn) * 2 + column] = block_refs[index][0]
        order_ref[(z ^ turn) * 2 + (column ^ 1)] = arrived_refs[index][1]
    feat_count = order_ref.shape[-1]
    count = weight_ref.shape[1]
    channels = weight_ref.shape[2]
    tiles = feat_count // 128
    group = 2 * tiles
    high, low = split_terms(order_ref[...].reshape(-1, feat_count))
    spectrum = (
        dot(forward_high[...], high) + dot(forward_high[...], low) + dot(forward_low[...], high)
    )
    for part in range(2):
        for tile in range(tiles):
            spread_ref[pl.ds(part * tiles + tile, count, stride=group), :] = spectrum[
                part * count : (part + 1) * count, tile * 128 : (tile + 1) * 128
            ]
    rows = lax.broadcasted_iota(jnp.int32, (8, 128), 0) % group
    lane = lax.broadcasted_iota(jnp.int32, (8, 128), 1) < channels
    sign = jnp.where(rows < tiles, -1.0, 1.0)
    for base in range(0, count * group, 8):
        block = spread_ref[base : base + 8, :]
        turned = pltpu.roll(block, channels, 1)
        firsts, seconds = [], []
        for start in range(0, 8, group):
            span = slice(start, start + group)
            left = jnp.concatenate([block[span], turned[span]], axis=0)[:, :channels]
            left_high, left_low = split_terms(left)
            left = jnp.concatenate([left_high, left_low], axis=0)
            product = dot(left, weight_ref[0, (base + start) // group])
            product = product[: 2 * group] + product[2 * group :]
            firsts.append(product[:group])
            seconds.append(product[group:])
        first = jnp.concatenate(firsts, axis=0)
        second = jnp.concatenate(seconds, axis=0)
        real = jnp.where(lane, first, pltpu.roll(second, channels, 1))
        imag = jnp.where(lane, pltpu.roll(first, channels, 1), second)
        crossed = jnp.where(rows < tiles, pltpu.roll(imag, 8 - tiles, 0), pltpu.roll(imag, tiles, 0))
        result_ref[base : base + 8, :] = real + sign * crossed
    for part in range(2):
        for tile in range(tiles):
            modes_ref[part * count : (part + 1) * count, tile * 128 : (tile + 1) * 128] = (
                result_ref[pl.ds(part * tiles + tile, count, stride=group), :]
            )
    back = back_rows(inverse_high, inverse_low, column ^ 1, modes_ref[...])
    order_ref[:layers] = back.reshape(send_ref.shape)
    store_turns(send_ref, order_ref, z)


def mix(blocks, arrived, weights, forward_table, inverse_tables):
    layers = len(blocks)
    _, rows, feat_count = blocks[0].shape
    count = weights.shape[1]
    scratch = pltpu.VMEM((count * feat_count // 64, 128), jnp.float32)
    return pl.pallas_call(
        functools.partial(mix_kernel, layers),
        out_shape=[
            jax.ShapeDtypeStruct((2 * count, feat_count), jnp.float32),
            jax.ShapeDtypeStruct((layers, rows, feat_count), jnp.float32),
        ],
        scratch_shapes=[pltpu.VMEM((2 * layers, rows, feat_count), jnp.float32), scratch, scratch],
        compiler_params=SMALL,
        name="mix",
    )(*blocks, *arrived, weights, *split_table(forward_table), *inverse_tables)


def keep_kernel(modes_ref, inverse_high, inverse_low, keep_ref, order_ref):
    z, x, y = quad()
    back = back_rows(inverse_high, inverse_low, x ^ y, modes_ref[...])
    order_ref[...] = back.reshape(keep_ref.shape)
    store_turns(keep_ref, order_ref, z)


def keep_rows(modes, inverse_tables, like):
    return pl.pallas_call(
        keep_kernel,
        out_shape=jax.ShapeDtypeStruct(like.shape, jnp.float32),
        scratch_shapes=[pltpu.VMEM(like.shape, jnp.float32)],
        compiler_params=SMALL,
        name="keep_rows",
    )(modes, *inverse_tables)


def gelu(values):
    square = jnp.minimum(values * values, 31.36)
    inner = jnp.full_like(square, GELU_TERMS[-1])
    for term in GELU_TERMS[-2::-1]:
        inner = inner * square + term
    half = 0.5 * values
    return half + half * jnp.tanh(values * inner)


def output_kernel(layers, flow_ref, table_ref, local_ref, bias_ref, modes_ref, *refs):
    own_refs, core_refs = refs[:layers], refs[layers : 2 * layers]
    out_hbm, mixed_hbm, order_ref, wide_ref, level_ref, done_ref, sent = refs[2 * layers :]
    cells_x, _, feat_count = flow_ref.shape
    channels = local_ref.shape[0]
    count = modes_ref.shape[0] // 2
    copies = []
    for part in range(2):
        copies.append(
            pltpu.make_async_copy(
                modes_ref.at[pl.ds(part * count, count)],
                mixed_hbm.at[0, :, pl.ds(part * feat_count, feat_count)],
                sent.at[cells_x + part],
            )
        )
        copies[-1].start()
    z, x, y = quad()
    wide_ref[...] = jnp.zeros_like(wide_ref)
    for start in range(0, WIDTH, channels):
        span = slice(start, start + channels)
        wide_ref[span, span] = local_ref[...]
        level_ref[:, span] = bias_ref[...].reshape(1, channels)
    for column, block_refs in ((x ^ y, own_refs), (x ^ y ^ 1, core_refs)):
        for turn, block_ref in zip(turns(layers), block_refs):
            order_ref[:, (z ^ turn) * 2 + column] = block_ref[...]
    table = table_ref[y, x ^ y]
    for cell in range(cells_x):
        high, low = split_terms(order_ref[cell].reshape(-1, feat_count))
        stack = jnp.concatenate([high, low, high], axis=0)
        for start in range(0, feat_count, WIDTH):
            columns = slice(start, start + WIDTH)
            total = dot(table, stack[:, columns]) + dot(flow_ref[cell, :, columns], wide_ref[...])
            done_ref[cell, :, columns] = gelu(total + level_ref[...]).astype(done_ref.dtype)
        copies.append(pltpu.make_async_copy(done_ref.at[cell], out_hbm.at[cell], sent.at[cell]))
        copies[-1].start()
    for copy in copies:
        copy.wait()


def make_output(flow_field, parts, table, local, bias, modes):
    cells_x, _, feat_count = flow_field.shape
    layers = len(parts) // 2
    rows, _ = modes.shape
    return pl.pallas_call(
        functools.partial(output_kernel, layers),
        out_specs=[pl.BlockSpec(memory_space=pl.ANY)] * 2,
        scratch_shapes=[
            pltpu.VMEM((cells_x, 2 * layers) + parts[0].shape[1:], jnp.float32),
            pltpu.VMEM((WIDTH, WIDTH), jnp.bfloat16),
            pltpu.VMEM((1, WIDTH), jnp.float32),
            pltpu.VMEM(flow_field.shape, jnp.bfloat16),
            pltpu.SemaphoreType.DMA((cells_x + 2,)),
        ],
        out_shape=[
            jax.ShapeDtypeStruct(flow_field.shape, jnp.bfloat16),
            jax.ShapeDtypeStruct((1, rows // 2, 2 * feat_count), jnp.float32),
        ],
        compiler_params=SMALL,
        name="make_output",
    )(flow_field, table, local, bias, modes, *parts)


def row_body(flow_field, spectral_weight, local_weight, bias_terms):
    cells_x, cells_y, feat_count = flow_field.shape
    peers = lax.axis_size("gx")
    groups_y = lax.axis_size("gy")
    rows_ky = MY // groups_y // peers
    forward_scale = 1.0 / math.sqrt(cells_x * peers * cells_y * groups_y)
    inverse_scale = 1.0 / math.sqrt(MX * MY)

    send, keep = forward_y(flow_field, cells_y * groups_y, peers // 2, rows_ky)
    blocks = along_columns(add_blocks(keep, flip_core(send)), peers)
    inverse_tables = split_table(inverse_x_table(cells_x, peers, rows_ky))
    modes, send = mix(
        blocks,
        [flip_core(block) for block in blocks],
        spectral_weight,
        forward_x_table(cells_x, peers, rows_ky) * forward_scale,
        inverse_tables,
    )
    arrived = flip_core(send)
    keep = keep_rows(modes, inverse_tables, send)
    own = along_columns(join_blocks(keep, arrived, cells_x), peers)
    parts = own + [flip_core(block) for block in own]
    high, low = split_table(inverse_y_table(cells_y, groups_y, peers, rows_ky) * inverse_scale)
    table = np.concatenate([high, high, low], axis=-1)
    return tuple(make_output(flow_field, parts, table, local_weight, bias_terms, modes))


def body(flow_field, spectral_weight, local_weight, bias_terms):
    peers = lax.axis_size("gx")
    extent = lax.axis_size("gy") * flow_field.shape[1]
    paired = lax.axis_size("gy") == 2 and peers & (peers - 1) == 0 and extent & (extent - 1) == 0
    if paired and spectral_weight.shape[1] == 2 * MX and WIDTH % local_weight.shape[0] == 0:
        return row_body(flow_field, spectral_weight, local_weight, bias_terms)
    return general_body(flow_field, spectral_weight, local_weight, bias_terms)


def solution(mesh):
    placed = (P(("group", "gx"), "gy", None), P("gy", "gx", None, None), P(), P())
    return jax.shard_map(
        body,
        mesh=mesh,
        in_specs=placed,
        out_specs=(P(("group", "gx"), "gy", None), P(("group", "gy"), "gx", None)),
        check_vma=False,
    )
```

```python
import functools
import math

import jax
import jax.numpy as jnp
import ml_dtypes
import numpy as np
from jax import lax
from jax.experimental import pallas as pl
from jax.experimental.pallas import tpu as pltpu
from jax.sharding import PartitionSpec as P

MX = 32
MY = 32


def wave_number(index, count):
    return jnp.where(index < count // 2, index, index - count)


def phase_table(waves, places, extent):
    product = waves[:, None] * places[None, :] % extent
    return 2.0 * math.pi / extent * product.astype(jnp.float32)


def row_tables(ky_rows, kx_rows, x_places, extent, width):
    angle = phase_table(wave_number(kx_rows, MX), x_places, extent)
    select = (ky_rows[:, None] == jnp.arange(width, dtype=jnp.int32)[None, :]).astype(jnp.float32)
    cosine = jnp.cos(angle)[:, :, None] * select[:, None, :]
    sine_part = jnp.sin(angle)[:, :, None] * select[:, None, :]
    return (cosine, sine_part)


def forward_rows(y_local, ky_rows, kx_rows, x_places, extent):
    cosine, sine_part = row_tables(ky_rows, kx_rows, x_places, extent, y_local.shape[0])
    real_in = y_local[:, 0]
    imag_in = y_local[:, 1]

    def contract(table, values):
        return jnp.einsum("rxk,kxf->rf", table, values, precision=lax.Precision.HIGHEST)

    real_out = contract(cosine, real_in) + contract(sine_part, imag_in)
    imag_out = contract(cosine, imag_in) - contract(sine_part, real_in)
    return jnp.concatenate([real_out, imag_out], axis=1)


def inverse_rows(running, shard_rows, ky_rows, kx_rows, x_places, extent):
    cosine, sine_part = row_tables(ky_rows, kx_rows, x_places, extent, running.shape[0])
    feat_count = shard_rows.shape[1] // 2
    real_part = shard_rows[:, :feat_count]
    imag_part = shard_rows[:, feat_count:]

    def contract(table, values):
        return jnp.einsum("rxk,rf->kxf", table, values, precision=lax.Precision.HIGHEST)

    new_real = contract(cosine, real_part) - contract(sine_part, imag_part)
    new_imag = contract(cosine, imag_part) + contract(sine_part, real_part)
    return jnp.stack([new_real, new_imag], axis=1)


def general_body(flow_field, spectral_weight, local_weight, bias_terms):
    cells_x, cells_y, feat_count = flow_field.shape
    channels = local_weight.shape[0]
    planes = feat_count // channels
    groups_x = lax.axis_size("gx")
    groups_y = lax.axis_size("gy")
    extent_x = cells_x * groups_x
    extent_y = cells_y * groups_y
    half_width = MY // groups_y
    quota_rows = spectral_weight.shape[1]
    high = lax.Precision.HIGHEST
    x_places = lax.axis_index("gx") * cells_x + jnp.arange(cells_x, dtype=jnp.int32)
    y_places = lax.axis_index("gy") * cells_y + jnp.arange(cells_y, dtype=jnp.int32)
    y_angle = phase_table(wave_number(jnp.arange(MY, dtype=jnp.int32), MY), y_places, extent_y)
    y_table = (
        jnp.stack([jnp.cos(y_angle), -jnp.sin(y_angle)], axis=1)
        .reshape(2 * MY, cells_y)
        .astype(jnp.bfloat16)
    )
    y_local = lax.psum_scatter(
        jnp.einsum("qy,xyf->qxf", y_table, flow_field, preferred_element_type=jnp.float32),
        "gy",
        scatter_dimension=0,
        tiled=True,
    )
    y_local = y_local.reshape(half_width, 2, cells_x, feat_count)
    rest_index = jnp.arange(lax.axis_size("gx") * quota_rows, dtype=jnp.int32)
    spectrum = lax.psum_scatter(
        forward_rows(y_local, rest_index // MX, rest_index % MX, x_places, extent_x),
        "gx",
        scatter_dimension=0,
        tiled=True,
    )
    spectrum = spectrum * (1.0 / math.sqrt(extent_x * extent_y))
    coeffs = spectrum.reshape(quota_rows, 2, planes, channels)
    weights = spectral_weight[0].astype(jnp.float32)
    product = jnp.einsum("rpzc,rco->rpzo", coeffs, weights, precision=high)
    mixed_real = product[:, 0, :, :channels] - product[:, 1, :, channels:]
    mixed_imag = product[:, 0, :, channels:] + product[:, 1, :, :channels]
    mixed_local = jnp.stack([mixed_real, mixed_imag], axis=1).reshape(quota_rows, 2 * feat_count)
    pointwise = jnp.einsum(
        "xyzc,co->xyzo",
        flow_field.reshape(cells_x, cells_y, planes, channels),
        local_weight,
        preferred_element_type=jnp.float32,
    )
    start_half = jnp.zeros((half_width, 2, cells_x, feat_count), jnp.float32)
    shard_rows = lax.all_gather(mixed_local, "gx", axis=0, tiled=True)
    rest_index = jnp.arange(shard_rows.shape[0], dtype=jnp.int32)
    back_half = inverse_rows(
        start_half, shard_rows, rest_index // MX, rest_index % MX, x_places, extent_x
    )
    back_whole = lax.all_gather(back_half, "gy", axis=0, tiled=True)
    y_cos = jnp.cos(y_angle)
    y_sin = jnp.sin(y_angle)
    spectral = (
        jnp.einsum("kn,kxf->xnf", y_cos, back_whole[:, 0], precision=high)
        - jnp.einsum("kn,kxf->xnf", y_sin, back_whole[:, 1], precision=high)
    ) * (1.0 / math.sqrt(MX * MY))
    total = spectral.reshape(cells_x, cells_y, planes, channels) + pointwise + bias_terms
    output = (
        jax.nn.gelu(total, approximate=False)
        .reshape(cells_x, cells_y, feat_count)
        .astype(jnp.bfloat16)
    )
    return (output, mixed_local.reshape(1, quota_rows, 2 * feat_count))


SMALL = pltpu.CompilerParams(vmem_limit_bytes=20 * 1024 * 1024)
LARGE = pltpu.CompilerParams(vmem_limit_bytes=53 * 1024 * 1024)
WIDTH = 256
GELU_TERMS = (
    0.7978849411010742,
    0.03633308410644531,
    -3.259492223151028e-05,
    -5.530622001970187e-05,
    3.964749794249656e-06,
    -1.3226382122866198e-07,
    1.7561855303327434e-09,
)


def angles(count, places, extent):
    index = np.arange(count)
    waves = np.where(index < count // 2, index, index - count)
    product = (waves[:, None] * np.asarray(places)[None, :]) % extent
    return (np.float32(2.0 * math.pi / extent) * product.astype(np.float32)).astype(np.float64)


def split_table(table):
    high = table.astype(ml_dtypes.bfloat16)
    low = (table - high.astype(np.float64)).astype(ml_dtypes.bfloat16)
    return high, low


def split_terms(values):
    high = values.astype(jnp.bfloat16)
    low = (values - high.astype(jnp.float32)).astype(jnp.bfloat16)
    return high, low


def quad():
    place = lax.axis_index("gx")
    return place // 2, place % 2, lax.axis_index("gy")


def turns(layers):
    half = layers // 2
    return list(range(half, -1, -1)) + list(range(half + 1, layers))


def forward_x_table(cells_x, peers, rows_ky):
    extent = cells_x * peers
    angle = angles(MX, np.arange(extent), extent)
    cosine, sine = np.cos(angle), np.sin(angle)
    out = np.zeros((2, rows_ky, MX, extent, rows_ky, 2))
    for row in range(rows_ky):
        out[0, row, :, :, row, 0] = cosine
        out[0, row, :, :, row, 1] = sine
        out[1, row, :, :, row, 1] = cosine
        out[1, row, :, :, row, 0] = -sine
    return out.reshape(2 * rows_ky * MX, extent * rows_ky * 2)


def inverse_x_table(cells_x, peers, rows_ky):
    extent = cells_x * peers
    angle = angles(MX, np.arange(extent), extent)
    cosine, sine = np.cos(angle).T, np.sin(angle).T
    out = np.zeros((extent, rows_ky, 2, 2, rows_ky, MX))
    for row in range(rows_ky):
        out[:, row, 0, 0, row, :] = cosine
        out[:, row, 0, 1, row, :] = -sine
        out[:, row, 1, 1, row, :] = cosine
        out[:, row, 1, 0, row, :] = sine
    out = out.reshape(peers // 2, 2, cells_x * rows_ky * 2, 2 * rows_ky * MX)
    return np.moveaxis(out, 1, 0).reshape(2, -1, 2 * rows_ky * MX)


def inverse_y_table(cells_y, groups_y, peers, rows_ky):
    extent = cells_y * groups_y
    angle = angles(MY, np.arange(extent), extent)
    full = np.stack([np.cos(angle), -np.sin(angle)], axis=1)
    full = full.reshape(groups_y, peers, rows_ky, 2, groups_y, cells_y)
    out = np.zeros((groups_y, 2, cells_y, peers, 2, rows_ky, 2))
    for y in range(groups_y):
        for column in range(2):
            for peer in range(peers):
                for place in range(2):
                    half = y ^ place ^ column ^ (peer % 2)
                    out[y, column, :, peer, place] = np.moveaxis(full[half, peer, :, :, y], -1, 0)
    return out.reshape(groups_y, 2, cells_y, 4 * peers * rows_ky)


def dot(left, right):
    return jnp.dot(left, right, preferred_element_type=jnp.float32)


def forward_y_table(shape, extent, layers, rows_ky):
    z, x, y = quad()
    peers = 2 * layers
    row = lax.broadcasted_iota(jnp.int32, (shape[0], 1), 0)
    block = row // (2 * rows_ky)
    place = block // 2 % layers
    turn = jnp.where(place <= layers // 2, layers // 2 - place, place)
    side = y ^ (1 - block // peers)
    owner = (side ^ (block % 2)) * peers + (z ^ turn) * 2 + (x ^ side)
    index = owner * rows_ky + row // 2 % rows_ky
    y_places = lax.broadcasted_iota(jnp.int32, (1, shape[1]), 1) + y * shape[1]
    steps = (wave_number(index, MY) * y_places) & (extent - 1)
    angle = 2.0 * math.pi / extent * steps.astype(jnp.float32)
    return jnp.where(row % 2 == 0, jnp.cos(angle), -jnp.sin(angle)).astype(jnp.bfloat16)


def forward_y_kernel(extent, rows_ky, flow_hbm, send_ref, keep_ref, flow_ref, arrived):
    layers, _, rows, feat_count = send_ref.shape
    cells_x, cells_y, _ = flow_ref.shape
    rows = rows // cells_x
    copies = [
        pltpu.make_async_copy(flow_hbm.at[x], flow_ref.at[x], arrived.at[x])
        for x in range(cells_x)
    ]
    for copy in copies:
        copy.start()
    table = forward_y_table((2 * MY, cells_y), extent, layers, rows_ky)
    for x in range(cells_x):
        copies[x].wait()
        result = dot(table, flow_ref[x]).reshape(2, layers, 2, rows, feat_count)
        send_ref[:, :, x * rows : (x + 1) * rows, :] = result[0]
        keep_ref[:, :, x * rows : (x + 1) * rows, :] = result[1]


def forward_y(flow_field, extent, layers, rows_ky):
    cells_x, _, feat_count = flow_field.shape
    shape = jax.ShapeDtypeStruct((layers, 2, cells_x * 2 * rows_ky, feat_count), jnp.float32)
    return pl.pallas_call(
        functools.partial(forward_y_kernel, extent, rows_ky),
        in_specs=[pl.BlockSpec(memory_space=pltpu.HBM)],
        out_shape=[shape] * 2,
        scratch_shapes=[
            pltpu.VMEM(flow_field.shape, flow_field.dtype),
            pltpu.SemaphoreType.DMA((cells_x,)),
        ],
        compiler_params=LARGE,
        name="forward_y",
    )(flow_field)


def flip_core(block):
    return lax.ppermute(block, "gy", [(0, 1), (1, 0)])


def along_columns(blocks, peers):
    arrived = []
    for turn, block in zip(turns(len(blocks)), blocks):
        pairs = [
            (2 * place + core, 2 * (place ^ (2 * turn + core)) + core)
            for place in range(peers)
            for core in range(2)
        ]
        arrived.append(lax.ppermute(block, ("gx", "gy"), pairs))
    return arrived


def small_call(kernel, out_shape, name):
    return pl.pallas_call(kernel, out_shape=out_shape, compiler_params=SMALL, name=name)


def add_kernel(keep_ref, arrived_ref, *out_refs):
    for turn, out_ref in enumerate(out_refs):
        out_ref[...] = keep_ref[turn] + arrived_ref[turn]


def add_blocks(keep, arrived):
    shape = jax.ShapeDtypeStruct(keep.shape[1:], keep.dtype)
    return small_call(add_kernel, [shape] * keep.shape[0], "add_blocks")(keep, arrived)


def join_kernel(keep_ref, arrived_ref, *out_refs):
    cells_x, rows, _ = out_refs[0].shape
    rows = rows // 2
    for turn, out_ref in enumerate(out_refs):
        for cell in range(cells_x):
            span = slice(cell * rows, (cell + 1) * rows)
            out_ref[cell] = jnp.concatenate(
                [keep_ref[turn, span, :], arrived_ref[turn, span, :]], axis=0
            )


def join_blocks(keep, arrived, cells_x):
    layers, rows, feat_count = keep.shape
    shape = jax.ShapeDtypeStruct((cells_x, 2 * rows // cells_x, feat_count), keep.dtype)
    return small_call(join_kernel, [shape] * layers, "join_blocks")(keep, arrived)


def back_rows(inverse_high, inverse_low, column, modes):
    high, low = split_terms(modes)
    table = inverse_high[column]
    return dot(table, high) + dot(table, low) + dot(inverse_low[column], high)


def store_turns(out_ref, order_ref, z):
    for index, turn in enumerate(turns(out_ref.shape[0])):
        out_ref[index] = order_ref[z ^ turn]


def mix_kernel(layers, *refs):
    block_refs, arrived_refs = refs[:layers], refs[layers : 2 * layers]
    weight_ref, forward_high, forward_low, inverse_high, inverse_low = refs[
        2 * layers : 2 * layers + 5
    ]
    modes_ref, send_ref, order_ref, spread_ref, result_ref = refs[2 * layers + 5 :]
    z, x, y = quad()
    column = x ^ y
    for index, turn in enumerate(turns(layers)):
        order_ref[(z ^ turn) * 2 + column] = block_refs[index][0]
        order_ref[(z ^ turn) * 2 + (column ^ 1)] = arrived_refs[index][1]
    feat_count = order_ref.shape[-1]
    count = weight_ref.shape[1]
    channels = weight_ref.shape[2]
    tiles = feat_count // 128
    group = 2 * tiles
    high, low = split_terms(order_ref[...].reshape(-1, feat_count))
    spectrum = (
        dot(forward_high[...], high) + dot(forward_high[...], low) + dot(forward_low[...], high)
    )
    for part in range(2):
        for tile in range(tiles):
            spread_ref[pl.ds(part * tiles + tile, count, stride=group), :] = spectrum[
                part * count : (part + 1) * count, tile * 128 : (tile + 1) * 128
            ]
    rows = lax.broadcasted_iota(jnp.int32, (8, 128), 0) % group
    lane = lax.broadcasted_iota(jnp.int32, (8, 128), 1) < channels
    sign = jnp.where(rows < tiles, -1.0, 1.0)
    for base in range(0, count * group, 8):
        block = spread_ref[base : base + 8, :]
        turned = pltpu.roll(block, channels, 1)
        firsts, seconds = [], []
        for start in range(0, 8, group):
            span = slice(start, start + group)
            left = jnp.concatenate([block[span], turned[span]], axis=0)[:, :channels]
            left_high, left_low = split_terms(left)
            left = jnp.concatenate([left_high, left_low], axis=0)
            product = dot(left, weight_ref[0, (base + start) // group])
            product = product[: 2 * group] + product[2 * group :]
            firsts.append(product[:group])
            seconds.append(product[group:])
        first = jnp.concatenate(firsts, axis=0)
        second = jnp.concatenate(seconds, axis=0)
        real = jnp.where(lane, first, pltpu.roll(second, channels, 1))
        imag = jnp.where(lane, pltpu.roll(first, channels, 1), second)
        crossed = jnp.where(rows < tiles, pltpu.roll(imag, 8 - tiles, 0), pltpu.roll(imag, tiles, 0))
        result_ref[base : base + 8, :] = real + sign * crossed
    for part in range(2):
        for tile in range(tiles):
            modes_ref[part * count : (part + 1) * count, tile * 128 : (tile + 1) * 128] = (
                result_ref[pl.ds(part * tiles + tile, count, stride=group), :]
            )
    back = back_rows(inverse_high, inverse_low, column ^ 1, modes_ref[...])
    order_ref[:layers] = back.reshape(send_ref.shape)
    store_turns(send_ref, order_ref, z)


def mix(blocks, arrived, weights, forward_table, inverse_tables):
    layers = len(blocks)
    _, rows, feat_count = blocks[0].shape
    count = weights.shape[1]
    scratch = pltpu.VMEM((count * feat_count // 64, 128), jnp.float32)
    return pl.pallas_call(
        functools.partial(mix_kernel, layers),
        out_shape=[
            jax.ShapeDtypeStruct((2 * count, feat_count), jnp.float32),
            jax.ShapeDtypeStruct((layers, rows, feat_count), jnp.float32),
        ],
        scratch_shapes=[pltpu.VMEM((2 * layers, rows, feat_count), jnp.float32), scratch, scratch],
        compiler_params=SMALL,
        name="mix",
    )(*blocks, *arrived, weights, *split_table(forward_table), *inverse_tables)


def keep_kernel(modes_ref, inverse_high, inverse_low, keep_ref, order_ref):
    z, x, y = quad()
    back = back_rows(inverse_high, inverse_low, x ^ y, modes_ref[...])
    order_ref[...] = back.reshape(keep_ref.shape)
    store_turns(keep_ref, order_ref, z)


def keep_rows(modes, inverse_tables, like):
    return pl.pallas_call(
        keep_kernel,
        out_shape=jax.ShapeDtypeStruct(like.shape, jnp.float32),
        scratch_shapes=[pltpu.VMEM(like.shape, jnp.float32)],
        compiler_params=SMALL,
        name="keep_rows",
    )(modes, *inverse_tables)


def gelu(values):
    square = jnp.minimum(values * values, 31.36)
    inner = jnp.full_like(square, GELU_TERMS[-1])
    for term in GELU_TERMS[-2::-1]:
        inner = inner * square + term
    half = 0.5 * values
    return half + half * jnp.tanh(values * inner)


def output_kernel(layers, flow_ref, table_ref, local_ref, bias_ref, modes_ref, *refs):
    own_refs, core_refs = refs[:layers], refs[layers : 2 * layers]
    out_hbm, mixed_hbm, order_ref, wide_ref, level_ref, done_ref, sent = refs[2 * layers :]
    cells_x, cells_y, feat_count = flow_ref.shape
    channels = local_ref.shape[0]
    count = modes_ref.shape[0] // 2
    copies = []
    for part in range(2):
        copies.append(
            pltpu.make_async_copy(
                modes_ref.at[pl.ds(part * count, count)],
                mixed_hbm.at[0, :, pl.ds(part * feat_count, feat_count)],
                sent.at[2 * cells_x + part],
            )
        )
        copies[-1].start()
    z, x, y = quad()
    wide_ref[...] = jnp.zeros_like(wide_ref)
    for start in range(0, WIDTH, channels):
        span = slice(start, start + channels)
        wide_ref[span, span] = local_ref[...]
        level_ref[:, span] = bias_ref[...].reshape(1, channels)
    for column, block_refs in ((x ^ y, own_refs), (x ^ y ^ 1, core_refs)):
        for turn, block_ref in zip(turns(layers), block_refs):
            order_ref[:, (z ^ turn) * 2 + column] = block_ref[...]
    table = table_ref[y, x ^ y]
    for cell in range(cells_x):
        high, low = split_terms(order_ref[cell].reshape(-1, feat_count))
        stack = jnp.concatenate([high, low, high], axis=0)
        for half in range(2):
            rows = slice(half * cells_y // 2, (half + 1) * cells_y // 2)
            for start in range(0, feat_count, WIDTH):
                columns = slice(start, start + WIDTH)
                total = dot(table[rows], stack[:, columns]) + dot(
                    flow_ref[cell, rows, columns], wide_ref[...]
                )
                done_ref[cell, rows, columns] = gelu(total + level_ref[...]).astype(done_ref.dtype)
            copies.append(
                pltpu.make_async_copy(
                    done_ref.at[cell, rows], out_hbm.at[cell, rows], sent.at[2 * cell + half]
                )
            )
            copies[-1].start()
    for copy in copies:
        copy.wait()


def make_output(flow_field, parts, table, local, bias, modes):
    cells_x, _, feat_count = flow_field.shape
    layers = len(parts) // 2
    rows, _ = modes.shape
    return pl.pallas_call(
        functools.partial(output_kernel, layers),
        out_specs=[pl.BlockSpec(memory_space=pl.ANY)] * 2,
        scratch_shapes=[
            pltpu.VMEM((cells_x, 2 * layers) + parts[0].shape[1:], jnp.float32),
            pltpu.VMEM((WIDTH, WIDTH), jnp.bfloat16),
            pltpu.VMEM((1, WIDTH), jnp.float32),
            pltpu.VMEM(flow_field.shape, jnp.bfloat16),
            pltpu.SemaphoreType.DMA((2 * cells_x + 2,)),
        ],
        out_shape=[
            jax.ShapeDtypeStruct(flow_field.shape, jnp.bfloat16),
            jax.ShapeDtypeStruct((1, rows // 2, 2 * feat_count), jnp.float32),
        ],
        compiler_params=SMALL,
        name="make_output",
    )(flow_field, table, local, bias, modes, *parts)


def row_body(flow_field, spectral_weight, local_weight, bias_terms):
    cells_x, cells_y, feat_count = flow_field.shape
    peers = lax.axis_size("gx")
    groups_y = lax.axis_size("gy")
    rows_ky = MY // groups_y // peers
    forward_scale = 1.0 / math.sqrt(cells_x * peers * cells_y * groups_y)
    inverse_scale = 1.0 / math.sqrt(MX * MY)

    send, keep = forward_y(flow_field, cells_y * groups_y, peers // 2, rows_ky)
    blocks = along_columns(add_blocks(keep, flip_core(send)), peers)
    inverse_tables = split_table(inverse_x_table(cells_x, peers, rows_ky))
    modes, send = mix(
        blocks,
        [flip_core(block) for block in blocks],
        spectral_weight,
        forward_x_table(cells_x, peers, rows_ky) * forward_scale,
        inverse_tables,
    )
    arrived = flip_core(send)
    keep = keep_rows(modes, inverse_tables, send)
    own = along_columns(join_blocks(keep, arrived, cells_x), peers)
    parts = own + [flip_core(block) for block in own]
    high, low = split_table(inverse_y_table(cells_y, groups_y, peers, rows_ky) * inverse_scale)
    table = np.concatenate([high, high, low], axis=-1)
    return tuple(make_output(flow_field, parts, table, local_weight, bias_terms, modes))


def body(flow_field, spectral_weight, local_weight, bias_terms):
    peers = lax.axis_size("gx")
    extent = lax.axis_size("gy") * flow_field.shape[1]
    paired = lax.axis_size("gy") == 2 and peers & (peers - 1) == 0 and extent & (extent - 1) == 0
    if paired and spectral_weight.shape[1] == 2 * MX and WIDTH % local_weight.shape[0] == 0:
        return row_body(flow_field, spectral_weight, local_weight, bias_terms)
    return general_body(flow_field, spectral_weight, local_weight, bias_terms)


def solution(mesh):
    placed = (P(("group", "gx"), "gy", None), P("gy", "gx", None, None), P(), P())
    return jax.shard_map(
        body,
        mesh=mesh,
        in_specs=placed,
        out_specs=(P(("group", "gx"), "gy", None), P(("group", "gy"), "gx", None)),
        check_vma=False,
    )
```

```python
import functools
import math

import jax
import jax.numpy as jnp
import ml_dtypes
import numpy as np
from jax import lax
from jax.experimental import pallas as pl
from jax.experimental.pallas import tpu as pltpu
from jax.sharding import PartitionSpec as P

MX = 32
MY = 32


def wave_number(index, count):
    return jnp.where(index < count // 2, index, index - count)


def phase_table(waves, places, extent):
    product = waves[:, None] * places[None, :] % extent
    return 2.0 * math.pi / extent * product.astype(jnp.float32)


def row_tables(ky_rows, kx_rows, x_places, extent, width):
    angle = phase_table(wave_number(kx_rows, MX), x_places, extent)
    select = (ky_rows[:, None] == jnp.arange(width, dtype=jnp.int32)[None, :]).astype(jnp.float32)
    cosine = jnp.cos(angle)[:, :, None] * select[:, None, :]
    sine_part = jnp.sin(angle)[:, :, None] * select[:, None, :]
    return (cosine, sine_part)


def forward_rows(y_local, ky_rows, kx_rows, x_places, extent):
    cosine, sine_part = row_tables(ky_rows, kx_rows, x_places, extent, y_local.shape[0])
    real_in = y_local[:, 0]
    imag_in = y_local[:, 1]

    def contract(table, values):
        return jnp.einsum("rxk,kxf->rf", table, values, precision=lax.Precision.HIGHEST)

    real_out = contract(cosine, real_in) + contract(sine_part, imag_in)
    imag_out = contract(cosine, imag_in) - contract(sine_part, real_in)
    return jnp.concatenate([real_out, imag_out], axis=1)


def inverse_rows(running, shard_rows, ky_rows, kx_rows, x_places, extent):
    cosine, sine_part = row_tables(ky_rows, kx_rows, x_places, extent, running.shape[0])
    feat_count = shard_rows.shape[1] // 2
    real_part = shard_rows[:, :feat_count]
    imag_part = shard_rows[:, feat_count:]

    def contract(table, values):
        return jnp.einsum("rxk,rf->kxf", table, values, precision=lax.Precision.HIGHEST)

    new_real = contract(cosine, real_part) - contract(sine_part, imag_part)
    new_imag = contract(cosine, imag_part) + contract(sine_part, real_part)
    return jnp.stack([new_real, new_imag], axis=1)


def general_body(flow_field, spectral_weight, local_weight, bias_terms):
    cells_x, cells_y, feat_count = flow_field.shape
    channels = local_weight.shape[0]
    planes = feat_count // channels
    groups_x = lax.axis_size("gx")
    groups_y = lax.axis_size("gy")
    extent_x = cells_x * groups_x
    extent_y = cells_y * groups_y
    half_width = MY // groups_y
    quota_rows = spectral_weight.shape[1]
    high = lax.Precision.HIGHEST
    x_places = lax.axis_index("gx") * cells_x + jnp.arange(cells_x, dtype=jnp.int32)
    y_places = lax.axis_index("gy") * cells_y + jnp.arange(cells_y, dtype=jnp.int32)
    y_angle = phase_table(wave_number(jnp.arange(MY, dtype=jnp.int32), MY), y_places, extent_y)
    y_table = (
        jnp.stack([jnp.cos(y_angle), -jnp.sin(y_angle)], axis=1)
        .reshape(2 * MY, cells_y)
        .astype(jnp.bfloat16)
    )
    y_local = lax.psum_scatter(
        jnp.einsum("qy,xyf->qxf", y_table, flow_field, preferred_element_type=jnp.float32),
        "gy",
        scatter_dimension=0,
        tiled=True,
    )
    y_local = y_local.reshape(half_width, 2, cells_x, feat_count)
    rest_index = jnp.arange(lax.axis_size("gx") * quota_rows, dtype=jnp.int32)
    spectrum = lax.psum_scatter(
        forward_rows(y_local, rest_index // MX, rest_index % MX, x_places, extent_x),
        "gx",
        scatter_dimension=0,
        tiled=True,
    )
    spectrum = spectrum * (1.0 / math.sqrt(extent_x * extent_y))
    coeffs = spectrum.reshape(quota_rows, 2, planes, channels)
    weights = spectral_weight[0].astype(jnp.float32)
    product = jnp.einsum("rpzc,rco->rpzo", coeffs, weights, precision=high)
    mixed_real = product[:, 0, :, :channels] - product[:, 1, :, channels:]
    mixed_imag = product[:, 0, :, channels:] + product[:, 1, :, :channels]
    mixed_local = jnp.stack([mixed_real, mixed_imag], axis=1).reshape(quota_rows, 2 * feat_count)
    pointwise = jnp.einsum(
        "xyzc,co->xyzo",
        flow_field.reshape(cells_x, cells_y, planes, channels),
        local_weight,
        preferred_element_type=jnp.float32,
    )
    start_half = jnp.zeros((half_width, 2, cells_x, feat_count), jnp.float32)
    shard_rows = lax.all_gather(mixed_local, "gx", axis=0, tiled=True)
    rest_index = jnp.arange(shard_rows.shape[0], dtype=jnp.int32)
    back_half = inverse_rows(
        start_half, shard_rows, rest_index // MX, rest_index % MX, x_places, extent_x
    )
    back_whole = lax.all_gather(back_half, "gy", axis=0, tiled=True)
    y_cos = jnp.cos(y_angle)
    y_sin = jnp.sin(y_angle)
    spectral = (
        jnp.einsum("kn,kxf->xnf", y_cos, back_whole[:, 0], precision=high)
        - jnp.einsum("kn,kxf->xnf", y_sin, back_whole[:, 1], precision=high)
    ) * (1.0 / math.sqrt(MX * MY))
    total = spectral.reshape(cells_x, cells_y, planes, channels) + pointwise + bias_terms
    output = (
        jax.nn.gelu(total, approximate=False)
        .reshape(cells_x, cells_y, feat_count)
        .astype(jnp.bfloat16)
    )
    return (output, mixed_local.reshape(1, quota_rows, 2 * feat_count))


SMALL = pltpu.CompilerParams(vmem_limit_bytes=20 * 1024 * 1024)
LARGE = pltpu.CompilerParams(vmem_limit_bytes=53 * 1024 * 1024)
WIDTH = 256
BIAS_TERMS = 3
GELU_TERMS = (
    0.7978849411010742,
    0.03633308410644531,
    -3.259492223151028e-05,
    -5.530622001970187e-05,
    3.964749794249656e-06,
    -1.3226382122866198e-07,
    1.7561855303327434e-09,
)


def angles(count, places, extent):
    index = np.arange(count)
    waves = np.where(index < count // 2, index, index - count)
    product = (waves[:, None] * np.asarray(places)[None, :]) % extent
    return (np.float32(2.0 * math.pi / extent) * product.astype(np.float32)).astype(np.float64)


def split_table(table):
    high = table.astype(ml_dtypes.bfloat16)
    low = (table - high.astype(np.float64)).astype(ml_dtypes.bfloat16)
    return high, low


def split_terms(values):
    high = values.astype(jnp.bfloat16)
    low = (values - high.astype(jnp.float32)).astype(jnp.bfloat16)
    return high, low


def quad():
    place = lax.axis_index("gx")
    return place // 2, place % 2, lax.axis_index("gy")


def turns(layers):
    half = layers // 2
    return list(range(half, layers)) + list(range(half - 1, -1, -1))


def forward_x_table(cells_x, peers, rows_ky):
    extent = cells_x * peers
    angle = angles(MX, np.arange(extent), extent)
    cosine, sine = np.cos(angle), np.sin(angle)
    out = np.zeros((2, rows_ky, MX, extent, rows_ky, 2))
    for row in range(rows_ky):
        out[0, row, :, :, row, 0] = cosine
        out[0, row, :, :, row, 1] = sine
        out[1, row, :, :, row, 1] = cosine
        out[1, row, :, :, row, 0] = -sine
    return out.reshape(2 * rows_ky * MX, extent * rows_ky * 2)


def inverse_x_table(cells_x, peers, rows_ky):
    extent = cells_x * peers
    angle = angles(MX, np.arange(extent), extent)
    cosine, sine = np.cos(angle).T, np.sin(angle).T
    out = np.zeros((extent, rows_ky, 2, 2, rows_ky, MX))
    for row in range(rows_ky):
        out[:, row, 0, 0, row, :] = cosine
        out[:, row, 0, 1, row, :] = -sine
        out[:, row, 1, 1, row, :] = cosine
        out[:, row, 1, 0, row, :] = sine
    out = out.reshape(peers // 2, 2, cells_x * rows_ky * 2, 2 * rows_ky * MX)
    return np.moveaxis(out, 1, 0).reshape(2, -1, 2 * rows_ky * MX)


def inverse_y_table(cells_y, groups_y, peers, rows_ky):
    extent = cells_y * groups_y
    angle = angles(MY, np.arange(extent), extent)
    full = np.stack([np.cos(angle), -np.sin(angle)], axis=1)
    full = full.reshape(groups_y, peers, rows_ky, 2, groups_y, cells_y)
    out = np.zeros((groups_y, 2, cells_y, peers, 2, rows_ky, 2))
    for y in range(groups_y):
        for column in range(2):
            for peer in range(peers):
                for place in range(2):
                    half = y ^ place ^ column ^ (peer % 2)
                    out[y, column, :, peer, place] = np.moveaxis(full[half, peer, :, :, y], -1, 0)
    return out.reshape(groups_y, 2, cells_y, 4 * peers * rows_ky)


def output_table(table):
    high, low = split_table(table)
    parts = [high, high, low, np.ones(table.shape[:-1] + (BIAS_TERMS,), high.dtype)]
    used = 3 * table.shape[-1] + BIAS_TERMS
    parts.append(np.zeros(table.shape[:-1] + (-used % 256,), high.dtype))
    return np.concatenate(parts, axis=-1)


def dot(left, right):
    return jnp.dot(left, right, preferred_element_type=jnp.float32)


def forward_y_table(shape, extent, layers, rows_ky):
    z, x, y = quad()
    peers = 2 * layers
    row = lax.broadcasted_iota(jnp.int32, (shape[0], 1), 0)
    block = row // (2 * rows_ky)
    place = block // 2 % layers
    turn = jnp.where(place < layers // 2, place + layers // 2, layers - 1 - place)
    side = y ^ (1 - block // peers)
    owner = (side ^ (block % 2)) * peers + (z ^ turn) * 2 + (x ^ side)
    index = owner * rows_ky + row // 2 % rows_ky
    y_places = lax.broadcasted_iota(jnp.int32, (1, shape[1]), 1) + y * shape[1]
    steps = (wave_number(index, MY) * y_places) & (extent - 1)
    angle = 2.0 * math.pi / extent * steps.astype(jnp.float32)
    return jnp.where(row % 2 == 0, jnp.cos(angle), -jnp.sin(angle)).astype(jnp.bfloat16)


def forward_y_kernel(extent, rows_ky, flow_hbm, send_ref, keep_ref, flow_ref, arrived):
    layers, _, rows, feat_count = send_ref.shape
    cells_x, cells_y, _ = flow_ref.shape
    rows = rows // cells_x
    copies = [
        pltpu.make_async_copy(flow_hbm.at[x], flow_ref.at[x], arrived.at[x])
        for x in range(cells_x)
    ]
    for copy in copies:
        copy.start()
    table = forward_y_table((2 * MY, cells_y), extent, layers, rows_ky)
    for x in range(cells_x):
        copies[x].wait()
        result = dot(table, flow_ref[x]).reshape(2, layers, 2, rows, feat_count)
        send_ref[:, :, x * rows : (x + 1) * rows, :] = result[0]
        keep_ref[:, :, x * rows : (x + 1) * rows, :] = result[1]


def forward_y(flow_field, extent, layers, rows_ky):
    cells_x, _, feat_count = flow_field.shape
    shape = jax.ShapeDtypeStruct((layers, 2, cells_x * 2 * rows_ky, feat_count), jnp.float32)
    return pl.pallas_call(
        functools.partial(forward_y_kernel, extent, rows_ky),
        in_specs=[pl.BlockSpec(memory_space=pltpu.HBM)],
        out_shape=[shape] * 2,
        scratch_shapes=[
            pltpu.VMEM(flow_field.shape, flow_field.dtype),
            pltpu.SemaphoreType.DMA((cells_x,)),
        ],
        compiler_params=LARGE,
        name="forward_y",
    )(flow_field)


def flip_core(block):
    return lax.ppermute(block, "gy", [(0, 1), (1, 0)])


def along_columns(blocks, peers):
    arrived = []
    for turn, block in zip(turns(len(blocks)), blocks):
        pairs = [
            (2 * place + core, 2 * (place ^ (2 * turn + core)) + core)
            for place in range(peers)
            for core in range(2)
        ]
        arrived.append(lax.ppermute(block, ("gx", "gy"), pairs))
    return arrived


def small_call(kernel, out_shape, name):
    return pl.pallas_call(kernel, out_shape=out_shape, compiler_params=SMALL, name=name)


def add_kernel(keep_ref, arrived_ref, *out_refs):
    for turn, out_ref in enumerate(out_refs):
        out_ref[...] = keep_ref[turn] + arrived_ref[turn]


def add_blocks(keep, arrived):
    shape = jax.ShapeDtypeStruct(keep.shape[1:], keep.dtype)
    return small_call(add_kernel, [shape] * keep.shape[0], "add_blocks")(keep, arrived)


def join_kernel(keep_ref, arrived_ref, *out_refs):
    cells_x, rows, _ = out_refs[0].shape
    rows = rows // 2
    for turn, out_ref in enumerate(out_refs):
        for cell in range(cells_x):
            span = slice(cell * rows, (cell + 1) * rows)
            out_ref[cell] = jnp.concatenate(
                [keep_ref[turn, span, :], arrived_ref[turn, span, :]], axis=0
            )


def join_blocks(keep, arrived, cells_x):
    layers, rows, feat_count = keep.shape
    shape = jax.ShapeDtypeStruct((cells_x, 2 * rows // cells_x, feat_count), keep.dtype)
    return small_call(join_kernel, [shape] * layers, "join_blocks")(keep, arrived)


def back_rows(inverse_high, inverse_low, column, modes):
    high, low = split_terms(modes)
    table = inverse_high[column]
    return dot(table, high) + dot(table, low) + dot(inverse_low[column], high)


def store_turns(out_ref, order_ref, z):
    for index, turn in enumerate(turns(out_ref.shape[0])):
        out_ref[index] = order_ref[z ^ turn]


def mix_kernel(layers, *refs):
    block_refs, arrived_refs = refs[:layers], refs[layers : 2 * layers]
    weight_ref, forward_high, forward_low, inverse_high, inverse_low = refs[
        2 * layers : 2 * layers + 5
    ]
    modes_ref, send_ref, order_ref, spread_ref, result_ref = refs[2 * layers + 5 :]
    z, x, y = quad()
    column = x ^ y
    for index, turn in enumerate(turns(layers)):
        order_ref[(z ^ turn) * 2 + column] = block_refs[index][0]
        order_ref[(z ^ turn) * 2 + (column ^ 1)] = arrived_refs[index][1]
    feat_count = order_ref.shape[-1]
    count = weight_ref.shape[1]
    channels = weight_ref.shape[2]
    tiles = feat_count // 128
    group = 2 * tiles
    high, low = split_terms(order_ref[...].reshape(-1, feat_count))
    spectrum = (
        dot(forward_high[...], high) + dot(forward_high[...], low) + dot(forward_low[...], high)
    )
    for part in range(2):
        for tile in range(tiles):
            spread_ref[pl.ds(part * tiles + tile, count, stride=group), :] = spectrum[
                part * count : (part + 1) * count, tile * 128 : (tile + 1) * 128
            ]
    rows = lax.broadcasted_iota(jnp.int32, (8, 128), 0) % group
    lane = lax.broadcasted_iota(jnp.int32, (8, 128), 1) < channels
    sign = jnp.where(rows < tiles, -1.0, 1.0)
    for base in range(0, count * group, 8):
        block = spread_ref[base : base + 8, :]
        turned = pltpu.roll(block, channels, 1)
        firsts, seconds = [], []
        for start in range(0, 8, group):
            span = slice(start, start + group)
            left = jnp.concatenate([block[span], turned[span]], axis=0)[:, :channels]
            left_high, left_low = split_terms(left)
            left = jnp.concatenate([left_high, left_low], axis=0)
            product = dot(left, weight_ref[0, (base + start) // group])
            product = product[: 2 * group] + product[2 * group :]
            firsts.append(product[:group])
            seconds.append(product[group:])
        first = jnp.concatenate(firsts, axis=0)
        second = jnp.concatenate(seconds, axis=0)
        real = jnp.where(lane, first, pltpu.roll(second, channels, 1))
        imag = jnp.where(lane, pltpu.roll(first, channels, 1), second)
        crossed = jnp.where(rows < tiles, pltpu.roll(imag, 8 - tiles, 0), pltpu.roll(imag, tiles, 0))
        result_ref[base : base + 8, :] = real + sign * crossed
    for part in range(2):
        for tile in range(tiles):
            modes_ref[part * count : (part + 1) * count, tile * 128 : (tile + 1) * 128] = (
                result_ref[pl.ds(part * tiles + tile, count, stride=group), :]
            )
    back = back_rows(inverse_high, inverse_low, column ^ 1, modes_ref[...])
    order_ref[:layers] = back.reshape(send_ref.shape)
    store_turns(send_ref, order_ref, z)


def mix(blocks, arrived, weights, forward_table, inverse_tables):
    layers = len(blocks)
    _, rows, feat_count = blocks[0].shape
    count = weights.shape[1]
    scratch = pltpu.VMEM((count * feat_count // 64, 128), jnp.float32)
    return pl.pallas_call(
        functools.partial(mix_kernel, layers),
        out_shape=[
            jax.ShapeDtypeStruct((2 * count, feat_count), jnp.float32),
            jax.ShapeDtypeStruct((layers, rows, feat_count), jnp.float32),
        ],
        scratch_shapes=[pltpu.VMEM((2 * layers, rows, feat_count), jnp.float32), scratch, scratch],
        compiler_params=SMALL,
        name="mix",
    )(*blocks, *arrived, weights, *split_table(forward_table), *inverse_tables)


def keep_kernel(modes_ref, inverse_high, inverse_low, keep_ref, order_ref):
    z, x, y = quad()
    back = back_rows(inverse_high, inverse_low, x ^ y, modes_ref[...])
    order_ref[...] = back.reshape(keep_ref.shape)
    store_turns(keep_ref, order_ref, z)


def keep_rows(modes, inverse_tables, like):
    return pl.pallas_call(
        keep_kernel,
        out_shape=jax.ShapeDtypeStruct(like.shape, jnp.float32),
        scratch_shapes=[pltpu.VMEM(like.shape, jnp.float32)],
        compiler_params=SMALL,
        name="keep_rows",
    )(modes, *inverse_tables)


def gelu(values):
    square = jnp.minimum(values * values, 31.36)
    inner = jnp.full_like(square, GELU_TERMS[-1])
    for term in GELU_TERMS[-2::-1]:
        inner = inner * square + term
    half = 0.5 * values
    return half + half * jnp.tanh(values * inner)


def output_kernel(layers, flow_ref, table_ref, local_ref, bias_ref, modes_ref, *refs):
    own_refs, core_refs = refs[:layers], refs[layers : 2 * layers]
    out_hbm, mixed_hbm, order_ref, wide_ref, level_ref, done_ref, sent = refs[2 * layers :]
    cells_x, _, feat_count = flow_ref.shape
    channels = local_ref.shape[0]
    count = modes_ref.shape[0] // 2
    copies = []
    for part in range(2):
        copies.append(
            pltpu.make_async_copy(
                modes_ref.at[pl.ds(part * count, count)],
                mixed_hbm.at[0, :, pl.ds(part * feat_count, feat_count)],
                sent.at[cells_x + part],
            )
        )
        copies[-1].start()
    z, x, y = quad()
    wide_ref[...] = jnp.zeros_like(wide_ref)
    for start in range(0, WIDTH, channels):
        span = slice(start, start + channels)
        wide_ref[span, span] = local_ref[...]
        level_ref[:, span] = bias_ref[...].reshape(1, channels)
    level = level_ref[...]
    levels = []
    for _ in range(BIAS_TERMS):
        levels.append(level.astype(jnp.bfloat16).astype(jnp.float32))
        level = level - levels[-1]
    terms = 3 * order_ref.shape[1] * order_ref.shape[2]
    filled = jnp.zeros((table_ref.shape[-1] - terms - BIAS_TERMS, WIDTH), jnp.float32)
    below = jnp.concatenate(levels + [filled], axis=0).astype(jnp.bfloat16)
    below = jnp.concatenate([below, wide_ref[...]], axis=0)
    for column, block_refs in ((x ^ y, own_refs), (x ^ y ^ 1, core_refs)):
        for turn, block_ref in zip(turns(layers), block_refs):
            order_ref[:, (z ^ turn) * 2 + column] = block_ref[...]
    table = table_ref[y, x ^ y]
    for cell in range(cells_x):
        high, low = split_terms(order_ref[cell].reshape(-1, feat_count))
        stack = jnp.concatenate([high, low, high], axis=0)
        for start in range(0, feat_count, WIDTH):
            columns = slice(start, start + WIDTH)
            total = dot(
                jnp.concatenate([table, flow_ref[cell, :, columns]], axis=1),
                jnp.concatenate([stack[:, columns], below], axis=0),
            )
            done_ref[cell, :, columns] = gelu(total).astype(done_ref.dtype)
        copies.append(pltpu.make_async_copy(done_ref.at[cell], out_hbm.at[cell], sent.at[cell]))
        copies[-1].start()
    for copy in copies:
        copy.wait()


def make_output(flow_field, parts, table, local, bias, modes):
    cells_x, _, feat_count = flow_field.shape
    layers = len(parts) // 2
    rows, _ = modes.shape
    return pl.pallas_call(
        functools.partial(output_kernel, layers),
        out_specs=[pl.BlockSpec(memory_space=pl.ANY)] * 2,
        scratch_shapes=[
            pltpu.VMEM((cells_x, 2 * layers) + parts[0].shape[1:], jnp.float32),
            pltpu.VMEM((WIDTH, WIDTH), jnp.bfloat16),
            pltpu.VMEM((1, WIDTH), jnp.float32),
            pltpu.VMEM(flow_field.shape, jnp.bfloat16),
            pltpu.SemaphoreType.DMA((cells_x + 2,)),
        ],
        out_shape=[
            jax.ShapeDtypeStruct(flow_field.shape, jnp.bfloat16),
            jax.ShapeDtypeStruct((1, rows // 2, 2 * feat_count), jnp.float32),
        ],
        compiler_params=SMALL,
        name="make_output",
    )(flow_field, table, local, bias, modes, *parts)


def row_body(flow_field, spectral_weight, local_weight, bias_terms):
    cells_x, cells_y, feat_count = flow_field.shape
    peers = lax.axis_size("gx")
    groups_y = lax.axis_size("gy")
    rows_ky = MY // groups_y // peers
    forward_scale = 1.0 / math.sqrt(cells_x * peers * cells_y * groups_y)
    inverse_scale = 1.0 / math.sqrt(MX * MY)

    send, keep = forward_y(flow_field, cells_y * groups_y, peers // 2, rows_ky)
    blocks = along_columns(add_blocks(keep, flip_core(send)), peers)
    inverse_tables = split_table(inverse_x_table(cells_x, peers, rows_ky))
    modes, send = mix(
        blocks,
        [flip_core(block) for block in blocks],
        spectral_weight,
        forward_x_table(cells_x, peers, rows_ky) * forward_scale,
        inverse_tables,
    )
    arrived = flip_core(send)
    keep = keep_rows(modes, inverse_tables, send)
    own = along_columns(join_blocks(keep, arrived, cells_x), peers)
    parts = own + [flip_core(block) for block in own]
    table = output_table(inverse_y_table(cells_y, groups_y, peers, rows_ky) * inverse_scale)
    return tuple(make_output(flow_field, parts, table, local_weight, bias_terms, modes))


def body(flow_field, spectral_weight, local_weight, bias_terms):
    peers = lax.axis_size("gx")
    extent = lax.axis_size("gy") * flow_field.shape[1]
    paired = lax.axis_size("gy") == 2 and peers & (peers - 1) == 0 and extent & (extent - 1) == 0
    if paired and spectral_weight.shape[1] == 2 * MX and WIDTH % local_weight.shape[0] == 0:
        return row_body(flow_field, spectral_weight, local_weight, bias_terms)
    return general_body(flow_field, spectral_weight, local_weight, bias_terms)


def solution(mesh):
    placed = (P(("group", "gx"), "gy", None), P("gy", "gx", None, None), P(), P())
    return jax.shard_map(
        body,
        mesh=mesh,
        in_specs=placed,
        out_specs=(P(("group", "gx"), "gy", None), P(("group", "gy"), "gx", None)),
        check_vma=False,
    )
```

```python
import functools
import math

import jax
import jax.numpy as jnp
import ml_dtypes
import numpy as np
from jax import lax
from jax.experimental import pallas as pl
from jax.experimental.pallas import tpu as pltpu
from jax.sharding import PartitionSpec as P

MX = 32
MY = 32


def wave_number(index, count):
    return jnp.where(index < count // 2, index, index - count)


def phase_table(waves, places, extent):
    product = waves[:, None] * places[None, :] % extent
    return 2.0 * math.pi / extent * product.astype(jnp.float32)


def row_tables(ky_rows, kx_rows, x_places, extent, width):
    angle = phase_table(wave_number(kx_rows, MX), x_places, extent)
    select = (ky_rows[:, None] == jnp.arange(width, dtype=jnp.int32)[None, :]).astype(jnp.float32)
    cosine = jnp.cos(angle)[:, :, None] * select[:, None, :]
    sine_part = jnp.sin(angle)[:, :, None] * select[:, None, :]
    return (cosine, sine_part)


def forward_rows(y_local, ky_rows, kx_rows, x_places, extent):
    cosine, sine_part = row_tables(ky_rows, kx_rows, x_places, extent, y_local.shape[0])
    real_in = y_local[:, 0]
    imag_in = y_local[:, 1]

    def contract(table, values):
        return jnp.einsum("rxk,kxf->rf", table, values, precision=lax.Precision.HIGHEST)

    real_out = contract(cosine, real_in) + contract(sine_part, imag_in)
    imag_out = contract(cosine, imag_in) - contract(sine_part, real_in)
    return jnp.concatenate([real_out, imag_out], axis=1)


def inverse_rows(running, shard_rows, ky_rows, kx_rows, x_places, extent):
    cosine, sine_part = row_tables(ky_rows, kx_rows, x_places, extent, running.shape[0])
    feat_count = shard_rows.shape[1] // 2
    real_part = shard_rows[:, :feat_count]
    imag_part = shard_rows[:, feat_count:]

    def contract(table, values):
        return jnp.einsum("rxk,rf->kxf", table, values, precision=lax.Precision.HIGHEST)

    new_real = contract(cosine, real_part) - contract(sine_part, imag_part)
    new_imag = contract(cosine, imag_part) + contract(sine_part, real_part)
    return jnp.stack([new_real, new_imag], axis=1)


def general_body(flow_field, spectral_weight, local_weight, bias_terms):
    cells_x, cells_y, feat_count = flow_field.shape
    channels = local_weight.shape[0]
    planes = feat_count // channels
    groups_x = lax.axis_size("gx")
    groups_y = lax.axis_size("gy")
    extent_x = cells_x * groups_x
    extent_y = cells_y * groups_y
    half_width = MY // groups_y
    quota_rows = spectral_weight.shape[1]
    high = lax.Precision.HIGHEST
    x_places = lax.axis_index("gx") * cells_x + jnp.arange(cells_x, dtype=jnp.int32)
    y_places = lax.axis_index("gy") * cells_y + jnp.arange(cells_y, dtype=jnp.int32)
    y_angle = phase_table(wave_number(jnp.arange(MY, dtype=jnp.int32), MY), y_places, extent_y)
    y_table = (
        jnp.stack([jnp.cos(y_angle), -jnp.sin(y_angle)], axis=1)
        .reshape(2 * MY, cells_y)
        .astype(jnp.bfloat16)
    )
    y_local = lax.psum_scatter(
        jnp.einsum("qy,xyf->qxf", y_table, flow_field, preferred_element_type=jnp.float32),
        "gy",
        scatter_dimension=0,
        tiled=True,
    )
    y_local = y_local.reshape(half_width, 2, cells_x, feat_count)
    rest_index = jnp.arange(lax.axis_size("gx") * quota_rows, dtype=jnp.int32)
    spectrum = lax.psum_scatter(
        forward_rows(y_local, rest_index // MX, rest_index % MX, x_places, extent_x),
        "gx",
        scatter_dimension=0,
        tiled=True,
    )
    spectrum = spectrum * (1.0 / math.sqrt(extent_x * extent_y))
    coeffs = spectrum.reshape(quota_rows, 2, planes, channels)
    weights = spectral_weight[0].astype(jnp.float32)
    product = jnp.einsum("rpzc,rco->rpzo", coeffs, weights, precision=high)
    mixed_real = product[:, 0, :, :channels] - product[:, 1, :, channels:]
    mixed_imag = product[:, 0, :, channels:] + product[:, 1, :, :channels]
    mixed_local = jnp.stack([mixed_real, mixed_imag], axis=1).reshape(quota_rows, 2 * feat_count)
    pointwise = jnp.einsum(
        "xyzc,co->xyzo",
        flow_field.reshape(cells_x, cells_y, planes, channels),
        local_weight,
        preferred_element_type=jnp.float32,
    )
    start_half = jnp.zeros((half_width, 2, cells_x, feat_count), jnp.float32)
    shard_rows = lax.all_gather(mixed_local, "gx", axis=0, tiled=True)
    rest_index = jnp.arange(shard_rows.shape[0], dtype=jnp.int32)
    back_half = inverse_rows(
        start_half, shard_rows, rest_index // MX, rest_index % MX, x_places, extent_x
    )
    back_whole = lax.all_gather(back_half, "gy", axis=0, tiled=True)
    y_cos = jnp.cos(y_angle)
    y_sin = jnp.sin(y_angle)
    spectral = (
        jnp.einsum("kn,kxf->xnf", y_cos, back_whole[:, 0], precision=high)
        - jnp.einsum("kn,kxf->xnf", y_sin, back_whole[:, 1], precision=high)
    ) * (1.0 / math.sqrt(MX * MY))
    total = spectral.reshape(cells_x, cells_y, planes, channels) + pointwise + bias_terms
    output = (
        jax.nn.gelu(total, approximate=False)
        .reshape(cells_x, cells_y, feat_count)
        .astype(jnp.bfloat16)
    )
    return (output, mixed_local.reshape(1, quota_rows, 2 * feat_count))


SMALL = pltpu.CompilerParams(vmem_limit_bytes=20 * 1024 * 1024)
LARGE = pltpu.CompilerParams(vmem_limit_bytes=53 * 1024 * 1024)
WIDTH = 256
BIAS_TERMS = 3
GELU_TERMS = (
    0.7978849411010742,
    0.03633308410644531,
    -3.259492223151028e-05,
    -5.530622001970187e-05,
    3.964749794249656e-06,
    -1.3226382122866198e-07,
    1.7561855303327434e-09,
)


def angles(count, places, extent):
    index = np.arange(count)
    waves = np.where(index < count // 2, index, index - count)
    product = (waves[:, None] * np.asarray(places)[None, :]) % extent
    return (np.float32(2.0 * math.pi / extent) * product.astype(np.float32)).astype(np.float64)


def split_table(table):
    high = table.astype(ml_dtypes.bfloat16)
    low = (table - high.astype(np.float64)).astype(ml_dtypes.bfloat16)
    return high, low


def split_terms(values):
    high = values.astype(jnp.bfloat16)
    low = (values - high.astype(jnp.float32)).astype(jnp.bfloat16)
    return high, low


def quad():
    place = lax.axis_index("gx")
    return place // 2, place % 2, lax.axis_index("gy")


def turns(layers):
    half = layers // 2
    return list(range(half, layers)) + list(range(half - 1, -1, -1))


def forward_x_table(cells_x, peers, rows_ky):
    extent = cells_x * peers
    angle = angles(MX, np.arange(extent), extent)
    cosine, sine = np.cos(angle), np.sin(angle)
    out = np.zeros((2, rows_ky, MX, extent, rows_ky, 2))
    for row in range(rows_ky):
        out[0, row, :, :, row, 0] = cosine
        out[0, row, :, :, row, 1] = sine
        out[1, row, :, :, row, 1] = cosine
        out[1, row, :, :, row, 0] = -sine
    return out.reshape(2 * rows_ky * MX, extent * rows_ky * 2)


def inverse_x_table(cells_x, peers, rows_ky):
    extent = cells_x * peers
    angle = angles(MX, np.arange(extent), extent)
    cosine, sine = np.cos(angle).T, np.sin(angle).T
    out = np.zeros((extent, rows_ky, 2, 2, rows_ky, MX))
    for row in range(rows_ky):
        out[:, row, 0, 0, row, :] = cosine
        out[:, row, 0, 1, row, :] = -sine
        out[:, row, 1, 1, row, :] = cosine
        out[:, row, 1, 0, row, :] = sine
    out = out.reshape(peers // 2, 2, cells_x * rows_ky * 2, 2 * rows_ky * MX)
    return np.moveaxis(out, 1, 0).reshape(2, -1, 2 * rows_ky * MX)


def inverse_y_table(cells_y, groups_y, peers, rows_ky):
    extent = cells_y * groups_y
    angle = angles(MY, np.arange(extent), extent)
    full = np.stack([np.cos(angle), -np.sin(angle)], axis=1)
    full = full.reshape(groups_y, peers, rows_ky, 2, groups_y, cells_y)
    out = np.zeros((groups_y, 2, cells_y, peers, 2, rows_ky, 2))
    for y in range(groups_y):
        for column in range(2):
            for peer in range(peers):
                for place in range(2):
                    half = y ^ place ^ column ^ (peer % 2)
                    out[y, column, :, peer, place] = np.moveaxis(full[half, peer, :, :, y], -1, 0)
    return out.reshape(groups_y, 2, cells_y, 4 * peers * rows_ky)


def output_table(table):
    high, low = split_table(table)
    parts = [high, high, low, np.ones(table.shape[:-1] + (BIAS_TERMS,), high.dtype)]
    used = 3 * table.shape[-1] + BIAS_TERMS
    parts.append(np.zeros(table.shape[:-1] + (-used % 256,), high.dtype))
    return np.concatenate(parts, axis=-1)


def dot(left, right):
    return jnp.dot(left, right, preferred_element_type=jnp.float32)


def forward_y_table(shape, extent, layers, rows_ky):
    z, x, y = quad()
    peers = 2 * layers
    row = lax.broadcasted_iota(jnp.int32, (shape[0], 1), 0)
    block = row // (2 * rows_ky)
    place = block // 2 % layers
    turn = jnp.where(place < layers // 2, place + layers // 2, layers - 1 - place)
    side = y ^ (1 - block // peers)
    owner = (side ^ (block % 2)) * peers + (z ^ turn) * 2 + (x ^ side)
    index = owner * rows_ky + row // 2 % rows_ky
    y_places = lax.broadcasted_iota(jnp.int32, (1, shape[1]), 1) + y * shape[1]
    steps = (wave_number(index, MY) * y_places) & (extent - 1)
    angle = 2.0 * math.pi / extent * steps.astype(jnp.float32)
    return jnp.where(row % 2 == 0, jnp.cos(angle), -jnp.sin(angle)).astype(jnp.bfloat16)


def forward_y_kernel(extent, rows_ky, flow_hbm, send_ref, keep_ref, flow_ref, arrived):
    layers, _, rows, feat_count = send_ref.shape
    cells_x, cells_y, _ = flow_ref.shape
    rows = rows // cells_x
    copies = [
        pltpu.make_async_copy(flow_hbm.at[x], flow_ref.at[x], arrived.at[x])
        for x in range(cells_x)
    ]
    for copy in copies:
        copy.start()
    table = forward_y_table((2 * MY, cells_y), extent, layers, rows_ky)
    for x in range(cells_x):
        copies[x].wait()
        result = dot(table, flow_ref[x]).reshape(2, layers, 2, rows, feat_count)
        send_ref[:, :, x * rows : (x + 1) * rows, :] = result[0]
        keep_ref[:, :, x * rows : (x + 1) * rows, :] = result[1]


def forward_y(flow_field, extent, layers, rows_ky):
    cells_x, _, feat_count = flow_field.shape
    shape = jax.ShapeDtypeStruct((layers, 2, cells_x * 2 * rows_ky, feat_count), jnp.float32)
    return pl.pallas_call(
        functools.partial(forward_y_kernel, extent, rows_ky),
        in_specs=[pl.BlockSpec(memory_space=pltpu.HBM)],
        out_shape=[shape] * 2,
        scratch_shapes=[
            pltpu.VMEM(flow_field.shape, flow_field.dtype),
            pltpu.SemaphoreType.DMA((cells_x,)),
        ],
        compiler_params=LARGE,
        name="forward_y",
    )(flow_field)


def flip_core(block):
    return lax.ppermute(block, "gy", [(0, 1), (1, 0)])


def along_columns(blocks, peers):
    arrived = []
    for turn, block in zip(turns(len(blocks)), blocks):
        pairs = [
            (2 * place + core, 2 * (place ^ (2 * turn + core)) + core)
            for place in range(peers)
            for core in range(2)
        ]
        arrived.append(lax.ppermute(block, ("gx", "gy"), pairs))
    return arrived


def small_call(kernel, out_shape, name):
    return pl.pallas_call(kernel, out_shape=out_shape, compiler_params=SMALL, name=name)


def second_kernel(block_ref, out_ref):
    out_ref[...] = block_ref[1]


def second_half(block):
    shape = jax.ShapeDtypeStruct(block.shape[1:], block.dtype)
    return small_call(second_kernel, shape, "second_half")(block)


def add_kernel(keep_ref, arrived_ref, *out_refs):
    for turn, out_ref in enumerate(out_refs):
        out_ref[...] = keep_ref[turn] + arrived_ref[turn]


def add_blocks(keep, arrived):
    shape = jax.ShapeDtypeStruct(keep.shape[1:], keep.dtype)
    return small_call(add_kernel, [shape] * keep.shape[0], "add_blocks")(keep, arrived)


def join_kernel(keep_ref, arrived_ref, *out_refs):
    cells_x, rows, _ = out_refs[0].shape
    rows = rows // 2
    for turn, out_ref in enumerate(out_refs):
        for cell in range(cells_x):
            span = slice(cell * rows, (cell + 1) * rows)
            out_ref[cell] = jnp.concatenate(
                [keep_ref[turn, span, :], arrived_ref[turn, span, :]], axis=0
            )


def join_blocks(keep, arrived, cells_x):
    layers, rows, feat_count = keep.shape
    shape = jax.ShapeDtypeStruct((cells_x, 2 * rows // cells_x, feat_count), keep.dtype)
    return small_call(join_kernel, [shape] * layers, "join_blocks")(keep, arrived)


def back_rows(inverse_high, inverse_low, column, modes):
    high, low = split_terms(modes)
    table = inverse_high[column]
    return dot(table, high) + dot(table, low) + dot(inverse_low[column], high)


def store_turns(out_ref, order_ref, z):
    for index, turn in enumerate(turns(out_ref.shape[0])):
        out_ref[index] = order_ref[z ^ turn]


def mix_kernel(layers, *refs):
    block_refs, arrived_refs = refs[:layers], refs[layers : 2 * layers]
    weight_ref, forward_high, forward_low, inverse_high, inverse_low = refs[
        2 * layers : 2 * layers + 5
    ]
    modes_ref, send_ref, order_ref, spread_ref, result_ref = refs[2 * layers + 5 :]
    z, x, y = quad()
    column = x ^ y
    for index, turn in enumerate(turns(layers)):
        order_ref[(z ^ turn) * 2 + column] = block_refs[index][0]
        order_ref[(z ^ turn) * 2 + (column ^ 1)] = arrived_refs[index][...]
    feat_count = order_ref.shape[-1]
    count = weight_ref.shape[1]
    channels = weight_ref.shape[2]
    tiles = feat_count // 128
    group = 2 * tiles
    high, low = split_terms(order_ref[...].reshape(-1, feat_count))
    spectrum = (
        dot(forward_high[...], high) + dot(forward_high[...], low) + dot(forward_low[...], high)
    )
    for part in range(2):
        for tile in range(tiles):
            spread_ref[pl.ds(part * tiles + tile, count, stride=group), :] = spectrum[
                part * count : (part + 1) * count, tile * 128 : (tile + 1) * 128
            ]
    rows = lax.broadcasted_iota(jnp.int32, (8, 128), 0) % group
    lane = lax.broadcasted_iota(jnp.int32, (8, 128), 1) < channels
    sign = jnp.where(rows < tiles, -1.0, 1.0)
    for base in range(0, count * group, 8):
        block = spread_ref[base : base + 8, :]
        turned = pltpu.roll(block, channels, 1)
        firsts, seconds = [], []
        for start in range(0, 8, group):
            span = slice(start, start + group)
            left = jnp.concatenate([block[span], turned[span]], axis=0)[:, :channels]
            left_high, left_low = split_terms(left)
            left = jnp.concatenate([left_high, left_low], axis=0)
            product = dot(left, weight_ref[0, (base + start) // group])
            product = product[: 2 * group] + product[2 * group :]
            firsts.append(product[:group])
            seconds.append(product[group:])
        first = jnp.concatenate(firsts, axis=0)
        second = jnp.concatenate(seconds, axis=0)
        real = jnp.where(lane, first, pltpu.roll(second, channels, 1))
        imag = jnp.where(lane, pltpu.roll(first, channels, 1), second)
        crossed = jnp.where(rows < tiles, pltpu.roll(imag, 8 - tiles, 0), pltpu.roll(imag, tiles, 0))
        result_ref[base : base + 8, :] = real + sign * crossed
    for part in range(2):
        for tile in range(tiles):
            modes_ref[part * count : (part + 1) * count, tile * 128 : (tile + 1) * 128] = (
                result_ref[pl.ds(part * tiles + tile, count, stride=group), :]
            )
    back = back_rows(inverse_high, inverse_low, column ^ 1, modes_ref[...])
    order_ref[:layers] = back.reshape(send_ref.shape)
    store_turns(send_ref, order_ref, z)


def mix(blocks, arrived, weights, forward_table, inverse_tables):
    layers = len(blocks)
    _, rows, feat_count = blocks[0].shape
    count = weights.shape[1]
    scratch = pltpu.VMEM((count * feat_count // 64, 128), jnp.float32)
    return pl.pallas_call(
        functools.partial(mix_kernel, layers),
        out_shape=[
            jax.ShapeDtypeStruct((2 * count, feat_count), jnp.float32),
            jax.ShapeDtypeStruct((layers, rows, feat_count), jnp.float32),
        ],
        scratch_shapes=[pltpu.VMEM((2 * layers, rows, feat_count), jnp.float32), scratch, scratch],
        compiler_params=SMALL,
        name="mix",
    )(*blocks, *arrived, weights, *split_table(forward_table), *inverse_tables)


def keep_kernel(modes_ref, inverse_high, inverse_low, mixed_ref, keep_ref, order_ref):
    z, x, y = quad()
    count = mixed_ref.shape[1]
    feat_count = modes_ref.shape[1]
    for part in range(2):
        mixed_ref[0, :, part * feat_count : (part + 1) * feat_count] = modes_ref[
            part * count : (part + 1) * count
        ]
    back = back_rows(inverse_high, inverse_low, x ^ y, modes_ref[...])
    order_ref[...] = back.reshape(keep_ref.shape)
    store_turns(keep_ref, order_ref, z)


def keep_rows(modes, inverse_tables, like):
    rows, feat_count = modes.shape
    return pl.pallas_call(
        keep_kernel,
        out_shape=[
            jax.ShapeDtypeStruct((1, rows // 2, 2 * feat_count), jnp.float32),
            jax.ShapeDtypeStruct(like.shape, jnp.float32),
        ],
        scratch_shapes=[pltpu.VMEM(like.shape, jnp.float32)],
        compiler_params=SMALL,
        name="keep_rows",
    )(modes, *inverse_tables)


def gelu(values):
    square = jnp.minimum(values * values, 31.36)
    inner = jnp.full_like(square, GELU_TERMS[-1])
    for term in GELU_TERMS[-2::-1]:
        inner = inner * square + term
    half = 0.5 * values
    return half + half * jnp.tanh(values * inner)


def output_kernel(layers, flow_ref, table_ref, local_ref, bias_ref, *refs):
    own_refs, core_refs = refs[:layers], refs[layers : 2 * layers]
    out_hbm, order_ref, wide_ref, level_ref, done_ref, sent = refs[2 * layers :]
    cells_x, _, feat_count = flow_ref.shape
    channels = local_ref.shape[0]
    z, x, y = quad()
    wide_ref[...] = jnp.zeros_like(wide_ref)
    for start in range(0, WIDTH, channels):
        span = slice(start, start + channels)
        wide_ref[span, span] = local_ref[...]
        level_ref[:, span] = bias_ref[...].reshape(1, channels)
    level = level_ref[...]
    levels = []
    for _ in range(BIAS_TERMS):
        levels.append(level.astype(jnp.bfloat16).astype(jnp.float32))
        level = level - levels[-1]
    terms = 3 * order_ref.shape[1] * order_ref.shape[2]
    filled = jnp.zeros((table_ref.shape[-1] - terms - BIAS_TERMS, WIDTH), jnp.float32)
    below = jnp.concatenate(levels + [filled], axis=0).astype(jnp.bfloat16)
    below = jnp.concatenate([below, wide_ref[...]], axis=0)
    for column, block_refs in ((x ^ y, own_refs), (x ^ y ^ 1, core_refs)):
        for turn, block_ref in zip(turns(layers), block_refs):
            order_ref[:, (z ^ turn) * 2 + column] = block_ref[...]
    table = table_ref[y, x ^ y]
    copies = []
    for cell in range(cells_x):
        high, low = split_terms(order_ref[cell].reshape(-1, feat_count))
        stack = jnp.concatenate([high, low, high], axis=0)
        for start in range(0, feat_count, WIDTH):
            columns = slice(start, start + WIDTH)
            total = dot(
                jnp.concatenate([table, flow_ref[cell, :, columns]], axis=1),
                jnp.concatenate([stack[:, columns], below], axis=0),
            )
            done_ref[cell, :, columns] = gelu(total).astype(done_ref.dtype)
        copies.append(pltpu.make_async_copy(done_ref.at[cell], out_hbm.at[cell], sent.at[cell]))
        copies[-1].start()
    for copy in copies:
        copy.wait()


def make_output(flow_field, parts, table, local, bias):
    cells_x, _, feat_count = flow_field.shape
    layers = len(parts) // 2
    return pl.pallas_call(
        functools.partial(output_kernel, layers),
        out_specs=pl.BlockSpec(memory_space=pl.ANY),
        scratch_shapes=[
            pltpu.VMEM((cells_x, 2 * layers) + parts[0].shape[1:], jnp.float32),
            pltpu.VMEM((WIDTH, WIDTH), jnp.bfloat16),
            pltpu.VMEM((1, WIDTH), jnp.float32),
            pltpu.VMEM(flow_field.shape, jnp.bfloat16),
            pltpu.SemaphoreType.DMA((cells_x,)),
        ],
        out_shape=jax.ShapeDtypeStruct(flow_field.shape, jnp.bfloat16),
        compiler_params=SMALL,
        name="make_output",
    )(flow_field, table, local, bias, *parts)


def row_body(flow_field, spectral_weight, local_weight, bias_terms):
    cells_x, cells_y, feat_count = flow_field.shape
    peers = lax.axis_size("gx")
    groups_y = lax.axis_size("gy")
    rows_ky = MY // groups_y // peers
    forward_scale = 1.0 / math.sqrt(cells_x * peers * cells_y * groups_y)
    inverse_scale = 1.0 / math.sqrt(MX * MY)

    send, keep = forward_y(flow_field, cells_y * groups_y, peers // 2, rows_ky)
    blocks = along_columns(add_blocks(keep, flip_core(send)), peers)
    inverse_tables = split_table(inverse_x_table(cells_x, peers, rows_ky))
    modes, send = mix(
        blocks,
        [flip_core(second_half(block)) for block in blocks],
        spectral_weight,
        forward_x_table(cells_x, peers, rows_ky) * forward_scale,
        inverse_tables,
    )
    arrived = flip_core(send)
    mixed, keep = keep_rows(modes, inverse_tables, send)
    own = along_columns(join_blocks(keep, arrived, cells_x), peers)
    parts = own + [flip_core(block) for block in own]
    table = output_table(inverse_y_table(cells_y, groups_y, peers, rows_ky) * inverse_scale)
    return make_output(flow_field, parts, table, local_weight, bias_terms), mixed


def body(flow_field, spectral_weight, local_weight, bias_terms):
    peers = lax.axis_size("gx")
    extent = lax.axis_size("gy") * flow_field.shape[1]
    paired = lax.axis_size("gy") == 2 and peers & (peers - 1) == 0 and extent & (extent - 1) == 0
    if paired and spectral_weight.shape[1] == 2 * MX and WIDTH % local_weight.shape[0] == 0:
        return row_body(flow_field, spectral_weight, local_weight, bias_terms)
    return general_body(flow_field, spectral_weight, local_weight, bias_terms)


def solution(mesh):
    placed = (P(("group", "gx"), "gy", None), P("gy", "gx", None, None), P(), P())
    return jax.shard_map(
        body,
        mesh=mesh,
        in_specs=placed,
        out_specs=(P(("group", "gx"), "gy", None), P(("group", "gy"), "gx", None)),
        check_vma=False,
    )
```

```python
import functools
import math

import jax
import jax.numpy as jnp
import ml_dtypes
import numpy as np
from jax import lax
from jax.experimental import pallas as pl
from jax.experimental.pallas import tpu as pltpu
from jax.sharding import PartitionSpec as P

MX = 32
MY = 32


def wave_number(index, count):
    return jnp.where(index < count // 2, index, index - count)


def phase_table(waves, places, extent):
    product = waves[:, None] * places[None, :] % extent
    return 2.0 * math.pi / extent * product.astype(jnp.float32)


def row_tables(ky_rows, kx_rows, x_places, extent, width):
    angle = phase_table(wave_number(kx_rows, MX), x_places, extent)
    select = (ky_rows[:, None] == jnp.arange(width, dtype=jnp.int32)[None, :]).astype(jnp.float32)
    cosine = jnp.cos(angle)[:, :, None] * select[:, None, :]
    sine_part = jnp.sin(angle)[:, :, None] * select[:, None, :]
    return (cosine, sine_part)


def forward_rows(y_local, ky_rows, kx_rows, x_places, extent):
    cosine, sine_part = row_tables(ky_rows, kx_rows, x_places, extent, y_local.shape[0])
    real_in = y_local[:, 0]
    imag_in = y_local[:, 1]

    def contract(table, values):
        return jnp.einsum("rxk,kxf->rf", table, values, precision=lax.Precision.HIGHEST)

    real_out = contract(cosine, real_in) + contract(sine_part, imag_in)
    imag_out = contract(cosine, imag_in) - contract(sine_part, real_in)
    return jnp.concatenate([real_out, imag_out], axis=1)


def inverse_rows(running, shard_rows, ky_rows, kx_rows, x_places, extent):
    cosine, sine_part = row_tables(ky_rows, kx_rows, x_places, extent, running.shape[0])
    feat_count = shard_rows.shape[1] // 2
    real_part = shard_rows[:, :feat_count]
    imag_part = shard_rows[:, feat_count:]

    def contract(table, values):
        return jnp.einsum("rxk,rf->kxf", table, values, precision=lax.Precision.HIGHEST)

    new_real = contract(cosine, real_part) - contract(sine_part, imag_part)
    new_imag = contract(cosine, imag_part) + contract(sine_part, real_part)
    return jnp.stack([new_real, new_imag], axis=1)


def general_body(flow_field, spectral_weight, local_weight, bias_terms):
    cells_x, cells_y, feat_count = flow_field.shape
    channels = local_weight.shape[0]
    planes = feat_count // channels
    groups_x = lax.axis_size("gx")
    groups_y = lax.axis_size("gy")
    extent_x = cells_x * groups_x
    extent_y = cells_y * groups_y
    half_width = MY // groups_y
    quota_rows = spectral_weight.shape[1]
    high = lax.Precision.HIGHEST
    x_places = lax.axis_index("gx") * cells_x + jnp.arange(cells_x, dtype=jnp.int32)
    y_places = lax.axis_index("gy") * cells_y + jnp.arange(cells_y, dtype=jnp.int32)
    y_angle = phase_table(wave_number(jnp.arange(MY, dtype=jnp.int32), MY), y_places, extent_y)
    y_table = (
        jnp.stack([jnp.cos(y_angle), -jnp.sin(y_angle)], axis=1)
        .reshape(2 * MY, cells_y)
        .astype(jnp.bfloat16)
    )
    y_local = lax.psum_scatter(
        jnp.einsum("qy,xyf->qxf", y_table, flow_field, preferred_element_type=jnp.float32),
        "gy",
        scatter_dimension=0,
        tiled=True,
    )
    y_local = y_local.reshape(half_width, 2, cells_x, feat_count)
    rest_index = jnp.arange(lax.axis_size("gx") * quota_rows, dtype=jnp.int32)
    spectrum = lax.psum_scatter(
        forward_rows(y_local, rest_index // MX, rest_index % MX, x_places, extent_x),
        "gx",
        scatter_dimension=0,
        tiled=True,
    )
    spectrum = spectrum * (1.0 / math.sqrt(extent_x * extent_y))
    coeffs = spectrum.reshape(quota_rows, 2, planes, channels)
    weights = spectral_weight[0].astype(jnp.float32)
    product = jnp.einsum("rpzc,rco->rpzo", coeffs, weights, precision=high)
    mixed_real = product[:, 0, :, :channels] - product[:, 1, :, channels:]
    mixed_imag = product[:, 0, :, channels:] + product[:, 1, :, :channels]
    mixed_local = jnp.stack([mixed_real, mixed_imag], axis=1).reshape(quota_rows, 2 * feat_count)
    pointwise = jnp.einsum(
        "xyzc,co->xyzo",
        flow_field.reshape(cells_x, cells_y, planes, channels),
        local_weight,
        preferred_element_type=jnp.float32,
    )
    start_half = jnp.zeros((half_width, 2, cells_x, feat_count), jnp.float32)
    shard_rows = lax.all_gather(mixed_local, "gx", axis=0, tiled=True)
    rest_index = jnp.arange(shard_rows.shape[0], dtype=jnp.int32)
    back_half = inverse_rows(
        start_half, shard_rows, rest_index // MX, rest_index % MX, x_places, extent_x
    )
    back_whole = lax.all_gather(back_half, "gy", axis=0, tiled=True)
    y_cos = jnp.cos(y_angle)
    y_sin = jnp.sin(y_angle)
    spectral = (
        jnp.einsum("kn,kxf->xnf", y_cos, back_whole[:, 0], precision=high)
        - jnp.einsum("kn,kxf->xnf", y_sin, back_whole[:, 1], precision=high)
    ) * (1.0 / math.sqrt(MX * MY))
    total = spectral.reshape(cells_x, cells_y, planes, channels) + pointwise + bias_terms
    output = (
        jax.nn.gelu(total, approximate=False)
        .reshape(cells_x, cells_y, feat_count)
        .astype(jnp.bfloat16)
    )
    return (output, mixed_local.reshape(1, quota_rows, 2 * feat_count))


SMALL = pltpu.CompilerParams(vmem_limit_bytes=20 * 1024 * 1024)
LARGE = pltpu.CompilerParams(vmem_limit_bytes=53 * 1024 * 1024)
WIDTH = 256
BIAS_TERMS = 3
SLAB = 32
GELU_TERMS = (
    0.7978849411010742,
    0.03633308410644531,
    -3.259492223151028e-05,
    -5.530622001970187e-05,
    3.964749794249656e-06,
    -1.3226382122866198e-07,
    1.7561855303327434e-09,
)


def angles(count, places, extent):
    index = np.arange(count)
    waves = np.where(index < count // 2, index, index - count)
    product = (waves[:, None] * np.asarray(places)[None, :]) % extent
    return (np.float32(2.0 * math.pi / extent) * product.astype(np.float32)).astype(np.float64)


def split_table(table):
    high = table.astype(ml_dtypes.bfloat16)
    low = (table - high.astype(np.float64)).astype(ml_dtypes.bfloat16)
    return high, low


def split_terms(values):
    high = values.astype(jnp.bfloat16)
    low = (values - high.astype(jnp.float32)).astype(jnp.bfloat16)
    return high, low


def quad():
    place = lax.axis_index("gx")
    return place // 2, place % 2, lax.axis_index("gy")


def turns(layers):
    half = layers // 2
    return list(range(half, layers)) + list(range(half - 1, -1, -1))


def forward_x_table(cells_x, peers, rows_ky):
    extent = cells_x * peers
    angle = angles(MX, np.arange(extent), extent)
    cosine, sine = np.cos(angle), np.sin(angle)
    out = np.zeros((2, rows_ky, MX, extent, rows_ky, 2))
    for row in range(rows_ky):
        out[0, row, :, :, row, 0] = cosine
        out[0, row, :, :, row, 1] = sine
        out[1, row, :, :, row, 1] = cosine
        out[1, row, :, :, row, 0] = -sine
    return out.reshape(2 * rows_ky * MX, extent * rows_ky * 2)


def inverse_x_table(cells_x, peers, rows_ky):
    extent = cells_x * peers
    angle = angles(MX, np.arange(extent), extent)
    cosine, sine = np.cos(angle).T, np.sin(angle).T
    out = np.zeros((extent, rows_ky, 2, 2, rows_ky, MX))
    for row in range(rows_ky):
        out[:, row, 0, 0, row, :] = cosine
        out[:, row, 0, 1, row, :] = -sine
        out[:, row, 1, 1, row, :] = cosine
        out[:, row, 1, 0, row, :] = sine
    out = out.reshape(peers // 2, 2, cells_x * rows_ky * 2, 2 * rows_ky * MX)
    return np.moveaxis(out, 1, 0).reshape(2, -1, 2 * rows_ky * MX)


def inverse_y_table(cells_y, groups_y, peers, rows_ky):
    extent = cells_y * groups_y
    angle = angles(MY, np.arange(extent), extent)
    full = np.stack([np.cos(angle), -np.sin(angle)], axis=1)
    full = full.reshape(groups_y, peers, rows_ky, 2, groups_y, cells_y)
    out = np.zeros((groups_y, 2, cells_y, peers, 2, rows_ky, 2))
    for y in range(groups_y):
        for column in range(2):
            for peer in range(peers):
                for place in range(2):
                    half = y ^ place ^ column ^ (peer % 2)
                    out[y, column, :, peer, place] = np.moveaxis(full[half, peer, :, :, y], -1, 0)
    return out.reshape(groups_y, 2, cells_y, 4 * peers * rows_ky)


def output_table(table):
    high, low = split_table(table)
    parts = [high, high, low, np.ones(table.shape[:-1] + (BIAS_TERMS,), high.dtype)]
    used = 3 * table.shape[-1] + BIAS_TERMS
    parts.append(np.zeros(table.shape[:-1] + (-used % 256,), high.dtype))
    return np.concatenate(parts, axis=-1)


def dot(left, right):
    return jnp.dot(left, right, preferred_element_type=jnp.float32)


def forward_y_table(shape, extent, layers, rows_ky):
    z, x, y = quad()
    peers = 2 * layers
    row = lax.broadcasted_iota(jnp.int32, (shape[0], 1), 0)
    block = row // (2 * rows_ky)
    place = block // 2 % layers
    turn = jnp.where(place < layers // 2, place + layers // 2, layers - 1 - place)
    side = y ^ (1 - block // peers)
    owner = (side ^ (block % 2)) * peers + (z ^ turn) * 2 + (x ^ side)
    index = owner * rows_ky + row // 2 % rows_ky
    y_places = lax.broadcasted_iota(jnp.int32, (1, shape[1]), 1) + y * shape[1]
    steps = (wave_number(index, MY) * y_places) & (extent - 1)
    angle = 2.0 * math.pi / extent * steps.astype(jnp.float32)
    return jnp.where(row % 2 == 0, jnp.cos(angle), -jnp.sin(angle)).astype(jnp.bfloat16)


def forward_y_kernel(extent, rows_ky, flow_hbm, send_ref, keep_ref, flow_ref, arrived):
    layers, _, rows, feat_count = send_ref.shape
    cells_x, cells_y, _ = flow_ref.shape
    rows = rows // cells_x
    copies = [
        pltpu.make_async_copy(flow_hbm.at[x], flow_ref.at[x], arrived.at[x])
        for x in range(cells_x)
    ]
    for copy in copies:
        copy.start()
    table = forward_y_table((2 * MY, cells_y), extent, layers, rows_ky)
    for x in range(cells_x):
        copies[x].wait()
        result = dot(table, flow_ref[x]).reshape(2, layers, 2, rows, feat_count)
        send_ref[:, :, x * rows : (x + 1) * rows, :] = result[0]
        keep_ref[:, :, x * rows : (x + 1) * rows, :] = result[1]


def forward_y(flow_field, extent, layers, rows_ky):
    cells_x, _, feat_count = flow_field.shape
    shape = jax.ShapeDtypeStruct((layers, 2, cells_x * 2 * rows_ky, feat_count), jnp.float32)
    return pl.pallas_call(
        functools.partial(forward_y_kernel, extent, rows_ky),
        in_specs=[pl.BlockSpec(memory_space=pltpu.HBM)],
        out_shape=[shape] * 2,
        scratch_shapes=[
            pltpu.VMEM(flow_field.shape, flow_field.dtype),
            pltpu.SemaphoreType.DMA((cells_x,)),
        ],
        compiler_params=LARGE,
        name="forward_y",
    )(flow_field)


def flip_core(block):
    return lax.ppermute(block, "gy", [(0, 1), (1, 0)])


def along_columns(blocks, peers):
    arrived = []
    for turn, block in zip(turns(len(blocks)), blocks):
        pairs = [
            (2 * place + core, 2 * (place ^ (2 * turn + core)) + core)
            for place in range(peers)
            for core in range(2)
        ]
        arrived.append(lax.ppermute(block, ("gx", "gy"), pairs))
    return arrived


def small_call(kernel, out_shape, name):
    return pl.pallas_call(kernel, out_shape=out_shape, compiler_params=SMALL, name=name)


def second_kernel(block_ref, out_ref):
    out_ref[...] = block_ref[1]


def second_half(block):
    shape = jax.ShapeDtypeStruct(block.shape[1:], block.dtype)
    return small_call(second_kernel, shape, "second_half")(block)


def add_kernel(keep_ref, arrived_ref, *out_refs):
    for turn, out_ref in enumerate(out_refs):
        out_ref[...] = keep_ref[turn] + arrived_ref[turn]


def add_blocks(keep, arrived):
    shape = jax.ShapeDtypeStruct(keep.shape[1:], keep.dtype)
    return small_call(add_kernel, [shape] * keep.shape[0], "add_blocks")(keep, arrived)


def join_kernel(keep_ref, arrived_ref, *out_refs):
    cells_x, rows, _ = out_refs[0].shape
    rows = rows // 2
    for turn, out_ref in enumerate(out_refs):
        for cell in range(cells_x):
            span = slice(cell * rows, (cell + 1) * rows)
            out_ref[cell] = jnp.concatenate(
                [keep_ref[turn, span, :], arrived_ref[turn, span, :]], axis=0
            )


def join_blocks(keep, arrived, cells_x):
    layers, rows, feat_count = keep.shape
    shape = jax.ShapeDtypeStruct((cells_x, 2 * rows // cells_x, feat_count), keep.dtype)
    return small_call(join_kernel, [shape] * layers, "join_blocks")(keep, arrived)


def back_rows(inverse_high, inverse_low, column, modes):
    high, low = split_terms(modes)
    table = inverse_high[column]
    return dot(table, high) + dot(table, low) + dot(inverse_low[column], high)


def store_turns(out_ref, order_ref, z):
    for index, turn in enumerate(turns(out_ref.shape[0])):
        out_ref[index] = order_ref[z ^ turn]


def mix_kernel(layers, *refs):
    block_refs, arrived_refs = refs[:layers], refs[layers : 2 * layers]
    weight_ref, forward_high, forward_low, inverse_high, inverse_low = refs[
        2 * layers : 2 * layers + 5
    ]
    modes_ref, send_ref, order_ref, spread_ref, result_ref = refs[2 * layers + 5 :]
    z, x, y = quad()
    column = x ^ y
    for index, turn in enumerate(turns(layers)):
        order_ref[(z ^ turn) * 2 + column] = block_refs[index][0]
        order_ref[(z ^ turn) * 2 + (column ^ 1)] = arrived_refs[index][...]
    feat_count = order_ref.shape[-1]
    count = weight_ref.shape[1]
    channels = weight_ref.shape[2]
    tiles = feat_count // 128
    group = 2 * tiles
    high, low = split_terms(order_ref[...].reshape(-1, feat_count))
    spectrum = (
        dot(forward_high[...], high) + dot(forward_high[...], low) + dot(forward_low[...], high)
    )
    for part in range(2):
        for tile in range(tiles):
            spread_ref[pl.ds(part * tiles + tile, count, stride=group), :] = spectrum[
                part * count : (part + 1) * count, tile * 128 : (tile + 1) * 128
            ]
    rows = lax.broadcasted_iota(jnp.int32, (8, 128), 0) % group
    lane = lax.broadcasted_iota(jnp.int32, (8, 128), 1) < channels
    sign = jnp.where(rows < tiles, -1.0, 1.0)
    for base in range(0, count * group, 8):
        block = spread_ref[base : base + 8, :]
        turned = pltpu.roll(block, channels, 1)
        firsts, seconds = [], []
        for start in range(0, 8, group):
            span = slice(start, start + group)
            left = jnp.concatenate([block[span], turned[span]], axis=0)[:, :channels]
            left_high, left_low = split_terms(left)
            left = jnp.concatenate([left_high, left_low], axis=0)
            product = dot(left, weight_ref[0, (base + start) // group])
            product = product[: 2 * group] + product[2 * group :]
            firsts.append(product[:group])
            seconds.append(product[group:])
        first = jnp.concatenate(firsts, axis=0)
        second = jnp.concatenate(seconds, axis=0)
        real = jnp.where(lane, first, pltpu.roll(second, channels, 1))
        imag = jnp.where(lane, pltpu.roll(first, channels, 1), second)
        crossed = jnp.where(rows < tiles, pltpu.roll(imag, 8 - tiles, 0), pltpu.roll(imag, tiles, 0))
        result_ref[base : base + 8, :] = real + sign * crossed
    for part in range(2):
        for tile in range(tiles):
            modes_ref[part * count : (part + 1) * count, tile * 128 : (tile + 1) * 128] = (
                result_ref[pl.ds(part * tiles + tile, count, stride=group), :]
            )
    back = back_rows(inverse_high, inverse_low, column ^ 1, modes_ref[...])
    order_ref[:layers] = back.reshape(send_ref.shape)
    store_turns(send_ref, order_ref, z)


def mix(blocks, arrived, weights, forward_table, inverse_tables):
    layers = len(blocks)
    _, rows, feat_count = blocks[0].shape
    count = weights.shape[1]
    scratch = pltpu.VMEM((count * feat_count // 64, 128), jnp.float32)
    return pl.pallas_call(
        functools.partial(mix_kernel, layers),
        out_shape=[
            jax.ShapeDtypeStruct((2 * count, feat_count), jnp.float32),
            jax.ShapeDtypeStruct((layers, rows, feat_count), jnp.float32),
        ],
        scratch_shapes=[pltpu.VMEM((2 * layers, rows, feat_count), jnp.float32), scratch, scratch],
        compiler_params=SMALL,
        name="mix",
    )(*blocks, *arrived, weights, *split_table(forward_table), *inverse_tables)


def keep_kernel(modes_ref, inverse_high, inverse_low, mixed_ref, keep_ref, order_ref):
    z, x, y = quad()
    count = mixed_ref.shape[1]
    feat_count = modes_ref.shape[1]
    for part in range(2):
        mixed_ref[0, :, part * feat_count : (part + 1) * feat_count] = modes_ref[
            part * count : (part + 1) * count
        ]
    back = back_rows(inverse_high, inverse_low, x ^ y, modes_ref[...])
    order_ref[...] = back.reshape(keep_ref.shape)
    store_turns(keep_ref, order_ref, z)


def keep_rows(modes, inverse_tables, like):
    rows, feat_count = modes.shape
    return pl.pallas_call(
        keep_kernel,
        out_shape=[
            jax.ShapeDtypeStruct((1, rows // 2, 2 * feat_count), jnp.float32),
            jax.ShapeDtypeStruct(like.shape, jnp.float32),
        ],
        scratch_shapes=[pltpu.VMEM(like.shape, jnp.float32)],
        compiler_params=SMALL,
        name="keep_rows",
    )(modes, *inverse_tables)


def gelu(values):
    square = jnp.minimum(values * values, 31.36)
    inner = jnp.full_like(square, GELU_TERMS[-1])
    for term in GELU_TERMS[-2::-1]:
        inner = inner * square + term
    half = 0.5 * values
    return half + half * jnp.tanh(values * inner)


def output_kernel(layers, flow_ref, table_ref, local_ref, bias_ref, *refs):
    own_refs, core_refs = refs[:layers], refs[layers : 2 * layers]
    out_hbm, order_ref, wide_ref, level_ref, total_ref, done_ref, sent = refs[2 * layers :]
    cells_x, cells_y, feat_count = flow_ref.shape
    channels = local_ref.shape[0]
    z, x, y = quad()
    wide_ref[...] = jnp.zeros_like(wide_ref)
    for start in range(0, WIDTH, channels):
        span = slice(start, start + channels)
        wide_ref[span, span] = local_ref[...]
        level_ref[:, span] = bias_ref[...].reshape(1, channels)
    level = level_ref[...]
    levels = []
    for _ in range(BIAS_TERMS):
        levels.append(level.astype(jnp.bfloat16).astype(jnp.float32))
        level = level - levels[-1]
    terms = 3 * order_ref.shape[1] * order_ref.shape[2]
    filled = jnp.zeros((table_ref.shape[-1] - terms - BIAS_TERMS, WIDTH), jnp.float32)
    below = jnp.concatenate(levels + [filled], axis=0).astype(jnp.bfloat16)
    below = jnp.concatenate([below, wide_ref[...]], axis=0)
    for column, block_refs in ((x ^ y, own_refs), (x ^ y ^ 1, core_refs)):
        for turn, block_ref in zip(turns(layers), block_refs):
            order_ref[:, (z ^ turn) * 2 + column] = block_ref[...]
    table = table_ref[y, x ^ y]
    copies = []
    for cell in range(cells_x):
        high, low = split_terms(order_ref[cell].reshape(-1, feat_count))
        stack = jnp.concatenate([high, low, high], axis=0)
        for start in range(0, feat_count, WIDTH):
            columns = slice(start, start + WIDTH)
            total_ref[:, columns] = dot(
                jnp.concatenate([table, flow_ref[cell, :, columns]], axis=1),
                jnp.concatenate([stack[:, columns], below], axis=0),
            )
            for row in range(0, cells_y, SLAB):
                slab = slice(row, row + SLAB)
                done_ref[cell, slab, columns] = gelu(total_ref[slab, columns]).astype(done_ref.dtype)
        copies.append(pltpu.make_async_copy(done_ref.at[cell], out_hbm.at[cell], sent.at[cell]))
        copies[-1].start()
    for copy in copies:
        copy.wait()


def make_output(flow_field, parts, table, local, bias):
    cells_x, _, feat_count = flow_field.shape
    layers = len(parts) // 2
    return pl.pallas_call(
        functools.partial(output_kernel, layers),
        out_specs=pl.BlockSpec(memory_space=pl.ANY),
        scratch_shapes=[
            pltpu.VMEM((cells_x, 2 * layers) + parts[0].shape[1:], jnp.float32),
            pltpu.VMEM((WIDTH, WIDTH), jnp.bfloat16),
            pltpu.VMEM((1, WIDTH), jnp.float32),
            pltpu.VMEM(flow_field.shape[1:], jnp.float32),
            pltpu.VMEM(flow_field.shape, jnp.bfloat16),
            pltpu.SemaphoreType.DMA((cells_x,)),
        ],
        out_shape=jax.ShapeDtypeStruct(flow_field.shape, jnp.bfloat16),
        compiler_params=SMALL,
        name="make_output",
    )(flow_field, table, local, bias, *parts)


def row_body(flow_field, spectral_weight, local_weight, bias_terms):
    cells_x, cells_y, feat_count = flow_field.shape
    peers = lax.axis_size("gx")
    groups_y = lax.axis_size("gy")
    rows_ky = MY // groups_y // peers
    forward_scale = 1.0 / math.sqrt(cells_x * peers * cells_y * groups_y)
    inverse_scale = 1.0 / math.sqrt(MX * MY)

    send, keep = forward_y(flow_field, cells_y * groups_y, peers // 2, rows_ky)
    blocks = along_columns(add_blocks(keep, flip_core(send)), peers)
    inverse_tables = split_table(inverse_x_table(cells_x, peers, rows_ky))
    modes, send = mix(
        blocks,
        [flip_core(second_half(block)) for block in blocks],
        spectral_weight,
        forward_x_table(cells_x, peers, rows_ky) * forward_scale,
        inverse_tables,
    )
    arrived = flip_core(send)
    mixed, keep = keep_rows(modes, inverse_tables, send)
    own = along_columns(join_blocks(keep, arrived, cells_x), peers)
    parts = own + [flip_core(block) for block in own]
    table = output_table(inverse_y_table(cells_y, groups_y, peers, rows_ky) * inverse_scale)
    return make_output(flow_field, parts, table, local_weight, bias_terms), mixed


def body(flow_field, spectral_weight, local_weight, bias_terms):
    peers = lax.axis_size("gx")
    extent = lax.axis_size("gy") * flow_field.shape[1]
    paired = lax.axis_size("gy") == 2 and peers & (peers - 1) == 0 and extent & (extent - 1) == 0
    if paired and spectral_weight.shape[1] == 2 * MX and WIDTH % local_weight.shape[0] == 0:
        return row_body(flow_field, spectral_weight, local_weight, bias_terms)
    return general_body(flow_field, spectral_weight, local_weight, bias_terms)


def solution(mesh):
    placed = (P(("group", "gx"), "gy", None), P("gy", "gx", None, None), P(), P())
    return jax.shard_map(
        body,
        mesh=mesh,
        in_specs=placed,
        out_specs=(P(("group", "gx"), "gy", None), P(("group", "gy"), "gx", None)),
        check_vma=False,
    )
```

```python
import functools
import math

import jax
import jax.numpy as jnp
import ml_dtypes
import numpy as np
from jax import lax
from jax.experimental import pallas as pl
from jax.experimental.pallas import tpu as pltpu
from jax.sharding import PartitionSpec as P

MX = 32
MY = 32


def wave_number(index, count):
    return jnp.where(index < count // 2, index, index - count)


def phase_table(waves, places, extent):
    product = waves[:, None] * places[None, :] % extent
    return 2.0 * math.pi / extent * product.astype(jnp.float32)


def row_tables(ky_rows, kx_rows, x_places, extent, width):
    angle = phase_table(wave_number(kx_rows, MX), x_places, extent)
    select = (ky_rows[:, None] == jnp.arange(width, dtype=jnp.int32)[None, :]).astype(jnp.float32)
    cosine = jnp.cos(angle)[:, :, None] * select[:, None, :]
    sine_part = jnp.sin(angle)[:, :, None] * select[:, None, :]
    return (cosine, sine_part)


def forward_rows(y_local, ky_rows, kx_rows, x_places, extent):
    cosine, sine_part = row_tables(ky_rows, kx_rows, x_places, extent, y_local.shape[0])
    real_in = y_local[:, 0]
    imag_in = y_local[:, 1]

    def contract(table, values):
        return jnp.einsum("rxk,kxf->rf", table, values, precision=lax.Precision.HIGHEST)

    real_out = contract(cosine, real_in) + contract(sine_part, imag_in)
    imag_out = contract(cosine, imag_in) - contract(sine_part, real_in)
    return jnp.concatenate([real_out, imag_out], axis=1)


def inverse_rows(running, shard_rows, ky_rows, kx_rows, x_places, extent):
    cosine, sine_part = row_tables(ky_rows, kx_rows, x_places, extent, running.shape[0])
    feat_count = shard_rows.shape[1] // 2
    real_part = shard_rows[:, :feat_count]
    imag_part = shard_rows[:, feat_count:]

    def contract(table, values):
        return jnp.einsum("rxk,rf->kxf", table, values, precision=lax.Precision.HIGHEST)

    new_real = contract(cosine, real_part) - contract(sine_part, imag_part)
    new_imag = contract(cosine, imag_part) + contract(sine_part, real_part)
    return jnp.stack([new_real, new_imag], axis=1)


def general_body(flow_field, spectral_weight, local_weight, bias_terms):
    cells_x, cells_y, feat_count = flow_field.shape
    channels = local_weight.shape[0]
    planes = feat_count // channels
    groups_x = lax.axis_size("gx")
    groups_y = lax.axis_size("gy")
    extent_x = cells_x * groups_x
    extent_y = cells_y * groups_y
    half_width = MY // groups_y
    quota_rows = spectral_weight.shape[1]
    high = lax.Precision.HIGHEST
    x_places = lax.axis_index("gx") * cells_x + jnp.arange(cells_x, dtype=jnp.int32)
    y_places = lax.axis_index("gy") * cells_y + jnp.arange(cells_y, dtype=jnp.int32)
    y_angle = phase_table(wave_number(jnp.arange(MY, dtype=jnp.int32), MY), y_places, extent_y)
    y_table = (
        jnp.stack([jnp.cos(y_angle), -jnp.sin(y_angle)], axis=1)
        .reshape(2 * MY, cells_y)
        .astype(jnp.bfloat16)
    )
    y_local = lax.psum_scatter(
        jnp.einsum("qy,xyf->qxf", y_table, flow_field, preferred_element_type=jnp.float32),
        "gy",
        scatter_dimension=0,
        tiled=True,
    )
    y_local = y_local.reshape(half_width, 2, cells_x, feat_count)
    rest_index = jnp.arange(lax.axis_size("gx") * quota_rows, dtype=jnp.int32)
    spectrum = lax.psum_scatter(
        forward_rows(y_local, rest_index // MX, rest_index % MX, x_places, extent_x),
        "gx",
        scatter_dimension=0,
        tiled=True,
    )
    spectrum = spectrum * (1.0 / math.sqrt(extent_x * extent_y))
    coeffs = spectrum.reshape(quota_rows, 2, planes, channels)
    weights = spectral_weight[0].astype(jnp.float32)
    product = jnp.einsum("rpzc,rco->rpzo", coeffs, weights, precision=high)
    mixed_real = product[:, 0, :, :channels] - product[:, 1, :, channels:]
    mixed_imag = product[:, 0, :, channels:] + product[:, 1, :, :channels]
    mixed_local = jnp.stack([mixed_real, mixed_imag], axis=1).reshape(quota_rows, 2 * feat_count)
    pointwise = jnp.einsum(
        "xyzc,co->xyzo",
        flow_field.reshape(cells_x, cells_y, planes, channels),
        local_weight,
        preferred_element_type=jnp.float32,
    )
    start_half = jnp.zeros((half_width, 2, cells_x, feat_count), jnp.float32)
    shard_rows = lax.all_gather(mixed_local, "gx", axis=0, tiled=True)
    rest_index = jnp.arange(shard_rows.shape[0], dtype=jnp.int32)
    back_half = inverse_rows(
        start_half, shard_rows, rest_index // MX, rest_index % MX, x_places, extent_x
    )
    back_whole = lax.all_gather(back_half, "gy", axis=0, tiled=True)
    y_cos = jnp.cos(y_angle)
    y_sin = jnp.sin(y_angle)
    spectral = (
        jnp.einsum("kn,kxf->xnf", y_cos, back_whole[:, 0], precision=high)
        - jnp.einsum("kn,kxf->xnf", y_sin, back_whole[:, 1], precision=high)
    ) * (1.0 / math.sqrt(MX * MY))
    total = spectral.reshape(cells_x, cells_y, planes, channels) + pointwise + bias_terms
    output = (
        jax.nn.gelu(total, approximate=False)
        .reshape(cells_x, cells_y, feat_count)
        .astype(jnp.bfloat16)
    )
    return (output, mixed_local.reshape(1, quota_rows, 2 * feat_count))


SMALL = pltpu.CompilerParams(vmem_limit_bytes=20 * 1024 * 1024)
LARGE = pltpu.CompilerParams(vmem_limit_bytes=53 * 1024 * 1024)
WIDTH = 256
BIAS_TERMS = 3
FIRST = 64
GELU_TERMS = (
    0.7978849411010742,
    0.03633308410644531,
    -3.259492223151028e-05,
    -5.530622001970187e-05,
    3.964749794249656e-06,
    -1.3226382122866198e-07,
    1.7561855303327434e-09,
)


def angles(count, places, extent):
    index = np.arange(count)
    waves = np.where(index < count // 2, index, index - count)
    product = (waves[:, None] * np.asarray(places)[None, :]) % extent
    return (np.float32(2.0 * math.pi / extent) * product.astype(np.float32)).astype(np.float64)


def split_table(table):
    high = table.astype(ml_dtypes.bfloat16)
    low = (table - high.astype(np.float64)).astype(ml_dtypes.bfloat16)
    return high, low


def split_terms(values):
    high = values.astype(jnp.bfloat16)
    low = (values - high.astype(jnp.float32)).astype(jnp.bfloat16)
    return high, low


def quad():
    place = lax.axis_index("gx")
    return place // 2, place % 2, lax.axis_index("gy")


def turns(layers):
    half = layers // 2
    return list(range(half, layers)) + list(range(half - 1, -1, -1))


def forward_x_table(cells_x, peers, rows_ky):
    extent = cells_x * peers
    angle = angles(MX, np.arange(extent), extent)
    cosine, sine = np.cos(angle), np.sin(angle)
    out = np.zeros((2, rows_ky, MX, extent, rows_ky, 2))
    for row in range(rows_ky):
        out[0, row, :, :, row, 0] = cosine
        out[0, row, :, :, row, 1] = sine
        out[1, row, :, :, row, 1] = cosine
        out[1, row, :, :, row, 0] = -sine
    return out.reshape(2 * rows_ky * MX, extent * rows_ky * 2)


def inverse_x_table(cells_x, peers, rows_ky):
    extent = cells_x * peers
    angle = angles(MX, np.arange(extent), extent)
    cosine, sine = np.cos(angle).T, np.sin(angle).T
    out = np.zeros((extent, rows_ky, 2, 2, rows_ky, MX))
    for row in range(rows_ky):
        out[:, row, 0, 0, row, :] = cosine
        out[:, row, 0, 1, row, :] = -sine
        out[:, row, 1, 1, row, :] = cosine
        out[:, row, 1, 0, row, :] = sine
    out = out.reshape(peers // 2, 2, cells_x * rows_ky * 2, 2 * rows_ky * MX)
    return np.moveaxis(out, 1, 0).reshape(2, -1, 2 * rows_ky * MX)


def inverse_y_table(cells_y, groups_y, peers, rows_ky):
    extent = cells_y * groups_y
    angle = angles(MY, np.arange(extent), extent)
    full = np.stack([np.cos(angle), -np.sin(angle)], axis=1)
    full = full.reshape(groups_y, peers, rows_ky, 2, groups_y, cells_y)
    out = np.zeros((groups_y, 2, cells_y, peers, 2, rows_ky, 2))
    for y in range(groups_y):
        for column in range(2):
            for peer in range(peers):
                for place in range(2):
                    half = y ^ place ^ column ^ (peer % 2)
                    out[y, column, :, peer, place] = np.moveaxis(full[half, peer, :, :, y], -1, 0)
    return out.reshape(groups_y, 2, cells_y, 4 * peers * rows_ky)


def output_table(table):
    high, low = split_table(table)
    parts = [high, high, low, np.ones(table.shape[:-1] + (BIAS_TERMS,), high.dtype)]
    used = 3 * table.shape[-1] + BIAS_TERMS
    parts.append(np.zeros(table.shape[:-1] + (-used % 256,), high.dtype))
    return np.concatenate(parts, axis=-1)


def dot(left, right):
    return jnp.dot(left, right, preferred_element_type=jnp.float32)


def forward_y_table(shape, extent, layers, rows_ky):
    z, x, y = quad()
    peers = 2 * layers
    row = lax.broadcasted_iota(jnp.int32, (shape[0], 1), 0)
    block = row // (2 * rows_ky)
    place = block // 2 % layers
    turn = jnp.where(place < layers // 2, place + layers // 2, layers - 1 - place)
    side = y ^ (1 - block // peers)
    owner = (side ^ (block % 2)) * peers + (z ^ turn) * 2 + (x ^ side)
    index = owner * rows_ky + row // 2 % rows_ky
    y_places = lax.broadcasted_iota(jnp.int32, (1, shape[1]), 1) + y * shape[1]
    steps = (wave_number(index, MY) * y_places) & (extent - 1)
    angle = 2.0 * math.pi / extent * steps.astype(jnp.float32)
    return jnp.where(row % 2 == 0, jnp.cos(angle), -jnp.sin(angle)).astype(jnp.bfloat16)


def forward_y_kernel(extent, rows_ky, flow_hbm, send_ref, keep_ref, flow_ref, arrived):
    layers, _, rows, feat_count = send_ref.shape
    cells_x, cells_y, _ = flow_ref.shape
    rows = rows // cells_x
    copies = [
        pltpu.make_async_copy(flow_hbm.at[x], flow_ref.at[x], arrived.at[x])
        for x in range(cells_x)
    ]
    for copy in copies:
        copy.start()
    table = forward_y_table((2 * MY, cells_y), extent, layers, rows_ky)
    for x in range(cells_x):
        copies[x].wait()
        result = dot(table, flow_ref[x]).reshape(2, layers, 2, rows, feat_count)
        send_ref[:, :, x * rows : (x + 1) * rows, :] = result[0]
        keep_ref[:, :, x * rows : (x + 1) * rows, :] = result[1]


def forward_y(flow_field, extent, layers, rows_ky):
    cells_x, _, feat_count = flow_field.shape
    shape = jax.ShapeDtypeStruct((layers, 2, cells_x * 2 * rows_ky, feat_count), jnp.float32)
    return pl.pallas_call(
        functools.partial(forward_y_kernel, extent, rows_ky),
        in_specs=[pl.BlockSpec(memory_space=pltpu.HBM)],
        out_shape=[shape] * 2,
        scratch_shapes=[
            pltpu.VMEM(flow_field.shape, flow_field.dtype),
            pltpu.SemaphoreType.DMA((cells_x,)),
        ],
        compiler_params=LARGE,
        name="forward_y",
    )(flow_field)


def flip_core(block):
    return lax.ppermute(block, "gy", [(0, 1), (1, 0)])


def along_columns(blocks, peers):
    arrived = []
    for turn, block in zip(turns(len(blocks)), blocks):
        pairs = [
            (2 * place + core, 2 * (place ^ (2 * turn + core)) + core)
            for place in range(peers)
            for core in range(2)
        ]
        arrived.append(lax.ppermute(block, ("gx", "gy"), pairs))
    return arrived


def small_call(kernel, out_shape, name):
    return pl.pallas_call(kernel, out_shape=out_shape, compiler_params=SMALL, name=name)


def second_kernel(block_ref, out_ref):
    out_ref[...] = block_ref[1]


def second_half(block):
    shape = jax.ShapeDtypeStruct(block.shape[1:], block.dtype)
    return small_call(second_kernel, shape, "second_half")(block)


def add_kernel(keep_ref, arrived_ref, *out_refs):
    for turn, out_ref in enumerate(out_refs):
        out_ref[...] = keep_ref[turn] + arrived_ref[turn]


def add_blocks(keep, arrived):
    shape = jax.ShapeDtypeStruct(keep.shape[1:], keep.dtype)
    return small_call(add_kernel, [shape] * keep.shape[0], "add_blocks")(keep, arrived)


def join_kernel(keep_ref, arrived_ref, *out_refs):
    cells_x, rows, _ = out_refs[0].shape
    rows = rows // 2
    for turn, out_ref in enumerate(out_refs):
        for cell in range(cells_x):
            span = slice(cell * rows, (cell + 1) * rows)
            out_ref[cell] = jnp.concatenate(
                [keep_ref[turn, span, :], arrived_ref[turn, span, :]], axis=0
            )


def join_blocks(keep, arrived, cells_x):
    layers, rows, feat_count = keep.shape
    shape = jax.ShapeDtypeStruct((cells_x, 2 * rows // cells_x, feat_count), keep.dtype)
    return small_call(join_kernel, [shape] * layers, "join_blocks")(keep, arrived)


def back_rows(inverse_high, inverse_low, column, modes):
    high, low = split_terms(modes)
    table = inverse_high[column]
    return dot(table, high) + dot(table, low) + dot(inverse_low[column], high)


def store_turns(out_ref, order_ref, z):
    for index, turn in enumerate(turns(out_ref.shape[0])):
        out_ref[index] = order_ref[z ^ turn]


def mix_kernel(layers, *refs):
    block_refs, arrived_refs = refs[:layers], refs[layers : 2 * layers]
    weight_ref, forward_high, forward_low, inverse_high, inverse_low = refs[
        2 * layers : 2 * layers + 5
    ]
    modes_ref, send_ref, order_ref, spread_ref, result_ref = refs[2 * layers + 5 :]
    z, x, y = quad()
    column = x ^ y
    for index, turn in enumerate(turns(layers)):
        order_ref[(z ^ turn) * 2 + column] = block_refs[index][0]
        order_ref[(z ^ turn) * 2 + (column ^ 1)] = arrived_refs[index][...]
    feat_count = order_ref.shape[-1]
    count = weight_ref.shape[1]
    channels = weight_ref.shape[2]
    tiles = feat_count // 128
    group = 2 * tiles
    high, low = split_terms(order_ref[...].reshape(-1, feat_count))
    spectrum = (
        dot(forward_high[...], high) + dot(forward_high[...], low) + dot(forward_low[...], high)
    )
    for part in range(2):
        for tile in range(tiles):
            spread_ref[pl.ds(part * tiles + tile, count, stride=group), :] = spectrum[
                part * count : (part + 1) * count, tile * 128 : (tile + 1) * 128
            ]
    rows = lax.broadcasted_iota(jnp.int32, (8, 128), 0) % group
    lane = lax.broadcasted_iota(jnp.int32, (8, 128), 1) < channels
    sign = jnp.where(rows < tiles, -1.0, 1.0)
    for base in range(0, count * group, 8):
        block = spread_ref[base : base + 8, :]
        turned = pltpu.roll(block, channels, 1)
        firsts, seconds = [], []
        for start in range(0, 8, group):
            span = slice(start, start + group)
            left = jnp.concatenate([block[span], turned[span]], axis=0)[:, :channels]
            left_high, left_low = split_terms(left)
            left = jnp.concatenate([left_high, left_low], axis=0)
            product = dot(left, weight_ref[0, (base + start) // group])
            product = product[: 2 * group] + product[2 * group :]
            firsts.append(product[:group])
            seconds.append(product[group:])
        first = jnp.concatenate(firsts, axis=0)
        second = jnp.concatenate(seconds, axis=0)
        real = jnp.where(lane, first, pltpu.roll(second, channels, 1))
        imag = jnp.where(lane, pltpu.roll(first, channels, 1), second)
        crossed = jnp.where(rows < tiles, pltpu.roll(imag, 8 - tiles, 0), pltpu.roll(imag, tiles, 0))
        result_ref[base : base + 8, :] = real + sign * crossed
    for part in range(2):
        for tile in range(tiles):
            modes_ref[part * count : (part + 1) * count, tile * 128 : (tile + 1) * 128] = (
                result_ref[pl.ds(part * tiles + tile, count, stride=group), :]
            )
    back = back_rows(inverse_high, inverse_low, column ^ 1, modes_ref[...])
    order_ref[:layers] = back.reshape(send_ref.shape)
    store_turns(send_ref, order_ref, z)


def mix(blocks, arrived, weights, forward_table, inverse_tables):
    layers = len(blocks)
    _, rows, feat_count = blocks[0].shape
    count = weights.shape[1]
    scratch = pltpu.VMEM((count * feat_count // 64, 128), jnp.float32)
    return pl.pallas_call(
        functools.partial(mix_kernel, layers),
        out_shape=[
            jax.ShapeDtypeStruct((2 * count, feat_count), jnp.float32),
            jax.ShapeDtypeStruct((layers, rows, feat_count), jnp.float32),
        ],
        scratch_shapes=[pltpu.VMEM((2 * layers, rows, feat_count), jnp.float32), scratch, scratch],
        compiler_params=SMALL,
        name="mix",
    )(*blocks, *arrived, weights, *split_table(forward_table), *inverse_tables)


def keep_kernel(modes_ref, inverse_high, inverse_low, mixed_ref, keep_ref, order_ref):
    z, x, y = quad()
    count = mixed_ref.shape[1]
    feat_count = modes_ref.shape[1]
    for part in range(2):
        mixed_ref[0, :, part * feat_count : (part + 1) * feat_count] = modes_ref[
            part * count : (part + 1) * count
        ]
    back = back_rows(inverse_high, inverse_low, x ^ y, modes_ref[...])
    order_ref[...] = back.reshape(keep_ref.shape)
    store_turns(keep_ref, order_ref, z)


def keep_rows(modes, inverse_tables, like):
    rows, feat_count = modes.shape
    return pl.pallas_call(
        keep_kernel,
        out_shape=[
            jax.ShapeDtypeStruct((1, rows // 2, 2 * feat_count), jnp.float32),
            jax.ShapeDtypeStruct(like.shape, jnp.float32),
        ],
        scratch_shapes=[pltpu.VMEM(like.shape, jnp.float32)],
        compiler_params=SMALL,
        name="keep_rows",
    )(modes, *inverse_tables)


def gelu(values):
    square = jnp.minimum(values * values, 31.36)
    inner = jnp.full_like(square, GELU_TERMS[-1])
    for term in GELU_TERMS[-2::-1]:
        inner = inner * square + term
    half = 0.5 * values
    return half + half * jnp.tanh(values * inner)


def output_kernel(layers, flow_ref, table_ref, local_ref, bias_ref, *refs):
    own_refs, core_refs = refs[:layers], refs[layers : 2 * layers]
    out_hbm, order_ref, wide_ref, level_ref, done_ref, sent = refs[2 * layers :]
    cells_x, cells_y, feat_count = flow_ref.shape
    channels = local_ref.shape[0]
    z, x, y = quad()
    wide_ref[...] = jnp.zeros_like(wide_ref)
    for start in range(0, WIDTH, channels):
        span = slice(start, start + channels)
        wide_ref[span, span] = local_ref[...]
        level_ref[:, span] = bias_ref[...].reshape(1, channels)
    level = level_ref[...]
    levels = []
    for _ in range(BIAS_TERMS):
        levels.append(level.astype(jnp.bfloat16).astype(jnp.float32))
        level = level - levels[-1]
    terms = 3 * order_ref.shape[1] * order_ref.shape[2]
    filled = jnp.zeros((table_ref.shape[-1] - terms - BIAS_TERMS, WIDTH), jnp.float32)
    below = jnp.concatenate(levels + [filled], axis=0).astype(jnp.bfloat16)
    below = jnp.concatenate([below, wide_ref[...]], axis=0)
    for column, block_refs in ((x ^ y, own_refs), (x ^ y ^ 1, core_refs)):
        for turn, block_ref in zip(turns(layers), block_refs):
            order_ref[:, (z ^ turn) * 2 + column] = block_ref[...]
    table = table_ref[y, x ^ y]
    copies = []
    for cell in range(cells_x):
        high, low = split_terms(order_ref[cell].reshape(-1, feat_count))
        stack = jnp.concatenate([high, low, high], axis=0)
        bounds = [0, FIRST, cells_y] if cell == 0 else [0, cells_y]
        for begin, end in zip(bounds[:-1], bounds[1:]):
            rows = slice(begin, end)
            for start in range(0, feat_count, WIDTH):
                columns = slice(start, start + WIDTH)
                total = dot(
                    jnp.concatenate([table[rows], flow_ref[cell, rows, columns]], axis=1),
                    jnp.concatenate([stack[:, columns], below], axis=0),
                )
                done_ref[cell, rows, columns] = gelu(total).astype(done_ref.dtype)
            copies.append(
                pltpu.make_async_copy(
                    done_ref.at[cell, rows], out_hbm.at[cell, rows], sent.at[len(copies)]
                )
            )
            copies[-1].start()
    for copy in copies:
        copy.wait()


def make_output(flow_field, parts, table, local, bias):
    cells_x, _, feat_count = flow_field.shape
    layers = len(parts) // 2
    return pl.pallas_call(
        functools.partial(output_kernel, layers),
        out_specs=pl.BlockSpec(memory_space=pl.ANY),
        scratch_shapes=[
            pltpu.VMEM((cells_x, 2 * layers) + parts[0].shape[1:], jnp.float32),
            pltpu.VMEM((WIDTH, WIDTH), jnp.bfloat16),
            pltpu.VMEM((1, WIDTH), jnp.float32),
            pltpu.VMEM(flow_field.shape, jnp.bfloat16),
            pltpu.SemaphoreType.DMA((cells_x + 1,)),
        ],
        out_shape=jax.ShapeDtypeStruct(flow_field.shape, jnp.bfloat16),
        compiler_params=SMALL,
        name="make_output",
    )(flow_field, table, local, bias, *parts)


def row_body(flow_field, spectral_weight, local_weight, bias_terms):
    cells_x, cells_y, feat_count = flow_field.shape
    peers = lax.axis_size("gx")
    groups_y = lax.axis_size("gy")
    rows_ky = MY // groups_y // peers
    forward_scale = 1.0 / math.sqrt(cells_x * peers * cells_y * groups_y)
    inverse_scale = 1.0 / math.sqrt(MX * MY)

    send, keep = forward_y(flow_field, cells_y * groups_y, peers // 2, rows_ky)
    blocks = along_columns(add_blocks(keep, flip_core(send)), peers)
    inverse_tables = split_table(inverse_x_table(cells_x, peers, rows_ky))
    modes, send = mix(
        blocks,
        [flip_core(second_half(block)) for block in blocks],
        spectral_weight,
        forward_x_table(cells_x, peers, rows_ky) * forward_scale,
        inverse_tables,
    )
    arrived = flip_core(send)
    mixed, keep = keep_rows(modes, inverse_tables, send)
    own = along_columns(join_blocks(keep, arrived, cells_x), peers)
    parts = own + [flip_core(block) for block in own]
    table = output_table(inverse_y_table(cells_y, groups_y, peers, rows_ky) * inverse_scale)
    return make_output(flow_field, parts, table, local_weight, bias_terms), mixed


def body(flow_field, spectral_weight, local_weight, bias_terms):
    peers = lax.axis_size("gx")
    extent = lax.axis_size("gy") * flow_field.shape[1]
    paired = lax.axis_size("gy") == 2 and peers & (peers - 1) == 0 and extent & (extent - 1) == 0
    if paired and spectral_weight.shape[1] == 2 * MX and WIDTH % local_weight.shape[0] == 0:
        return row_body(flow_field, spectral_weight, local_weight, bias_terms)
    return general_body(flow_field, spectral_weight, local_weight, bias_terms)


def solution(mesh):
    placed = (P(("group", "gx"), "gy", None), P("gy", "gx", None, None), P(), P())
    return jax.shard_map(
        body,
        mesh=mesh,
        in_specs=placed,
        out_specs=(P(("group", "gx"), "gy", None), P(("group", "gy"), "gx", None)),
        check_vma=False,
    )
```

```python
import functools
import math

import jax
import jax.numpy as jnp
import ml_dtypes
import numpy as np
from jax import lax
from jax.experimental import pallas as pl
from jax.experimental.pallas import tpu as pltpu
from jax.sharding import PartitionSpec as P

MX = 32
MY = 32


def wave_number(index, count):
    return jnp.where(index < count // 2, index, index - count)


def phase_table(waves, places, extent):
    product = waves[:, None] * places[None, :] % extent
    return 2.0 * math.pi / extent * product.astype(jnp.float32)


def row_tables(ky_rows, kx_rows, x_places, extent, width):
    angle = phase_table(wave_number(kx_rows, MX), x_places, extent)
    select = (ky_rows[:, None] == jnp.arange(width, dtype=jnp.int32)[None, :]).astype(jnp.float32)
    cosine = jnp.cos(angle)[:, :, None] * select[:, None, :]
    sine_part = jnp.sin(angle)[:, :, None] * select[:, None, :]
    return (cosine, sine_part)


def forward_rows(y_local, ky_rows, kx_rows, x_places, extent):
    cosine, sine_part = row_tables(ky_rows, kx_rows, x_places, extent, y_local.shape[0])
    real_in = y_local[:, 0]
    imag_in = y_local[:, 1]

    def contract(table, values):
        return jnp.einsum("rxk,kxf->rf", table, values, precision=lax.Precision.HIGHEST)

    real_out = contract(cosine, real_in) + contract(sine_part, imag_in)
    imag_out = contract(cosine, imag_in) - contract(sine_part, real_in)
    return jnp.concatenate([real_out, imag_out], axis=1)


def inverse_rows(running, shard_rows, ky_rows, kx_rows, x_places, extent):
    cosine, sine_part = row_tables(ky_rows, kx_rows, x_places, extent, running.shape[0])
    feat_count = shard_rows.shape[1] // 2
    real_part = shard_rows[:, :feat_count]
    imag_part = shard_rows[:, feat_count:]

    def contract(table, values):
        return jnp.einsum("rxk,rf->kxf", table, values, precision=lax.Precision.HIGHEST)

    new_real = contract(cosine, real_part) - contract(sine_part, imag_part)
    new_imag = contract(cosine, imag_part) + contract(sine_part, real_part)
    return jnp.stack([new_real, new_imag], axis=1)


def general_body(flow_field, spectral_weight, local_weight, bias_terms):
    cells_x, cells_y, feat_count = flow_field.shape
    channels = local_weight.shape[0]
    planes = feat_count // channels
    groups_x = lax.axis_size("gx")
    groups_y = lax.axis_size("gy")
    extent_x = cells_x * groups_x
    extent_y = cells_y * groups_y
    half_width = MY // groups_y
    quota_rows = spectral_weight.shape[1]
    high = lax.Precision.HIGHEST
    x_places = lax.axis_index("gx") * cells_x + jnp.arange(cells_x, dtype=jnp.int32)
    y_places = lax.axis_index("gy") * cells_y + jnp.arange(cells_y, dtype=jnp.int32)
    y_angle = phase_table(wave_number(jnp.arange(MY, dtype=jnp.int32), MY), y_places, extent_y)
    y_table = (
        jnp.stack([jnp.cos(y_angle), -jnp.sin(y_angle)], axis=1)
        .reshape(2 * MY, cells_y)
        .astype(jnp.bfloat16)
    )
    y_local = lax.psum_scatter(
        jnp.einsum("qy,xyf->qxf", y_table, flow_field, preferred_element_type=jnp.float32),
        "gy",
        scatter_dimension=0,
        tiled=True,
    )
    y_local = y_local.reshape(half_width, 2, cells_x, feat_count)
    rest_index = jnp.arange(lax.axis_size("gx") * quota_rows, dtype=jnp.int32)
    spectrum = lax.psum_scatter(
        forward_rows(y_local, rest_index // MX, rest_index % MX, x_places, extent_x),
        "gx",
        scatter_dimension=0,
        tiled=True,
    )
    spectrum = spectrum * (1.0 / math.sqrt(extent_x * extent_y))
    coeffs = spectrum.reshape(quota_rows, 2, planes, channels)
    weights = spectral_weight[0].astype(jnp.float32)
    product = jnp.einsum("rpzc,rco->rpzo", coeffs, weights, precision=high)
    mixed_real = product[:, 0, :, :channels] - product[:, 1, :, channels:]
    mixed_imag = product[:, 0, :, channels:] + product[:, 1, :, :channels]
    mixed_local = jnp.stack([mixed_real, mixed_imag], axis=1).reshape(quota_rows, 2 * feat_count)
    pointwise = jnp.einsum(
        "xyzc,co->xyzo",
        flow_field.reshape(cells_x, cells_y, planes, channels),
        local_weight,
        preferred_element_type=jnp.float32,
    )
    start_half = jnp.zeros((half_width, 2, cells_x, feat_count), jnp.float32)
    shard_rows = lax.all_gather(mixed_local, "gx", axis=0, tiled=True)
    rest_index = jnp.arange(shard_rows.shape[0], dtype=jnp.int32)
    back_half = inverse_rows(
        start_half, shard_rows, rest_index // MX, rest_index % MX, x_places, extent_x
    )
    back_whole = lax.all_gather(back_half, "gy", axis=0, tiled=True)
    y_cos = jnp.cos(y_angle)
    y_sin = jnp.sin(y_angle)
    spectral = (
        jnp.einsum("kn,kxf->xnf", y_cos, back_whole[:, 0], precision=high)
        - jnp.einsum("kn,kxf->xnf", y_sin, back_whole[:, 1], precision=high)
    ) * (1.0 / math.sqrt(MX * MY))
    total = spectral.reshape(cells_x, cells_y, planes, channels) + pointwise + bias_terms
    output = (
        jax.nn.gelu(total, approximate=False)
        .reshape(cells_x, cells_y, feat_count)
        .astype(jnp.bfloat16)
    )
    return (output, mixed_local.reshape(1, quota_rows, 2 * feat_count))


SMALL = pltpu.CompilerParams(vmem_limit_bytes=20 * 1024 * 1024)
LARGE = pltpu.CompilerParams(vmem_limit_bytes=53 * 1024 * 1024)
WIDTH = 256
BIAS_TERMS = 3
FIRST = 64
POWER_TERMS = tuple(-2.0 * math.log2(math.e) * term for term in (
    0.7978849411010742,
    0.03633308410644531,
    -3.259492223151028e-05,
    -5.530622001970187e-05,
    3.964749794249656e-06,
    -1.3226382122866198e-07,
    1.7561855303327434e-09,
))


def angles(count, places, extent):
    index = np.arange(count)
    waves = np.where(index < count // 2, index, index - count)
    product = (waves[:, None] * np.asarray(places)[None, :]) % extent
    return (np.float32(2.0 * math.pi / extent) * product.astype(np.float32)).astype(np.float64)


def split_table(table):
    high = table.astype(ml_dtypes.bfloat16)
    low = (table - high.astype(np.float64)).astype(ml_dtypes.bfloat16)
    return high, low


def split_terms(values):
    high = values.astype(jnp.bfloat16)
    low = (values - high.astype(jnp.float32)).astype(jnp.bfloat16)
    return high, low


def quad():
    place = lax.axis_index("gx")
    return place // 2, place % 2, lax.axis_index("gy")


def turns(layers):
    half = layers // 2
    return list(range(half, layers)) + list(range(half - 1, -1, -1))


def forward_x_table(cells_x, peers, rows_ky):
    extent = cells_x * peers
    angle = angles(MX, np.arange(extent), extent)
    cosine, sine = np.cos(angle), np.sin(angle)
    out = np.zeros((2, rows_ky, MX, extent, rows_ky, 2))
    for row in range(rows_ky):
        out[0, row, :, :, row, 0] = cosine
        out[0, row, :, :, row, 1] = sine
        out[1, row, :, :, row, 1] = cosine
        out[1, row, :, :, row, 0] = -sine
    return out.reshape(2 * rows_ky * MX, extent * rows_ky * 2)


def inverse_x_table(cells_x, peers, rows_ky):
    extent = cells_x * peers
    angle = angles(MX, np.arange(extent), extent)
    cosine, sine = np.cos(angle).T, np.sin(angle).T
    out = np.zeros((extent, rows_ky, 2, 2, rows_ky, MX))
    for row in range(rows_ky):
        out[:, row, 0, 0, row, :] = cosine
        out[:, row, 0, 1, row, :] = -sine
        out[:, row, 1, 1, row, :] = cosine
        out[:, row, 1, 0, row, :] = sine
    out = out.reshape(peers // 2, 2, cells_x * rows_ky * 2, 2 * rows_ky * MX)
    return np.moveaxis(out, 1, 0).reshape(2, -1, 2 * rows_ky * MX)


def inverse_y_table(cells_y, groups_y, peers, rows_ky):
    extent = cells_y * groups_y
    angle = angles(MY, np.arange(extent), extent)
    full = np.stack([np.cos(angle), -np.sin(angle)], axis=1)
    full = full.reshape(groups_y, peers, rows_ky, 2, groups_y, cells_y)
    out = np.zeros((groups_y, 2, cells_y, peers, 2, rows_ky, 2))
    for y in range(groups_y):
        for column in range(2):
            for peer in range(peers):
                for place in range(2):
                    half = y ^ place ^ column ^ (peer % 2)
                    out[y, column, :, peer, place] = np.moveaxis(full[half, peer, :, :, y], -1, 0)
    return out.reshape(groups_y, 2, cells_y, 4 * peers * rows_ky)


def output_table(table):
    high, low = split_table(table)
    parts = [high, high, low, np.ones(table.shape[:-1] + (BIAS_TERMS,), high.dtype)]
    used = 3 * table.shape[-1] + BIAS_TERMS
    parts.append(np.zeros(table.shape[:-1] + (-used % 256,), high.dtype))
    return np.concatenate(parts, axis=-1)


def dot(left, right):
    return jnp.dot(left, right, preferred_element_type=jnp.float32)


def forward_y_table(shape, extent, layers, rows_ky):
    z, x, y = quad()
    peers = 2 * layers
    row = lax.broadcasted_iota(jnp.int32, (shape[0], 1), 0)
    block = row // (2 * rows_ky)
    place = block // 2 % layers
    turn = jnp.where(place < layers // 2, place + layers // 2, layers - 1 - place)
    side = y ^ (1 - block // peers)
    owner = (side ^ (block % 2)) * peers + (z ^ turn) * 2 + (x ^ side)
    index = owner * rows_ky + row // 2 % rows_ky
    y_places = lax.broadcasted_iota(jnp.int32, (1, shape[1]), 1) + y * shape[1]
    steps = (wave_number(index, MY) * y_places) & (extent - 1)
    angle = 2.0 * math.pi / extent * steps.astype(jnp.float32)
    return jnp.where(row % 2 == 0, jnp.cos(angle), -jnp.sin(angle)).astype(jnp.bfloat16)


def forward_y_kernel(extent, rows_ky, flow_hbm, send_ref, keep_ref, flow_ref, arrived):
    layers, _, rows, feat_count = send_ref.shape
    cells_x, cells_y, _ = flow_ref.shape
    rows = rows // cells_x
    copies = [
        pltpu.make_async_copy(flow_hbm.at[x], flow_ref.at[x], arrived.at[x])
        for x in range(cells_x)
    ]
    for copy in copies:
        copy.start()
    table = forward_y_table((2 * MY, cells_y), extent, layers, rows_ky)
    for x in range(cells_x):
        copies[x].wait()
        result = dot(table, flow_ref[x]).reshape(2, layers, 2, rows, feat_count)
        send_ref[:, :, x * rows : (x + 1) * rows, :] = result[0]
        keep_ref[:, :, x * rows : (x + 1) * rows, :] = result[1]


def forward_y(flow_field, extent, layers, rows_ky):
    cells_x, _, feat_count = flow_field.shape
    shape = jax.ShapeDtypeStruct((layers, 2, cells_x * 2 * rows_ky, feat_count), jnp.float32)
    return pl.pallas_call(
        functools.partial(forward_y_kernel, extent, rows_ky),
        in_specs=[pl.BlockSpec(memory_space=pltpu.HBM)],
        out_shape=[shape] * 2,
        scratch_shapes=[
            pltpu.VMEM(flow_field.shape, flow_field.dtype),
            pltpu.SemaphoreType.DMA((cells_x,)),
        ],
        compiler_params=LARGE,
        name="forward_y",
    )(flow_field)


def flip_core(block):
    return lax.ppermute(block, "gy", [(0, 1), (1, 0)])


def along_columns(blocks, peers):
    arrived = []
    for turn, block in zip(turns(len(blocks)), blocks):
        pairs = [
            (2 * place + core, 2 * (place ^ (2 * turn + core)) + core)
            for place in range(peers)
            for core in range(2)
        ]
        arrived.append(lax.ppermute(block, ("gx", "gy"), pairs))
    return arrived


def small_call(kernel, out_shape, name):
    return pl.pallas_call(kernel, out_shape=out_shape, compiler_params=SMALL, name=name)


def second_kernel(block_ref, out_ref):
    out_ref[...] = block_ref[1]


def second_half(block):
    shape = jax.ShapeDtypeStruct(block.shape[1:], block.dtype)
    return small_call(second_kernel, shape, "second_half")(block)


def add_kernel(keep_ref, arrived_ref, *out_refs):
    for turn, out_ref in enumerate(out_refs):
        out_ref[...] = keep_ref[turn] + arrived_ref[turn]


def add_blocks(keep, arrived):
    shape = jax.ShapeDtypeStruct(keep.shape[1:], keep.dtype)
    return small_call(add_kernel, [shape] * keep.shape[0], "add_blocks")(keep, arrived)


def join_kernel(keep_ref, arrived_ref, *out_refs):
    cells_x, rows, _ = out_refs[0].shape
    rows = rows // 2
    for turn, out_ref in enumerate(out_refs):
        for cell in range(cells_x):
            span = slice(cell * rows, (cell + 1) * rows)
            out_ref[cell] = jnp.concatenate(
                [keep_ref[turn, span, :], arrived_ref[turn, span, :]], axis=0
            )


def join_blocks(keep, arrived, cells_x):
    layers, rows, feat_count = keep.shape
    shape = jax.ShapeDtypeStruct((cells_x, 2 * rows // cells_x, feat_count), keep.dtype)
    return small_call(join_kernel, [shape] * layers, "join_blocks")(keep, arrived)


def back_rows(inverse_high, inverse_low, column, modes):
    high, low = split_terms(modes)
    table = inverse_high[column]
    return dot(table, high) + dot(table, low) + dot(inverse_low[column], high)


def store_turns(out_ref, order_ref, z):
    for index, turn in enumerate(turns(out_ref.shape[0])):
        out_ref[index] = order_ref[z ^ turn]


def mix_kernel(layers, *refs):
    block_refs, arrived_refs = refs[:layers], refs[layers : 2 * layers]
    weight_ref, forward_high, forward_low, inverse_high, inverse_low = refs[
        2 * layers : 2 * layers + 5
    ]
    modes_ref, send_ref, order_ref, spread_ref, result_ref = refs[2 * layers + 5 :]
    z, x, y = quad()
    column = x ^ y
    for index, turn in enumerate(turns(layers)):
        order_ref[(z ^ turn) * 2 + column] = block_refs[index][0]
        order_ref[(z ^ turn) * 2 + (column ^ 1)] = arrived_refs[index][...]
    feat_count = order_ref.shape[-1]
    count = weight_ref.shape[1]
    channels = weight_ref.shape[2]
    tiles = feat_count // 128
    group = 2 * tiles
    high, low = split_terms(order_ref[...].reshape(-1, feat_count))
    spectrum = (
        dot(forward_high[...], high) + dot(forward_high[...], low) + dot(forward_low[...], high)
    )
    for part in range(2):
        for tile in range(tiles):
            spread_ref[pl.ds(part * tiles + tile, count, stride=group), :] = spectrum[
                part * count : (part + 1) * count, tile * 128 : (tile + 1) * 128
            ]
    rows = lax.broadcasted_iota(jnp.int32, (8, 128), 0) % group
    lane = lax.broadcasted_iota(jnp.int32, (8, 128), 1) < channels
    sign = jnp.where(rows < tiles, -1.0, 1.0)
    for base in range(0, count * group, 8):
        block = spread_ref[base : base + 8, :]
        turned = pltpu.roll(block, channels, 1)
        firsts, seconds = [], []
        for start in range(0, 8, group):
            span = slice(start, start + group)
            left = jnp.concatenate([block[span], turned[span]], axis=0)[:, :channels]
            left_high, left_low = split_terms(left)
            left = jnp.concatenate([left_high, left_low], axis=0)
            product = dot(left, weight_ref[0, (base + start) // group])
            product = product[: 2 * group] + product[2 * group :]
            firsts.append(product[:group])
            seconds.append(product[group:])
        first = jnp.concatenate(firsts, axis=0)
        second = jnp.concatenate(seconds, axis=0)
        real = jnp.where(lane, first, pltpu.roll(second, channels, 1))
        imag = jnp.where(lane, pltpu.roll(first, channels, 1), second)
        crossed = jnp.where(rows < tiles, pltpu.roll(imag, 8 - tiles, 0), pltpu.roll(imag, tiles, 0))
        result_ref[base : base + 8, :] = real + sign * crossed
    for part in range(2):
        for tile in range(tiles):
            modes_ref[part * count : (part + 1) * count, tile * 128 : (tile + 1) * 128] = (
                result_ref[pl.ds(part * tiles + tile, count, stride=group), :]
            )
    back = back_rows(inverse_high, inverse_low, column ^ 1, modes_ref[...])
    order_ref[:layers] = back.reshape(send_ref.shape)
    store_turns(send_ref, order_ref, z)


def mix(blocks, arrived, weights, forward_table, inverse_tables):
    layers = len(blocks)
    _, rows, feat_count = blocks[0].shape
    count = weights.shape[1]
    scratch = pltpu.VMEM((count * feat_count // 64, 128), jnp.float32)
    return pl.pallas_call(
        functools.partial(mix_kernel, layers),
        out_shape=[
            jax.ShapeDtypeStruct((2 * count, feat_count), jnp.float32),
            jax.ShapeDtypeStruct((layers, rows, feat_count), jnp.float32),
        ],
        scratch_shapes=[pltpu.VMEM((2 * layers, rows, feat_count), jnp.float32), scratch, scratch],
        compiler_params=SMALL,
        name="mix",
    )(*blocks, *arrived, weights, *split_table(forward_table), *inverse_tables)


def keep_kernel(modes_ref, inverse_high, inverse_low, mixed_ref, keep_ref, order_ref):
    z, x, y = quad()
    count = mixed_ref.shape[1]
    feat_count = modes_ref.shape[1]
    for part in range(2):
        mixed_ref[0, :, part * feat_count : (part + 1) * feat_count] = modes_ref[
            part * count : (part + 1) * count
        ]
    back = back_rows(inverse_high, inverse_low, x ^ y, modes_ref[...])
    order_ref[...] = back.reshape(keep_ref.shape)
    store_turns(keep_ref, order_ref, z)


def keep_rows(modes, inverse_tables, like):
    rows, feat_count = modes.shape
    return pl.pallas_call(
        keep_kernel,
        out_shape=[
            jax.ShapeDtypeStruct((1, rows // 2, 2 * feat_count), jnp.float32),
            jax.ShapeDtypeStruct(like.shape, jnp.float32),
        ],
        scratch_shapes=[pltpu.VMEM(like.shape, jnp.float32)],
        compiler_params=SMALL,
        name="keep_rows",
    )(modes, *inverse_tables)


def gelu(values):
    square = jnp.minimum(values * values, 31.36)
    power = jnp.full_like(square, POWER_TERMS[-1])
    for term in POWER_TERMS[-2::-1]:
        power = power * square + term
    below = 1.0 + jnp.exp2(jnp.minimum(values * power, 64.0))
    return values * pl.reciprocal(below, approx=True)


def output_kernel(layers, flow_ref, table_ref, local_ref, bias_ref, *refs):
    own_refs, core_refs = refs[:layers], refs[layers : 2 * layers]
    out_hbm, order_ref, wide_ref, level_ref, done_ref, sent = refs[2 * layers :]
    cells_x, cells_y, feat_count = flow_ref.shape
    channels = local_ref.shape[0]
    z, x, y = quad()
    wide_ref[...] = jnp.zeros_like(wide_ref)
    for start in range(0, WIDTH, channels):
        span = slice(start, start + channels)
        wide_ref[span, span] = local_ref[...]
        level_ref[:, span] = bias_ref[...].reshape(1, channels)
    level = level_ref[...]
    levels = []
    for _ in range(BIAS_TERMS):
        levels.append(level.astype(jnp.bfloat16).astype(jnp.float32))
        level = level - levels[-1]
    terms = 3 * order_ref.shape[1] * order_ref.shape[2]
    filled = jnp.zeros((table_ref.shape[-1] - terms - BIAS_TERMS, WIDTH), jnp.float32)
    below = jnp.concatenate(levels + [filled], axis=0).astype(jnp.bfloat16)
    below = jnp.concatenate([below, wide_ref[...]], axis=0)
    for column, block_refs in ((x ^ y, own_refs), (x ^ y ^ 1, core_refs)):
        for turn, block_ref in zip(turns(layers), block_refs):
            order_ref[:, (z ^ turn) * 2 + column] = block_ref[...]
    table = table_ref[y, x ^ y]
    copies = []
    for cell in range(cells_x):
        high, low = split_terms(order_ref[cell].reshape(-1, feat_count))
        stack = jnp.concatenate([high, low, high], axis=0)
        bounds = [0, FIRST, cells_y] if cell == 0 else [0, cells_y]
        for begin, end in zip(bounds[:-1], bounds[1:]):
            rows = slice(begin, end)
            for start in range(0, feat_count, WIDTH):
                columns = slice(start, start + WIDTH)
                total = dot(
                    jnp.concatenate([table[rows], flow_ref[cell, rows, columns]], axis=1),
                    jnp.concatenate([stack[:, columns], below], axis=0),
                )
                done_ref[cell, rows, columns] = gelu(total).astype(done_ref.dtype)
            copies.append(
                pltpu.make_async_copy(
                    done_ref.at[cell, rows], out_hbm.at[cell, rows], sent.at[len(copies)]
                )
            )
            copies[-1].start()
    for copy in copies:
        copy.wait()


def make_output(flow_field, parts, table, local, bias):
    cells_x, _, feat_count = flow_field.shape
    layers = len(parts) // 2
    return pl.pallas_call(
        functools.partial(output_kernel, layers),
        out_specs=pl.BlockSpec(memory_space=pl.ANY),
        scratch_shapes=[
            pltpu.VMEM((cells_x, 2 * layers) + parts[0].shape[1:], jnp.float32),
            pltpu.VMEM((WIDTH, WIDTH), jnp.bfloat16),
            pltpu.VMEM((1, WIDTH), jnp.float32),
            pltpu.VMEM(flow_field.shape, jnp.bfloat16),
            pltpu.SemaphoreType.DMA((cells_x + 1,)),
        ],
        out_shape=jax.ShapeDtypeStruct(flow_field.shape, jnp.bfloat16),
        compiler_params=SMALL,
        name="make_output",
    )(flow_field, table, local, bias, *parts)


def row_body(flow_field, spectral_weight, local_weight, bias_terms):
    cells_x, cells_y, feat_count = flow_field.shape
    peers = lax.axis_size("gx")
    groups_y = lax.axis_size("gy")
    rows_ky = MY // groups_y // peers
    forward_scale = 1.0 / math.sqrt(cells_x * peers * cells_y * groups_y)
    inverse_scale = 1.0 / math.sqrt(MX * MY)

    send, keep = forward_y(flow_field, cells_y * groups_y, peers // 2, rows_ky)
    blocks = along_columns(add_blocks(keep, flip_core(send)), peers)
    inverse_tables = split_table(inverse_x_table(cells_x, peers, rows_ky))
    modes, send = mix(
        blocks,
        [flip_core(second_half(block)) for block in blocks],
        spectral_weight,
        forward_x_table(cells_x, peers, rows_ky) * forward_scale,
        inverse_tables,
    )
    arrived = flip_core(send)
    mixed, keep = keep_rows(modes, inverse_tables, send)
    own = along_columns(join_blocks(keep, arrived, cells_x), peers)
    parts = own + [flip_core(block) for block in own]
    table = output_table(inverse_y_table(cells_y, groups_y, peers, rows_ky) * inverse_scale)
    return make_output(flow_field, parts, table, local_weight, bias_terms), mixed


def body(flow_field, spectral_weight, local_weight, bias_terms):
    peers = lax.axis_size("gx")
    extent = lax.axis_size("gy") * flow_field.shape[1]
    paired = lax.axis_size("gy") == 2 and peers & (peers - 1) == 0 and extent & (extent - 1) == 0
    if paired and spectral_weight.shape[1] == 2 * MX and WIDTH % local_weight.shape[0] == 0:
        return row_body(flow_field, spectral_weight, local_weight, bias_terms)
    return general_body(flow_field, spectral_weight, local_weight, bias_terms)


def solution(mesh):
    placed = (P(("group", "gx"), "gy", None), P("gy", "gx", None, None), P(), P())
    return jax.shard_map(
        body,
        mesh=mesh,
        in_specs=placed,
        out_specs=(P(("group", "gx"), "gy", None), P(("group", "gy"), "gx", None)),
        check_vma=False,
    )
```

```python
import functools
import math

import jax
import jax.numpy as jnp
import ml_dtypes
import numpy as np
from jax import lax
from jax.experimental import pallas as pl
from jax.experimental.pallas import tpu as pltpu
from jax.sharding import PartitionSpec as P

MX = 32
MY = 32


def wave_number(index, count):
    return jnp.where(index < count // 2, index, index - count)


def phase_table(waves, places, extent):
    product = waves[:, None] * places[None, :] % extent
    return 2.0 * math.pi / extent * product.astype(jnp.float32)


def row_tables(ky_rows, kx_rows, x_places, extent, width):
    angle = phase_table(wave_number(kx_rows, MX), x_places, extent)
    select = (ky_rows[:, None] == jnp.arange(width, dtype=jnp.int32)[None, :]).astype(jnp.float32)
    cosine = jnp.cos(angle)[:, :, None] * select[:, None, :]
    sine_part = jnp.sin(angle)[:, :, None] * select[:, None, :]
    return (cosine, sine_part)


def forward_rows(y_local, ky_rows, kx_rows, x_places, extent):
    cosine, sine_part = row_tables(ky_rows, kx_rows, x_places, extent, y_local.shape[0])
    real_in = y_local[:, 0]
    imag_in = y_local[:, 1]

    def contract(table, values):
        return jnp.einsum("rxk,kxf->rf", table, values, precision=lax.Precision.HIGHEST)

    real_out = contract(cosine, real_in) + contract(sine_part, imag_in)
    imag_out = contract(cosine, imag_in) - contract(sine_part, real_in)
    return jnp.concatenate([real_out, imag_out], axis=1)


def inverse_rows(running, shard_rows, ky_rows, kx_rows, x_places, extent):
    cosine, sine_part = row_tables(ky_rows, kx_rows, x_places, extent, running.shape[0])
    feat_count = shard_rows.shape[1] // 2
    real_part = shard_rows[:, :feat_count]
    imag_part = shard_rows[:, feat_count:]

    def contract(table, values):
        return jnp.einsum("rxk,rf->kxf", table, values, precision=lax.Precision.HIGHEST)

    new_real = contract(cosine, real_part) - contract(sine_part, imag_part)
    new_imag = contract(cosine, imag_part) + contract(sine_part, real_part)
    return jnp.stack([new_real, new_imag], axis=1)


def general_body(flow_field, spectral_weight, local_weight, bias_terms):
    cells_x, cells_y, feat_count = flow_field.shape
    channels = local_weight.shape[0]
    planes = feat_count // channels
    groups_x = lax.axis_size("gx")
    groups_y = lax.axis_size("gy")
    extent_x = cells_x * groups_x
    extent_y = cells_y * groups_y
    half_width = MY // groups_y
    quota_rows = spectral_weight.shape[1]
    high = lax.Precision.HIGHEST
    x_places = lax.axis_index("gx") * cells_x + jnp.arange(cells_x, dtype=jnp.int32)
    y_places = lax.axis_index("gy") * cells_y + jnp.arange(cells_y, dtype=jnp.int32)
    y_angle = phase_table(wave_number(jnp.arange(MY, dtype=jnp.int32), MY), y_places, extent_y)
    y_table = (
        jnp.stack([jnp.cos(y_angle), -jnp.sin(y_angle)], axis=1)
        .reshape(2 * MY, cells_y)
        .astype(jnp.bfloat16)
    )
    y_local = lax.psum_scatter(
        jnp.einsum("qy,xyf->qxf", y_table, flow_field, preferred_element_type=jnp.float32),
        "gy",
        scatter_dimension=0,
        tiled=True,
    )
    y_local = y_local.reshape(half_width, 2, cells_x, feat_count)
    rest_index = jnp.arange(lax.axis_size("gx") * quota_rows, dtype=jnp.int32)
    spectrum = lax.psum_scatter(
        forward_rows(y_local, rest_index // MX, rest_index % MX, x_places, extent_x),
        "gx",
        scatter_dimension=0,
        tiled=True,
    )
    spectrum = spectrum * (1.0 / math.sqrt(extent_x * extent_y))
    coeffs = spectrum.reshape(quota_rows, 2, planes, channels)
    weights = spectral_weight[0].astype(jnp.float32)
    product = jnp.einsum("rpzc,rco->rpzo", coeffs, weights, precision=high)
    mixed_real = product[:, 0, :, :channels] - product[:, 1, :, channels:]
    mixed_imag = product[:, 0, :, channels:] + product[:, 1, :, :channels]
    mixed_local = jnp.stack([mixed_real, mixed_imag], axis=1).reshape(quota_rows, 2 * feat_count)
    pointwise = jnp.einsum(
        "xyzc,co->xyzo",
        flow_field.reshape(cells_x, cells_y, planes, channels),
        local_weight,
        preferred_element_type=jnp.float32,
    )
    start_half = jnp.zeros((half_width, 2, cells_x, feat_count), jnp.float32)
    shard_rows = lax.all_gather(mixed_local, "gx", axis=0, tiled=True)
    rest_index = jnp.arange(shard_rows.shape[0], dtype=jnp.int32)
    back_half = inverse_rows(
        start_half, shard_rows, rest_index // MX, rest_index % MX, x_places, extent_x
    )
    back_whole = lax.all_gather(back_half, "gy", axis=0, tiled=True)
    y_cos = jnp.cos(y_angle)
    y_sin = jnp.sin(y_angle)
    spectral = (
        jnp.einsum("kn,kxf->xnf", y_cos, back_whole[:, 0], precision=high)
        - jnp.einsum("kn,kxf->xnf", y_sin, back_whole[:, 1], precision=high)
    ) * (1.0 / math.sqrt(MX * MY))
    total = spectral.reshape(cells_x, cells_y, planes, channels) + pointwise + bias_terms
    output = (
        jax.nn.gelu(total, approximate=False)
        .reshape(cells_x, cells_y, feat_count)
        .astype(jnp.bfloat16)
    )
    return (output, mixed_local.reshape(1, quota_rows, 2 * feat_count))


SMALL = pltpu.CompilerParams(vmem_limit_bytes=20 * 1024 * 1024)
LARGE = pltpu.CompilerParams(vmem_limit_bytes=53 * 1024 * 1024)
WIDTH = 256
BIAS_TERMS = 3
FIRST = 64
GELU_TERMS = (
    1.5957645177841187,
    0.29075613617897034,
    -0.0014313592109829187,
    -0.006452994421124458,
    0.0015898864949122071,
    -0.0001365363277727738,
)


def angles(count, places, extent):
    index = np.arange(count)
    waves = np.where(index < count // 2, index, index - count)
    product = (waves[:, None] * np.asarray(places)[None, :]) % extent
    return (np.float32(2.0 * math.pi / extent) * product.astype(np.float32)).astype(np.float64)


def split_table(table):
    high = table.astype(ml_dtypes.bfloat16)
    low = (table - high.astype(np.float64)).astype(ml_dtypes.bfloat16)
    return high, low


def split_terms(values):
    high = values.astype(jnp.bfloat16)
    low = (values - high.astype(jnp.float32)).astype(jnp.bfloat16)
    return high, low


def quad():
    place = lax.axis_index("gx")
    return place // 2, place % 2, lax.axis_index("gy")


def turns(layers):
    half = layers // 2
    return list(range(half, layers)) + list(range(half - 1, -1, -1))


def forward_x_table(cells_x, peers, rows_ky):
    extent = cells_x * peers
    angle = angles(MX, np.arange(extent), extent)
    cosine, sine = np.cos(angle), np.sin(angle)
    out = np.zeros((2, rows_ky, MX, extent, rows_ky, 2))
    for row in range(rows_ky):
        out[0, row, :, :, row, 0] = cosine
        out[0, row, :, :, row, 1] = sine
        out[1, row, :, :, row, 1] = cosine
        out[1, row, :, :, row, 0] = -sine
    return out.reshape(2 * rows_ky * MX, extent * rows_ky * 2)


def inverse_x_table(cells_x, peers, rows_ky):
    extent = cells_x * peers
    angle = angles(MX, np.arange(extent), extent)
    cosine, sine = np.cos(angle).T, np.sin(angle).T
    out = np.zeros((extent, rows_ky, 2, 2, rows_ky, MX))
    for row in range(rows_ky):
        out[:, row, 0, 0, row, :] = cosine
        out[:, row, 0, 1, row, :] = -sine
        out[:, row, 1, 1, row, :] = cosine
        out[:, row, 1, 0, row, :] = sine
    out = out.reshape(peers // 2, 2, cells_x * rows_ky * 2, 2 * rows_ky * MX)
    return np.moveaxis(out, 1, 0)


def inverse_y_table(cells_y, groups_y, peers, rows_ky):
    extent = cells_y * groups_y
    angle = angles(MY, np.arange(extent), extent)
    full = np.stack([np.cos(angle), -np.sin(angle)], axis=1)
    full = full.reshape(groups_y, peers, rows_ky, 2, groups_y, cells_y)
    out = np.zeros((groups_y, 2, cells_y, peers, 2, rows_ky, 2))
    for y in range(groups_y):
        for column in range(2):
            for peer in range(peers):
                for place in range(2):
                    half = y ^ place ^ column ^ (peer % 2)
                    out[y, column, :, peer, place] = np.moveaxis(full[half, peer, :, :, y], -1, 0)
    return out.reshape(groups_y, 2, cells_y, 4 * peers * rows_ky)


def output_table(table):
    high, low = split_table(table)
    parts = [high, high, low, np.ones(table.shape[:-1] + (BIAS_TERMS,), high.dtype)]
    used = 3 * table.shape[-1] + BIAS_TERMS
    parts.append(np.zeros(table.shape[:-1] + (-used % 256,), high.dtype))
    return np.concatenate(parts, axis=-1)


def dot(left, right):
    return jnp.dot(left, right, preferred_element_type=jnp.float32)


def column_of(turn, x, y):
    return x ^ y ^ (1 if turn == 0 else 0)


def forward_y_table(shape, extent, layers, rows_ky):
    z, x, y = quad()
    peers = 2 * layers
    row = lax.broadcasted_iota(jnp.int32, (shape[0], 1), 0)
    block = row // (2 * rows_ky)
    place = block // 2 % layers
    turn = jnp.where(place < layers // 2, place + layers // 2, layers - 1 - place)
    side = y ^ (1 - block // peers)
    column = x ^ side ^ jnp.where(turn == 0, 1, 0)
    owner = (side ^ (block % 2)) * peers + (z ^ turn) * 2 + column
    index = owner * rows_ky + row // 2 % rows_ky
    y_places = lax.broadcasted_iota(jnp.int32, (1, shape[1]), 1) + y * shape[1]
    steps = (wave_number(index, MY) * y_places) & (extent - 1)
    angle = 2.0 * math.pi / extent * steps.astype(jnp.float32)
    return jnp.where(row % 2 == 0, jnp.cos(angle), -jnp.sin(angle)).astype(jnp.bfloat16)


def forward_y_kernel(extent, rows_ky, flow_hbm, send_ref, keep_ref, flow_ref, arrived):
    layers, _, rows, feat_count = send_ref.shape
    cells_x, cells_y, _ = flow_ref.shape
    rows = rows // cells_x
    copies = [
        pltpu.make_async_copy(flow_hbm.at[x], flow_ref.at[x], arrived.at[x])
        for x in range(cells_x)
    ]
    for copy in copies:
        copy.start()
    table = forward_y_table((2 * MY, cells_y), extent, layers, rows_ky)
    for x in range(cells_x):
        copies[x].wait()
        result = dot(table, flow_ref[x]).reshape(2, layers, 2, rows, feat_count)
        send_ref[:, :, x * rows : (x + 1) * rows, :] = result[0]
        keep_ref[:, :, x * rows : (x + 1) * rows, :] = result[1]


def forward_y(flow_field, extent, layers, rows_ky):
    cells_x, _, feat_count = flow_field.shape
    shape = jax.ShapeDtypeStruct((layers, 2, cells_x * 2 * rows_ky, feat_count), jnp.float32)
    return pl.pallas_call(
        functools.partial(forward_y_kernel, extent, rows_ky),
        in_specs=[pl.BlockSpec(memory_space=pltpu.HBM)],
        out_shape=[shape] * 2,
        scratch_shapes=[
            pltpu.VMEM(flow_field.shape, flow_field.dtype),
            pltpu.SemaphoreType.DMA((cells_x,)),
        ],
        compiler_params=LARGE,
        name="forward_y",
    )(flow_field)


def flip_core(block):
    return lax.ppermute(block, "gy", [(0, 1), (1, 0)])


def along_columns(blocks, peers):
    arrived = []
    for turn, block in zip(turns(len(blocks)), blocks):
        pairs = [
            (2 * place + core, 2 * (place ^ (2 * turn + column_of(turn, 0, core))) + core)
            for place in range(peers)
            for core in range(2)
        ]
        arrived.append(lax.ppermute(block, ("gx", "gy"), pairs))
    return arrived


def small_call(kernel, out_shape, name):
    return pl.pallas_call(kernel, out_shape=out_shape, compiler_params=SMALL, name=name)


def second_kernel(*refs):
    for index, block_ref in enumerate(refs[:-1]):
        refs[-1][index] = block_ref[1]


def second_halves(blocks):
    shape = jax.ShapeDtypeStruct((len(blocks),) + blocks[0].shape[1:], blocks[0].dtype)
    return small_call(second_kernel, shape, "second_halves")(*blocks)


def stack_kernel(*refs):
    for index, block_ref in enumerate(refs[:-1]):
        refs[-1][index] = block_ref[...]


def stack_blocks(blocks):
    shape = jax.ShapeDtypeStruct((len(blocks),) + blocks[0].shape, blocks[0].dtype)
    return small_call(stack_kernel, shape, "stack_blocks")(*blocks)


def add_kernel(keep_ref, arrived_ref, *out_refs):
    for turn, out_ref in enumerate(out_refs):
        out_ref[...] = keep_ref[turn] + arrived_ref[turn]


def add_blocks(keep, arrived):
    shape = jax.ShapeDtypeStruct(keep.shape[1:], keep.dtype)
    return small_call(add_kernel, [shape] * keep.shape[0], "add_blocks")(keep, arrived)


def join_kernel(keep_ref, arrived_ref, *out_refs):
    cells_x, rows, _ = out_refs[0].shape
    rows = rows // 2
    for turn, out_ref in enumerate(out_refs):
        for cell in range(cells_x):
            span = slice(cell * rows, (cell + 1) * rows)
            out_ref[cell] = jnp.concatenate(
                [keep_ref[turn, span, :], arrived_ref[turn, span, :]], axis=0
            )


def join_blocks(keep, arrived, cells_x):
    layers, rows, feat_count = keep.shape
    shape = jax.ShapeDtypeStruct((cells_x, 2 * rows // cells_x, feat_count), keep.dtype)
    return small_call(join_kernel, [shape] * layers, "join_blocks")(keep, arrived)


def back_rows(inverse_high, inverse_low, modes, shape, other):
    z, x, y = quad()
    places = [(column_of(turn, x, y) ^ other, z ^ turn) for turn in turns(shape[0])]
    table_high, table_low = [
        jnp.concatenate([ref[column, place] for column, place in places], axis=0)
        for ref in (inverse_high, inverse_low)
    ]
    high, low = split_terms(modes)
    back = dot(table_high, high) + dot(table_high, low) + dot(table_low, high)
    return back.reshape(shape)


def mix_kernel(layers, *refs):
    block_refs, arrived_ref = refs[:layers], refs[layers]
    weight_ref, forward_high, forward_low, inverse_high, inverse_low = refs[
        layers + 1 : layers + 6
    ]
    modes_ref, send_ref, order_ref, spread_ref, result_ref = refs[layers + 6 :]
    z, x, y = quad()
    for index, turn in enumerate(turns(layers)):
        column = column_of(turn, x, y)
        order_ref[(z ^ turn) * 2 + column] = block_refs[index][0]
        order_ref[(z ^ turn) * 2 + (column ^ 1)] = arrived_ref[index]
    feat_count = order_ref.shape[-1]
    count = weight_ref.shape[1]
    channels = weight_ref.shape[2]
    tiles = feat_count // 128
    group = 2 * tiles
    high, low = split_terms(order_ref[...].reshape(-1, feat_count))
    spectrum = (
        dot(forward_high[...], high) + dot(forward_high[...], low) + dot(forward_low[...], high)
    )
    for part in range(2):
        for tile in range(tiles):
            spread_ref[pl.ds(part * tiles + tile, count, stride=group), :] = spectrum[
                part * count : (part + 1) * count, tile * 128 : (tile + 1) * 128
            ]
    rows = lax.broadcasted_iota(jnp.int32, (8, 128), 0) % group
    lane = lax.broadcasted_iota(jnp.int32, (8, 128), 1) < channels
    sign = jnp.where(rows < tiles, -1.0, 1.0)
    for base in range(0, count * group, 8):
        block = spread_ref[base : base + 8, :]
        turned = pltpu.roll(block, channels, 1)
        firsts, seconds = [], []
        for start in range(0, 8, group):
            span = slice(start, start + group)
            left = jnp.concatenate([block[span], turned[span]], axis=0)[:, :channels]
            left_high, left_low = split_terms(left)
            left = jnp.concatenate([left_high, left_low], axis=0)
            product = dot(left, weight_ref[0, (base + start) // group])
            product = product[: 2 * group] + product[2 * group :]
            firsts.append(product[:group])
            seconds.append(product[group:])
        first = jnp.concatenate(firsts, axis=0)
        second = jnp.concatenate(seconds, axis=0)
        real = jnp.where(lane, first, pltpu.roll(second, channels, 1))
        imag = jnp.where(lane, pltpu.roll(first, channels, 1), second)
        crossed = jnp.where(rows < tiles, pltpu.roll(imag, 8 - tiles, 0), pltpu.roll(imag, tiles, 0))
        result_ref[base : base + 8, :] = real + sign * crossed
    for part in range(2):
        for tile in range(tiles):
            modes_ref[part * count : (part + 1) * count, tile * 128 : (tile + 1) * 128] = (
                result_ref[pl.ds(part * tiles + tile, count, stride=group), :]
            )
    send_ref[...] = back_rows(inverse_high, inverse_low, modes_ref[...], send_ref.shape, 1)


def mix(blocks, arrived, weights, forward_table, inverse_tables):
    layers = len(blocks)
    _, rows, feat_count = blocks[0].shape
    count = weights.shape[1]
    scratch = pltpu.VMEM((count * feat_count // 64, 128), jnp.float32)
    return pl.pallas_call(
        functools.partial(mix_kernel, layers),
        out_shape=[
            jax.ShapeDtypeStruct((2 * count, feat_count), jnp.float32),
            jax.ShapeDtypeStruct((layers, rows, feat_count), jnp.float32),
        ],
        scratch_shapes=[pltpu.VMEM((2 * layers, rows, feat_count), jnp.float32), scratch, scratch],
        compiler_params=SMALL,
        name="mix",
    )(*blocks, arrived, weights, *split_table(forward_table), *inverse_tables)


def keep_kernel(modes_ref, inverse_high, inverse_low, mixed_ref, keep_ref):
    count = mixed_ref.shape[1]
    feat_count = modes_ref.shape[1]
    for part in range(2):
        mixed_ref[0, :, part * feat_count : (part + 1) * feat_count] = modes_ref[
            part * count : (part + 1) * count
        ]
    keep_ref[...] = back_rows(inverse_high, inverse_low, modes_ref[...], keep_ref.shape, 0)


def keep_rows(modes, inverse_tables, like):
    rows, feat_count = modes.shape
    return pl.pallas_call(
        keep_kernel,
        out_shape=[
            jax.ShapeDtypeStruct((1, rows // 2, 2 * feat_count), jnp.float32),
            jax.ShapeDtypeStruct(like.shape, jnp.float32),
        ],
        compiler_params=SMALL,
        name="keep_rows",
    )(modes, *inverse_tables)


def gelu(half):
    square = jnp.minimum(half * half, 6.25)
    inner = jnp.full_like(square, GELU_TERMS[-1])
    for term in GELU_TERMS[-2::-1]:
        inner = inner * square + term
    return half + half * jnp.tanh(half * inner)


def output_kernel(
    flow_ref, table_ref, local_ref, bias_ref, own_ref, core_ref,
    out_hbm, order_ref, wide_ref, level_ref, done_ref, sent,
):
    cells_x, cells_y, feat_count = flow_ref.shape
    channels = local_ref.shape[0]
    z, x, y = quad()
    wide_ref[...] = jnp.zeros_like(wide_ref)
    for start in range(0, WIDTH, channels):
        span = slice(start, start + channels)
        wide_ref[span, span] = local_ref[...] * 0.5
        level_ref[:, span] = bias_ref[...].reshape(1, channels) * 0.5
    level = level_ref[...]
    levels = []
    for _ in range(BIAS_TERMS):
        levels.append(level.astype(jnp.bfloat16).astype(jnp.float32))
        level = level - levels[-1]
    terms = 3 * order_ref.shape[1] * order_ref.shape[2]
    filled = jnp.zeros((table_ref.shape[-1] - terms - BIAS_TERMS, WIDTH), jnp.float32)
    below = jnp.concatenate(levels + [filled], axis=0).astype(jnp.bfloat16)
    below = jnp.concatenate([below, wide_ref[...]], axis=0)
    for index, turn in enumerate(turns(own_ref.shape[0])):
        column = column_of(turn, x, y)
        for peer, ref in ((column, own_ref), (column ^ 1, core_ref)):
            block = ref[index]
            if turn == 0:
                rows = block.shape[1] // 2
                block = jnp.concatenate([block[:, rows:], block[:, :rows]], axis=1)
            order_ref[:, (z ^ turn) * 2 + peer] = block
    table = table_ref[y, x ^ y]
    copies = []
    for cell in range(cells_x):
        high, low = split_terms(order_ref[cell].reshape(-1, feat_count))
        stack = jnp.concatenate([high, low, high], axis=0)
        bounds = [0, FIRST, cells_y] if cell == 0 else [0, cells_y]
        for begin, end in zip(bounds[:-1], bounds[1:]):
            rows = slice(begin, end)
            for start in range(0, feat_count, WIDTH):
                columns = slice(start, start + WIDTH)
                total = dot(
                    jnp.concatenate([table[rows], flow_ref[cell, rows, columns]], axis=1),
                    jnp.concatenate([stack[:, columns], below], axis=0),
                )
                done_ref[cell, rows, columns] = gelu(total).astype(done_ref.dtype)
            copies.append(
                pltpu.make_async_copy(
                    done_ref.at[cell, rows], out_hbm.at[cell, rows], sent.at[len(copies)]
                )
            )
            copies[-1].start()
    for copy in copies:
        copy.wait()


def make_output(flow_field, own, core, table, local, bias):
    cells_x, _, feat_count = flow_field.shape
    return pl.pallas_call(
        output_kernel,
        out_specs=pl.BlockSpec(memory_space=pl.ANY),
        scratch_shapes=[
            pltpu.VMEM((cells_x, 2 * own.shape[0]) + own.shape[2:], jnp.float32),
            pltpu.VMEM((WIDTH, WIDTH), jnp.bfloat16),
            pltpu.VMEM((1, WIDTH), jnp.float32),
            pltpu.VMEM(flow_field.shape, jnp.bfloat16),
            pltpu.SemaphoreType.DMA((cells_x + 1,)),
        ],
        out_shape=jax.ShapeDtypeStruct(flow_field.shape, jnp.bfloat16),
        compiler_params=SMALL,
        name="make_output",
    )(flow_field, table, local, bias, own, core)


def row_body(flow_field, spectral_weight, local_weight, bias_terms):
    cells_x, cells_y, feat_count = flow_field.shape
    peers = lax.axis_size("gx")
    groups_y = lax.axis_size("gy")
    rows_ky = MY // groups_y // peers
    forward_scale = 1.0 / math.sqrt(cells_x * peers * cells_y * groups_y)
    inverse_scale = 1.0 / math.sqrt(MX * MY)

    send, keep = forward_y(flow_field, cells_y * groups_y, peers // 2, rows_ky)
    blocks = along_columns(add_blocks(keep, flip_core(send)), peers)
    inverse_tables = split_table(inverse_x_table(cells_x, peers, rows_ky))
    modes, send = mix(
        blocks,
        flip_core(second_halves(blocks)),
        spectral_weight,
        forward_x_table(cells_x, peers, rows_ky) * forward_scale,
        inverse_tables,
    )
    arrived = flip_core(send)
    mixed, keep = keep_rows(modes, inverse_tables, send)
    own = along_columns(join_blocks(keep, arrived, cells_x), peers)
    own = stack_blocks(own)
    table = output_table(inverse_y_table(cells_y, groups_y, peers, rows_ky) * (0.5 * inverse_scale))
    return make_output(flow_field, own, flip_core(own), table, local_weight, bias_terms), mixed


def body(flow_field, spectral_weight, local_weight, bias_terms):
    peers = lax.axis_size("gx")
    extent = lax.axis_size("gy") * flow_field.shape[1]
    paired = lax.axis_size("gy") == 2 and peers & (peers - 1) == 0 and extent & (extent - 1) == 0
    if paired and spectral_weight.shape[1] == 2 * MX and WIDTH % local_weight.shape[0] == 0:
        return row_body(flow_field, spectral_weight, local_weight, bias_terms)
    return general_body(flow_field, spectral_weight, local_weight, bias_terms)


def solution(mesh):
    placed = (P(("group", "gx"), "gy", None), P("gy", "gx", None, None), P(), P())
    return jax.shard_map(
        body,
        mesh=mesh,
        in_specs=placed,
        out_specs=(P(("group", "gx"), "gy", None), P(("group", "gy"), "gx", None)),
        check_vma=False,
    )
```

```python
import functools
import math

import jax
import jax.numpy as jnp
import ml_dtypes
import numpy as np
from jax import lax
from jax.experimental import pallas as pl
from jax.experimental.pallas import tpu as pltpu
from jax.sharding import PartitionSpec as P

MX = 32
MY = 32


def wave_number(index, count):
    return jnp.where(index < count // 2, index, index - count)


def phase_table(waves, places, extent):
    product = waves[:, None] * places[None, :] % extent
    return 2.0 * math.pi / extent * product.astype(jnp.float32)


def row_tables(ky_rows, kx_rows, x_places, extent, width):
    angle = phase_table(wave_number(kx_rows, MX), x_places, extent)
    select = (ky_rows[:, None] == jnp.arange(width, dtype=jnp.int32)[None, :]).astype(jnp.float32)
    cosine = jnp.cos(angle)[:, :, None] * select[:, None, :]
    sine_part = jnp.sin(angle)[:, :, None] * select[:, None, :]
    return (cosine, sine_part)


def forward_rows(y_local, ky_rows, kx_rows, x_places, extent):
    cosine, sine_part = row_tables(ky_rows, kx_rows, x_places, extent, y_local.shape[0])
    real_in = y_local[:, 0]
    imag_in = y_local[:, 1]

    def contract(table, values):
        return jnp.einsum("rxk,kxf->rf", table, values, precision=lax.Precision.HIGHEST)

    real_out = contract(cosine, real_in) + contract(sine_part, imag_in)
    imag_out = contract(cosine, imag_in) - contract(sine_part, real_in)
    return jnp.concatenate([real_out, imag_out], axis=1)


def inverse_rows(running, shard_rows, ky_rows, kx_rows, x_places, extent):
    cosine, sine_part = row_tables(ky_rows, kx_rows, x_places, extent, running.shape[0])
    feat_count = shard_rows.shape[1] // 2
    real_part = shard_rows[:, :feat_count]
    imag_part = shard_rows[:, feat_count:]

    def contract(table, values):
        return jnp.einsum("rxk,rf->kxf", table, values, precision=lax.Precision.HIGHEST)

    new_real = contract(cosine, real_part) - contract(sine_part, imag_part)
    new_imag = contract(cosine, imag_part) + contract(sine_part, real_part)
    return jnp.stack([new_real, new_imag], axis=1)


def general_body(flow_field, spectral_weight, local_weight, bias_terms):
    cells_x, cells_y, feat_count = flow_field.shape
    channels = local_weight.shape[0]
    planes = feat_count // channels
    groups_x = lax.axis_size("gx")
    groups_y = lax.axis_size("gy")
    extent_x = cells_x * groups_x
    extent_y = cells_y * groups_y
    half_width = MY // groups_y
    quota_rows = spectral_weight.shape[1]
    high = lax.Precision.HIGHEST
    x_places = lax.axis_index("gx") * cells_x + jnp.arange(cells_x, dtype=jnp.int32)
    y_places = lax.axis_index("gy") * cells_y + jnp.arange(cells_y, dtype=jnp.int32)
    y_angle = phase_table(wave_number(jnp.arange(MY, dtype=jnp.int32), MY), y_places, extent_y)
    y_table = (
        jnp.stack([jnp.cos(y_angle), -jnp.sin(y_angle)], axis=1)
        .reshape(2 * MY, cells_y)
        .astype(jnp.bfloat16)
    )
    y_local = lax.psum_scatter(
        jnp.einsum("qy,xyf->qxf", y_table, flow_field, preferred_element_type=jnp.float32),
        "gy",
        scatter_dimension=0,
        tiled=True,
    )
    y_local = y_local.reshape(half_width, 2, cells_x, feat_count)
    rest_index = jnp.arange(lax.axis_size("gx") * quota_rows, dtype=jnp.int32)
    spectrum = lax.psum_scatter(
        forward_rows(y_local, rest_index // MX, rest_index % MX, x_places, extent_x),
        "gx",
        scatter_dimension=0,
        tiled=True,
    )
    spectrum = spectrum * (1.0 / math.sqrt(extent_x * extent_y))
    coeffs = spectrum.reshape(quota_rows, 2, planes, channels)
    weights = spectral_weight[0].astype(jnp.float32)
    product = jnp.einsum("rpzc,rco->rpzo", coeffs, weights, precision=high)
    mixed_real = product[:, 0, :, :channels] - product[:, 1, :, channels:]
    mixed_imag = product[:, 0, :, channels:] + product[:, 1, :, :channels]
    mixed_local = jnp.stack([mixed_real, mixed_imag], axis=1).reshape(quota_rows, 2 * feat_count)
    pointwise = jnp.einsum(
        "xyzc,co->xyzo",
        flow_field.reshape(cells_x, cells_y, planes, channels),
        local_weight,
        preferred_element_type=jnp.float32,
    )
    start_half = jnp.zeros((half_width, 2, cells_x, feat_count), jnp.float32)
    shard_rows = lax.all_gather(mixed_local, "gx", axis=0, tiled=True)
    rest_index = jnp.arange(shard_rows.shape[0], dtype=jnp.int32)
    back_half = inverse_rows(
        start_half, shard_rows, rest_index // MX, rest_index % MX, x_places, extent_x
    )
    back_whole = lax.all_gather(back_half, "gy", axis=0, tiled=True)
    y_cos = jnp.cos(y_angle)
    y_sin = jnp.sin(y_angle)
    spectral = (
        jnp.einsum("kn,kxf->xnf", y_cos, back_whole[:, 0], precision=high)
        - jnp.einsum("kn,kxf->xnf", y_sin, back_whole[:, 1], precision=high)
    ) * (1.0 / math.sqrt(MX * MY))
    total = spectral.reshape(cells_x, cells_y, planes, channels) + pointwise + bias_terms
    output = (
        jax.nn.gelu(total, approximate=False)
        .reshape(cells_x, cells_y, feat_count)
        .astype(jnp.bfloat16)
    )
    return (output, mixed_local.reshape(1, quota_rows, 2 * feat_count))


SMALL = pltpu.CompilerParams(vmem_limit_bytes=20 * 1024 * 1024)
LARGE = pltpu.CompilerParams(vmem_limit_bytes=53 * 1024 * 1024)
WIDTH = 256
BIAS_TERMS = 3
GELU_TERMS = (
    1.5957645177841187,
    0.29075613617897034,
    -0.0014313592109829187,
    -0.006452994421124458,
    0.0015898864949122071,
    -0.0001365363277727738,
)


def angles(count, places, extent):
    index = np.arange(count)
    waves = np.where(index < count // 2, index, index - count)
    product = (waves[:, None] * np.asarray(places)[None, :]) % extent
    return (np.float32(2.0 * math.pi / extent) * product.astype(np.float32)).astype(np.float64)


def split_table(table):
    high = table.astype(ml_dtypes.bfloat16)
    low = (table - high.astype(np.float64)).astype(ml_dtypes.bfloat16)
    return high, low


def split_terms(values):
    high = values.astype(jnp.bfloat16)
    low = (values - high.astype(jnp.float32)).astype(jnp.bfloat16)
    return high, low


def quad():
    place = lax.axis_index("gx")
    return place // 2, place % 2, lax.axis_index("gy")


def turns(layers):
    return list(range(1, layers)) + [0]


def forward_x_table(cells_x, peers, rows_ky):
    extent = cells_x * peers
    angle = angles(MX, np.arange(extent), extent)
    cosine, sine = np.cos(angle), np.sin(angle)
    out = np.zeros((2, rows_ky, MX, extent, rows_ky, 2))
    for row in range(rows_ky):
        out[0, row, :, :, row, 0] = cosine
        out[0, row, :, :, row, 1] = sine
        out[1, row, :, :, row, 1] = cosine
        out[1, row, :, :, row, 0] = -sine
    return out.reshape(2 * rows_ky * MX, extent * rows_ky * 2)


def inverse_x_table(cells_x, peers, rows_ky):
    extent = cells_x * peers
    angle = angles(MX, np.arange(extent), extent)
    cosine, sine = np.cos(angle).T, np.sin(angle).T
    out = np.zeros((extent, rows_ky, 2, 2, rows_ky, MX))
    for row in range(rows_ky):
        out[:, row, 0, 0, row, :] = cosine
        out[:, row, 0, 1, row, :] = -sine
        out[:, row, 1, 1, row, :] = cosine
        out[:, row, 1, 0, row, :] = sine
    out = out.reshape(peers // 2, 2, cells_x * rows_ky * 2, 2 * rows_ky * MX)
    return np.moveaxis(out, 1, 0).reshape(2, -1, 2 * rows_ky * MX)


def inverse_y_table(cells_y, groups_y, peers, rows_ky):
    extent = cells_y * groups_y
    angle = angles(MY, np.arange(extent), extent)
    full = np.stack([np.cos(angle), -np.sin(angle)], axis=1)
    full = full.reshape(groups_y, peers, rows_ky, 2, groups_y, cells_y)
    out = np.zeros((groups_y, 2, cells_y, peers, 2, rows_ky, 2))
    for y in range(groups_y):
        for column in range(2):
            for peer in range(peers):
                for place in range(2):
                    half = y ^ place ^ column ^ (peer % 2)
                    out[y, column, :, peer, place] = np.moveaxis(full[half, peer, :, :, y], -1, 0)
    return out.reshape(groups_y, 2, cells_y, 4 * peers * rows_ky)


def output_table(table):
    high, low = split_table(table)
    parts = [high, high, low, np.ones(table.shape[:-1] + (BIAS_TERMS,), high.dtype)]
    used = 3 * table.shape[-1] + BIAS_TERMS
    parts.append(np.zeros(table.shape[:-1] + (-used % 256,), high.dtype))
    return np.concatenate(parts, axis=-1)


def dot(left, right):
    return jnp.dot(left, right, preferred_element_type=jnp.float32)


def forward_y_table(shape, extent, layers, rows_ky):
    z, x, y = quad()
    peers = 2 * layers
    row = lax.broadcasted_iota(jnp.int32, (shape[0], 1), 0)
    block = row // (2 * rows_ky)
    place = block // 2 % layers
    turn = (place + 1) % layers
    side = y ^ (1 - block // peers)
    owner = (side ^ (block % 2)) * peers + (z ^ turn) * 2 + (x ^ side)
    index = owner * rows_ky + row // 2 % rows_ky
    y_places = lax.broadcasted_iota(jnp.int32, (1, shape[1]), 1) + y * shape[1]
    steps = (wave_number(index, MY) * y_places) & (extent - 1)
    angle = 2.0 * math.pi / extent * steps.astype(jnp.float32)
    return jnp.where(row % 2 == 0, jnp.cos(angle), -jnp.sin(angle)).astype(jnp.bfloat16)


def forward_y_kernel(extent, rows_ky, flow_hbm, send_ref, keep_ref, flow_ref, arrived):
    layers, _, rows, feat_count = send_ref.shape
    cells_x, cells_y, _ = flow_ref.shape
    rows = rows // cells_x
    copies = [
        pltpu.make_async_copy(flow_hbm.at[x], flow_ref.at[x], arrived.at[x])
        for x in range(cells_x)
    ]
    for copy in copies:
        copy.start()
    table = forward_y_table((2 * MY, cells_y), extent, layers, rows_ky)
    for x in range(cells_x):
        copies[x].wait()
        result = dot(table, flow_ref[x]).reshape(2, layers, 2, rows, feat_count)
        send_ref[:, :, x * rows : (x + 1) * rows, :] = result[0]
        keep_ref[:, :, x * rows : (x + 1) * rows, :] = result[1]


def forward_y(flow_field, extent, layers, rows_ky):
    cells_x, _, feat_count = flow_field.shape
    shape = jax.ShapeDtypeStruct((layers, 2, cells_x * 2 * rows_ky, feat_count), jnp.float32)
    return pl.pallas_call(
        functools.partial(forward_y_kernel, extent, rows_ky),
        in_specs=[pl.BlockSpec(memory_space=pltpu.HBM)],
        out_shape=[shape] * 2,
        scratch_shapes=[
            pltpu.VMEM(flow_field.shape, flow_field.dtype),
            pltpu.SemaphoreType.DMA((cells_x,)),
        ],
        compiler_params=LARGE,
        name="forward_y",
    )(flow_field)


def flip_core(block):
    return lax.ppermute(block, "gy", [(0, 1), (1, 0)])


def along_columns(blocks, peers):
    arrived = []
    for turn, block in zip(turns(len(blocks)), blocks):
        pairs = [
            (2 * place + core, 2 * (place ^ (2 * turn + core)) + core)
            for place in range(peers)
            for core in range(2)
        ]
        arrived.append(lax.ppermute(block, ("gx", "gy"), pairs))
    return arrived


def small_call(kernel, out_shape, name):
    return pl.pallas_call(kernel, out_shape=out_shape, compiler_params=SMALL, name=name)


def second_kernel(block_ref, out_ref):
    out_ref[...] = block_ref[1]


def second_half(block):
    shape = jax.ShapeDtypeStruct(block.shape[1:], block.dtype)
    return small_call(second_kernel, shape, "second_half")(block)


def add_kernel(keep_ref, arrived_ref, *out_refs):
    for turn, out_ref in enumerate(out_refs):
        out_ref[...] = keep_ref[turn] + arrived_ref[turn]


def add_blocks(keep, arrived):
    shape = jax.ShapeDtypeStruct(keep.shape[1:], keep.dtype)
    return small_call(add_kernel, [shape] * keep.shape[0], "add_blocks")(keep, arrived)


def join_kernel(keep_ref, arrived_ref, *out_refs):
    cells_x, rows, _ = out_refs[0].shape
    rows = rows // 2
    for turn, out_ref in enumerate(out_refs):
        for cell in range(cells_x):
            span = slice(cell * rows, (cell + 1) * rows)
            out_ref[cell] = jnp.concatenate(
                [keep_ref[turn, span, :], arrived_ref[turn, span, :]], axis=0
            )


def join_blocks(keep, arrived, cells_x):
    layers, rows, feat_count = keep.shape
    shape = jax.ShapeDtypeStruct((cells_x, 2 * rows // cells_x, feat_count), keep.dtype)
    return small_call(join_kernel, [shape] * layers, "join_blocks")(keep, arrived)


def back_rows(inverse_high, inverse_low, column, modes):
    high, low = split_terms(modes)
    table = inverse_high[column]
    return dot(table, high) + dot(table, low) + dot(inverse_low[column], high)


def store_turns(out_ref, order_ref, z):
    for index, turn in enumerate(turns(out_ref.shape[0])):
        out_ref[index] = order_ref[z ^ turn]


def mix_kernel(layers, *refs):
    block_refs, arrived_refs = refs[:layers], refs[layers : 2 * layers]
    weight_ref, forward_high, forward_low, inverse_high, inverse_low = refs[
        2 * layers : 2 * layers + 5
    ]
    modes_ref, send_ref, order_ref, spread_ref, result_ref = refs[2 * layers + 5 :]
    z, x, y = quad()
    column = x ^ y
    for index, turn in enumerate(turns(layers)):
        order_ref[(z ^ turn) * 2 + column] = block_refs[index][0]
        order_ref[(z ^ turn) * 2 + (column ^ 1)] = arrived_refs[index][...]
    feat_count = order_ref.shape[-1]
    count = weight_ref.shape[1]
    channels = weight_ref.shape[2]
    tiles = feat_count // 128
    group = 2 * tiles
    high, low = split_terms(order_ref[...].reshape(-1, feat_count))
    spectrum = (
        dot(forward_high[...], high) + dot(forward_high[...], low) + dot(forward_low[...], high)
    )
    for part in range(2):
        for tile in range(tiles):
            spread_ref[pl.ds(part * tiles + tile, count, stride=group), :] = spectrum[
                part * count : (part + 1) * count, tile * 128 : (tile + 1) * 128
            ]
    rows = lax.broadcasted_iota(jnp.int32, (8, 128), 0) % group
    lane = lax.broadcasted_iota(jnp.int32, (8, 128), 1) < channels
    sign = jnp.where(rows < tiles, -1.0, 1.0)
    for base in range(0, count * group, 8):
        block = spread_ref[base : base + 8, :]
        turned = pltpu.roll(block, channels, 1)
        firsts, seconds = [], []
        for start in range(0, 8, group):
            span = slice(start, start + group)
            left = jnp.concatenate([block[span], turned[span]], axis=0)[:, :channels]
            left_high, left_low = split_terms(left)
            left = jnp.concatenate([left_high, left_low], axis=0)
            product = dot(left, weight_ref[0, (base + start) // group])
            product = product[: 2 * group] + product[2 * group :]
            firsts.append(product[:group])
            seconds.append(product[group:])
        first = jnp.concatenate(firsts, axis=0)
        second = jnp.concatenate(seconds, axis=0)
        real = jnp.where(lane, first, pltpu.roll(second, channels, 1))
        imag = jnp.where(lane, pltpu.roll(first, channels, 1), second)
        crossed = jnp.where(rows < tiles, pltpu.roll(imag, 8 - tiles, 0), pltpu.roll(imag, tiles, 0))
        result_ref[base : base + 8, :] = real + sign * crossed
    for part in range(2):
        for tile in range(tiles):
            modes_ref[part * count : (part + 1) * count, tile * 128 : (tile + 1) * 128] = (
                result_ref[pl.ds(part * tiles + tile, count, stride=group), :]
            )
    back = back_rows(inverse_high, inverse_low, column ^ 1, modes_ref[...])
    order_ref[:layers] = back.reshape(send_ref.shape)
    store_turns(send_ref, order_ref, z)


def mix(blocks, arrived, weights, forward_table, inverse_tables):
    layers = len(blocks)
    _, rows, feat_count = blocks[0].shape
    count = weights.shape[1]
    scratch = pltpu.VMEM((count * feat_count // 64, 128), jnp.float32)
    return pl.pallas_call(
        functools.partial(mix_kernel, layers),
        out_shape=[
            jax.ShapeDtypeStruct((2 * count, feat_count), jnp.float32),
            jax.ShapeDtypeStruct((layers, rows, feat_count), jnp.float32),
        ],
        scratch_shapes=[pltpu.VMEM((2 * layers, rows, feat_count), jnp.float32), scratch, scratch],
        compiler_params=SMALL,
        name="mix",
    )(*blocks, *arrived, weights, *split_table(forward_table), *inverse_tables)


def keep_kernel(modes_ref, inverse_high, inverse_low, mixed_ref, keep_ref, order_ref):
    z, x, y = quad()
    count = mixed_ref.shape[1]
    feat_count = modes_ref.shape[1]
    for part in range(2):
        mixed_ref[0, :, part * feat_count : (part + 1) * feat_count] = modes_ref[
            part * count : (part + 1) * count
        ]
    back = back_rows(inverse_high, inverse_low, x ^ y, modes_ref[...])
    order_ref[...] = back.reshape(keep_ref.shape)
    store_turns(keep_ref, order_ref, z)


def keep_rows(modes, inverse_tables, like):
    rows, feat_count = modes.shape
    return pl.pallas_call(
        keep_kernel,
        out_shape=[
            jax.ShapeDtypeStruct((1, rows // 2, 2 * feat_count), jnp.float32),
            jax.ShapeDtypeStruct(like.shape, jnp.float32),
        ],
        scratch_shapes=[pltpu.VMEM(like.shape, jnp.float32)],
        compiler_params=SMALL,
        name="keep_rows",
    )(modes, *inverse_tables)


def gelu(half):
    square = jnp.minimum(half * half, 6.25)
    inner = jnp.full_like(square, GELU_TERMS[-1])
    for term in GELU_TERMS[-2::-1]:
        inner = inner * square + term
    return half + half * jnp.tanh(half * inner)


def output_kernel(layers, flow_ref, table_ref, local_ref, bias_ref, *refs):
    own_refs, core_refs = refs[:layers], refs[layers : 2 * layers]
    out_hbm, order_ref, wide_ref, level_ref, done_ref, sent = refs[2 * layers :]
    cells_x, _, feat_count = flow_ref.shape
    channels = local_ref.shape[0]
    z, x, y = quad()
    wide_ref[...] = jnp.zeros_like(wide_ref)
    for start in range(0, WIDTH, channels):
        span = slice(start, start + channels)
        wide_ref[span, span] = local_ref[...] * 0.5
        level_ref[:, span] = bias_ref[...].reshape(1, channels) * 0.5
    level = level_ref[...]
    levels = []
    for _ in range(BIAS_TERMS):
        levels.append(level.astype(jnp.bfloat16).astype(jnp.float32))
        level = level - levels[-1]
    terms = 3 * order_ref.shape[1] * order_ref.shape[2]
    filled = jnp.zeros((table_ref.shape[-1] - terms - BIAS_TERMS, WIDTH), jnp.float32)
    below = jnp.concatenate(levels + [filled], axis=0).astype(jnp.bfloat16)
    below = jnp.concatenate([below, wide_ref[...]], axis=0)
    for column, block_refs in ((x ^ y, own_refs), (x ^ y ^ 1, core_refs)):
        for turn, block_ref in zip(turns(layers), block_refs):
            order_ref[:, (z ^ turn) * 2 + column] = block_ref[...]
    table = table_ref[y, x ^ y]
    copies = []
    for cell in range(cells_x):
        high, low = split_terms(order_ref[cell].reshape(-1, feat_count))
        stack = jnp.concatenate([high, low, high], axis=0)
        for start in range(0, feat_count, WIDTH):
            columns = slice(start, start + WIDTH)
            total = dot(
                jnp.concatenate([table, flow_ref[cell, :, columns]], axis=1),
                jnp.concatenate([stack[:, columns], below], axis=0),
            )
            done_ref[cell, :, columns] = gelu(total).astype(done_ref.dtype)
        copies.append(pltpu.make_async_copy(done_ref.at[cell], out_hbm.at[cell], sent.at[cell]))
        copies[-1].start()
    for copy in copies:
        copy.wait()


def make_output(flow_field, parts, table, local, bias):
    cells_x, _, feat_count = flow_field.shape
    layers = len(parts) // 2
    return pl.pallas_call(
        functools.partial(output_kernel, layers),
        out_specs=pl.BlockSpec(memory_space=pl.ANY),
        scratch_shapes=[
            pltpu.VMEM((cells_x, 2 * layers) + parts[0].shape[1:], jnp.float32),
            pltpu.VMEM((WIDTH, WIDTH), jnp.bfloat16),
            pltpu.VMEM((1, WIDTH), jnp.float32),
            pltpu.VMEM(flow_field.shape, jnp.bfloat16),
            pltpu.SemaphoreType.DMA((cells_x,)),
        ],
        out_shape=jax.ShapeDtypeStruct(flow_field.shape, jnp.bfloat16),
        compiler_params=SMALL,
        name="make_output",
    )(flow_field, table, local, bias, *parts)


def row_body(flow_field, spectral_weight, local_weight, bias_terms):
    cells_x, cells_y, feat_count = flow_field.shape
    peers = lax.axis_size("gx")
    groups_y = lax.axis_size("gy")
    rows_ky = MY // groups_y // peers
    forward_scale = 1.0 / math.sqrt(cells_x * peers * cells_y * groups_y)
    inverse_scale = 1.0 / math.sqrt(MX * MY)

    send, keep = forward_y(flow_field, cells_y * groups_y, peers // 2, rows_ky)
    blocks = along_columns(add_blocks(keep, flip_core(send)), peers)
    inverse_tables = split_table(inverse_x_table(cells_x, peers, rows_ky))
    modes, send = mix(
        blocks,
        [flip_core(second_half(block)) for block in blocks],
        spectral_weight,
        forward_x_table(cells_x, peers, rows_ky) * forward_scale,
        inverse_tables,
    )
    arrived = flip_core(send)
    mixed, keep = keep_rows(modes, inverse_tables, send)
    own = along_columns(join_blocks(keep, arrived, cells_x), peers)
    parts = own + [flip_core(block) for block in own]
    table = output_table(inverse_y_table(cells_y, groups_y, peers, rows_ky) * (0.5 * inverse_scale))
    return make_output(flow_field, parts, table, local_weight, bias_terms), mixed


def body(flow_field, spectral_weight, local_weight, bias_terms):
    peers = lax.axis_size("gx")
    extent = lax.axis_size("gy") * flow_field.shape[1]
    paired = lax.axis_size("gy") == 2 and peers & (peers - 1) == 0 and extent & (extent - 1) == 0
    if paired and spectral_weight.shape[1] == 2 * MX and WIDTH % local_weight.shape[0] == 0:
        return row_body(flow_field, spectral_weight, local_weight, bias_terms)
    return general_body(flow_field, spectral_weight, local_weight, bias_terms)


def solution(mesh):
    placed = (P(("group", "gx"), "gy", None), P("gy", "gx", None, None), P(), P())
    return jax.shard_map(
        body,
        mesh=mesh,
        in_specs=placed,
        out_specs=(P(("group", "gx"), "gy", None), P(("group", "gy"), "gx", None)),
        check_vma=False,
    )
```

```python
import functools
import math

import jax
import jax.numpy as jnp
import ml_dtypes
import numpy as np
from jax import lax
from jax.experimental import pallas as pl
from jax.experimental.pallas import tpu as pltpu
from jax.sharding import PartitionSpec as P

MX = 32
MY = 32


def wave_number(index, count):
    return jnp.where(index < count // 2, index, index - count)


def phase_table(waves, places, extent):
    product = waves[:, None] * places[None, :] % extent
    return 2.0 * math.pi / extent * product.astype(jnp.float32)


def row_tables(ky_rows, kx_rows, x_places, extent, width):
    angle = phase_table(wave_number(kx_rows, MX), x_places, extent)
    select = (ky_rows[:, None] == jnp.arange(width, dtype=jnp.int32)[None, :]).astype(jnp.float32)
    cosine = jnp.cos(angle)[:, :, None] * select[:, None, :]
    sine_part = jnp.sin(angle)[:, :, None] * select[:, None, :]
    return (cosine, sine_part)


def forward_rows(y_local, ky_rows, kx_rows, x_places, extent):
    cosine, sine_part = row_tables(ky_rows, kx_rows, x_places, extent, y_local.shape[0])
    real_in = y_local[:, 0]
    imag_in = y_local[:, 1]

    def contract(table, values):
        return jnp.einsum("rxk,kxf->rf", table, values, precision=lax.Precision.HIGHEST)

    real_out = contract(cosine, real_in) + contract(sine_part, imag_in)
    imag_out = contract(cosine, imag_in) - contract(sine_part, real_in)
    return jnp.concatenate([real_out, imag_out], axis=1)


def inverse_rows(running, shard_rows, ky_rows, kx_rows, x_places, extent):
    cosine, sine_part = row_tables(ky_rows, kx_rows, x_places, extent, running.shape[0])
    feat_count = shard_rows.shape[1] // 2
    real_part = shard_rows[:, :feat_count]
    imag_part = shard_rows[:, feat_count:]

    def contract(table, values):
        return jnp.einsum("rxk,rf->kxf", table, values, precision=lax.Precision.HIGHEST)

    new_real = contract(cosine, real_part) - contract(sine_part, imag_part)
    new_imag = contract(cosine, imag_part) + contract(sine_part, real_part)
    return jnp.stack([new_real, new_imag], axis=1)


def general_body(flow_field, spectral_weight, local_weight, bias_terms):
    cells_x, cells_y, feat_count = flow_field.shape
    channels = local_weight.shape[0]
    planes = feat_count // channels
    groups_x = lax.axis_size("gx")
    groups_y = lax.axis_size("gy")
    extent_x = cells_x * groups_x
    extent_y = cells_y * groups_y
    half_width = MY // groups_y
    quota_rows = spectral_weight.shape[1]
    high = lax.Precision.HIGHEST
    x_places = lax.axis_index("gx") * cells_x + jnp.arange(cells_x, dtype=jnp.int32)
    y_places = lax.axis_index("gy") * cells_y + jnp.arange(cells_y, dtype=jnp.int32)
    y_angle = phase_table(wave_number(jnp.arange(MY, dtype=jnp.int32), MY), y_places, extent_y)
    y_table = (
        jnp.stack([jnp.cos(y_angle), -jnp.sin(y_angle)], axis=1)
        .reshape(2 * MY, cells_y)
        .astype(jnp.bfloat16)
    )
    y_local = lax.psum_scatter(
        jnp.einsum("qy,xyf->qxf", y_table, flow_field, preferred_element_type=jnp.float32),
        "gy",
        scatter_dimension=0,
        tiled=True,
    )
    y_local = y_local.reshape(half_width, 2, cells_x, feat_count)
    rest_index = jnp.arange(lax.axis_size("gx") * quota_rows, dtype=jnp.int32)
    spectrum = lax.psum_scatter(
        forward_rows(y_local, rest_index // MX, rest_index % MX, x_places, extent_x),
        "gx",
        scatter_dimension=0,
        tiled=True,
    )
    spectrum = spectrum * (1.0 / math.sqrt(extent_x * extent_y))
    coeffs = spectrum.reshape(quota_rows, 2, planes, channels)
    weights = spectral_weight[0].astype(jnp.float32)
    product = jnp.einsum("rpzc,rco->rpzo", coeffs, weights, precision=high)
    mixed_real = product[:, 0, :, :channels] - product[:, 1, :, channels:]
    mixed_imag = product[:, 0, :, channels:] + product[:, 1, :, :channels]
    mixed_local = jnp.stack([mixed_real, mixed_imag], axis=1).reshape(quota_rows, 2 * feat_count)
    pointwise = jnp.einsum(
        "xyzc,co->xyzo",
        flow_field.reshape(cells_x, cells_y, planes, channels),
        local_weight,
        preferred_element_type=jnp.float32,
    )
    start_half = jnp.zeros((half_width, 2, cells_x, feat_count), jnp.float32)
    shard_rows = lax.all_gather(mixed_local, "gx", axis=0, tiled=True)
    rest_index = jnp.arange(shard_rows.shape[0], dtype=jnp.int32)
    back_half = inverse_rows(
        start_half, shard_rows, rest_index // MX, rest_index % MX, x_places, extent_x
    )
    back_whole = lax.all_gather(back_half, "gy", axis=0, tiled=True)
    y_cos = jnp.cos(y_angle)
    y_sin = jnp.sin(y_angle)
    spectral = (
        jnp.einsum("kn,kxf->xnf", y_cos, back_whole[:, 0], precision=high)
        - jnp.einsum("kn,kxf->xnf", y_sin, back_whole[:, 1], precision=high)
    ) * (1.0 / math.sqrt(MX * MY))
    total = spectral.reshape(cells_x, cells_y, planes, channels) + pointwise + bias_terms
    output = (
        jax.nn.gelu(total, approximate=False)
        .reshape(cells_x, cells_y, feat_count)
        .astype(jnp.bfloat16)
    )
    return (output, mixed_local.reshape(1, quota_rows, 2 * feat_count))


SMALL = pltpu.CompilerParams(vmem_limit_bytes=20 * 1024 * 1024)
LARGE = pltpu.CompilerParams(vmem_limit_bytes=53 * 1024 * 1024)
WIDTH = 256
BIAS_TERMS = 3
GELU_TERMS = (
    1.5957645177841187,
    0.29075613617897034,
    -0.0014313592109829187,
    -0.006452994421124458,
    0.0015898864949122071,
    -0.0001365363277727738,
)


def angles(count, places, extent):
    index = np.arange(count)
    waves = np.where(index < count // 2, index, index - count)
    product = (waves[:, None] * np.asarray(places)[None, :]) % extent
    return (np.float32(2.0 * math.pi / extent) * product.astype(np.float32)).astype(np.float64)


def split_table(table):
    high = table.astype(ml_dtypes.bfloat16)
    low = (table - high.astype(np.float64)).astype(ml_dtypes.bfloat16)
    return high, low


def split_terms(values):
    high = values.astype(jnp.bfloat16)
    low = (values - high.astype(jnp.float32)).astype(jnp.bfloat16)
    return high, low


def quad():
    place = lax.axis_index("gx")
    return place // 2, place % 2, lax.axis_index("gy")


def turns(layers):
    return list(range(layers - 1, -1, -1))


def forward_x_table(cells_x, peers, rows_ky):
    extent = cells_x * peers
    angle = angles(MX, np.arange(extent), extent)
    cosine, sine = np.cos(angle), np.sin(angle)
    out = np.zeros((2, rows_ky, MX, extent, rows_ky, 2))
    for row in range(rows_ky):
        out[0, row, :, :, row, 0] = cosine
        out[0, row, :, :, row, 1] = sine
        out[1, row, :, :, row, 1] = cosine
        out[1, row, :, :, row, 0] = -sine
    return out.reshape(2 * rows_ky * MX, extent * rows_ky * 2)


def inverse_x_table(cells_x, peers, rows_ky):
    extent = cells_x * peers
    angle = angles(MX, np.arange(extent), extent)
    cosine, sine = np.cos(angle).T, np.sin(angle).T
    out = np.zeros((extent, rows_ky, 2, 2, rows_ky, MX))
    for row in range(rows_ky):
        out[:, row, 0, 0, row, :] = cosine
        out[:, row, 0, 1, row, :] = -sine
        out[:, row, 1, 1, row, :] = cosine
        out[:, row, 1, 0, row, :] = sine
    out = out.reshape(peers // 2, 2, cells_x * rows_ky * 2, 2 * rows_ky * MX)
    return np.moveaxis(out, 1, 0).reshape(2, -1, 2 * rows_ky * MX)


def inverse_y_table(cells_y, groups_y, peers, rows_ky):
    extent = cells_y * groups_y
    angle = angles(MY, np.arange(extent), extent)
    full = np.stack([np.cos(angle), -np.sin(angle)], axis=1)
    full = full.reshape(groups_y, peers, rows_ky, 2, groups_y, cells_y)
    out = np.zeros((groups_y, 2, cells_y, peers, 2, rows_ky, 2))
    for y in range(groups_y):
        for column in range(2):
            for peer in range(peers):
                for place in range(2):
                    half = y ^ place ^ column ^ (peer % 2)
                    out[y, column, :, peer, place] = np.moveaxis(full[half, peer, :, :, y], -1, 0)
    return out.reshape(groups_y, 2, cells_y, 4 * peers * rows_ky)


def output_table(table):
    high, low = split_table(table)
    parts = [high, high, low, np.ones(table.shape[:-1] + (BIAS_TERMS,), high.dtype)]
    used = 3 * table.shape[-1] + BIAS_TERMS
    parts.append(np.zeros(table.shape[:-1] + (-used % 256,), high.dtype))
    return np.concatenate(parts, axis=-1)


def dot(left, right):
    return jnp.dot(left, right, preferred_element_type=jnp.float32)


def forward_y_table(shape, extent, layers, rows_ky):
    z, x, y = quad()
    peers = 2 * layers
    row = lax.broadcasted_iota(jnp.int32, (shape[0], 1), 0)
    block = row // (2 * rows_ky)
    place = block // 2 % layers
    turn = layers - 1 - place
    side = y ^ (1 - block // peers)
    owner = (side ^ (block % 2)) * peers + (z ^ turn) * 2 + (x ^ side)
    index = owner * rows_ky + row // 2 % rows_ky
    y_places = lax.broadcasted_iota(jnp.int32, (1, shape[1]), 1) + y * shape[1]
    steps = (wave_number(index, MY) * y_places) & (extent - 1)
    angle = 2.0 * math.pi / extent * steps.astype(jnp.float32)
    return jnp.where(row % 2 == 0, jnp.cos(angle), -jnp.sin(angle)).astype(jnp.bfloat16)


def forward_y_kernel(extent, rows_ky, flow_hbm, send_ref, keep_ref, flow_ref, arrived):
    layers, _, rows, feat_count = send_ref.shape
    cells_x, cells_y, _ = flow_ref.shape
    rows = rows // cells_x
    copies = [
        pltpu.make_async_copy(flow_hbm.at[x], flow_ref.at[x], arrived.at[x])
        for x in range(cells_x)
    ]
    for copy in copies:
        copy.start()
    table = forward_y_table((2 * MY, cells_y), extent, layers, rows_ky)
    for x in range(cells_x):
        copies[x].wait()
        result = dot(table, flow_ref[x]).reshape(2, layers, 2, rows, feat_count)
        send_ref[:, :, x * rows : (x + 1) * rows, :] = result[0]
        keep_ref[:, :, x * rows : (x + 1) * rows, :] = result[1]


def forward_y(flow_field, extent, layers, rows_ky):
    cells_x, _, feat_count = flow_field.shape
    shape = jax.ShapeDtypeStruct((layers, 2, cells_x * 2 * rows_ky, feat_count), jnp.float32)
    return pl.pallas_call(
        functools.partial(forward_y_kernel, extent, rows_ky),
        in_specs=[pl.BlockSpec(memory_space=pltpu.HBM)],
        out_shape=[shape] * 2,
        scratch_shapes=[
            pltpu.VMEM(flow_field.shape, flow_field.dtype),
            pltpu.SemaphoreType.DMA((cells_x,)),
        ],
        compiler_params=LARGE,
        name="forward_y",
    )(flow_field)


def flip_core(block):
    return lax.ppermute(block, "gy", [(0, 1), (1, 0)])


def along_columns(blocks, peers):
    arrived = []
    for turn, block in zip(turns(len(blocks)), blocks):
        pairs = [
            (2 * place + core, 2 * (place ^ (2 * turn + core)) + core)
            for place in range(peers)
            for core in range(2)
        ]
        arrived.append(lax.ppermute(block, ("gx", "gy"), pairs))
    return arrived


def small_call(kernel, out_shape, name):
    return pl.pallas_call(kernel, out_shape=out_shape, compiler_params=SMALL, name=name)


def second_kernel(block_ref, out_ref):
    out_ref[...] = block_ref[1]


def second_half(block):
    shape = jax.ShapeDtypeStruct(block.shape[1:], block.dtype)
    return small_call(second_kernel, shape, "second_half")(block)


def add_kernel(keep_ref, arrived_ref, *out_refs):
    for turn, out_ref in enumerate(out_refs):
        out_ref[...] = keep_ref[turn] + arrived_ref[turn]


def add_blocks(keep, arrived):
    shape = jax.ShapeDtypeStruct(keep.shape[1:], keep.dtype)
    return small_call(add_kernel, [shape] * keep.shape[0], "add_blocks")(keep, arrived)


def join_kernel(keep_ref, arrived_ref, *out_refs):
    cells_x, rows, _ = out_refs[0].shape
    rows = rows // 2
    for turn, out_ref in enumerate(out_refs):
        for cell in range(cells_x):
            span = slice(cell * rows, (cell + 1) * rows)
            out_ref[cell] = jnp.concatenate(
                [keep_ref[turn, span, :], arrived_ref[turn, span, :]], axis=0
            )


def join_blocks(keep, arrived, cells_x):
    layers, rows, feat_count = keep.shape
    shape = jax.ShapeDtypeStruct((cells_x, 2 * rows // cells_x, feat_count), keep.dtype)
    return small_call(join_kernel, [shape] * layers, "join_blocks")(keep, arrived)


def back_rows(inverse_high, inverse_low, column, modes):
    high, low = split_terms(modes)
    table = inverse_high[column]
    return dot(table, high) + dot(table, low) + dot(inverse_low[column], high)


def store_turns(out_ref, order_ref, z):
    for index, turn in enumerate(turns(out_ref.shape[0])):
        out_ref[index] = order_ref[z ^ turn]


def mix_kernel(layers, *refs):
    block_refs, arrived_refs = refs[:layers], refs[layers : 2 * layers]
    weight_ref, forward_high, forward_low, inverse_high, inverse_low = refs[
        2 * layers : 2 * layers + 5
    ]
    modes_ref, send_ref, order_ref, spread_ref, result_ref = refs[2 * layers + 5 :]
    z, x, y = quad()
    column = x ^ y
    for index, turn in enumerate(turns(layers)):
        order_ref[(z ^ turn) * 2 + column] = block_refs[index][0]
        order_ref[(z ^ turn) * 2 + (column ^ 1)] = arrived_refs[index][...]
    feat_count = order_ref.shape[-1]
    count = weight_ref.shape[1]
    channels = weight_ref.shape[2]
    tiles = feat_count // 128
    group = 2 * tiles
    high, low = split_terms(order_ref[...].reshape(-1, feat_count))
    spectrum = (
        dot(forward_high[...], high) + dot(forward_high[...], low) + dot(forward_low[...], high)
    )
    for part in range(2):
        for tile in range(tiles):
            spread_ref[pl.ds(part * tiles + tile, count, stride=group), :] = spectrum[
                part * count : (part + 1) * count, tile * 128 : (tile + 1) * 128
            ]
    rows = lax.broadcasted_iota(jnp.int32, (8, 128), 0) % group
    lane = lax.broadcasted_iota(jnp.int32, (8, 128), 1) < channels
    sign = jnp.where(rows < tiles, -1.0, 1.0)
    for base in range(0, count * group, 8):
        block = spread_ref[base : base + 8, :]
        turned = pltpu.roll(block, channels, 1)
        firsts, seconds = [], []
        for start in range(0, 8, group):
            span = slice(start, start + group)
            left = jnp.concatenate([block[span], turned[span]], axis=0)[:, :channels]
            left_high, left_low = split_terms(left)
            left = jnp.concatenate([left_high, left_low], axis=0)
            product = dot(left, weight_ref[0, (base + start) // group])
            product = product[: 2 * group] + product[2 * group :]
            firsts.append(product[:group])
            seconds.append(product[group:])
        first = jnp.concatenate(firsts, axis=0)
        second = jnp.concatenate(seconds, axis=0)
        real = jnp.where(lane, first, pltpu.roll(second, channels, 1))
        imag = jnp.where(lane, pltpu.roll(first, channels, 1), second)
        crossed = jnp.where(rows < tiles, pltpu.roll(imag, 8 - tiles, 0), pltpu.roll(imag, tiles, 0))
        result_ref[base : base + 8, :] = real + sign * crossed
    for part in range(2):
        for tile in range(tiles):
            modes_ref[part * count : (part + 1) * count, tile * 128 : (tile + 1) * 128] = (
                result_ref[pl.ds(part * tiles + tile, count, stride=group), :]
            )
    back = back_rows(inverse_high, inverse_low, column ^ 1, modes_ref[...])
    order_ref[:layers] = back.reshape(send_ref.shape)
    store_turns(send_ref, order_ref, z)


def mix(blocks, arrived, weights, forward_table, inverse_tables):
    layers = len(blocks)
    _, rows, feat_count = blocks[0].shape
    count = weights.shape[1]
    scratch = pltpu.VMEM((count * feat_count // 64, 128), jnp.float32)
    return pl.pallas_call(
        functools.partial(mix_kernel, layers),
        out_shape=[
            jax.ShapeDtypeStruct((2 * count, feat_count), jnp.float32),
            jax.ShapeDtypeStruct((layers, rows, feat_count), jnp.float32),
        ],
        scratch_shapes=[pltpu.VMEM((2 * layers, rows, feat_count), jnp.float32), scratch, scratch],
        compiler_params=SMALL,
        name="mix",
    )(*blocks, *arrived, weights, *split_table(forward_table), *inverse_tables)


def keep_kernel(modes_ref, inverse_high, inverse_low, mixed_ref, keep_ref, order_ref):
    z, x, y = quad()
    count = mixed_ref.shape[1]
    feat_count = modes_ref.shape[1]
    for part in range(2):
        mixed_ref[0, :, part * feat_count : (part + 1) * feat_count] = modes_ref[
            part * count : (part + 1) * count
        ]
    back = back_rows(inverse_high, inverse_low, x ^ y, modes_ref[...])
    order_ref[...] = back.reshape(keep_ref.shape)
    store_turns(keep_ref, order_ref, z)


def keep_rows(modes, inverse_tables, like):
    rows, feat_count = modes.shape
    return pl.pallas_call(
        keep_kernel,
        out_shape=[
            jax.ShapeDtypeStruct((1, rows // 2, 2 * feat_count), jnp.float32),
            jax.ShapeDtypeStruct(like.shape, jnp.float32),
        ],
        scratch_shapes=[pltpu.VMEM(like.shape, jnp.float32)],
        compiler_params=SMALL,
        name="keep_rows",
    )(modes, *inverse_tables)


def gelu(half):
    square = jnp.minimum(half * half, 6.25)
    inner = jnp.full_like(square, GELU_TERMS[-1])
    for term in GELU_TERMS[-2::-1]:
        inner = inner * square + term
    return half + half * jnp.tanh(half * inner)


def output_kernel(layers, flow_ref, table_ref, local_ref, bias_ref, *refs):
    own_refs, core_refs = refs[:layers], refs[layers : 2 * layers]
    out_hbm, order_ref, wide_ref, level_ref, done_ref, sent = refs[2 * layers :]
    cells_x, _, feat_count = flow_ref.shape
    channels = local_ref.shape[0]
    z, x, y = quad()
    wide_ref[...] = jnp.zeros_like(wide_ref)
    for start in range(0, WIDTH, channels):
        span = slice(start, start + channels)
        wide_ref[span, span] = local_ref[...] * 0.5
        level_ref[:, span] = bias_ref[...].reshape(1, channels) * 0.5
    level = level_ref[...]
    levels = []
    for _ in range(BIAS_TERMS):
        levels.append(level.astype(jnp.bfloat16).astype(jnp.float32))
        level = level - levels[-1]
    terms = 3 * order_ref.shape[1] * order_ref.shape[2]
    filled = jnp.zeros((table_ref.shape[-1] - terms - BIAS_TERMS, WIDTH), jnp.float32)
    below = jnp.concatenate(levels + [filled], axis=0).astype(jnp.bfloat16)
    below = jnp.concatenate([below, wide_ref[...]], axis=0)
    for column, block_refs in ((x ^ y, own_refs), (x ^ y ^ 1, core_refs)):
        for turn, block_ref in zip(turns(layers), block_refs):
            order_ref[:, (z ^ turn) * 2 + column] = block_ref[...]
    table = table_ref[y, x ^ y]
    copies = []
    for cell in range(cells_x):
        high, low = split_terms(order_ref[cell].reshape(-1, feat_count))
        stack = jnp.concatenate([high, low, high], axis=0)
        for start in range(0, feat_count, WIDTH):
            columns = slice(start, start + WIDTH)
            total = dot(
                jnp.concatenate([table, flow_ref[cell, :, columns]], axis=1),
                jnp.concatenate([stack[:, columns], below], axis=0),
            )
            done_ref[cell, :, columns] = gelu(total).astype(done_ref.dtype)
        copies.append(pltpu.make_async_copy(done_ref.at[cell], out_hbm.at[cell], sent.at[cell]))
        copies[-1].start()
    for copy in copies:
        copy.wait()


def make_output(flow_field, parts, table, local, bias):
    cells_x, _, feat_count = flow_field.shape
    layers = len(parts) // 2
    return pl.pallas_call(
        functools.partial(output_kernel, layers),
        out_specs=pl.BlockSpec(memory_space=pl.ANY),
        scratch_shapes=[
            pltpu.VMEM((cells_x, 2 * layers) + parts[0].shape[1:], jnp.float32),
            pltpu.VMEM((WIDTH, WIDTH), jnp.bfloat16),
            pltpu.VMEM((1, WIDTH), jnp.float32),
            pltpu.VMEM(flow_field.shape, jnp.bfloat16),
            pltpu.SemaphoreType.DMA((cells_x,)),
        ],
        out_shape=jax.ShapeDtypeStruct(flow_field.shape, jnp.bfloat16),
        compiler_params=SMALL,
        name="make_output",
    )(flow_field, table, local, bias, *parts)


def row_body(flow_field, spectral_weight, local_weight, bias_terms):
    cells_x, cells_y, feat_count = flow_field.shape
    peers = lax.axis_size("gx")
    groups_y = lax.axis_size("gy")
    rows_ky = MY // groups_y // peers
    forward_scale = 1.0 / math.sqrt(cells_x * peers * cells_y * groups_y)
    inverse_scale = 1.0 / math.sqrt(MX * MY)

    send, keep = forward_y(flow_field, cells_y * groups_y, peers // 2, rows_ky)
    blocks = along_columns(add_blocks(keep, flip_core(send)), peers)
    inverse_tables = split_table(inverse_x_table(cells_x, peers, rows_ky))
    modes, send = mix(
        blocks,
        [flip_core(second_half(block)) for block in blocks],
        spectral_weight,
        forward_x_table(cells_x, peers, rows_ky) * forward_scale,
        inverse_tables,
    )
    arrived = flip_core(send)
    mixed, keep = keep_rows(modes, inverse_tables, send)
    own = along_columns(join_blocks(keep, arrived, cells_x), peers)
    parts = own + [flip_core(block) for block in own]
    table = output_table(inverse_y_table(cells_y, groups_y, peers, rows_ky) * (0.5 * inverse_scale))
    return make_output(flow_field, parts, table, local_weight, bias_terms), mixed


def body(flow_field, spectral_weight, local_weight, bias_terms):
    peers = lax.axis_size("gx")
    extent = lax.axis_size("gy") * flow_field.shape[1]
    paired = lax.axis_size("gy") == 2 and peers & (peers - 1) == 0 and extent & (extent - 1) == 0
    if paired and spectral_weight.shape[1] == 2 * MX and WIDTH % local_weight.shape[0] == 0:
        return row_body(flow_field, spectral_weight, local_weight, bias_terms)
    return general_body(flow_field, spectral_weight, local_weight, bias_terms)


def solution(mesh):
    placed = (P(("group", "gx"), "gy", None), P("gy", "gx", None, None), P(), P())
    return jax.shard_map(
        body,
        mesh=mesh,
        in_specs=placed,
        out_specs=(P(("group", "gx"), "gy", None), P(("group", "gy"), "gx", None)),
        check_vma=False,
    )
```

```python
import functools
import math

import jax
import jax.numpy as jnp
import ml_dtypes
import numpy as np
from jax import lax
from jax.experimental import pallas as pl
from jax.experimental.pallas import tpu as pltpu
from jax.sharding import PartitionSpec as P

MX = 32
MY = 32


def wave_number(index, count):
    return jnp.where(index < count // 2, index, index - count)


def phase_table(waves, places, extent):
    product = waves[:, None] * places[None, :] % extent
    return 2.0 * math.pi / extent * product.astype(jnp.float32)


def row_tables(ky_rows, kx_rows, x_places, extent, width):
    angle = phase_table(wave_number(kx_rows, MX), x_places, extent)
    select = (ky_rows[:, None] == jnp.arange(width, dtype=jnp.int32)[None, :]).astype(jnp.float32)
    cosine = jnp.cos(angle)[:, :, None] * select[:, None, :]
    sine_part = jnp.sin(angle)[:, :, None] * select[:, None, :]
    return (cosine, sine_part)


def forward_rows(y_local, ky_rows, kx_rows, x_places, extent):
    cosine, sine_part = row_tables(ky_rows, kx_rows, x_places, extent, y_local.shape[0])
    real_in = y_local[:, 0]
    imag_in = y_local[:, 1]

    def contract(table, values):
        return jnp.einsum("rxk,kxf->rf", table, values, precision=lax.Precision.HIGHEST)

    real_out = contract(cosine, real_in) + contract(sine_part, imag_in)
    imag_out = contract(cosine, imag_in) - contract(sine_part, real_in)
    return jnp.concatenate([real_out, imag_out], axis=1)


def inverse_rows(running, shard_rows, ky_rows, kx_rows, x_places, extent):
    cosine, sine_part = row_tables(ky_rows, kx_rows, x_places, extent, running.shape[0])
    feat_count = shard_rows.shape[1] // 2
    real_part = shard_rows[:, :feat_count]
    imag_part = shard_rows[:, feat_count:]

    def contract(table, values):
        return jnp.einsum("rxk,rf->kxf", table, values, precision=lax.Precision.HIGHEST)

    new_real = contract(cosine, real_part) - contract(sine_part, imag_part)
    new_imag = contract(cosine, imag_part) + contract(sine_part, real_part)
    return jnp.stack([new_real, new_imag], axis=1)


def general_body(flow_field, spectral_weight, local_weight, bias_terms):
    cells_x, cells_y, feat_count = flow_field.shape
    channels = local_weight.shape[0]
    planes = feat_count // channels
    groups_x = lax.axis_size("gx")
    groups_y = lax.axis_size("gy")
    extent_x = cells_x * groups_x
    extent_y = cells_y * groups_y
    half_width = MY // groups_y
    quota_rows = spectral_weight.shape[1]
    high = lax.Precision.HIGHEST
    x_places = lax.axis_index("gx") * cells_x + jnp.arange(cells_x, dtype=jnp.int32)
    y_places = lax.axis_index("gy") * cells_y + jnp.arange(cells_y, dtype=jnp.int32)
    y_angle = phase_table(wave_number(jnp.arange(MY, dtype=jnp.int32), MY), y_places, extent_y)
    y_table = (
        jnp.stack([jnp.cos(y_angle), -jnp.sin(y_angle)], axis=1)
        .reshape(2 * MY, cells_y)
        .astype(jnp.bfloat16)
    )
    y_local = lax.psum_scatter(
        jnp.einsum("qy,xyf->qxf", y_table, flow_field, preferred_element_type=jnp.float32),
        "gy",
        scatter_dimension=0,
        tiled=True,
    )
    y_local = y_local.reshape(half_width, 2, cells_x, feat_count)
    rest_index = jnp.arange(lax.axis_size("gx") * quota_rows, dtype=jnp.int32)
    spectrum = lax.psum_scatter(
        forward_rows(y_local, rest_index // MX, rest_index % MX, x_places, extent_x),
        "gx",
        scatter_dimension=0,
        tiled=True,
    )
    spectrum = spectrum * (1.0 / math.sqrt(extent_x * extent_y))
    coeffs = spectrum.reshape(quota_rows, 2, planes, channels)
    weights = spectral_weight[0].astype(jnp.float32)
    product = jnp.einsum("rpzc,rco->rpzo", coeffs, weights, precision=high)
    mixed_real = product[:, 0, :, :channels] - product[:, 1, :, channels:]
    mixed_imag = product[:, 0, :, channels:] + product[:, 1, :, :channels]
    mixed_local = jnp.stack([mixed_real, mixed_imag], axis=1).reshape(quota_rows, 2 * feat_count)
    pointwise = jnp.einsum(
        "xyzc,co->xyzo",
        flow_field.reshape(cells_x, cells_y, planes, channels),
        local_weight,
        preferred_element_type=jnp.float32,
    )
    start_half = jnp.zeros((half_width, 2, cells_x, feat_count), jnp.float32)
    shard_rows = lax.all_gather(mixed_local, "gx", axis=0, tiled=True)
    rest_index = jnp.arange(shard_rows.shape[0], dtype=jnp.int32)
    back_half = inverse_rows(
        start_half, shard_rows, rest_index // MX, rest_index % MX, x_places, extent_x
    )
    back_whole = lax.all_gather(back_half, "gy", axis=0, tiled=True)
    y_cos = jnp.cos(y_angle)
    y_sin = jnp.sin(y_angle)
    spectral = (
        jnp.einsum("kn,kxf->xnf", y_cos, back_whole[:, 0], precision=high)
        - jnp.einsum("kn,kxf->xnf", y_sin, back_whole[:, 1], precision=high)
    ) * (1.0 / math.sqrt(MX * MY))
    total = spectral.reshape(cells_x, cells_y, planes, channels) + pointwise + bias_terms
    output = (
        jax.nn.gelu(total, approximate=False)
        .reshape(cells_x, cells_y, feat_count)
        .astype(jnp.bfloat16)
    )
    return (output, mixed_local.reshape(1, quota_rows, 2 * feat_count))


SMALL = pltpu.CompilerParams(vmem_limit_bytes=20 * 1024 * 1024)
LARGE = pltpu.CompilerParams(vmem_limit_bytes=53 * 1024 * 1024)
WIDTH = 256
BIAS_TERMS = 3
GELU_TERMS = (
    1.5957645177841187,
    0.29075613617897034,
    -0.0014313592109829187,
    -0.006452994421124458,
    0.0015898864949122071,
    -0.0001365363277727738,
)


def angles(count, places, extent):
    index = np.arange(count)
    waves = np.where(index < count // 2, index, index - count)
    product = (waves[:, None] * np.asarray(places)[None, :]) % extent
    return (np.float32(2.0 * math.pi / extent) * product.astype(np.float32)).astype(np.float64)


def split_table(table):
    high = table.astype(ml_dtypes.bfloat16)
    low = (table - high.astype(np.float64)).astype(ml_dtypes.bfloat16)
    return high, low


def split_terms(values):
    high = values.astype(jnp.bfloat16)
    low = (values - high.astype(jnp.float32)).astype(jnp.bfloat16)
    return high, low


def quad():
    place = lax.axis_index("gx")
    return place // 2, place % 2, lax.axis_index("gy")


def turns(layers, inverse=False):
    half = layers // 2
    if inverse:
        return list(range(layers - 1, -1, -1))
    return list(range(half, layers)) + list(range(half - 1, -1, -1))


def forward_x_table(cells_x, peers, rows_ky):
    extent = cells_x * peers
    angle = angles(MX, np.arange(extent), extent)
    cosine, sine = np.cos(angle), np.sin(angle)
    out = np.zeros((2, rows_ky, MX, extent, rows_ky, 2))
    for row in range(rows_ky):
        out[0, row, :, :, row, 0] = cosine
        out[0, row, :, :, row, 1] = sine
        out[1, row, :, :, row, 1] = cosine
        out[1, row, :, :, row, 0] = -sine
    return out.reshape(2 * rows_ky * MX, extent * rows_ky * 2)


def inverse_x_table(cells_x, peers, rows_ky):
    extent = cells_x * peers
    angle = angles(MX, np.arange(extent), extent)
    cosine, sine = np.cos(angle).T, np.sin(angle).T
    out = np.zeros((extent, rows_ky, 2, 2, rows_ky, MX))
    for row in range(rows_ky):
        out[:, row, 0, 0, row, :] = cosine
        out[:, row, 0, 1, row, :] = -sine
        out[:, row, 1, 1, row, :] = cosine
        out[:, row, 1, 0, row, :] = sine
    out = out.reshape(peers // 2, 2, cells_x * rows_ky * 2, 2 * rows_ky * MX)
    return np.moveaxis(out, 1, 0).reshape(2, -1, 2 * rows_ky * MX)


def inverse_y_table(cells_y, groups_y, peers, rows_ky):
    extent = cells_y * groups_y
    angle = angles(MY, np.arange(extent), extent)
    full = np.stack([np.cos(angle), -np.sin(angle)], axis=1)
    full = full.reshape(groups_y, peers, rows_ky, 2, groups_y, cells_y)
    out = np.zeros((groups_y, 2, cells_y, peers, 2, rows_ky, 2))
    for y in range(groups_y):
        for column in range(2):
            for peer in range(peers):
                for place in range(2):
                    half = y ^ place ^ column ^ (peer % 2)
                    out[y, column, :, peer, place] = np.moveaxis(full[half, peer, :, :, y], -1, 0)
    return out.reshape(groups_y, 2, cells_y, 4 * peers * rows_ky)


def output_table(table):
    high, low = split_table(table)
    parts = [high, high, low, np.ones(table.shape[:-1] + (BIAS_TERMS,), high.dtype)]
    used = 3 * table.shape[-1] + BIAS_TERMS
    parts.append(np.zeros(table.shape[:-1] + (-used % 256,), high.dtype))
    return np.concatenate(parts, axis=-1)


def dot(left, right):
    return jnp.dot(left, right, preferred_element_type=jnp.float32)


def forward_y_table(shape, extent, layers, rows_ky):
    z, x, y = quad()
    peers = 2 * layers
    row = lax.broadcasted_iota(jnp.int32, (shape[0], 1), 0)
    block = row // (2 * rows_ky)
    place = block // 2 % layers
    turn = jnp.where(place < layers // 2, place + layers // 2, layers - 1 - place)
    side = y ^ (1 - block // peers)
    owner = (side ^ (block % 2)) * peers + (z ^ turn) * 2 + (x ^ side)
    index = owner * rows_ky + row // 2 % rows_ky
    y_places = lax.broadcasted_iota(jnp.int32, (1, shape[1]), 1) + y * shape[1]
    steps = (wave_number(index, MY) * y_places) & (extent - 1)
    angle = 2.0 * math.pi / extent * steps.astype(jnp.float32)
    return jnp.where(row % 2 == 0, jnp.cos(angle), -jnp.sin(angle)).astype(jnp.bfloat16)


def forward_y_kernel(extent, rows_ky, flow_hbm, send_ref, keep_ref, flow_ref, arrived):
    layers, _, rows, feat_count = send_ref.shape
    cells_x, cells_y, _ = flow_ref.shape
    rows = rows // cells_x
    copies = [
        pltpu.make_async_copy(flow_hbm.at[x], flow_ref.at[x], arrived.at[x])
        for x in range(cells_x)
    ]
    for copy in copies:
        copy.start()
    table = forward_y_table((2 * MY, cells_y), extent, layers, rows_ky)
    for x in range(cells_x):
        copies[x].wait()
        result = dot(table, flow_ref[x]).reshape(2, layers, 2, rows, feat_count)
        send_ref[:, :, x * rows : (x + 1) * rows, :] = result[0]
        keep_ref[:, :, x * rows : (x + 1) * rows, :] = result[1]


def forward_y(flow_field, extent, layers, rows_ky):
    cells_x, _, feat_count = flow_field.shape
    shape = jax.ShapeDtypeStruct((layers, 2, cells_x * 2 * rows_ky, feat_count), jnp.float32)
    return pl.pallas_call(
        functools.partial(forward_y_kernel, extent, rows_ky),
        in_specs=[pl.BlockSpec(memory_space=pltpu.HBM)],
        out_shape=[shape] * 2,
        scratch_shapes=[
            pltpu.VMEM(flow_field.shape, flow_field.dtype),
            pltpu.SemaphoreType.DMA((cells_x,)),
        ],
        compiler_params=LARGE,
        name="forward_y",
    )(flow_field)


def flip_core(block):
    return lax.ppermute(block, "gy", [(0, 1), (1, 0)])


def along_columns(blocks, peers, inverse=False):
    arrived = []
    for turn, block in zip(turns(len(blocks), inverse), blocks):
        pairs = [
            (2 * place + core, 2 * (place ^ (2 * turn + core)) + core)
            for place in range(peers)
            for core in range(2)
        ]
        arrived.append(lax.ppermute(block, ("gx", "gy"), pairs))
    return arrived


def small_call(kernel, out_shape, name):
    return pl.pallas_call(kernel, out_shape=out_shape, compiler_params=SMALL, name=name)


def second_kernel(block_ref, out_ref):
    out_ref[...] = block_ref[1]


def second_half(block):
    shape = jax.ShapeDtypeStruct(block.shape[1:], block.dtype)
    return small_call(second_kernel, shape, "second_half")(block)


def add_kernel(keep_ref, arrived_ref, *out_refs):
    for turn, out_ref in enumerate(out_refs):
        out_ref[...] = keep_ref[turn] + arrived_ref[turn]


def add_blocks(keep, arrived):
    shape = jax.ShapeDtypeStruct(keep.shape[1:], keep.dtype)
    return small_call(add_kernel, [shape] * keep.shape[0], "add_blocks")(keep, arrived)


def join_kernel(keep_ref, arrived_ref, *out_refs):
    cells_x, rows, _ = out_refs[0].shape
    rows = rows // 2
    for turn, out_ref in enumerate(out_refs):
        for cell in range(cells_x):
            span = slice(cell * rows, (cell + 1) * rows)
            out_ref[cell] = jnp.concatenate(
                [keep_ref[turn, span, :], arrived_ref[turn, span, :]], axis=0
            )


def join_blocks(keep, arrived, cells_x):
    layers, rows, feat_count = keep.shape
    shape = jax.ShapeDtypeStruct((cells_x, 2 * rows // cells_x, feat_count), keep.dtype)
    return small_call(join_kernel, [shape] * layers, "join_blocks")(keep, arrived)


def back_rows(inverse_high, inverse_low, column, modes):
    high, low = split_terms(modes)
    table = inverse_high[column]
    return dot(table, high) + dot(table, low) + dot(inverse_low[column], high)


def store_turns(out_ref, order_ref, z):
    for index, turn in enumerate(turns(out_ref.shape[0], True)):
        out_ref[index] = order_ref[z ^ turn]


def mix_kernel(layers, *refs):
    block_refs, arrived_refs = refs[:layers], refs[layers : 2 * layers]
    weight_ref, forward_high, forward_low, inverse_high, inverse_low = refs[
        2 * layers : 2 * layers + 5
    ]
    modes_ref, send_ref, order_ref, spread_ref, result_ref = refs[2 * layers + 5 :]
    z, x, y = quad()
    column = x ^ y
    for index, turn in enumerate(turns(layers)):
        order_ref[(z ^ turn) * 2 + column] = block_refs[index][0]
        order_ref[(z ^ turn) * 2 + (column ^ 1)] = arrived_refs[index][...]
    feat_count = order_ref.shape[-1]
    count = weight_ref.shape[1]
    channels = weight_ref.shape[2]
    tiles = feat_count // 128
    group = 2 * tiles
    high, low = split_terms(order_ref[...].reshape(-1, feat_count))
    spectrum = (
        dot(forward_high[...], high) + dot(forward_high[...], low) + dot(forward_low[...], high)
    )
    for part in range(2):
        for tile in range(tiles):
            spread_ref[pl.ds(part * tiles + tile, count, stride=group), :] = spectrum[
                part * count : (part + 1) * count, tile * 128 : (tile + 1) * 128
            ]
    rows = lax.broadcasted_iota(jnp.int32, (8, 128), 0) % group
    lane = lax.broadcasted_iota(jnp.int32, (8, 128), 1) < channels
    sign = jnp.where(rows < tiles, -1.0, 1.0)
    for base in range(0, count * group, 8):
        block = spread_ref[base : base + 8, :]
        turned = pltpu.roll(block, channels, 1)
        firsts, seconds = [], []
        for start in range(0, 8, group):
            span = slice(start, start + group)
            left = jnp.concatenate([block[span], turned[span]], axis=0)[:, :channels]
            left_high, left_low = split_terms(left)
            left = jnp.concatenate([left_high, left_low], axis=0)
            product = dot(left, weight_ref[0, (base + start) // group])
            product = product[: 2 * group] + product[2 * group :]
            firsts.append(product[:group])
            seconds.append(product[group:])
        first = jnp.concatenate(firsts, axis=0)
        second = jnp.concatenate(seconds, axis=0)
        real = jnp.where(lane, first, pltpu.roll(second, channels, 1))
        imag = jnp.where(lane, pltpu.roll(first, channels, 1), second)
        crossed = jnp.where(rows < tiles, pltpu.roll(imag, 8 - tiles, 0), pltpu.roll(imag, tiles, 0))
        result_ref[base : base + 8, :] = real + sign * crossed
    for part in range(2):
        for tile in range(tiles):
            modes_ref[part * count : (part + 1) * count, tile * 128 : (tile + 1) * 128] = (
                result_ref[pl.ds(part * tiles + tile, count, stride=group), :]
            )
    back = back_rows(inverse_high, inverse_low, column ^ 1, modes_ref[...])
    order_ref[:layers] = back.reshape(send_ref.shape)
    store_turns(send_ref, order_ref, z)


def mix(blocks, arrived, weights, forward_table, inverse_tables):
    layers = len(blocks)
    _, rows, feat_count = blocks[0].shape
    count = weights.shape[1]
    scratch = pltpu.VMEM((count * feat_count // 64, 128), jnp.float32)
    return pl.pallas_call(
        functools.partial(mix_kernel, layers),
        out_shape=[
            jax.ShapeDtypeStruct((2 * count, feat_count), jnp.float32),
            jax.ShapeDtypeStruct((layers, rows, feat_count), jnp.float32),
        ],
        scratch_shapes=[pltpu.VMEM((2 * layers, rows, feat_count), jnp.float32), scratch, scratch],
        compiler_params=SMALL,
        name="mix",
    )(*blocks, *arrived, weights, *split_table(forward_table), *inverse_tables)


def keep_kernel(modes_ref, inverse_high, inverse_low, mixed_ref, keep_ref, order_ref):
    z, x, y = quad()
    count = mixed_ref.shape[1]
    feat_count = modes_ref.shape[1]
    for part in range(2):
        mixed_ref[0, :, part * feat_count : (part + 1) * feat_count] = modes_ref[
            part * count : (part + 1) * count
        ]
    back = back_rows(inverse_high, inverse_low, x ^ y, modes_ref[...])
    order_ref[...] = back.reshape(keep_ref.shape)
    store_turns(keep_ref, order_ref, z)


def keep_rows(modes, inverse_tables, like):
    rows, feat_count = modes.shape
    return pl.pallas_call(
        keep_kernel,
        out_shape=[
            jax.ShapeDtypeStruct((1, rows // 2, 2 * feat_count), jnp.float32),
            jax.ShapeDtypeStruct(like.shape, jnp.float32),
        ],
        scratch_shapes=[pltpu.VMEM(like.shape, jnp.float32)],
        compiler_params=SMALL,
        name="keep_rows",
    )(modes, *inverse_tables)


def gelu(half):
    square = jnp.minimum(half * half, 6.25)
    inner = jnp.full_like(square, GELU_TERMS[-1])
    for term in GELU_TERMS[-2::-1]:
        inner = inner * square + term
    return half + half * jnp.tanh(half * inner)


def output_kernel(layers, flow_ref, table_ref, local_ref, bias_ref, *refs):
    own_refs, core_refs = refs[:layers], refs[layers : 2 * layers]
    out_hbm, order_ref, wide_ref, level_ref, done_ref, sent = refs[2 * layers :]
    cells_x, _, feat_count = flow_ref.shape
    channels = local_ref.shape[0]
    z, x, y = quad()
    wide_ref[...] = jnp.zeros_like(wide_ref)
    for start in range(0, WIDTH, channels):
        span = slice(start, start + channels)
        wide_ref[span, span] = local_ref[...] * 0.5
        level_ref[:, span] = bias_ref[...].reshape(1, channels) * 0.5
    level = level_ref[...]
    levels = []
    for _ in range(BIAS_TERMS):
        levels.append(level.astype(jnp.bfloat16).astype(jnp.float32))
        level = level - levels[-1]
    terms = 3 * order_ref.shape[1] * order_ref.shape[2]
    filled = jnp.zeros((table_ref.shape[-1] - terms - BIAS_TERMS, WIDTH), jnp.float32)
    below = jnp.concatenate(levels + [filled], axis=0).astype(jnp.bfloat16)
    below = jnp.concatenate([below, wide_ref[...]], axis=0)
    for column, block_refs in ((x ^ y, own_refs), (x ^ y ^ 1, core_refs)):
        for turn, block_ref in zip(turns(layers, True), block_refs):
            order_ref[:, (z ^ turn) * 2 + column] = block_ref[...]
    table = table_ref[y, x ^ y]
    copies = []
    for cell in range(cells_x):
        high, low = split_terms(order_ref[cell].reshape(-1, feat_count))
        stack = jnp.concatenate([high, low, high], axis=0)
        for start in range(0, feat_count, WIDTH):
            columns = slice(start, start + WIDTH)
            total = dot(
                jnp.concatenate([table, flow_ref[cell, :, columns]], axis=1),
                jnp.concatenate([stack[:, columns], below], axis=0),
            )
            done_ref[cell, :, columns] = gelu(total).astype(done_ref.dtype)
        copies.append(pltpu.make_async_copy(done_ref.at[cell], out_hbm.at[cell], sent.at[cell]))
        copies[-1].start()
    for copy in copies:
        copy.wait()


def make_output(flow_field, parts, table, local, bias):
    cells_x, _, feat_count = flow_field.shape
    layers = len(parts) // 2
    return pl.pallas_call(
        functools.partial(output_kernel, layers),
        out_specs=pl.BlockSpec(memory_space=pl.ANY),
        scratch_shapes=[
            pltpu.VMEM((cells_x, 2 * layers) + parts[0].shape[1:], jnp.float32),
            pltpu.VMEM((WIDTH, WIDTH), jnp.bfloat16),
            pltpu.VMEM((1, WIDTH), jnp.float32),
            pltpu.VMEM(flow_field.shape, jnp.bfloat16),
            pltpu.SemaphoreType.DMA((cells_x,)),
        ],
        out_shape=jax.ShapeDtypeStruct(flow_field.shape, jnp.bfloat16),
        compiler_params=SMALL,
        name="make_output",
    )(flow_field, table, local, bias, *parts)


def row_body(flow_field, spectral_weight, local_weight, bias_terms):
    cells_x, cells_y, feat_count = flow_field.shape
    peers = lax.axis_size("gx")
    groups_y = lax.axis_size("gy")
    rows_ky = MY // groups_y // peers
    forward_scale = 1.0 / math.sqrt(cells_x * peers * cells_y * groups_y)
    inverse_scale = 1.0 / math.sqrt(MX * MY)

    send, keep = forward_y(flow_field, cells_y * groups_y, peers // 2, rows_ky)
    blocks = along_columns(add_blocks(keep, flip_core(send)), peers)
    inverse_tables = split_table(inverse_x_table(cells_x, peers, rows_ky))
    modes, send = mix(
        blocks,
        [flip_core(second_half(block)) for block in blocks],
        spectral_weight,
        forward_x_table(cells_x, peers, rows_ky) * forward_scale,
        inverse_tables,
    )
    arrived = flip_core(send)
    mixed, keep = keep_rows(modes, inverse_tables, send)
    own = along_columns(join_blocks(keep, arrived, cells_x), peers, True)
    parts = own + [flip_core(block) for block in own]
    table = output_table(inverse_y_table(cells_y, groups_y, peers, rows_ky) * (0.5 * inverse_scale))
    return make_output(flow_field, parts, table, local_weight, bias_terms), mixed


def body(flow_field, spectral_weight, local_weight, bias_terms):
    peers = lax.axis_size("gx")
    extent = lax.axis_size("gy") * flow_field.shape[1]
    paired = lax.axis_size("gy") == 2 and peers & (peers - 1) == 0 and extent & (extent - 1) == 0
    if paired and spectral_weight.shape[1] == 2 * MX and WIDTH % local_weight.shape[0] == 0:
        return row_body(flow_field, spectral_weight, local_weight, bias_terms)
    return general_body(flow_field, spectral_weight, local_weight, bias_terms)


def solution(mesh):
    placed = (P(("group", "gx"), "gy", None), P("gy", "gx", None, None), P(), P())
    return jax.shard_map(
        body,
        mesh=mesh,
        in_specs=placed,
        out_specs=(P(("group", "gx"), "gy", None), P(("group", "gy"), "gx", None)),
        check_vma=False,
    )
```

```python
import functools
import math

import jax
import jax.numpy as jnp
import ml_dtypes
import numpy as np
from jax import lax
from jax.experimental import pallas as pl
from jax.experimental.pallas import tpu as pltpu
from jax.sharding import PartitionSpec as P

MX = 32
MY = 32


def wave_number(index, count):
    return jnp.where(index < count // 2, index, index - count)


def phase_table(waves, places, extent):
    product = waves[:, None] * places[None, :] % extent
    return 2.0 * math.pi / extent * product.astype(jnp.float32)


def row_tables(ky_rows, kx_rows, x_places, extent, width):
    angle = phase_table(wave_number(kx_rows, MX), x_places, extent)
    select = (ky_rows[:, None] == jnp.arange(width, dtype=jnp.int32)[None, :]).astype(jnp.float32)
    cosine = jnp.cos(angle)[:, :, None] * select[:, None, :]
    sine_part = jnp.sin(angle)[:, :, None] * select[:, None, :]
    return (cosine, sine_part)


def forward_rows(y_local, ky_rows, kx_rows, x_places, extent):
    cosine, sine_part = row_tables(ky_rows, kx_rows, x_places, extent, y_local.shape[0])
    real_in = y_local[:, 0]
    imag_in = y_local[:, 1]

    def contract(table, values):
        return jnp.einsum("rxk,kxf->rf", table, values, precision=lax.Precision.HIGHEST)

    real_out = contract(cosine, real_in) + contract(sine_part, imag_in)
    imag_out = contract(cosine, imag_in) - contract(sine_part, real_in)
    return jnp.concatenate([real_out, imag_out], axis=1)


def inverse_rows(running, shard_rows, ky_rows, kx_rows, x_places, extent):
    cosine, sine_part = row_tables(ky_rows, kx_rows, x_places, extent, running.shape[0])
    feat_count = shard_rows.shape[1] // 2
    real_part = shard_rows[:, :feat_count]
    imag_part = shard_rows[:, feat_count:]

    def contract(table, values):
        return jnp.einsum("rxk,rf->kxf", table, values, precision=lax.Precision.HIGHEST)

    new_real = contract(cosine, real_part) - contract(sine_part, imag_part)
    new_imag = contract(cosine, imag_part) + contract(sine_part, real_part)
    return jnp.stack([new_real, new_imag], axis=1)


def general_body(flow_field, spectral_weight, local_weight, bias_terms):
    cells_x, cells_y, feat_count = flow_field.shape
    channels = local_weight.shape[0]
    planes = feat_count // channels
    groups_x = lax.axis_size("gx")
    groups_y = lax.axis_size("gy")
    extent_x = cells_x * groups_x
    extent_y = cells_y * groups_y
    half_width = MY // groups_y
    quota_rows = spectral_weight.shape[1]
    high = lax.Precision.HIGHEST
    x_places = lax.axis_index("gx") * cells_x + jnp.arange(cells_x, dtype=jnp.int32)
    y_places = lax.axis_index("gy") * cells_y + jnp.arange(cells_y, dtype=jnp.int32)
    y_angle = phase_table(wave_number(jnp.arange(MY, dtype=jnp.int32), MY), y_places, extent_y)
    y_table = (
        jnp.stack([jnp.cos(y_angle), -jnp.sin(y_angle)], axis=1)
        .reshape(2 * MY, cells_y)
        .astype(jnp.bfloat16)
    )
    y_local = lax.psum_scatter(
        jnp.einsum("qy,xyf->qxf", y_table, flow_field, preferred_element_type=jnp.float32),
        "gy",
        scatter_dimension=0,
        tiled=True,
    )
    y_local = y_local.reshape(half_width, 2, cells_x, feat_count)
    rest_index = jnp.arange(lax.axis_size("gx") * quota_rows, dtype=jnp.int32)
    spectrum = lax.psum_scatter(
        forward_rows(y_local, rest_index // MX, rest_index % MX, x_places, extent_x),
        "gx",
        scatter_dimension=0,
        tiled=True,
    )
    spectrum = spectrum * (1.0 / math.sqrt(extent_x * extent_y))
    coeffs = spectrum.reshape(quota_rows, 2, planes, channels)
    weights = spectral_weight[0].astype(jnp.float32)
    product = jnp.einsum("rpzc,rco->rpzo", coeffs, weights, precision=high)
    mixed_real = product[:, 0, :, :channels] - product[:, 1, :, channels:]
    mixed_imag = product[:, 0, :, channels:] + product[:, 1, :, :channels]
    mixed_local = jnp.stack([mixed_real, mixed_imag], axis=1).reshape(quota_rows, 2 * feat_count)
    pointwise = jnp.einsum(
        "xyzc,co->xyzo",
        flow_field.reshape(cells_x, cells_y, planes, channels),
        local_weight,
        preferred_element_type=jnp.float32,
    )
    start_half = jnp.zeros((half_width, 2, cells_x, feat_count), jnp.float32)
    shard_rows = lax.all_gather(mixed_local, "gx", axis=0, tiled=True)
    rest_index = jnp.arange(shard_rows.shape[0], dtype=jnp.int32)
    back_half = inverse_rows(
        start_half, shard_rows, rest_index // MX, rest_index % MX, x_places, extent_x
    )
    back_whole = lax.all_gather(back_half, "gy", axis=0, tiled=True)
    y_cos = jnp.cos(y_angle)
    y_sin = jnp.sin(y_angle)
    spectral = (
        jnp.einsum("kn,kxf->xnf", y_cos, back_whole[:, 0], precision=high)
        - jnp.einsum("kn,kxf->xnf", y_sin, back_whole[:, 1], precision=high)
    ) * (1.0 / math.sqrt(MX * MY))
    total = spectral.reshape(cells_x, cells_y, planes, channels) + pointwise + bias_terms
    output = (
        jax.nn.gelu(total, approximate=False)
        .reshape(cells_x, cells_y, feat_count)
        .astype(jnp.bfloat16)
    )
    return (output, mixed_local.reshape(1, quota_rows, 2 * feat_count))


SMALL = pltpu.CompilerParams(vmem_limit_bytes=20 * 1024 * 1024)
LARGE = pltpu.CompilerParams(vmem_limit_bytes=53 * 1024 * 1024)
WIDTH = 256
BIAS_TERMS = 3
GELU_TERMS = (
    1.5957645177841187,
    0.29075613617897034,
    -0.0014313592109829187,
    -0.006452994421124458,
    0.0015898864949122071,
    -0.0001365363277727738,
)


def angles(count, places, extent):
    index = np.arange(count)
    waves = np.where(index < count // 2, index, index - count)
    product = (waves[:, None] * np.asarray(places)[None, :]) % extent
    return (np.float32(2.0 * math.pi / extent) * product.astype(np.float32)).astype(np.float64)


def split_table(table):
    high = table.astype(ml_dtypes.bfloat16)
    low = (table - high.astype(np.float64)).astype(ml_dtypes.bfloat16)
    return high, low


def split_terms(values):
    high = values.astype(jnp.bfloat16)
    low = (values - high.astype(jnp.float32)).astype(jnp.bfloat16)
    return high, low


def quad():
    place = lax.axis_index("gx")
    return place // 2, place % 2, lax.axis_index("gy")


def turns(layers):
    half = layers // 2
    return list(range(half, layers)) + list(range(half - 1, -1, -1))


def forward_x_table(cells_x, peers, rows_ky):
    extent = cells_x * peers
    angle = angles(MX, np.arange(extent), extent)
    cosine, sine = np.cos(angle), np.sin(angle)
    out = np.zeros((2, rows_ky, MX, extent, rows_ky, 2))
    for row in range(rows_ky):
        out[0, row, :, :, row, 0] = cosine
        out[0, row, :, :, row, 1] = sine
        out[1, row, :, :, row, 1] = cosine
        out[1, row, :, :, row, 0] = -sine
    return out.reshape(2 * rows_ky * MX, extent * rows_ky * 2)


def inverse_x_table(cells_x, peers, rows_ky):
    extent = cells_x * peers
    angle = angles(MX, np.arange(extent), extent)
    cosine, sine = np.cos(angle).T, np.sin(angle).T
    out = np.zeros((extent, rows_ky, 2, 2, rows_ky, MX))
    for row in range(rows_ky):
        out[:, row, 0, 0, row, :] = cosine
        out[:, row, 0, 1, row, :] = -sine
        out[:, row, 1, 1, row, :] = cosine
        out[:, row, 1, 0, row, :] = sine
    out = out.reshape(peers // 2, 2, cells_x * rows_ky * 2, 2 * rows_ky * MX)
    return np.moveaxis(out, 1, 0).reshape(2, -1, 2 * rows_ky * MX)


def inverse_y_table(cells_y, groups_y, peers, rows_ky):
    extent = cells_y * groups_y
    angle = angles(MY, np.arange(extent), extent)
    full = np.stack([np.cos(angle), -np.sin(angle)], axis=1)
    full = full.reshape(groups_y, peers, rows_ky, 2, groups_y, cells_y)
    out = np.zeros((groups_y, 2, cells_y, peers, 2, rows_ky, 2))
    for y in range(groups_y):
        for column in range(2):
            for peer in range(peers):
                for place in range(2):
                    half = y ^ place ^ column ^ (peer % 2)
                    out[y, column, :, peer, place] = np.moveaxis(full[half, peer, :, :, y], -1, 0)
    return out.reshape(groups_y, 2, cells_y, 4 * peers * rows_ky)


def output_table(table):
    high, low = split_table(table)
    parts = [high, high, low, np.ones(table.shape[:-1] + (BIAS_TERMS,), high.dtype)]
    used = 3 * table.shape[-1] + BIAS_TERMS
    parts.append(np.zeros(table.shape[:-1] + (-used % 256,), high.dtype))
    return np.concatenate(parts, axis=-1)


def dot(left, right):
    return jnp.dot(left, right, preferred_element_type=jnp.float32)


def forward_y_table(shape, extent, layers, rows_ky):
    z, x, y = quad()
    peers = 2 * layers
    row = lax.broadcasted_iota(jnp.int32, (shape[0], 1), 0)
    block = row // (2 * rows_ky)
    place = block // 2 % layers
    turn = jnp.where(place < layers // 2, place + layers // 2, layers - 1 - place)
    side = y ^ (1 - block // peers)
    owner = (side ^ (block % 2)) * peers + (z ^ turn) * 2 + (x ^ side)
    index = owner * rows_ky + row // 2 % rows_ky
    y_places = lax.broadcasted_iota(jnp.int32, (1, shape[1]), 1) + y * shape[1]
    steps = (wave_number(index, MY) * y_places) & (extent - 1)
    angle = 2.0 * math.pi / extent * steps.astype(jnp.float32)
    return jnp.where(row % 2 == 0, jnp.cos(angle), -jnp.sin(angle)).astype(jnp.bfloat16)


def forward_y_kernel(extent, rows_ky, flow_hbm, send_ref, keep_ref, flow_ref, arrived):
    layers, _, rows, feat_count = send_ref.shape
    cells_x, cells_y, _ = flow_ref.shape
    rows = rows // cells_x
    copies = [
        pltpu.make_async_copy(flow_hbm.at[x], flow_ref.at[x], arrived.at[x])
        for x in range(cells_x)
    ]
    for copy in copies:
        copy.start()
    table = forward_y_table((2 * MY, cells_y), extent, layers, rows_ky)
    for x in range(cells_x):
        copies[x].wait()
        result = dot(table, flow_ref[x]).reshape(2, layers, 2, rows, feat_count)
        send_ref[:, :, x * rows : (x + 1) * rows, :] = result[0]
        keep_ref[:, :, x * rows : (x + 1) * rows, :] = result[1]


def forward_y(flow_field, extent, layers, rows_ky):
    cells_x, _, feat_count = flow_field.shape
    shape = jax.ShapeDtypeStruct((layers, 2, cells_x * 2 * rows_ky, feat_count), jnp.float32)
    return pl.pallas_call(
        functools.partial(forward_y_kernel, extent, rows_ky),
        in_specs=[pl.BlockSpec(memory_space=pltpu.HBM)],
        out_shape=[shape] * 2,
        scratch_shapes=[
            pltpu.VMEM(flow_field.shape, flow_field.dtype),
            pltpu.SemaphoreType.DMA((cells_x,)),
        ],
        compiler_params=LARGE,
        name="forward_y",
    )(flow_field)


def flip_core(block):
    return lax.ppermute(block, "gy", [(0, 1), (1, 0)])


def along_columns(blocks, peers):
    arrived = []
    for turn, block in zip(turns(len(blocks)), blocks):
        pairs = [
            (2 * place + core, 2 * (place ^ (2 * turn + core)) + core)
            for place in range(peers)
            for core in range(2)
        ]
        arrived.append(lax.ppermute(block, ("gx", "gy"), pairs))
    return arrived


def small_call(kernel, out_shape, name):
    return pl.pallas_call(kernel, out_shape=out_shape, compiler_params=SMALL, name=name)


def second_kernel(block_ref, out_ref):
    out_ref[...] = block_ref[1]


def second_half(block):
    shape = jax.ShapeDtypeStruct(block.shape[1:], block.dtype)
    return small_call(second_kernel, shape, "second_half")(block)


def add_kernel(keep_ref, arrived_ref, *out_refs):
    for turn, out_ref in enumerate(out_refs):
        out_ref[...] = keep_ref[turn] + arrived_ref[turn]


def add_blocks(keep, arrived):
    shape = jax.ShapeDtypeStruct(keep.shape[1:], keep.dtype)
    return small_call(add_kernel, [shape] * keep.shape[0], "add_blocks")(keep, arrived)


def join_kernel(keep_ref, arrived_ref, *out_refs):
    cells_x, rows, _ = out_refs[0].shape
    rows = rows // 2
    for turn, out_ref in enumerate(out_refs):
        for cell in range(cells_x):
            span = slice(cell * rows, (cell + 1) * rows)
            out_ref[cell] = jnp.concatenate(
                [keep_ref[turn, span, :], arrived_ref[turn, span, :]], axis=0
            )


def join_blocks(keep, arrived, cells_x):
    layers, rows, feat_count = keep.shape
    shape = jax.ShapeDtypeStruct((cells_x, 2 * rows // cells_x, feat_count), keep.dtype)
    return small_call(join_kernel, [shape] * layers, "join_blocks")(keep, arrived)


def back_rows(inverse_high, inverse_low, column, modes):
    high, low = split_terms(modes)
    table = inverse_high[column]
    return dot(table, high) + dot(table, low) + dot(inverse_low[column], high)


def store_turns(out_ref, order_ref, z):
    for index, turn in enumerate(turns(out_ref.shape[0])):
        out_ref[index] = order_ref[z ^ turn]


def mix_kernel(layers, *refs):
    block_refs, arrived_refs = refs[:layers], refs[layers : 2 * layers]
    weight_ref, forward_high, forward_low, inverse_high, inverse_low = refs[
        2 * layers : 2 * layers + 5
    ]
    modes_ref, send_ref, order_ref, spread_ref, result_ref = refs[2 * layers + 5 :]
    z, x, y = quad()
    column = x ^ y
    for index, turn in enumerate(turns(layers)):
        order_ref[(z ^ turn) * 2 + column] = block_refs[index][0]
        order_ref[(z ^ turn) * 2 + (column ^ 1)] = arrived_refs[index][...]
    feat_count = order_ref.shape[-1]
    count = weight_ref.shape[1]
    channels = weight_ref.shape[2]
    tiles = feat_count // 128
    group = 2 * tiles
    high, low = split_terms(order_ref[...].reshape(-1, feat_count))
    spectrum = (
        dot(forward_high[...], high) + dot(forward_high[...], low) + dot(forward_low[...], high)
    )
    for part in range(2):
        for tile in range(tiles):
            spread_ref[pl.ds(part * tiles + tile, count, stride=group), :] = spectrum[
                part * count : (part + 1) * count, tile * 128 : (tile + 1) * 128
            ]
    rows = lax.broadcasted_iota(jnp.int32, (8, 128), 0) % group
    lane = lax.broadcasted_iota(jnp.int32, (8, 128), 1) < channels
    sign = jnp.where(rows < tiles, -1.0, 1.0)
    for base in range(0, count * group, 8):
        block = spread_ref[base : base + 8, :]
        turned = pltpu.roll(block, channels, 1)
        firsts, seconds = [], []
        for start in range(0, 8, group):
            span = slice(start, start + group)
            left = jnp.concatenate([block[span], turned[span]], axis=0)[:, :channels]
            left_high, left_low = split_terms(left)
            left = jnp.concatenate([left_high, left_low], axis=0)
            product = dot(left, weight_ref[0, (base + start) // group])
            product = product[: 2 * group] + product[2 * group :]
            firsts.append(product[:group])
            seconds.append(product[group:])
        first = jnp.concatenate(firsts, axis=0)
        second = jnp.concatenate(seconds, axis=0)
        real = jnp.where(lane, first, pltpu.roll(second, channels, 1))
        imag = jnp.where(lane, pltpu.roll(first, channels, 1), second)
        crossed = jnp.where(rows < tiles, pltpu.roll(imag, 8 - tiles, 0), pltpu.roll(imag, tiles, 0))
        result_ref[base : base + 8, :] = real + sign * crossed
    for part in range(2):
        for tile in range(tiles):
            modes_ref[part * count : (part + 1) * count, tile * 128 : (tile + 1) * 128] = (
                result_ref[pl.ds(part * tiles + tile, count, stride=group), :]
            )
    back = back_rows(inverse_high, inverse_low, column ^ 1, modes_ref[...])
    order_ref[:layers] = back.reshape(send_ref.shape)
    store_turns(send_ref, order_ref, z)


def mix(blocks, arrived, weights, forward_table, inverse_tables):
    layers = len(blocks)
    _, rows, feat_count = blocks[0].shape
    count = weights.shape[1]
    scratch = pltpu.VMEM((count * feat_count // 64, 128), jnp.float32)
    return pl.pallas_call(
        functools.partial(mix_kernel, layers),
        out_shape=[
            jax.ShapeDtypeStruct((2 * count, feat_count), jnp.float32),
            jax.ShapeDtypeStruct((layers, rows, feat_count), jnp.float32),
        ],
        scratch_shapes=[pltpu.VMEM((2 * layers, rows, feat_count), jnp.float32), scratch, scratch],
        compiler_params=SMALL,
        name="mix",
    )(*blocks, *arrived, weights, *split_table(forward_table), *inverse_tables)


def keep_kernel(modes_ref, inverse_high, inverse_low, mixed_ref, keep_ref, order_ref):
    z, x, y = quad()
    count = mixed_ref.shape[1]
    feat_count = modes_ref.shape[1]
    for part in range(2):
        mixed_ref[0, :, part * feat_count : (part + 1) * feat_count] = modes_ref[
            part * count : (part + 1) * count
        ]
    back = back_rows(inverse_high, inverse_low, x ^ y, modes_ref[...])
    order_ref[...] = back.reshape(keep_ref.shape)
    store_turns(keep_ref, order_ref, z)


def keep_rows(modes, inverse_tables, like):
    rows, feat_count = modes.shape
    return pl.pallas_call(
        keep_kernel,
        out_shape=[
            jax.ShapeDtypeStruct((1, rows // 2, 2 * feat_count), jnp.float32),
            jax.ShapeDtypeStruct(like.shape, jnp.float32),
        ],
        scratch_shapes=[pltpu.VMEM(like.shape, jnp.float32)],
        compiler_params=SMALL,
        name="keep_rows",
    )(modes, *inverse_tables)


def gelu(half):
    square = jnp.minimum(half * half, 6.25)
    inner = jnp.full_like(square, GELU_TERMS[-1])
    for term in GELU_TERMS[-2::-1]:
        inner = inner * square + term
    return half + half * jnp.tanh(half * inner)


def output_kernel(layers, flow_ref, table_ref, local_ref, bias_ref, *refs):
    own_refs, core_refs = refs[:layers], refs[layers : 2 * layers]
    out_hbm, order_ref, wide_ref, level_ref, done_ref, sent = refs[2 * layers :]
    cells_x, _, feat_count = flow_ref.shape
    channels = local_ref.shape[0]
    z, x, y = quad()
    wide_ref[...] = jnp.zeros_like(wide_ref)
    for start in range(0, WIDTH, channels):
        span = slice(start, start + channels)
        wide_ref[span, span] = local_ref[...] * 0.5
        level_ref[:, span] = bias_ref[...].reshape(1, channels) * 0.5
    level = level_ref[...]
    levels = []
    for _ in range(BIAS_TERMS):
        levels.append(level.astype(jnp.bfloat16).astype(jnp.float32))
        level = level - levels[-1]
    terms = 3 * order_ref.shape[1] * order_ref.shape[2]
    filled = jnp.zeros((table_ref.shape[-1] - terms - BIAS_TERMS, WIDTH), jnp.float32)
    below = jnp.concatenate(levels + [filled], axis=0).astype(jnp.bfloat16)
    below = jnp.concatenate([below, wide_ref[...]], axis=0)
    for column, block_refs in ((x ^ y, own_refs), (x ^ y ^ 1, core_refs)):
        for turn, block_ref in zip(turns(layers), block_refs):
            order_ref[:, (z ^ turn) * 2 + column] = block_ref[...]
    table = table_ref[y, x ^ y]
    copies = []
    for cell in range(cells_x):
        high, low = split_terms(order_ref[cell].reshape(-1, feat_count))
        stack = jnp.concatenate([high, low, high], axis=0)
        for start in range(0, feat_count, WIDTH):
            columns = slice(start, start + WIDTH)
            total = dot(
                jnp.concatenate([table, flow_ref[cell, :, columns]], axis=1),
                jnp.concatenate([stack[:, columns], below], axis=0),
            )
            done_ref[cell, :, columns] = gelu(total).astype(done_ref.dtype)
        copies.append(pltpu.make_async_copy(done_ref.at[cell], out_hbm.at[cell], sent.at[cell]))
        copies[-1].start()
    for copy in copies:
        copy.wait()


def make_output(flow_field, parts, table, local, bias):
    cells_x, _, feat_count = flow_field.shape
    layers = len(parts) // 2
    return pl.pallas_call(
        functools.partial(output_kernel, layers),
        out_specs=pl.BlockSpec(memory_space=pl.ANY),
        scratch_shapes=[
            pltpu.VMEM((cells_x, 2 * layers) + parts[0].shape[1:], jnp.float32),
            pltpu.VMEM((WIDTH, WIDTH), jnp.bfloat16),
            pltpu.VMEM((1, WIDTH), jnp.float32),
            pltpu.VMEM(flow_field.shape, jnp.bfloat16),
            pltpu.SemaphoreType.DMA((cells_x,)),
        ],
        out_shape=jax.ShapeDtypeStruct(flow_field.shape, jnp.bfloat16),
        compiler_params=SMALL,
        name="make_output",
    )(flow_field, table, local, bias, *parts)


def row_body(flow_field, spectral_weight, local_weight, bias_terms):
    cells_x, cells_y, feat_count = flow_field.shape
    peers = lax.axis_size("gx")
    groups_y = lax.axis_size("gy")
    rows_ky = MY // groups_y // peers
    forward_scale = 1.0 / math.sqrt(cells_x * peers * cells_y * groups_y)
    inverse_scale = 1.0 / math.sqrt(MX * MY)

    send, keep = forward_y(flow_field, cells_y * groups_y, peers // 2, rows_ky)
    blocks = along_columns(add_blocks(keep, flip_core(send)), peers)
    inverse_tables = split_table(inverse_x_table(cells_x, peers, rows_ky))
    modes, send = mix(
        blocks,
        [flip_core(second_half(block)) for block in blocks],
        spectral_weight,
        forward_x_table(cells_x, peers, rows_ky) * forward_scale,
        inverse_tables,
    )
    arrived = flip_core(send)
    mixed, keep = keep_rows(modes, inverse_tables, send)
    own = along_columns(join_blocks(keep, arrived, cells_x), peers)
    parts = own + [flip_core(block) for block in own]
    table = output_table(inverse_y_table(cells_y, groups_y, peers, rows_ky) * (0.5 * inverse_scale))
    return make_output(flow_field, parts, table, local_weight, bias_terms), mixed


def body(flow_field, spectral_weight, local_weight, bias_terms):
    peers = lax.axis_size("gx")
    extent = lax.axis_size("gy") * flow_field.shape[1]
    paired = lax.axis_size("gy") == 2 and peers & (peers - 1) == 0 and extent & (extent - 1) == 0
    if paired and spectral_weight.shape[1] == 2 * MX and WIDTH % local_weight.shape[0] == 0:
        return row_body(flow_field, spectral_weight, local_weight, bias_terms)
    return general_body(flow_field, spectral_weight, local_weight, bias_terms)


def solution(mesh):
    placed = (P(("group", "gx"), "gy", None), P("gy", "gx", None, None), P(), P())
    return jax.shard_map(
        body,
        mesh=mesh,
        in_specs=placed,
        out_specs=(P(("group", "gx"), "gy", None), P(("group", "gy"), "gx", None)),
        check_vma=False,
    )
```

```python
import functools
import math

import jax
import jax.numpy as jnp
import ml_dtypes
import numpy as np
from jax import lax
from jax.experimental import pallas as pl
from jax.experimental.pallas import tpu as pltpu
from jax.sharding import PartitionSpec as P

MX = 32
MY = 32


def wave_number(index, count):
    return jnp.where(index < count // 2, index, index - count)


def phase_table(waves, places, extent):
    product = waves[:, None] * places[None, :] % extent
    return 2.0 * math.pi / extent * product.astype(jnp.float32)


def row_tables(ky_rows, kx_rows, x_places, extent, width):
    angle = phase_table(wave_number(kx_rows, MX), x_places, extent)
    select = (ky_rows[:, None] == jnp.arange(width, dtype=jnp.int32)[None, :]).astype(jnp.float32)
    cosine = jnp.cos(angle)[:, :, None] * select[:, None, :]
    sine_part = jnp.sin(angle)[:, :, None] * select[:, None, :]
    return (cosine, sine_part)


def forward_rows(y_local, ky_rows, kx_rows, x_places, extent):
    cosine, sine_part = row_tables(ky_rows, kx_rows, x_places, extent, y_local.shape[0])
    real_in = y_local[:, 0]
    imag_in = y_local[:, 1]

    def contract(table, values):
        return jnp.einsum("rxk,kxf->rf", table, values, precision=lax.Precision.HIGHEST)

    real_out = contract(cosine, real_in) + contract(sine_part, imag_in)
    imag_out = contract(cosine, imag_in) - contract(sine_part, real_in)
    return jnp.concatenate([real_out, imag_out], axis=1)


def inverse_rows(running, shard_rows, ky_rows, kx_rows, x_places, extent):
    cosine, sine_part = row_tables(ky_rows, kx_rows, x_places, extent, running.shape[0])
    feat_count = shard_rows.shape[1] // 2
    real_part = shard_rows[:, :feat_count]
    imag_part = shard_rows[:, feat_count:]

    def contract(table, values):
        return jnp.einsum("rxk,rf->kxf", table, values, precision=lax.Precision.HIGHEST)

    new_real = contract(cosine, real_part) - contract(sine_part, imag_part)
    new_imag = contract(cosine, imag_part) + contract(sine_part, real_part)
    return jnp.stack([new_real, new_imag], axis=1)


def general_body(flow_field, spectral_weight, local_weight, bias_terms):
    cells_x, cells_y, feat_count = flow_field.shape
    channels = local_weight.shape[0]
    planes = feat_count // channels
    groups_x = lax.axis_size("gx")
    groups_y = lax.axis_size("gy")
    extent_x = cells_x * groups_x
    extent_y = cells_y * groups_y
    half_width = MY // groups_y
    quota_rows = spectral_weight.shape[1]
    high = lax.Precision.HIGHEST
    x_places = lax.axis_index("gx") * cells_x + jnp.arange(cells_x, dtype=jnp.int32)
    y_places = lax.axis_index("gy") * cells_y + jnp.arange(cells_y, dtype=jnp.int32)
    y_angle = phase_table(wave_number(jnp.arange(MY, dtype=jnp.int32), MY), y_places, extent_y)
    y_table = (
        jnp.stack([jnp.cos(y_angle), -jnp.sin(y_angle)], axis=1)
        .reshape(2 * MY, cells_y)
        .astype(jnp.bfloat16)
    )
    y_local = lax.psum_scatter(
        jnp.einsum("qy,xyf->qxf", y_table, flow_field, preferred_element_type=jnp.float32),
        "gy",
        scatter_dimension=0,
        tiled=True,
    )
    y_local = y_local.reshape(half_width, 2, cells_x, feat_count)
    rest_index = jnp.arange(lax.axis_size("gx") * quota_rows, dtype=jnp.int32)
    spectrum = lax.psum_scatter(
        forward_rows(y_local, rest_index // MX, rest_index % MX, x_places, extent_x),
        "gx",
        scatter_dimension=0,
        tiled=True,
    )
    spectrum = spectrum * (1.0 / math.sqrt(extent_x * extent_y))
    coeffs = spectrum.reshape(quota_rows, 2, planes, channels)
    weights = spectral_weight[0].astype(jnp.float32)
    product = jnp.einsum("rpzc,rco->rpzo", coeffs, weights, precision=high)
    mixed_real = product[:, 0, :, :channels] - product[:, 1, :, channels:]
    mixed_imag = product[:, 0, :, channels:] + product[:, 1, :, :channels]
    mixed_local = jnp.stack([mixed_real, mixed_imag], axis=1).reshape(quota_rows, 2 * feat_count)
    pointwise = jnp.einsum(
        "xyzc,co->xyzo",
        flow_field.reshape(cells_x, cells_y, planes, channels),
        local_weight,
        preferred_element_type=jnp.float32,
    )
    start_half = jnp.zeros((half_width, 2, cells_x, feat_count), jnp.float32)
    shard_rows = lax.all_gather(mixed_local, "gx", axis=0, tiled=True)
    rest_index = jnp.arange(shard_rows.shape[0], dtype=jnp.int32)
    back_half = inverse_rows(
        start_half, shard_rows, rest_index // MX, rest_index % MX, x_places, extent_x
    )
    back_whole = lax.all_gather(back_half, "gy", axis=0, tiled=True)
    y_cos = jnp.cos(y_angle)
    y_sin = jnp.sin(y_angle)
    spectral = (
        jnp.einsum("kn,kxf->xnf", y_cos, back_whole[:, 0], precision=high)
        - jnp.einsum("kn,kxf->xnf", y_sin, back_whole[:, 1], precision=high)
    ) * (1.0 / math.sqrt(MX * MY))
    total = spectral.reshape(cells_x, cells_y, planes, channels) + pointwise + bias_terms
    output = (
        jax.nn.gelu(total, approximate=False)
        .reshape(cells_x, cells_y, feat_count)
        .astype(jnp.bfloat16)
    )
    return (output, mixed_local.reshape(1, quota_rows, 2 * feat_count))


SMALL = pltpu.CompilerParams(vmem_limit_bytes=20 * 1024 * 1024)
LARGE = pltpu.CompilerParams(vmem_limit_bytes=53 * 1024 * 1024)
WIDTH = 256
BIAS_TERMS = 3
GELU_TERMS = (
    1.5957645177841187,
    0.29075613617897034,
    -0.0014313592109829187,
    -0.006452994421124458,
    0.0015898864949122071,
    -0.0001365363277727738,
)


def angles(count, places, extent):
    index = np.arange(count)
    waves = np.where(index < count // 2, index, index - count)
    product = (waves[:, None] * np.asarray(places)[None, :]) % extent
    return (np.float32(2.0 * math.pi / extent) * product.astype(np.float32)).astype(np.float64)


def split_table(table):
    high = table.astype(ml_dtypes.bfloat16)
    low = (table - high.astype(np.float64)).astype(ml_dtypes.bfloat16)
    return high, low


def split_terms(values):
    high = values.astype(jnp.bfloat16)
    low = (values - high.astype(jnp.float32)).astype(jnp.bfloat16)
    return high, low


def quad():
    place = lax.axis_index("gx")
    return place // 2, place % 2, lax.axis_index("gy")


def turns(layers, inverse=False):
    half = layers // 2
    if inverse:
        return list(range(half, layers)) + list(range(half - 1, -1, -1))
    return list(range(layers - 1, -1, -1))


def forward_x_table(cells_x, peers, rows_ky):
    extent = cells_x * peers
    angle = angles(MX, np.arange(extent), extent)
    cosine, sine = np.cos(angle), np.sin(angle)
    out = np.zeros((2, rows_ky, MX, extent, rows_ky, 2))
    for row in range(rows_ky):
        out[0, row, :, :, row, 0] = cosine
        out[0, row, :, :, row, 1] = sine
        out[1, row, :, :, row, 1] = cosine
        out[1, row, :, :, row, 0] = -sine
    return out.reshape(2 * rows_ky * MX, extent * rows_ky * 2)


def inverse_x_table(cells_x, peers, rows_ky):
    extent = cells_x * peers
    angle = angles(MX, np.arange(extent), extent)
    cosine, sine = np.cos(angle).T, np.sin(angle).T
    out = np.zeros((extent, rows_ky, 2, 2, rows_ky, MX))
    for row in range(rows_ky):
        out[:, row, 0, 0, row, :] = cosine
        out[:, row, 0, 1, row, :] = -sine
        out[:, row, 1, 1, row, :] = cosine
        out[:, row, 1, 0, row, :] = sine
    out = out.reshape(peers // 2, 2, cells_x * rows_ky * 2, 2 * rows_ky * MX)
    return np.moveaxis(out, 1, 0).reshape(2, -1, 2 * rows_ky * MX)


def inverse_y_table(cells_y, groups_y, peers, rows_ky):
    extent = cells_y * groups_y
    angle = angles(MY, np.arange(extent), extent)
    full = np.stack([np.cos(angle), -np.sin(angle)], axis=1)
    full = full.reshape(groups_y, peers, rows_ky, 2, groups_y, cells_y)
    out = np.zeros((groups_y, 2, cells_y, peers, 2, rows_ky, 2))
    for y in range(groups_y):
        for column in range(2):
            for peer in range(peers):
                for place in range(2):
                    half = y ^ place ^ column ^ (peer % 2)
                    out[y, column, :, peer, place] = np.moveaxis(full[half, peer, :, :, y], -1, 0)
    return out.reshape(groups_y, 2, cells_y, 4 * peers * rows_ky)


def output_table(table):
    high, low = split_table(table)
    parts = [high, high, low, np.ones(table.shape[:-1] + (BIAS_TERMS,), high.dtype)]
    used = 3 * table.shape[-1] + BIAS_TERMS
    parts.append(np.zeros(table.shape[:-1] + (-used % 256,), high.dtype))
    return np.concatenate(parts, axis=-1)


def dot(left, right):
    return jnp.dot(left, right, preferred_element_type=jnp.float32)


def forward_y_table(shape, extent, layers, rows_ky):
    z, x, y = quad()
    peers = 2 * layers
    row = lax.broadcasted_iota(jnp.int32, (shape[0], 1), 0)
    block = row // (2 * rows_ky)
    place = block // 2 % layers
    turn = layers - 1 - place
    side = y ^ (1 - block // peers)
    owner = (side ^ (block % 2)) * peers + (z ^ turn) * 2 + (x ^ side)
    index = owner * rows_ky + row // 2 % rows_ky
    y_places = lax.broadcasted_iota(jnp.int32, (1, shape[1]), 1) + y * shape[1]
    steps = (wave_number(index, MY) * y_places) & (extent - 1)
    angle = 2.0 * math.pi / extent * steps.astype(jnp.float32)
    return jnp.where(row % 2 == 0, jnp.cos(angle), -jnp.sin(angle)).astype(jnp.bfloat16)


def forward_y_kernel(extent, rows_ky, flow_hbm, send_ref, keep_ref, flow_ref, arrived):
    layers, _, rows, feat_count = send_ref.shape
    cells_x, cells_y, _ = flow_ref.shape
    rows = rows // cells_x
    copies = [
        pltpu.make_async_copy(flow_hbm.at[x], flow_ref.at[x], arrived.at[x])
        for x in range(cells_x)
    ]
    for copy in copies:
        copy.start()
    table = forward_y_table((2 * MY, cells_y), extent, layers, rows_ky)
    for x in range(cells_x):
        copies[x].wait()
        result = dot(table, flow_ref[x]).reshape(2, layers, 2, rows, feat_count)
        send_ref[:, :, x * rows : (x + 1) * rows, :] = result[0]
        keep_ref[:, :, x * rows : (x + 1) * rows, :] = result[1]


def forward_y(flow_field, extent, layers, rows_ky):
    cells_x, _, feat_count = flow_field.shape
    shape = jax.ShapeDtypeStruct((layers, 2, cells_x * 2 * rows_ky, feat_count), jnp.float32)
    return pl.pallas_call(
        functools.partial(forward_y_kernel, extent, rows_ky),
        in_specs=[pl.BlockSpec(memory_space=pltpu.HBM)],
        out_shape=[shape] * 2,
        scratch_shapes=[
            pltpu.VMEM(flow_field.shape, flow_field.dtype),
            pltpu.SemaphoreType.DMA((cells_x,)),
        ],
        compiler_params=LARGE,
        name="forward_y",
    )(flow_field)


def flip_core(block):
    return lax.ppermute(block, "gy", [(0, 1), (1, 0)])


def along_columns(blocks, peers, inverse=False):
    arrived = []
    for turn, block in zip(turns(len(blocks), inverse), blocks):
        pairs = [
            (2 * place + core, 2 * (place ^ (2 * turn + core)) + core)
            for place in range(peers)
            for core in range(2)
        ]
        arrived.append(lax.ppermute(block, ("gx", "gy"), pairs))
    return arrived


def small_call(kernel, out_shape, name):
    return pl.pallas_call(kernel, out_shape=out_shape, compiler_params=SMALL, name=name)


def second_kernel(block_ref, out_ref):
    out_ref[...] = block_ref[1]


def second_half(block):
    shape = jax.ShapeDtypeStruct(block.shape[1:], block.dtype)
    return small_call(second_kernel, shape, "second_half")(block)


def add_kernel(keep_ref, arrived_ref, *out_refs):
    for turn, out_ref in enumerate(out_refs):
        out_ref[...] = keep_ref[turn] + arrived_ref[turn]


def add_blocks(keep, arrived):
    shape = jax.ShapeDtypeStruct(keep.shape[1:], keep.dtype)
    return small_call(add_kernel, [shape] * keep.shape[0], "add_blocks")(keep, arrived)


def join_kernel(keep_ref, arrived_ref, *out_refs):
    cells_x, rows, _ = out_refs[0].shape
    rows = rows // 2
    for turn, out_ref in enumerate(out_refs):
        for cell in range(cells_x):
            span = slice(cell * rows, (cell + 1) * rows)
            out_ref[cell] = jnp.concatenate(
                [keep_ref[turn, span, :], arrived_ref[turn, span, :]], axis=0
            )


def join_blocks(keep, arrived, cells_x):
    layers, rows, feat_count = keep.shape
    shape = jax.ShapeDtypeStruct((cells_x, 2 * rows // cells_x, feat_count), keep.dtype)
    return small_call(join_kernel, [shape] * layers, "join_blocks")(keep, arrived)


def back_rows(inverse_high, inverse_low, column, modes):
    high, low = split_terms(modes)
    table = inverse_high[column]
    return dot(table, high) + dot(table, low) + dot(inverse_low[column], high)


def store_turns(out_ref, order_ref, z):
    for index, turn in enumerate(turns(out_ref.shape[0], True)):
        out_ref[index] = order_ref[z ^ turn]


def mix_kernel(layers, *refs):
    block_refs, arrived_refs = refs[:layers], refs[layers : 2 * layers]
    weight_ref, forward_high, forward_low, inverse_high, inverse_low = refs[
        2 * layers : 2 * layers + 5
    ]
    modes_ref, send_ref, order_ref, spread_ref, result_ref = refs[2 * layers + 5 :]
    z, x, y = quad()
    column = x ^ y
    for index, turn in enumerate(turns(layers)):
        order_ref[(z ^ turn) * 2 + column] = block_refs[index][0]
        order_ref[(z ^ turn) * 2 + (column ^ 1)] = arrived_refs[index][...]
    feat_count = order_ref.shape[-1]
    count = weight_ref.shape[1]
    channels = weight_ref.shape[2]
    tiles = feat_count // 128
    group = 2 * tiles
    high, low = split_terms(order_ref[...].reshape(-1, feat_count))
    spectrum = (
        dot(forward_high[...], high) + dot(forward_high[...], low) + dot(forward_low[...], high)
    )
    for part in range(2):
        for tile in range(tiles):
            spread_ref[pl.ds(part * tiles + tile, count, stride=group), :] = spectrum[
                part * count : (part + 1) * count, tile * 128 : (tile + 1) * 128
            ]
    rows = lax.broadcasted_iota(jnp.int32, (8, 128), 0) % group
    lane = lax.broadcasted_iota(jnp.int32, (8, 128), 1) < channels
    sign = jnp.where(rows < tiles, -1.0, 1.0)
    for base in range(0, count * group, 8):
        block = spread_ref[base : base + 8, :]
        turned = pltpu.roll(block, channels, 1)
        firsts, seconds = [], []
        for start in range(0, 8, group):
            span = slice(start, start + group)
            left = jnp.concatenate([block[span], turned[span]], axis=0)[:, :channels]
            left_high, left_low = split_terms(left)
            left = jnp.concatenate([left_high, left_low], axis=0)
            product = dot(left, weight_ref[0, (base + start) // group])
            product = product[: 2 * group] + product[2 * group :]
            firsts.append(product[:group])
            seconds.append(product[group:])
        first = jnp.concatenate(firsts, axis=0)
        second = jnp.concatenate(seconds, axis=0)
        real = jnp.where(lane, first, pltpu.roll(second, channels, 1))
        imag = jnp.where(lane, pltpu.roll(first, channels, 1), second)
        crossed = jnp.where(rows < tiles, pltpu.roll(imag, 8 - tiles, 0), pltpu.roll(imag, tiles, 0))
        result_ref[base : base + 8, :] = real + sign * crossed
    for part in range(2):
        for tile in range(tiles):
            modes_ref[part * count : (part + 1) * count, tile * 128 : (tile + 1) * 128] = (
                result_ref[pl.ds(part * tiles + tile, count, stride=group), :]
            )
    back = back_rows(inverse_high, inverse_low, column ^ 1, modes_ref[...])
    order_ref[:layers] = back.reshape(send_ref.shape)
    store_turns(send_ref, order_ref, z)


def mix(blocks, arrived, weights, forward_table, inverse_tables):
    layers = len(blocks)
    _, rows, feat_count = blocks[0].shape
    count = weights.shape[1]
    scratch = pltpu.VMEM((count * feat_count // 64, 128), jnp.float32)
    return pl.pallas_call(
        functools.partial(mix_kernel, layers),
        out_shape=[
            jax.ShapeDtypeStruct((2 * count, feat_count), jnp.float32),
            jax.ShapeDtypeStruct((layers, rows, feat_count), jnp.float32),
        ],
        scratch_shapes=[pltpu.VMEM((2 * layers, rows, feat_count), jnp.float32), scratch, scratch],
        compiler_params=SMALL,
        name="mix",
    )(*blocks, *arrived, weights, *split_table(forward_table), *inverse_tables)


def keep_kernel(modes_ref, inverse_high, inverse_low, mixed_ref, keep_ref, order_ref):
    z, x, y = quad()
    count = mixed_ref.shape[1]
    feat_count = modes_ref.shape[1]
    for part in range(2):
        mixed_ref[0, :, part * feat_count : (part + 1) * feat_count] = modes_ref[
            part * count : (part + 1) * count
        ]
    back = back_rows(inverse_high, inverse_low, x ^ y, modes_ref[...])
    order_ref[...] = back.reshape(keep_ref.shape)
    store_turns(keep_ref, order_ref, z)


def keep_rows(modes, inverse_tables, like):
    rows, feat_count = modes.shape
    return pl.pallas_call(
        keep_kernel,
        out_shape=[
            jax.ShapeDtypeStruct((1, rows // 2, 2 * feat_count), jnp.float32),
            jax.ShapeDtypeStruct(like.shape, jnp.float32),
        ],
        scratch_shapes=[pltpu.VMEM(like.shape, jnp.float32)],
        compiler_params=SMALL,
        name="keep_rows",
    )(modes, *inverse_tables)


def gelu(half):
    square = jnp.minimum(half * half, 6.25)
    inner = jnp.full_like(square, GELU_TERMS[-1])
    for term in GELU_TERMS[-2::-1]:
        inner = inner * square + term
    return half + half * jnp.tanh(half * inner)


def output_kernel(layers, flow_ref, table_ref, local_ref, bias_ref, *refs):
    own_refs, core_refs = refs[:layers], refs[layers : 2 * layers]
    out_hbm, order_ref, wide_ref, level_ref, done_ref, sent = refs[2 * layers :]
    cells_x, _, feat_count = flow_ref.shape
    channels = local_ref.shape[0]
    z, x, y = quad()
    wide_ref[...] = jnp.zeros_like(wide_ref)
    for start in range(0, WIDTH, channels):
        span = slice(start, start + channels)
        wide_ref[span, span] = local_ref[...] * 0.5
        level_ref[:, span] = bias_ref[...].reshape(1, channels) * 0.5
    level = level_ref[...]
    levels = []
    for _ in range(BIAS_TERMS):
        levels.append(level.astype(jnp.bfloat16).astype(jnp.float32))
        level = level - levels[-1]
    terms = 3 * order_ref.shape[1] * order_ref.shape[2]
    filled = jnp.zeros((table_ref.shape[-1] - terms - BIAS_TERMS, WIDTH), jnp.float32)
    below = jnp.concatenate(levels + [filled], axis=0).astype(jnp.bfloat16)
    below = jnp.concatenate([below, wide_ref[...]], axis=0)
    for column, block_refs in ((x ^ y, own_refs), (x ^ y ^ 1, core_refs)):
        for turn, block_ref in zip(turns(layers, True), block_refs):
            order_ref[:, (z ^ turn) * 2 + column] = block_ref[...]
    table = table_ref[y, x ^ y]
    copies = []
    for cell in range(cells_x):
        high, low = split_terms(order_ref[cell].reshape(-1, feat_count))
        stack = jnp.concatenate([high, low, high], axis=0)
        for start in range(0, feat_count, WIDTH):
            columns = slice(start, start + WIDTH)
            total = dot(
                jnp.concatenate([table, flow_ref[cell, :, columns]], axis=1),
                jnp.concatenate([stack[:, columns], below], axis=0),
            )
            done_ref[cell, :, columns] = gelu(total).astype(done_ref.dtype)
        copies.append(pltpu.make_async_copy(done_ref.at[cell], out_hbm.at[cell], sent.at[cell]))
        copies[-1].start()
    for copy in copies:
        copy.wait()


def make_output(flow_field, parts, table, local, bias):
    cells_x, _, feat_count = flow_field.shape
    layers = len(parts) // 2
    return pl.pallas_call(
        functools.partial(output_kernel, layers),
        out_specs=pl.BlockSpec(memory_space=pl.ANY),
        scratch_shapes=[
            pltpu.VMEM((cells_x, 2 * layers) + parts[0].shape[1:], jnp.float32),
            pltpu.VMEM((WIDTH, WIDTH), jnp.bfloat16),
            pltpu.VMEM((1, WIDTH), jnp.float32),
            pltpu.VMEM(flow_field.shape, jnp.bfloat16),
            pltpu.SemaphoreType.DMA((cells_x,)),
        ],
        out_shape=jax.ShapeDtypeStruct(flow_field.shape, jnp.bfloat16),
        compiler_params=SMALL,
        name="make_output",
    )(flow_field, table, local, bias, *parts)


def row_body(flow_field, spectral_weight, local_weight, bias_terms):
    cells_x, cells_y, feat_count = flow_field.shape
    peers = lax.axis_size("gx")
    groups_y = lax.axis_size("gy")
    rows_ky = MY // groups_y // peers
    forward_scale = 1.0 / math.sqrt(cells_x * peers * cells_y * groups_y)
    inverse_scale = 1.0 / math.sqrt(MX * MY)

    send, keep = forward_y(flow_field, cells_y * groups_y, peers // 2, rows_ky)
    blocks = along_columns(add_blocks(keep, flip_core(send)), peers)
    inverse_tables = split_table(inverse_x_table(cells_x, peers, rows_ky))
    modes, send = mix(
        blocks,
        [flip_core(second_half(block)) for block in blocks],
        spectral_weight,
        forward_x_table(cells_x, peers, rows_ky) * forward_scale,
        inverse_tables,
    )
    arrived = flip_core(send)
    mixed, keep = keep_rows(modes, inverse_tables, send)
    own = along_columns(join_blocks(keep, arrived, cells_x), peers, True)
    parts = own + [flip_core(block) for block in own]
    table = output_table(inverse_y_table(cells_y, groups_y, peers, rows_ky) * (0.5 * inverse_scale))
    return make_output(flow_field, parts, table, local_weight, bias_terms), mixed


def body(flow_field, spectral_weight, local_weight, bias_terms):
    peers = lax.axis_size("gx")
    extent = lax.axis_size("gy") * flow_field.shape[1]
    paired = lax.axis_size("gy") == 2 and peers & (peers - 1) == 0 and extent & (extent - 1) == 0
    if paired and spectral_weight.shape[1] == 2 * MX and WIDTH % local_weight.shape[0] == 0:
        return row_body(flow_field, spectral_weight, local_weight, bias_terms)
    return general_body(flow_field, spectral_weight, local_weight, bias_terms)


def solution(mesh):
    placed = (P(("group", "gx"), "gy", None), P("gy", "gx", None, None), P(), P())
    return jax.shard_map(
        body,
        mesh=mesh,
        in_specs=placed,
        out_specs=(P(("group", "gx"), "gy", None), P(("group", "gy"), "gx", None)),
        check_vma=False,
    )
```

```python
import functools
import math

import jax
import jax.numpy as jnp
import ml_dtypes
import numpy as np
from jax import lax
from jax.experimental import pallas as pl
from jax.experimental.pallas import tpu as pltpu
from jax.sharding import PartitionSpec as P

MX = 32
MY = 32


def wave_number(index, count):
    return jnp.where(index < count // 2, index, index - count)


def phase_table(waves, places, extent):
    product = waves[:, None] * places[None, :] % extent
    return 2.0 * math.pi / extent * product.astype(jnp.float32)


def row_tables(ky_rows, kx_rows, x_places, extent, width):
    angle = phase_table(wave_number(kx_rows, MX), x_places, extent)
    select = (ky_rows[:, None] == jnp.arange(width, dtype=jnp.int32)[None, :]).astype(jnp.float32)
    cosine = jnp.cos(angle)[:, :, None] * select[:, None, :]
    sine_part = jnp.sin(angle)[:, :, None] * select[:, None, :]
    return (cosine, sine_part)


def forward_rows(y_local, ky_rows, kx_rows, x_places, extent):
    cosine, sine_part = row_tables(ky_rows, kx_rows, x_places, extent, y_local.shape[0])
    real_in = y_local[:, 0]
    imag_in = y_local[:, 1]

    def contract(table, values):
        return jnp.einsum("rxk,kxf->rf", table, values, precision=lax.Precision.HIGHEST)

    real_out = contract(cosine, real_in) + contract(sine_part, imag_in)
    imag_out = contract(cosine, imag_in) - contract(sine_part, real_in)
    return jnp.concatenate([real_out, imag_out], axis=1)


def inverse_rows(running, shard_rows, ky_rows, kx_rows, x_places, extent):
    cosine, sine_part = row_tables(ky_rows, kx_rows, x_places, extent, running.shape[0])
    feat_count = shard_rows.shape[1] // 2
    real_part = shard_rows[:, :feat_count]
    imag_part = shard_rows[:, feat_count:]

    def contract(table, values):
        return jnp.einsum("rxk,rf->kxf", table, values, precision=lax.Precision.HIGHEST)

    new_real = contract(cosine, real_part) - contract(sine_part, imag_part)
    new_imag = contract(cosine, imag_part) + contract(sine_part, real_part)
    return jnp.stack([new_real, new_imag], axis=1)


def general_body(flow_field, spectral_weight, local_weight, bias_terms):
    cells_x, cells_y, feat_count = flow_field.shape
    channels = local_weight.shape[0]
    planes = feat_count // channels
    groups_x = lax.axis_size("gx")
    groups_y = lax.axis_size("gy")
    extent_x = cells_x * groups_x
    extent_y = cells_y * groups_y
    half_width = MY // groups_y
    quota_rows = spectral_weight.shape[1]
    high = lax.Precision.HIGHEST
    x_places = lax.axis_index("gx") * cells_x + jnp.arange(cells_x, dtype=jnp.int32)
    y_places = lax.axis_index("gy") * cells_y + jnp.arange(cells_y, dtype=jnp.int32)
    y_angle = phase_table(wave_number(jnp.arange(MY, dtype=jnp.int32), MY), y_places, extent_y)
    y_table = (
        jnp.stack([jnp.cos(y_angle), -jnp.sin(y_angle)], axis=1)
        .reshape(2 * MY, cells_y)
        .astype(jnp.bfloat16)
    )
    y_local = lax.psum_scatter(
        jnp.einsum("qy,xyf->qxf", y_table, flow_field, preferred_element_type=jnp.float32),
        "gy",
        scatter_dimension=0,
        tiled=True,
    )
    y_local = y_local.reshape(half_width, 2, cells_x, feat_count)
    rest_index = jnp.arange(lax.axis_size("gx") * quota_rows, dtype=jnp.int32)
    spectrum = lax.psum_scatter(
        forward_rows(y_local, rest_index // MX, rest_index % MX, x_places, extent_x),
        "gx",
        scatter_dimension=0,
        tiled=True,
    )
    spectrum = spectrum * (1.0 / math.sqrt(extent_x * extent_y))
    coeffs = spectrum.reshape(quota_rows, 2, planes, channels)
    weights = spectral_weight[0].astype(jnp.float32)
    product = jnp.einsum("rpzc,rco->rpzo", coeffs, weights, precision=high)
    mixed_real = product[:, 0, :, :channels] - product[:, 1, :, channels:]
    mixed_imag = product[:, 0, :, channels:] + product[:, 1, :, :channels]
    mixed_local = jnp.stack([mixed_real, mixed_imag], axis=1).reshape(quota_rows, 2 * feat_count)
    pointwise = jnp.einsum(
        "xyzc,co->xyzo",
        flow_field.reshape(cells_x, cells_y, planes, channels),
        local_weight,
        preferred_element_type=jnp.float32,
    )
    start_half = jnp.zeros((half_width, 2, cells_x, feat_count), jnp.float32)
    shard_rows = lax.all_gather(mixed_local, "gx", axis=0, tiled=True)
    rest_index = jnp.arange(shard_rows.shape[0], dtype=jnp.int32)
    back_half = inverse_rows(
        start_half, shard_rows, rest_index // MX, rest_index % MX, x_places, extent_x
    )
    back_whole = lax.all_gather(back_half, "gy", axis=0, tiled=True)
    y_cos = jnp.cos(y_angle)
    y_sin = jnp.sin(y_angle)
    spectral = (
        jnp.einsum("kn,kxf->xnf", y_cos, back_whole[:, 0], precision=high)
        - jnp.einsum("kn,kxf->xnf", y_sin, back_whole[:, 1], precision=high)
    ) * (1.0 / math.sqrt(MX * MY))
    total = spectral.reshape(cells_x, cells_y, planes, channels) + pointwise + bias_terms
    output = (
        jax.nn.gelu(total, approximate=False)
        .reshape(cells_x, cells_y, feat_count)
        .astype(jnp.bfloat16)
    )
    return (output, mixed_local.reshape(1, quota_rows, 2 * feat_count))


SMALL = pltpu.CompilerParams(vmem_limit_bytes=20 * 1024 * 1024)
LARGE = pltpu.CompilerParams(vmem_limit_bytes=53 * 1024 * 1024)
WIDTH = 256
BIAS_TERMS = 3
GELU_TERMS = (
    1.5957645177841187,
    0.29075613617897034,
    -0.0014313592109829187,
    -0.006452994421124458,
    0.0015898864949122071,
    -0.0001365363277727738,
)


def angles(count, places, extent):
    index = np.arange(count)
    waves = np.where(index < count // 2, index, index - count)
    product = (waves[:, None] * np.asarray(places)[None, :]) % extent
    return (np.float32(2.0 * math.pi / extent) * product.astype(np.float32)).astype(np.float64)


def split_table(table):
    high = table.astype(ml_dtypes.bfloat16)
    low = (table - high.astype(np.float64)).astype(ml_dtypes.bfloat16)
    return high, low


def split_terms(values):
    high = values.astype(jnp.bfloat16)
    low = (values - high.astype(jnp.float32)).astype(jnp.bfloat16)
    return high, low


def quad():
    place = lax.axis_index("gx")
    return place // 2, place % 2, lax.axis_index("gy")


def turns(layers):
    half = layers // 2
    return list(range(half, 0, -1)) + list(range(half + 1, layers)) + [0]


def forward_x_table(cells_x, peers, rows_ky):
    extent = cells_x * peers
    angle = angles(MX, np.arange(extent), extent)
    cosine, sine = np.cos(angle), np.sin(angle)
    out = np.zeros((2, rows_ky, MX, extent, rows_ky, 2))
    for row in range(rows_ky):
        out[0, row, :, :, row, 0] = cosine
        out[0, row, :, :, row, 1] = sine
        out[1, row, :, :, row, 1] = cosine
        out[1, row, :, :, row, 0] = -sine
    return out.reshape(2 * rows_ky * MX, extent * rows_ky * 2)


def inverse_x_table(cells_x, peers, rows_ky):
    extent = cells_x * peers
    angle = angles(MX, np.arange(extent), extent)
    cosine, sine = np.cos(angle).T, np.sin(angle).T
    out = np.zeros((extent, rows_ky, 2, 2, rows_ky, MX))
    for row in range(rows_ky):
        out[:, row, 0, 0, row, :] = cosine
        out[:, row, 0, 1, row, :] = -sine
        out[:, row, 1, 1, row, :] = cosine
        out[:, row, 1, 0, row, :] = sine
    out = out.reshape(peers // 2, 2, cells_x * rows_ky * 2, 2 * rows_ky * MX)
    return np.moveaxis(out, 1, 0).reshape(2, -1, 2 * rows_ky * MX)


def inverse_y_table(cells_y, groups_y, peers, rows_ky):
    extent = cells_y * groups_y
    angle = angles(MY, np.arange(extent), extent)
    full = np.stack([np.cos(angle), -np.sin(angle)], axis=1)
    full = full.reshape(groups_y, peers, rows_ky, 2, groups_y, cells_y)
    out = np.zeros((groups_y, 2, cells_y, peers, 2, rows_ky, 2))
    for y in range(groups_y):
        for column in range(2):
            for peer in range(peers):
                for place in range(2):
                    half = y ^ place ^ column ^ (peer % 2)
                    out[y, column, :, peer, place] = np.moveaxis(full[half, peer, :, :, y], -1, 0)
    return out.reshape(groups_y, 2, cells_y, 4 * peers * rows_ky)


def output_table(table):
    high, low = split_table(table)
    parts = [high, high, low, np.ones(table.shape[:-1] + (BIAS_TERMS,), high.dtype)]
    used = 3 * table.shape[-1] + BIAS_TERMS
    parts.append(np.zeros(table.shape[:-1] + (-used % 256,), high.dtype))
    return np.concatenate(parts, axis=-1)


def dot(left, right):
    return jnp.dot(left, right, preferred_element_type=jnp.float32)


def forward_y_table(shape, extent, layers, rows_ky):
    z, x, y = quad()
    peers = 2 * layers
    row = lax.broadcasted_iota(jnp.int32, (shape[0], 1), 0)
    block = row // (2 * rows_ky)
    place = block // 2 % layers
    turn = jnp.where(place < layers // 2, layers // 2 - place, (place + 1) % layers)
    side = y ^ (1 - block // peers)
    owner = (side ^ (block % 2)) * peers + (z ^ turn) * 2 + (x ^ side)
    index = owner * rows_ky + row // 2 % rows_ky
    y_places = lax.broadcasted_iota(jnp.int32, (1, shape[1]), 1) + y * shape[1]
    steps = (wave_number(index, MY) * y_places) & (extent - 1)
    angle = 2.0 * math.pi / extent * steps.astype(jnp.float32)
    return jnp.where(row % 2 == 0, jnp.cos(angle), -jnp.sin(angle)).astype(jnp.bfloat16)


def forward_y_kernel(extent, rows_ky, flow_hbm, send_ref, keep_ref, flow_ref, arrived):
    layers, _, rows, feat_count = send_ref.shape
    cells_x, cells_y, _ = flow_ref.shape
    rows = rows // cells_x
    copies = [
        pltpu.make_async_copy(flow_hbm.at[x], flow_ref.at[x], arrived.at[x])
        for x in range(cells_x)
    ]
    for copy in copies:
        copy.start()
    table = forward_y_table((2 * MY, cells_y), extent, layers, rows_ky)
    for x in range(cells_x):
        copies[x].wait()
        result = dot(table, flow_ref[x]).reshape(2, layers, 2, rows, feat_count)
        send_ref[:, :, x * rows : (x + 1) * rows, :] = result[0]
        keep_ref[:, :, x * rows : (x + 1) * rows, :] = result[1]


def forward_y(flow_field, extent, layers, rows_ky):
    cells_x, _, feat_count = flow_field.shape
    shape = jax.ShapeDtypeStruct((layers, 2, cells_x * 2 * rows_ky, feat_count), jnp.float32)
    return pl.pallas_call(
        functools.partial(forward_y_kernel, extent, rows_ky),
        in_specs=[pl.BlockSpec(memory_space=pltpu.HBM)],
        out_shape=[shape] * 2,
        scratch_shapes=[
            pltpu.VMEM(flow_field.shape, flow_field.dtype),
            pltpu.SemaphoreType.DMA((cells_x,)),
        ],
        compiler_params=LARGE,
        name="forward_y",
    )(flow_field)


def flip_core(block):
    return lax.ppermute(block, "gy", [(0, 1), (1, 0)])


def along_columns(blocks, peers):
    arrived = []
    for turn, block in zip(turns(len(blocks)), blocks):
        pairs = [
            (2 * place + core, 2 * (place ^ (2 * turn + core)) + core)
            for place in range(peers)
            for core in range(2)
        ]
        arrived.append(lax.ppermute(block, ("gx", "gy"), pairs))
    return arrived


def small_call(kernel, out_shape, name):
    return pl.pallas_call(kernel, out_shape=out_shape, compiler_params=SMALL, name=name)


def second_kernel(block_ref, out_ref):
    out_ref[...] = block_ref[1]


def second_half(block):
    shape = jax.ShapeDtypeStruct(block.shape[1:], block.dtype)
    return small_call(second_kernel, shape, "second_half")(block)


def add_kernel(keep_ref, arrived_ref, *out_refs):
    for turn, out_ref in enumerate(out_refs):
        out_ref[...] = keep_ref[turn] + arrived_ref[turn]


def add_blocks(keep, arrived):
    shape = jax.ShapeDtypeStruct(keep.shape[1:], keep.dtype)
    return small_call(add_kernel, [shape] * keep.shape[0], "add_blocks")(keep, arrived)


def join_kernel(keep_ref, arrived_ref, *out_refs):
    cells_x, rows, _ = out_refs[0].shape
    rows = rows // 2
    for turn, out_ref in enumerate(out_refs):
        for cell in range(cells_x):
            span = slice(cell * rows, (cell + 1) * rows)
            out_ref[cell] = jnp.concatenate(
                [keep_ref[turn, span, :], arrived_ref[turn, span, :]], axis=0
            )


def join_blocks(keep, arrived, cells_x):
    layers, rows, feat_count = keep.shape
    shape = jax.ShapeDtypeStruct((cells_x, 2 * rows // cells_x, feat_count), keep.dtype)
    return small_call(join_kernel, [shape] * layers, "join_blocks")(keep, arrived)


def back_rows(inverse_high, inverse_low, column, modes):
    high, low = split_terms(modes)
    table = inverse_high[column]
    return dot(table, high) + dot(table, low) + dot(inverse_low[column], high)


def store_turns(out_ref, order_ref, z):
    for index, turn in enumerate(turns(out_ref.shape[0])):
        out_ref[index] = order_ref[z ^ turn]


def mix_kernel(layers, *refs):
    block_refs, arrived_refs = refs[:layers], refs[layers : 2 * layers]
    weight_ref, forward_high, forward_low, inverse_high, inverse_low = refs[
        2 * layers : 2 * layers + 5
    ]
    modes_ref, send_ref, order_ref, spread_ref, result_ref = refs[2 * layers + 5 :]
    z, x, y = quad()
    column = x ^ y
    for index, turn in enumerate(turns(layers)):
        order_ref[(z ^ turn) * 2 + column] = block_refs[index][0]
        order_ref[(z ^ turn) * 2 + (column ^ 1)] = arrived_refs[index][...]
    feat_count = order_ref.shape[-1]
    count = weight_ref.shape[1]
    channels = weight_ref.shape[2]
    tiles = feat_count // 128
    group = 2 * tiles
    high, low = split_terms(order_ref[...].reshape(-1, feat_count))
    spectrum = (
        dot(forward_high[...], high) + dot(forward_high[...], low) + dot(forward_low[...], high)
    )
    for part in range(2):
        for tile in range(tiles):
            spread_ref[pl.ds(part * tiles + tile, count, stride=group), :] = spectrum[
                part * count : (part + 1) * count, tile * 128 : (tile + 1) * 128
            ]
    rows = lax.broadcasted_iota(jnp.int32, (8, 128), 0) % group
    lane = lax.broadcasted_iota(jnp.int32, (8, 128), 1) < channels
    sign = jnp.where(rows < tiles, -1.0, 1.0)
    for base in range(0, count * group, 8):
        block = spread_ref[base : base + 8, :]
        turned = pltpu.roll(block, channels, 1)
        firsts, seconds = [], []
        for start in range(0, 8, group):
            span = slice(start, start + group)
            left = jnp.concatenate([block[span], turned[span]], axis=0)[:, :channels]
            left_high, left_low = split_terms(left)
            left = jnp.concatenate([left_high, left_low], axis=0)
            product = dot(left, weight_ref[0, (base + start) // group])
            product = product[: 2 * group] + product[2 * group :]
            firsts.append(product[:group])
            seconds.append(product[group:])
        first = jnp.concatenate(firsts, axis=0)
        second = jnp.concatenate(seconds, axis=0)
        real = jnp.where(lane, first, pltpu.roll(second, channels, 1))
        imag = jnp.where(lane, pltpu.roll(first, channels, 1), second)
        crossed = jnp.where(rows < tiles, pltpu.roll(imag, 8 - tiles, 0), pltpu.roll(imag, tiles, 0))
        result_ref[base : base + 8, :] = real + sign * crossed
    for part in range(2):
        for tile in range(tiles):
            modes_ref[part * count : (part + 1) * count, tile * 128 : (tile + 1) * 128] = (
                result_ref[pl.ds(part * tiles + tile, count, stride=group), :]
            )
    back = back_rows(inverse_high, inverse_low, column ^ 1, modes_ref[...])
    order_ref[:layers] = back.reshape(send_ref.shape)
    store_turns(send_ref, order_ref, z)


def mix(blocks, arrived, weights, forward_table, inverse_tables):
    layers = len(blocks)
    _, rows, feat_count = blocks[0].shape
    count = weights.shape[1]
    scratch = pltpu.VMEM((count * feat_count // 64, 128), jnp.float32)
    return pl.pallas_call(
        functools.partial(mix_kernel, layers),
        out_shape=[
            jax.ShapeDtypeStruct((2 * count, feat_count), jnp.float32),
            jax.ShapeDtypeStruct((layers, rows, feat_count), jnp.float32),
        ],
        scratch_shapes=[pltpu.VMEM((2 * layers, rows, feat_count), jnp.float32), scratch, scratch],
        compiler_params=SMALL,
        name="mix",
    )(*blocks, *arrived, weights, *split_table(forward_table), *inverse_tables)


def keep_kernel(modes_ref, inverse_high, inverse_low, mixed_ref, keep_ref, order_ref):
    z, x, y = quad()
    count = mixed_ref.shape[1]
    feat_count = modes_ref.shape[1]
    for part in range(2):
        mixed_ref[0, :, part * feat_count : (part + 1) * feat_count] = modes_ref[
            part * count : (part + 1) * count
        ]
    back = back_rows(inverse_high, inverse_low, x ^ y, modes_ref[...])
    order_ref[...] = back.reshape(keep_ref.shape)
    store_turns(keep_ref, order_ref, z)


def keep_rows(modes, inverse_tables, like):
    rows, feat_count = modes.shape
    return pl.pallas_call(
        keep_kernel,
        out_shape=[
            jax.ShapeDtypeStruct((1, rows // 2, 2 * feat_count), jnp.float32),
            jax.ShapeDtypeStruct(like.shape, jnp.float32),
        ],
        scratch_shapes=[pltpu.VMEM(like.shape, jnp.float32)],
        compiler_params=SMALL,
        name="keep_rows",
    )(modes, *inverse_tables)


def gelu(half):
    square = jnp.minimum(half * half, 6.25)
    inner = jnp.full_like(square, GELU_TERMS[-1])
    for term in GELU_TERMS[-2::-1]:
        inner = inner * square + term
    return half + half * jnp.tanh(half * inner)


def output_kernel(layers, flow_ref, table_ref, local_ref, bias_ref, *refs):
    own_refs, core_refs = refs[:layers], refs[layers : 2 * layers]
    out_hbm, order_ref, wide_ref, level_ref, done_ref, sent = refs[2 * layers :]
    cells_x, _, feat_count = flow_ref.shape
    channels = local_ref.shape[0]
    z, x, y = quad()
    wide_ref[...] = jnp.zeros_like(wide_ref)
    for start in range(0, WIDTH, channels):
        span = slice(start, start + channels)
        wide_ref[span, span] = local_ref[...] * 0.5
        level_ref[:, span] = bias_ref[...].reshape(1, channels) * 0.5
    level = level_ref[...]
    levels = []
    for _ in range(BIAS_TERMS):
        levels.append(level.astype(jnp.bfloat16).astype(jnp.float32))
        level = level - levels[-1]
    terms = 3 * order_ref.shape[1] * order_ref.shape[2]
    filled = jnp.zeros((table_ref.shape[-1] - terms - BIAS_TERMS, WIDTH), jnp.float32)
    below = jnp.concatenate(levels + [filled], axis=0).astype(jnp.bfloat16)
    below = jnp.concatenate([below, wide_ref[...]], axis=0)
    for column, block_refs in ((x ^ y, own_refs), (x ^ y ^ 1, core_refs)):
        for turn, block_ref in zip(turns(layers), block_refs):
            order_ref[:, (z ^ turn) * 2 + column] = block_ref[...]
    table = table_ref[y, x ^ y]
    copies = []
    for cell in range(cells_x):
        high, low = split_terms(order_ref[cell].reshape(-1, feat_count))
        stack = jnp.concatenate([high, low, high], axis=0)
        for start in range(0, feat_count, WIDTH):
            columns = slice(start, start + WIDTH)
            total = dot(
                jnp.concatenate([table, flow_ref[cell, :, columns]], axis=1),
                jnp.concatenate([stack[:, columns], below], axis=0),
            )
            done_ref[cell, :, columns] = gelu(total).astype(done_ref.dtype)
        copies.append(pltpu.make_async_copy(done_ref.at[cell], out_hbm.at[cell], sent.at[cell]))
        copies[-1].start()
    for copy in copies:
        copy.wait()


def make_output(flow_field, parts, table, local, bias):
    cells_x, _, feat_count = flow_field.shape
    layers = len(parts) // 2
    return pl.pallas_call(
        functools.partial(output_kernel, layers),
        out_specs=pl.BlockSpec(memory_space=pl.ANY),
        scratch_shapes=[
            pltpu.VMEM((cells_x, 2 * layers) + parts[0].shape[1:], jnp.float32),
            pltpu.VMEM((WIDTH, WIDTH), jnp.bfloat16),
            pltpu.VMEM((1, WIDTH), jnp.float32),
            pltpu.VMEM(flow_field.shape, jnp.bfloat16),
            pltpu.SemaphoreType.DMA((cells_x,)),
        ],
        out_shape=jax.ShapeDtypeStruct(flow_field.shape, jnp.bfloat16),
        compiler_params=SMALL,
        name="make_output",
    )(flow_field, table, local, bias, *parts)


def row_body(flow_field, spectral_weight, local_weight, bias_terms):
    cells_x, cells_y, feat_count = flow_field.shape
    peers = lax.axis_size("gx")
    groups_y = lax.axis_size("gy")
    rows_ky = MY // groups_y // peers
    forward_scale = 1.0 / math.sqrt(cells_x * peers * cells_y * groups_y)
    inverse_scale = 1.0 / math.sqrt(MX * MY)

    send, keep = forward_y(flow_field, cells_y * groups_y, peers // 2, rows_ky)
    blocks = along_columns(add_blocks(keep, flip_core(send)), peers)
    inverse_tables = split_table(inverse_x_table(cells_x, peers, rows_ky))
    modes, send = mix(
        blocks,
        [flip_core(second_half(block)) for block in blocks],
        spectral_weight,
        forward_x_table(cells_x, peers, rows_ky) * forward_scale,
        inverse_tables,
    )
    arrived = flip_core(send)
    mixed, keep = keep_rows(modes, inverse_tables, send)
    own = along_columns(join_blocks(keep, arrived, cells_x), peers)
    parts = own + [flip_core(block) for block in own]
    table = output_table(inverse_y_table(cells_y, groups_y, peers, rows_ky) * (0.5 * inverse_scale))
    return make_output(flow_field, parts, table, local_weight, bias_terms), mixed


def body(flow_field, spectral_weight, local_weight, bias_terms):
    peers = lax.axis_size("gx")
    extent = lax.axis_size("gy") * flow_field.shape[1]
    paired = lax.axis_size("gy") == 2 and peers & (peers - 1) == 0 and extent & (extent - 1) == 0
    if paired and spectral_weight.shape[1] == 2 * MX and WIDTH % local_weight.shape[0] == 0:
        return row_body(flow_field, spectral_weight, local_weight, bias_terms)
    return general_body(flow_field, spectral_weight, local_weight, bias_terms)


def solution(mesh):
    placed = (P(("group", "gx"), "gy", None), P("gy", "gx", None, None), P(), P())
    return jax.shard_map(
        body,
        mesh=mesh,
        in_specs=placed,
        out_specs=(P(("group", "gx"), "gy", None), P(("group", "gy"), "gx", None)),
        check_vma=False,
    )
```

```python
import functools
import math

import jax
import jax.numpy as jnp
import ml_dtypes
import numpy as np
from jax import lax
from jax.experimental import pallas as pl
from jax.experimental.pallas import tpu as pltpu
from jax.sharding import PartitionSpec as P

MX = 32
MY = 32


def wave_number(index, count):
    return jnp.where(index < count // 2, index, index - count)


def phase_table(waves, places, extent):
    product = waves[:, None] * places[None, :] % extent
    return 2.0 * math.pi / extent * product.astype(jnp.float32)


def row_tables(ky_rows, kx_rows, x_places, extent, width):
    angle = phase_table(wave_number(kx_rows, MX), x_places, extent)
    select = (ky_rows[:, None] == jnp.arange(width, dtype=jnp.int32)[None, :]).astype(jnp.float32)
    cosine = jnp.cos(angle)[:, :, None] * select[:, None, :]
    sine_part = jnp.sin(angle)[:, :, None] * select[:, None, :]
    return (cosine, sine_part)


def forward_rows(y_local, ky_rows, kx_rows, x_places, extent):
    cosine, sine_part = row_tables(ky_rows, kx_rows, x_places, extent, y_local.shape[0])
    real_in = y_local[:, 0]
    imag_in = y_local[:, 1]

    def contract(table, values):
        return jnp.einsum("rxk,kxf->rf", table, values, precision=lax.Precision.HIGHEST)

    real_out = contract(cosine, real_in) + contract(sine_part, imag_in)
    imag_out = contract(cosine, imag_in) - contract(sine_part, real_in)
    return jnp.concatenate([real_out, imag_out], axis=1)


def inverse_rows(running, shard_rows, ky_rows, kx_rows, x_places, extent):
    cosine, sine_part = row_tables(ky_rows, kx_rows, x_places, extent, running.shape[0])
    feat_count = shard_rows.shape[1] // 2
    real_part = shard_rows[:, :feat_count]
    imag_part = shard_rows[:, feat_count:]

    def contract(table, values):
        return jnp.einsum("rxk,rf->kxf", table, values, precision=lax.Precision.HIGHEST)

    new_real = contract(cosine, real_part) - contract(sine_part, imag_part)
    new_imag = contract(cosine, imag_part) + contract(sine_part, real_part)
    return jnp.stack([new_real, new_imag], axis=1)


def general_body(flow_field, spectral_weight, local_weight, bias_terms):
    cells_x, cells_y, feat_count = flow_field.shape
    channels = local_weight.shape[0]
    planes = feat_count // channels
    groups_x = lax.axis_size("gx")
    groups_y = lax.axis_size("gy")
    extent_x = cells_x * groups_x
    extent_y = cells_y * groups_y
    half_width = MY // groups_y
    quota_rows = spectral_weight.shape[1]
    high = lax.Precision.HIGHEST
    x_places = lax.axis_index("gx") * cells_x + jnp.arange(cells_x, dtype=jnp.int32)
    y_places = lax.axis_index("gy") * cells_y + jnp.arange(cells_y, dtype=jnp.int32)
    y_angle = phase_table(wave_number(jnp.arange(MY, dtype=jnp.int32), MY), y_places, extent_y)
    y_table = (
        jnp.stack([jnp.cos(y_angle), -jnp.sin(y_angle)], axis=1)
        .reshape(2 * MY, cells_y)
        .astype(jnp.bfloat16)
    )
    y_local = lax.psum_scatter(
        jnp.einsum("qy,xyf->qxf", y_table, flow_field, preferred_element_type=jnp.float32),
        "gy",
        scatter_dimension=0,
        tiled=True,
    )
    y_local = y_local.reshape(half_width, 2, cells_x, feat_count)
    rest_index = jnp.arange(lax.axis_size("gx") * quota_rows, dtype=jnp.int32)
    spectrum = lax.psum_scatter(
        forward_rows(y_local, rest_index // MX, rest_index % MX, x_places, extent_x),
        "gx",
        scatter_dimension=0,
        tiled=True,
    )
    spectrum = spectrum * (1.0 / math.sqrt(extent_x * extent_y))
    coeffs = spectrum.reshape(quota_rows, 2, planes, channels)
    weights = spectral_weight[0].astype(jnp.float32)
    product = jnp.einsum("rpzc,rco->rpzo", coeffs, weights, precision=high)
    mixed_real = product[:, 0, :, :channels] - product[:, 1, :, channels:]
    mixed_imag = product[:, 0, :, channels:] + product[:, 1, :, :channels]
    mixed_local = jnp.stack([mixed_real, mixed_imag], axis=1).reshape(quota_rows, 2 * feat_count)
    pointwise = jnp.einsum(
        "xyzc,co->xyzo",
        flow_field.reshape(cells_x, cells_y, planes, channels),
        local_weight,
        preferred_element_type=jnp.float32,
    )
    start_half = jnp.zeros((half_width, 2, cells_x, feat_count), jnp.float32)
    shard_rows = lax.all_gather(mixed_local, "gx", axis=0, tiled=True)
    rest_index = jnp.arange(shard_rows.shape[0], dtype=jnp.int32)
    back_half = inverse_rows(
        start_half, shard_rows, rest_index // MX, rest_index % MX, x_places, extent_x
    )
    back_whole = lax.all_gather(back_half, "gy", axis=0, tiled=True)
    y_cos = jnp.cos(y_angle)
    y_sin = jnp.sin(y_angle)
    spectral = (
        jnp.einsum("kn,kxf->xnf", y_cos, back_whole[:, 0], precision=high)
        - jnp.einsum("kn,kxf->xnf", y_sin, back_whole[:, 1], precision=high)
    ) * (1.0 / math.sqrt(MX * MY))
    total = spectral.reshape(cells_x, cells_y, planes, channels) + pointwise + bias_terms
    output = (
        jax.nn.gelu(total, approximate=False)
        .reshape(cells_x, cells_y, feat_count)
        .astype(jnp.bfloat16)
    )
    return (output, mixed_local.reshape(1, quota_rows, 2 * feat_count))


SMALL = pltpu.CompilerParams(vmem_limit_bytes=20 * 1024 * 1024)
LARGE = pltpu.CompilerParams(vmem_limit_bytes=53 * 1024 * 1024)
WIDTH = 256
BIAS_TERMS = 3
FIRST = 64
GELU_TERMS = (
    1.5957645177841187,
    0.29075613617897034,
    -0.0014313592109829187,
    -0.006452994421124458,
    0.0015898864949122071,
    -0.0001365363277727738,
)


def angles(count, places, extent):
    index = np.arange(count)
    waves = np.where(index < count // 2, index, index - count)
    product = (waves[:, None] * np.asarray(places)[None, :]) % extent
    return (np.float32(2.0 * math.pi / extent) * product.astype(np.float32)).astype(np.float64)


def split_table(table):
    high = table.astype(ml_dtypes.bfloat16)
    low = (table - high.astype(np.float64)).astype(ml_dtypes.bfloat16)
    return high, low


def split_terms(values):
    high = values.astype(jnp.bfloat16)
    low = (values - high.astype(jnp.float32)).astype(jnp.bfloat16)
    return high, low


def quad():
    place = lax.axis_index("gx")
    return place // 2, place % 2, lax.axis_index("gy")


def turns(layers):
    half = layers // 2
    return list(range(half, layers)) + list(range(half - 1, -1, -1))


def forward_x_table(cells_x, peers, rows_ky):
    extent = cells_x * peers
    angle = angles(MX, np.arange(extent), extent)
    cosine, sine = np.cos(angle), np.sin(angle)
    out = np.zeros((2, rows_ky, MX, extent, rows_ky, 2))
    for row in range(rows_ky):
        out[0, row, :, :, row, 0] = cosine
        out[0, row, :, :, row, 1] = sine
        out[1, row, :, :, row, 1] = cosine
        out[1, row, :, :, row, 0] = -sine
    return out.reshape(2 * rows_ky * MX, extent * rows_ky * 2)


def inverse_x_table(cells_x, peers, rows_ky):
    extent = cells_x * peers
    angle = angles(MX, np.arange(extent), extent)
    cosine, sine = np.cos(angle).T, np.sin(angle).T
    out = np.zeros((extent, rows_ky, 2, 2, rows_ky, MX))
    for row in range(rows_ky):
        out[:, row, 0, 0, row, :] = cosine
        out[:, row, 0, 1, row, :] = -sine
        out[:, row, 1, 1, row, :] = cosine
        out[:, row, 1, 0, row, :] = sine
    out = out.reshape(peers // 2, 2, cells_x * rows_ky * 2, 2 * rows_ky * MX)
    return np.moveaxis(out, 1, 0)


def inverse_y_table(cells_y, groups_y, peers, rows_ky):
    extent = cells_y * groups_y
    angle = angles(MY, np.arange(extent), extent)
    full = np.stack([np.cos(angle), -np.sin(angle)], axis=1)
    full = full.reshape(groups_y, peers, rows_ky, 2, groups_y, cells_y)
    out = np.zeros((groups_y, 2, cells_y, peers, 2, rows_ky, 2))
    for y in range(groups_y):
        for column in range(2):
            for peer in range(peers):
                for place in range(2):
                    half = y ^ place ^ column ^ (peer % 2)
                    out[y, column, :, peer, place] = np.moveaxis(full[half, peer, :, :, y], -1, 0)
    return out.reshape(groups_y, 2, cells_y, 4 * peers * rows_ky)


def output_table(table):
    high, low = split_table(table)
    parts = [high, high, low, np.ones(table.shape[:-1] + (BIAS_TERMS,), high.dtype)]
    used = 3 * table.shape[-1] + BIAS_TERMS
    parts.append(np.zeros(table.shape[:-1] + (-used % 256,), high.dtype))
    return np.concatenate(parts, axis=-1)


def dot(left, right):
    return jnp.dot(left, right, preferred_element_type=jnp.float32)


def column_of(x, y):
    return x ^ y


def forward_y_table(shape, extent, layers, rows_ky):
    z, x, y = quad()
    peers = 2 * layers
    row = lax.broadcasted_iota(jnp.int32, (shape[0], 1), 0)
    block = row // (2 * rows_ky)
    place = block // 2 % layers
    turn = jnp.where(place < layers // 2, place + layers // 2, layers - 1 - place)
    side = y ^ (1 - block // peers)
    owner = (side ^ (block % 2)) * peers + (z ^ turn) * 2 + column_of(x, side)
    index = owner * rows_ky + row // 2 % rows_ky
    y_places = lax.broadcasted_iota(jnp.int32, (1, shape[1]), 1) + y * shape[1]
    steps = (wave_number(index, MY) * y_places) & (extent - 1)
    angle = 2.0 * math.pi / extent * steps.astype(jnp.float32)
    return jnp.where(row % 2 == 0, jnp.cos(angle), -jnp.sin(angle)).astype(jnp.bfloat16)


def forward_y_kernel(extent, rows_ky, flow_hbm, send_ref, keep_ref, flow_ref, arrived):
    layers, _, rows, feat_count = send_ref.shape
    cells_x, cells_y, _ = flow_ref.shape
    rows = rows // cells_x
    copies = [
        pltpu.make_async_copy(flow_hbm.at[x], flow_ref.at[x], arrived.at[x])
        for x in range(cells_x)
    ]
    for copy in copies:
        copy.start()
    table = forward_y_table((2 * MY, cells_y), extent, layers, rows_ky)
    for x in range(cells_x):
        copies[x].wait()
        result = dot(table, flow_ref[x]).reshape(2, layers, 2, rows, feat_count)
        send_ref[:, :, x * rows : (x + 1) * rows, :] = result[0]
        keep_ref[:, :, x * rows : (x + 1) * rows, :] = result[1]


def forward_y(flow_field, extent, layers, rows_ky):
    cells_x, _, feat_count = flow_field.shape
    shape = jax.ShapeDtypeStruct((layers, 2, cells_x * 2 * rows_ky, feat_count), jnp.float32)
    return pl.pallas_call(
        functools.partial(forward_y_kernel, extent, rows_ky),
        in_specs=[pl.BlockSpec(memory_space=pltpu.HBM)],
        out_shape=[shape] * 2,
        scratch_shapes=[
            pltpu.VMEM(flow_field.shape, flow_field.dtype),
            pltpu.SemaphoreType.DMA((cells_x,)),
        ],
        compiler_params=LARGE,
        name="forward_y",
    )(flow_field)


def flip_core(block):
    return lax.ppermute(block, "gy", [(0, 1), (1, 0)])


def along_columns(blocks, peers):
    arrived = []
    for turn, block in zip(turns(len(blocks)), blocks):
        pairs = [
            (2 * place + core, 2 * (place ^ (2 * turn + column_of(0, core))) + core)
            for place in range(peers)
            for core in range(2)
        ]
        arrived.append(lax.ppermute(block, ("gx", "gy"), pairs))
    return arrived


def small_call(kernel, out_shape, name):
    return pl.pallas_call(kernel, out_shape=out_shape, compiler_params=SMALL, name=name)


def second_kernel(*refs):
    for index, block_ref in enumerate(refs[:-1]):
        refs[-1][index] = block_ref[1]


def second_halves(blocks):
    shape = jax.ShapeDtypeStruct((len(blocks),) + blocks[0].shape[1:], blocks[0].dtype)
    return small_call(second_kernel, shape, "second_halves")(*blocks)


def stack_kernel(*refs):
    for index, block_ref in enumerate(refs[:-1]):
        refs[-1][index] = block_ref[...]


def stack_blocks(blocks):
    shape = jax.ShapeDtypeStruct((len(blocks),) + blocks[0].shape, blocks[0].dtype)
    return small_call(stack_kernel, shape, "stack_blocks")(*blocks)


def add_kernel(keep_ref, arrived_ref, *out_refs):
    for turn, out_ref in enumerate(out_refs):
        out_ref[...] = keep_ref[turn] + arrived_ref[turn]


def add_blocks(keep, arrived):
    shape = jax.ShapeDtypeStruct(keep.shape[1:], keep.dtype)
    return small_call(add_kernel, [shape] * keep.shape[0], "add_blocks")(keep, arrived)


def join_kernel(keep_ref, arrived_ref, *out_refs):
    cells_x, rows, _ = out_refs[0].shape
    rows = rows // 2
    for turn, out_ref in enumerate(out_refs):
        for cell in range(cells_x):
            span = slice(cell * rows, (cell + 1) * rows)
            out_ref[cell] = jnp.concatenate(
                [keep_ref[turn, span, :], arrived_ref[turn, span, :]], axis=0
            )


def join_blocks(keep, arrived, cells_x):
    layers, rows, feat_count = keep.shape
    shape = jax.ShapeDtypeStruct((cells_x, 2 * rows // cells_x, feat_count), keep.dtype)
    return small_call(join_kernel, [shape] * layers, "join_blocks")(keep, arrived)


def back_rows(inverse_high, inverse_low, modes, shape, other):
    z, x, y = quad()
    places = [(column_of(x, y) ^ other, z ^ turn) for turn in turns(shape[0])]
    table_high, table_low = [
        jnp.concatenate([ref[column, place] for column, place in places], axis=0)
        for ref in (inverse_high, inverse_low)
    ]
    high, low = split_terms(modes)
    back = dot(table_high, high) + dot(table_high, low) + dot(table_low, high)
    return back.reshape(shape)


def mix_kernel(layers, *refs):
    block_refs, arrived_ref = refs[:layers], refs[layers]
    weight_ref, forward_high, forward_low, inverse_high, inverse_low = refs[
        layers + 1 : layers + 6
    ]
    modes_ref, send_ref, order_ref, spread_ref, result_ref = refs[layers + 6 :]
    z, x, y = quad()
    for index, turn in enumerate(turns(layers)):
        column = column_of(x, y)
        order_ref[(z ^ turn) * 2 + column] = block_refs[index][0]
        order_ref[(z ^ turn) * 2 + (column ^ 1)] = arrived_ref[index]
    feat_count = order_ref.shape[-1]
    count = weight_ref.shape[1]
    channels = weight_ref.shape[2]
    tiles = feat_count // 128
    group = 2 * tiles
    high, low = split_terms(order_ref[...].reshape(-1, feat_count))
    spectrum = (
        dot(forward_high[...], high) + dot(forward_high[...], low) + dot(forward_low[...], high)
    )
    for part in range(2):
        for tile in range(tiles):
            spread_ref[pl.ds(part * tiles + tile, count, stride=group), :] = spectrum[
                part * count : (part + 1) * count, tile * 128 : (tile + 1) * 128
            ]
    rows = lax.broadcasted_iota(jnp.int32, (8, 128), 0) % group
    lane = lax.broadcasted_iota(jnp.int32, (8, 128), 1) < channels
    sign = jnp.where(rows < tiles, -1.0, 1.0)
    for base in range(0, count * group, 8):
        block = spread_ref[base : base + 8, :]
        turned = pltpu.roll(block, channels, 1)
        firsts, seconds = [], []
        for start in range(0, 8, group):
            span = slice(start, start + group)
            left = jnp.concatenate([block[span], turned[span]], axis=0)[:, :channels]
            left_high, left_low = split_terms(left)
            left = jnp.concatenate([left_high, left_low], axis=0)
            product = dot(left, weight_ref[0, (base + start) // group])
            product = product[: 2 * group] + product[2 * group :]
            firsts.append(product[:group])
            seconds.append(product[group:])
        first = jnp.concatenate(firsts, axis=0)
        second = jnp.concatenate(seconds, axis=0)
        real = jnp.where(lane, first, pltpu.roll(second, channels, 1))
        imag = jnp.where(lane, pltpu.roll(first, channels, 1), second)
        crossed = jnp.where(rows < tiles, pltpu.roll(imag, 8 - tiles, 0), pltpu.roll(imag, tiles, 0))
        result_ref[base : base + 8, :] = real + sign * crossed
    for part in range(2):
        for tile in range(tiles):
            modes_ref[part * count : (part + 1) * count, tile * 128 : (tile + 1) * 128] = (
                result_ref[pl.ds(part * tiles + tile, count, stride=group), :]
            )
    send_ref[...] = back_rows(inverse_high, inverse_low, modes_ref[...], send_ref.shape, 1)


def mix(blocks, arrived, weights, forward_table, inverse_tables):
    layers = len(blocks)
    _, rows, feat_count = blocks[0].shape
    count = weights.shape[1]
    scratch = pltpu.VMEM((count * feat_count // 64, 128), jnp.float32)
    return pl.pallas_call(
        functools.partial(mix_kernel, layers),
        out_shape=[
            jax.ShapeDtypeStruct((2 * count, feat_count), jnp.float32),
            jax.ShapeDtypeStruct((layers, rows, feat_count), jnp.float32),
        ],
        scratch_shapes=[pltpu.VMEM((2 * layers, rows, feat_count), jnp.float32), scratch, scratch],
        compiler_params=SMALL,
        name="mix",
    )(*blocks, arrived, weights, *split_table(forward_table), *inverse_tables)


def keep_kernel(modes_ref, inverse_high, inverse_low, mixed_ref, keep_ref):
    count = mixed_ref.shape[1]
    feat_count = modes_ref.shape[1]
    for part in range(2):
        mixed_ref[0, :, part * feat_count : (part + 1) * feat_count] = modes_ref[
            part * count : (part + 1) * count
        ]
    keep_ref[...] = back_rows(inverse_high, inverse_low, modes_ref[...], keep_ref.shape, 0)


def keep_rows(modes, inverse_tables, like):
    rows, feat_count = modes.shape
    return pl.pallas_call(
        keep_kernel,
        out_shape=[
            jax.ShapeDtypeStruct((1, rows // 2, 2 * feat_count), jnp.float32),
            jax.ShapeDtypeStruct(like.shape, jnp.float32),
        ],
        compiler_params=SMALL,
        name="keep_rows",
    )(modes, *inverse_tables)


def gelu(half):
    square = jnp.minimum(half * half, 6.25)
    inner = jnp.full_like(square, GELU_TERMS[-1])
    for term in GELU_TERMS[-2::-1]:
        inner = inner * square + term
    return half + half * jnp.tanh(half * inner)


def output_kernel(
    flow_ref, table_ref, local_ref, bias_ref, own_ref, core_ref,
    out_hbm, order_ref, wide_ref, level_ref, done_ref, sent,
):
    cells_x, cells_y, feat_count = flow_ref.shape
    channels = local_ref.shape[0]
    z, x, y = quad()
    wide_ref[...] = jnp.zeros_like(wide_ref)
    for start in range(0, WIDTH, channels):
        span = slice(start, start + channels)
        wide_ref[span, span] = local_ref[...] * 0.5
        level_ref[:, span] = bias_ref[...].reshape(1, channels) * 0.5
    level = level_ref[...]
    levels = []
    for _ in range(BIAS_TERMS):
        levels.append(level.astype(jnp.bfloat16).astype(jnp.float32))
        level = level - levels[-1]
    terms = 3 * order_ref.shape[1] * order_ref.shape[2]
    filled = jnp.zeros((table_ref.shape[-1] - terms - BIAS_TERMS, WIDTH), jnp.float32)
    below = jnp.concatenate(levels + [filled], axis=0).astype(jnp.bfloat16)
    below = jnp.concatenate([below, wide_ref[...]], axis=0)
    for index, turn in enumerate(turns(own_ref.shape[0])):
        column = column_of(x, y)
        for peer, ref in ((column, own_ref), (column ^ 1, core_ref)):
            order_ref[:, (z ^ turn) * 2 + peer] = ref[index]
    table = table_ref[y, x ^ y]
    copies = []
    for cell in range(cells_x):
        high, low = split_terms(order_ref[cell].reshape(-1, feat_count))
        stack = jnp.concatenate([high, low, high], axis=0)
        bounds = [0, FIRST, cells_y] if cell == 0 else [0, cells_y]
        for begin, end in zip(bounds[:-1], bounds[1:]):
            rows = slice(begin, end)
            for start in range(0, feat_count, WIDTH):
                columns = slice(start, start + WIDTH)
                total = dot(
                    jnp.concatenate([table[rows], flow_ref[cell, rows, columns]], axis=1),
                    jnp.concatenate([stack[:, columns], below], axis=0),
                )
                done_ref[cell, rows, columns] = gelu(total).astype(done_ref.dtype)
            copies.append(
                pltpu.make_async_copy(
                    done_ref.at[cell, rows], out_hbm.at[cell, rows], sent.at[len(copies)]
                )
            )
            copies[-1].start()
    for copy in copies:
        copy.wait()


def make_output(flow_field, own, core, table, local, bias):
    cells_x, _, feat_count = flow_field.shape
    return pl.pallas_call(
        output_kernel,
        out_specs=pl.BlockSpec(memory_space=pl.ANY),
        scratch_shapes=[
            pltpu.VMEM((cells_x, 2 * own.shape[0]) + own.shape[2:], jnp.float32),
            pltpu.VMEM((WIDTH, WIDTH), jnp.bfloat16),
            pltpu.VMEM((1, WIDTH), jnp.float32),
            pltpu.VMEM(flow_field.shape, jnp.bfloat16),
            pltpu.SemaphoreType.DMA((cells_x + 1,)),
        ],
        out_shape=jax.ShapeDtypeStruct(flow_field.shape, jnp.bfloat16),
        compiler_params=SMALL,
        name="make_output",
    )(flow_field, table, local, bias, own, core)


def row_body(flow_field, spectral_weight, local_weight, bias_terms):
    cells_x, cells_y, feat_count = flow_field.shape
    peers = lax.axis_size("gx")
    groups_y = lax.axis_size("gy")
    rows_ky = MY // groups_y // peers
    forward_scale = 1.0 / math.sqrt(cells_x * peers * cells_y * groups_y)
    inverse_scale = 1.0 / math.sqrt(MX * MY)

    send, keep = forward_y(flow_field, cells_y * groups_y, peers // 2, rows_ky)
    blocks = along_columns(add_blocks(keep, flip_core(send)), peers)
    inverse_tables = split_table(inverse_x_table(cells_x, peers, rows_ky))
    modes, send = mix(
        blocks,
        flip_core(second_halves(blocks)),
        spectral_weight,
        forward_x_table(cells_x, peers, rows_ky) * forward_scale,
        inverse_tables,
    )
    arrived = flip_core(send)
    mixed, keep = keep_rows(modes, inverse_tables, send)
    own = along_columns(join_blocks(keep, arrived, cells_x), peers)
    own = stack_blocks(own)
    table = output_table(inverse_y_table(cells_y, groups_y, peers, rows_ky) * (0.5 * inverse_scale))
    return make_output(flow_field, own, flip_core(own), table, local_weight, bias_terms), mixed


def body(flow_field, spectral_weight, local_weight, bias_terms):
    peers = lax.axis_size("gx")
    extent = lax.axis_size("gy") * flow_field.shape[1]
    paired = lax.axis_size("gy") == 2 and peers & (peers - 1) == 0 and extent & (extent - 1) == 0
    if paired and spectral_weight.shape[1] == 2 * MX and WIDTH % local_weight.shape[0] == 0:
        return row_body(flow_field, spectral_weight, local_weight, bias_terms)
    return general_body(flow_field, spectral_weight, local_weight, bias_terms)


def solution(mesh):
    placed = (P(("group", "gx"), "gy", None), P("gy", "gx", None, None), P(), P())
    return jax.shard_map(
        body,
        mesh=mesh,
        in_specs=placed,
        out_specs=(P(("group", "gx"), "gy", None), P(("group", "gy"), "gx", None)),
        check_vma=False,
    )
```

```python
import functools
import math

import jax
import jax.numpy as jnp
import ml_dtypes
import numpy as np
from jax import lax
from jax.experimental import pallas as pl
from jax.experimental.pallas import tpu as pltpu
from jax.sharding import PartitionSpec as P

MX = 32
MY = 32


def wave_number(index, count):
    return jnp.where(index < count // 2, index, index - count)


def phase_table(waves, places, extent):
    product = waves[:, None] * places[None, :] % extent
    return 2.0 * math.pi / extent * product.astype(jnp.float32)


def row_tables(ky_rows, kx_rows, x_places, extent, width):
    angle = phase_table(wave_number(kx_rows, MX), x_places, extent)
    select = (ky_rows[:, None] == jnp.arange(width, dtype=jnp.int32)[None, :]).astype(jnp.float32)
    cosine = jnp.cos(angle)[:, :, None] * select[:, None, :]
    sine_part = jnp.sin(angle)[:, :, None] * select[:, None, :]
    return (cosine, sine_part)


def forward_rows(y_local, ky_rows, kx_rows, x_places, extent):
    cosine, sine_part = row_tables(ky_rows, kx_rows, x_places, extent, y_local.shape[0])
    real_in = y_local[:, 0]
    imag_in = y_local[:, 1]

    def contract(table, values):
        return jnp.einsum("rxk,kxf->rf", table, values, precision=lax.Precision.HIGHEST)

    real_out = contract(cosine, real_in) + contract(sine_part, imag_in)
    imag_out = contract(cosine, imag_in) - contract(sine_part, real_in)
    return jnp.concatenate([real_out, imag_out], axis=1)


def inverse_rows(running, shard_rows, ky_rows, kx_rows, x_places, extent):
    cosine, sine_part = row_tables(ky_rows, kx_rows, x_places, extent, running.shape[0])
    feat_count = shard_rows.shape[1] // 2
    real_part = shard_rows[:, :feat_count]
    imag_part = shard_rows[:, feat_count:]

    def contract(table, values):
        return jnp.einsum("rxk,rf->kxf", table, values, precision=lax.Precision.HIGHEST)

    new_real = contract(cosine, real_part) - contract(sine_part, imag_part)
    new_imag = contract(cosine, imag_part) + contract(sine_part, real_part)
    return jnp.stack([new_real, new_imag], axis=1)


def general_body(flow_field, spectral_weight, local_weight, bias_terms):
    cells_x, cells_y, feat_count = flow_field.shape
    channels = local_weight.shape[0]
    planes = feat_count // channels
    groups_x = lax.axis_size("gx")
    groups_y = lax.axis_size("gy")
    extent_x = cells_x * groups_x
    extent_y = cells_y * groups_y
    half_width = MY // groups_y
    quota_rows = spectral_weight.shape[1]
    high = lax.Precision.HIGHEST
    x_places = lax.axis_index("gx") * cells_x + jnp.arange(cells_x, dtype=jnp.int32)
    y_places = lax.axis_index("gy") * cells_y + jnp.arange(cells_y, dtype=jnp.int32)
    y_angle = phase_table(wave_number(jnp.arange(MY, dtype=jnp.int32), MY), y_places, extent_y)
    y_table = (
        jnp.stack([jnp.cos(y_angle), -jnp.sin(y_angle)], axis=1)
        .reshape(2 * MY, cells_y)
        .astype(jnp.bfloat16)
    )
    y_local = lax.psum_scatter(
        jnp.einsum("qy,xyf->qxf", y_table, flow_field, preferred_element_type=jnp.float32),
        "gy",
        scatter_dimension=0,
        tiled=True,
    )
    y_local = y_local.reshape(half_width, 2, cells_x, feat_count)
    rest_index = jnp.arange(lax.axis_size("gx") * quota_rows, dtype=jnp.int32)
    spectrum = lax.psum_scatter(
        forward_rows(y_local, rest_index // MX, rest_index % MX, x_places, extent_x),
        "gx",
        scatter_dimension=0,
        tiled=True,
    )
    spectrum = spectrum * (1.0 / math.sqrt(extent_x * extent_y))
    coeffs = spectrum.reshape(quota_rows, 2, planes, channels)
    weights = spectral_weight[0].astype(jnp.float32)
    product = jnp.einsum("rpzc,rco->rpzo", coeffs, weights, precision=high)
    mixed_real = product[:, 0, :, :channels] - product[:, 1, :, channels:]
    mixed_imag = product[:, 0, :, channels:] + product[:, 1, :, :channels]
    mixed_local = jnp.stack([mixed_real, mixed_imag], axis=1).reshape(quota_rows, 2 * feat_count)
    pointwise = jnp.einsum(
        "xyzc,co->xyzo",
        flow_field.reshape(cells_x, cells_y, planes, channels),
        local_weight,
        preferred_element_type=jnp.float32,
    )
    start_half = jnp.zeros((half_width, 2, cells_x, feat_count), jnp.float32)
    shard_rows = lax.all_gather(mixed_local, "gx", axis=0, tiled=True)
    rest_index = jnp.arange(shard_rows.shape[0], dtype=jnp.int32)
    back_half = inverse_rows(
        start_half, shard_rows, rest_index // MX, rest_index % MX, x_places, extent_x
    )
    back_whole = lax.all_gather(back_half, "gy", axis=0, tiled=True)
    y_cos = jnp.cos(y_angle)
    y_sin = jnp.sin(y_angle)
    spectral = (
        jnp.einsum("kn,kxf->xnf", y_cos, back_whole[:, 0], precision=high)
        - jnp.einsum("kn,kxf->xnf", y_sin, back_whole[:, 1], precision=high)
    ) * (1.0 / math.sqrt(MX * MY))
    total = spectral.reshape(cells_x, cells_y, planes, channels) + pointwise + bias_terms
    output = (
        jax.nn.gelu(total, approximate=False)
        .reshape(cells_x, cells_y, feat_count)
        .astype(jnp.bfloat16)
    )
    return (output, mixed_local.reshape(1, quota_rows, 2 * feat_count))


SMALL = pltpu.CompilerParams(vmem_limit_bytes=20 * 1024 * 1024)
LARGE = pltpu.CompilerParams(vmem_limit_bytes=53 * 1024 * 1024)
WIDTH = 256
BIAS_TERMS = 3
FIRST = 64
GELU_TERMS = (
    1.5957645177841187,
    0.29075613617897034,
    -0.0014313592109829187,
    -0.006452994421124458,
    0.0015898864949122071,
    -0.0001365363277727738,
)


def angles(count, places, extent):
    index = np.arange(count)
    waves = np.where(index < count // 2, index, index - count)
    product = (waves[:, None] * np.asarray(places)[None, :]) % extent
    return (np.float32(2.0 * math.pi / extent) * product.astype(np.float32)).astype(np.float64)


def split_table(table):
    high = table.astype(ml_dtypes.bfloat16)
    low = (table - high.astype(np.float64)).astype(ml_dtypes.bfloat16)
    return high, low


def split_terms(values):
    high = values.astype(jnp.bfloat16)
    low = (values - high.astype(jnp.float32)).astype(jnp.bfloat16)
    return high, low


def quad():
    place = lax.axis_index("gx")
    return place // 2, place % 2, lax.axis_index("gy")


def turns(layers):
    half = layers // 2
    return list(range(half, layers)) + list(range(half - 1, -1, -1))


def forward_x_table(cells_x, peers, rows_ky):
    extent = cells_x * peers
    angle = angles(MX, np.arange(extent), extent)
    cosine, sine = np.cos(angle), np.sin(angle)
    out = np.zeros((2, rows_ky, MX, extent, rows_ky, 2))
    for row in range(rows_ky):
        out[0, row, :, :, row, 0] = cosine
        out[0, row, :, :, row, 1] = sine
        out[1, row, :, :, row, 1] = cosine
        out[1, row, :, :, row, 0] = -sine
    return out.reshape(2 * rows_ky * MX, extent * rows_ky * 2)


def inverse_x_table(cells_x, peers, rows_ky):
    extent = cells_x * peers
    angle = angles(MX, np.arange(extent), extent)
    cosine, sine = np.cos(angle).T, np.sin(angle).T
    out = np.zeros((extent, rows_ky, 2, 2, rows_ky, MX))
    for row in range(rows_ky):
        out[:, row, 0, 0, row, :] = cosine
        out[:, row, 0, 1, row, :] = -sine
        out[:, row, 1, 1, row, :] = cosine
        out[:, row, 1, 0, row, :] = sine
    out = out.reshape(peers // 2, 2, cells_x * rows_ky * 2, 2 * rows_ky * MX)
    return np.moveaxis(out, 1, 0)


def inverse_y_table(cells_y, groups_y, peers, rows_ky):
    extent = cells_y * groups_y
    angle = angles(MY, np.arange(extent), extent)
    full = np.stack([np.cos(angle), -np.sin(angle)], axis=1)
    full = full.reshape(groups_y, peers, rows_ky, 2, groups_y, cells_y)
    out = np.zeros((groups_y, 2, cells_y, peers, 2, rows_ky, 2))
    for y in range(groups_y):
        for column in range(2):
            for peer in range(peers):
                for place in range(2):
                    half = y ^ place ^ column ^ (peer % 2)
                    out[y, column, :, peer, place] = np.moveaxis(full[half, peer, :, :, y], -1, 0)
    return out.reshape(groups_y, 2, cells_y, 4 * peers * rows_ky)


def output_table(table):
    high, low = split_table(table)
    parts = [high, high, low, np.ones(table.shape[:-1] + (BIAS_TERMS,), high.dtype)]
    used = 3 * table.shape[-1] + BIAS_TERMS
    parts.append(np.zeros(table.shape[:-1] + (-used % 256,), high.dtype))
    return np.concatenate(parts, axis=-1)


def dot(left, right):
    return jnp.dot(left, right, preferred_element_type=jnp.float32)


def column_of(x, y):
    return x ^ y


def forward_y_table(shape, extent, layers, rows_ky):
    z, x, y = quad()
    peers = 2 * layers
    row = lax.broadcasted_iota(jnp.int32, (shape[0], 1), 0)
    block = row // (2 * rows_ky)
    place = block // 2 % layers
    turn = jnp.where(place < layers // 2, place + layers // 2, layers - 1 - place)
    side = y ^ (1 - block // peers)
    owner = (side ^ (block % 2)) * peers + (z ^ turn) * 2 + column_of(x, side)
    index = owner * rows_ky + row // 2 % rows_ky
    y_places = lax.broadcasted_iota(jnp.int32, (1, shape[1]), 1) + y * shape[1]
    steps = (wave_number(index, MY) * y_places) & (extent - 1)
    angle = 2.0 * math.pi / extent * steps.astype(jnp.float32)
    return jnp.where(row % 2 == 0, jnp.cos(angle), -jnp.sin(angle)).astype(jnp.bfloat16)


def forward_y_kernel(extent, rows_ky, flow_hbm, send_ref, keep_ref, flow_ref, arrived):
    layers, _, rows, feat_count = send_ref.shape
    cells_x, cells_y, _ = flow_ref.shape
    rows = rows // cells_x
    copies = [
        pltpu.make_async_copy(flow_hbm.at[x], flow_ref.at[x], arrived.at[x])
        for x in range(cells_x)
    ]
    for copy in copies:
        copy.start()
    table = forward_y_table((2 * MY, cells_y), extent, layers, rows_ky)
    for x in range(cells_x):
        copies[x].wait()
        result = dot(table, flow_ref[x]).reshape(2, layers, 2, rows, feat_count)
        send_ref[:, :, x * rows : (x + 1) * rows, :] = result[0]
        keep_ref[:, :, x * rows : (x + 1) * rows, :] = result[1]


def forward_y(flow_field, extent, layers, rows_ky):
    cells_x, _, feat_count = flow_field.shape
    shape = jax.ShapeDtypeStruct((layers, 2, cells_x * 2 * rows_ky, feat_count), jnp.float32)
    return pl.pallas_call(
        functools.partial(forward_y_kernel, extent, rows_ky),
        in_specs=[pl.BlockSpec(memory_space=pltpu.HBM)],
        out_shape=[shape] * 2,
        scratch_shapes=[
            pltpu.VMEM(flow_field.shape, flow_field.dtype),
            pltpu.SemaphoreType.DMA((cells_x,)),
        ],
        compiler_params=LARGE,
        name="forward_y",
    )(flow_field)


def flip_core(block):
    return lax.ppermute(block, "gy", [(0, 1), (1, 0)])


def along_columns(blocks, peers):
    arrived = []
    for turn, block in zip(turns(len(blocks)), blocks):
        pairs = [
            (2 * place + core, 2 * (place ^ (2 * turn + column_of(0, core))) + core)
            for place in range(peers)
            for core in range(2)
        ]
        arrived.append(lax.ppermute(block, ("gx", "gy"), pairs))
    return arrived


def small_call(kernel, out_shape, name):
    return pl.pallas_call(kernel, out_shape=out_shape, compiler_params=SMALL, name=name)


def second_kernel(*refs):
    for index, block_ref in enumerate(refs[:-1]):
        refs[-1][index] = block_ref[1]


def second_halves(blocks):
    shape = jax.ShapeDtypeStruct((len(blocks),) + blocks[0].shape[1:], blocks[0].dtype)
    return small_call(second_kernel, shape, "second_halves")(*blocks)


def add_kernel(keep_ref, arrived_ref, *out_refs):
    for turn, out_ref in enumerate(out_refs):
        out_ref[...] = keep_ref[turn] + arrived_ref[turn]


def add_blocks(keep, arrived):
    shape = jax.ShapeDtypeStruct(keep.shape[1:], keep.dtype)
    return small_call(add_kernel, [shape] * keep.shape[0], "add_blocks")(keep, arrived)


def join_kernel(keep_ref, arrived_ref, *out_refs):
    cells_x, rows, _ = out_refs[0].shape
    rows = rows // 2
    for turn, out_ref in enumerate(out_refs):
        for cell in range(cells_x):
            span = slice(cell * rows, (cell + 1) * rows)
            out_ref[cell] = jnp.concatenate(
                [keep_ref[turn, span, :], arrived_ref[turn, span, :]], axis=0
            )


def join_blocks(keep, arrived, cells_x):
    layers, rows, feat_count = keep.shape
    shape = jax.ShapeDtypeStruct((cells_x, 2 * rows // cells_x, feat_count), keep.dtype)
    return small_call(join_kernel, [shape] * layers, "join_blocks")(keep, arrived)


def back_rows(inverse_high, inverse_low, modes, shape, other):
    z, x, y = quad()
    places = [(column_of(x, y) ^ other, z ^ turn) for turn in turns(shape[0])]
    table_high, table_low = [
        jnp.concatenate([ref[column, place] for column, place in places], axis=0)
        for ref in (inverse_high, inverse_low)
    ]
    high, low = split_terms(modes)
    back = dot(table_high, high) + dot(table_high, low) + dot(table_low, high)
    return back.reshape(shape)


def mix_kernel(layers, *refs):
    block_refs, arrived_ref = refs[:layers], refs[layers]
    weight_ref, forward_high, forward_low, inverse_high, inverse_low = refs[
        layers + 1 : layers + 6
    ]
    modes_ref, send_ref, order_ref, spread_ref, result_ref = refs[layers + 6 :]
    z, x, y = quad()
    for index, turn in enumerate(turns(layers)):
        column = column_of(x, y)
        order_ref[(z ^ turn) * 2 + column] = block_refs[index][0]
        order_ref[(z ^ turn) * 2 + (column ^ 1)] = arrived_ref[index]
    feat_count = order_ref.shape[-1]
    count = weight_ref.shape[1]
    channels = weight_ref.shape[2]
    tiles = feat_count // 128
    group = 2 * tiles
    high, low = split_terms(order_ref[...].reshape(-1, feat_count))
    spectrum = (
        dot(forward_high[...], high) + dot(forward_high[...], low) + dot(forward_low[...], high)
    )
    for part in range(2):
        for tile in range(tiles):
            spread_ref[pl.ds(part * tiles + tile, count, stride=group), :] = spectrum[
                part * count : (part + 1) * count, tile * 128 : (tile + 1) * 128
            ]
    rows = lax.broadcasted_iota(jnp.int32, (8, 128), 0) % group
    lane = lax.broadcasted_iota(jnp.int32, (8, 128), 1) < channels
    sign = jnp.where(rows < tiles, -1.0, 1.0)
    for base in range(0, count * group, 8):
        block = spread_ref[base : base + 8, :]
        turned = pltpu.roll(block, channels, 1)
        firsts, seconds = [], []
        for start in range(0, 8, group):
            span = slice(start, start + group)
            left = jnp.concatenate([block[span], turned[span]], axis=0)[:, :channels]
            product = dot(left.astype(jnp.bfloat16), weight_ref[0, (base + start) // group])
            firsts.append(product[:group])
            seconds.append(product[group:])
        first = jnp.concatenate(firsts, axis=0)
        second = jnp.concatenate(seconds, axis=0)
        real = jnp.where(lane, first, pltpu.roll(second, channels, 1))
        imag = jnp.where(lane, pltpu.roll(first, channels, 1), second)
        crossed = jnp.where(rows < tiles, pltpu.roll(imag, 8 - tiles, 0), pltpu.roll(imag, tiles, 0))
        result_ref[base : base + 8, :] = real + sign * crossed
    for part in range(2):
        for tile in range(tiles):
            modes_ref[part * count : (part + 1) * count, tile * 128 : (tile + 1) * 128] = (
                result_ref[pl.ds(part * tiles + tile, count, stride=group), :]
            )
    send_ref[...] = back_rows(inverse_high, inverse_low, modes_ref[...], send_ref.shape, 1)


def mix(blocks, arrived, weights, forward_table, inverse_tables):
    layers = len(blocks)
    _, rows, feat_count = blocks[0].shape
    count = weights.shape[1]
    scratch = pltpu.VMEM((count * feat_count // 64, 128), jnp.float32)
    return pl.pallas_call(
        functools.partial(mix_kernel, layers),
        out_shape=[
            jax.ShapeDtypeStruct((2 * count, feat_count), jnp.float32),
            jax.ShapeDtypeStruct((layers, rows, feat_count), jnp.float32),
        ],
        scratch_shapes=[pltpu.VMEM((2 * layers, rows, feat_count), jnp.float32), scratch, scratch],
        compiler_params=SMALL,
        name="mix",
    )(*blocks, arrived, weights, *split_table(forward_table), *inverse_tables)


def keep_kernel(modes_ref, inverse_high, inverse_low, mixed_ref, keep_ref):
    count = mixed_ref.shape[1]
    feat_count = modes_ref.shape[1]
    for part in range(2):
        mixed_ref[0, :, part * feat_count : (part + 1) * feat_count] = modes_ref[
            part * count : (part + 1) * count
        ]
    keep_ref[...] = back_rows(inverse_high, inverse_low, modes_ref[...], keep_ref.shape, 0)


def keep_rows(modes, inverse_tables, like):
    rows, feat_count = modes.shape
    return pl.pallas_call(
        keep_kernel,
        out_shape=[
            jax.ShapeDtypeStruct((1, rows // 2, 2 * feat_count), jnp.float32),
            jax.ShapeDtypeStruct(like.shape, jnp.float32),
        ],
        compiler_params=SMALL,
        name="keep_rows",
    )(modes, *inverse_tables)


def gelu(half):
    square = jnp.minimum(half * half, 6.25)
    inner = jnp.full_like(square, GELU_TERMS[-1])
    for term in GELU_TERMS[-2::-1]:
        inner = inner * square + term
    return half + half * jnp.tanh(half * inner)


def output_kernel(layers, flow_ref, table_ref, local_ref, bias_ref, *refs):
    own_refs, core_refs = refs[:layers], refs[layers : 2 * layers]
    out_hbm, order_ref, wide_ref, level_ref, done_ref, sent = refs[2 * layers :]
    cells_x, _, feat_count = flow_ref.shape
    channels = local_ref.shape[0]
    z, x, y = quad()
    wide_ref[...] = jnp.zeros_like(wide_ref)
    for start in range(0, WIDTH, channels):
        span = slice(start, start + channels)
        wide_ref[span, span] = local_ref[...] * 0.5
        level_ref[:, span] = bias_ref[...].reshape(1, channels) * 0.5
    level = level_ref[...]
    levels = []
    for _ in range(BIAS_TERMS):
        levels.append(level.astype(jnp.bfloat16).astype(jnp.float32))
        level = level - levels[-1]
    terms = 3 * order_ref.shape[1] * order_ref.shape[2]
    filled = jnp.zeros((table_ref.shape[-1] - terms - BIAS_TERMS, WIDTH), jnp.float32)
    below = jnp.concatenate(levels + [filled], axis=0).astype(jnp.bfloat16)
    below = jnp.concatenate([below, wide_ref[...]], axis=0)
    for column, block_refs in ((x ^ y, own_refs), (x ^ y ^ 1, core_refs)):
        for turn, block_ref in zip(turns(layers), block_refs):
            order_ref[:, (z ^ turn) * 2 + column] = block_ref[...]
    table = table_ref[y, x ^ y]
    copies = []
    for cell in range(cells_x):
        high, low = split_terms(order_ref[cell].reshape(-1, feat_count))
        stack = jnp.concatenate([high, low, high], axis=0)
        for start in range(0, feat_count, WIDTH):
            columns = slice(start, start + WIDTH)
            total = dot(
                jnp.concatenate([table, flow_ref[cell, :, columns]], axis=1),
                jnp.concatenate([stack[:, columns], below], axis=0),
            )
            done_ref[cell, :, columns] = gelu(total).astype(done_ref.dtype)
        copies.append(pltpu.make_async_copy(done_ref.at[cell], out_hbm.at[cell], sent.at[cell]))
        copies[-1].start()
    for copy in copies:
        copy.wait()


def make_output(flow_field, parts, table, local, bias):
    cells_x, _, feat_count = flow_field.shape
    layers = len(parts) // 2
    return pl.pallas_call(
        functools.partial(output_kernel, layers),
        out_specs=pl.BlockSpec(memory_space=pl.ANY),
        scratch_shapes=[
            pltpu.VMEM((cells_x, 2 * layers) + parts[0].shape[1:], jnp.float32),
            pltpu.VMEM((WIDTH, WIDTH), jnp.bfloat16),
            pltpu.VMEM((1, WIDTH), jnp.float32),
            pltpu.VMEM(flow_field.shape, jnp.bfloat16),
            pltpu.SemaphoreType.DMA((cells_x,)),
        ],
        out_shape=jax.ShapeDtypeStruct(flow_field.shape, jnp.bfloat16),
        compiler_params=SMALL,
        name="make_output",
    )(flow_field, table, local, bias, *parts)


def row_body(flow_field, spectral_weight, local_weight, bias_terms):
    cells_x, cells_y, feat_count = flow_field.shape
    peers = lax.axis_size("gx")
    groups_y = lax.axis_size("gy")
    rows_ky = MY // groups_y // peers
    forward_scale = 1.0 / math.sqrt(cells_x * peers * cells_y * groups_y)
    inverse_scale = 1.0 / math.sqrt(MX * MY)

    send, keep = forward_y(flow_field, cells_y * groups_y, peers // 2, rows_ky)
    blocks = along_columns(add_blocks(keep, flip_core(send)), peers)
    inverse_tables = split_table(inverse_x_table(cells_x, peers, rows_ky))
    modes, send = mix(
        blocks,
        flip_core(second_halves(blocks)),
        spectral_weight,
        forward_x_table(cells_x, peers, rows_ky) * forward_scale,
        inverse_tables,
    )
    arrived = flip_core(send)
    mixed, keep = keep_rows(modes, inverse_tables, send)
    own = along_columns(join_blocks(keep, arrived, cells_x), peers)
    parts = own + [flip_core(block) for block in own]
    table = output_table(inverse_y_table(cells_y, groups_y, peers, rows_ky) * (0.5 * inverse_scale))
    return make_output(flow_field, parts, table, local_weight, bias_terms), mixed


def body(flow_field, spectral_weight, local_weight, bias_terms):
    peers = lax.axis_size("gx")
    extent = lax.axis_size("gy") * flow_field.shape[1]
    paired = lax.axis_size("gy") == 2 and peers & (peers - 1) == 0 and extent & (extent - 1) == 0
    if paired and spectral_weight.shape[1] == 2 * MX and WIDTH % local_weight.shape[0] == 0:
        return row_body(flow_field, spectral_weight, local_weight, bias_terms)
    return general_body(flow_field, spectral_weight, local_weight, bias_terms)


def solution(mesh):
    placed = (P(("group", "gx"), "gy", None), P("gy", "gx", None, None), P(), P())
    return jax.shard_map(
        body,
        mesh=mesh,
        in_specs=placed,
        out_specs=(P(("group", "gx"), "gy", None), P(("group", "gy"), "gx", None)),
        check_vma=False,
    )
```

```python
import functools
import math

import jax
import jax.numpy as jnp
import ml_dtypes
import numpy as np
from jax import lax
from jax.experimental import pallas as pl
from jax.experimental.pallas import tpu as pltpu
from jax.sharding import PartitionSpec as P

MX = 32
MY = 32


def wave_number(index, count):
    return jnp.where(index < count // 2, index, index - count)


def phase_table(waves, places, extent):
    product = waves[:, None] * places[None, :] % extent
    return 2.0 * math.pi / extent * product.astype(jnp.float32)


def row_tables(ky_rows, kx_rows, x_places, extent, width):
    angle = phase_table(wave_number(kx_rows, MX), x_places, extent)
    select = (ky_rows[:, None] == jnp.arange(width, dtype=jnp.int32)[None, :]).astype(jnp.float32)
    cosine = jnp.cos(angle)[:, :, None] * select[:, None, :]
    sine_part = jnp.sin(angle)[:, :, None] * select[:, None, :]
    return (cosine, sine_part)


def forward_rows(y_local, ky_rows, kx_rows, x_places, extent):
    cosine, sine_part = row_tables(ky_rows, kx_rows, x_places, extent, y_local.shape[0])
    real_in = y_local[:, 0]
    imag_in = y_local[:, 1]

    def contract(table, values):
        return jnp.einsum("rxk,kxf->rf", table, values, precision=lax.Precision.HIGHEST)

    real_out = contract(cosine, real_in) + contract(sine_part, imag_in)
    imag_out = contract(cosine, imag_in) - contract(sine_part, real_in)
    return jnp.concatenate([real_out, imag_out], axis=1)


def inverse_rows(running, shard_rows, ky_rows, kx_rows, x_places, extent):
    cosine, sine_part = row_tables(ky_rows, kx_rows, x_places, extent, running.shape[0])
    feat_count = shard_rows.shape[1] // 2
    real_part = shard_rows[:, :feat_count]
    imag_part = shard_rows[:, feat_count:]

    def contract(table, values):
        return jnp.einsum("rxk,rf->kxf", table, values, precision=lax.Precision.HIGHEST)

    new_real = contract(cosine, real_part) - contract(sine_part, imag_part)
    new_imag = contract(cosine, imag_part) + contract(sine_part, real_part)
    return jnp.stack([new_real, new_imag], axis=1)


def general_body(flow_field, spectral_weight, local_weight, bias_terms):
    cells_x, cells_y, feat_count = flow_field.shape
    channels = local_weight.shape[0]
    planes = feat_count // channels
    groups_x = lax.axis_size("gx")
    groups_y = lax.axis_size("gy")
    extent_x = cells_x * groups_x
    extent_y = cells_y * groups_y
    half_width = MY // groups_y
    quota_rows = spectral_weight.shape[1]
    high = lax.Precision.HIGHEST
    x_places = lax.axis_index("gx") * cells_x + jnp.arange(cells_x, dtype=jnp.int32)
    y_places = lax.axis_index("gy") * cells_y + jnp.arange(cells_y, dtype=jnp.int32)
    y_angle = phase_table(wave_number(jnp.arange(MY, dtype=jnp.int32), MY), y_places, extent_y)
    y_table = (
        jnp.stack([jnp.cos(y_angle), -jnp.sin(y_angle)], axis=1)
        .reshape(2 * MY, cells_y)
        .astype(jnp.bfloat16)
    )
    y_local = lax.psum_scatter(
        jnp.einsum("qy,xyf->qxf", y_table, flow_field, preferred_element_type=jnp.float32),
        "gy",
        scatter_dimension=0,
        tiled=True,
    )
    y_local = y_local.reshape(half_width, 2, cells_x, feat_count)
    rest_index = jnp.arange(lax.axis_size("gx") * quota_rows, dtype=jnp.int32)
    spectrum = lax.psum_scatter(
        forward_rows(y_local, rest_index // MX, rest_index % MX, x_places, extent_x),
        "gx",
        scatter_dimension=0,
        tiled=True,
    )
    spectrum = spectrum * (1.0 / math.sqrt(extent_x * extent_y))
    coeffs = spectrum.reshape(quota_rows, 2, planes, channels)
    weights = spectral_weight[0].astype(jnp.float32)
    product = jnp.einsum("rpzc,rco->rpzo", coeffs, weights, precision=high)
    mixed_real = product[:, 0, :, :channels] - product[:, 1, :, channels:]
    mixed_imag = product[:, 0, :, channels:] + product[:, 1, :, :channels]
    mixed_local = jnp.stack([mixed_real, mixed_imag], axis=1).reshape(quota_rows, 2 * feat_count)
    pointwise = jnp.einsum(
        "xyzc,co->xyzo",
        flow_field.reshape(cells_x, cells_y, planes, channels),
        local_weight,
        preferred_element_type=jnp.float32,
    )
    start_half = jnp.zeros((half_width, 2, cells_x, feat_count), jnp.float32)
    shard_rows = lax.all_gather(mixed_local, "gx", axis=0, tiled=True)
    rest_index = jnp.arange(shard_rows.shape[0], dtype=jnp.int32)
    back_half = inverse_rows(
        start_half, shard_rows, rest_index // MX, rest_index % MX, x_places, extent_x
    )
    back_whole = lax.all_gather(back_half, "gy", axis=0, tiled=True)
    y_cos = jnp.cos(y_angle)
    y_sin = jnp.sin(y_angle)
    spectral = (
        jnp.einsum("kn,kxf->xnf", y_cos, back_whole[:, 0], precision=high)
        - jnp.einsum("kn,kxf->xnf", y_sin, back_whole[:, 1], precision=high)
    ) * (1.0 / math.sqrt(MX * MY))
    total = spectral.reshape(cells_x, cells_y, planes, channels) + pointwise + bias_terms
    output = (
        jax.nn.gelu(total, approximate=False)
        .reshape(cells_x, cells_y, feat_count)
        .astype(jnp.bfloat16)
    )
    return (output, mixed_local.reshape(1, quota_rows, 2 * feat_count))


SMALL = pltpu.CompilerParams(vmem_limit_bytes=20 * 1024 * 1024)
LARGE = pltpu.CompilerParams(vmem_limit_bytes=53 * 1024 * 1024)
WIDTH = 256
BIAS_TERMS = 3
FIRST = 64
GELU_TERMS = (
    1.5957645177841187,
    0.29075613617897034,
    -0.0014313592109829187,
    -0.006452994421124458,
    0.0015898864949122071,
    -0.0001365363277727738,
)


def angles(count, places, extent):
    index = np.arange(count)
    waves = np.where(index < count // 2, index, index - count)
    product = (waves[:, None] * np.asarray(places)[None, :]) % extent
    return (np.float32(2.0 * math.pi / extent) * product.astype(np.float32)).astype(np.float64)


def split_table(table):
    high = table.astype(ml_dtypes.bfloat16)
    low = (table - high.astype(np.float64)).astype(ml_dtypes.bfloat16)
    return high, low


def split_terms(values):
    high = values.astype(jnp.bfloat16)
    low = (values - high.astype(jnp.float32)).astype(jnp.bfloat16)
    return high, low


def quad():
    place = lax.axis_index("gx")
    return place // 2, place % 2, lax.axis_index("gy")


def turns(layers):
    half = layers // 2
    return list(range(half, layers)) + list(range(half - 1, -1, -1))


def forward_x_table(cells_x, peers, rows_ky):
    extent = cells_x * peers
    angle = angles(MX, np.arange(extent), extent)
    cosine, sine = np.cos(angle), np.sin(angle)
    out = np.zeros((2, rows_ky, MX, extent, rows_ky, 2))
    for row in range(rows_ky):
        out[0, row, :, :, row, 0] = cosine
        out[0, row, :, :, row, 1] = sine
        out[1, row, :, :, row, 1] = cosine
        out[1, row, :, :, row, 0] = -sine
    return out.reshape(2 * rows_ky * MX, extent * rows_ky * 2)


def inverse_x_table(cells_x, peers, rows_ky):
    extent = cells_x * peers
    angle = angles(MX, np.arange(extent), extent)
    cosine, sine = np.cos(angle).T, np.sin(angle).T
    out = np.zeros((extent, rows_ky, 2, 2, rows_ky, MX))
    for row in range(rows_ky):
        out[:, row, 0, 0, row, :] = cosine
        out[:, row, 0, 1, row, :] = -sine
        out[:, row, 1, 1, row, :] = cosine
        out[:, row, 1, 0, row, :] = sine
    out = out.reshape(peers // 2, 2, cells_x * rows_ky * 2, 2 * rows_ky * MX)
    return np.moveaxis(out, 1, 0)


def inverse_y_table(cells_y, groups_y, peers, rows_ky):
    extent = cells_y * groups_y
    angle = angles(MY, np.arange(extent), extent)
    full = np.stack([np.cos(angle), -np.sin(angle)], axis=1)
    full = full.reshape(groups_y, peers, rows_ky, 2, groups_y, cells_y)
    out = np.zeros((groups_y, 2, cells_y, peers, 2, rows_ky, 2))
    for y in range(groups_y):
        for column in range(2):
            for peer in range(peers):
                for place in range(2):
                    half = y ^ place ^ column ^ (peer % 2)
                    out[y, column, :, peer, place] = np.moveaxis(full[half, peer, :, :, y], -1, 0)
    return out.reshape(groups_y, 2, cells_y, 4 * peers * rows_ky)


def output_table(table):
    high, low = split_table(table)
    parts = [high, high, low, np.ones(table.shape[:-1] + (BIAS_TERMS,), high.dtype)]
    used = 3 * table.shape[-1] + BIAS_TERMS
    parts.append(np.zeros(table.shape[:-1] + (-used % 256,), high.dtype))
    return np.concatenate(parts, axis=-1)


def dot(left, right):
    return jnp.dot(left, right, preferred_element_type=jnp.float32)


def column_of(x, y):
    return x ^ y


def forward_y_table(shape, extent, layers, rows_ky):
    z, x, y = quad()
    peers = 2 * layers
    row = lax.broadcasted_iota(jnp.int32, (shape[0], 1), 0)
    block = row // (2 * rows_ky)
    place = block // 2 % layers
    turn = jnp.where(place < layers // 2, place + layers // 2, layers - 1 - place)
    side = y ^ (1 - block // peers)
    owner = (side ^ (block % 2)) * peers + (z ^ turn) * 2 + column_of(x, side)
    index = owner * rows_ky + row // 2 % rows_ky
    y_places = lax.broadcasted_iota(jnp.int32, (1, shape[1]), 1) + y * shape[1]
    steps = (wave_number(index, MY) * y_places) & (extent - 1)
    angle = 2.0 * math.pi / extent * steps.astype(jnp.float32)
    return jnp.where(row % 2 == 0, jnp.cos(angle), -jnp.sin(angle)).astype(jnp.bfloat16)


def forward_y_kernel(extent, rows_ky, flow_hbm, send_ref, keep_ref, flow_ref, arrived):
    layers, _, rows, feat_count = send_ref.shape
    cells_x, cells_y, _ = flow_ref.shape
    rows = rows // cells_x
    copies = [
        pltpu.make_async_copy(flow_hbm.at[x], flow_ref.at[x], arrived.at[x])
        for x in range(cells_x)
    ]
    for copy in copies:
        copy.start()
    table = forward_y_table((2 * MY, cells_y), extent, layers, rows_ky)
    for x in range(cells_x):
        copies[x].wait()
        result = dot(table, flow_ref[x]).reshape(2, layers, 2, rows, feat_count)
        send_ref[:, :, x * rows : (x + 1) * rows, :] = result[0]
        keep_ref[:, :, x * rows : (x + 1) * rows, :] = result[1]


def forward_y(flow_field, extent, layers, rows_ky):
    cells_x, _, feat_count = flow_field.shape
    shape = jax.ShapeDtypeStruct((layers, 2, cells_x * 2 * rows_ky, feat_count), jnp.float32)
    return pl.pallas_call(
        functools.partial(forward_y_kernel, extent, rows_ky),
        in_specs=[pl.BlockSpec(memory_space=pltpu.HBM)],
        out_shape=[shape] * 2,
        scratch_shapes=[
            pltpu.VMEM(flow_field.shape, flow_field.dtype),
            pltpu.SemaphoreType.DMA((cells_x,)),
        ],
        compiler_params=LARGE,
        name="forward_y",
    )(flow_field)


def flip_core(block):
    return lax.ppermute(block, "gy", [(0, 1), (1, 0)])


def along_columns(blocks, peers):
    arrived = []
    for turn, block in zip(turns(len(blocks)), blocks):
        pairs = [
            (2 * place + core, 2 * (place ^ (2 * turn + column_of(0, core))) + core)
            for place in range(peers)
            for core in range(2)
        ]
        arrived.append(lax.ppermute(block, ("gx", "gy"), pairs))
    return arrived


def small_call(kernel, out_shape, name):
    return pl.pallas_call(kernel, out_shape=out_shape, compiler_params=SMALL, name=name)


def second_kernel(*refs):
    for index, block_ref in enumerate(refs[:-1]):
        refs[-1][index] = block_ref[1]


def second_halves(blocks):
    shape = jax.ShapeDtypeStruct((len(blocks),) + blocks[0].shape[1:], blocks[0].dtype)
    return small_call(second_kernel, shape, "second_halves")(*blocks)


def stack_kernel(*refs):
    for index, block_ref in enumerate(refs[:-1]):
        refs[-1][index] = block_ref[...]


def stack_blocks(blocks):
    shape = jax.ShapeDtypeStruct((len(blocks),) + blocks[0].shape, blocks[0].dtype)
    return small_call(stack_kernel, shape, "stack_blocks")(*blocks)


def add_kernel(keep_ref, arrived_ref, *out_refs):
    for turn, out_ref in enumerate(out_refs):
        out_ref[...] = keep_ref[turn] + arrived_ref[turn]


def add_blocks(keep, arrived):
    shape = jax.ShapeDtypeStruct(keep.shape[1:], keep.dtype)
    return small_call(add_kernel, [shape] * keep.shape[0], "add_blocks")(keep, arrived)


def join_kernel(keep_ref, arrived_ref, *out_refs):
    cells_x, rows, _ = out_refs[0].shape
    rows = rows // 2
    for turn, out_ref in enumerate(out_refs):
        for cell in range(cells_x):
            span = slice(cell * rows, (cell + 1) * rows)
            out_ref[cell] = jnp.concatenate(
                [keep_ref[turn, span, :], arrived_ref[turn, span, :]], axis=0
            )


def join_blocks(keep, arrived, cells_x):
    layers, rows, feat_count = keep.shape
    shape = jax.ShapeDtypeStruct((cells_x, 2 * rows // cells_x, feat_count), keep.dtype)
    return small_call(join_kernel, [shape] * layers, "join_blocks")(keep, arrived)


def back_rows(inverse_high, inverse_low, modes, shape, other):
    z, x, y = quad()
    places = [(column_of(x, y) ^ other, z ^ turn) for turn in turns(shape[0])]
    table_high, table_low = [
        jnp.concatenate([ref[column, place] for column, place in places], axis=0)
        for ref in (inverse_high, inverse_low)
    ]
    high, low = split_terms(modes)
    back = dot(table_high, high) + dot(table_high, low) + dot(table_low, high)
    return back.reshape(shape)


def mix_kernel(layers, *refs):
    block_refs, arrived_ref = refs[:layers], refs[layers]
    weight_ref, forward_high, forward_low, inverse_high, inverse_low = refs[
        layers + 1 : layers + 6
    ]
    modes_ref, send_ref, order_ref, spread_ref, result_ref = refs[layers + 6 :]
    z, x, y = quad()
    for index, turn in enumerate(turns(layers)):
        column = column_of(x, y)
        order_ref[(z ^ turn) * 2 + column] = block_refs[index][0]
        order_ref[(z ^ turn) * 2 + (column ^ 1)] = arrived_ref[index]
    feat_count = order_ref.shape[-1]
    count = weight_ref.shape[1]
    channels = weight_ref.shape[2]
    tiles = feat_count // 128
    group = 2 * tiles
    high, low = split_terms(order_ref[...].reshape(-1, feat_count))
    spectrum = (
        dot(forward_high[...], high) + dot(forward_high[...], low) + dot(forward_low[...], high)
    )
    for part in range(2):
        for tile in range(tiles):
            spread_ref[pl.ds(part * tiles + tile, count, stride=group), :] = spectrum[
                part * count : (part + 1) * count, tile * 128 : (tile + 1) * 128
            ]
    rows = lax.broadcasted_iota(jnp.int32, (8, 128), 0) % group
    lane = lax.broadcasted_iota(jnp.int32, (8, 128), 1) < channels
    sign = jnp.where(rows < tiles, -1.0, 1.0)
    for base in range(0, count * group, 8):
        block = spread_ref[base : base + 8, :]
        turned = pltpu.roll(block, channels, 1)
        firsts, seconds = [], []
        for start in range(0, 8, group):
            span = slice(start, start + group)
            left = jnp.concatenate([block[span], turned[span]], axis=0)[:, :channels]
            left_high, left_low = split_terms(left)
            left = jnp.concatenate([left_high, left_low], axis=0)
            product = dot(left, weight_ref[0, (base + start) // group])
            product = product[: 2 * group] + product[2 * group :]
            firsts.append(product[:group])
            seconds.append(product[group:])
        first = jnp.concatenate(firsts, axis=0)
        second = jnp.concatenate(seconds, axis=0)
        real = jnp.where(lane, first, pltpu.roll(second, channels, 1))
        imag = jnp.where(lane, pltpu.roll(first, channels, 1), second)
        crossed = jnp.where(rows < tiles, pltpu.roll(imag, 8 - tiles, 0), pltpu.roll(imag, tiles, 0))
        result_ref[base : base + 8, :] = real + sign * crossed
    for part in range(2):
        for tile in range(tiles):
            modes_ref[part * count : (part + 1) * count, tile * 128 : (tile + 1) * 128] = (
                result_ref[pl.ds(part * tiles + tile, count, stride=group), :]
            )
    send_ref[...] = back_rows(inverse_high, inverse_low, modes_ref[...], send_ref.shape, 1)


def mix(blocks, arrived, weights, forward_table, inverse_tables):
    layers = len(blocks)
    _, rows, feat_count = blocks[0].shape
    count = weights.shape[1]
    scratch = pltpu.VMEM((count * feat_count // 64, 128), jnp.float32)
    return pl.pallas_call(
        functools.partial(mix_kernel, layers),
        out_shape=[
            jax.ShapeDtypeStruct((2 * count, feat_count), jnp.float32),
            jax.ShapeDtypeStruct((layers, rows, feat_count), jnp.float32),
        ],
        scratch_shapes=[pltpu.VMEM((2 * layers, rows, feat_count), jnp.float32), scratch, scratch],
        compiler_params=SMALL,
        name="mix",
    )(*blocks, arrived, weights, *split_table(forward_table), *inverse_tables)


def keep_kernel(modes_ref, inverse_high, inverse_low, mixed_ref, keep_ref):
    count = mixed_ref.shape[1]
    feat_count = modes_ref.shape[1]
    for part in range(2):
        mixed_ref[0, :, part * feat_count : (part + 1) * feat_count] = modes_ref[
            part * count : (part + 1) * count
        ]
    keep_ref[...] = back_rows(inverse_high, inverse_low, modes_ref[...], keep_ref.shape, 0)


def keep_rows(modes, inverse_tables, like):
    rows, feat_count = modes.shape
    return pl.pallas_call(
        keep_kernel,
        out_shape=[
            jax.ShapeDtypeStruct((1, rows // 2, 2 * feat_count), jnp.float32),
            jax.ShapeDtypeStruct(like.shape, jnp.float32),
        ],
        compiler_params=SMALL,
        name="keep_rows",
    )(modes, *inverse_tables)


def gelu(half):
    square = jnp.minimum(half * half, 6.25)
    inner = jnp.full_like(square, GELU_TERMS[-1])
    for term in GELU_TERMS[-2::-1]:
        inner = inner * square + term
    return half + half * jnp.tanh(half * inner)


def output_kernel(layers, flow_ref, table_ref, local_ref, bias_ref, *refs):
    own_refs = refs[:layers]
    core_refs = [ref.at[index] for ref in refs[layers : layers + 2] for index in range(layers // 2)]
    out_hbm, order_ref, wide_ref, level_ref, done_ref, sent = refs[layers + 2 :]
    cells_x, _, feat_count = flow_ref.shape
    channels = local_ref.shape[0]
    z, x, y = quad()
    wide_ref[...] = jnp.zeros_like(wide_ref)
    for start in range(0, WIDTH, channels):
        span = slice(start, start + channels)
        wide_ref[span, span] = local_ref[...] * 0.5
        level_ref[:, span] = bias_ref[...].reshape(1, channels) * 0.5
    level = level_ref[...]
    levels = []
    for _ in range(BIAS_TERMS):
        levels.append(level.astype(jnp.bfloat16).astype(jnp.float32))
        level = level - levels[-1]
    terms = 3 * order_ref.shape[1] * order_ref.shape[2]
    filled = jnp.zeros((table_ref.shape[-1] - terms - BIAS_TERMS, WIDTH), jnp.float32)
    below = jnp.concatenate(levels + [filled], axis=0).astype(jnp.bfloat16)
    below = jnp.concatenate([below, wide_ref[...]], axis=0)
    for column, block_refs in ((x ^ y, own_refs), (x ^ y ^ 1, core_refs)):
        for turn, block_ref in zip(turns(layers), block_refs):
            order_ref[:, (z ^ turn) * 2 + column] = block_ref[...]
    table = table_ref[y, x ^ y]
    copies = []
    for cell in range(cells_x):
        high, low = split_terms(order_ref[cell].reshape(-1, feat_count))
        stack = jnp.concatenate([high, low, high], axis=0)
        for start in range(0, feat_count, WIDTH):
            columns = slice(start, start + WIDTH)
            total = dot(
                jnp.concatenate([table, flow_ref[cell, :, columns]], axis=1),
                jnp.concatenate([stack[:, columns], below], axis=0),
            )
            done_ref[cell, :, columns] = gelu(total).astype(done_ref.dtype)
        copies.append(pltpu.make_async_copy(done_ref.at[cell], out_hbm.at[cell], sent.at[cell]))
        copies[-1].start()
    for copy in copies:
        copy.wait()


def make_output(flow_field, parts, table, local, bias):
    cells_x, _, feat_count = flow_field.shape
    layers = len(parts) - 2
    return pl.pallas_call(
        functools.partial(output_kernel, layers),
        out_specs=pl.BlockSpec(memory_space=pl.ANY),
        scratch_shapes=[
            pltpu.VMEM((cells_x, 2 * layers) + parts[0].shape[1:], jnp.float32),
            pltpu.VMEM((WIDTH, WIDTH), jnp.bfloat16),
            pltpu.VMEM((1, WIDTH), jnp.float32),
            pltpu.VMEM(flow_field.shape, jnp.bfloat16),
            pltpu.SemaphoreType.DMA((cells_x,)),
        ],
        out_shape=jax.ShapeDtypeStruct(flow_field.shape, jnp.bfloat16),
        compiler_params=SMALL,
        name="make_output",
    )(flow_field, table, local, bias, *parts)


def row_body(flow_field, spectral_weight, local_weight, bias_terms):
    cells_x, cells_y, feat_count = flow_field.shape
    peers = lax.axis_size("gx")
    groups_y = lax.axis_size("gy")
    rows_ky = MY // groups_y // peers
    forward_scale = 1.0 / math.sqrt(cells_x * peers * cells_y * groups_y)
    inverse_scale = 1.0 / math.sqrt(MX * MY)

    send, keep = forward_y(flow_field, cells_y * groups_y, peers // 2, rows_ky)
    blocks = along_columns(add_blocks(keep, flip_core(send)), peers)
    inverse_tables = split_table(inverse_x_table(cells_x, peers, rows_ky))
    modes, send = mix(
        blocks,
        flip_core(second_halves(blocks)),
        spectral_weight,
        forward_x_table(cells_x, peers, rows_ky) * forward_scale,
        inverse_tables,
    )
    arrived = flip_core(send)
    mixed, keep = keep_rows(modes, inverse_tables, send)
    own = along_columns(join_blocks(keep, arrived, cells_x), peers)
    middle = len(own) // 2
    parts = own + [flip_core(stack_blocks(half)) for half in (own[:middle], own[middle:])]
    table = output_table(inverse_y_table(cells_y, groups_y, peers, rows_ky) * (0.5 * inverse_scale))
    return make_output(flow_field, parts, table, local_weight, bias_terms), mixed


def body(flow_field, spectral_weight, local_weight, bias_terms):
    peers = lax.axis_size("gx")
    extent = lax.axis_size("gy") * flow_field.shape[1]
    paired = lax.axis_size("gy") == 2 and peers & (peers - 1) == 0 and extent & (extent - 1) == 0
    if paired and spectral_weight.shape[1] == 2 * MX and WIDTH % local_weight.shape[0] == 0:
        return row_body(flow_field, spectral_weight, local_weight, bias_terms)
    return general_body(flow_field, spectral_weight, local_weight, bias_terms)


def solution(mesh):
    placed = (P(("group", "gx"), "gy", None), P("gy", "gx", None, None), P(), P())
    return jax.shard_map(
        body,
        mesh=mesh,
        in_specs=placed,
        out_specs=(P(("group", "gx"), "gy", None), P(("group", "gy"), "gx", None)),
        check_vma=False,
    )
```

```python
import functools
import math

import jax
import jax.numpy as jnp
import ml_dtypes
import numpy as np
from jax import lax
from jax.experimental import pallas as pl
from jax.experimental.pallas import tpu as pltpu
from jax.sharding import PartitionSpec as P

MX = 32
MY = 32


def wave_number(index, count):
    return jnp.where(index < count // 2, index, index - count)


def phase_table(waves, places, extent):
    product = waves[:, None] * places[None, :] % extent
    return 2.0 * math.pi / extent * product.astype(jnp.float32)


def row_tables(ky_rows, kx_rows, x_places, extent, width):
    angle = phase_table(wave_number(kx_rows, MX), x_places, extent)
    select = (ky_rows[:, None] == jnp.arange(width, dtype=jnp.int32)[None, :]).astype(jnp.float32)
    cosine = jnp.cos(angle)[:, :, None] * select[:, None, :]
    sine_part = jnp.sin(angle)[:, :, None] * select[:, None, :]
    return (cosine, sine_part)


def forward_rows(y_local, ky_rows, kx_rows, x_places, extent):
    cosine, sine_part = row_tables(ky_rows, kx_rows, x_places, extent, y_local.shape[0])
    real_in = y_local[:, 0]
    imag_in = y_local[:, 1]

    def contract(table, values):
        return jnp.einsum("rxk,kxf->rf", table, values, precision=lax.Precision.HIGHEST)

    real_out = contract(cosine, real_in) + contract(sine_part, imag_in)
    imag_out = contract(cosine, imag_in) - contract(sine_part, real_in)
    return jnp.concatenate([real_out, imag_out], axis=1)


def inverse_rows(running, shard_rows, ky_rows, kx_rows, x_places, extent):
    cosine, sine_part = row_tables(ky_rows, kx_rows, x_places, extent, running.shape[0])
    feat_count = shard_rows.shape[1] // 2
    real_part = shard_rows[:, :feat_count]
    imag_part = shard_rows[:, feat_count:]

    def contract(table, values):
        return jnp.einsum("rxk,rf->kxf", table, values, precision=lax.Precision.HIGHEST)

    new_real = contract(cosine, real_part) - contract(sine_part, imag_part)
    new_imag = contract(cosine, imag_part) + contract(sine_part, real_part)
    return jnp.stack([new_real, new_imag], axis=1)


def general_body(flow_field, spectral_weight, local_weight, bias_terms):
    cells_x, cells_y, feat_count = flow_field.shape
    channels = local_weight.shape[0]
    planes = feat_count // channels
    groups_x = lax.axis_size("gx")
    groups_y = lax.axis_size("gy")
    extent_x = cells_x * groups_x
    extent_y = cells_y * groups_y
    half_width = MY // groups_y
    quota_rows = spectral_weight.shape[1]
    high = lax.Precision.HIGHEST
    x_places = lax.axis_index("gx") * cells_x + jnp.arange(cells_x, dtype=jnp.int32)
    y_places = lax.axis_index("gy") * cells_y + jnp.arange(cells_y, dtype=jnp.int32)
    y_angle = phase_table(wave_number(jnp.arange(MY, dtype=jnp.int32), MY), y_places, extent_y)
    y_table = (
        jnp.stack([jnp.cos(y_angle), -jnp.sin(y_angle)], axis=1)
        .reshape(2 * MY, cells_y)
        .astype(jnp.bfloat16)
    )
    y_local = lax.psum_scatter(
        jnp.einsum("qy,xyf->qxf", y_table, flow_field, preferred_element_type=jnp.float32),
        "gy",
        scatter_dimension=0,
        tiled=True,
    )
    y_local = y_local.reshape(half_width, 2, cells_x, feat_count)
    rest_index = jnp.arange(lax.axis_size("gx") * quota_rows, dtype=jnp.int32)
    spectrum = lax.psum_scatter(
        forward_rows(y_local, rest_index // MX, rest_index % MX, x_places, extent_x),
        "gx",
        scatter_dimension=0,
        tiled=True,
    )
    spectrum = spectrum * (1.0 / math.sqrt(extent_x * extent_y))
    coeffs = spectrum.reshape(quota_rows, 2, planes, channels)
    weights = spectral_weight[0].astype(jnp.float32)
    product = jnp.einsum("rpzc,rco->rpzo", coeffs, weights, precision=high)
    mixed_real = product[:, 0, :, :channels] - product[:, 1, :, channels:]
    mixed_imag = product[:, 0, :, channels:] + product[:, 1, :, :channels]
    mixed_local = jnp.stack([mixed_real, mixed_imag], axis=1).reshape(quota_rows, 2 * feat_count)
    pointwise = jnp.einsum(
        "xyzc,co->xyzo",
        flow_field.reshape(cells_x, cells_y, planes, channels),
        local_weight,
        preferred_element_type=jnp.float32,
    )
    start_half = jnp.zeros((half_width, 2, cells_x, feat_count), jnp.float32)
    shard_rows = lax.all_gather(mixed_local, "gx", axis=0, tiled=True)
    rest_index = jnp.arange(shard_rows.shape[0], dtype=jnp.int32)
    back_half = inverse_rows(
        start_half, shard_rows, rest_index // MX, rest_index % MX, x_places, extent_x
    )
    back_whole = lax.all_gather(back_half, "gy", axis=0, tiled=True)
    y_cos = jnp.cos(y_angle)
    y_sin = jnp.sin(y_angle)
    spectral = (
        jnp.einsum("kn,kxf->xnf", y_cos, back_whole[:, 0], precision=high)
        - jnp.einsum("kn,kxf->xnf", y_sin, back_whole[:, 1], precision=high)
    ) * (1.0 / math.sqrt(MX * MY))
    total = spectral.reshape(cells_x, cells_y, planes, channels) + pointwise + bias_terms
    output = (
        jax.nn.gelu(total, approximate=False)
        .reshape(cells_x, cells_y, feat_count)
        .astype(jnp.bfloat16)
    )
    return (output, mixed_local.reshape(1, quota_rows, 2 * feat_count))


SMALL = pltpu.CompilerParams(vmem_limit_bytes=20 * 1024 * 1024)
LARGE = pltpu.CompilerParams(vmem_limit_bytes=53 * 1024 * 1024)
WIDTH = 256
BIAS_TERMS = 3
FIRST = 64
GELU_TERMS = (
    1.5957645177841187,
    0.29075613617897034,
    -0.0014313592109829187,
    -0.006452994421124458,
    0.0015898864949122071,
    -0.0001365363277727738,
)


def angles(count, places, extent):
    index = np.arange(count)
    waves = np.where(index < count // 2, index, index - count)
    product = (waves[:, None] * np.asarray(places)[None, :]) % extent
    return (np.float32(2.0 * math.pi / extent) * product.astype(np.float32)).astype(np.float64)


def split_table(table):
    high = table.astype(ml_dtypes.bfloat16)
    low = (table - high.astype(np.float64)).astype(ml_dtypes.bfloat16)
    return high, low


def split_terms(values):
    high = values.astype(jnp.bfloat16)
    low = (values - high.astype(jnp.float32)).astype(jnp.bfloat16)
    return high, low


def quad():
    place = lax.axis_index("gx")
    return place // 2, place % 2, lax.axis_index("gy")


def partner(index, layers, y):
    turn = index // 2
    return layers // 2 - 1 - turn + y * (2 * turn + 1), index % 2


def peer_of(index, layers, y):
    z, x, _ = quad()
    turn, flip = partner(index, layers, y)
    return (z ^ turn) * 2 + (x ^ flip)


def forward_x_table(cells_x, peers, rows_ky):
    extent = cells_x * peers
    angle = angles(MX, np.arange(extent), extent)
    cosine, sine = np.cos(angle), np.sin(angle)
    out = np.zeros((2, rows_ky, MX, extent, rows_ky, 2))
    for row in range(rows_ky):
        out[0, row, :, :, row, 0] = cosine
        out[0, row, :, :, row, 1] = sine
        out[1, row, :, :, row, 1] = cosine
        out[1, row, :, :, row, 0] = -sine
    return out.reshape(2 * rows_ky * MX, extent * rows_ky * 2)


def inverse_x_table(cells_x, peers, rows_ky):
    extent = cells_x * peers
    angle = angles(MX, np.arange(extent), extent)
    cosine, sine = np.cos(angle).T, np.sin(angle).T
    out = np.zeros((extent, rows_ky, 2, 2, rows_ky, MX))
    for row in range(rows_ky):
        out[:, row, 0, 0, row, :] = cosine
        out[:, row, 0, 1, row, :] = -sine
        out[:, row, 1, 1, row, :] = cosine
        out[:, row, 1, 0, row, :] = sine
    out = out.reshape(peers // 2, 2, cells_x * rows_ky * 2, 2 * rows_ky * MX)
    return np.moveaxis(out, 1, 0)


def inverse_y_table(cells_y, groups_y, peers, rows_ky):
    extent = cells_y * groups_y
    angle = angles(MY, np.arange(extent), extent)
    full = np.stack([np.cos(angle), -np.sin(angle)], axis=1)
    full = full.reshape(groups_y, peers, rows_ky, 2, groups_y, cells_y)
    out = np.zeros((groups_y, 2, cells_y, peers, 2, rows_ky, 2))
    for y in range(groups_y):
        for near in range(2):
            for peer in range(peers):
                far = peer // (peers // 2) ^ near
                for place in range(2):
                    block = full[place ^ far, peer, :, :, y]
                    out[y, near, :, peer, place] = np.moveaxis(block, -1, 0)
    return out.reshape(groups_y, 2, cells_y, 4 * peers * rows_ky)


def output_table(table):
    high, low = split_table(table)
    parts = [high, high, low, np.ones(table.shape[:-1] + (BIAS_TERMS,), high.dtype)]
    used = 3 * table.shape[-1] + BIAS_TERMS
    parts.append(np.zeros(table.shape[:-1] + (-used % 256,), high.dtype))
    return np.concatenate(parts, axis=-1)


def dot(left, right):
    return jnp.dot(left, right, preferred_element_type=jnp.float32)


def forward_y_table(shape, extent, layers, rows_ky):
    z, x, y = quad()
    peers = 2 * layers
    row = lax.broadcasted_iota(jnp.int32, (shape[0], 1), 0)
    block = row // (2 * rows_ky)
    side = y ^ (1 - block // peers)
    turn, flip = partner(block // 2 % layers, layers, side)
    owner = (side ^ (block % 2)) * peers + (z ^ turn) * 2 + (x ^ flip)
    index = owner * rows_ky + row // 2 % rows_ky
    y_places = lax.broadcasted_iota(jnp.int32, (1, shape[1]), 1) + y * shape[1]
    steps = (wave_number(index, MY) * y_places) & (extent - 1)
    angle = 2.0 * math.pi / extent * steps.astype(jnp.float32)
    return jnp.where(row % 2 == 0, jnp.cos(angle), -jnp.sin(angle)).astype(jnp.bfloat16)


def forward_y_kernel(extent, rows_ky, flow_hbm, send_ref, keep_ref, flow_ref, arrived):
    layers, _, rows, feat_count = send_ref.shape
    cells_x, cells_y, _ = flow_ref.shape
    rows = rows // cells_x
    copies = [
        pltpu.make_async_copy(flow_hbm.at[x], flow_ref.at[x], arrived.at[x])
        for x in range(cells_x)
    ]
    for copy in copies:
        copy.start()
    table = forward_y_table((2 * MY, cells_y), extent, layers, rows_ky)
    for x in range(cells_x):
        copies[x].wait()
        result = dot(table, flow_ref[x]).reshape(2, layers, 2, rows, feat_count)
        send_ref[:, :, x * rows : (x + 1) * rows, :] = result[0]
        keep_ref[:, :, x * rows : (x + 1) * rows, :] = result[1]


def forward_y(flow_field, extent, layers, rows_ky):
    cells_x, _, feat_count = flow_field.shape
    shape = jax.ShapeDtypeStruct((layers, 2, cells_x * 2 * rows_ky, feat_count), jnp.float32)
    return pl.pallas_call(
        functools.partial(forward_y_kernel, extent, rows_ky),
        in_specs=[pl.BlockSpec(memory_space=pltpu.HBM)],
        out_shape=[shape] * 2,
        scratch_shapes=[
            pltpu.VMEM(flow_field.shape, flow_field.dtype),
            pltpu.SemaphoreType.DMA((cells_x,)),
        ],
        compiler_params=LARGE,
        name="forward_y",
    )(flow_field)


def flip_core(block):
    return lax.ppermute(block, "gy", [(0, 1), (1, 0)])


def along_chips(blocks, peers):
    arrived = []
    for index, block in enumerate(blocks):
        pairs = []
        for core in range(2):
            turn, flip = partner(index, len(blocks), core)
            pairs += [
                (2 * place + core, 2 * (place ^ (2 * turn + flip)) + core) for place in range(peers)
            ]
        arrived.append(lax.ppermute(block, ("gx", "gy"), pairs))
    return arrived


def small_call(kernel, out_shape, name):
    return pl.pallas_call(kernel, out_shape=out_shape, compiler_params=SMALL, name=name)


def second_kernel(*refs):
    for index, block_ref in enumerate(refs[:-1]):
        refs[-1][index] = block_ref[1]


def second_halves(blocks):
    shape = jax.ShapeDtypeStruct((len(blocks),) + blocks[0].shape[1:], blocks[0].dtype)
    return small_call(second_kernel, shape, "second_halves")(*blocks)


def stack_kernel(*refs):
    for index, block_ref in enumerate(refs[:-1]):
        refs[-1][index] = block_ref[...]


def stack_blocks(blocks):
    shape = jax.ShapeDtypeStruct((len(blocks),) + blocks[0].shape, blocks[0].dtype)
    return small_call(stack_kernel, shape, "stack_blocks")(*blocks)


def add_kernel(keep_ref, arrived_ref, *out_refs):
    for turn, out_ref in enumerate(out_refs):
        out_ref[...] = keep_ref[turn] + arrived_ref[turn]


def add_blocks(keep, arrived):
    shape = jax.ShapeDtypeStruct(keep.shape[1:], keep.dtype)
    return small_call(add_kernel, [shape] * keep.shape[0], "add_blocks")(keep, arrived)


def join_kernel(keep_ref, arrived_ref, *out_refs):
    cells_x, rows, _ = out_refs[0].shape
    rows = rows // 2
    for turn, out_ref in enumerate(out_refs):
        for cell in range(cells_x):
            span = slice(cell * rows, (cell + 1) * rows)
            out_ref[cell] = jnp.concatenate(
                [keep_ref[turn, span, :], arrived_ref[turn, span, :]], axis=0
            )


def join_blocks(keep, arrived, cells_x):
    layers, rows, feat_count = keep.shape
    shape = jax.ShapeDtypeStruct((cells_x, 2 * rows // cells_x, feat_count), keep.dtype)
    return small_call(join_kernel, [shape] * layers, "join_blocks")(keep, arrived)


def back_rows(inverse_high, inverse_low, modes, shape, other):
    z, x, y = quad()
    places = []
    for index in range(shape[0]):
        turn, flip = partner(index, shape[0], y ^ other)
        places.append((x ^ flip, z ^ turn))
    table_high, table_low = [
        jnp.concatenate([ref[column, place] for column, place in places], axis=0)
        for ref in (inverse_high, inverse_low)
    ]
    high, low = split_terms(modes)
    back = dot(table_high, high) + dot(table_high, low) + dot(table_low, high)
    return back.reshape(shape)


def mix_kernel(layers, *refs):
    block_refs, arrived_ref = refs[:layers], refs[layers]
    weight_ref, forward_high, forward_low, inverse_high, inverse_low = refs[
        layers + 1 : layers + 6
    ]
    modes_ref, send_ref, order_ref, spread_ref, result_ref = refs[layers + 6 :]
    _, _, y = quad()
    for index in range(layers):
        order_ref[peer_of(index, layers, y)] = block_refs[index][0]
        order_ref[peer_of(index, layers, 1 - y)] = arrived_ref[index]
    feat_count = order_ref.shape[-1]
    count = weight_ref.shape[1]
    channels = weight_ref.shape[2]
    tiles = feat_count // 128
    group = 2 * tiles
    high, low = split_terms(order_ref[...].reshape(-1, feat_count))
    spectrum = (
        dot(forward_high[...], high) + dot(forward_high[...], low) + dot(forward_low[...], high)
    )
    for part in range(2):
        for tile in range(tiles):
            spread_ref[pl.ds(part * tiles + tile, count, stride=group), :] = spectrum[
                part * count : (part + 1) * count, tile * 128 : (tile + 1) * 128
            ]
    rows = lax.broadcasted_iota(jnp.int32, (8, 128), 0) % group
    lane = lax.broadcasted_iota(jnp.int32, (8, 128), 1) < channels
    sign = jnp.where(rows < tiles, -1.0, 1.0)
    for base in range(0, count * group, 8):
        block = spread_ref[base : base + 8, :]
        turned = pltpu.roll(block, channels, 1)
        firsts, seconds = [], []
        for start in range(0, 8, group):
            span = slice(start, start + group)
            left = jnp.concatenate([block[span], turned[span]], axis=0)[:, :channels]
            left_high, left_low = split_terms(left)
            left = jnp.concatenate([left_high, left_low], axis=0)
            product = dot(left, weight_ref[0, (base + start) // group])
            product = product[: 2 * group] + product[2 * group :]
            firsts.append(product[:group])
            seconds.append(product[group:])
        first = jnp.concatenate(firsts, axis=0)
        second = jnp.concatenate(seconds, axis=0)
        real = jnp.where(lane, first, pltpu.roll(second, channels, 1))
        imag = jnp.where(lane, pltpu.roll(first, channels, 1), second)
        crossed = jnp.where(rows < tiles, pltpu.roll(imag, 8 - tiles, 0), pltpu.roll(imag, tiles, 0))
        result_ref[base : base + 8, :] = real + sign * crossed
    for part in range(2):
        for tile in range(tiles):
            modes_ref[part * count : (part + 1) * count, tile * 128 : (tile + 1) * 128] = (
                result_ref[pl.ds(part * tiles + tile, count, stride=group), :]
            )
    send_ref[...] = back_rows(inverse_high, inverse_low, modes_ref[...], send_ref.shape, 1)


def mix(blocks, arrived, weights, forward_table, inverse_tables):
    layers = len(blocks)
    _, rows, feat_count = blocks[0].shape
    count = weights.shape[1]
    scratch = pltpu.VMEM((count * feat_count // 64, 128), jnp.float32)
    return pl.pallas_call(
        functools.partial(mix_kernel, layers),
        out_shape=[
            jax.ShapeDtypeStruct((2 * count, feat_count), jnp.float32),
            jax.ShapeDtypeStruct((layers, rows, feat_count), jnp.float32),
        ],
        scratch_shapes=[pltpu.VMEM((2 * layers, rows, feat_count), jnp.float32), scratch, scratch],
        compiler_params=SMALL,
        name="mix",
    )(*blocks, arrived, weights, *split_table(forward_table), *inverse_tables)


def keep_kernel(modes_ref, inverse_high, inverse_low, mixed_ref, keep_ref):
    count = mixed_ref.shape[1]
    feat_count = modes_ref.shape[1]
    for part in range(2):
        mixed_ref[0, :, part * feat_count : (part + 1) * feat_count] = modes_ref[
            part * count : (part + 1) * count
        ]
    keep_ref[...] = back_rows(inverse_high, inverse_low, modes_ref[...], keep_ref.shape, 0)


def keep_rows(modes, inverse_tables, like):
    rows, feat_count = modes.shape
    return pl.pallas_call(
        keep_kernel,
        out_shape=[
            jax.ShapeDtypeStruct((1, rows // 2, 2 * feat_count), jnp.float32),
            jax.ShapeDtypeStruct(like.shape, jnp.float32),
        ],
        compiler_params=SMALL,
        name="keep_rows",
    )(modes, *inverse_tables)


def gelu(half):
    square = jnp.minimum(half * half, 6.25)
    inner = jnp.full_like(square, GELU_TERMS[-1])
    for term in GELU_TERMS[-2::-1]:
        inner = inner * square + term
    return half + half * jnp.tanh(half * inner)


def output_kernel(layers, flow_ref, table_ref, local_ref, bias_ref, *refs):
    own_refs = refs[:layers]
    core_refs = [ref.at[index] for ref in refs[layers : layers + 2] for index in range(layers // 2)]
    out_hbm, order_ref, wide_ref, level_ref, done_ref, sent = refs[layers + 2 :]
    cells_x, _, feat_count = flow_ref.shape
    channels = local_ref.shape[0]
    z, x, y = quad()
    wide_ref[...] = jnp.zeros_like(wide_ref)
    for start in range(0, WIDTH, channels):
        span = slice(start, start + channels)
        wide_ref[span, span] = local_ref[...] * 0.5
        level_ref[:, span] = bias_ref[...].reshape(1, channels) * 0.5
    level = level_ref[...]
    levels = []
    for _ in range(BIAS_TERMS):
        levels.append(level.astype(jnp.bfloat16).astype(jnp.float32))
        level = level - levels[-1]
    terms = 3 * order_ref.shape[1] * order_ref.shape[2]
    filled = jnp.zeros((table_ref.shape[-1] - terms - BIAS_TERMS, WIDTH), jnp.float32)
    below = jnp.concatenate(levels + [filled], axis=0).astype(jnp.bfloat16)
    below = jnp.concatenate([below, wide_ref[...]], axis=0)
    for core, block_refs in ((y, own_refs), (1 - y, core_refs)):
        for index, block_ref in enumerate(block_refs):
            order_ref[:, peer_of(index, layers, core)] = block_ref[...]
    table = table_ref[y, z // (layers // 2)]
    copies = []
    for cell in range(cells_x):
        high, low = split_terms(order_ref[cell].reshape(-1, feat_count))
        stack = jnp.concatenate([high, low, high], axis=0)
        for start in range(0, feat_count, WIDTH):
            columns = slice(start, start + WIDTH)
            total = dot(
                jnp.concatenate([table, flow_ref[cell, :, columns]], axis=1),
                jnp.concatenate([stack[:, columns], below], axis=0),
            )
            done_ref[cell, :, columns] = gelu(total).astype(done_ref.dtype)
        copies.append(pltpu.make_async_copy(done_ref.at[cell], out_hbm.at[cell], sent.at[cell]))
        copies[-1].start()
    for copy in copies:
        copy.wait()


def make_output(flow_field, parts, table, local, bias):
    cells_x, _, feat_count = flow_field.shape
    layers = len(parts) - 2
    return pl.pallas_call(
        functools.partial(output_kernel, layers),
        out_specs=pl.BlockSpec(memory_space=pl.ANY),
        scratch_shapes=[
            pltpu.VMEM((cells_x, 2 * layers) + parts[0].shape[1:], jnp.float32),
            pltpu.VMEM((WIDTH, WIDTH), jnp.bfloat16),
            pltpu.VMEM((1, WIDTH), jnp.float32),
            pltpu.VMEM(flow_field.shape, jnp.bfloat16),
            pltpu.SemaphoreType.DMA((cells_x,)),
        ],
        out_shape=jax.ShapeDtypeStruct(flow_field.shape, jnp.bfloat16),
        compiler_params=SMALL,
        name="make_output",
    )(flow_field, table, local, bias, *parts)


def row_body(flow_field, spectral_weight, local_weight, bias_terms):
    cells_x, cells_y, feat_count = flow_field.shape
    peers = lax.axis_size("gx")
    groups_y = lax.axis_size("gy")
    rows_ky = MY // groups_y // peers
    forward_scale = 1.0 / math.sqrt(cells_x * peers * cells_y * groups_y)
    inverse_scale = 1.0 / math.sqrt(MX * MY)

    send, keep = forward_y(flow_field, cells_y * groups_y, peers // 2, rows_ky)
    blocks = along_chips(add_blocks(keep, flip_core(send)), peers)
    inverse_tables = split_table(inverse_x_table(cells_x, peers, rows_ky))
    modes, send = mix(
        blocks,
        flip_core(second_halves(blocks)),
        spectral_weight,
        forward_x_table(cells_x, peers, rows_ky) * forward_scale,
        inverse_tables,
    )
    arrived = flip_core(send)
    mixed, keep = keep_rows(modes, inverse_tables, send)
    own = along_chips(join_blocks(keep, arrived, cells_x), peers)
    middle = len(own) // 2
    parts = own + [flip_core(stack_blocks(half)) for half in (own[:middle], own[middle:])]
    table = output_table(inverse_y_table(cells_y, groups_y, peers, rows_ky) * (0.5 * inverse_scale))
    return make_output(flow_field, parts, table, local_weight, bias_terms), mixed


def body(flow_field, spectral_weight, local_weight, bias_terms):
    peers = lax.axis_size("gx")
    extent = lax.axis_size("gy") * flow_field.shape[1]
    paired = lax.axis_size("gy") == 2 and peers & (peers - 1) == 0 and extent & (extent - 1) == 0
    if paired and spectral_weight.shape[1] == 2 * MX and WIDTH % local_weight.shape[0] == 0:
        return row_body(flow_field, spectral_weight, local_weight, bias_terms)
    return general_body(flow_field, spectral_weight, local_weight, bias_terms)


def solution(mesh):
    placed = (P(("group", "gx"), "gy", None), P("gy", "gx", None, None), P(), P())
    return jax.shard_map(
        body,
        mesh=mesh,
        in_specs=placed,
        out_specs=(P(("group", "gx"), "gy", None), P(("group", "gy"), "gx", None)),
        check_vma=False,
    )
```

```python
import functools
import math

import jax
import jax.numpy as jnp
import ml_dtypes
import numpy as np
from jax import lax
from jax.experimental import pallas as pl
from jax.experimental.pallas import tpu as pltpu
from jax.sharding import PartitionSpec as P

MX = 32
MY = 32


def wave_number(index, count):
    return jnp.where(index < count // 2, index, index - count)


def phase_table(waves, places, extent):
    product = waves[:, None] * places[None, :] % extent
    return 2.0 * math.pi / extent * product.astype(jnp.float32)


def row_tables(ky_rows, kx_rows, x_places, extent, width):
    angle = phase_table(wave_number(kx_rows, MX), x_places, extent)
    select = (ky_rows[:, None] == jnp.arange(width, dtype=jnp.int32)[None, :]).astype(jnp.float32)
    cosine = jnp.cos(angle)[:, :, None] * select[:, None, :]
    sine_part = jnp.sin(angle)[:, :, None] * select[:, None, :]
    return (cosine, sine_part)


def forward_rows(y_local, ky_rows, kx_rows, x_places, extent):
    cosine, sine_part = row_tables(ky_rows, kx_rows, x_places, extent, y_local.shape[0])
    real_in = y_local[:, 0]
    imag_in = y_local[:, 1]

    def contract(table, values):
        return jnp.einsum("rxk,kxf->rf", table, values, precision=lax.Precision.HIGHEST)

    real_out = contract(cosine, real_in) + contract(sine_part, imag_in)
    imag_out = contract(cosine, imag_in) - contract(sine_part, real_in)
    return jnp.concatenate([real_out, imag_out], axis=1)


def inverse_rows(running, shard_rows, ky_rows, kx_rows, x_places, extent):
    cosine, sine_part = row_tables(ky_rows, kx_rows, x_places, extent, running.shape[0])
    feat_count = shard_rows.shape[1] // 2
    real_part = shard_rows[:, :feat_count]
    imag_part = shard_rows[:, feat_count:]

    def contract(table, values):
        return jnp.einsum("rxk,rf->kxf", table, values, precision=lax.Precision.HIGHEST)

    new_real = contract(cosine, real_part) - contract(sine_part, imag_part)
    new_imag = contract(cosine, imag_part) + contract(sine_part, real_part)
    return jnp.stack([new_real, new_imag], axis=1)


def general_body(flow_field, spectral_weight, local_weight, bias_terms):
    cells_x, cells_y, feat_count = flow_field.shape
    channels = local_weight.shape[0]
    planes = feat_count // channels
    groups_x = lax.axis_size("gx")
    groups_y = lax.axis_size("gy")
    extent_x = cells_x * groups_x
    extent_y = cells_y * groups_y
    half_width = MY // groups_y
    quota_rows = spectral_weight.shape[1]
    high = lax.Precision.HIGHEST
    x_places = lax.axis_index("gx") * cells_x + jnp.arange(cells_x, dtype=jnp.int32)
    y_places = lax.axis_index("gy") * cells_y + jnp.arange(cells_y, dtype=jnp.int32)
    y_angle = phase_table(wave_number(jnp.arange(MY, dtype=jnp.int32), MY), y_places, extent_y)
    y_table = (
        jnp.stack([jnp.cos(y_angle), -jnp.sin(y_angle)], axis=1)
        .reshape(2 * MY, cells_y)
        .astype(jnp.bfloat16)
    )
    y_local = lax.psum_scatter(
        jnp.einsum("qy,xyf->qxf", y_table, flow_field, preferred_element_type=jnp.float32),
        "gy",
        scatter_dimension=0,
        tiled=True,
    )
    y_local = y_local.reshape(half_width, 2, cells_x, feat_count)
    rest_index = jnp.arange(lax.axis_size("gx") * quota_rows, dtype=jnp.int32)
    spectrum = lax.psum_scatter(
        forward_rows(y_local, rest_index // MX, rest_index % MX, x_places, extent_x),
        "gx",
        scatter_dimension=0,
        tiled=True,
    )
    spectrum = spectrum * (1.0 / math.sqrt(extent_x * extent_y))
    coeffs = spectrum.reshape(quota_rows, 2, planes, channels)
    weights = spectral_weight[0].astype(jnp.float32)
    product = jnp.einsum("rpzc,rco->rpzo", coeffs, weights, precision=high)
    mixed_real = product[:, 0, :, :channels] - product[:, 1, :, channels:]
    mixed_imag = product[:, 0, :, channels:] + product[:, 1, :, :channels]
    mixed_local = jnp.stack([mixed_real, mixed_imag], axis=1).reshape(quota_rows, 2 * feat_count)
    pointwise = jnp.einsum(
        "xyzc,co->xyzo",
        flow_field.reshape(cells_x, cells_y, planes, channels),
        local_weight,
        preferred_element_type=jnp.float32,
    )
    start_half = jnp.zeros((half_width, 2, cells_x, feat_count), jnp.float32)
    shard_rows = lax.all_gather(mixed_local, "gx", axis=0, tiled=True)
    rest_index = jnp.arange(shard_rows.shape[0], dtype=jnp.int32)
    back_half = inverse_rows(
        start_half, shard_rows, rest_index // MX, rest_index % MX, x_places, extent_x
    )
    back_whole = lax.all_gather(back_half, "gy", axis=0, tiled=True)
    y_cos = jnp.cos(y_angle)
    y_sin = jnp.sin(y_angle)
    spectral = (
        jnp.einsum("kn,kxf->xnf", y_cos, back_whole[:, 0], precision=high)
        - jnp.einsum("kn,kxf->xnf", y_sin, back_whole[:, 1], precision=high)
    ) * (1.0 / math.sqrt(MX * MY))
    total = spectral.reshape(cells_x, cells_y, planes, channels) + pointwise + bias_terms
    output = (
        jax.nn.gelu(total, approximate=False)
        .reshape(cells_x, cells_y, feat_count)
        .astype(jnp.bfloat16)
    )
    return (output, mixed_local.reshape(1, quota_rows, 2 * feat_count))


SMALL = pltpu.CompilerParams(vmem_limit_bytes=20 * 1024 * 1024)
LARGE = pltpu.CompilerParams(vmem_limit_bytes=53 * 1024 * 1024)
WIDTH = 256
BIAS_TERMS = 3
FIRST = 64
GELU_TERMS = (
    1.5957645177841187,
    0.29075613617897034,
    -0.0014313592109829187,
    -0.006452994421124458,
    0.0015898864949122071,
    -0.0001365363277727738,
)


def angles(count, places, extent):
    index = np.arange(count)
    waves = np.where(index < count // 2, index, index - count)
    product = (waves[:, None] * np.asarray(places)[None, :]) % extent
    return (np.float32(2.0 * math.pi / extent) * product.astype(np.float32)).astype(np.float64)


def split_table(table):
    high = table.astype(ml_dtypes.bfloat16)
    low = (table - high.astype(np.float64)).astype(ml_dtypes.bfloat16)
    return high, low


def split_terms(values):
    high = values.astype(jnp.bfloat16)
    low = (values - high.astype(jnp.float32)).astype(jnp.bfloat16)
    return high, low


def quad():
    place = lax.axis_index("gx")
    return place // 2, place % 2, lax.axis_index("gy")


def turns(layers):
    half = layers // 2
    return list(range(half, layers)) + list(range(half - 1, -1, -1))


def forward_x_table(cells_x, peers, rows_ky):
    extent = cells_x * peers
    angle = angles(MX, np.arange(extent), extent)
    cosine, sine = np.cos(angle), np.sin(angle)
    out = np.zeros((2, rows_ky, MX, extent, rows_ky, 2))
    for row in range(rows_ky):
        out[0, row, :, :, row, 0] = cosine
        out[0, row, :, :, row, 1] = sine
        out[1, row, :, :, row, 1] = cosine
        out[1, row, :, :, row, 0] = -sine
    return out.reshape(2 * rows_ky * MX, extent * rows_ky * 2)


def inverse_x_table(cells_x, peers, rows_ky):
    extent = cells_x * peers
    angle = angles(MX, np.arange(extent), extent)
    cosine, sine = np.cos(angle).T, np.sin(angle).T
    out = np.zeros((extent, rows_ky, 2, 2, rows_ky, MX))
    for row in range(rows_ky):
        out[:, row, 0, 0, row, :] = cosine
        out[:, row, 0, 1, row, :] = -sine
        out[:, row, 1, 1, row, :] = cosine
        out[:, row, 1, 0, row, :] = sine
    out = out.reshape(peers // 2, 2, cells_x * rows_ky * 2, 2 * rows_ky * MX)
    return np.moveaxis(out, 1, 0)


def inverse_y_table(cells_y, groups_y, peers, rows_ky):
    extent = cells_y * groups_y
    angle = angles(MY, np.arange(extent), extent)
    full = np.stack([np.cos(angle), -np.sin(angle)], axis=1)
    full = full.reshape(groups_y, peers, rows_ky, 2, groups_y, cells_y)
    out = np.zeros((groups_y, 2, cells_y, peers, 2, rows_ky, 2))
    for y in range(groups_y):
        for column in range(2):
            for peer in range(peers):
                for place in range(2):
                    half = y ^ place ^ column ^ (peer % 2)
                    out[y, column, :, peer, place] = np.moveaxis(full[half, peer, :, :, y], -1, 0)
    return out.reshape(groups_y, 2, cells_y, 4 * peers * rows_ky)


def output_table(table):
    high, low = split_table(table)
    parts = [high, high, low, np.ones(table.shape[:-1] + (BIAS_TERMS,), high.dtype)]
    used = 3 * table.shape[-1] + BIAS_TERMS
    parts.append(np.zeros(table.shape[:-1] + (-used % 256,), high.dtype))
    return np.concatenate(parts, axis=-1)


def dot(left, right):
    return jnp.dot(left, right, preferred_element_type=jnp.float32)


def column_of(x, y):
    return x ^ y


def forward_y_table(shape, extent, layers, rows_ky):
    z, x, y = quad()
    peers = 2 * layers
    row = lax.broadcasted_iota(jnp.int32, (shape[0], 1), 0)
    block = row // (2 * rows_ky)
    place = block // 2 % layers
    turn = jnp.where(place < layers // 2, place + layers // 2, layers - 1 - place)
    side = y ^ (1 - block // peers)
    owner = (side ^ (block % 2)) * peers + (z ^ turn) * 2 + column_of(x, side)
    index = owner * rows_ky + row // 2 % rows_ky
    y_places = lax.broadcasted_iota(jnp.int32, (1, shape[1]), 1) + y * shape[1]
    steps = (wave_number(index, MY) * y_places) & (extent - 1)
    angle = 2.0 * math.pi / extent * steps.astype(jnp.float32)
    return jnp.where(row % 2 == 0, jnp.cos(angle), -jnp.sin(angle)).astype(jnp.bfloat16)


def forward_y_kernel(extent, rows_ky, flow_hbm, send_ref, keep_ref, flow_ref, arrived):
    layers, _, rows, feat_count = send_ref.shape
    cells_x, cells_y, _ = flow_ref.shape
    rows = rows // cells_x
    copies = [
        pltpu.make_async_copy(flow_hbm.at[x], flow_ref.at[x], arrived.at[x])
        for x in range(cells_x)
    ]
    for copy in copies:
        copy.start()
    table = forward_y_table((2 * MY, cells_y), extent, layers, rows_ky)
    for x in range(cells_x):
        copies[x].wait()
        result = dot(table, flow_ref[x]).reshape(2, layers, 2, rows, feat_count)
        send_ref[:, :, x * rows : (x + 1) * rows, :] = result[0]
        keep_ref[:, :, x * rows : (x + 1) * rows, :] = result[1]


def forward_y(flow_field, extent, layers, rows_ky):
    cells_x, _, feat_count = flow_field.shape
    shape = jax.ShapeDtypeStruct((layers, 2, cells_x * 2 * rows_ky, feat_count), jnp.float32)
    return pl.pallas_call(
        functools.partial(forward_y_kernel, extent, rows_ky),
        in_specs=[pl.BlockSpec(memory_space=pltpu.HBM)],
        out_shape=[shape] * 2,
        scratch_shapes=[
            pltpu.VMEM(flow_field.shape, flow_field.dtype),
            pltpu.SemaphoreType.DMA((cells_x,)),
        ],
        compiler_params=LARGE,
        name="forward_y",
    )(flow_field)


def flip_core(block):
    return lax.ppermute(block, "gy", [(0, 1), (1, 0)])


def along_columns(blocks, peers, order):
    arrived = []
    for turn, block in zip(order, blocks):
        pairs = [
            (2 * place + core, 2 * (place ^ (2 * turn + column_of(0, core))) + core)
            for place in range(peers)
            for core in range(2)
        ]
        arrived.append(lax.ppermute(block, ("gx", "gy"), pairs))
    return arrived


def small_call(kernel, out_shape, name):
    return pl.pallas_call(kernel, out_shape=out_shape, compiler_params=SMALL, name=name)


def second_kernel(*refs):
    for index, block_ref in enumerate(refs[:-1]):
        refs[-1][index] = block_ref[1]


def second_halves(blocks):
    shape = jax.ShapeDtypeStruct((len(blocks),) + blocks[0].shape[1:], blocks[0].dtype)
    return small_call(second_kernel, shape, "second_halves")(*blocks)


def stack_kernel(*refs):
    for index, block_ref in enumerate(refs[:-1]):
        refs[-1][index] = block_ref[...]


def stack_blocks(blocks):
    shape = jax.ShapeDtypeStruct((len(blocks),) + blocks[0].shape, blocks[0].dtype)
    return small_call(stack_kernel, shape, "stack_blocks")(*blocks)


def add_kernel(keep_ref, arrived_ref, *out_refs):
    for turn, out_ref in enumerate(out_refs):
        out_ref[...] = keep_ref[turn] + arrived_ref[turn]


def add_blocks(keep, arrived):
    shape = jax.ShapeDtypeStruct(keep.shape[1:], keep.dtype)
    return small_call(add_kernel, [shape] * keep.shape[0], "add_blocks")(keep, arrived)


def join_kernel(keep_ref, arrived_ref, *out_refs):
    cells_x, rows, _ = out_refs[0].shape
    rows = rows // 2
    for turn, out_ref in enumerate(out_refs):
        for cell in range(cells_x):
            span = slice(cell * rows, (cell + 1) * rows)
            out_ref[cell] = jnp.concatenate(
                [keep_ref[turn, span, :], arrived_ref[turn, span, :]], axis=0
            )


def join_blocks(keep, arrived, cells_x):
    layers, rows, feat_count = keep.shape
    shape = jax.ShapeDtypeStruct((cells_x, 2 * rows // cells_x, feat_count), keep.dtype)
    return small_call(join_kernel, [shape] * layers, "join_blocks")(keep, arrived)


def back_rows(inverse_high, inverse_low, modes, shape, other):
    z, x, y = quad()
    places = [(column_of(x, y) ^ other, z ^ turn) for turn in turns(shape[0])]
    table_high, table_low = [
        jnp.concatenate([ref[column, place] for column, place in places], axis=0)
        for ref in (inverse_high, inverse_low)
    ]
    high, low = split_terms(modes)
    back = dot(table_high, high) + dot(table_high, low) + dot(table_low, high)
    return back.reshape(shape)


def mix_kernel(layers, *refs):
    block_refs, arrived_ref = refs[:layers], refs[layers]
    weight_ref, forward_high, forward_low, inverse_high, inverse_low = refs[
        layers + 1 : layers + 6
    ]
    modes_ref, far_ref, near_ref, order_ref, spread_ref, result_ref = refs[layers + 6 :]
    z, x, y = quad()
    for index, turn in enumerate(turns(layers)):
        column = column_of(x, y)
        order_ref[(z ^ turn) * 2 + column] = block_refs[index][0]
        order_ref[(z ^ turn) * 2 + (column ^ 1)] = arrived_ref[index]
    feat_count = order_ref.shape[-1]
    count = weight_ref.shape[1]
    channels = weight_ref.shape[2]
    tiles = feat_count // 128
    group = 2 * tiles
    high, low = split_terms(order_ref[...].reshape(-1, feat_count))
    spectrum = (
        dot(forward_high[...], high) + dot(forward_high[...], low) + dot(forward_low[...], high)
    )
    for part in range(2):
        for tile in range(tiles):
            spread_ref[pl.ds(part * tiles + tile, count, stride=group), :] = spectrum[
                part * count : (part + 1) * count, tile * 128 : (tile + 1) * 128
            ]
    rows = lax.broadcasted_iota(jnp.int32, (8, 128), 0) % group
    lane = lax.broadcasted_iota(jnp.int32, (8, 128), 1) < channels
    sign = jnp.where(rows < tiles, -1.0, 1.0)
    for base in range(0, count * group, 8):
        block = spread_ref[base : base + 8, :]
        turned = pltpu.roll(block, channels, 1)
        firsts, seconds = [], []
        for start in range(0, 8, group):
            span = slice(start, start + group)
            left = jnp.concatenate([block[span], turned[span]], axis=0)[:, :channels]
            left_high, left_low = split_terms(left)
            left = jnp.concatenate([left_high, left_low], axis=0)
            product = dot(left, weight_ref[0, (base + start) // group])
            product = product[: 2 * group] + product[2 * group :]
            firsts.append(product[:group])
            seconds.append(product[group:])
        first = jnp.concatenate(firsts, axis=0)
        second = jnp.concatenate(seconds, axis=0)
        real = jnp.where(lane, first, pltpu.roll(second, channels, 1))
        imag = jnp.where(lane, pltpu.roll(first, channels, 1), second)
        crossed = jnp.where(rows < tiles, pltpu.roll(imag, 8 - tiles, 0), pltpu.roll(imag, tiles, 0))
        result_ref[base : base + 8, :] = real + sign * crossed
    for part in range(2):
        for tile in range(tiles):
            modes_ref[part * count : (part + 1) * count, tile * 128 : (tile + 1) * 128] = (
                result_ref[pl.ds(part * tiles + tile, count, stride=group), :]
            )
    shape = (layers,) + far_ref.shape[1:]
    send = back_rows(inverse_high, inverse_low, modes_ref[...], shape, 1)
    far_ref[...] = send[: layers // 2]
    near_ref[...] = send[layers // 2 :]


def mix(blocks, arrived, weights, forward_table, inverse_tables):
    layers = len(blocks)
    _, rows, feat_count = blocks[0].shape
    count = weights.shape[1]
    scratch = pltpu.VMEM((count * feat_count // 64, 128), jnp.float32)
    return pl.pallas_call(
        functools.partial(mix_kernel, layers),
        out_shape=[
            jax.ShapeDtypeStruct((2 * count, feat_count), jnp.float32),
            jax.ShapeDtypeStruct((layers // 2, rows, feat_count), jnp.float32),
            jax.ShapeDtypeStruct((layers // 2, rows, feat_count), jnp.float32),
        ],
        scratch_shapes=[pltpu.VMEM((2 * layers, rows, feat_count), jnp.float32), scratch, scratch],
        compiler_params=SMALL,
        name="mix",
    )(*blocks, arrived, weights, *split_table(forward_table), *inverse_tables)


def keep_kernel(modes_ref, inverse_high, inverse_low, far_ref, near_ref):
    half = far_ref.shape[0]
    shape = (2 * half,) + far_ref.shape[1:]
    keep = back_rows(inverse_high, inverse_low, modes_ref[...], shape, 0)
    far_ref[...] = keep[:half]
    near_ref[...] = keep[half:]


def keep_rows(modes, inverse_tables, like):
    return pl.pallas_call(
        keep_kernel,
        out_shape=[jax.ShapeDtypeStruct(like.shape, jnp.float32)] * 2,
        compiler_params=SMALL,
        name="keep_rows",
    )(modes, *inverse_tables)


def gelu(half):
    square = jnp.minimum(half * half, 6.25)
    inner = jnp.full_like(square, GELU_TERMS[-1])
    for term in GELU_TERMS[-2::-1]:
        inner = inner * square + term
    return half + half * jnp.tanh(half * inner)


def output_kernel(layers, flow_ref, table_ref, local_ref, bias_ref, modes_ref, *refs):
    own_refs = refs[layers // 2 : layers] + refs[: layers // 2]
    near_ref, far_ref = refs[layers : layers + 2]
    core_refs = [ref.at[index] for ref in (far_ref, near_ref) for index in range(layers // 2)]
    out_hbm, mixed_hbm, order_ref, wide_ref, level_ref, done_ref, sent = refs[layers + 2 :]
    cells_x, _, feat_count = flow_ref.shape
    channels = local_ref.shape[0]
    z, x, y = quad()
    wide_ref[...] = jnp.zeros_like(wide_ref)
    for start in range(0, WIDTH, channels):
        span = slice(start, start + channels)
        wide_ref[span, span] = local_ref[...] * 0.5
        level_ref[:, span] = bias_ref[...].reshape(1, channels) * 0.5
    level = level_ref[...]
    levels = []
    for _ in range(BIAS_TERMS):
        levels.append(level.astype(jnp.bfloat16).astype(jnp.float32))
        level = level - levels[-1]
    terms = 3 * order_ref.shape[1] * order_ref.shape[2]
    filled = jnp.zeros((table_ref.shape[-1] - terms - BIAS_TERMS, WIDTH), jnp.float32)
    below = jnp.concatenate(levels + [filled], axis=0).astype(jnp.bfloat16)
    below = jnp.concatenate([below, wide_ref[...]], axis=0)
    for column, block_refs in ((x ^ y, own_refs), (x ^ y ^ 1, core_refs)):
        for turn, block_ref in zip(turns(layers), block_refs):
            order_ref[:, (z ^ turn) * 2 + column] = block_ref[...]
    table = table_ref[y, x ^ y]
    count = modes_ref.shape[0] // 2
    copies = []
    for part in range(2):
        copies.append(
            pltpu.make_async_copy(
                modes_ref.at[pl.ds(part * count, count)],
                mixed_hbm.at[0, :, pl.ds(part * feat_count, feat_count)],
                sent.at[cells_x + part],
            )
        )
        copies[-1].start()
    for cell in range(cells_x):
        high, low = split_terms(order_ref[cell].reshape(-1, feat_count))
        stack = jnp.concatenate([high, low, high], axis=0)
        for start in range(0, feat_count, WIDTH):
            columns = slice(start, start + WIDTH)
            total = dot(
                jnp.concatenate([table, flow_ref[cell, :, columns]], axis=1),
                jnp.concatenate([stack[:, columns], below], axis=0),
            )
            done_ref[cell, :, columns] = gelu(total).astype(done_ref.dtype)
        copies.append(pltpu.make_async_copy(done_ref.at[cell], out_hbm.at[cell], sent.at[cell]))
        copies[-1].start()
    for copy in copies:
        copy.wait()


def make_output(flow_field, parts, table, local, bias, modes):
    cells_x, _, feat_count = flow_field.shape
    layers = len(parts) - 2
    rows, _ = modes.shape
    return pl.pallas_call(
        functools.partial(output_kernel, layers),
        out_specs=[pl.BlockSpec(memory_space=pl.ANY)] * 2,
        scratch_shapes=[
            pltpu.VMEM((cells_x, 2 * layers) + parts[0].shape[1:], jnp.float32),
            pltpu.VMEM((WIDTH, WIDTH), jnp.bfloat16),
            pltpu.VMEM((1, WIDTH), jnp.float32),
            pltpu.VMEM(flow_field.shape, jnp.bfloat16),
            pltpu.SemaphoreType.DMA((cells_x + 2,)),
        ],
        out_shape=[
            jax.ShapeDtypeStruct(flow_field.shape, jnp.bfloat16),
            jax.ShapeDtypeStruct((1, rows // 2, 2 * feat_count), jnp.float32),
        ],
        compiler_params=SMALL,
        name="make_output",
    )(flow_field, table, local, bias, modes, *parts)


def row_body(flow_field, spectral_weight, local_weight, bias_terms):
    cells_x, cells_y, feat_count = flow_field.shape
    peers = lax.axis_size("gx")
    groups_y = lax.axis_size("gy")
    rows_ky = MY // groups_y // peers
    forward_scale = 1.0 / math.sqrt(cells_x * peers * cells_y * groups_y)
    inverse_scale = 1.0 / math.sqrt(MX * MY)

    send, keep = forward_y(flow_field, cells_y * groups_y, peers // 2, rows_ky)
    order = turns(peers // 2)
    blocks = along_columns(add_blocks(keep, flip_core(send)), peers, order)
    inverse_tables = split_table(inverse_x_table(cells_x, peers, rows_ky))
    modes, far, near = mix(
        blocks,
        flip_core(second_halves(blocks)),
        spectral_weight,
        forward_x_table(cells_x, peers, rows_ky) * forward_scale,
        inverse_tables,
    )
    middle = peers // 4
    arrived_near, arrived_far = flip_core(near), flip_core(far)
    keep_far, keep_near = keep_rows(modes, inverse_tables, far)
    own_near = along_columns(join_blocks(keep_near, arrived_near, cells_x), peers, order[middle:])
    own_far = along_columns(join_blocks(keep_far, arrived_far, cells_x), peers, order[:middle])
    flipped = [flip_core(stack_blocks(own)) for own in (own_near, own_far)]
    parts = own_near + own_far + flipped
    table = output_table(inverse_y_table(cells_y, groups_y, peers, rows_ky) * (0.5 * inverse_scale))
    return tuple(make_output(flow_field, parts, table, local_weight, bias_terms, modes))


def body(flow_field, spectral_weight, local_weight, bias_terms):
    peers = lax.axis_size("gx")
    extent = lax.axis_size("gy") * flow_field.shape[1]
    paired = lax.axis_size("gy") == 2 and peers & (peers - 1) == 0 and extent & (extent - 1) == 0
    if paired and spectral_weight.shape[1] == 2 * MX and WIDTH % local_weight.shape[0] == 0:
        return row_body(flow_field, spectral_weight, local_weight, bias_terms)
    return general_body(flow_field, spectral_weight, local_weight, bias_terms)


def solution(mesh):
    placed = (P(("group", "gx"), "gy", None), P("gy", "gx", None, None), P(), P())
    return jax.shard_map(
        body,
        mesh=mesh,
        in_specs=placed,
        out_specs=(P(("group", "gx"), "gy", None), P(("group", "gy"), "gx", None)),
        check_vma=False,
    )
```

```python
import functools
import math

import jax
import jax.numpy as jnp
import ml_dtypes
import numpy as np
from jax import lax
from jax.experimental import pallas as pl
from jax.experimental.pallas import tpu as pltpu
from jax.sharding import PartitionSpec as P

MX = 32
MY = 32


def wave_number(index, count):
    return jnp.where(index < count // 2, index, index - count)


def phase_table(waves, places, extent):
    product = waves[:, None] * places[None, :] % extent
    return 2.0 * math.pi / extent * product.astype(jnp.float32)


def row_tables(ky_rows, kx_rows, x_places, extent, width):
    angle = phase_table(wave_number(kx_rows, MX), x_places, extent)
    select = (ky_rows[:, None] == jnp.arange(width, dtype=jnp.int32)[None, :]).astype(jnp.float32)
    cosine = jnp.cos(angle)[:, :, None] * select[:, None, :]
    sine_part = jnp.sin(angle)[:, :, None] * select[:, None, :]
    return (cosine, sine_part)


def forward_rows(y_local, ky_rows, kx_rows, x_places, extent):
    cosine, sine_part = row_tables(ky_rows, kx_rows, x_places, extent, y_local.shape[0])
    real_in = y_local[:, 0]
    imag_in = y_local[:, 1]

    def contract(table, values):
        return jnp.einsum("rxk,kxf->rf", table, values, precision=lax.Precision.HIGHEST)

    real_out = contract(cosine, real_in) + contract(sine_part, imag_in)
    imag_out = contract(cosine, imag_in) - contract(sine_part, real_in)
    return jnp.concatenate([real_out, imag_out], axis=1)


def inverse_rows(running, shard_rows, ky_rows, kx_rows, x_places, extent):
    cosine, sine_part = row_tables(ky_rows, kx_rows, x_places, extent, running.shape[0])
    feat_count = shard_rows.shape[1] // 2
    real_part = shard_rows[:, :feat_count]
    imag_part = shard_rows[:, feat_count:]

    def contract(table, values):
        return jnp.einsum("rxk,rf->kxf", table, values, precision=lax.Precision.HIGHEST)

    new_real = contract(cosine, real_part) - contract(sine_part, imag_part)
    new_imag = contract(cosine, imag_part) + contract(sine_part, real_part)
    return jnp.stack([new_real, new_imag], axis=1)


def general_body(flow_field, spectral_weight, local_weight, bias_terms):
    cells_x, cells_y, feat_count = flow_field.shape
    channels = local_weight.shape[0]
    planes = feat_count // channels
    groups_x = lax.axis_size("gx")
    groups_y = lax.axis_size("gy")
    extent_x = cells_x * groups_x
    extent_y = cells_y * groups_y
    half_width = MY // groups_y
    quota_rows = spectral_weight.shape[1]
    high = lax.Precision.HIGHEST
    x_places = lax.axis_index("gx") * cells_x + jnp.arange(cells_x, dtype=jnp.int32)
    y_places = lax.axis_index("gy") * cells_y + jnp.arange(cells_y, dtype=jnp.int32)
    y_angle = phase_table(wave_number(jnp.arange(MY, dtype=jnp.int32), MY), y_places, extent_y)
    y_table = (
        jnp.stack([jnp.cos(y_angle), -jnp.sin(y_angle)], axis=1)
        .reshape(2 * MY, cells_y)
        .astype(jnp.bfloat16)
    )
    y_local = lax.psum_scatter(
        jnp.einsum("qy,xyf->qxf", y_table, flow_field, preferred_element_type=jnp.float32),
        "gy",
        scatter_dimension=0,
        tiled=True,
    )
    y_local = y_local.reshape(half_width, 2, cells_x, feat_count)
    rest_index = jnp.arange(lax.axis_size("gx") * quota_rows, dtype=jnp.int32)
    spectrum = lax.psum_scatter(
        forward_rows(y_local, rest_index // MX, rest_index % MX, x_places, extent_x),
        "gx",
        scatter_dimension=0,
        tiled=True,
    )
    spectrum = spectrum * (1.0 / math.sqrt(extent_x * extent_y))
    coeffs = spectrum.reshape(quota_rows, 2, planes, channels)
    weights = spectral_weight[0].astype(jnp.float32)
    product = jnp.einsum("rpzc,rco->rpzo", coeffs, weights, precision=high)
    mixed_real = product[:, 0, :, :channels] - product[:, 1, :, channels:]
    mixed_imag = product[:, 0, :, channels:] + product[:, 1, :, :channels]
    mixed_local = jnp.stack([mixed_real, mixed_imag], axis=1).reshape(quota_rows, 2 * feat_count)
    pointwise = jnp.einsum(
        "xyzc,co->xyzo",
        flow_field.reshape(cells_x, cells_y, planes, channels),
        local_weight,
        preferred_element_type=jnp.float32,
    )
    start_half = jnp.zeros((half_width, 2, cells_x, feat_count), jnp.float32)
    shard_rows = lax.all_gather(mixed_local, "gx", axis=0, tiled=True)
    rest_index = jnp.arange(shard_rows.shape[0], dtype=jnp.int32)
    back_half = inverse_rows(
        start_half, shard_rows, rest_index // MX, rest_index % MX, x_places, extent_x
    )
    back_whole = lax.all_gather(back_half, "gy", axis=0, tiled=True)
    y_cos = jnp.cos(y_angle)
    y_sin = jnp.sin(y_angle)
    spectral = (
        jnp.einsum("kn,kxf->xnf", y_cos, back_whole[:, 0], precision=high)
        - jnp.einsum("kn,kxf->xnf", y_sin, back_whole[:, 1], precision=high)
    ) * (1.0 / math.sqrt(MX * MY))
    total = spectral.reshape(cells_x, cells_y, planes, channels) + pointwise + bias_terms
    output = (
        jax.nn.gelu(total, approximate=False)
        .reshape(cells_x, cells_y, feat_count)
        .astype(jnp.bfloat16)
    )
    return (output, mixed_local.reshape(1, quota_rows, 2 * feat_count))


SMALL = pltpu.CompilerParams(vmem_limit_bytes=20 * 1024 * 1024)
LARGE = pltpu.CompilerParams(vmem_limit_bytes=53 * 1024 * 1024)
WIDTH = 256
BIAS_TERMS = 3
FIRST = 64
GELU_TERMS = (
    1.5957645177841187,
    0.29075613617897034,
    -0.0014313592109829187,
    -0.006452994421124458,
    0.0015898864949122071,
    -0.0001365363277727738,
)


def angles(count, places, extent):
    index = np.arange(count)
    waves = np.where(index < count // 2, index, index - count)
    product = (waves[:, None] * np.asarray(places)[None, :]) % extent
    return (np.float32(2.0 * math.pi / extent) * product.astype(np.float32)).astype(np.float64)


def split_table(table):
    high = table.astype(ml_dtypes.bfloat16)
    low = (table - high.astype(np.float64)).astype(ml_dtypes.bfloat16)
    return high, low


def split_terms(values):
    high = values.astype(jnp.bfloat16)
    low = (values - high.astype(jnp.float32)).astype(jnp.bfloat16)
    return high, low


def quad():
    place = lax.axis_index("gx")
    return place // 2, place % 2, lax.axis_index("gy")


def turns(layers):
    half = layers // 2
    return list(range(half, layers)) + list(range(half - 1, -1, -1))


def forward_x_table(cells_x, peers, rows_ky):
    extent = cells_x * peers
    angle = angles(MX, np.arange(extent), extent)
    cosine, sine = np.cos(angle), np.sin(angle)
    out = np.zeros((2, rows_ky, MX, extent, rows_ky, 2))
    for row in range(rows_ky):
        out[0, row, :, :, row, 0] = cosine
        out[0, row, :, :, row, 1] = sine
        out[1, row, :, :, row, 1] = cosine
        out[1, row, :, :, row, 0] = -sine
    return out.reshape(2 * rows_ky * MX, extent * rows_ky * 2)


def inverse_x_table(cells_x, peers, rows_ky):
    extent = cells_x * peers
    angle = angles(MX, np.arange(extent), extent)
    cosine, sine = np.cos(angle).T, np.sin(angle).T
    out = np.zeros((extent, rows_ky, 2, 2, rows_ky, MX))
    for row in range(rows_ky):
        out[:, row, 0, 0, row, :] = cosine
        out[:, row, 0, 1, row, :] = -sine
        out[:, row, 1, 1, row, :] = cosine
        out[:, row, 1, 0, row, :] = sine
    out = out.reshape(peers // 2, 2, cells_x * rows_ky * 2, 2 * rows_ky * MX)
    return np.moveaxis(out, 1, 0)


def inverse_y_table(cells_y, groups_y, peers, rows_ky):
    extent = cells_y * groups_y
    angle = angles(MY, np.arange(extent), extent)
    full = np.stack([np.cos(angle), -np.sin(angle)], axis=1)
    full = full.reshape(groups_y, peers, rows_ky, 2, groups_y, cells_y)
    out = np.zeros((groups_y, 2, cells_y, peers, 2, rows_ky, 2))
    for y in range(groups_y):
        for column in range(2):
            for peer in range(peers):
                for place in range(2):
                    half = y ^ place ^ column ^ (peer % 2)
                    out[y, column, :, peer, place] = np.moveaxis(full[half, peer, :, :, y], -1, 0)
    return out.reshape(groups_y, 2, cells_y, 4 * peers * rows_ky)


def output_table(table):
    high, low = split_table(table)
    parts = [high, high, low, np.ones(table.shape[:-1] + (BIAS_TERMS,), high.dtype)]
    used = 3 * table.shape[-1] + BIAS_TERMS
    parts.append(np.zeros(table.shape[:-1] + (-used % 256,), high.dtype))
    return np.concatenate(parts, axis=-1)


def dot(left, right):
    return jnp.dot(left, right, preferred_element_type=jnp.float32)


def column_of(x, y):
    return x ^ y


def forward_y_table(shape, extent, layers, rows_ky):
    z, x, y = quad()
    peers = 2 * layers
    row = lax.broadcasted_iota(jnp.int32, (shape[0], 1), 0)
    block = row // (2 * rows_ky)
    place = block // 2 % layers
    turn = jnp.where(place < layers // 2, place + layers // 2, layers - 1 - place)
    side = y ^ (1 - block // peers)
    owner = (side ^ (block % 2)) * peers + (z ^ turn) * 2 + column_of(x, side)
    index = owner * rows_ky + row // 2 % rows_ky
    y_places = lax.broadcasted_iota(jnp.int32, (1, shape[1]), 1) + y * shape[1]
    steps = (wave_number(index, MY) * y_places) & (extent - 1)
    angle = 2.0 * math.pi / extent * steps.astype(jnp.float32)
    return jnp.where(row % 2 == 0, jnp.cos(angle), -jnp.sin(angle)).astype(jnp.bfloat16)


def forward_y_kernel(extent, rows_ky, flow_hbm, *refs):
    out_refs, (flow_ref, arrived) = refs[:4], refs[4:]
    half, _, rows, feat_count = out_refs[0].shape
    layers = 2 * half
    cells_x, cells_y, _ = flow_ref.shape
    rows = rows // cells_x
    copies = [
        pltpu.make_async_copy(flow_hbm.at[x], flow_ref.at[x], arrived.at[x])
        for x in range(cells_x)
    ]
    for copy in copies:
        copy.start()
    table = forward_y_table((2 * MY, cells_y), extent, layers, rows_ky)
    for x in range(cells_x):
        copies[x].wait()
        result = dot(table, flow_ref[x]).reshape(4, half, 2, rows, feat_count)
        for index, out_ref in enumerate(out_refs):
            out_ref[:, :, x * rows : (x + 1) * rows, :] = result[index]


def forward_y(flow_field, extent, layers, rows_ky):
    cells_x, _, feat_count = flow_field.shape
    shape = jax.ShapeDtypeStruct((layers // 2, 2, cells_x * 2 * rows_ky, feat_count), jnp.float32)
    return pl.pallas_call(
        functools.partial(forward_y_kernel, extent, rows_ky),
        in_specs=[pl.BlockSpec(memory_space=pltpu.HBM)],
        out_shape=[shape] * 4,
        scratch_shapes=[
            pltpu.VMEM(flow_field.shape, flow_field.dtype),
            pltpu.SemaphoreType.DMA((cells_x,)),
        ],
        compiler_params=LARGE,
        name="forward_y",
    )(flow_field)


def flip_core(block):
    return lax.ppermute(block, "gy", [(0, 1), (1, 0)])


def along_columns(blocks, peers, order):
    arrived = []
    for turn, block in zip(order, blocks):
        pairs = [
            (2 * place + core, 2 * (place ^ (2 * turn + column_of(0, core))) + core)
            for place in range(peers)
            for core in range(2)
        ]
        arrived.append(lax.ppermute(block, ("gx", "gy"), pairs))
    return arrived


def small_call(kernel, out_shape, name):
    return pl.pallas_call(kernel, out_shape=out_shape, compiler_params=SMALL, name=name)


def second_kernel(*refs):
    for index, block_ref in enumerate(refs[:-1]):
        refs[-1][index] = block_ref[1]


def second_halves(blocks):
    shape = jax.ShapeDtypeStruct((len(blocks),) + blocks[0].shape[1:], blocks[0].dtype)
    return small_call(second_kernel, shape, "second_halves")(*blocks)


def stack_kernel(*refs):
    for index, block_ref in enumerate(refs[:-1]):
        refs[-1][index] = block_ref[...]


def stack_blocks(blocks):
    shape = jax.ShapeDtypeStruct((len(blocks),) + blocks[0].shape, blocks[0].dtype)
    return small_call(stack_kernel, shape, "stack_blocks")(*blocks)


def add_kernel(keep_ref, arrived_ref, *out_refs):
    for turn, out_ref in enumerate(out_refs):
        out_ref[...] = keep_ref[turn] + arrived_ref[turn]


def add_blocks(keep, arrived):
    shape = jax.ShapeDtypeStruct(keep.shape[1:], keep.dtype)
    return small_call(add_kernel, [shape] * keep.shape[0], "add_blocks")(keep, arrived)


def join_kernel(keep_ref, arrived_ref, *out_refs):
    cells_x, rows, _ = out_refs[0].shape
    rows = rows // 2
    for turn, out_ref in enumerate(out_refs):
        for cell in range(cells_x):
            span = slice(cell * rows, (cell + 1) * rows)
            out_ref[cell] = jnp.concatenate(
                [keep_ref[turn, span, :], arrived_ref[turn, span, :]], axis=0
            )


def join_blocks(keep, arrived, cells_x):
    layers, rows, feat_count = keep.shape
    shape = jax.ShapeDtypeStruct((cells_x, 2 * rows // cells_x, feat_count), keep.dtype)
    return small_call(join_kernel, [shape] * layers, "join_blocks")(keep, arrived)


def back_rows(inverse_high, inverse_low, modes, shape, other):
    z, x, y = quad()
    places = [(column_of(x, y) ^ other, z ^ turn) for turn in turns(shape[0])]
    table_high, table_low = [
        jnp.concatenate([ref[column, place] for column, place in places], axis=0)
        for ref in (inverse_high, inverse_low)
    ]
    high, low = split_terms(modes)
    back = dot(table_high, high) + dot(table_high, low) + dot(table_low, high)
    return back.reshape(shape)


def mix_kernel(layers, *refs):
    block_refs, arrived_ref = refs[:layers], refs[layers]
    weight_ref, forward_high, forward_low, inverse_high, inverse_low = refs[
        layers + 1 : layers + 6
    ]
    modes_ref, far_ref, near_ref, order_ref, spread_ref, result_ref = refs[layers + 6 :]
    z, x, y = quad()
    for index, turn in enumerate(turns(layers)):
        column = column_of(x, y)
        order_ref[(z ^ turn) * 2 + column] = block_refs[index][0]
        order_ref[(z ^ turn) * 2 + (column ^ 1)] = arrived_ref[index]
    feat_count = order_ref.shape[-1]
    count = weight_ref.shape[1]
    channels = weight_ref.shape[2]
    tiles = feat_count // 128
    group = 2 * tiles
    high, low = split_terms(order_ref[...].reshape(-1, feat_count))
    spectrum = (
        dot(forward_high[...], high) + dot(forward_high[...], low) + dot(forward_low[...], high)
    )
    for part in range(2):
        for tile in range(tiles):
            spread_ref[pl.ds(part * tiles + tile, count, stride=group), :] = spectrum[
                part * count : (part + 1) * count, tile * 128 : (tile + 1) * 128
            ]
    rows = lax.broadcasted_iota(jnp.int32, (8, 128), 0) % group
    lane = lax.broadcasted_iota(jnp.int32, (8, 128), 1) < channels
    sign = jnp.where(rows < tiles, -1.0, 1.0)
    for base in range(0, count * group, 8):
        block = spread_ref[base : base + 8, :]
        turned = pltpu.roll(block, channels, 1)
        firsts, seconds = [], []
        for start in range(0, 8, group):
            span = slice(start, start + group)
            left = jnp.concatenate([block[span], turned[span]], axis=0)[:, :channels]
            left_high, left_low = split_terms(left)
            left = jnp.concatenate([left_high, left_low], axis=0)
            product = dot(left, weight_ref[0, (base + start) // group])
            product = product[: 2 * group] + product[2 * group :]
            firsts.append(product[:group])
            seconds.append(product[group:])
        first = jnp.concatenate(firsts, axis=0)
        second = jnp.concatenate(seconds, axis=0)
        real = jnp.where(lane, first, pltpu.roll(second, channels, 1))
        imag = jnp.where(lane, pltpu.roll(first, channels, 1), second)
        crossed = jnp.where(rows < tiles, pltpu.roll(imag, 8 - tiles, 0), pltpu.roll(imag, tiles, 0))
        result_ref[base : base + 8, :] = real + sign * crossed
    for part in range(2):
        for tile in range(tiles):
            modes_ref[part * count : (part + 1) * count, tile * 128 : (tile + 1) * 128] = (
                result_ref[pl.ds(part * tiles + tile, count, stride=group), :]
            )
    shape = (layers,) + far_ref.shape[1:]
    send = back_rows(inverse_high, inverse_low, modes_ref[...], shape, 1)
    far_ref[...] = send[: layers // 2]
    near_ref[...] = send[layers // 2 :]


def mix(blocks, arrived, weights, forward_table, inverse_tables):
    layers = len(blocks)
    _, rows, feat_count = blocks[0].shape
    count = weights.shape[1]
    scratch = pltpu.VMEM((count * feat_count // 64, 128), jnp.float32)
    return pl.pallas_call(
        functools.partial(mix_kernel, layers),
        out_shape=[
            jax.ShapeDtypeStruct((2 * count, feat_count), jnp.float32),
            jax.ShapeDtypeStruct((layers // 2, rows, feat_count), jnp.float32),
            jax.ShapeDtypeStruct((layers // 2, rows, feat_count), jnp.float32),
        ],
        scratch_shapes=[pltpu.VMEM((2 * layers, rows, feat_count), jnp.float32), scratch, scratch],
        compiler_params=SMALL,
        name="mix",
    )(*blocks, arrived, weights, *split_table(forward_table), *inverse_tables)


def keep_kernel(modes_ref, inverse_high, inverse_low, far_ref, near_ref):
    half = far_ref.shape[0]
    shape = (2 * half,) + far_ref.shape[1:]
    keep = back_rows(inverse_high, inverse_low, modes_ref[...], shape, 0)
    far_ref[...] = keep[:half]
    near_ref[...] = keep[half:]


def keep_rows(modes, inverse_tables, like):
    return pl.pallas_call(
        keep_kernel,
        out_shape=[jax.ShapeDtypeStruct(like.shape, jnp.float32)] * 2,
        compiler_params=SMALL,
        name="keep_rows",
    )(modes, *inverse_tables)


def gelu(half):
    square = jnp.minimum(half * half, 6.25)
    inner = jnp.full_like(square, GELU_TERMS[-1])
    for term in GELU_TERMS[-2::-1]:
        inner = inner * square + term
    return half + half * jnp.tanh(half * inner)


def output_kernel(layers, flow_ref, table_ref, local_ref, bias_ref, modes_ref, *refs):
    own_refs = refs[layers // 2 : layers] + refs[: layers // 2]
    near_ref, far_ref = refs[layers : layers + 2]
    core_refs = [ref.at[index] for ref in (far_ref, near_ref) for index in range(layers // 2)]
    out_hbm, mixed_hbm, order_ref, wide_ref, level_ref, done_ref, sent = refs[layers + 2 :]
    cells_x, _, feat_count = flow_ref.shape
    channels = local_ref.shape[0]
    z, x, y = quad()
    wide_ref[...] = jnp.zeros_like(wide_ref)
    for start in range(0, WIDTH, channels):
        span = slice(start, start + channels)
        wide_ref[span, span] = local_ref[...] * 0.5
        level_ref[:, span] = bias_ref[...].reshape(1, channels) * 0.5
    level = level_ref[...]
    levels = []
    for _ in range(BIAS_TERMS):
        levels.append(level.astype(jnp.bfloat16).astype(jnp.float32))
        level = level - levels[-1]
    terms = 3 * order_ref.shape[1] * order_ref.shape[2]
    filled = jnp.zeros((table_ref.shape[-1] - terms - BIAS_TERMS, WIDTH), jnp.float32)
    below = jnp.concatenate(levels + [filled], axis=0).astype(jnp.bfloat16)
    below = jnp.concatenate([below, wide_ref[...]], axis=0)
    for column, block_refs in ((x ^ y, own_refs), (x ^ y ^ 1, core_refs)):
        for turn, block_ref in zip(turns(layers), block_refs):
            order_ref[:, (z ^ turn) * 2 + column] = block_ref[...]
    table = table_ref[y, x ^ y]
    count = modes_ref.shape[0] // 2
    copies = []
    for part in range(2):
        copies.append(
            pltpu.make_async_copy(
                modes_ref.at[pl.ds(part * count, count)],
                mixed_hbm.at[0, :, pl.ds(part * feat_count, feat_count)],
                sent.at[cells_x + part],
            )
        )
        copies[-1].start()
    for cell in range(cells_x):
        high, low = split_terms(order_ref[cell].reshape(-1, feat_count))
        stack = jnp.concatenate([high, low, high], axis=0)
        for start in range(0, feat_count, WIDTH):
            columns = slice(start, start + WIDTH)
            total = dot(
                jnp.concatenate([table, flow_ref[cell, :, columns]], axis=1),
                jnp.concatenate([stack[:, columns], below], axis=0),
            )
            done_ref[cell, :, columns] = gelu(total).astype(done_ref.dtype)
        copies.append(pltpu.make_async_copy(done_ref.at[cell], out_hbm.at[cell], sent.at[cell]))
        copies[-1].start()
    for copy in copies:
        copy.wait()


def make_output(flow_field, parts, table, local, bias, modes):
    cells_x, _, feat_count = flow_field.shape
    layers = len(parts) - 2
    rows, _ = modes.shape
    return pl.pallas_call(
        functools.partial(output_kernel, layers),
        out_specs=[pl.BlockSpec(memory_space=pl.ANY)] * 2,
        scratch_shapes=[
            pltpu.VMEM((cells_x, 2 * layers) + parts[0].shape[1:], jnp.float32),
            pltpu.VMEM((WIDTH, WIDTH), jnp.bfloat16),
            pltpu.VMEM((1, WIDTH), jnp.float32),
            pltpu.VMEM(flow_field.shape, jnp.bfloat16),
            pltpu.SemaphoreType.DMA((cells_x + 2,)),
        ],
        out_shape=[
            jax.ShapeDtypeStruct(flow_field.shape, jnp.bfloat16),
            jax.ShapeDtypeStruct((1, rows // 2, 2 * feat_count), jnp.float32),
        ],
        compiler_params=SMALL,
        name="make_output",
    )(flow_field, table, local, bias, modes, *parts)


def row_body(flow_field, spectral_weight, local_weight, bias_terms):
    cells_x, cells_y, feat_count = flow_field.shape
    peers = lax.axis_size("gx")
    groups_y = lax.axis_size("gy")
    rows_ky = MY // groups_y // peers
    forward_scale = 1.0 / math.sqrt(cells_x * peers * cells_y * groups_y)
    inverse_scale = 1.0 / math.sqrt(MX * MY)

    send_far, send_near, keep_far, keep_near = forward_y(
        flow_field, cells_y * groups_y, peers // 2, rows_ky
    )
    order = turns(peers // 2)
    middle = peers // 4
    near = along_columns(add_blocks(keep_near, flip_core(send_near)), peers, order[middle:])
    far = along_columns(add_blocks(keep_far, flip_core(send_far)), peers, order[:middle])
    blocks = far + near
    inverse_tables = split_table(inverse_x_table(cells_x, peers, rows_ky))
    modes, far, near = mix(
        blocks,
        flip_core(second_halves(blocks)),
        spectral_weight,
        forward_x_table(cells_x, peers, rows_ky) * forward_scale,
        inverse_tables,
    )
    arrived_near, arrived_far = flip_core(near), flip_core(far)
    keep_far, keep_near = keep_rows(modes, inverse_tables, far)
    own_near = along_columns(join_blocks(keep_near, arrived_near, cells_x), peers, order[middle:])
    own_far = along_columns(join_blocks(keep_far, arrived_far, cells_x), peers, order[:middle])
    flipped = [flip_core(stack_blocks(own)) for own in (own_near, own_far)]
    parts = own_near + own_far + flipped
    table = output_table(inverse_y_table(cells_y, groups_y, peers, rows_ky) * (0.5 * inverse_scale))
    return tuple(make_output(flow_field, parts, table, local_weight, bias_terms, modes))


def body(flow_field, spectral_weight, local_weight, bias_terms):
    peers = lax.axis_size("gx")
    extent = lax.axis_size("gy") * flow_field.shape[1]
    paired = lax.axis_size("gy") == 2 and peers & (peers - 1) == 0 and extent & (extent - 1) == 0
    if paired and spectral_weight.shape[1] == 2 * MX and WIDTH % local_weight.shape[0] == 0:
        return row_body(flow_field, spectral_weight, local_weight, bias_terms)
    return general_body(flow_field, spectral_weight, local_weight, bias_terms)


def solution(mesh):
    placed = (P(("group", "gx"), "gy", None), P("gy", "gx", None, None), P(), P())
    return jax.shard_map(
        body,
        mesh=mesh,
        in_specs=placed,
        out_specs=(P(("group", "gx"), "gy", None), P(("group", "gy"), "gx", None)),
        check_vma=False,
    )
```

```python
import functools
import math

import jax
import jax.numpy as jnp
import ml_dtypes
import numpy as np
from jax import lax
from jax.experimental import pallas as pl
from jax.experimental.pallas import tpu as pltpu
from jax.sharding import PartitionSpec as P

MX = 32
MY = 32


def wave_number(index, count):
    return jnp.where(index < count // 2, index, index - count)


def phase_table(waves, places, extent):
    product = waves[:, None] * places[None, :] % extent
    return 2.0 * math.pi / extent * product.astype(jnp.float32)


def row_tables(ky_rows, kx_rows, x_places, extent, width):
    angle = phase_table(wave_number(kx_rows, MX), x_places, extent)
    select = (ky_rows[:, None] == jnp.arange(width, dtype=jnp.int32)[None, :]).astype(jnp.float32)
    cosine = jnp.cos(angle)[:, :, None] * select[:, None, :]
    sine_part = jnp.sin(angle)[:, :, None] * select[:, None, :]
    return (cosine, sine_part)


def forward_rows(y_local, ky_rows, kx_rows, x_places, extent):
    cosine, sine_part = row_tables(ky_rows, kx_rows, x_places, extent, y_local.shape[0])
    real_in = y_local[:, 0]
    imag_in = y_local[:, 1]

    def contract(table, values):
        return jnp.einsum("rxk,kxf->rf", table, values, precision=lax.Precision.HIGHEST)

    real_out = contract(cosine, real_in) + contract(sine_part, imag_in)
    imag_out = contract(cosine, imag_in) - contract(sine_part, real_in)
    return jnp.concatenate([real_out, imag_out], axis=1)


def inverse_rows(running, shard_rows, ky_rows, kx_rows, x_places, extent):
    cosine, sine_part = row_tables(ky_rows, kx_rows, x_places, extent, running.shape[0])
    feat_count = shard_rows.shape[1] // 2
    real_part = shard_rows[:, :feat_count]
    imag_part = shard_rows[:, feat_count:]

    def contract(table, values):
        return jnp.einsum("rxk,rf->kxf", table, values, precision=lax.Precision.HIGHEST)

    new_real = contract(cosine, real_part) - contract(sine_part, imag_part)
    new_imag = contract(cosine, imag_part) + contract(sine_part, real_part)
    return jnp.stack([new_real, new_imag], axis=1)


def general_body(flow_field, spectral_weight, local_weight, bias_terms):
    cells_x, cells_y, feat_count = flow_field.shape
    channels = local_weight.shape[0]
    planes = feat_count // channels
    groups_x = lax.axis_size("gx")
    groups_y = lax.axis_size("gy")
    extent_x = cells_x * groups_x
    extent_y = cells_y * groups_y
    half_width = MY // groups_y
    quota_rows = spectral_weight.shape[1]
    high = lax.Precision.HIGHEST
    x_places = lax.axis_index("gx") * cells_x + jnp.arange(cells_x, dtype=jnp.int32)
    y_places = lax.axis_index("gy") * cells_y + jnp.arange(cells_y, dtype=jnp.int32)
    y_angle = phase_table(wave_number(jnp.arange(MY, dtype=jnp.int32), MY), y_places, extent_y)
    y_table = (
        jnp.stack([jnp.cos(y_angle), -jnp.sin(y_angle)], axis=1)
        .reshape(2 * MY, cells_y)
        .astype(jnp.bfloat16)
    )
    y_local = lax.psum_scatter(
        jnp.einsum("qy,xyf->qxf", y_table, flow_field, preferred_element_type=jnp.float32),
        "gy",
        scatter_dimension=0,
        tiled=True,
    )
    y_local = y_local.reshape(half_width, 2, cells_x, feat_count)
    rest_index = jnp.arange(lax.axis_size("gx") * quota_rows, dtype=jnp.int32)
    spectrum = lax.psum_scatter(
        forward_rows(y_local, rest_index // MX, rest_index % MX, x_places, extent_x),
        "gx",
        scatter_dimension=0,
        tiled=True,
    )
    spectrum = spectrum * (1.0 / math.sqrt(extent_x * extent_y))
    coeffs = spectrum.reshape(quota_rows, 2, planes, channels)
    weights = spectral_weight[0].astype(jnp.float32)
    product = jnp.einsum("rpzc,rco->rpzo", coeffs, weights, precision=high)
    mixed_real = product[:, 0, :, :channels] - product[:, 1, :, channels:]
    mixed_imag = product[:, 0, :, channels:] + product[:, 1, :, :channels]
    mixed_local = jnp.stack([mixed_real, mixed_imag], axis=1).reshape(quota_rows, 2 * feat_count)
    pointwise = jnp.einsum(
        "xyzc,co->xyzo",
        flow_field.reshape(cells_x, cells_y, planes, channels),
        local_weight,
        preferred_element_type=jnp.float32,
    )
    start_half = jnp.zeros((half_width, 2, cells_x, feat_count), jnp.float32)
    shard_rows = lax.all_gather(mixed_local, "gx", axis=0, tiled=True)
    rest_index = jnp.arange(shard_rows.shape[0], dtype=jnp.int32)
    back_half = inverse_rows(
        start_half, shard_rows, rest_index // MX, rest_index % MX, x_places, extent_x
    )
    back_whole = lax.all_gather(back_half, "gy", axis=0, tiled=True)
    y_cos = jnp.cos(y_angle)
    y_sin = jnp.sin(y_angle)
    spectral = (
        jnp.einsum("kn,kxf->xnf", y_cos, back_whole[:, 0], precision=high)
        - jnp.einsum("kn,kxf->xnf", y_sin, back_whole[:, 1], precision=high)
    ) * (1.0 / math.sqrt(MX * MY))
    total = spectral.reshape(cells_x, cells_y, planes, channels) + pointwise + bias_terms
    output = (
        jax.nn.gelu(total, approximate=False)
        .reshape(cells_x, cells_y, feat_count)
        .astype(jnp.bfloat16)
    )
    return (output, mixed_local.reshape(1, quota_rows, 2 * feat_count))


SMALL = pltpu.CompilerParams(vmem_limit_bytes=20 * 1024 * 1024)
LARGE = pltpu.CompilerParams(vmem_limit_bytes=53 * 1024 * 1024)
WIDTH = 256
BIAS_TERMS = 3
FIRST = 64
GELU_TERMS = (
    1.5957645177841187,
    0.29075613617897034,
    -0.0014313592109829187,
    -0.006452994421124458,
    0.0015898864949122071,
    -0.0001365363277727738,
)


def angles(count, places, extent):
    index = np.arange(count)
    waves = np.where(index < count // 2, index, index - count)
    product = (waves[:, None] * np.asarray(places)[None, :]) % extent
    return (np.float32(2.0 * math.pi / extent) * product.astype(np.float32)).astype(np.float64)


def split_table(table):
    high = table.astype(ml_dtypes.bfloat16)
    low = (table - high.astype(np.float64)).astype(ml_dtypes.bfloat16)
    return high, low


def split_terms(values):
    high = values.astype(jnp.bfloat16)
    low = (values - high.astype(jnp.float32)).astype(jnp.bfloat16)
    return high, low


def quad():
    place = lax.axis_index("gx")
    return place // 2, place % 2, lax.axis_index("gy")


def turns(layers):
    half = layers // 2
    return list(range(half, layers)) + list(range(half - 1, -1, -1))


def forward_x_table(cells_x, peers, rows_ky):
    extent = cells_x * peers
    angle = angles(MX, np.arange(extent), extent)
    cosine, sine = np.cos(angle), np.sin(angle)
    out = np.zeros((2, rows_ky, MX, extent, rows_ky, 2))
    for row in range(rows_ky):
        out[0, row, :, :, row, 0] = cosine
        out[0, row, :, :, row, 1] = sine
        out[1, row, :, :, row, 1] = cosine
        out[1, row, :, :, row, 0] = -sine
    return out.reshape(2 * rows_ky * MX, extent * rows_ky * 2)


def inverse_x_table(cells_x, peers, rows_ky):
    extent = cells_x * peers
    angle = angles(MX, np.arange(extent), extent)
    cosine, sine = np.cos(angle).T, np.sin(angle).T
    out = np.zeros((extent, rows_ky, 2, 2, rows_ky, MX))
    for row in range(rows_ky):
        out[:, row, 0, 0, row, :] = cosine
        out[:, row, 0, 1, row, :] = -sine
        out[:, row, 1, 1, row, :] = cosine
        out[:, row, 1, 0, row, :] = sine
    out = out.reshape(peers // 2, 2, cells_x * rows_ky * 2, 2 * rows_ky * MX)
    return np.moveaxis(out, 1, 0)


def inverse_y_table(cells_y, groups_y, peers, rows_ky):
    extent = cells_y * groups_y
    angle = angles(MY, np.arange(extent), extent)
    full = np.stack([np.cos(angle), -np.sin(angle)], axis=1)
    full = full.reshape(groups_y, peers, rows_ky, 2, groups_y, cells_y)
    out = np.zeros((groups_y, 2, cells_y, peers, 2, rows_ky, 2))
    for y in range(groups_y):
        for column in range(2):
            for peer in range(peers):
                for place in range(2):
                    half = y ^ place ^ column ^ (peer % 2)
                    out[y, column, :, peer, place] = np.moveaxis(full[half, peer, :, :, y], -1, 0)
    return out.reshape(groups_y, 2, cells_y, 4 * peers * rows_ky)


def output_table(table):
    high, low = split_table(table)
    parts = [high, high, low, np.ones(table.shape[:-1] + (BIAS_TERMS,), high.dtype)]
    used = 3 * table.shape[-1] + BIAS_TERMS
    parts.append(np.zeros(table.shape[:-1] + (-used % 256,), high.dtype))
    return np.concatenate(parts, axis=-1)


def dot(left, right):
    return jnp.dot(left, right, preferred_element_type=jnp.float32)


def column_of(x, y):
    return x ^ y


def forward_y_table(shape, extent, layers, rows_ky):
    z, x, y = quad()
    peers = 2 * layers
    row = lax.broadcasted_iota(jnp.int32, (shape[0], 1), 0)
    block = row // (2 * rows_ky)
    place = block // 2 % layers
    turn = jnp.where(place < layers // 2, place + layers // 2, layers - 1 - place)
    side = y ^ (1 - block // peers)
    owner = (side ^ (block % 2)) * peers + (z ^ turn) * 2 + column_of(x, side)
    index = owner * rows_ky + row // 2 % rows_ky
    y_places = lax.broadcasted_iota(jnp.int32, (1, shape[1]), 1) + y * shape[1]
    steps = (wave_number(index, MY) * y_places) & (extent - 1)
    angle = 2.0 * math.pi / extent * steps.astype(jnp.float32)
    return jnp.where(row % 2 == 0, jnp.cos(angle), -jnp.sin(angle)).astype(jnp.bfloat16)


def forward_y_kernel(extent, rows_ky, flow_hbm, *refs):
    out_refs, (flow_ref, arrived) = refs[:4], refs[4:]
    half, _, rows, feat_count = out_refs[0].shape
    layers = 2 * half
    cells_x, cells_y, _ = flow_ref.shape
    rows = rows // cells_x
    copies = [
        pltpu.make_async_copy(flow_hbm.at[x], flow_ref.at[x], arrived.at[x])
        for x in range(cells_x)
    ]
    for copy in copies:
        copy.start()
    table = forward_y_table((2 * MY, cells_y), extent, layers, rows_ky)
    for x in range(cells_x):
        copies[x].wait()
        result = dot(table, flow_ref[x]).reshape(4, half, 2, rows, feat_count)
        for index, out_ref in enumerate(out_refs):
            out_ref[:, :, x * rows : (x + 1) * rows, :] = result[index]


def forward_y(flow_field, extent, layers, rows_ky):
    cells_x, _, feat_count = flow_field.shape
    shape = jax.ShapeDtypeStruct((layers // 2, 2, cells_x * 2 * rows_ky, feat_count), jnp.float32)
    return pl.pallas_call(
        functools.partial(forward_y_kernel, extent, rows_ky),
        in_specs=[pl.BlockSpec(memory_space=pltpu.HBM)],
        out_shape=[shape] * 4,
        scratch_shapes=[
            pltpu.VMEM(flow_field.shape, flow_field.dtype),
            pltpu.SemaphoreType.DMA((cells_x,)),
        ],
        compiler_params=LARGE,
        name="forward_y",
    )(flow_field)


def flip_core(block):
    return lax.ppermute(block, "gy", [(0, 1), (1, 0)])


def along_columns(blocks, peers, order):
    arrived = []
    for turn, block in zip(order, blocks):
        pairs = [
            (2 * place + core, 2 * (place ^ (2 * turn + column_of(0, core))) + core)
            for place in range(peers)
            for core in range(2)
        ]
        arrived.append(lax.ppermute(block, ("gx", "gy"), pairs))
    return arrived


def small_call(kernel, out_shape, name):
    return pl.pallas_call(kernel, out_shape=out_shape, compiler_params=SMALL, name=name)


def second_kernel(*refs):
    for index, block_ref in enumerate(refs[:-1]):
        refs[-1][index] = block_ref[1]


def second_halves(blocks):
    shape = jax.ShapeDtypeStruct((len(blocks),) + blocks[0].shape[1:], blocks[0].dtype)
    return small_call(second_kernel, shape, "second_halves")(*blocks)


def stack_kernel(*refs):
    for index, block_ref in enumerate(refs[:-1]):
        refs[-1][index] = block_ref[...]


def stack_blocks(blocks):
    shape = jax.ShapeDtypeStruct((len(blocks),) + blocks[0].shape, blocks[0].dtype)
    return small_call(stack_kernel, shape, "stack_blocks")(*blocks)


def add_kernel(keep_ref, arrived_ref, *out_refs):
    for turn, out_ref in enumerate(out_refs):
        out_ref[...] = keep_ref[turn] + arrived_ref[turn]


def add_blocks(keep, arrived):
    shape = jax.ShapeDtypeStruct(keep.shape[1:], keep.dtype)
    return small_call(add_kernel, [shape] * keep.shape[0], "add_blocks")(keep, arrived)


def join_kernel(keep_ref, arrived_ref, *out_refs):
    cells_x, rows, _ = out_refs[0].shape
    rows = rows // 2
    for turn, out_ref in enumerate(out_refs):
        for cell in range(cells_x):
            span = slice(cell * rows, (cell + 1) * rows)
            out_ref[cell] = jnp.concatenate(
                [keep_ref[turn, span, :], arrived_ref[turn, span, :]], axis=0
            )


def join_blocks(keep, arrived, cells_x):
    layers, rows, feat_count = keep.shape
    shape = jax.ShapeDtypeStruct((cells_x, 2 * rows // cells_x, feat_count), keep.dtype)
    return small_call(join_kernel, [shape] * layers, "join_blocks")(keep, arrived)


def back_rows(inverse_high, inverse_low, modes, shape, other):
    z, x, y = quad()
    places = [(column_of(x, y) ^ other, z ^ turn) for turn in turns(shape[0])]
    table_high, table_low = [
        jnp.concatenate([ref[column, place] for column, place in places], axis=0)
        for ref in (inverse_high, inverse_low)
    ]
    high, low = split_terms(modes)
    back = dot(table_high, high) + dot(table_high, low) + dot(table_low, high)
    return back.reshape(shape)


def mix_kernel(layers, *refs):
    half = layers // 2
    block_refs = refs[:layers]
    far_arrived, near_arrived = refs[layers : layers + 2]
    weight_ref, forward_high, forward_low, inverse_high, inverse_low = refs[
        layers + 2 : layers + 7
    ]
    modes_ref, far_ref, near_ref, order_ref, spread_ref, result_ref = refs[layers + 7 :]
    z, x, y = quad()
    column = column_of(x, y)
    for index, turn in enumerate(turns(layers)):
        arrived_ref = near_arrived if index >= half else far_arrived
        order_ref[(z ^ turn) * 2 + column] = block_refs[index][0]
        order_ref[(z ^ turn) * 2 + (column ^ 1)] = arrived_ref[index % half]
    feat_count = order_ref.shape[-1]
    count = weight_ref.shape[1]
    channels = weight_ref.shape[2]
    tiles = feat_count // 128
    group = 2 * tiles
    high, low = split_terms(order_ref[...].reshape(-1, feat_count))
    spectrum = (
        dot(forward_high[...], high) + dot(forward_high[...], low) + dot(forward_low[...], high)
    )
    for part in range(2):
        for tile in range(tiles):
            spread_ref[pl.ds(part * tiles + tile, count, stride=group), :] = spectrum[
                part * count : (part + 1) * count, tile * 128 : (tile + 1) * 128
            ]
    rows = lax.broadcasted_iota(jnp.int32, (8, 128), 0) % group
    lane = lax.broadcasted_iota(jnp.int32, (8, 128), 1) < channels
    sign = jnp.where(rows < tiles, -1.0, 1.0)
    for base in range(0, count * group, 8):
        block = spread_ref[base : base + 8, :]
        turned = pltpu.roll(block, channels, 1)
        firsts, seconds = [], []
        for start in range(0, 8, group):
            span = slice(start, start + group)
            left = jnp.concatenate([block[span], turned[span]], axis=0)[:, :channels]
            left_high, left_low = split_terms(left)
            left = jnp.concatenate([left_high, left_low], axis=0)
            product = dot(left, weight_ref[0, (base + start) // group])
            product = product[: 2 * group] + product[2 * group :]
            firsts.append(product[:group])
            seconds.append(product[group:])
        first = jnp.concatenate(firsts, axis=0)
        second = jnp.concatenate(seconds, axis=0)
        real = jnp.where(lane, first, pltpu.roll(second, channels, 1))
        imag = jnp.where(lane, pltpu.roll(first, channels, 1), second)
        crossed = jnp.where(rows < tiles, pltpu.roll(imag, 8 - tiles, 0), pltpu.roll(imag, tiles, 0))
        result_ref[base : base + 8, :] = real + sign * crossed
    for part in range(2):
        for tile in range(tiles):
            modes_ref[part * count : (part + 1) * count, tile * 128 : (tile + 1) * 128] = (
                result_ref[pl.ds(part * tiles + tile, count, stride=group), :]
            )
    shape = (layers,) + far_ref.shape[1:]
    send = back_rows(inverse_high, inverse_low, modes_ref[...], shape, 1)
    far_ref[...] = send[: layers // 2]
    near_ref[...] = send[layers // 2 :]


def mix(blocks, arrived, weights, forward_table, inverse_tables):
    layers = len(blocks)
    _, rows, feat_count = blocks[0].shape
    count = weights.shape[1]
    scratch = pltpu.VMEM((count * feat_count // 64, 128), jnp.float32)
    return pl.pallas_call(
        functools.partial(mix_kernel, layers),
        out_shape=[
            jax.ShapeDtypeStruct((2 * count, feat_count), jnp.float32),
            jax.ShapeDtypeStruct((layers // 2, rows, feat_count), jnp.float32),
            jax.ShapeDtypeStruct((layers // 2, rows, feat_count), jnp.float32),
        ],
        scratch_shapes=[pltpu.VMEM((2 * layers, rows, feat_count), jnp.float32), scratch, scratch],
        compiler_params=SMALL,
        name="mix",
    )(*blocks, *arrived, weights, *split_table(forward_table), *inverse_tables)


def keep_kernel(modes_ref, inverse_high, inverse_low, far_ref, near_ref):
    half = far_ref.shape[0]
    shape = (2 * half,) + far_ref.shape[1:]
    keep = back_rows(inverse_high, inverse_low, modes_ref[...], shape, 0)
    far_ref[...] = keep[:half]
    near_ref[...] = keep[half:]


def keep_rows(modes, inverse_tables, like):
    return pl.pallas_call(
        keep_kernel,
        out_shape=[jax.ShapeDtypeStruct(like.shape, jnp.float32)] * 2,
        compiler_params=SMALL,
        name="keep_rows",
    )(modes, *inverse_tables)


def gelu(half):
    square = jnp.minimum(half * half, 6.25)
    inner = jnp.full_like(square, GELU_TERMS[-1])
    for term in GELU_TERMS[-2::-1]:
        inner = inner * square + term
    return half + half * jnp.tanh(half * inner)


def output_kernel(layers, flow_ref, table_ref, local_ref, bias_ref, modes_ref, *refs):
    own_refs = refs[layers // 2 : layers] + refs[: layers // 2]
    near_ref, far_ref = refs[layers : layers + 2]
    core_refs = [ref.at[index] for ref in (far_ref, near_ref) for index in range(layers // 2)]
    out_hbm, mixed_hbm, order_ref, wide_ref, level_ref, done_ref, sent = refs[layers + 2 :]
    cells_x, _, feat_count = flow_ref.shape
    channels = local_ref.shape[0]
    z, x, y = quad()
    wide_ref[...] = jnp.zeros_like(wide_ref)
    for start in range(0, WIDTH, channels):
        span = slice(start, start + channels)
        wide_ref[span, span] = local_ref[...] * 0.5
        level_ref[:, span] = bias_ref[...].reshape(1, channels) * 0.5
    level = level_ref[...]
    levels = []
    for _ in range(BIAS_TERMS):
        levels.append(level.astype(jnp.bfloat16).astype(jnp.float32))
        level = level - levels[-1]
    terms = 3 * order_ref.shape[1] * order_ref.shape[2]
    filled = jnp.zeros((table_ref.shape[-1] - terms - BIAS_TERMS, WIDTH), jnp.float32)
    below = jnp.concatenate(levels + [filled], axis=0).astype(jnp.bfloat16)
    below = jnp.concatenate([below, wide_ref[...]], axis=0)
    for column, block_refs in ((x ^ y, own_refs), (x ^ y ^ 1, core_refs)):
        for turn, block_ref in zip(turns(layers), block_refs):
            order_ref[:, (z ^ turn) * 2 + column] = block_ref[...]
    table = table_ref[y, x ^ y]
    count = modes_ref.shape[0] // 2
    copies = []
    for part in range(2):
        copies.append(
            pltpu.make_async_copy(
                modes_ref.at[pl.ds(part * count, count)],
                mixed_hbm.at[0, :, pl.ds(part * feat_count, feat_count)],
                sent.at[cells_x + part],
            )
        )
        copies[-1].start()
    for cell in range(cells_x):
        high, low = split_terms(order_ref[cell].reshape(-1, feat_count))
        stack = jnp.concatenate([high, low, high], axis=0)
        for start in range(0, feat_count, WIDTH):
            columns = slice(start, start + WIDTH)
            total = dot(
                jnp.concatenate([table, flow_ref[cell, :, columns]], axis=1),
                jnp.concatenate([stack[:, columns], below], axis=0),
            )
            done_ref[cell, :, columns] = gelu(total).astype(done_ref.dtype)
        copies.append(pltpu.make_async_copy(done_ref.at[cell], out_hbm.at[cell], sent.at[cell]))
        copies[-1].start()
    for copy in copies:
        copy.wait()


def make_output(flow_field, parts, table, local, bias, modes):
    cells_x, _, feat_count = flow_field.shape
    layers = len(parts) - 2
    rows, _ = modes.shape
    return pl.pallas_call(
        functools.partial(output_kernel, layers),
        out_specs=[pl.BlockSpec(memory_space=pl.ANY)] * 2,
        scratch_shapes=[
            pltpu.VMEM((cells_x, 2 * layers) + parts[0].shape[1:], jnp.float32),
            pltpu.VMEM((WIDTH, WIDTH), jnp.bfloat16),
            pltpu.VMEM((1, WIDTH), jnp.float32),
            pltpu.VMEM(flow_field.shape, jnp.bfloat16),
            pltpu.SemaphoreType.DMA((cells_x + 2,)),
        ],
        out_shape=[
            jax.ShapeDtypeStruct(flow_field.shape, jnp.bfloat16),
            jax.ShapeDtypeStruct((1, rows // 2, 2 * feat_count), jnp.float32),
        ],
        compiler_params=SMALL,
        name="make_output",
    )(flow_field, table, local, bias, modes, *parts)


def row_body(flow_field, spectral_weight, local_weight, bias_terms):
    cells_x, cells_y, feat_count = flow_field.shape
    peers = lax.axis_size("gx")
    groups_y = lax.axis_size("gy")
    rows_ky = MY // groups_y // peers
    forward_scale = 1.0 / math.sqrt(cells_x * peers * cells_y * groups_y)
    inverse_scale = 1.0 / math.sqrt(MX * MY)

    send_far, send_near, keep_far, keep_near = forward_y(
        flow_field, cells_y * groups_y, peers // 2, rows_ky
    )
    order = turns(peers // 2)
    middle = peers // 4
    near = along_columns(add_blocks(keep_near, flip_core(send_near)), peers, order[middle:])
    far = along_columns(add_blocks(keep_far, flip_core(send_far)), peers, order[:middle])
    blocks = far + near
    inverse_tables = split_table(inverse_x_table(cells_x, peers, rows_ky))
    modes, send_far, send_near = mix(
        blocks,
        [flip_core(second_halves(far)), flip_core(second_halves(near))],
        spectral_weight,
        forward_x_table(cells_x, peers, rows_ky) * forward_scale,
        inverse_tables,
    )
    arrived_near, arrived_far = flip_core(send_near), flip_core(send_far)
    keep_far, keep_near = keep_rows(modes, inverse_tables, send_far)
    own_near = along_columns(join_blocks(keep_near, arrived_near, cells_x), peers, order[middle:])
    own_far = along_columns(join_blocks(keep_far, arrived_far, cells_x), peers, order[:middle])
    flipped = [flip_core(stack_blocks(own)) for own in (own_near, own_far)]
    parts = own_near + own_far + flipped
    table = output_table(inverse_y_table(cells_y, groups_y, peers, rows_ky) * (0.5 * inverse_scale))
    return tuple(make_output(flow_field, parts, table, local_weight, bias_terms, modes))


def body(flow_field, spectral_weight, local_weight, bias_terms):
    peers = lax.axis_size("gx")
    extent = lax.axis_size("gy") * flow_field.shape[1]
    paired = lax.axis_size("gy") == 2 and peers & (peers - 1) == 0 and extent & (extent - 1) == 0
    if paired and spectral_weight.shape[1] == 2 * MX and WIDTH % local_weight.shape[0] == 0:
        return row_body(flow_field, spectral_weight, local_weight, bias_terms)
    return general_body(flow_field, spectral_weight, local_weight, bias_terms)


def solution(mesh):
    placed = (P(("group", "gx"), "gy", None), P("gy", "gx", None, None), P(), P())
    return jax.shard_map(
        body,
        mesh=mesh,
        in_specs=placed,
        out_specs=(P(("group", "gx"), "gy", None), P(("group", "gy"), "gx", None)),
        check_vma=False,
    )
```

```python
import functools
import math

import jax
import jax.numpy as jnp
import ml_dtypes
import numpy as np
from jax import lax
from jax.experimental import pallas as pl
from jax.experimental.pallas import tpu as pltpu
from jax.sharding import PartitionSpec as P

MX = 32
MY = 32


def wave_number(index, count):
    return jnp.where(index < count // 2, index, index - count)


def phase_table(waves, places, extent):
    product = waves[:, None] * places[None, :] % extent
    return 2.0 * math.pi / extent * product.astype(jnp.float32)


def row_tables(ky_rows, kx_rows, x_places, extent, width):
    angle = phase_table(wave_number(kx_rows, MX), x_places, extent)
    select = (ky_rows[:, None] == jnp.arange(width, dtype=jnp.int32)[None, :]).astype(jnp.float32)
    cosine = jnp.cos(angle)[:, :, None] * select[:, None, :]
    sine_part = jnp.sin(angle)[:, :, None] * select[:, None, :]
    return (cosine, sine_part)


def forward_rows(y_local, ky_rows, kx_rows, x_places, extent):
    cosine, sine_part = row_tables(ky_rows, kx_rows, x_places, extent, y_local.shape[0])
    real_in = y_local[:, 0]
    imag_in = y_local[:, 1]

    def contract(table, values):
        return jnp.einsum("rxk,kxf->rf", table, values, precision=lax.Precision.HIGHEST)

    real_out = contract(cosine, real_in) + contract(sine_part, imag_in)
    imag_out = contract(cosine, imag_in) - contract(sine_part, real_in)
    return jnp.concatenate([real_out, imag_out], axis=1)


def inverse_rows(running, shard_rows, ky_rows, kx_rows, x_places, extent):
    cosine, sine_part = row_tables(ky_rows, kx_rows, x_places, extent, running.shape[0])
    feat_count = shard_rows.shape[1] // 2
    real_part = shard_rows[:, :feat_count]
    imag_part = shard_rows[:, feat_count:]

    def contract(table, values):
        return jnp.einsum("rxk,rf->kxf", table, values, precision=lax.Precision.HIGHEST)

    new_real = contract(cosine, real_part) - contract(sine_part, imag_part)
    new_imag = contract(cosine, imag_part) + contract(sine_part, real_part)
    return jnp.stack([new_real, new_imag], axis=1)


def general_body(flow_field, spectral_weight, local_weight, bias_terms):
    cells_x, cells_y, feat_count = flow_field.shape
    channels = local_weight.shape[0]
    planes = feat_count // channels
    groups_x = lax.axis_size("gx")
    groups_y = lax.axis_size("gy")
    extent_x = cells_x * groups_x
    extent_y = cells_y * groups_y
    half_width = MY // groups_y
    quota_rows = spectral_weight.shape[1]
    high = lax.Precision.HIGHEST
    x_places = lax.axis_index("gx") * cells_x + jnp.arange(cells_x, dtype=jnp.int32)
    y_places = lax.axis_index("gy") * cells_y + jnp.arange(cells_y, dtype=jnp.int32)
    y_angle = phase_table(wave_number(jnp.arange(MY, dtype=jnp.int32), MY), y_places, extent_y)
    y_table = (
        jnp.stack([jnp.cos(y_angle), -jnp.sin(y_angle)], axis=1)
        .reshape(2 * MY, cells_y)
        .astype(jnp.bfloat16)
    )
    y_local = lax.psum_scatter(
        jnp.einsum("qy,xyf->qxf", y_table, flow_field, preferred_element_type=jnp.float32),
        "gy",
        scatter_dimension=0,
        tiled=True,
    )
    y_local = y_local.reshape(half_width, 2, cells_x, feat_count)
    rest_index = jnp.arange(lax.axis_size("gx") * quota_rows, dtype=jnp.int32)
    spectrum = lax.psum_scatter(
        forward_rows(y_local, rest_index // MX, rest_index % MX, x_places, extent_x),
        "gx",
        scatter_dimension=0,
        tiled=True,
    )
    spectrum = spectrum * (1.0 / math.sqrt(extent_x * extent_y))
    coeffs = spectrum.reshape(quota_rows, 2, planes, channels)
    weights = spectral_weight[0].astype(jnp.float32)
    product = jnp.einsum("rpzc,rco->rpzo", coeffs, weights, precision=high)
    mixed_real = product[:, 0, :, :channels] - product[:, 1, :, channels:]
    mixed_imag = product[:, 0, :, channels:] + product[:, 1, :, :channels]
    mixed_local = jnp.stack([mixed_real, mixed_imag], axis=1).reshape(quota_rows, 2 * feat_count)
    pointwise = jnp.einsum(
        "xyzc,co->xyzo",
        flow_field.reshape(cells_x, cells_y, planes, channels),
        local_weight,
        preferred_element_type=jnp.float32,
    )
    start_half = jnp.zeros((half_width, 2, cells_x, feat_count), jnp.float32)
    shard_rows = lax.all_gather(mixed_local, "gx", axis=0, tiled=True)
    rest_index = jnp.arange(shard_rows.shape[0], dtype=jnp.int32)
    back_half = inverse_rows(
        start_half, shard_rows, rest_index // MX, rest_index % MX, x_places, extent_x
    )
    back_whole = lax.all_gather(back_half, "gy", axis=0, tiled=True)
    y_cos = jnp.cos(y_angle)
    y_sin = jnp.sin(y_angle)
    spectral = (
        jnp.einsum("kn,kxf->xnf", y_cos, back_whole[:, 0], precision=high)
        - jnp.einsum("kn,kxf->xnf", y_sin, back_whole[:, 1], precision=high)
    ) * (1.0 / math.sqrt(MX * MY))
    total = spectral.reshape(cells_x, cells_y, planes, channels) + pointwise + bias_terms
    output = (
        jax.nn.gelu(total, approximate=False)
        .reshape(cells_x, cells_y, feat_count)
        .astype(jnp.bfloat16)
    )
    return (output, mixed_local.reshape(1, quota_rows, 2 * feat_count))


SMALL = pltpu.CompilerParams(vmem_limit_bytes=20 * 1024 * 1024)
LARGE = pltpu.CompilerParams(vmem_limit_bytes=53 * 1024 * 1024)
WIDTH = 256
BIAS_TERMS = 3
FIRST = 64
GELU_TERMS = (
    1.5957645177841187,
    0.29075613617897034,
    -0.0014313592109829187,
    -0.006452994421124458,
    0.0015898864949122071,
    -0.0001365363277727738,
)


def angles(count, places, extent):
    index = np.arange(count)
    waves = np.where(index < count // 2, index, index - count)
    product = (waves[:, None] * np.asarray(places)[None, :]) % extent
    return (np.float32(2.0 * math.pi / extent) * product.astype(np.float32)).astype(np.float64)


def split_table(table):
    high = table.astype(ml_dtypes.bfloat16)
    low = (table - high.astype(np.float64)).astype(ml_dtypes.bfloat16)
    return high, low


def split_terms(values):
    high = values.astype(jnp.bfloat16)
    low = (values - high.astype(jnp.float32)).astype(jnp.bfloat16)
    return high, low


def quad():
    place = lax.axis_index("gx")
    return place // 2, place % 2, lax.axis_index("gy")


def turns(layers, inverse=False):
    half = layers // 2
    if inverse:
        return list(range(half, layers)) + list(range(half - 1, -1, -1))
    return list(range(layers - 1, -1, -1))


def forward_x_table(cells_x, peers, rows_ky):
    extent = cells_x * peers
    angle = angles(MX, np.arange(extent), extent)
    cosine, sine = np.cos(angle), np.sin(angle)
    out = np.zeros((2, rows_ky, MX, extent, rows_ky, 2))
    for row in range(rows_ky):
        out[0, row, :, :, row, 0] = cosine
        out[0, row, :, :, row, 1] = sine
        out[1, row, :, :, row, 1] = cosine
        out[1, row, :, :, row, 0] = -sine
    return out.reshape(2 * rows_ky * MX, extent * rows_ky * 2)


def inverse_x_table(cells_x, peers, rows_ky):
    extent = cells_x * peers
    angle = angles(MX, np.arange(extent), extent)
    cosine, sine = np.cos(angle).T, np.sin(angle).T
    out = np.zeros((extent, rows_ky, 2, 2, rows_ky, MX))
    for row in range(rows_ky):
        out[:, row, 0, 0, row, :] = cosine
        out[:, row, 0, 1, row, :] = -sine
        out[:, row, 1, 1, row, :] = cosine
        out[:, row, 1, 0, row, :] = sine
    out = out.reshape(peers // 2, 2, cells_x * rows_ky * 2, 2 * rows_ky * MX)
    return np.moveaxis(out, 1, 0)


def inverse_y_table(cells_y, groups_y, peers, rows_ky):
    extent = cells_y * groups_y
    angle = angles(MY, np.arange(extent), extent)
    full = np.stack([np.cos(angle), -np.sin(angle)], axis=1)
    full = full.reshape(groups_y, peers, rows_ky, 2, groups_y, cells_y)
    out = np.zeros((groups_y, 2, cells_y, peers, 2, rows_ky, 2))
    for y in range(groups_y):
        for column in range(2):
            for peer in range(peers):
                for place in range(2):
                    half = y ^ place ^ column ^ (peer % 2)
                    out[y, column, :, peer, place] = np.moveaxis(full[half, peer, :, :, y], -1, 0)
    return out.reshape(groups_y, 2, cells_y, 4 * peers * rows_ky)


def output_table(table):
    high, low = split_table(table)
    parts = [high, high, low, np.ones(table.shape[:-1] + (BIAS_TERMS,), high.dtype)]
    used = 3 * table.shape[-1] + BIAS_TERMS
    parts.append(np.zeros(table.shape[:-1] + (-used % 256,), high.dtype))
    return np.concatenate(parts, axis=-1)


def dot(left, right):
    return jnp.dot(left, right, preferred_element_type=jnp.float32)


def column_of(x, y):
    return x ^ y


def forward_y_table(shape, extent, layers, rows_ky):
    z, x, y = quad()
    peers = 2 * layers
    row = lax.broadcasted_iota(jnp.int32, (shape[0], 1), 0)
    block = row // (2 * rows_ky)
    place = block // 2 % layers
    turn = layers - 1 - place
    side = y ^ (1 - block // peers)
    owner = (side ^ (block % 2)) * peers + (z ^ turn) * 2 + column_of(x, side)
    index = owner * rows_ky + row // 2 % rows_ky
    y_places = lax.broadcasted_iota(jnp.int32, (1, shape[1]), 1) + y * shape[1]
    steps = (wave_number(index, MY) * y_places) & (extent - 1)
    angle = 2.0 * math.pi / extent * steps.astype(jnp.float32)
    return jnp.where(row % 2 == 0, jnp.cos(angle), -jnp.sin(angle)).astype(jnp.bfloat16)


def forward_y_kernel(extent, rows_ky, flow_hbm, *refs):
    out_refs, (flow_ref, arrived) = refs[:4], refs[4:]
    half, _, rows, feat_count = out_refs[0].shape
    layers = 2 * half
    cells_x, cells_y, _ = flow_ref.shape
    rows = rows // cells_x
    copies = [
        pltpu.make_async_copy(flow_hbm.at[x], flow_ref.at[x], arrived.at[x])
        for x in range(cells_x)
    ]
    for copy in copies:
        copy.start()
    table = forward_y_table((2 * MY, cells_y), extent, layers, rows_ky)
    for x in range(cells_x):
        copies[x].wait()
        result = dot(table, flow_ref[x]).reshape(4, half, 2, rows, feat_count)
        for index, out_ref in enumerate(out_refs):
            out_ref[:, :, x * rows : (x + 1) * rows, :] = result[index]


def forward_y(flow_field, extent, layers, rows_ky):
    cells_x, _, feat_count = flow_field.shape
    shape = jax.ShapeDtypeStruct((layers // 2, 2, cells_x * 2 * rows_ky, feat_count), jnp.float32)
    return pl.pallas_call(
        functools.partial(forward_y_kernel, extent, rows_ky),
        in_specs=[pl.BlockSpec(memory_space=pltpu.HBM)],
        out_shape=[shape] * 4,
        scratch_shapes=[
            pltpu.VMEM(flow_field.shape, flow_field.dtype),
            pltpu.SemaphoreType.DMA((cells_x,)),
        ],
        compiler_params=LARGE,
        name="forward_y",
    )(flow_field)


def flip_core(block):
    return lax.ppermute(block, "gy", [(0, 1), (1, 0)])


def along_columns(blocks, peers, order):
    arrived = []
    for turn, block in zip(order, blocks):
        pairs = [
            (2 * place + core, 2 * (place ^ (2 * turn + column_of(0, core))) + core)
            for place in range(peers)
            for core in range(2)
        ]
        arrived.append(lax.ppermute(block, ("gx", "gy"), pairs))
    return arrived


def small_call(kernel, out_shape, name):
    return pl.pallas_call(kernel, out_shape=out_shape, compiler_params=SMALL, name=name)


def second_kernel(*refs):
    for index, block_ref in enumerate(refs[:-1]):
        refs[-1][index] = block_ref[1]


def second_halves(blocks):
    shape = jax.ShapeDtypeStruct((len(blocks),) + blocks[0].shape[1:], blocks[0].dtype)
    return small_call(second_kernel, shape, "second_halves")(*blocks)


def stack_kernel(*refs):
    for index, block_ref in enumerate(refs[:-1]):
        refs[-1][index] = block_ref[...]


def stack_blocks(blocks):
    shape = jax.ShapeDtypeStruct((len(blocks),) + blocks[0].shape, blocks[0].dtype)
    return small_call(stack_kernel, shape, "stack_blocks")(*blocks)


def add_kernel(keep_ref, arrived_ref, *out_refs):
    for turn, out_ref in enumerate(out_refs):
        out_ref[...] = keep_ref[turn] + arrived_ref[turn]


def add_blocks(keep, arrived):
    shape = jax.ShapeDtypeStruct(keep.shape[1:], keep.dtype)
    return small_call(add_kernel, [shape] * keep.shape[0], "add_blocks")(keep, arrived)


def join_kernel(keep_ref, arrived_ref, *out_refs):
    cells_x, rows, _ = out_refs[0].shape
    rows = rows // 2
    for turn, out_ref in enumerate(out_refs):
        for cell in range(cells_x):
            span = slice(cell * rows, (cell + 1) * rows)
            out_ref[cell] = jnp.concatenate(
                [keep_ref[turn, span, :], arrived_ref[turn, span, :]], axis=0
            )


def join_blocks(keep, arrived, cells_x):
    layers, rows, feat_count = keep.shape
    shape = jax.ShapeDtypeStruct((cells_x, 2 * rows // cells_x, feat_count), keep.dtype)
    return small_call(join_kernel, [shape] * layers, "join_blocks")(keep, arrived)


def back_rows(inverse_high, inverse_low, modes, shape, other):
    z, x, y = quad()
    places = [(column_of(x, y) ^ other, z ^ turn) for turn in turns(shape[0], True)]
    table_high, table_low = [
        jnp.concatenate([ref[column, place] for column, place in places], axis=0)
        for ref in (inverse_high, inverse_low)
    ]
    high, low = split_terms(modes)
    back = dot(table_high, high) + dot(table_high, low) + dot(table_low, high)
    return back.reshape(shape)


def mix_kernel(layers, *refs):
    half = layers // 2
    block_refs = refs[:layers]
    far_arrived, near_arrived = refs[layers : layers + 2]
    weight_ref, forward_high, forward_low, inverse_high, inverse_low = refs[
        layers + 2 : layers + 7
    ]
    modes_ref, far_ref, near_ref, order_ref, spread_ref, result_ref = refs[layers + 7 :]
    z, x, y = quad()
    column = column_of(x, y)
    for index, turn in enumerate(turns(layers)):
        arrived_ref = near_arrived if index >= half else far_arrived
        order_ref[(z ^ turn) * 2 + column] = block_refs[index][0]
        order_ref[(z ^ turn) * 2 + (column ^ 1)] = arrived_ref[index % half]
    feat_count = order_ref.shape[-1]
    count = weight_ref.shape[1]
    channels = weight_ref.shape[2]
    tiles = feat_count // 128
    group = 2 * tiles
    high, low = split_terms(order_ref[...].reshape(-1, feat_count))
    spectrum = (
        dot(forward_high[...], high) + dot(forward_high[...], low) + dot(forward_low[...], high)
    )
    for part in range(2):
        for tile in range(tiles):
            spread_ref[pl.ds(part * tiles + tile, count, stride=group), :] = spectrum[
                part * count : (part + 1) * count, tile * 128 : (tile + 1) * 128
            ]
    rows = lax.broadcasted_iota(jnp.int32, (8, 128), 0) % group
    lane = lax.broadcasted_iota(jnp.int32, (8, 128), 1) < channels
    sign = jnp.where(rows < tiles, -1.0, 1.0)
    for base in range(0, count * group, 8):
        block = spread_ref[base : base + 8, :]
        turned = pltpu.roll(block, channels, 1)
        firsts, seconds = [], []
        for start in range(0, 8, group):
            span = slice(start, start + group)
            left = jnp.concatenate([block[span], turned[span]], axis=0)[:, :channels]
            left_high, left_low = split_terms(left)
            left = jnp.concatenate([left_high, left_low], axis=0)
            product = dot(left, weight_ref[0, (base + start) // group])
            product = product[: 2 * group] + product[2 * group :]
            firsts.append(product[:group])
            seconds.append(product[group:])
        first = jnp.concatenate(firsts, axis=0)
        second = jnp.concatenate(seconds, axis=0)
        real = jnp.where(lane, first, pltpu.roll(second, channels, 1))
        imag = jnp.where(lane, pltpu.roll(first, channels, 1), second)
        crossed = jnp.where(rows < tiles, pltpu.roll(imag, 8 - tiles, 0), pltpu.roll(imag, tiles, 0))
        result_ref[base : base + 8, :] = real + sign * crossed
    for part in range(2):
        for tile in range(tiles):
            modes_ref[part * count : (part + 1) * count, tile * 128 : (tile + 1) * 128] = (
                result_ref[pl.ds(part * tiles + tile, count, stride=group), :]
            )
    shape = (layers,) + far_ref.shape[1:]
    send = back_rows(inverse_high, inverse_low, modes_ref[...], shape, 1)
    far_ref[...] = send[: layers // 2]
    near_ref[...] = send[layers // 2 :]


def mix(blocks, arrived, weights, forward_table, inverse_tables):
    layers = len(blocks)
    _, rows, feat_count = blocks[0].shape
    count = weights.shape[1]
    scratch = pltpu.VMEM((count * feat_count // 64, 128), jnp.float32)
    return pl.pallas_call(
        functools.partial(mix_kernel, layers),
        out_shape=[
            jax.ShapeDtypeStruct((2 * count, feat_count), jnp.float32),
            jax.ShapeDtypeStruct((layers // 2, rows, feat_count), jnp.float32),
            jax.ShapeDtypeStruct((layers // 2, rows, feat_count), jnp.float32),
        ],
        scratch_shapes=[pltpu.VMEM((2 * layers, rows, feat_count), jnp.float32), scratch, scratch],
        compiler_params=SMALL,
        name="mix",
    )(*blocks, *arrived, weights, *split_table(forward_table), *inverse_tables)


def keep_kernel(modes_ref, inverse_high, inverse_low, far_ref, near_ref):
    half = far_ref.shape[0]
    shape = (2 * half,) + far_ref.shape[1:]
    keep = back_rows(inverse_high, inverse_low, modes_ref[...], shape, 0)
    far_ref[...] = keep[:half]
    near_ref[...] = keep[half:]


def keep_rows(modes, inverse_tables, like):
    return pl.pallas_call(
        keep_kernel,
        out_shape=[jax.ShapeDtypeStruct(like.shape, jnp.float32)] * 2,
        compiler_params=SMALL,
        name="keep_rows",
    )(modes, *inverse_tables)


def gelu(half):
    square = jnp.minimum(half * half, 6.25)
    inner = jnp.full_like(square, GELU_TERMS[-1])
    for term in GELU_TERMS[-2::-1]:
        inner = inner * square + term
    return half + half * jnp.tanh(half * inner)


def output_kernel(layers, flow_ref, table_ref, local_ref, bias_ref, modes_ref, *refs):
    own_refs = refs[layers // 2 : layers] + refs[: layers // 2]
    near_ref, far_ref = refs[layers : layers + 2]
    core_refs = [ref.at[index] for ref in (far_ref, near_ref) for index in range(layers // 2)]
    out_hbm, mixed_hbm, order_ref, wide_ref, level_ref, done_ref, sent = refs[layers + 2 :]
    cells_x, _, feat_count = flow_ref.shape
    channels = local_ref.shape[0]
    z, x, y = quad()
    wide_ref[...] = jnp.zeros_like(wide_ref)
    for start in range(0, WIDTH, channels):
        span = slice(start, start + channels)
        wide_ref[span, span] = local_ref[...] * 0.5
        level_ref[:, span] = bias_ref[...].reshape(1, channels) * 0.5
    level = level_ref[...]
    levels = []
    for _ in range(BIAS_TERMS):
        levels.append(level.astype(jnp.bfloat16).astype(jnp.float32))
        level = level - levels[-1]
    terms = 3 * order_ref.shape[1] * order_ref.shape[2]
    filled = jnp.zeros((table_ref.shape[-1] - terms - BIAS_TERMS, WIDTH), jnp.float32)
    below = jnp.concatenate(levels + [filled], axis=0).astype(jnp.bfloat16)
    below = jnp.concatenate([below, wide_ref[...]], axis=0)
    for column, block_refs in ((x ^ y, own_refs), (x ^ y ^ 1, core_refs)):
        for turn, block_ref in zip(turns(layers, True), block_refs):
            order_ref[:, (z ^ turn) * 2 + column] = block_ref[...]
    table = table_ref[y, x ^ y]
    count = modes_ref.shape[0] // 2
    copies = []
    for part in range(2):
        copies.append(
            pltpu.make_async_copy(
                modes_ref.at[pl.ds(part * count, count)],
                mixed_hbm.at[0, :, pl.ds(part * feat_count, feat_count)],
                sent.at[cells_x + part],
            )
        )
        copies[-1].start()
    for cell in range(cells_x):
        high, low = split_terms(order_ref[cell].reshape(-1, feat_count))
        stack = jnp.concatenate([high, low, high], axis=0)
        for start in range(0, feat_count, WIDTH):
            columns = slice(start, start + WIDTH)
            total = dot(
                jnp.concatenate([table, flow_ref[cell, :, columns]], axis=1),
                jnp.concatenate([stack[:, columns], below], axis=0),
            )
            done_ref[cell, :, columns] = gelu(total).astype(done_ref.dtype)
        copies.append(pltpu.make_async_copy(done_ref.at[cell], out_hbm.at[cell], sent.at[cell]))
        copies[-1].start()
    for copy in copies:
        copy.wait()


def make_output(flow_field, parts, table, local, bias, modes):
    cells_x, _, feat_count = flow_field.shape
    layers = len(parts) - 2
    rows, _ = modes.shape
    return pl.pallas_call(
        functools.partial(output_kernel, layers),
        out_specs=[pl.BlockSpec(memory_space=pl.ANY)] * 2,
        scratch_shapes=[
            pltpu.VMEM((cells_x, 2 * layers) + parts[0].shape[1:], jnp.float32),
            pltpu.VMEM((WIDTH, WIDTH), jnp.bfloat16),
            pltpu.VMEM((1, WIDTH), jnp.float32),
            pltpu.VMEM(flow_field.shape, jnp.bfloat16),
            pltpu.SemaphoreType.DMA((cells_x + 2,)),
        ],
        out_shape=[
            jax.ShapeDtypeStruct(flow_field.shape, jnp.bfloat16),
            jax.ShapeDtypeStruct((1, rows // 2, 2 * feat_count), jnp.float32),
        ],
        compiler_params=SMALL,
        name="make_output",
    )(flow_field, table, local, bias, modes, *parts)


def row_body(flow_field, spectral_weight, local_weight, bias_terms):
    cells_x, cells_y, feat_count = flow_field.shape
    peers = lax.axis_size("gx")
    groups_y = lax.axis_size("gy")
    rows_ky = MY // groups_y // peers
    forward_scale = 1.0 / math.sqrt(cells_x * peers * cells_y * groups_y)
    inverse_scale = 1.0 / math.sqrt(MX * MY)

    send_far, send_near, keep_far, keep_near = forward_y(
        flow_field, cells_y * groups_y, peers // 2, rows_ky
    )
    order = turns(peers // 2)
    middle = peers // 4
    near = along_columns(add_blocks(keep_near, flip_core(send_near)), peers, order[middle:])
    far = along_columns(add_blocks(keep_far, flip_core(send_far)), peers, order[:middle])
    blocks = far + near
    inverse_tables = split_table(inverse_x_table(cells_x, peers, rows_ky))
    modes, send_far, send_near = mix(
        blocks,
        [flip_core(second_halves(far)), flip_core(second_halves(near))],
        spectral_weight,
        forward_x_table(cells_x, peers, rows_ky) * forward_scale,
        inverse_tables,
    )
    arrived_near, arrived_far = flip_core(send_near), flip_core(send_far)
    keep_far, keep_near = keep_rows(modes, inverse_tables, send_far)
    order = turns(peers // 2, True)
    own_near = along_columns(join_blocks(keep_near, arrived_near, cells_x), peers, order[middle:])
    own_far = along_columns(join_blocks(keep_far, arrived_far, cells_x), peers, order[:middle])
    flipped = [flip_core(stack_blocks(own)) for own in (own_near, own_far)]
    parts = own_near + own_far + flipped
    table = output_table(inverse_y_table(cells_y, groups_y, peers, rows_ky) * (0.5 * inverse_scale))
    return tuple(make_output(flow_field, parts, table, local_weight, bias_terms, modes))


def body(flow_field, spectral_weight, local_weight, bias_terms):
    peers = lax.axis_size("gx")
    extent = lax.axis_size("gy") * flow_field.shape[1]
    paired = lax.axis_size("gy") == 2 and peers & (peers - 1) == 0 and extent & (extent - 1) == 0
    if paired and spectral_weight.shape[1] == 2 * MX and WIDTH % local_weight.shape[0] == 0:
        return row_body(flow_field, spectral_weight, local_weight, bias_terms)
    return general_body(flow_field, spectral_weight, local_weight, bias_terms)


def solution(mesh):
    placed = (P(("group", "gx"), "gy", None), P("gy", "gx", None, None), P(), P())
    return jax.shard_map(
        body,
        mesh=mesh,
        in_specs=placed,
        out_specs=(P(("group", "gx"), "gy", None), P(("group", "gy"), "gx", None)),
        check_vma=False,
    )
```

```python
import functools
import math

import jax
import jax.numpy as jnp
import ml_dtypes
import numpy as np
from jax import lax
from jax.experimental import pallas as pl
from jax.experimental.pallas import tpu as pltpu
from jax.sharding import PartitionSpec as P

MX = 32
MY = 32


def wave_number(index, count):
    return jnp.where(index < count // 2, index, index - count)


def phase_table(waves, places, extent):
    product = waves[:, None] * places[None, :] % extent
    return 2.0 * math.pi / extent * product.astype(jnp.float32)


def row_tables(ky_rows, kx_rows, x_places, extent, width):
    angle = phase_table(wave_number(kx_rows, MX), x_places, extent)
    select = (ky_rows[:, None] == jnp.arange(width, dtype=jnp.int32)[None, :]).astype(jnp.float32)
    cosine = jnp.cos(angle)[:, :, None] * select[:, None, :]
    sine_part = jnp.sin(angle)[:, :, None] * select[:, None, :]
    return (cosine, sine_part)


def forward_rows(y_local, ky_rows, kx_rows, x_places, extent):
    cosine, sine_part = row_tables(ky_rows, kx_rows, x_places, extent, y_local.shape[0])
    real_in = y_local[:, 0]
    imag_in = y_local[:, 1]

    def contract(table, values):
        return jnp.einsum("rxk,kxf->rf", table, values, precision=lax.Precision.HIGHEST)

    real_out = contract(cosine, real_in) + contract(sine_part, imag_in)
    imag_out = contract(cosine, imag_in) - contract(sine_part, real_in)
    return jnp.concatenate([real_out, imag_out], axis=1)


def inverse_rows(running, shard_rows, ky_rows, kx_rows, x_places, extent):
    cosine, sine_part = row_tables(ky_rows, kx_rows, x_places, extent, running.shape[0])
    feat_count = shard_rows.shape[1] // 2
    real_part = shard_rows[:, :feat_count]
    imag_part = shard_rows[:, feat_count:]

    def contract(table, values):
        return jnp.einsum("rxk,rf->kxf", table, values, precision=lax.Precision.HIGHEST)

    new_real = contract(cosine, real_part) - contract(sine_part, imag_part)
    new_imag = contract(cosine, imag_part) + contract(sine_part, real_part)
    return jnp.stack([new_real, new_imag], axis=1)


def general_body(flow_field, spectral_weight, local_weight, bias_terms):
    cells_x, cells_y, feat_count = flow_field.shape
    channels = local_weight.shape[0]
    planes = feat_count // channels
    groups_x = lax.axis_size("gx")
    groups_y = lax.axis_size("gy")
    extent_x = cells_x * groups_x
    extent_y = cells_y * groups_y
    half_width = MY // groups_y
    quota_rows = spectral_weight.shape[1]
    high = lax.Precision.HIGHEST
    x_places = lax.axis_index("gx") * cells_x + jnp.arange(cells_x, dtype=jnp.int32)
    y_places = lax.axis_index("gy") * cells_y + jnp.arange(cells_y, dtype=jnp.int32)
    y_angle = phase_table(wave_number(jnp.arange(MY, dtype=jnp.int32), MY), y_places, extent_y)
    y_table = (
        jnp.stack([jnp.cos(y_angle), -jnp.sin(y_angle)], axis=1)
        .reshape(2 * MY, cells_y)
        .astype(jnp.bfloat16)
    )
    y_local = lax.psum_scatter(
        jnp.einsum("qy,xyf->qxf", y_table, flow_field, preferred_element_type=jnp.float32),
        "gy",
        scatter_dimension=0,
        tiled=True,
    )
    y_local = y_local.reshape(half_width, 2, cells_x, feat_count)
    rest_index = jnp.arange(lax.axis_size("gx") * quota_rows, dtype=jnp.int32)
    spectrum = lax.psum_scatter(
        forward_rows(y_local, rest_index // MX, rest_index % MX, x_places, extent_x),
        "gx",
        scatter_dimension=0,
        tiled=True,
    )
    spectrum = spectrum * (1.0 / math.sqrt(extent_x * extent_y))
    coeffs = spectrum.reshape(quota_rows, 2, planes, channels)
    weights = spectral_weight[0].astype(jnp.float32)
    product = jnp.einsum("rpzc,rco->rpzo", coeffs, weights, precision=high)
    mixed_real = product[:, 0, :, :channels] - product[:, 1, :, channels:]
    mixed_imag = product[:, 0, :, channels:] + product[:, 1, :, :channels]
    mixed_local = jnp.stack([mixed_real, mixed_imag], axis=1).reshape(quota_rows, 2 * feat_count)
    pointwise = jnp.einsum(
        "xyzc,co->xyzo",
        flow_field.reshape(cells_x, cells_y, planes, channels),
        local_weight,
        preferred_element_type=jnp.float32,
    )
    start_half = jnp.zeros((half_width, 2, cells_x, feat_count), jnp.float32)
    shard_rows = lax.all_gather(mixed_local, "gx", axis=0, tiled=True)
    rest_index = jnp.arange(shard_rows.shape[0], dtype=jnp.int32)
    back_half = inverse_rows(
        start_half, shard_rows, rest_index // MX, rest_index % MX, x_places, extent_x
    )
    back_whole = lax.all_gather(back_half, "gy", axis=0, tiled=True)
    y_cos = jnp.cos(y_angle)
    y_sin = jnp.sin(y_angle)
    spectral = (
        jnp.einsum("kn,kxf->xnf", y_cos, back_whole[:, 0], precision=high)
        - jnp.einsum("kn,kxf->xnf", y_sin, back_whole[:, 1], precision=high)
    ) * (1.0 / math.sqrt(MX * MY))
    total = spectral.reshape(cells_x, cells_y, planes, channels) + pointwise + bias_terms
    output = (
        jax.nn.gelu(total, approximate=False)
        .reshape(cells_x, cells_y, feat_count)
        .astype(jnp.bfloat16)
    )
    return (output, mixed_local.reshape(1, quota_rows, 2 * feat_count))


SMALL = pltpu.CompilerParams(vmem_limit_bytes=20 * 1024 * 1024)
LARGE = pltpu.CompilerParams(vmem_limit_bytes=53 * 1024 * 1024)
WIDTH = 256
BIAS_TERMS = 3
LAST = 64
FIRST = 64
GELU_TERMS = (
    1.5957645177841187,
    0.29075613617897034,
    -0.0014313592109829187,
    -0.006452994421124458,
    0.0015898864949122071,
    -0.0001365363277727738,
)


def angles(count, places, extent):
    index = np.arange(count)
    waves = np.where(index < count // 2, index, index - count)
    product = (waves[:, None] * np.asarray(places)[None, :]) % extent
    return (np.float32(2.0 * math.pi / extent) * product.astype(np.float32)).astype(np.float64)


def split_table(table):
    high = table.astype(ml_dtypes.bfloat16)
    low = (table - high.astype(np.float64)).astype(ml_dtypes.bfloat16)
    return high, low


def split_terms(values):
    high = values.astype(jnp.bfloat16)
    low = (values - high.astype(jnp.float32)).astype(jnp.bfloat16)
    return high, low


def quad():
    place = lax.axis_index("gx")
    return place // 2, place % 2, lax.axis_index("gy")


def turns(layers, inverse=False):
    half = layers // 2
    if inverse:
        return list(range(half, layers)) + list(range(half - 1, -1, -1))
    return list(range(layers - 1, -1, -1))


def forward_x_table(cells_x, peers, rows_ky):
    extent = cells_x * peers
    angle = angles(MX, np.arange(extent), extent)
    cosine, sine = np.cos(angle), np.sin(angle)
    out = np.zeros((2, rows_ky, MX, extent, rows_ky, 2))
    for row in range(rows_ky):
        out[0, row, :, :, row, 0] = cosine
        out[0, row, :, :, row, 1] = sine
        out[1, row, :, :, row, 1] = cosine
        out[1, row, :, :, row, 0] = -sine
    return out.reshape(2 * rows_ky * MX, extent * rows_ky * 2)


def inverse_x_table(cells_x, peers, rows_ky):
    extent = cells_x * peers
    angle = angles(MX, np.arange(extent), extent)
    cosine, sine = np.cos(angle).T, np.sin(angle).T
    out = np.zeros((extent, rows_ky, 2, 2, rows_ky, MX))
    for row in range(rows_ky):
        out[:, row, 0, 0, row, :] = cosine
        out[:, row, 0, 1, row, :] = -sine
        out[:, row, 1, 1, row, :] = cosine
        out[:, row, 1, 0, row, :] = sine
    out = out.reshape(peers // 2, 2, cells_x * rows_ky * 2, 2 * rows_ky * MX)
    return np.moveaxis(out, 1, 0)


def inverse_y_table(cells_y, groups_y, peers, rows_ky):
    extent = cells_y * groups_y
    angle = angles(MY, np.arange(extent), extent)
    full = np.stack([np.cos(angle), -np.sin(angle)], axis=1)
    full = full.reshape(groups_y, peers, rows_ky, 2, groups_y, cells_y)
    out = np.zeros((groups_y, 2, cells_y, peers, 2, rows_ky, 2))
    for y in range(groups_y):
        for column in range(2):
            for peer in range(peers):
                for place in range(2):
                    half = y ^ place ^ column ^ (peer % 2)
                    out[y, column, :, peer, place] = np.moveaxis(full[half, peer, :, :, y], -1, 0)
    return out.reshape(groups_y, 2, cells_y, 4 * peers * rows_ky)


def output_table(table):
    high, low = split_table(table)
    parts = [high, high, low, np.ones(table.shape[:-1] + (BIAS_TERMS,), high.dtype)]
    used = 3 * table.shape[-1] + BIAS_TERMS
    parts.append(np.zeros(table.shape[:-1] + (-used % 256,), high.dtype))
    return np.concatenate(parts, axis=-1)


def dot(left, right):
    return jnp.dot(left, right, preferred_element_type=jnp.float32)


def column_of(x, y):
    return x ^ y


def forward_y_table(shape, extent, layers, rows_ky):
    z, x, y = quad()
    peers = 2 * layers
    row = lax.broadcasted_iota(jnp.int32, (shape[0], 1), 0)
    block = row // (2 * rows_ky)
    place = block // 2 % layers
    turn = layers - 1 - place
    side = y ^ (1 - block // peers)
    owner = (side ^ (block % 2)) * peers + (z ^ turn) * 2 + column_of(x, side)
    index = owner * rows_ky + row // 2 % rows_ky
    y_places = lax.broadcasted_iota(jnp.int32, (1, shape[1]), 1) + y * shape[1]
    steps = (wave_number(index, MY) * y_places) & (extent - 1)
    angle = 2.0 * math.pi / extent * steps.astype(jnp.float32)
    return jnp.where(row % 2 == 0, jnp.cos(angle), -jnp.sin(angle)).astype(jnp.bfloat16)


def forward_y_kernel(extent, rows_ky, flow_hbm, *refs):
    out_refs, (flow_ref, arrived) = refs[:4], refs[4:]
    half, _, rows, feat_count = out_refs[0].shape
    layers = 2 * half
    cells_x, cells_y, _ = flow_ref.shape
    rows = rows // cells_x
    copies = [
        pltpu.make_async_copy(flow_hbm.at[x], flow_ref.at[x], arrived.at[x])
        for x in range(cells_x)
    ]
    for copy in copies:
        copy.start()
    table = forward_y_table((2 * MY, cells_y), extent, layers, rows_ky)
    for x in range(cells_x):
        copies[x].wait()
        result = dot(table, flow_ref[x]).reshape(4, half, 2, rows, feat_count)
        for index, out_ref in enumerate(out_refs):
            out_ref[:, :, x * rows : (x + 1) * rows, :] = result[index]


def forward_y(flow_field, extent, layers, rows_ky):
    cells_x, _, feat_count = flow_field.shape
    shape = jax.ShapeDtypeStruct((layers // 2, 2, cells_x * 2 * rows_ky, feat_count), jnp.float32)
    return pl.pallas_call(
        functools.partial(forward_y_kernel, extent, rows_ky),
        in_specs=[pl.BlockSpec(memory_space=pltpu.HBM)],
        out_shape=[shape] * 4,
        scratch_shapes=[
            pltpu.VMEM(flow_field.shape, flow_field.dtype),
            pltpu.SemaphoreType.DMA((cells_x,)),
        ],
        compiler_params=LARGE,
        name="forward_y",
    )(flow_field)


def flip_core(block):
    return lax.ppermute(block, "gy", [(0, 1), (1, 0)])


def along_columns(blocks, peers, order):
    arrived = []
    for turn, block in zip(order, blocks):
        pairs = [
            (2 * place + core, 2 * (place ^ (2 * turn + column_of(0, core))) + core)
            for place in range(peers)
            for core in range(2)
        ]
        arrived.append(lax.ppermute(block, ("gx", "gy"), pairs))
    return arrived


def small_call(kernel, out_shape, name):
    return pl.pallas_call(kernel, out_shape=out_shape, compiler_params=SMALL, name=name)


def second_kernel(*refs):
    for index, block_ref in enumerate(refs[:-1]):
        refs[-1][index] = block_ref[1]


def second_halves(blocks):
    shape = jax.ShapeDtypeStruct((len(blocks),) + blocks[0].shape[1:], blocks[0].dtype)
    return small_call(second_kernel, shape, "second_halves")(*blocks)


def stack_kernel(*refs):
    for index, block_ref in enumerate(refs[:-1]):
        refs[-1][index] = block_ref[...]


def stack_blocks(blocks):
    shape = jax.ShapeDtypeStruct((len(blocks),) + blocks[0].shape, blocks[0].dtype)
    return small_call(stack_kernel, shape, "stack_blocks")(*blocks)


def add_kernel(keep_ref, arrived_ref, *out_refs):
    for turn, out_ref in enumerate(out_refs):
        out_ref[...] = keep_ref[turn] + arrived_ref[turn]


def add_blocks(keep, arrived):
    shape = jax.ShapeDtypeStruct(keep.shape[1:], keep.dtype)
    return small_call(add_kernel, [shape] * keep.shape[0], "add_blocks")(keep, arrived)


def join_kernel(keep_ref, arrived_ref, *out_refs):
    cells_x, rows, _ = out_refs[0].shape
    rows = rows // 2
    for turn, out_ref in enumerate(out_refs):
        for cell in range(cells_x):
            span = slice(cell * rows, (cell + 1) * rows)
            out_ref[cell] = jnp.concatenate(
                [keep_ref[turn, span, :], arrived_ref[turn, span, :]], axis=0
            )


def join_blocks(keep, arrived, cells_x):
    layers, rows, feat_count = keep.shape
    shape = jax.ShapeDtypeStruct((cells_x, 2 * rows // cells_x, feat_count), keep.dtype)
    return small_call(join_kernel, [shape] * layers, "join_blocks")(keep, arrived)


def back_rows(inverse_high, inverse_low, modes, shape, other):
    z, x, y = quad()
    places = [(column_of(x, y) ^ other, z ^ turn) for turn in turns(shape[0], True)]
    table_high, table_low = [
        jnp.concatenate([ref[column, place] for column, place in places], axis=0)
        for ref in (inverse_high, inverse_low)
    ]
    high, low = split_terms(modes)
    back = dot(table_high, high) + dot(table_high, low) + dot(table_low, high)
    return back.reshape(shape)


def mix_kernel(layers, *refs):
    half = layers // 2
    block_refs = refs[:layers]
    far_arrived, near_arrived = refs[layers : layers + 2]
    weight_ref, forward_high, forward_low, inverse_high, inverse_low = refs[
        layers + 2 : layers + 7
    ]
    modes_ref, far_ref, near_ref, order_ref, spread_ref, result_ref = refs[layers + 7 :]
    z, x, y = quad()
    column = column_of(x, y)
    for index, turn in enumerate(turns(layers)):
        arrived_ref = near_arrived if index >= half else far_arrived
        order_ref[(z ^ turn) * 2 + column] = block_refs[index][0]
        order_ref[(z ^ turn) * 2 + (column ^ 1)] = arrived_ref[index % half]
    feat_count = order_ref.shape[-1]
    count = weight_ref.shape[1]
    channels = weight_ref.shape[2]
    tiles = feat_count // 128
    group = 2 * tiles
    high, low = split_terms(order_ref[...].reshape(-1, feat_count))
    spectrum = (
        dot(forward_high[...], high) + dot(forward_high[...], low) + dot(forward_low[...], high)
    )
    for part in range(2):
        for tile in range(tiles):
            spread_ref[pl.ds(part * tiles + tile, count, stride=group), :] = spectrum[
                part * count : (part + 1) * count, tile * 128 : (tile + 1) * 128
            ]
    rows = lax.broadcasted_iota(jnp.int32, (8, 128), 0) % group
    lane = lax.broadcasted_iota(jnp.int32, (8, 128), 1) < channels
    sign = jnp.where(rows < tiles, -1.0, 1.0)
    for base in range(0, count * group, 8):
        block = spread_ref[base : base + 8, :]
        turned = pltpu.roll(block, channels, 1)
        firsts, seconds = [], []
        for start in range(0, 8, group):
            span = slice(start, start + group)
            left = jnp.concatenate([block[span], turned[span]], axis=0)[:, :channels]
            left_high, left_low = split_terms(left)
            left = jnp.concatenate([left_high, left_low], axis=0)
            product = dot(left, weight_ref[0, (base + start) // group])
            product = product[: 2 * group] + product[2 * group :]
            firsts.append(product[:group])
            seconds.append(product[group:])
        first = jnp.concatenate(firsts, axis=0)
        second = jnp.concatenate(seconds, axis=0)
        real = jnp.where(lane, first, pltpu.roll(second, channels, 1))
        imag = jnp.where(lane, pltpu.roll(first, channels, 1), second)
        crossed = jnp.where(rows < tiles, pltpu.roll(imag, 8 - tiles, 0), pltpu.roll(imag, tiles, 0))
        result_ref[base : base + 8, :] = real + sign * crossed
    for part in range(2):
        for tile in range(tiles):
            modes_ref[part * count : (part + 1) * count, tile * 128 : (tile + 1) * 128] = (
                result_ref[pl.ds(part * tiles + tile, count, stride=group), :]
            )
    shape = (layers,) + far_ref.shape[1:]
    send = back_rows(inverse_high, inverse_low, modes_ref[...], shape, 1)
    far_ref[...] = send[: layers // 2]
    near_ref[...] = send[layers // 2 :]


def mix(blocks, arrived, weights, forward_table, inverse_tables):
    layers = len(blocks)
    _, rows, feat_count = blocks[0].shape
    count = weights.shape[1]
    scratch = pltpu.VMEM((count * feat_count // 64, 128), jnp.float32)
    return pl.pallas_call(
        functools.partial(mix_kernel, layers),
        out_shape=[
            jax.ShapeDtypeStruct((2 * count, feat_count), jnp.float32),
            jax.ShapeDtypeStruct((layers // 2, rows, feat_count), jnp.float32),
            jax.ShapeDtypeStruct((layers // 2, rows, feat_count), jnp.float32),
        ],
        scratch_shapes=[pltpu.VMEM((2 * layers, rows, feat_count), jnp.float32), scratch, scratch],
        compiler_params=SMALL,
        name="mix",
    )(*blocks, *arrived, weights, *split_table(forward_table), *inverse_tables)


def keep_kernel(modes_ref, inverse_high, inverse_low, far_ref, near_ref):
    half = far_ref.shape[0]
    shape = (2 * half,) + far_ref.shape[1:]
    keep = back_rows(inverse_high, inverse_low, modes_ref[...], shape, 0)
    far_ref[...] = keep[:half]
    near_ref[...] = keep[half:]


def keep_rows(modes, inverse_tables, like):
    return pl.pallas_call(
        keep_kernel,
        out_shape=[jax.ShapeDtypeStruct(like.shape, jnp.float32)] * 2,
        compiler_params=SMALL,
        name="keep_rows",
    )(modes, *inverse_tables)


def gelu(half):
    square = jnp.minimum(half * half, 6.25)
    inner = jnp.full_like(square, GELU_TERMS[-1])
    for term in GELU_TERMS[-2::-1]:
        inner = inner * square + term
    return half + half * jnp.tanh(half * inner)


def output_kernel(layers, flow_ref, table_ref, local_ref, bias_ref, modes_ref, *refs):
    own_refs = refs[layers // 2 : layers] + refs[: layers // 2]
    near_ref, far_ref = refs[layers : layers + 2]
    core_refs = [ref.at[index] for ref in (far_ref, near_ref) for index in range(layers // 2)]
    out_hbm, mixed_hbm, order_ref, wide_ref, level_ref, done_ref, sent = refs[layers + 2 :]
    cells_x, cells_y, feat_count = flow_ref.shape
    channels = local_ref.shape[0]
    z, x, y = quad()
    wide_ref[...] = jnp.zeros_like(wide_ref)
    for start in range(0, WIDTH, channels):
        span = slice(start, start + channels)
        wide_ref[span, span] = local_ref[...] * 0.5
        level_ref[:, span] = bias_ref[...].reshape(1, channels) * 0.5
    level = level_ref[...]
    levels = []
    for _ in range(BIAS_TERMS):
        levels.append(level.astype(jnp.bfloat16).astype(jnp.float32))
        level = level - levels[-1]
    terms = 3 * order_ref.shape[1] * order_ref.shape[2]
    filled = jnp.zeros((table_ref.shape[-1] - terms - BIAS_TERMS, WIDTH), jnp.float32)
    below = jnp.concatenate(levels + [filled], axis=0).astype(jnp.bfloat16)
    below = jnp.concatenate([below, wide_ref[...]], axis=0)
    for column, block_refs in ((x ^ y, own_refs), (x ^ y ^ 1, core_refs)):
        for turn, block_ref in zip(turns(layers, True), block_refs):
            order_ref[:, (z ^ turn) * 2 + column] = block_ref[...]
    table = table_ref[y, x ^ y]
    count = modes_ref.shape[0] // 2
    copies = []
    for part in range(2):
        copies.append(
            pltpu.make_async_copy(
                modes_ref.at[pl.ds(part * count, count)],
                mixed_hbm.at[0, :, pl.ds(part * feat_count, feat_count)],
                sent.at[part],
            )
        )
        copies[-1].start()
    for cell in range(cells_x):
        high, low = split_terms(order_ref[cell].reshape(-1, feat_count))
        stack = jnp.concatenate([high, low, high], axis=0)
        bounds = [0, cells_y - LAST, cells_y] if cell == cells_x - 1 else [0, cells_y]
        for begin, end in zip(bounds[:-1], bounds[1:]):
            rows = slice(begin, end)
            for start in range(0, feat_count, WIDTH):
                columns = slice(start, start + WIDTH)
                total = dot(
                    jnp.concatenate([table[rows], flow_ref[cell, rows, columns]], axis=1),
                    jnp.concatenate([stack[:, columns], below], axis=0),
                )
                done_ref[cell, rows, columns] = gelu(total).astype(done_ref.dtype)
            copies.append(
                pltpu.make_async_copy(
                    done_ref.at[cell, rows], out_hbm.at[cell, rows], sent.at[len(copies)]
                )
            )
            copies[-1].start()
    for copy in copies:
        copy.wait()


def make_output(flow_field, parts, table, local, bias, modes):
    cells_x, _, feat_count = flow_field.shape
    layers = len(parts) - 2
    rows, _ = modes.shape
    return pl.pallas_call(
        functools.partial(output_kernel, layers),
        out_specs=[pl.BlockSpec(memory_space=pl.ANY)] * 2,
        scratch_shapes=[
            pltpu.VMEM((cells_x, 2 * layers) + parts[0].shape[1:], jnp.float32),
            pltpu.VMEM((WIDTH, WIDTH), jnp.bfloat16),
            pltpu.VMEM((1, WIDTH), jnp.float32),
            pltpu.VMEM(flow_field.shape, jnp.bfloat16),
            pltpu.SemaphoreType.DMA((cells_x + 3,)),
        ],
        out_shape=[
            jax.ShapeDtypeStruct(flow_field.shape, jnp.bfloat16),
            jax.ShapeDtypeStruct((1, rows // 2, 2 * feat_count), jnp.float32),
        ],
        compiler_params=SMALL,
        name="make_output",
    )(flow_field, table, local, bias, modes, *parts)


def row_body(flow_field, spectral_weight, local_weight, bias_terms):
    cells_x, cells_y, feat_count = flow_field.shape
    peers = lax.axis_size("gx")
    groups_y = lax.axis_size("gy")
    rows_ky = MY // groups_y // peers
    forward_scale = 1.0 / math.sqrt(cells_x * peers * cells_y * groups_y)
    inverse_scale = 1.0 / math.sqrt(MX * MY)

    send_far, send_near, keep_far, keep_near = forward_y(
        flow_field, cells_y * groups_y, peers // 2, rows_ky
    )
    order = turns(peers // 2)
    middle = peers // 4
    near = along_columns(add_blocks(keep_near, flip_core(send_near)), peers, order[middle:])
    far = along_columns(add_blocks(keep_far, flip_core(send_far)), peers, order[:middle])
    blocks = far + near
    inverse_tables = split_table(inverse_x_table(cells_x, peers, rows_ky))
    modes, send_far, send_near = mix(
        blocks,
        [flip_core(second_halves(far)), flip_core(second_halves(near))],
        spectral_weight,
        forward_x_table(cells_x, peers, rows_ky) * forward_scale,
        inverse_tables,
    )
    arrived_near, arrived_far = flip_core(send_near), flip_core(send_far)
    keep_far, keep_near = keep_rows(modes, inverse_tables, send_far)
    order = turns(peers // 2, True)
    own_near = along_columns(join_blocks(keep_near, arrived_near, cells_x), peers, order[middle:])
    own_far = along_columns(join_blocks(keep_far, arrived_far, cells_x), peers, order[:middle])
    flipped = [flip_core(stack_blocks(own)) for own in (own_near, own_far)]
    parts = own_near + own_far + flipped
    table = output_table(inverse_y_table(cells_y, groups_y, peers, rows_ky) * (0.5 * inverse_scale))
    return tuple(make_output(flow_field, parts, table, local_weight, bias_terms, modes))


def body(flow_field, spectral_weight, local_weight, bias_terms):
    peers = lax.axis_size("gx")
    extent = lax.axis_size("gy") * flow_field.shape[1]
    paired = lax.axis_size("gy") == 2 and peers & (peers - 1) == 0 and extent & (extent - 1) == 0
    if paired and spectral_weight.shape[1] == 2 * MX and WIDTH % local_weight.shape[0] == 0:
        return row_body(flow_field, spectral_weight, local_weight, bias_terms)
    return general_body(flow_field, spectral_weight, local_weight, bias_terms)


def solution(mesh):
    placed = (P(("group", "gx"), "gy", None), P("gy", "gx", None, None), P(), P())
    return jax.shard_map(
        body,
        mesh=mesh,
        in_specs=placed,
        out_specs=(P(("group", "gx"), "gy", None), P(("group", "gy"), "gx", None)),
        check_vma=False,
    )
```

```python
import functools
import math

import jax
import jax.numpy as jnp
import ml_dtypes
import numpy as np
from jax import lax
from jax.experimental import pallas as pl
from jax.experimental.pallas import tpu as pltpu
from jax.sharding import PartitionSpec as P

MX = 32
MY = 32


def wave_number(index, count):
    return jnp.where(index < count // 2, index, index - count)


def phase_table(waves, places, extent):
    product = waves[:, None] * places[None, :] % extent
    return 2.0 * math.pi / extent * product.astype(jnp.float32)


def row_tables(ky_rows, kx_rows, x_places, extent, width):
    angle = phase_table(wave_number(kx_rows, MX), x_places, extent)
    select = (ky_rows[:, None] == jnp.arange(width, dtype=jnp.int32)[None, :]).astype(jnp.float32)
    cosine = jnp.cos(angle)[:, :, None] * select[:, None, :]
    sine_part = jnp.sin(angle)[:, :, None] * select[:, None, :]
    return (cosine, sine_part)


def forward_rows(y_local, ky_rows, kx_rows, x_places, extent):
    cosine, sine_part = row_tables(ky_rows, kx_rows, x_places, extent, y_local.shape[0])
    real_in = y_local[:, 0]
    imag_in = y_local[:, 1]

    def contract(table, values):
        return jnp.einsum("rxk,kxf->rf", table, values, precision=lax.Precision.HIGHEST)

    real_out = contract(cosine, real_in) + contract(sine_part, imag_in)
    imag_out = contract(cosine, imag_in) - contract(sine_part, real_in)
    return jnp.concatenate([real_out, imag_out], axis=1)


def inverse_rows(running, shard_rows, ky_rows, kx_rows, x_places, extent):
    cosine, sine_part = row_tables(ky_rows, kx_rows, x_places, extent, running.shape[0])
    feat_count = shard_rows.shape[1] // 2
    real_part = shard_rows[:, :feat_count]
    imag_part = shard_rows[:, feat_count:]

    def contract(table, values):
        return jnp.einsum("rxk,rf->kxf", table, values, precision=lax.Precision.HIGHEST)

    new_real = contract(cosine, real_part) - contract(sine_part, imag_part)
    new_imag = contract(cosine, imag_part) + contract(sine_part, real_part)
    return jnp.stack([new_real, new_imag], axis=1)


def general_body(flow_field, spectral_weight, local_weight, bias_terms):
    cells_x, cells_y, feat_count = flow_field.shape
    channels = local_weight.shape[0]
    planes = feat_count // channels
    groups_x = lax.axis_size("gx")
    groups_y = lax.axis_size("gy")
    extent_x = cells_x * groups_x
    extent_y = cells_y * groups_y
    half_width = MY // groups_y
    quota_rows = spectral_weight.shape[1]
    high = lax.Precision.HIGHEST
    x_places = lax.axis_index("gx") * cells_x + jnp.arange(cells_x, dtype=jnp.int32)
    y_places = lax.axis_index("gy") * cells_y + jnp.arange(cells_y, dtype=jnp.int32)
    y_angle = phase_table(wave_number(jnp.arange(MY, dtype=jnp.int32), MY), y_places, extent_y)
    y_table = (
        jnp.stack([jnp.cos(y_angle), -jnp.sin(y_angle)], axis=1)
        .reshape(2 * MY, cells_y)
        .astype(jnp.bfloat16)
    )
    y_local = lax.psum_scatter(
        jnp.einsum("qy,xyf->qxf", y_table, flow_field, preferred_element_type=jnp.float32),
        "gy",
        scatter_dimension=0,
        tiled=True,
    )
    y_local = y_local.reshape(half_width, 2, cells_x, feat_count)
    rest_index = jnp.arange(lax.axis_size("gx") * quota_rows, dtype=jnp.int32)
    spectrum = lax.psum_scatter(
        forward_rows(y_local, rest_index // MX, rest_index % MX, x_places, extent_x),
        "gx",
        scatter_dimension=0,
        tiled=True,
    )
    spectrum = spectrum * (1.0 / math.sqrt(extent_x * extent_y))
    coeffs = spectrum.reshape(quota_rows, 2, planes, channels)
    weights = spectral_weight[0].astype(jnp.float32)
    product = jnp.einsum("rpzc,rco->rpzo", coeffs, weights, precision=high)
    mixed_real = product[:, 0, :, :channels] - product[:, 1, :, channels:]
    mixed_imag = product[:, 0, :, channels:] + product[:, 1, :, :channels]
    mixed_local = jnp.stack([mixed_real, mixed_imag], axis=1).reshape(quota_rows, 2 * feat_count)
    pointwise = jnp.einsum(
        "xyzc,co->xyzo",
        flow_field.reshape(cells_x, cells_y, planes, channels),
        local_weight,
        preferred_element_type=jnp.float32,
    )
    start_half = jnp.zeros((half_width, 2, cells_x, feat_count), jnp.float32)
    shard_rows = lax.all_gather(mixed_local, "gx", axis=0, tiled=True)
    rest_index = jnp.arange(shard_rows.shape[0], dtype=jnp.int32)
    back_half = inverse_rows(
        start_half, shard_rows, rest_index // MX, rest_index % MX, x_places, extent_x
    )
    back_whole = lax.all_gather(back_half, "gy", axis=0, tiled=True)
    y_cos = jnp.cos(y_angle)
    y_sin = jnp.sin(y_angle)
    spectral = (
        jnp.einsum("kn,kxf->xnf", y_cos, back_whole[:, 0], precision=high)
        - jnp.einsum("kn,kxf->xnf", y_sin, back_whole[:, 1], precision=high)
    ) * (1.0 / math.sqrt(MX * MY))
    total = spectral.reshape(cells_x, cells_y, planes, channels) + pointwise + bias_terms
    output = (
        jax.nn.gelu(total, approximate=False)
        .reshape(cells_x, cells_y, feat_count)
        .astype(jnp.bfloat16)
    )
    return (output, mixed_local.reshape(1, quota_rows, 2 * feat_count))


SMALL = pltpu.CompilerParams(vmem_limit_bytes=20 * 1024 * 1024)
LARGE = pltpu.CompilerParams(vmem_limit_bytes=53 * 1024 * 1024)
WIDTH = 256
BIAS_TERMS = 3
LAST = 64
GELU_TERMS = (
    1.5957645177841187,
    0.29075613617897034,
    -0.0014313592109829187,
    -0.006452994421124458,
    0.0015898864949122071,
    -0.0001365363277727738,
)


def angles(count, places, extent):
    index = np.arange(count)
    waves = np.where(index < count // 2, index, index - count)
    product = (waves[:, None] * np.asarray(places)[None, :]) % extent
    return (np.float32(2.0 * math.pi / extent) * product.astype(np.float32)).astype(np.float64)


def split_table(table):
    high = table.astype(ml_dtypes.bfloat16)
    low = (table - high.astype(np.float64)).astype(ml_dtypes.bfloat16)
    return high, low


def split_terms(values):
    high = values.astype(jnp.bfloat16)
    low = (values - high.astype(jnp.float32)).astype(jnp.bfloat16)
    return high, low


def quad():
    place = lax.axis_index("gx")
    return place // 2, place % 2, lax.axis_index("gy")


def turns(layers, inverse=False):
    half = layers // 2
    if inverse:
        return list(range(half, layers)) + list(range(half - 1, -1, -1))
    return list(range(layers - 1, -1, -1))


def forward_x_table(cells_x, peers, rows_ky):
    extent = cells_x * peers
    angle = angles(MX, np.arange(extent), extent)
    cosine, sine = np.cos(angle), np.sin(angle)
    out = np.zeros((2, rows_ky, MX, extent, rows_ky, 2))
    for row in range(rows_ky):
        out[0, row, :, :, row, 0] = cosine
        out[0, row, :, :, row, 1] = sine
        out[1, row, :, :, row, 1] = cosine
        out[1, row, :, :, row, 0] = -sine
    return out.reshape(2 * rows_ky * MX, extent * rows_ky * 2)


def inverse_x_table(cells_x, peers, rows_ky):
    extent = cells_x * peers
    angle = angles(MX, np.arange(extent), extent)
    cosine, sine = np.cos(angle).T, np.sin(angle).T
    out = np.zeros((extent, rows_ky, 2, 2, rows_ky, MX))
    for row in range(rows_ky):
        out[:, row, 0, 0, row, :] = cosine
        out[:, row, 0, 1, row, :] = -sine
        out[:, row, 1, 1, row, :] = cosine
        out[:, row, 1, 0, row, :] = sine
    out = out.reshape(peers // 2, 2, cells_x * rows_ky * 2, 2 * rows_ky * MX)
    return np.moveaxis(out, 1, 0)


def inverse_y_table(cells_y, groups_y, peers, rows_ky):
    extent = cells_y * groups_y
    angle = angles(MY, np.arange(extent), extent)
    full = np.stack([np.cos(angle), -np.sin(angle)], axis=1)
    full = full.reshape(groups_y, peers, rows_ky, 2, groups_y, cells_y)
    out = np.zeros((groups_y, 2, cells_y, peers, 2, rows_ky, 2))
    for y in range(groups_y):
        for column in range(2):
            for peer in range(peers):
                for place in range(2):
                    half = y ^ place ^ column ^ (peer % 2)
                    out[y, column, :, peer, place] = np.moveaxis(full[half, peer, :, :, y], -1, 0)
    return out.reshape(groups_y, 2, cells_y, 4 * peers * rows_ky)


def joined_table(table):
    high, low = split_table(table)
    return np.concatenate([high, high, low], axis=-1)


def joined_terms(values):
    high, low = split_terms(values)
    return jnp.concatenate([high, low, high], axis=0)


def output_table(table):
    high, low = split_table(table)
    parts = [high, high, low, np.ones(table.shape[:-1] + (BIAS_TERMS,), high.dtype)]
    used = 3 * table.shape[-1] + BIAS_TERMS
    parts.append(np.zeros(table.shape[:-1] + (-used % 256,), high.dtype))
    return np.concatenate(parts, axis=-1)


def dot(left, right):
    return jnp.dot(left, right, preferred_element_type=jnp.float32)


def column_of(x, y):
    return x ^ y


def forward_y_table(shape, extent, layers, rows_ky):
    z, x, y = quad()
    peers = 2 * layers
    row = lax.broadcasted_iota(jnp.int32, (shape[0], 1), 0)
    block = row // (2 * rows_ky)
    place = block // 2 % layers
    turn = layers - 1 - place
    side = y ^ (1 - block // peers)
    owner = (side ^ (block % 2)) * peers + (z ^ turn) * 2 + column_of(x, side)
    index = owner * rows_ky + row // 2 % rows_ky
    y_places = lax.broadcasted_iota(jnp.int32, (1, shape[1]), 1) + y * shape[1]
    steps = (wave_number(index, MY) * y_places) & (extent - 1)
    angle = 2.0 * math.pi / extent * steps.astype(jnp.float32)
    return jnp.where(row % 2 == 0, jnp.cos(angle), -jnp.sin(angle)).astype(jnp.bfloat16)


def forward_y_kernel(extent, rows_ky, flow_hbm, *refs):
    out_refs, (flow_ref, arrived) = refs[:4], refs[4:]
    half, _, rows, feat_count = out_refs[0].shape
    layers = 2 * half
    cells_x, cells_y, _ = flow_ref.shape
    rows = rows // cells_x
    copies = [
        pltpu.make_async_copy(flow_hbm.at[x], flow_ref.at[x], arrived.at[x])
        for x in range(cells_x)
    ]
    for copy in copies:
        copy.start()
    table = forward_y_table((2 * MY, cells_y), extent, layers, rows_ky)
    for x in range(cells_x):
        copies[x].wait()
        result = dot(table, flow_ref[x]).reshape(4, half, 2, rows, feat_count)
        for index, out_ref in enumerate(out_refs):
            out_ref[:, :, x * rows : (x + 1) * rows, :] = result[index]


def forward_y(flow_field, extent, layers, rows_ky):
    cells_x, _, feat_count = flow_field.shape
    shape = jax.ShapeDtypeStruct((layers // 2, 2, cells_x * 2 * rows_ky, feat_count), jnp.float32)
    return pl.pallas_call(
        functools.partial(forward_y_kernel, extent, rows_ky),
        in_specs=[pl.BlockSpec(memory_space=pltpu.HBM)],
        out_shape=[shape] * 4,
        scratch_shapes=[
            pltpu.VMEM(flow_field.shape, flow_field.dtype),
            pltpu.SemaphoreType.DMA((cells_x,)),
        ],
        compiler_params=LARGE,
        name="forward_y",
    )(flow_field)


def flip_core(block):
    return lax.ppermute(block, "gy", [(0, 1), (1, 0)])


def along_columns(blocks, peers, order):
    arrived = []
    for turn, block in zip(order, blocks):
        pairs = [
            (2 * place + core, 2 * (place ^ (2 * turn + column_of(0, core))) + core)
            for place in range(peers)
            for core in range(2)
        ]
        arrived.append(lax.ppermute(block, ("gx", "gy"), pairs))
    return arrived


def small_call(kernel, out_shape, name):
    return pl.pallas_call(kernel, out_shape=out_shape, compiler_params=SMALL, name=name)


def second_kernel(*refs):
    for index, block_ref in enumerate(refs[:-1]):
        refs[-1][index] = block_ref[1]


def second_halves(blocks):
    shape = jax.ShapeDtypeStruct((len(blocks),) + blocks[0].shape[1:], blocks[0].dtype)
    return small_call(second_kernel, shape, "second_halves")(*blocks)


def stack_kernel(*refs):
    for index, block_ref in enumerate(refs[:-1]):
        refs[-1][index] = block_ref[...]


def stack_blocks(blocks):
    shape = jax.ShapeDtypeStruct((len(blocks),) + blocks[0].shape, blocks[0].dtype)
    return small_call(stack_kernel, shape, "stack_blocks")(*blocks)


def add_kernel(keep_ref, arrived_ref, *out_refs):
    for turn, out_ref in enumerate(out_refs):
        out_ref[...] = keep_ref[turn] + arrived_ref[turn]


def add_blocks(keep, arrived):
    shape = jax.ShapeDtypeStruct(keep.shape[1:], keep.dtype)
    return small_call(add_kernel, [shape] * keep.shape[0], "add_blocks")(keep, arrived)


def join_kernel(keep_ref, arrived_ref, *out_refs):
    cells_x, rows, _ = out_refs[0].shape
    rows = rows // 2
    for turn, out_ref in enumerate(out_refs):
        for cell in range(cells_x):
            span = slice(cell * rows, (cell + 1) * rows)
            out_ref[cell] = jnp.concatenate(
                [keep_ref[turn, span, :], arrived_ref[turn, span, :]], axis=0
            )


def join_blocks(keep, arrived, cells_x):
    layers, rows, feat_count = keep.shape
    shape = jax.ShapeDtypeStruct((cells_x, 2 * rows // cells_x, feat_count), keep.dtype)
    return small_call(join_kernel, [shape] * layers, "join_blocks")(keep, arrived)


def back_rows(inverse_table, modes, shape, other):
    z, x, y = quad()
    places = [(column_of(x, y) ^ other, z ^ turn) for turn in turns(shape[0], True)]
    table = jnp.concatenate([inverse_table[column, place] for column, place in places], axis=0)
    back = dot(table, joined_terms(modes))
    return back.reshape(shape)


def mix_kernel(layers, *refs):
    half = layers // 2
    block_refs = refs[:layers]
    far_arrived, near_arrived = refs[layers : layers + 2]
    weight_ref, forward_table, inverse_table = refs[layers + 2 : layers + 5]
    modes_ref, far_ref, near_ref, order_ref, spread_ref, result_ref = refs[layers + 5 :]
    z, x, y = quad()
    column = column_of(x, y)
    for index, turn in enumerate(turns(layers)):
        arrived_ref = near_arrived if index >= half else far_arrived
        order_ref[(z ^ turn) * 2 + column] = block_refs[index][0]
        order_ref[(z ^ turn) * 2 + (column ^ 1)] = arrived_ref[index % half]
    feat_count = order_ref.shape[-1]
    count = weight_ref.shape[1]
    channels = weight_ref.shape[2]
    tiles = feat_count // 128
    group = 2 * tiles
    spectrum = dot(forward_table[...], joined_terms(order_ref[...].reshape(-1, feat_count)))
    for part in range(2):
        for tile in range(tiles):
            spread_ref[pl.ds(part * tiles + tile, count, stride=group), :] = spectrum[
                part * count : (part + 1) * count, tile * 128 : (tile + 1) * 128
            ]
    rows = lax.broadcasted_iota(jnp.int32, (8, 128), 0) % group
    lane = lax.broadcasted_iota(jnp.int32, (8, 128), 1) < channels
    sign = jnp.where(rows < tiles, -1.0, 1.0)
    for base in range(0, count * group, 8):
        block = spread_ref[base : base + 8, :]
        turned = pltpu.roll(block, channels, 1)
        firsts, seconds = [], []
        for start in range(0, 8, group):
            span = slice(start, start + group)
            left = jnp.concatenate([block[span], turned[span]], axis=0)[:, :channels]
            left_high, left_low = split_terms(left)
            left = jnp.concatenate([left_high, left_low], axis=0)
            product = dot(left, weight_ref[0, (base + start) // group])
            product = product[: 2 * group] + product[2 * group :]
            firsts.append(product[:group])
            seconds.append(product[group:])
        first = jnp.concatenate(firsts, axis=0)
        second = jnp.concatenate(seconds, axis=0)
        real = jnp.where(lane, first, pltpu.roll(second, channels, 1))
        imag = jnp.where(lane, pltpu.roll(first, channels, 1), second)
        crossed = jnp.where(rows < tiles, pltpu.roll(imag, 8 - tiles, 0), pltpu.roll(imag, tiles, 0))
        result_ref[base : base + 8, :] = real + sign * crossed
    for part in range(2):
        for tile in range(tiles):
            modes_ref[part * count : (part + 1) * count, tile * 128 : (tile + 1) * 128] = (
                result_ref[pl.ds(part * tiles + tile, count, stride=group), :]
            )
    shape = (layers,) + far_ref.shape[1:]
    send = back_rows(inverse_table, modes_ref[...], shape, 1)
    far_ref[...] = send[: layers // 2]
    near_ref[...] = send[layers // 2 :]


def mix(blocks, arrived, weights, forward_table, inverse_table):
    layers = len(blocks)
    _, rows, feat_count = blocks[0].shape
    count = weights.shape[1]
    scratch = pltpu.VMEM((count * feat_count // 64, 128), jnp.float32)
    return pl.pallas_call(
        functools.partial(mix_kernel, layers),
        out_shape=[
            jax.ShapeDtypeStruct((2 * count, feat_count), jnp.float32),
            jax.ShapeDtypeStruct((layers // 2, rows, feat_count), jnp.float32),
            jax.ShapeDtypeStruct((layers // 2, rows, feat_count), jnp.float32),
        ],
        scratch_shapes=[pltpu.VMEM((2 * layers, rows, feat_count), jnp.float32), scratch, scratch],
        compiler_params=SMALL,
        name="mix",
    )(*blocks, *arrived, weights, joined_table(forward_table), inverse_table)


def keep_kernel(modes_ref, inverse_table, far_ref, near_ref):
    half = far_ref.shape[0]
    shape = (2 * half,) + far_ref.shape[1:]
    keep = back_rows(inverse_table, modes_ref[...], shape, 0)
    far_ref[...] = keep[:half]
    near_ref[...] = keep[half:]


def keep_rows(modes, inverse_table, like):
    return pl.pallas_call(
        keep_kernel,
        out_shape=[jax.ShapeDtypeStruct(like.shape, jnp.float32)] * 2,
        compiler_params=SMALL,
        name="keep_rows",
    )(modes, inverse_table)


def gelu(half):
    square = jnp.minimum(half * half, 6.25)
    inner = jnp.full_like(square, GELU_TERMS[-1])
    for term in GELU_TERMS[-2::-1]:
        inner = inner * square + term
    return half + half * jnp.tanh(half * inner)


def output_kernel(layers, flow_ref, table_ref, local_ref, bias_ref, modes_ref, *refs):
    own_refs = refs[layers // 2 : layers] + refs[: layers // 2]
    near_ref, far_ref = refs[layers : layers + 2]
    core_refs = [ref.at[index] for ref in (far_ref, near_ref) for index in range(layers // 2)]
    out_hbm, mixed_hbm, order_ref, wide_ref, level_ref, done_ref, sent = refs[layers + 2 :]
    cells_x, cells_y, feat_count = flow_ref.shape
    channels = local_ref.shape[0]
    z, x, y = quad()
    wide_ref[...] = jnp.zeros_like(wide_ref)
    for start in range(0, WIDTH, channels):
        span = slice(start, start + channels)
        wide_ref[span, span] = local_ref[...] * 0.5
        level_ref[:, span] = bias_ref[...].reshape(1, channels) * 0.5
    level = level_ref[...]
    levels = []
    for _ in range(BIAS_TERMS):
        levels.append(level.astype(jnp.bfloat16).astype(jnp.float32))
        level = level - levels[-1]
    terms = 3 * order_ref.shape[1] * order_ref.shape[2]
    filled = jnp.zeros((table_ref.shape[-1] - terms - BIAS_TERMS, WIDTH), jnp.float32)
    below = jnp.concatenate(levels + [filled], axis=0).astype(jnp.bfloat16)
    below = jnp.concatenate([below, wide_ref[...]], axis=0)
    for column, block_refs in ((x ^ y, own_refs), (x ^ y ^ 1, core_refs)):
        for turn, block_ref in zip(turns(layers, True), block_refs):
            order_ref[:, (z ^ turn) * 2 + column] = block_ref[...]
    table = table_ref[y, x ^ y]
    count = modes_ref.shape[0] // 2
    copies = []
    for part in range(2):
        copies.append(
            pltpu.make_async_copy(
                modes_ref.at[pl.ds(part * count, count)],
                mixed_hbm.at[0, :, pl.ds(part * feat_count, feat_count)],
                sent.at[part],
            )
        )
        copies[-1].start()
    for cell in range(cells_x):
        high, low = split_terms(order_ref[cell].reshape(-1, feat_count))
        stack = jnp.concatenate([high, low, high], axis=0)
        bounds = [0, cells_y - LAST, cells_y] if cell == cells_x - 1 else [0, cells_y]
        for begin, end in zip(bounds[:-1], bounds[1:]):
            rows = slice(begin, end)
            for start in range(0, feat_count, WIDTH):
                columns = slice(start, start + WIDTH)
                total = dot(
                    jnp.concatenate([table[rows], flow_ref[cell, rows, columns]], axis=1),
                    jnp.concatenate([stack[:, columns], below], axis=0),
                )
                done_ref[cell, rows, columns] = gelu(total).astype(done_ref.dtype)
            copies.append(
                pltpu.make_async_copy(
                    done_ref.at[cell, rows], out_hbm.at[cell, rows], sent.at[len(copies)]
                )
            )
            copies[-1].start()
    for copy in copies:
        copy.wait()


def make_output(flow_field, parts, table, local, bias, modes):
    cells_x, _, feat_count = flow_field.shape
    layers = len(parts) - 2
    rows, _ = modes.shape
    return pl.pallas_call(
        functools.partial(output_kernel, layers),
        out_specs=[pl.BlockSpec(memory_space=pl.ANY)] * 2,
        scratch_shapes=[
            pltpu.VMEM((cells_x, 2 * layers) + parts[0].shape[1:], jnp.float32),
            pltpu.VMEM((WIDTH, WIDTH), jnp.bfloat16),
            pltpu.VMEM((1, WIDTH), jnp.float32),
            pltpu.VMEM(flow_field.shape, jnp.bfloat16),
            pltpu.SemaphoreType.DMA((cells_x + 3,)),
        ],
        out_shape=[
            jax.ShapeDtypeStruct(flow_field.shape, jnp.bfloat16),
            jax.ShapeDtypeStruct((1, rows // 2, 2 * feat_count), jnp.float32),
        ],
        compiler_params=SMALL,
        name="make_output",
    )(flow_field, table, local, bias, modes, *parts)


def row_body(flow_field, spectral_weight, local_weight, bias_terms):
    cells_x, cells_y, feat_count = flow_field.shape
    peers = lax.axis_size("gx")
    groups_y = lax.axis_size("gy")
    rows_ky = MY // groups_y // peers
    forward_scale = 1.0 / math.sqrt(cells_x * peers * cells_y * groups_y)
    inverse_scale = 1.0 / math.sqrt(MX * MY)

    send_far, send_near, keep_far, keep_near = forward_y(
        flow_field, cells_y * groups_y, peers // 2, rows_ky
    )
    order = turns(peers // 2)
    middle = peers // 4
    near = along_columns(add_blocks(keep_near, flip_core(send_near)), peers, order[middle:])
    far = along_columns(add_blocks(keep_far, flip_core(send_far)), peers, order[:middle])
    blocks = far + near
    inverse_table = joined_table(inverse_x_table(cells_x, peers, rows_ky))
    modes, send_far, send_near = mix(
        blocks,
        [flip_core(second_halves(far)), flip_core(second_halves(near))],
        spectral_weight,
        forward_x_table(cells_x, peers, rows_ky) * forward_scale,
        inverse_table,
    )
    arrived_near, arrived_far = flip_core(send_near), flip_core(send_far)
    keep_far, keep_near = keep_rows(modes, inverse_table, send_far)
    order = turns(peers // 2, True)
    own_near = along_columns(join_blocks(keep_near, arrived_near, cells_x), peers, order[middle:])
    own_far = along_columns(join_blocks(keep_far, arrived_far, cells_x), peers, order[:middle])
    flipped = [flip_core(stack_blocks(own)) for own in (own_near, own_far)]
    parts = own_near + own_far + flipped
    table = output_table(inverse_y_table(cells_y, groups_y, peers, rows_ky) * (0.5 * inverse_scale))
    return tuple(make_output(flow_field, parts, table, local_weight, bias_terms, modes))


def body(flow_field, spectral_weight, local_weight, bias_terms):
    peers = lax.axis_size("gx")
    extent = lax.axis_size("gy") * flow_field.shape[1]
    paired = lax.axis_size("gy") == 2 and peers & (peers - 1) == 0 and extent & (extent - 1) == 0
    if paired and spectral_weight.shape[1] == 2 * MX and WIDTH % local_weight.shape[0] == 0:
        return row_body(flow_field, spectral_weight, local_weight, bias_terms)
    return general_body(flow_field, spectral_weight, local_weight, bias_terms)


def solution(mesh):
    placed = (P(("group", "gx"), "gy", None), P("gy", "gx", None, None), P(), P())
    return jax.shard_map(
        body,
        mesh=mesh,
        in_specs=placed,
        out_specs=(P(("group", "gx"), "gy", None), P(("group", "gy"), "gx", None)),
        check_vma=False,
    )
```

```python
import functools
import math

import jax
import jax.numpy as jnp
import ml_dtypes
import numpy as np
from jax import lax
from jax.experimental import pallas as pl
from jax.experimental.pallas import tpu as pltpu
from jax.sharding import PartitionSpec as P

MX = 32
MY = 32


def wave_number(index, count):
    return jnp.where(index < count // 2, index, index - count)


def phase_table(waves, places, extent):
    product = waves[:, None] * places[None, :] % extent
    return 2.0 * math.pi / extent * product.astype(jnp.float32)


def row_tables(ky_rows, kx_rows, x_places, extent, width):
    angle = phase_table(wave_number(kx_rows, MX), x_places, extent)
    select = (ky_rows[:, None] == jnp.arange(width, dtype=jnp.int32)[None, :]).astype(jnp.float32)
    cosine = jnp.cos(angle)[:, :, None] * select[:, None, :]
    sine_part = jnp.sin(angle)[:, :, None] * select[:, None, :]
    return (cosine, sine_part)


def forward_rows(y_local, ky_rows, kx_rows, x_places, extent):
    cosine, sine_part = row_tables(ky_rows, kx_rows, x_places, extent, y_local.shape[0])
    real_in = y_local[:, 0]
    imag_in = y_local[:, 1]

    def contract(table, values):
        return jnp.einsum("rxk,kxf->rf", table, values, precision=lax.Precision.HIGHEST)

    real_out = contract(cosine, real_in) + contract(sine_part, imag_in)
    imag_out = contract(cosine, imag_in) - contract(sine_part, real_in)
    return jnp.concatenate([real_out, imag_out], axis=1)


def inverse_rows(running, shard_rows, ky_rows, kx_rows, x_places, extent):
    cosine, sine_part = row_tables(ky_rows, kx_rows, x_places, extent, running.shape[0])
    feat_count = shard_rows.shape[1] // 2
    real_part = shard_rows[:, :feat_count]
    imag_part = shard_rows[:, feat_count:]

    def contract(table, values):
        return jnp.einsum("rxk,rf->kxf", table, values, precision=lax.Precision.HIGHEST)

    new_real = contract(cosine, real_part) - contract(sine_part, imag_part)
    new_imag = contract(cosine, imag_part) + contract(sine_part, real_part)
    return jnp.stack([new_real, new_imag], axis=1)


def general_body(flow_field, spectral_weight, local_weight, bias_terms):
    cells_x, cells_y, feat_count = flow_field.shape
    channels = local_weight.shape[0]
    planes = feat_count // channels
    groups_x = lax.axis_size("gx")
    groups_y = lax.axis_size("gy")
    extent_x = cells_x * groups_x
    extent_y = cells_y * groups_y
    half_width = MY // groups_y
    quota_rows = spectral_weight.shape[1]
    high = lax.Precision.HIGHEST
    x_places = lax.axis_index("gx") * cells_x + jnp.arange(cells_x, dtype=jnp.int32)
    y_places = lax.axis_index("gy") * cells_y + jnp.arange(cells_y, dtype=jnp.int32)
    y_angle = phase_table(wave_number(jnp.arange(MY, dtype=jnp.int32), MY), y_places, extent_y)
    y_table = (
        jnp.stack([jnp.cos(y_angle), -jnp.sin(y_angle)], axis=1)
        .reshape(2 * MY, cells_y)
        .astype(jnp.bfloat16)
    )
    y_local = lax.psum_scatter(
        jnp.einsum("qy,xyf->qxf", y_table, flow_field, preferred_element_type=jnp.float32),
        "gy",
        scatter_dimension=0,
        tiled=True,
    )
    y_local = y_local.reshape(half_width, 2, cells_x, feat_count)
    rest_index = jnp.arange(lax.axis_size("gx") * quota_rows, dtype=jnp.int32)
    spectrum = lax.psum_scatter(
        forward_rows(y_local, rest_index // MX, rest_index % MX, x_places, extent_x),
        "gx",
        scatter_dimension=0,
        tiled=True,
    )
    spectrum = spectrum * (1.0 / math.sqrt(extent_x * extent_y))
    coeffs = spectrum.reshape(quota_rows, 2, planes, channels)
    weights = spectral_weight[0].astype(jnp.float32)
    product = jnp.einsum("rpzc,rco->rpzo", coeffs, weights, precision=high)
    mixed_real = product[:, 0, :, :channels] - product[:, 1, :, channels:]
    mixed_imag = product[:, 0, :, channels:] + product[:, 1, :, :channels]
    mixed_local = jnp.stack([mixed_real, mixed_imag], axis=1).reshape(quota_rows, 2 * feat_count)
    pointwise = jnp.einsum(
        "xyzc,co->xyzo",
        flow_field.reshape(cells_x, cells_y, planes, channels),
        local_weight,
        preferred_element_type=jnp.float32,
    )
    start_half = jnp.zeros((half_width, 2, cells_x, feat_count), jnp.float32)
    shard_rows = lax.all_gather(mixed_local, "gx", axis=0, tiled=True)
    rest_index = jnp.arange(shard_rows.shape[0], dtype=jnp.int32)
    back_half = inverse_rows(
        start_half, shard_rows, rest_index // MX, rest_index % MX, x_places, extent_x
    )
    back_whole = lax.all_gather(back_half, "gy", axis=0, tiled=True)
    y_cos = jnp.cos(y_angle)
    y_sin = jnp.sin(y_angle)
    spectral = (
        jnp.einsum("kn,kxf->xnf", y_cos, back_whole[:, 0], precision=high)
        - jnp.einsum("kn,kxf->xnf", y_sin, back_whole[:, 1], precision=high)
    ) * (1.0 / math.sqrt(MX * MY))
    total = spectral.reshape(cells_x, cells_y, planes, channels) + pointwise + bias_terms
    output = (
        jax.nn.gelu(total, approximate=False)
        .reshape(cells_x, cells_y, feat_count)
        .astype(jnp.bfloat16)
    )
    return (output, mixed_local.reshape(1, quota_rows, 2 * feat_count))


SMALL = pltpu.CompilerParams(vmem_limit_bytes=20 * 1024 * 1024)
LARGE = pltpu.CompilerParams(vmem_limit_bytes=53 * 1024 * 1024)
WIDTH = 256
BIAS_TERMS = 3
LAST = 64
GELU_TERMS = (
    1.5957645177841187,
    0.29075613617897034,
    -0.0014313592109829187,
    -0.006452994421124458,
    0.0015898864949122071,
    -0.0001365363277727738,
)


def angles(count, places, extent):
    index = np.arange(count)
    waves = np.where(index < count // 2, index, index - count)
    product = (waves[:, None] * np.asarray(places)[None, :]) % extent
    return (np.float32(2.0 * math.pi / extent) * product.astype(np.float32)).astype(np.float64)


def split_table(table):
    high = table.astype(ml_dtypes.bfloat16)
    low = (table - high.astype(np.float64)).astype(ml_dtypes.bfloat16)
    return high, low


def split_terms(values):
    high = values.astype(jnp.bfloat16)
    low = (values - high.astype(jnp.float32)).astype(jnp.bfloat16)
    return high, low


def quad():
    place = lax.axis_index("gx")
    return place // 2, place % 2, lax.axis_index("gy")


def turns(layers, inverse=False):
    half = layers // 2
    if inverse:
        return list(range(half, layers)) + list(range(half - 1, -1, -1))
    return list(range(layers - 1, -1, -1))


def forward_x_table(cells_x, peers, rows_ky):
    extent = cells_x * peers
    angle = angles(MX, np.arange(extent), extent)
    cosine, sine = np.cos(angle), np.sin(angle)
    out = np.zeros((2, rows_ky, MX, extent, rows_ky, 2))
    for row in range(rows_ky):
        out[0, row, :, :, row, 0] = cosine
        out[0, row, :, :, row, 1] = sine
        out[1, row, :, :, row, 1] = cosine
        out[1, row, :, :, row, 0] = -sine
    return out.reshape(2 * rows_ky * MX, extent * rows_ky * 2)


def inverse_x_table(cells_x, peers, rows_ky):
    extent = cells_x * peers
    angle = angles(MX, np.arange(extent), extent)
    cosine, sine = np.cos(angle).T, np.sin(angle).T
    out = np.zeros((extent, rows_ky, 2, 2, rows_ky, MX))
    for row in range(rows_ky):
        out[:, row, 0, 0, row, :] = cosine
        out[:, row, 0, 1, row, :] = -sine
        out[:, row, 1, 1, row, :] = cosine
        out[:, row, 1, 0, row, :] = sine
    out = out.reshape(peers // 2, 2, cells_x * rows_ky * 2, 2 * rows_ky * MX)
    return np.moveaxis(out, 1, 0)


def inverse_y_table(cells_y, groups_y, peers, rows_ky):
    extent = cells_y * groups_y
    angle = angles(MY, np.arange(extent), extent)
    full = np.stack([np.cos(angle), -np.sin(angle)], axis=1)
    full = full.reshape(groups_y, peers, rows_ky, 2, groups_y, cells_y)
    out = np.zeros((groups_y, 2, cells_y, peers, 2, rows_ky, 2))
    for y in range(groups_y):
        for column in range(2):
            for peer in range(peers):
                for place in range(2):
                    half = y ^ place ^ column ^ (peer % 2)
                    out[y, column, :, peer, place] = np.moveaxis(full[half, peer, :, :, y], -1, 0)
    return out.reshape(groups_y, 2, cells_y, 4 * peers * rows_ky)


def output_table(table):
    high, low = split_table(table)
    parts = [high, high, low, np.ones(table.shape[:-1] + (BIAS_TERMS,), high.dtype)]
    used = 3 * table.shape[-1] + BIAS_TERMS
    parts.append(np.zeros(table.shape[:-1] + (-used % 256,), high.dtype))
    return np.concatenate(parts, axis=-1)


def dot(left, right):
    return jnp.dot(left, right, preferred_element_type=jnp.float32)


def column_of(x, y):
    return x ^ y


def forward_y_table(shape, extent, layers, rows_ky):
    z, x, y = quad()
    peers = 2 * layers
    row = lax.broadcasted_iota(jnp.int32, (shape[0], 1), 0)
    block = row // (2 * rows_ky)
    place = block // 2 % layers
    turn = layers - 1 - place
    side = y ^ (1 - block // peers)
    owner = (side ^ (block % 2)) * peers + (z ^ turn) * 2 + column_of(x, side)
    index = owner * rows_ky + row // 2 % rows_ky
    y_places = lax.broadcasted_iota(jnp.int32, (1, shape[1]), 1) + y * shape[1]
    steps = (wave_number(index, MY) * y_places) & (extent - 1)
    angle = 2.0 * math.pi / extent * steps.astype(jnp.float32)
    return jnp.where(row % 2 == 0, jnp.cos(angle), -jnp.sin(angle)).astype(jnp.bfloat16)


def forward_y_kernel(extent, rows_ky, flow_hbm, *refs):
    out_refs, (flow_ref, arrived) = refs[:4], refs[4:]
    half, _, rows, feat_count = out_refs[0].shape
    layers = 2 * half
    cells_x, cells_y, _ = flow_ref.shape
    rows = rows // cells_x
    copies = [
        pltpu.make_async_copy(flow_hbm.at[x], flow_ref.at[x], arrived.at[x])
        for x in range(cells_x)
    ]
    for copy in copies:
        copy.start()
    table = forward_y_table((2 * MY, cells_y), extent, layers, rows_ky)
    for x in range(cells_x):
        copies[x].wait()
        result = dot(table, flow_ref[x]).reshape(4, half, 2, rows, feat_count)
        for index, out_ref in enumerate(out_refs):
            out_ref[:, :, x * rows : (x + 1) * rows, :] = result[index]


def forward_y(flow_field, extent, layers, rows_ky):
    cells_x, _, feat_count = flow_field.shape
    shape = jax.ShapeDtypeStruct((layers // 2, 2, cells_x * 2 * rows_ky, feat_count), jnp.float32)
    return pl.pallas_call(
        functools.partial(forward_y_kernel, extent, rows_ky),
        in_specs=[pl.BlockSpec(memory_space=pltpu.HBM)],
        out_shape=[shape] * 4,
        scratch_shapes=[
            pltpu.VMEM(flow_field.shape, flow_field.dtype),
            pltpu.SemaphoreType.DMA((cells_x,)),
        ],
        compiler_params=LARGE,
        name="forward_y",
    )(flow_field)


def flip_core(block):
    return lax.ppermute(block, "gy", [(0, 1), (1, 0)])


def along_columns(blocks, peers, order):
    arrived = []
    for turn, block in zip(order, blocks):
        pairs = [
            (2 * place + core, 2 * (place ^ (2 * turn + column_of(0, core))) + core)
            for place in range(peers)
            for core in range(2)
        ]
        arrived.append(lax.ppermute(block, ("gx", "gy"), pairs))
    return arrived


def small_call(kernel, out_shape, name):
    return pl.pallas_call(kernel, out_shape=out_shape, compiler_params=SMALL, name=name)


def second_kernel(*refs):
    for index, block_ref in enumerate(refs[:-1]):
        refs[-1][index] = block_ref[1]


def second_halves(blocks):
    shape = jax.ShapeDtypeStruct((len(blocks),) + blocks[0].shape[1:], blocks[0].dtype)
    return small_call(second_kernel, shape, "second_halves")(*blocks)


def stack_kernel(*refs):
    for index, block_ref in enumerate(refs[:-1]):
        refs[-1][index] = block_ref[...]


def stack_blocks(blocks):
    shape = jax.ShapeDtypeStruct((len(blocks),) + blocks[0].shape, blocks[0].dtype)
    return small_call(stack_kernel, shape, "stack_blocks")(*blocks)


def add_kernel(keep_ref, arrived_ref, *out_refs):
    for turn, out_ref in enumerate(out_refs):
        out_ref[...] = keep_ref[turn] + arrived_ref[turn]


def add_blocks(keep, arrived):
    shape = jax.ShapeDtypeStruct(keep.shape[1:], keep.dtype)
    return small_call(add_kernel, [shape] * keep.shape[0], "add_blocks")(keep, arrived)


def join_kernel(keep_ref, arrived_ref, *out_refs):
    cells_x, rows, _ = out_refs[0].shape
    rows = rows // 2
    for turn, out_ref in enumerate(out_refs):
        for cell in range(cells_x):
            span = slice(cell * rows, (cell + 1) * rows)
            out_ref[cell] = jnp.concatenate(
                [keep_ref[turn, span, :], arrived_ref[turn, span, :]], axis=0
            )


def join_blocks(keep, arrived, cells_x):
    layers, rows, feat_count = keep.shape
    shape = jax.ShapeDtypeStruct((cells_x, 2 * rows // cells_x, feat_count), keep.dtype)
    return small_call(join_kernel, [shape] * layers, "join_blocks")(keep, arrived)


def back_rows(inverse_high, inverse_low, modes, chosen, shape, other):
    z, x, y = quad()
    places = [(column_of(x, y) ^ other, z ^ turn) for turn in chosen]
    table_high, table_low = [
        jnp.concatenate([ref[column, place] for column, place in places], axis=0)
        for ref in (inverse_high, inverse_low)
    ]
    high, low = split_terms(modes)
    back = dot(table_high, high) + dot(table_high, low) + dot(table_low, high)
    return back.reshape(shape)


def mix_kernel(layers, *refs):
    half = layers // 2
    block_refs = refs[:layers]
    far_arrived, near_arrived = refs[layers : layers + 2]
    weight_ref, forward_high, forward_low, inverse_high, inverse_low = refs[
        layers + 2 : layers + 7
    ]
    modes_ref, far_ref, order_ref, spread_ref, result_ref = refs[layers + 7 :]
    z, x, y = quad()
    column = column_of(x, y)
    for index, turn in enumerate(turns(layers)):
        arrived_ref = near_arrived if index >= half else far_arrived
        order_ref[(z ^ turn) * 2 + column] = block_refs[index][0]
        order_ref[(z ^ turn) * 2 + (column ^ 1)] = arrived_ref[index % half]
    feat_count = order_ref.shape[-1]
    count = weight_ref.shape[1]
    channels = weight_ref.shape[2]
    tiles = feat_count // 128
    group = 2 * tiles
    high, low = split_terms(order_ref[...].reshape(-1, feat_count))
    spectrum = (
        dot(forward_high[...], high) + dot(forward_high[...], low) + dot(forward_low[...], high)
    )
    for part in range(2):
        for tile in range(tiles):
            spread_ref[pl.ds(part * tiles + tile, count, stride=group), :] = spectrum[
                part * count : (part + 1) * count, tile * 128 : (tile + 1) * 128
            ]
    rows = lax.broadcasted_iota(jnp.int32, (8, 128), 0) % group
    lane = lax.broadcasted_iota(jnp.int32, (8, 128), 1) < channels
    sign = jnp.where(rows < tiles, -1.0, 1.0)
    for base in range(0, count * group, 8):
        block = spread_ref[base : base + 8, :]
        turned = pltpu.roll(block, channels, 1)
        firsts, seconds = [], []
        for start in range(0, 8, group):
            span = slice(start, start + group)
            left = jnp.concatenate([block[span], turned[span]], axis=0)[:, :channels]
            left_high, left_low = split_terms(left)
            left = jnp.concatenate([left_high, left_low], axis=0)
            product = dot(left, weight_ref[0, (base + start) // group])
            product = product[: 2 * group] + product[2 * group :]
            firsts.append(product[:group])
            seconds.append(product[group:])
        first = jnp.concatenate(firsts, axis=0)
        second = jnp.concatenate(seconds, axis=0)
        real = jnp.where(lane, first, pltpu.roll(second, channels, 1))
        imag = jnp.where(lane, pltpu.roll(first, channels, 1), second)
        crossed = jnp.where(rows < tiles, pltpu.roll(imag, 8 - tiles, 0), pltpu.roll(imag, tiles, 0))
        result_ref[base : base + 8, :] = real + sign * crossed
    for part in range(2):
        for tile in range(tiles):
            modes_ref[part * count : (part + 1) * count, tile * 128 : (tile + 1) * 128] = (
                result_ref[pl.ds(part * tiles + tile, count, stride=group), :]
            )
    chosen = turns(layers, True)[:half]
    far_ref[...] = back_rows(
        inverse_high, inverse_low, modes_ref[...], chosen, far_ref.shape, 1
    )


def mix(blocks, arrived, weights, forward_table, inverse_tables):
    layers = len(blocks)
    _, rows, feat_count = blocks[0].shape
    count = weights.shape[1]
    scratch = pltpu.VMEM((count * feat_count // 64, 128), jnp.float32)
    return pl.pallas_call(
        functools.partial(mix_kernel, layers),
        out_shape=[
            jax.ShapeDtypeStruct((2 * count, feat_count), jnp.float32),
            jax.ShapeDtypeStruct((layers // 2, rows, feat_count), jnp.float32),
        ],
        scratch_shapes=[pltpu.VMEM((2 * layers, rows, feat_count), jnp.float32), scratch, scratch],
        compiler_params=SMALL,
        name="mix",
    )(*blocks, *arrived, weights, *split_table(forward_table), *inverse_tables)


def keep_kernel(modes_ref, inverse_high, inverse_low, far_ref, near_ref, send_ref):
    half = far_ref.shape[0]
    order = turns(2 * half, True)
    modes = modes_ref[...]
    shape = (2 * half,) + far_ref.shape[1:]
    send_ref[...] = back_rows(inverse_high, inverse_low, modes, order[half:], send_ref.shape, 1)
    keep = back_rows(inverse_high, inverse_low, modes, order, shape, 0)
    far_ref[...] = keep[:half]
    near_ref[...] = keep[half:]


def keep_rows(modes, inverse_tables, like):
    return pl.pallas_call(
        keep_kernel,
        out_shape=[jax.ShapeDtypeStruct(like.shape, jnp.float32)] * 3,
        compiler_params=SMALL,
        name="keep_rows",
    )(modes, *inverse_tables)


def gelu(half):
    square = jnp.minimum(half * half, 6.25)
    inner = jnp.full_like(square, GELU_TERMS[-1])
    for term in GELU_TERMS[-2::-1]:
        inner = inner * square + term
    return half + half * jnp.tanh(half * inner)


def output_kernel(layers, flow_ref, table_ref, local_ref, bias_ref, modes_ref, *refs):
    own_refs = refs[layers // 2 : layers] + refs[: layers // 2]
    near_ref, far_ref = refs[layers : layers + 2]
    core_refs = [ref.at[index] for ref in (far_ref, near_ref) for index in range(layers // 2)]
    out_hbm, mixed_hbm, order_ref, wide_ref, level_ref, done_ref, sent = refs[layers + 2 :]
    cells_x, cells_y, feat_count = flow_ref.shape
    channels = local_ref.shape[0]
    z, x, y = quad()
    wide_ref[...] = jnp.zeros_like(wide_ref)
    for start in range(0, WIDTH, channels):
        span = slice(start, start + channels)
        wide_ref[span, span] = local_ref[...] * 0.5
        level_ref[:, span] = bias_ref[...].reshape(1, channels) * 0.5
    level = level_ref[...]
    levels = []
    for _ in range(BIAS_TERMS):
        levels.append(level.astype(jnp.bfloat16).astype(jnp.float32))
        level = level - levels[-1]
    terms = 3 * order_ref.shape[1] * order_ref.shape[2]
    filled = jnp.zeros((table_ref.shape[-1] - terms - BIAS_TERMS, WIDTH), jnp.float32)
    below = jnp.concatenate(levels + [filled], axis=0).astype(jnp.bfloat16)
    below = jnp.concatenate([below, wide_ref[...]], axis=0)
    for column, block_refs in ((x ^ y, own_refs), (x ^ y ^ 1, core_refs)):
        for turn, block_ref in zip(turns(layers, True), block_refs):
            order_ref[:, (z ^ turn) * 2 + column] = block_ref[...]
    table = table_ref[y, x ^ y]
    count = modes_ref.shape[0] // 2
    copies = []
    for part in range(2):
        copies.append(
            pltpu.make_async_copy(
                modes_ref.at[pl.ds(part * count, count)],
                mixed_hbm.at[0, :, pl.ds(part * feat_count, feat_count)],
                sent.at[part],
            )
        )
        copies[-1].start()
    for cell in range(cells_x):
        high, low = split_terms(order_ref[cell].reshape(-1, feat_count))
        stack = jnp.concatenate([high, low, high], axis=0)
        bounds = [0, cells_y - LAST, cells_y] if cell == cells_x - 1 else [0, cells_y]
        for begin, end in zip(bounds[:-1], bounds[1:]):
            rows = slice(begin, end)
            for start in range(0, feat_count, WIDTH):
                columns = slice(start, start + WIDTH)
                total = dot(
                    jnp.concatenate([table[rows], flow_ref[cell, rows, columns]], axis=1),
                    jnp.concatenate([stack[:, columns], below], axis=0),
                )
                done_ref[cell, rows, columns] = gelu(total).astype(done_ref.dtype)
            copies.append(
                pltpu.make_async_copy(
                    done_ref.at[cell, rows], out_hbm.at[cell, rows], sent.at[len(copies)]
                )
            )
            copies[-1].start()
    for copy in copies:
        copy.wait()


def make_output(flow_field, parts, table, local, bias, modes):
    cells_x, _, feat_count = flow_field.shape
    layers = len(parts) - 2
    rows, _ = modes.shape
    return pl.pallas_call(
        functools.partial(output_kernel, layers),
        out_specs=[pl.BlockSpec(memory_space=pl.ANY)] * 2,
        scratch_shapes=[
            pltpu.VMEM((cells_x, 2 * layers) + parts[0].shape[1:], jnp.float32),
            pltpu.VMEM((WIDTH, WIDTH), jnp.bfloat16),
            pltpu.VMEM((1, WIDTH), jnp.float32),
            pltpu.VMEM(flow_field.shape, jnp.bfloat16),
            pltpu.SemaphoreType.DMA((cells_x + 3,)),
        ],
        out_shape=[
            jax.ShapeDtypeStruct(flow_field.shape, jnp.bfloat16),
            jax.ShapeDtypeStruct((1, rows // 2, 2 * feat_count), jnp.float32),
        ],
        compiler_params=SMALL,
        name="make_output",
    )(flow_field, table, local, bias, modes, *parts)


def row_body(flow_field, spectral_weight, local_weight, bias_terms):
    cells_x, cells_y, feat_count = flow_field.shape
    peers = lax.axis_size("gx")
    groups_y = lax.axis_size("gy")
    rows_ky = MY // groups_y // peers
    forward_scale = 1.0 / math.sqrt(cells_x * peers * cells_y * groups_y)
    inverse_scale = 1.0 / math.sqrt(MX * MY)

    send_far, send_near, keep_far, keep_near = forward_y(
        flow_field, cells_y * groups_y, peers // 2, rows_ky
    )
    order = turns(peers // 2)
    middle = peers // 4
    near = along_columns(add_blocks(keep_near, flip_core(send_near)), peers, order[middle:])
    far = along_columns(add_blocks(keep_far, flip_core(send_far)), peers, order[:middle])
    blocks = far + near
    inverse_tables = split_table(inverse_x_table(cells_x, peers, rows_ky))
    modes, send_far = mix(
        blocks,
        [flip_core(second_halves(far)), flip_core(second_halves(near))],
        spectral_weight,
        forward_x_table(cells_x, peers, rows_ky) * forward_scale,
        inverse_tables,
    )
    keep_far, keep_near, send_near = keep_rows(modes, inverse_tables, send_far)
    arrived_near, arrived_far = flip_core(send_near), flip_core(send_far)
    order = turns(peers // 2, True)
    own_near = along_columns(join_blocks(keep_near, arrived_near, cells_x), peers, order[middle:])
    own_far = along_columns(join_blocks(keep_far, arrived_far, cells_x), peers, order[:middle])
    flipped = [flip_core(stack_blocks(own)) for own in (own_near, own_far)]
    parts = own_near + own_far + flipped
    table = output_table(inverse_y_table(cells_y, groups_y, peers, rows_ky) * (0.5 * inverse_scale))
    return tuple(make_output(flow_field, parts, table, local_weight, bias_terms, modes))


def body(flow_field, spectral_weight, local_weight, bias_terms):
    peers = lax.axis_size("gx")
    extent = lax.axis_size("gy") * flow_field.shape[1]
    paired = lax.axis_size("gy") == 2 and peers & (peers - 1) == 0 and extent & (extent - 1) == 0
    if paired and spectral_weight.shape[1] == 2 * MX and WIDTH % local_weight.shape[0] == 0:
        return row_body(flow_field, spectral_weight, local_weight, bias_terms)
    return general_body(flow_field, spectral_weight, local_weight, bias_terms)


def solution(mesh):
    placed = (P(("group", "gx"), "gy", None), P("gy", "gx", None, None), P(), P())
    return jax.shard_map(
        body,
        mesh=mesh,
        in_specs=placed,
        out_specs=(P(("group", "gx"), "gy", None), P(("group", "gy"), "gx", None)),
        check_vma=False,
    )
```

```python
import functools
import math

import jax
import jax.numpy as jnp
import ml_dtypes
import numpy as np
from jax import lax
from jax.experimental import pallas as pl
from jax.experimental.pallas import tpu as pltpu
from jax.sharding import PartitionSpec as P

MX = 32
MY = 32


def wave_number(index, count):
    return jnp.where(index < count // 2, index, index - count)


def phase_table(waves, places, extent):
    product = waves[:, None] * places[None, :] % extent
    return 2.0 * math.pi / extent * product.astype(jnp.float32)


def row_tables(ky_rows, kx_rows, x_places, extent, width):
    angle = phase_table(wave_number(kx_rows, MX), x_places, extent)
    select = (ky_rows[:, None] == jnp.arange(width, dtype=jnp.int32)[None, :]).astype(jnp.float32)
    cosine = jnp.cos(angle)[:, :, None] * select[:, None, :]
    sine_part = jnp.sin(angle)[:, :, None] * select[:, None, :]
    return (cosine, sine_part)


def forward_rows(y_local, ky_rows, kx_rows, x_places, extent):
    cosine, sine_part = row_tables(ky_rows, kx_rows, x_places, extent, y_local.shape[0])
    real_in = y_local[:, 0]
    imag_in = y_local[:, 1]

    def contract(table, values):
        return jnp.einsum("rxk,kxf->rf", table, values, precision=lax.Precision.HIGHEST)

    real_out = contract(cosine, real_in) + contract(sine_part, imag_in)
    imag_out = contract(cosine, imag_in) - contract(sine_part, real_in)
    return jnp.concatenate([real_out, imag_out], axis=1)


def inverse_rows(running, shard_rows, ky_rows, kx_rows, x_places, extent):
    cosine, sine_part = row_tables(ky_rows, kx_rows, x_places, extent, running.shape[0])
    feat_count = shard_rows.shape[1] // 2
    real_part = shard_rows[:, :feat_count]
    imag_part = shard_rows[:, feat_count:]

    def contract(table, values):
        return jnp.einsum("rxk,rf->kxf", table, values, precision=lax.Precision.HIGHEST)

    new_real = contract(cosine, real_part) - contract(sine_part, imag_part)
    new_imag = contract(cosine, imag_part) + contract(sine_part, real_part)
    return jnp.stack([new_real, new_imag], axis=1)


def general_body(flow_field, spectral_weight, local_weight, bias_terms):
    cells_x, cells_y, feat_count = flow_field.shape
    channels = local_weight.shape[0]
    planes = feat_count // channels
    groups_x = lax.axis_size("gx")
    groups_y = lax.axis_size("gy")
    extent_x = cells_x * groups_x
    extent_y = cells_y * groups_y
    half_width = MY // groups_y
    quota_rows = spectral_weight.shape[1]
    high = lax.Precision.HIGHEST
    x_places = lax.axis_index("gx") * cells_x + jnp.arange(cells_x, dtype=jnp.int32)
    y_places = lax.axis_index("gy") * cells_y + jnp.arange(cells_y, dtype=jnp.int32)
    y_angle = phase_table(wave_number(jnp.arange(MY, dtype=jnp.int32), MY), y_places, extent_y)
    y_table = (
        jnp.stack([jnp.cos(y_angle), -jnp.sin(y_angle)], axis=1)
        .reshape(2 * MY, cells_y)
        .astype(jnp.bfloat16)
    )
    y_local = lax.psum_scatter(
        jnp.einsum("qy,xyf->qxf", y_table, flow_field, preferred_element_type=jnp.float32),
        "gy",
        scatter_dimension=0,
        tiled=True,
    )
    y_local = y_local.reshape(half_width, 2, cells_x, feat_count)
    rest_index = jnp.arange(lax.axis_size("gx") * quota_rows, dtype=jnp.int32)
    spectrum = lax.psum_scatter(
        forward_rows(y_local, rest_index // MX, rest_index % MX, x_places, extent_x),
        "gx",
        scatter_dimension=0,
        tiled=True,
    )
    spectrum = spectrum * (1.0 / math.sqrt(extent_x * extent_y))
    coeffs = spectrum.reshape(quota_rows, 2, planes, channels)
    weights = spectral_weight[0].astype(jnp.float32)
    product = jnp.einsum("rpzc,rco->rpzo", coeffs, weights, precision=high)
    mixed_real = product[:, 0, :, :channels] - product[:, 1, :, channels:]
    mixed_imag = product[:, 0, :, channels:] + product[:, 1, :, :channels]
    mixed_local = jnp.stack([mixed_real, mixed_imag], axis=1).reshape(quota_rows, 2 * feat_count)
    pointwise = jnp.einsum(
        "xyzc,co->xyzo",
        flow_field.reshape(cells_x, cells_y, planes, channels),
        local_weight,
        preferred_element_type=jnp.float32,
    )
    start_half = jnp.zeros((half_width, 2, cells_x, feat_count), jnp.float32)
    shard_rows = lax.all_gather(mixed_local, "gx", axis=0, tiled=True)
    rest_index = jnp.arange(shard_rows.shape[0], dtype=jnp.int32)
    back_half = inverse_rows(
        start_half, shard_rows, rest_index // MX, rest_index % MX, x_places, extent_x
    )
    back_whole = lax.all_gather(back_half, "gy", axis=0, tiled=True)
    y_cos = jnp.cos(y_angle)
    y_sin = jnp.sin(y_angle)
    spectral = (
        jnp.einsum("kn,kxf->xnf", y_cos, back_whole[:, 0], precision=high)
        - jnp.einsum("kn,kxf->xnf", y_sin, back_whole[:, 1], precision=high)
    ) * (1.0 / math.sqrt(MX * MY))
    total = spectral.reshape(cells_x, cells_y, planes, channels) + pointwise + bias_terms
    output = (
        jax.nn.gelu(total, approximate=False)
        .reshape(cells_x, cells_y, feat_count)
        .astype(jnp.bfloat16)
    )
    return (output, mixed_local.reshape(1, quota_rows, 2 * feat_count))


SMALL = pltpu.CompilerParams(vmem_limit_bytes=20 * 1024 * 1024)
LARGE = pltpu.CompilerParams(vmem_limit_bytes=53 * 1024 * 1024)
WIDTH = 256
BIAS_TERMS = 3
LAST = 64
FIRST = 64
GELU_TERMS = (
    1.5957645177841187,
    0.29075613617897034,
    -0.0014313592109829187,
    -0.006452994421124458,
    0.0015898864949122071,
    -0.0001365363277727738,
)


def angles(count, places, extent):
    index = np.arange(count)
    waves = np.where(index < count // 2, index, index - count)
    product = (waves[:, None] * np.asarray(places)[None, :]) % extent
    return (np.float32(2.0 * math.pi / extent) * product.astype(np.float32)).astype(np.float64)


def split_table(table):
    high = table.astype(ml_dtypes.bfloat16)
    low = (table - high.astype(np.float64)).astype(ml_dtypes.bfloat16)
    return high, low


def split_terms(values):
    high = values.astype(jnp.bfloat16)
    low = (values - high.astype(jnp.float32)).astype(jnp.bfloat16)
    return high, low


def quad():
    place = lax.axis_index("gx")
    return place // 2, place % 2, lax.axis_index("gy")


def turns(layers, inverse=False):
    half = layers // 2
    if inverse:
        return list(range(half, layers)) + list(range(half))
    return list(range(layers - 1, -1, -1))


def forward_x_table(cells_x, peers, rows_ky):
    extent = cells_x * peers
    angle = angles(MX, np.arange(extent), extent)
    cosine, sine = np.cos(angle), np.sin(angle)
    out = np.zeros((2, rows_ky, MX, extent, rows_ky, 2))
    for row in range(rows_ky):
        out[0, row, :, :, row, 0] = cosine
        out[0, row, :, :, row, 1] = sine
        out[1, row, :, :, row, 1] = cosine
        out[1, row, :, :, row, 0] = -sine
    return out.reshape(2 * rows_ky * MX, extent * rows_ky * 2)


def inverse_x_table(cells_x, peers, rows_ky):
    extent = cells_x * peers
    angle = angles(MX, np.arange(extent), extent)
    cosine, sine = np.cos(angle).T, np.sin(angle).T
    out = np.zeros((extent, rows_ky, 2, 2, rows_ky, MX))
    for row in range(rows_ky):
        out[:, row, 0, 0, row, :] = cosine
        out[:, row, 0, 1, row, :] = -sine
        out[:, row, 1, 1, row, :] = cosine
        out[:, row, 1, 0, row, :] = sine
    out = out.reshape(peers // 2, 2, cells_x * rows_ky * 2, 2 * rows_ky * MX)
    return np.moveaxis(out, 1, 0)


def inverse_y_table(cells_y, groups_y, peers, rows_ky):
    extent = cells_y * groups_y
    angle = angles(MY, np.arange(extent), extent)
    full = np.stack([np.cos(angle), -np.sin(angle)], axis=1)
    full = full.reshape(groups_y, peers, rows_ky, 2, groups_y, cells_y)
    out = np.zeros((groups_y, 2, cells_y, peers, 2, rows_ky, 2))
    for y in range(groups_y):
        for column in range(2):
            for peer in range(peers):
                for place in range(2):
                    half = y ^ place ^ column ^ (peer % 2)
                    out[y, column, :, peer, place] = np.moveaxis(full[half, peer, :, :, y], -1, 0)
    return out.reshape(groups_y, 2, cells_y, 4 * peers * rows_ky)


def output_table(table):
    high, low = split_table(table)
    parts = [high, high, low, np.ones(table.shape[:-1] + (BIAS_TERMS,), high.dtype)]
    used = 3 * table.shape[-1] + BIAS_TERMS
    parts.append(np.zeros(table.shape[:-1] + (-used % 256,), high.dtype))
    return np.concatenate(parts, axis=-1)


def dot(left, right):
    return jnp.dot(left, right, preferred_element_type=jnp.float32)


def column_of(x, y):
    return x ^ y


def forward_y_table(shape, extent, layers, rows_ky):
    z, x, y = quad()
    peers = 2 * layers
    row = lax.broadcasted_iota(jnp.int32, (shape[0], 1), 0)
    block = row // (2 * rows_ky)
    place = block // 2 % layers
    turn = layers - 1 - place
    side = y ^ (1 - block // peers)
    owner = (side ^ (block % 2)) * peers + (z ^ turn) * 2 + column_of(x, side)
    index = owner * rows_ky + row // 2 % rows_ky
    y_places = lax.broadcasted_iota(jnp.int32, (1, shape[1]), 1) + y * shape[1]
    steps = (wave_number(index, MY) * y_places) & (extent - 1)
    angle = 2.0 * math.pi / extent * steps.astype(jnp.float32)
    return jnp.where(row % 2 == 0, jnp.cos(angle), -jnp.sin(angle)).astype(jnp.bfloat16)


def forward_y_kernel(extent, rows_ky, flow_hbm, *refs):
    out_refs, (flow_ref, arrived) = refs[:4], refs[4:]
    half, _, rows, feat_count = out_refs[0].shape
    layers = 2 * half
    cells_x, cells_y, _ = flow_ref.shape
    rows = rows // cells_x
    copies = [
        pltpu.make_async_copy(flow_hbm.at[x], flow_ref.at[x], arrived.at[x])
        for x in range(cells_x)
    ]
    for copy in copies:
        copy.start()
    table = forward_y_table((2 * MY, cells_y), extent, layers, rows_ky)
    for x in range(cells_x):
        copies[x].wait()
        result = dot(table, flow_ref[x]).reshape(4, half, 2, rows, feat_count)
        for index, out_ref in enumerate(out_refs):
            out_ref[:, :, x * rows : (x + 1) * rows, :] = result[index]


def forward_y(flow_field, extent, layers, rows_ky):
    cells_x, _, feat_count = flow_field.shape
    shape = jax.ShapeDtypeStruct((layers // 2, 2, cells_x * 2 * rows_ky, feat_count), jnp.float32)
    return pl.pallas_call(
        functools.partial(forward_y_kernel, extent, rows_ky),
        in_specs=[pl.BlockSpec(memory_space=pltpu.HBM)],
        out_shape=[shape] * 4,
        scratch_shapes=[
            pltpu.VMEM(flow_field.shape, flow_field.dtype),
            pltpu.SemaphoreType.DMA((cells_x,)),
        ],
        compiler_params=LARGE,
        name="forward_y",
    )(flow_field)


def flip_core(block):
    return lax.ppermute(block, "gy", [(0, 1), (1, 0)])


def along_columns(blocks, peers, order):
    arrived = []
    for turn, block in zip(order, blocks):
        pairs = [
            (2 * place + core, 2 * (place ^ (2 * turn + column_of(0, core))) + core)
            for place in range(peers)
            for core in range(2)
        ]
        arrived.append(lax.ppermute(block, ("gx", "gy"), pairs))
    return arrived


def small_call(kernel, out_shape, name):
    return pl.pallas_call(kernel, out_shape=out_shape, compiler_params=SMALL, name=name)


def second_kernel(*refs):
    for index, block_ref in enumerate(refs[:-1]):
        refs[-1][index] = block_ref[1]


def second_halves(blocks):
    shape = jax.ShapeDtypeStruct((len(blocks),) + blocks[0].shape[1:], blocks[0].dtype)
    return small_call(second_kernel, shape, "second_halves")(*blocks)


def stack_kernel(*refs):
    for index, block_ref in enumerate(refs[:-1]):
        refs[-1][index] = block_ref[...]


def stack_blocks(blocks):
    shape = jax.ShapeDtypeStruct((len(blocks),) + blocks[0].shape, blocks[0].dtype)
    return small_call(stack_kernel, shape, "stack_blocks")(*blocks)


def add_kernel(keep_ref, arrived_ref, *out_refs):
    for turn, out_ref in enumerate(out_refs):
        out_ref[...] = keep_ref[turn] + arrived_ref[turn]


def add_blocks(keep, arrived):
    shape = jax.ShapeDtypeStruct(keep.shape[1:], keep.dtype)
    return small_call(add_kernel, [shape] * keep.shape[0], "add_blocks")(keep, arrived)


def join_kernel(keep_ref, arrived_ref, *out_refs):
    cells_x, rows, _ = out_refs[0].shape
    rows = rows // 2
    for turn, out_ref in enumerate(out_refs):
        for cell in range(cells_x):
            span = slice(cell * rows, (cell + 1) * rows)
            out_ref[cell] = jnp.concatenate(
                [keep_ref[turn, span, :], arrived_ref[turn, span, :]], axis=0
            )


def join_blocks(keep, arrived, cells_x):
    layers, rows, feat_count = keep.shape
    shape = jax.ShapeDtypeStruct((cells_x, 2 * rows // cells_x, feat_count), keep.dtype)
    return small_call(join_kernel, [shape] * layers, "join_blocks")(keep, arrived)


def back_rows(inverse_high, inverse_low, modes, shape, other):
    z, x, y = quad()
    places = [(column_of(x, y) ^ other, z ^ turn) for turn in turns(shape[0], True)]
    table_high, table_low = [
        jnp.concatenate([ref[column, place] for column, place in places], axis=0)
        for ref in (inverse_high, inverse_low)
    ]
    high, low = split_terms(modes)
    back = dot(table_high, high) + dot(table_high, low) + dot(table_low, high)
    return back.reshape(shape)


def mix_kernel(layers, *refs):
    half = layers // 2
    block_refs = refs[:layers]
    far_arrived, near_arrived = refs[layers : layers + 2]
    weight_ref, forward_high, forward_low, inverse_high, inverse_low = refs[
        layers + 2 : layers + 7
    ]
    modes_ref, far_ref, near_ref, order_ref, spread_ref, result_ref = refs[layers + 7 :]
    z, x, y = quad()
    column = column_of(x, y)
    for index, turn in enumerate(turns(layers)):
        arrived_ref = near_arrived if index >= half else far_arrived
        order_ref[(z ^ turn) * 2 + column] = block_refs[index][0]
        order_ref[(z ^ turn) * 2 + (column ^ 1)] = arrived_ref[index % half]
    feat_count = order_ref.shape[-1]
    count = weight_ref.shape[1]
    channels = weight_ref.shape[2]
    tiles = feat_count // 128
    group = 2 * tiles
    high, low = split_terms(order_ref[...].reshape(-1, feat_count))
    spectrum = (
        dot(forward_high[...], high) + dot(forward_high[...], low) + dot(forward_low[...], high)
    )
    for part in range(2):
        for tile in range(tiles):
            spread_ref[pl.ds(part * tiles + tile, count, stride=group), :] = spectrum[
                part * count : (part + 1) * count, tile * 128 : (tile + 1) * 128
            ]
    rows = lax.broadcasted_iota(jnp.int32, (8, 128), 0) % group
    lane = lax.broadcasted_iota(jnp.int32, (8, 128), 1) < channels
    sign = jnp.where(rows < tiles, -1.0, 1.0)
    for base in range(0, count * group, 8):
        block = spread_ref[base : base + 8, :]
        turned = pltpu.roll(block, channels, 1)
        firsts, seconds = [], []
        for start in range(0, 8, group):
            span = slice(start, start + group)
            left = jnp.concatenate([block[span], turned[span]], axis=0)[:, :channels]
            left_high, left_low = split_terms(left)
            left = jnp.concatenate([left_high, left_low], axis=0)
            product = dot(left, weight_ref[0, (base + start) // group])
            product = product[: 2 * group] + product[2 * group :]
            firsts.append(product[:group])
            seconds.append(product[group:])
        first = jnp.concatenate(firsts, axis=0)
        second = jnp.concatenate(seconds, axis=0)
        real = jnp.where(lane, first, pltpu.roll(second, channels, 1))
        imag = jnp.where(lane, pltpu.roll(first, channels, 1), second)
        crossed = jnp.where(rows < tiles, pltpu.roll(imag, 8 - tiles, 0), pltpu.roll(imag, tiles, 0))
        result_ref[base : base + 8, :] = real + sign * crossed
    for part in range(2):
        for tile in range(tiles):
            modes_ref[part * count : (part + 1) * count, tile * 128 : (tile + 1) * 128] = (
                result_ref[pl.ds(part * tiles + tile, count, stride=group), :]
            )
    shape = (layers,) + far_ref.shape[1:]
    send = back_rows(inverse_high, inverse_low, modes_ref[...], shape, 1)
    far_ref[...] = send[: layers // 2]
    near_ref[...] = send[layers // 2 :]


def mix(blocks, arrived, weights, forward_table, inverse_tables):
    layers = len(blocks)
    _, rows, feat_count = blocks[0].shape
    count = weights.shape[1]
    scratch = pltpu.VMEM((count * feat_count // 64, 128), jnp.float32)
    return pl.pallas_call(
        functools.partial(mix_kernel, layers),
        out_shape=[
            jax.ShapeDtypeStruct((2 * count, feat_count), jnp.float32),
            jax.ShapeDtypeStruct((layers // 2, rows, feat_count), jnp.float32),
            jax.ShapeDtypeStruct((layers // 2, rows, feat_count), jnp.float32),
        ],
        scratch_shapes=[pltpu.VMEM((2 * layers, rows, feat_count), jnp.float32), scratch, scratch],
        compiler_params=SMALL,
        name="mix",
    )(*blocks, *arrived, weights, *split_table(forward_table), *inverse_tables)


def keep_kernel(modes_ref, inverse_high, inverse_low, far_ref, near_ref):
    half = far_ref.shape[0]
    shape = (2 * half,) + far_ref.shape[1:]
    keep = back_rows(inverse_high, inverse_low, modes_ref[...], shape, 0)
    far_ref[...] = keep[:half]
    near_ref[...] = keep[half:]


def keep_rows(modes, inverse_tables, like):
    return pl.pallas_call(
        keep_kernel,
        out_shape=[jax.ShapeDtypeStruct(like.shape, jnp.float32)] * 2,
        compiler_params=SMALL,
        name="keep_rows",
    )(modes, *inverse_tables)


def gelu(half):
    square = jnp.minimum(half * half, 6.25)
    inner = jnp.full_like(square, GELU_TERMS[-1])
    for term in GELU_TERMS[-2::-1]:
        inner = inner * square + term
    return half + half * jnp.tanh(half * inner)


def output_kernel(layers, flow_ref, table_ref, local_ref, bias_ref, modes_ref, *refs):
    own_refs = refs[layers // 2 : layers] + refs[: layers // 2]
    near_ref, far_ref = refs[layers : layers + 2]
    core_refs = [ref.at[index] for ref in (far_ref, near_ref) for index in range(layers // 2)]
    out_hbm, mixed_hbm, order_ref, wide_ref, level_ref, done_ref, sent = refs[layers + 2 :]
    cells_x, cells_y, feat_count = flow_ref.shape
    channels = local_ref.shape[0]
    z, x, y = quad()
    wide_ref[...] = jnp.zeros_like(wide_ref)
    for start in range(0, WIDTH, channels):
        span = slice(start, start + channels)
        wide_ref[span, span] = local_ref[...] * 0.5
        level_ref[:, span] = bias_ref[...].reshape(1, channels) * 0.5
    level = level_ref[...]
    levels = []
    for _ in range(BIAS_TERMS):
        levels.append(level.astype(jnp.bfloat16).astype(jnp.float32))
        level = level - levels[-1]
    terms = 3 * order_ref.shape[1] * order_ref.shape[2]
    filled = jnp.zeros((table_ref.shape[-1] - terms - BIAS_TERMS, WIDTH), jnp.float32)
    below = jnp.concatenate(levels + [filled], axis=0).astype(jnp.bfloat16)
    below = jnp.concatenate([below, wide_ref[...]], axis=0)
    for column, block_refs in ((x ^ y, own_refs), (x ^ y ^ 1, core_refs)):
        for turn, block_ref in zip(turns(layers, True), block_refs):
            order_ref[:, (z ^ turn) * 2 + column] = block_ref[...]
    table = table_ref[y, x ^ y]
    count = modes_ref.shape[0] // 2
    copies = []
    for part in range(2):
        copies.append(
            pltpu.make_async_copy(
                modes_ref.at[pl.ds(part * count, count)],
                mixed_hbm.at[0, :, pl.ds(part * feat_count, feat_count)],
                sent.at[part],
            )
        )
        copies[-1].start()
    for cell in range(cells_x):
        high, low = split_terms(order_ref[cell].reshape(-1, feat_count))
        stack = jnp.concatenate([high, low, high], axis=0)
        bounds = [0, cells_y - LAST, cells_y] if cell == cells_x - 1 else [0, cells_y]
        for begin, end in zip(bounds[:-1], bounds[1:]):
            rows = slice(begin, end)
            for start in range(0, feat_count, WIDTH):
                columns = slice(start, start + WIDTH)
                total = dot(
                    jnp.concatenate([table[rows], flow_ref[cell, rows, columns]], axis=1),
                    jnp.concatenate([stack[:, columns], below], axis=0),
                )
                done_ref[cell, rows, columns] = gelu(total).astype(done_ref.dtype)
            copies.append(
                pltpu.make_async_copy(
                    done_ref.at[cell, rows], out_hbm.at[cell, rows], sent.at[len(copies)]
                )
            )
            copies[-1].start()
    for copy in copies:
        copy.wait()


def make_output(flow_field, parts, table, local, bias, modes):
    cells_x, _, feat_count = flow_field.shape
    layers = len(parts) - 2
    rows, _ = modes.shape
    return pl.pallas_call(
        functools.partial(output_kernel, layers),
        out_specs=[pl.BlockSpec(memory_space=pl.ANY)] * 2,
        scratch_shapes=[
            pltpu.VMEM((cells_x, 2 * layers) + parts[0].shape[1:], jnp.float32),
            pltpu.VMEM((WIDTH, WIDTH), jnp.bfloat16),
            pltpu.VMEM((1, WIDTH), jnp.float32),
            pltpu.VMEM(flow_field.shape, jnp.bfloat16),
            pltpu.SemaphoreType.DMA((cells_x + 3,)),
        ],
        out_shape=[
            jax.ShapeDtypeStruct(flow_field.shape, jnp.bfloat16),
            jax.ShapeDtypeStruct((1, rows // 2, 2 * feat_count), jnp.float32),
        ],
        compiler_params=SMALL,
        name="make_output",
    )(flow_field, table, local, bias, modes, *parts)


def row_body(flow_field, spectral_weight, local_weight, bias_terms):
    cells_x, cells_y, feat_count = flow_field.shape
    peers = lax.axis_size("gx")
    groups_y = lax.axis_size("gy")
    rows_ky = MY // groups_y // peers
    forward_scale = 1.0 / math.sqrt(cells_x * peers * cells_y * groups_y)
    inverse_scale = 1.0 / math.sqrt(MX * MY)

    send_far, send_near, keep_far, keep_near = forward_y(
        flow_field, cells_y * groups_y, peers // 2, rows_ky
    )
    order = turns(peers // 2)
    middle = peers // 4
    near = along_columns(add_blocks(keep_near, flip_core(send_near)), peers, order[middle:])
    far = along_columns(add_blocks(keep_far, flip_core(send_far)), peers, order[:middle])
    blocks = far + near
    inverse_tables = split_table(inverse_x_table(cells_x, peers, rows_ky))
    modes, send_far, send_near = mix(
        blocks,
        [flip_core(second_halves(far)), flip_core(second_halves(near))],
        spectral_weight,
        forward_x_table(cells_x, peers, rows_ky) * forward_scale,
        inverse_tables,
    )
    arrived_near, arrived_far = flip_core(send_near), flip_core(send_far)
    keep_far, keep_near = keep_rows(modes, inverse_tables, send_far)
    order = turns(peers // 2, True)
    own_near = along_columns(join_blocks(keep_near, arrived_near, cells_x), peers, order[middle:])
    own_far = along_columns(join_blocks(keep_far, arrived_far, cells_x), peers, order[:middle])
    flipped = [flip_core(stack_blocks(own)) for own in (own_near, own_far)]
    parts = own_near + own_far + flipped
    table = output_table(inverse_y_table(cells_y, groups_y, peers, rows_ky) * (0.5 * inverse_scale))
    return tuple(make_output(flow_field, parts, table, local_weight, bias_terms, modes))


def body(flow_field, spectral_weight, local_weight, bias_terms):
    peers = lax.axis_size("gx")
    extent = lax.axis_size("gy") * flow_field.shape[1]
    paired = lax.axis_size("gy") == 2 and peers & (peers - 1) == 0 and extent & (extent - 1) == 0
    if paired and spectral_weight.shape[1] == 2 * MX and WIDTH % local_weight.shape[0] == 0:
        return row_body(flow_field, spectral_weight, local_weight, bias_terms)
    return general_body(flow_field, spectral_weight, local_weight, bias_terms)


def solution(mesh):
    placed = (P(("group", "gx"), "gy", None), P("gy", "gx", None, None), P(), P())
    return jax.shard_map(
        body,
        mesh=mesh,
        in_specs=placed,
        out_specs=(P(("group", "gx"), "gy", None), P(("group", "gy"), "gx", None)),
        check_vma=False,
    )
```
